32 devices in a mesh: group: 4 (over z), span: 8 (over y, x, core).
Axes of the slice: x: 2, y: 2, z: 4, core: 2. Of those that a mesh axis runs over, the one named last changes fastest.
Arguments:
- tokens: bfloat16 [16384, 1024], P(('group', 'span')), may hold values from -16 to 16
- params: bfloat16 [12623872], P(('group', 'span')), may hold values from -14 to 4
- cotangent: bfloat16 [16384, 1024], P(('group', 'span')), may hold values from -6 to 6
- offsets: int32 [4, 4], P('group'), may hold values from 0 to 4096, as said below
Outputs:
- output: bfloat16 [16384, 1024], P(('group', 'span'))
- grad_tokens: float32 [16384, 1024], P(('group', 'span'))
- grad_params: float32 [12623872], P(('group', 'span'))
- stats: float32 [4], replicated
The draws below stay inside these ranges and needn't reach their ends.
Inputs may be any that keep to these rules, and one draw needn't show every extreme that they name: `offsets`: each row lists, for one group, 0, the starts of its second and third sequences, and 4096. The first sequence ends on the group's first device and the third starts on its last device.
All inputs are finite; a program needn't handle non-finite values.
Results may differ from the reference program's by a relative error of at most 0.014.
Values may be sent and summed in bfloat16 or wider, within the bound.
No kernel may reach another device: no remote copies, remote signals or barrier semaphores. Data moves between devices by JAX's collectives and lax.ppermute only.
A program may use at most 320 MiB of HBM per device.

```python
import math
import jax
import jax.numpy as jnp
from jax import lax

D = 1024
HEADS_Q = 8
HEADS_KV = 2
HEAD_DIM = 64
SSM_HEADS = 24
SSM_DIM = 64
STATE = 128
CONV = 4
FF = 2048
TOK_DEV = 512
GROUPS = 4
GROUP_TOK = 4096
TOKENS = 16384
PARAMS = 12620104
P_FLAT = 12623872
N_GROUP = 4


def draw_tokens(key, part):
    place = jnp.arange(TOKENS, dtype=jnp.float32) / TOKENS
    row_scale = 0.2 * jnp.exp(place * math.log(30.0))
    values = jnp.clip(jax.random.normal(key, (TOKENS, D), jnp.float32), -2.6, 2.6) * row_scale[:, None]
    return values.astype(jnp.bfloat16)


def draw_offsets(key, part):
    lowest = TOK_DEV // 4
    highest = TOK_DEV - min(64, TOK_DEV // 2)
    first_size = jax.random.randint(key, (GROUPS, 1), lowest, highest)
    last_size = jax.random.randint(jax.random.fold_in(key, 1), (GROUPS, 1), lowest, highest)
    zeros_col = jnp.zeros((GROUPS, 1), jnp.int32)
    end_col = jnp.full((GROUPS, 1), GROUP_TOK, jnp.int32)
    return jnp.concatenate([zeros_col, first_size.astype(jnp.int32), (GROUP_TOK - last_size).astype(jnp.int32), end_col], axis=1).astype(jnp.int32)


def draw_params(key, part):

    def noise_of(stream_id, amount):
        sub_key = jax.random.fold_in(key, stream_id)
        return jnp.clip(jax.random.normal(sub_key, (amount,), jnp.float32), -4.0, 4.0)

    def spread(stream_id, amount, lowest, highest):
        return jax.random.uniform(jax.random.fold_in(key, stream_id), (amount,), jnp.float32, lowest, highest)
    ssm_inner = SSM_HEADS * SSM_DIM
    channels = ssm_inner + 2 * STATE
    step_bias = math.log(2.0 / math.sqrt(GROUP_TOK)) + spread(11, SSM_HEADS, -0.5, 0.5)
    log_rate = spread(12, SSM_HEADS, math.log(0.5 / GROUP_TOK), math.log(1.0 / 40.0))
    decay_log = log_rate - jnp.log(jax.nn.softplus(step_bias))
    pieces = [1.0 + 0.1 * noise_of(0, D), noise_of(1, D * HEADS_Q * HEAD_DIM) * (2.0 / math.sqrt(D)), noise_of(2, D * HEADS_KV * HEAD_DIM) / math.sqrt(D), noise_of(3, D * HEADS_KV * HEAD_DIM) / math.sqrt(D), noise_of(4, HEADS_Q * HEAD_DIM * D) * (6.0 / math.sqrt(HEADS_Q * HEAD_DIM)), noise_of(5, D * ssm_inner) / math.sqrt(D), noise_of(6, D * ssm_inner) / math.sqrt(D), noise_of(7, D * 2 * STATE) / math.sqrt(D), noise_of(8, D * SSM_HEADS) / math.sqrt(D), noise_of(9, CONV * channels) * 0.5, noise_of(10, channels) * 0.1, step_bias, decay_log, spread(13, SSM_HEADS, 0.5, 1.5), 1.0 + 0.1 * noise_of(14, ssm_inner), noise_of(15, ssm_inner * D) * (2.0 / math.sqrt(ssm_inner)), 1.0 + 0.1 * noise_of(16, D), noise_of(17, D * FF) / math.sqrt(D), noise_of(18, D * FF) / math.sqrt(D), noise_of(19, FF * D) / math.sqrt(FF), jnp.zeros((P_FLAT - PARAMS,), jnp.float32)]
    return jnp.concatenate(pieces).astype(jnp.bfloat16)


def levels(own_key, dims, shards, smallest, largest):
    level, own = 1.0, jax.random.fold_in(own_key, 6)
    for position, shards_of in shards:
        steps = jnp.exp(jax.random.uniform(jax.random.fold_in(own, position), (shards_of,), jnp.float32, smallest / len(shards), largest / len(shards)))
        level = level * jnp.repeat(steps, dims[position] // shards_of).reshape([-1 if axis == position else 1 for axis in range(len(dims))])
    return level


def scatter_about(stream_key, dims, scale, most, shards=(), held_as=jnp.bfloat16):
    level = levels(stream_key, dims, shards, -0.22, 0.18) if shards else 1.0
    values = jax.random.normal(stream_key, dims, jnp.float32) * scale * level
    return jnp.minimum(jnp.maximum(values, -most), most).astype(held_as)


def setup_inputs(seed: int = 0) -> dict:
    streams_of = jax.random.split(jax.random.key(seed), 5)
    return {
        "tokens": draw_tokens(jax.random.fold_in(streams_of[4], 71), 0),
        "params": draw_params(jax.random.fold_in(streams_of[4], 71), 0),
        "cotangent": scatter_about(streams_of[2], (TOKENS, D), 1.0, 6.0, ((0, 32),)),
        "offsets": draw_offsets(jax.random.fold_in(streams_of[4], 71), 0),
    }


epsilon = 1e-05
rope_base = 100000000000.0
masked_score = -1e+30
highest = lax.Precision.HIGHEST

@jax.custom_vjp
def low(v):
    return lax.optimization_barrier(v.astype(jnp.bfloat16)).astype(jnp.float32)

@jax.custom_vjp
def low_back(v):
    return v

def low_keep(v):
    return (low(v), None)

def low_pass(kept, grad):
    return (grad,)

def back_keep(v):
    return (v, None)

def back_low(kept, grad):
    return (low(grad),)
low.defvjp(low_keep, low_pass)
low_back.defvjp(back_keep, back_low)

def layout():
    ssm_inner = SSM_HEADS * SSM_DIM
    channels = ssm_inner + 2 * STATE
    return [('norm_attn', (D,)), ('w_query', (D, HEADS_Q * HEAD_DIM)), ('w_key', (D, HEADS_KV * HEAD_DIM)), ('w_value', (D, HEADS_KV * HEAD_DIM)), ('w_attn_out', (HEADS_Q * HEAD_DIM, D)), ('w_gate_ssm', (D, ssm_inner)), ('w_x_ssm', (D, ssm_inner)), ('w_b_c', (D, 2 * STATE)), ('w_step', (D, SSM_HEADS)), ('conv_weight', (CONV, channels)), ('conv_bias', (channels,)), ('step_bias', (SSM_HEADS,)), ('decay_log', (SSM_HEADS,)), ('skip_gain', (SSM_HEADS,)), ('norm_ssm', (ssm_inner,)), ('w_ssm_out', (ssm_inner, D)), ('norm_ffn', (D,)), ('w_gate', (D, FF)), ('w_up_proj', (D, FF)), ('w_down', (FF, D))]

def unpack(flat_vector):
    unpacked = {}
    offset = 0
    for name_key, extent in layout():
        amount = math.prod(extent)
        unpacked[name_key] = flat_vector[offset:offset + amount].reshape(extent)
        offset += amount
    return unpacked

def product(left, right):
    return jnp.dot(left, right, precision=highest)

def rms_norm(values, gain):
    return values * lax.rsqrt(lax.optimization_barrier(jnp.mean(values * values, axis=-1, keepdims=True)) + epsilon) * gain

def gated_norm(ssm_y, gate_ssm, gain):
    return rms_norm(ssm_y * jax.nn.silu(gate_ssm), gain)

def sequence_info(row_index, bounds):
    starts = bounds[:-1]
    inside = row_index[:, None] >= starts[None, :]
    seq_id = lax.optimization_barrier(jnp.sum(inside.astype(jnp.int32), axis=1)).astype(jnp.int32) - 1
    seq_start = lax.optimization_barrier(jnp.max(jnp.where(inside, starts[None, :], 0), axis=1)).astype(jnp.int32)
    return (seq_id, (row_index - seq_start).astype(jnp.int32))

def rotary_tables(positions):
    half_dim = HEAD_DIM // 2
    freqs = jnp.exp(-jnp.arange(half_dim, dtype=jnp.float32) * (2.0 * math.log(rope_base) / HEAD_DIM))
    angles = positions.astype(jnp.float32)[:, None] * freqs[None, :]
    return (jnp.cos(angles), jnp.sin(angles))

def rotate(values, cosine, sine, heads):
    row_count = values.shape[0]
    half_dim = HEAD_DIM // 2
    split_heads = values.reshape(row_count, heads, HEAD_DIM)
    first_half = split_heads[..., :half_dim]
    second_half = split_heads[..., half_dim:]
    cos_b = cosine[:, None, :]
    sin_b = sine[:, None, :]
    turned = jnp.concatenate([first_half * cos_b - second_half * sin_b, second_half * cos_b + first_half * sin_b], axis=-1)
    return turned.reshape(row_count, heads * HEAD_DIM)

def conv_apply(extended, conv_weight, conv_bias, positions):
    row_count = positions.shape[0]
    conv_total = conv_bias[None, :]
    for tap_index in range(CONV):
        window = extended[tap_index:tap_index + row_count]
        valid_rows = (positions >= CONV - 1 - tap_index)[:, None]
        conv_total = conv_total + jnp.where(valid_rows, window, 0.0) * conv_weight[tap_index][None, :]
    return jax.nn.silu(conv_total)

def split_conv(conv_values):
    ssm_inner = SSM_HEADS * SSM_DIM
    x_ssm = conv_values[:, :ssm_inner].reshape(conv_values.shape[0], SSM_HEADS, SSM_DIM)
    return (x_ssm, conv_values[:, ssm_inner:ssm_inner + STATE], conv_values[:, ssm_inner + STATE:])

def ssd_entry(cumul, seq_id, positions):
    carried = (seq_id == seq_id[0]) & (positions[0] > 0)
    return jnp.where(carried[:, None], jnp.exp(cumul), 0.0)

def ssd_output(x_ssm, b_in, c_in, step_size, decay, skip_gain, seq_id, positions, state_in):
    row_count = seq_id.shape[0]
    cumul = jnp.cumsum(step_size * decay[None, :], axis=0)
    order_rows = jnp.arange(row_count)
    visible = (seq_id[:, None] == seq_id[None, :]) & (order_rows[:, None] >= order_rows[None, :])
    log_gaps = cumul.T[:, :, None] - cumul.T[:, None, :]
    kernel = jnp.exp(jnp.where(visible[None], log_gaps, masked_score))
    inner_products = jnp.dot(c_in, b_in.T, precision=highest)
    scaled_x = x_ssm * step_size[:, :, None]
    intra_part = jnp.einsum('hts,shp->thp', kernel * inner_products[None], scaled_x, precision=highest)
    entry_decay = ssd_entry(cumul, seq_id, positions)
    from_state = jnp.einsum('hpn,tn->thp', state_in, c_in, precision=highest) * entry_decay[:, :, None]
    return intra_part + from_state + skip_gain[None, :, None] * x_ssm

def ssd_summary(x_ssm, b_in, step_size, decay, seq_id, positions):
    cumul = jnp.cumsum(step_size * decay[None, :], axis=0)
    carried_last = (seq_id[-1] == seq_id[0]) & (positions[0] > 0)
    carry_all = jnp.where(carried_last, jnp.exp(cumul[-1]), 0.0)
    tail_decay = jnp.exp(jnp.where((seq_id == seq_id[-1])[:, None], cumul[-1:] - cumul, masked_score))
    local_state = jnp.einsum('sh,shp,sn->hpn', tail_decay, x_ssm * step_size[:, :, None], b_in, precision=highest)
    return (carry_all, local_state)

def ssd_group(x_ssm, b_in, c_in, step_size, decay, skip_gain, seq_id, positions):
    row_count = seq_id.shape[0]
    blocks = row_count // TOK_DEV

    def one_step(state_in, pieces):
        x_block, b_block, c_block, step_block, seq_block, pos_block = pieces
        output = ssd_output(x_block, b_block, c_block, step_block, decay, skip_gain, seq_block, pos_block, state_in)
        carry_all, local_state = ssd_summary(x_block, b_block, step_block, decay, seq_block, pos_block)
        return (carry_all[:, None, None] * state_in + local_state, output)

    def split_blocks(array):
        return array.reshape((blocks, TOK_DEV) + array.shape[1:])
    initial = jnp.zeros((SSM_HEADS, SSM_DIM, STATE), jnp.float32)
    pieces = tuple((split_blocks(array) for array in (x_ssm, b_in, c_in, step_size, seq_id, positions)))
    _, outputs = lax.scan(jax.checkpoint(one_step), initial, pieces)
    return outputs.reshape(row_count, SSM_HEADS * SSM_DIM)

def attention(q_rot, k_rot, value_low, row_index, seq_id):
    row_count = row_index.shape[0]
    block_rows = math.gcd(row_count, 512)
    group_ratio = HEADS_Q // HEADS_KV
    key_heads = k_rot.reshape(row_count, HEADS_KV, HEAD_DIM)
    value_heads = value_low.reshape(row_count, HEADS_KV, HEAD_DIM)
    score_scale = HEAD_DIM ** (-0.5)

    def one_block(pieces):
        q_block, row_block, seq_block = pieces
        q_heads = q_block.reshape(block_rows, HEADS_KV, group_ratio, HEAD_DIM)
        scores = low_back(jnp.einsum('tgjd,kgd->gjtk', q_heads, key_heads, precision=highest) * score_scale)
        visible = (seq_block[:, None] == seq_id[None, :]) & (row_index[None, :] <= row_block[:, None])
        probs = jax.nn.softmax(jnp.where(visible[None, None], scores, masked_score), axis=-1)
        mixed_values = jnp.einsum('gjtk,kgd->tgjd', low(probs), value_heads, precision=highest)
        return mixed_values.reshape(block_rows, HEADS_Q * HEAD_DIM)
    outputs = lax.map(jax.checkpoint(one_block), (q_rot.reshape(row_count // block_rows, block_rows, -1), row_index.reshape(-1, block_rows), seq_id.reshape(-1, block_rows)))
    return outputs.reshape(row_count, HEADS_Q * HEAD_DIM)

def group_forward(weights, x_rows, bounds):
    row_index = jnp.arange(x_rows.shape[0], dtype=jnp.int32)
    seq_id, positions = sequence_info(row_index, bounds)
    cosine, sine = rotary_tables(positions)
    hidden = low(rms_norm(x_rows, weights['norm_attn']))
    query = low_back(product(hidden, weights['w_query']))
    key_raw = low_back(product(hidden, weights['w_key']))
    value_low = low(low_back(product(hidden, weights['w_value'])))
    q_rot = low(rotate(query, cosine, sine, HEADS_Q))
    k_rot = low(rotate(key_raw, cosine, sine, HEADS_KV))
    attended = low(low_back(attention(q_rot, k_rot, value_low, row_index, seq_id)))
    attn_out = low_back(product(attended, weights['w_attn_out']))
    gate_ssm = low_back(product(hidden, weights['w_gate_ssm']))
    xbc = low_back(jnp.concatenate([product(hidden, weights['w_x_ssm']), product(hidden, weights['w_b_c'])], axis=1))
    step_raw = low_back(product(hidden, weights['w_step']))
    extended = jnp.concatenate([jnp.zeros((CONV - 1, xbc.shape[1]), jnp.float32), xbc], axis=0)
    conv_values = conv_apply(extended, weights['conv_weight'], weights['conv_bias'], positions)
    x_ssm, b_in, c_in = split_conv(conv_values)
    step_size = jax.nn.softplus(step_raw + weights['step_bias'][None, :])
    decay = -jnp.exp(weights['decay_log'])
    ssm_y = ssd_group(x_ssm, b_in, c_in, step_size, decay, weights['skip_gain'], seq_id, positions)
    ssm_low = low(gated_norm(ssm_y, gate_ssm, weights['norm_ssm']))
    ssm_out = low_back(product(ssm_low, weights['w_ssm_out']))
    middle = x_rows + attn_out + ssm_out
    hidden_two = low(rms_norm(middle, weights['norm_ffn']))
    gate_ffn = low_back(product(hidden_two, weights['w_gate']))
    upper = low_back(product(hidden_two, weights['w_up_proj']))
    activation = low(jax.nn.silu(gate_ffn) * upper)
    ffn_out = product(activation, weights['w_down'])
    result = middle + ffn_out
    squares = jnp.stack([jnp.sum(result * result), jnp.sum(attn_out * attn_out), jnp.sum(ssm_out * ssm_out), jnp.sum(ffn_out * ffn_out)])
    return (result, squares)

def reference(tokens, params, cotangent, offsets):
    x_all = tokens.astype(jnp.float32).reshape(N_GROUP, GROUP_TOK, D)
    flat_vector = params.astype(jnp.float32)

    def whole(x_groups, flat_now):
        weights = unpack(flat_now)

        def per_group(pieces):
            return group_forward(weights, pieces[0], pieces[1])
        result, squares = lax.map(per_group, (x_groups, offsets))
        return (result, squares)
    result, pullback, squares = jax.vjp(whole, x_all, flat_vector, has_aux=True)
    grad_x, grad_flat = pullback(cotangent.astype(jnp.float32).reshape(N_GROUP, GROUP_TOK, D))
    stats = jnp.sqrt(lax.optimization_barrier(jnp.sum(squares, axis=0)) / (TOKENS * D))
    return (result.reshape(TOKENS, D).astype(jnp.bfloat16), grad_x.reshape(TOKENS, D), grad_flat, stats)
```

```python
import math

import jax
import jax.numpy as jnp
import numpy as np
from jax import lax
from jax.experimental import pallas as pl
from jax.experimental.pallas import tpu as pltpu
from jax.sharding import Mesh, PartitionSpec as P

D = 1024
HEADS_Q = 8
HEADS_KV = 2
HEAD_DIM = 64
SSM_HEADS = 24
SSM_DIM = 64
STATE = 128
CONV = 4
FF = 2048
(
    NORM_ATTN,
    W_QUERY,
    W_KEY,
    W_VALUE,
    W_ATTN_OUT,
    W_GATE_SSM,
    W_X_SSM,
    W_B_C,
    W_STEP,
    CONV_WEIGHT,
    CONV_BIAS,
    STEP_BIAS,
    DECAY_LOG,
    SKIP_GAIN,
    NORM_SSM,
    W_SSM_OUT,
    NORM_FFN,
    W_GATE,
    W_UP_PROJ,
    W_DOWN,
) = range(20)


epsilon = 1e-05
rope_base = 100000000000.0
masked_score = -1e30
highest = lax.Precision.HIGHEST
small_names = (
    NORM_ATTN,
    CONV_WEIGHT,
    CONV_BIAS,
    STEP_BIAS,
    DECAY_LOG,
    SKIP_GAIN,
    NORM_SSM,
    NORM_FFN,
)


def passed_along(value, axis, steps):
    count = lax.axis_size(axis)
    first, last = (max(0, -steps), min(count, count - steps))
    return lax.ppermute(value, axis, [(source, source + steps) for source in range(first, last)])


def prefix(value, axis, combine, identity):
    peers, place = (lax.axis_size(axis), lax.axis_index(axis))
    everything = jax.tree.map(
        lambda part, kind: lax.all_gather(part.astype(kind), axis),
        value,
        (jnp.bfloat16, jnp.bfloat16),
    )
    start = jax.tree.map(
        lambda part, zero: jnp.broadcast_to(jnp.asarray(zero, part.dtype), part.shape),
        value,
        identity,
    )

    def prefix_turn(k, before):
        reached = k < place
        new = combine(
            before, jax.tree.map(lambda part, own: part[k].astype(own.dtype), everything, value)
        )
        return jax.tree.map(lambda a, b: jnp.where(reached, a, b), new, before)

    return lax.fori_loop(0, peers, prefix_turn, start)


def carried_in(value, axis, combine, identity):
    peers, place = (lax.axis_size(axis), lax.axis_index(axis))
    everything = jax.tree.map(
        lambda part, kind: lax.all_gather(part.astype(kind), axis),
        value,
        jax.tree.map(lambda a: jnp.bfloat16 if a.dtype == jnp.float32 else a.dtype, value),
    )
    start = jax.tree.map(
        lambda part, zero: jnp.broadcast_to(jnp.asarray(zero, part.dtype), part.shape),
        value,
        identity,
    )

    def carried_turn(k, before):
        at = peers - 1 - k
        reached = at > place
        new = combine(
            before, jax.tree.map(lambda part, own: part[at].astype(own.dtype), everything, value)
        )
        return jax.tree.map(lambda a, b: jnp.where(reached, a, b), new, before)

    return lax.fori_loop(0, peers, carried_turn, start)


def layout():
    ssm_inner = SSM_HEADS * SSM_DIM
    channels = ssm_inner + 2 * STATE
    return [
        (NORM_ATTN, (D,)),
        (W_QUERY, (D, HEADS_Q * HEAD_DIM)),
        (W_KEY, (D, HEADS_KV * HEAD_DIM)),
        (W_VALUE, (D, HEADS_KV * HEAD_DIM)),
        (W_ATTN_OUT, (HEADS_Q * HEAD_DIM, D)),
        (W_GATE_SSM, (D, ssm_inner)),
        (W_X_SSM, (D, ssm_inner)),
        (W_B_C, (D, 2 * STATE)),
        (W_STEP, (D, SSM_HEADS)),
        (CONV_WEIGHT, (CONV, channels)),
        (CONV_BIAS, (channels,)),
        (STEP_BIAS, (SSM_HEADS,)),
        (DECAY_LOG, (SSM_HEADS,)),
        (SKIP_GAIN, (SSM_HEADS,)),
        (NORM_SSM, (ssm_inner,)),
        (W_SSM_OUT, (ssm_inner, D)),
        (NORM_FFN, (D,)),
        (W_GATE, (D, FF)),
        (W_UP_PROJ, (D, FF)),
        (W_DOWN, (FF, D)),
    ]


def unpack(flat_vector):
    unpacked = {}
    offset = 0
    for name_key, extent in layout():
        amount = math.prod(extent)
        unpacked[name_key] = flat_vector[offset : offset + amount].reshape(extent)
        offset += amount
    return unpacked


def matmul(left, right):
    return jnp.dot(left, right, preferred_element_type=jnp.float32)


def matmul_left_t(left, right):
    return lax.dot_general(
        left, right, (((0,), (0,)), ((), ())), preferred_element_type=jnp.float32
    )


def matmul_right_t(left, right):
    return lax.dot_general(
        left, right, (((1,), (1,)), ((), ())), preferred_element_type=jnp.float32
    )


def rms_norm(values, gain):
    return values * lax.rsqrt(jnp.mean(values * values, axis=-1, keepdims=True) + epsilon) * gain


def gated_norm(ssm_y, gate_ssm, gain):
    return rms_norm(ssm_y * jax.nn.silu(gate_ssm), gain)


def swiglu(gate_ffn, upper):
    return jax.nn.silu(gate_ffn) * upper


def sequence_info(row_index, bounds):
    starts = bounds[:-1]
    inside = row_index[:, None] >= starts[None, :]
    seq_id = jnp.sum(inside.astype(jnp.int32), axis=1) - 1
    seq_start = jnp.max(jnp.where(inside, starts[None, :], 0), axis=1)
    return (seq_id, row_index - seq_start)


def rotary_tables(positions):
    half_dim = HEAD_DIM // 2
    freqs = jnp.exp(
        -jnp.arange(half_dim, dtype=jnp.float32) * (2.0 * math.log(rope_base) / HEAD_DIM)
    )
    angles = positions.astype(jnp.float32)[:, None] * freqs[None, :]
    return (jnp.cos(angles), jnp.sin(angles))


def rotate(values, cosine, sine, heads):
    row_count = values.shape[0]
    half_dim = HEAD_DIM // 2
    split_heads = values.reshape(row_count, heads, HEAD_DIM)
    first_half = split_heads[..., :half_dim]
    second_half = split_heads[..., half_dim:]
    cos_b = cosine[:, None, :]
    sin_b = sine[:, None, :]
    turned = jnp.concatenate(
        [first_half * cos_b - second_half * sin_b, second_half * cos_b + first_half * sin_b],
        axis=-1,
    )
    return turned.reshape(row_count, heads * HEAD_DIM)


def conv_apply(extended, conv_weight, conv_bias, positions):
    row_count = positions.shape[0]
    conv_total = conv_bias[None, :]
    for tap_index in range(CONV):
        window = extended[tap_index : tap_index + row_count]
        valid_rows = (positions >= CONV - 1 - tap_index)[:, None]
        conv_total = (
            conv_total + jnp.where(valid_rows, window, 0.0) * conv_weight[tap_index][None, :]
        )
    return jax.nn.silu(conv_total)


def split_conv(conv_values):
    ssm_inner = SSM_HEADS * SSM_DIM
    x_ssm = conv_values[:, :ssm_inner].reshape(conv_values.shape[0], SSM_HEADS, SSM_DIM)
    return (
        x_ssm,
        conv_values[:, ssm_inner : ssm_inner + STATE],
        conv_values[:, ssm_inner + STATE :],
    )


def ssd_entry(cumul, seq_id, positions):
    carried = (seq_id == seq_id[0]) & (positions[0] > 0)
    return jnp.where(carried[:, None], jnp.exp(cumul), 0.0)


def ssd_output(x_ssm, b_in, c_in, step_size, decay, skip_gain, seq_id, positions, state_in):
    row_count = seq_id.shape[0]
    cumul = jnp.cumsum(step_size * decay[None, :], axis=0)
    order_rows = jnp.arange(row_count)
    visible = (seq_id[:, None] == seq_id[None, :]) & (order_rows[:, None] >= order_rows[None, :])
    log_gaps = cumul.T[:, :, None] - cumul.T[:, None, :]
    kernel = jnp.exp(jnp.where(visible[None], log_gaps, masked_score))
    inner_products = jnp.dot(c_in, b_in.T, precision=highest)
    scaled_x = x_ssm * step_size[:, :, None]
    intra_part = jnp.einsum(
        "hts,shp->thp", kernel * inner_products[None], scaled_x, precision=highest
    )
    entry_decay = ssd_entry(cumul, seq_id, positions)
    from_state = (
        jnp.einsum("hpn,tn->thp", state_in, c_in, precision=highest) * entry_decay[:, :, None]
    )
    return intra_part + from_state + skip_gain[None, :, None] * x_ssm


def ssd_summary(x_ssm, b_in, step_size, decay, seq_id, positions):
    cumul = jnp.cumsum(step_size * decay[None, :], axis=0)
    carried_last = (seq_id[-1] == seq_id[0]) & (positions[0] > 0)
    carry_all = jnp.where(carried_last, jnp.exp(cumul[-1]), 0.0)
    tail_decay = jnp.exp(
        jnp.where((seq_id == seq_id[-1])[:, None], cumul[-1:] - cumul, masked_score)
    )
    local_state = jnp.einsum(
        "sh,shp,sn->hpn", tail_decay, x_ssm * step_size[:, :, None], b_in, precision=highest
    )
    return (carry_all, local_state)


def chain_states(earlier, later):
    return (earlier[0] * later[0], earlier[1] * later[0][:, None, None] + later[1])


def add_rows(target, addend, first_row):
    current = lax.dynamic_slice_in_dim(target, first_row, addend.shape[0], 0)
    return lax.dynamic_update_slice_in_dim(target, current + addend, first_row, 0)


FAST = (4, 8)
LINE = 128
SHARD = 3082
SPAD = 3088
WIN = 3104
PLANE = 8 * SHARD
DEPTH = 4
TALL = {1: 1024, 2: 1024, 4: 512, 8: 256, 12: 128, 16: 128}
GRID = ("z", "y", "x", "c")
ZC = ("z", "c")
SWAP = [(0, 1), (1, 0)]


def zc_pairs(*pairs):
    return [(2 * a + c, 2 * b + c) for a, b, c in pairs]


def gather_lines(params):
    z, y, x, c = (lax.axis_index(name) for name in GRID)
    lines = jnp.pad(params.reshape(SHARD, LINE), ((0, SPAD - SHARD), (0, 0)))
    sibling = lax.ppermute(lines, ZC, [(2 * k + 1 - k % 2, 2 * k + k % 2) for k in range(4)])
    batches = []
    for batch in range(2):
        buffers = []
        for part in range(2):
            here = jnp.where(c == part, lines, sibling)
            if batch == 0:
                one = lax.ppermute(here, ZC, zc_pairs((0, 1, 0), (1, 2, 1)))
                side = lax.ppermute(here, ZC, zc_pairs((1, 0, 1)))
                two = lax.ppermute(one, ZC, zc_pairs((1, 2, 0), (2, 3, 1)))
                three = lax.ppermute(two, ZC, zc_pairs((2, 3, 0)))
            else:
                one = lax.ppermute(here, ZC, zc_pairs((2, 1, 0), (3, 2, 1)))
                side = lax.ppermute(here, ZC, zc_pairs((2, 3, 0)))
                two = lax.ppermute(one, ZC, zc_pairs((1, 0, 0), (2, 1, 1)))
                three = lax.ppermute(two, ZC, zc_pairs((1, 0, 1)))
            mine = z == 2 * batch + c
            column = jnp.where(mine, here, one + side + two + three)
            over_x = lax.ppermute(column, "x", SWAP)
            over_y = lax.ppermute(column, "y", SWAP)
            if part == 0:
                corner = lax.ppermute(over_x, "y", SWAP)
            else:
                corner = lax.ppermute(over_y, "x", SWAP)
            local = [column, over_x, over_y, corner]
            buffers += local + [lax.ppermute(piece, "c", SWAP) for piece in local]
        batches.append(buffers)
    shard = np.arange(32)
    sz, sy, sx, sc = shard // 8, shard // 4 % 2, shard // 2 % 2, shard % 2
    away = jnp.where(sz % 2 == c, 0, 4)
    where = sc * 8 + away + 2 * (sy ^ y) + (sx ^ x) + 16 * (sz // 2)
    return batches, where.astype(jnp.int32)


def unpack_lines(buffers, first, where, segments):
    jobs, starts = [], []
    reach = 0
    for offset, rows, columns in segments:
        per_row = columns // LINE
        lane, base = offset % LINE, offset // LINE
        if per_row == 1 and rows < 1024:
            lane, tall = 0, rows
        else:
            tall = TALL[per_row]
        starts.append(len(jobs))
        for k in range(rows // tall):
            jobs.append((base + k * tall * per_row, tall * per_row, 1 if lane else 0))
    window = max(job[1] for job in jobs) + 32
    table = np.zeros((len(jobs), 5), np.int32)
    for k, (line, count, extra) in enumerate(jobs):
        owner = line // SHARD
        inside = line - owner * SHARD
        begin = min(inside // 16 * 16, SPAD - window)
        crosses = int(line + count + extra > (owner + 1) * SHARD)
        table[k] = (owner, begin, begin - inside, crosses, (owner + 1) * SHARD - line)
    base_row = (int(-table[:, 2].min()) + 7) // 8 * 8
    table[:, 2] += base_row
    table[:, 4] += base_row
    room = int(max((table[:, 2] + window).max(), ((table[:, 4] + window) * table[:, 3]).max()))
    room = (room + 15) // 8 * 8
    total = len(jobs)
    count_buffers = len(buffers)
    shapes = []
    for offset, rows, columns in segments:
        per_row = columns // LINE
        tall = rows if per_row == 1 and rows < 1024 else TALL[per_row]
        shapes.append((rows, columns, tall, per_row, offset % LINE if tall != rows or per_row != 1 else 0))
    sizes = sorted({(tall, columns) for _, columns, tall, _, _ in shapes})

    def kernel(table_ref, where_ref, *refs):
        sources = refs[:count_buffers]
        outs = refs[count_buffers : count_buffers + len(segments)]
        rest = refs[count_buffers + len(segments) :]
        stages = dict(zip(sizes, rest))
        raw, flat, in_sem, out_sem = rest[len(sizes) :]
        step = pl.program_id(0)

        def fetch(job, slot):
            owner = table_ref[job, 0]
            begin = pl.multiple_of(table_ref[job, 1], 16)
            for b in range(count_buffers):

                @pl.when(where_ref[owner] == first + b)
                def _():
                    pltpu.make_async_copy(
                        sources[b].at[pl.ds(begin, window), :], raw.at[slot, 0], in_sem.at[slot, 0]
                    ).start()

            @pl.when(table_ref[job, 3] == 1)
            def _():
                for b in range(count_buffers):

                    @pl.when(where_ref[owner + 1] == first + b)
                    def _():
                        pltpu.make_async_copy(
                            sources[b].at[pl.ds(0, window), :], raw.at[slot, 1], in_sem.at[slot, 1]
                        ).start()

        def fetched(slot, half):
            return pltpu.make_async_copy(
                sources[0].at[pl.ds(0, window), :], raw.at[slot, half], in_sem.at[slot, half]
            )

        @pl.when(step == 0)
        def _():
            for k in range(min(DEPTH - 1, total)):
                fetch(k, k)

        @pl.when(step + DEPTH - 1 < total)
        def _():
            fetch(step + DEPTH - 1, lax.rem(step + DEPTH - 1, DEPTH))

        slot = lax.rem(step, DEPTH)
        fetched(slot, 0).wait()
        flat[pl.ds(table_ref[step, 2], window), :] = raw[slot, 0].astype(jnp.float32)

        @pl.when(table_ref[step, 3] == 1)
        def _():
            fetched(slot, 1).wait()
            flat[pl.ds(table_ref[step, 4], window), :] = raw[slot, 1].astype(jnp.float32)

        for index, (rows, columns, tall, per_row, lane) in enumerate(shapes):
            begin = starts[index]
            blocks = rows // tall
            stage = stages[(tall, columns)]

            @pl.when((step >= begin) & (step < begin + blocks))
            def _():
                block = step - begin
                side = lax.rem(block, 2)

                def written(k, s):
                    return pltpu.make_async_copy(
                        stage.at[s],
                        outs[index].at[pl.ds(pl.multiple_of(k * tall, 16), tall), :],
                        out_sem.at[s],
                    )

                @pl.when(block >= 2)
                def _():
                    written(block - 2, side).wait()

                def tile(j):
                    picked = flat[pl.ds(base_row + j, tall, stride=per_row), :]
                    return pltpu.roll(picked, LINE - lane, 1) if lane else picked

                if lane:
                    lanes = lax.broadcasted_iota(jnp.int32, (tall, LINE), 1)
                    now = tile(0)
                    for j in range(per_row):
                        later = tile(j + 1)
                        stage[side, :, j * LINE : (j + 1) * LINE] = jnp.where(
                            lanes < LINE - lane, now, later
                        ).astype(jnp.bfloat16)
                        now = later
                else:
                    for j in range(per_row):
                        stage[side, :, j * LINE : (j + 1) * LINE] = tile(j).astype(jnp.bfloat16)
                written(block, side).start()

                @pl.when(block == blocks - 1)
                def _():
                    if blocks > 1:
                        written(block - 1, 1 - side).wait()
                    written(block, side).wait()

    return pl.pallas_call(
        kernel,
        grid_spec=pltpu.PrefetchScalarGridSpec(
            num_scalar_prefetch=2,
            grid=(total,),
            in_specs=[pl.BlockSpec(memory_space=pl.ANY)] * count_buffers,
            out_specs=[pl.BlockSpec(memory_space=pl.ANY)] * len(segments),
            scratch_shapes=[pltpu.VMEM((2,) + size, jnp.bfloat16) for size in sizes]
            + [
                pltpu.VMEM((DEPTH, 2, window, LINE), jnp.bfloat16),
                pltpu.VMEM((room, LINE), jnp.float32),
                pltpu.SemaphoreType.DMA((DEPTH, 2)),
                pltpu.SemaphoreType.DMA((2,)),
            ],
        ),
        out_shape=[jax.ShapeDtypeStruct((rows, columns), jnp.bfloat16) for _, rows, columns in segments],
        compiler_params=pltpu.CompilerParams(vmem_limit_bytes=48 * 2**20),
        cost_estimate=pl.CostEstimate(flops=0, bytes_accessed=total * window * LINE * 4, transcendentals=0),
        name="unpack",
    )(jnp.asarray(table), where, *buffers)


def pack_lines(target, target_rows, first_row, segments, lane, phase, extras, carry, tail_rows):
    tall = 256
    lefts, rights, plan = [], [], []
    left_of, right_of = {}, {}
    row = first_row
    begin = 0
    for left, right in segments:
        for value, seen, kept in ((left, left_of, lefts), (right, right_of, rights)):
            if id(value) not in seen:
                seen[id(value)] = len(kept)
                kept.append(value)
        blocks = left.shape[1] // tall
        plan.append((left_of[id(left)], right_of[id(right)], right.shape[1] // LINE, begin, blocks, row))
        begin += blocks
        row += left.shape[1] * right.shape[1] // LINE
    end_row = row
    total = begin
    biggest = max(entry[2] for entry in plan) * tall
    tokens = lefts[0].shape[0]
    count_left, count_right, count_extra = len(lefts), len(rights), len(extras)
    rolled = [jnp.roll(right, lane, axis=1) if lane else right for right in rights]
    carry_in = [carry] if lane else []
    targets = [] if target is None else [target]

    def left_spec(index):
        mine = [entry for entry in plan if entry[0] == index]

        def place(step):
            block = 0
            for _, _, _, start, blocks, _ in mine:
                block = jnp.where(step >= start, jnp.minimum(step - start, blocks - 1), block)
            return (0, block)

        return pl.BlockSpec((tokens, tall), place)

    def kernel(*refs):
        left_refs = refs[:count_left]
        right_refs = refs[count_left : count_left + count_right]
        at = count_left + count_right
        extra_refs = refs[at : at + count_extra]
        at += count_extra
        carry_refs = refs[at : at + len(carry_in)]
        at += len(carry_in) + len(targets)
        out = refs[at]
        flat, stage, shift, last, sems, extra_sems = refs[at + 1 :]
        step = pl.program_id(0)
        side = lax.rem(step, 2)

        def extra_copy(k):
            rows = extras[k][0].shape[0]
            return pltpu.make_async_copy(
                extra_refs[k], out.at[pl.ds(extras[k][1], rows), :], extra_sems.at[k]
            )

        @pl.when(step == 0)
        def _():
            for k in range(count_extra):
                extra_copy(k).start()
            if lane:
                shift[0:8, :] = carry_refs[0][...]
            if phase:
                flat[0:8, :] = jnp.zeros((8, LINE), jnp.float32)

        for left_at, right_at, per_row, start, blocks, row in plan:
            lines = per_row * tall

            def written(block, s, row=row, lines=lines):
                return pltpu.make_async_copy(
                    stage.at[s, pl.ds(0, lines), :],
                    out.at[pl.ds(pl.multiple_of(row + block * lines, 16), lines), :],
                    sems.at[s],
                )

            @pl.when((step >= start) & (step < start + blocks))
            def _():
                block = step - start
                if phase:

                    @pl.when(step > 0)
                    def _():
                        flat[0:8, :] = flat[lines : lines + 8, :]

                turned = left_refs[left_at][...].T
                lanes = lax.broadcasted_iota(jnp.int32, (tall, LINE), 1)
                for j0 in range(0, per_row, 2):
                    wide = min(2, per_row - j0)
                    tile = jnp.dot(
                        turned,
                        right_refs[right_at][:, j0 * LINE : (j0 + wide) * LINE],
                        preferred_element_type=jnp.float32,
                    )
                    for j in range(wide):
                        piece = tile[:, j * LINE : (j + 1) * LINE]
                        if lane and j0 + j == 0:
                            shift[8 : 8 + tall, :] = piece
                            piece = jnp.where(lanes < lane, shift[7 : 7 + tall, :], piece)
                            shift[0:8, :] = shift[tall : tall + 8, :]
                        if per_row == 1:
                            flat[phase : phase + tall, :] = piece
                        else:
                            flat[pl.ds(phase + j0 + j, tall, stride=per_row), :] = piece

                stage[side, 0:lines, :] = flat[0:lines, :].astype(jnp.bfloat16)
                written(block, side).start()

            @pl.when((step > start) & (step <= start + blocks))
            def _():
                written(step - start - 1, 1 - side).wait()

            if start + blocks == total:

                @pl.when(step == total - 1)
                def _():
                    written(blocks - 1, side).wait()

        @pl.when(step == total - 1)
        def _():
            if tail_rows:
                lanes = lax.broadcasted_iota(jnp.int32, (tail_rows, LINE), 1)
                rows_at = lax.broadcasted_iota(jnp.int32, (tail_rows, LINE), 0)
                final = jnp.broadcast_to(shift[7:8, :], (tail_rows, LINE))
                last[...] = jnp.where((rows_at == 0) & (lanes < lane), final, 0.0).astype(jnp.bfloat16)
                closing = pltpu.make_async_copy(
                    last, out.at[pl.ds(end_row, tail_rows), :], extra_sems.at[count_extra]
                )
                closing.start()
                closing.wait()
            for k in range(count_extra):
                extra_copy(k).wait()

    whole = [pl.BlockSpec(array.shape, lambda step: (0, 0)) for array in rolled]
    flops = sum(2 * tokens * entry[4] * tall * entry[2] * LINE for entry in plan)
    return pl.pallas_call(
        kernel,
        grid=(total,),
        in_specs=[left_spec(k) for k in range(count_left)]
        + whole
        + [pl.BlockSpec(array.shape, lambda step: (0, 0)) for array, _ in extras]
        + [pl.BlockSpec(array.shape, lambda step: (0, 0)) for array in carry_in]
        + [pl.BlockSpec(memory_space=pl.ANY)] * len(targets),
        out_specs=pl.BlockSpec(memory_space=pl.ANY),
        out_shape=jax.ShapeDtypeStruct((target_rows, LINE), jnp.bfloat16),
        scratch_shapes=[
            pltpu.VMEM((biggest + 16, LINE), jnp.float32),
            pltpu.VMEM((2, biggest, LINE), jnp.bfloat16),
            pltpu.VMEM((tall + 8, LINE), jnp.float32),
            pltpu.VMEM((max(tail_rows, 16), LINE), jnp.bfloat16),
            pltpu.SemaphoreType.DMA((2,)),
            pltpu.SemaphoreType.DMA((count_extra + 1,)),
        ],
        input_output_aliases={count_left + count_right + count_extra + len(carry_in): 0} if targets else {},
        compiler_params=pltpu.CompilerParams(vmem_limit_bytes=48 * 2**20),
        cost_estimate=pl.CostEstimate(flops=flops, bytes_accessed=total * biggest * LINE * 2, transcendentals=0),
        name="pack",
    )(*lefts, *rolled, *[array for array, _ in extras], *carry_in, *targets)


def added(*parts):
    total = parts[0].astype(jnp.float32)
    for part in parts[1:]:
        total = total + part.astype(jnp.float32)
    return total.astype(jnp.bfloat16)


def reduce_lines(flat, batch, shift):
    z, y, x, c = (lax.axis_index(name) for name in GRID)
    length = PLANE + 32
    keep = lax.dynamic_slice(flat, (c * PLANE, 0), (length, LINE))
    send = lax.dynamic_slice(flat, ((1 - c) * PLANE, 0), (length, LINE))
    chip = added(keep, lax.ppermute(send, "c", SWAP))

    def window(sy, sx, part):
        shard = sy * 4 + sx * 2 + part
        start = (shift + SHARD * shard) // 16 * 16
        return lax.dynamic_slice(chip, (start, 0), (WIN, LINE))

    ends = []
    for part in range(2):
        if part == 0:
            away = jnp.stack([window(1 - y, 0, part), window(1 - y, 1, part)])
            home = jnp.stack([window(y, 0, part), window(y, 1, part)])
            first_axis, second_axis, place = "y", "x", x
        else:
            away = jnp.stack([window(0, 1 - x, part), window(1, 1 - x, part)])
            home = jnp.stack([window(0, x, part), window(1, x, part)])
            first_axis, second_axis, place = "x", "y", y
        half = added(home, lax.ppermute(away, first_axis, SWAP))
        other = lax.dynamic_index_in_dim(half, 1 - place, 0, keepdims=False)
        mine = lax.dynamic_index_in_dim(half, place, 0, keepdims=False)
        column = added(mine, lax.ppermute(other, second_axis, SWAP))
        if batch == 0:
            one = added(column, lax.ppermute(column, ZC, zc_pairs((3, 2, 0), (3, 2, 1))))
            side = lax.ppermute(column, ZC, zc_pairs((0, 1, 1)))
            two = added(one, lax.ppermute(one, ZC, zc_pairs((2, 1, 0), (2, 1, 1))), side)
            end = added(two, lax.ppermute(two, ZC, zc_pairs((1, 0, 0))))
        else:
            one = added(column, lax.ppermute(column, ZC, zc_pairs((0, 1, 0), (0, 1, 1))))
            side = lax.ppermute(column, ZC, zc_pairs((3, 2, 0)))
            two = added(one, lax.ppermute(one, ZC, zc_pairs((1, 2, 0), (1, 2, 1))), side)
            end = added(two, lax.ppermute(two, ZC, zc_pairs((2, 3, 1))))
        ends.append(end)
    mine = jnp.where(c == 0, ends[0], ends[1])
    other = jnp.where(c == 0, ends[1], ends[0])
    holders = [(2 * k + k % 2, 2 * k + 1 - k % 2) for k in range(4)]
    handed = lax.ppermute(other, ZC, holders)
    return jnp.where(c == z % 2, mine, handed)


def offsets_of():
    places, at = {}, 0
    for name_key, extent in layout():
        places[name_key] = (at, extent)
        at += math.prod(extent)
    return places


def fast_weights(params):
    places = offsets_of()
    (early, late), where = gather_lines(params)
    early_names = (W_QUERY, W_KEY, W_VALUE, W_ATTN_OUT, W_GATE_SSM, W_X_SSM, W_B_C)
    late_names = (W_SSM_OUT, W_GATE, W_UP_PROJ, W_DOWN)

    def segment(name_key):
        at, extent = places[name_key]
        return (at, extent[0], extent[1])

    misc_at = places[W_STEP][0]
    first = unpack_lines(
        early, 0, where,
        [segment(name_key) for name_key in early_names] + [(0, 16, LINE), (misc_at, 288, LINE)],
    )
    second = unpack_lines(
        early + late, 0, where,
        [segment(name_key) for name_key in late_names] + [(places[NORM_FFN][0], 16, LINE)],
    )
    weights = dict(zip(early_names, first))
    weights.update(zip(late_names, second))
    weights[NORM_ATTN] = first[-2].reshape(-1)[:D]
    misc = first[-1].reshape(-1)
    for name_key in (W_STEP,) + small_names[1:-1]:
        at, extent = places[name_key]
        weights[name_key] = misc[at - misc_at : at - misc_at + math.prod(extent)].reshape(extent)
    lane = places[NORM_FFN][0] % LINE
    weights[NORM_FFN] = second[-1].reshape(-1)[lane : lane + D]
    return weights


def fast_gradients(small, pairs):
    places = offsets_of()
    z, y, x, c = (lax.axis_index(name) for name in GRID)
    ssm_low, grad_branch = pairs[W_SSM_OUT]
    out_at = places[W_SSM_OUT][0]
    lane = places[W_GATE][0] % LINE
    boundary = 2 * PLANE * LINE
    tail_from = (boundary - out_at) // D
    tail = matmul_left_t(ssm_low[:, tail_from:], grad_branch).reshape(-1)
    tail = tail[boundary - out_at - tail_from * D :]
    head = jnp.concatenate([jnp.zeros((14 * LINE,), jnp.float32), tail, small[NORM_FFN]])
    head_rows = head.shape[0] // LINE
    carry = jnp.zeros((8, LINE), jnp.float32).at[7, :lane].set(head[head_rows * LINE :])
    head = head[: head_rows * LINE].reshape(head_rows, LINE).astype(jnp.bfloat16)
    length = 2 * PLANE + 32
    late = pack_lines(
        None, length, head_rows,
        [pairs[W_GATE], pairs[W_UP_PROJ], pairs[W_DOWN]],
        lane, 0, [(head, 0)], carry, 48,
    )
    late_sum = reduce_lines(late, 1, 14)
    first_row = (8 + out_at // LINE) // 16 * 16
    early_rows = first_row + SSM_HEADS * SSM_DIM * D // LINE
    early = pack_lines(
        None, early_rows, first_row, [pairs[W_SSM_OUT]],
        lane, (8 + out_at // LINE) % 8, [], jnp.zeros((8, LINE), jnp.float32), 0,
    )
    names = (W_STEP,) + small_names[1:-1]
    misc = [small[name_key].reshape(-1) for name_key in names]
    count = sum(part.shape[0] for part in misc)
    misc_rows = (count // LINE + 16) // 16 * 16
    opening = matmul_left_t(ssm_low[:, :16], grad_branch).reshape(-1)
    misc = jnp.concatenate(misc + [opening[: misc_rows * LINE - count]])
    misc = misc.reshape(misc_rows, LINE).astype(jnp.bfloat16)
    first = jnp.concatenate([jnp.zeros((8 * LINE,), jnp.float32), small[NORM_ATTN]])
    first = first.reshape(16, LINE).astype(jnp.bfloat16)
    early = pack_lines(
        early, early_rows, 16,
        [pairs[k] for k in (W_QUERY, W_KEY, W_VALUE, W_ATTN_OUT, W_GATE_SSM, W_X_SSM, W_B_C)],
        0, 0, [(first, 0), (misc, 8 + places[W_STEP][0] // LINE)], None, 0,
    )
    early_sum = reduce_lines(early, 0, 8)
    shard = SHARD * (4 * y + 2 * x + c)
    start = jnp.where(z < 2, (8 + shard) % 16, (14 + shard) % 16)
    lines = jnp.where(z < 2, early_sum, late_sum)
    return lax.dynamic_slice(lines, (start, 0), (SHARD, LINE)).astype(jnp.float32).reshape(-1)


def body(span, group, fast, tokens, params, cotangent, offsets):
    rows_dev = tokens.shape[0]
    group_rows = rows_dev * lax.axis_size(span)
    all_rows = group_rows * lax.axis_size(group)
    group_ratio = HEADS_Q // HEADS_KV
    ssm_inner = SSM_HEADS * SSM_DIM
    score_scale = HEAD_DIM ** (-0.5)
    bounds = offsets[0]
    my_start = lax.axis_index(span) * rows_dev
    row_index = my_start + jnp.arange(rows_dev, dtype=jnp.int32)
    seq_id, positions = sequence_info(row_index, bounds)
    first_start = row_index[0] - positions[0]
    last_row = my_start + rows_dev - 1
    cosine, sine = rotary_tables(positions)
    if fast:
        weights = fast_weights(params)
    else:
        weights = unpack(lax.all_gather(params, group + span, axis=0, tiled=True))
    small_f32 = {name_key: weights[name_key].astype(jnp.float32) for name_key in small_names}
    x_rows = tokens.astype(jnp.float32)
    normed_one, norm_one_back = jax.vjp(rms_norm, x_rows, small_f32[NORM_ATTN])
    hidden = normed_one.astype(jnp.bfloat16)
    query = matmul(hidden, weights[W_QUERY])
    key_raw = matmul(hidden, weights[W_KEY])
    value_low = matmul(hidden, weights[W_VALUE]).astype(jnp.bfloat16)
    q_rot = rotate(query, cosine, sine, HEADS_Q).astype(jnp.bfloat16)
    k_rot = rotate(key_raw, cosine, sine, HEADS_KV).astype(jnp.bfloat16)
    q_heads = q_rot.reshape(rows_dev, HEADS_KV, group_ratio, HEAD_DIM)

    def block_scores(key_block, key_rows):
        scores = (
            jnp.einsum(
                "tgjd,kgd->gjtk",
                q_heads,
                key_block.reshape(-1, HEADS_KV, HEAD_DIM),
                preferred_element_type=jnp.float32,
            )
            * score_scale
        )
        key_seq, _ = sequence_info(key_rows, bounds)
        visible = (seq_id[:, None] == key_seq[None, :]) & (key_rows[None, :] <= row_index[:, None])
        return (scores, visible[None, None])

    def over_blocks(carry_now, piece_pair, step_fn):
        keys_piece, values_piece = piece_pair
        piece_rows = keys_piece.shape[0]
        block_rows = math.gcd(piece_rows, 512)
        block_count = piece_rows // block_rows

        def one_block(state_now, inputs):
            index_block, key_block, value_block = inputs
            key_start = index_block * block_rows
            needed = (key_start <= last_row) & (key_start + block_rows > first_start)

            def compute(state_in_block):
                key_rows = key_start + jnp.arange(block_rows, dtype=jnp.int32)
                return step_fn(state_in_block, key_block, value_block, key_rows, key_start)

            def unchanged(state_in_block):
                return state_in_block

            return (lax.cond(needed, compute, unchanged, state_now), None)

        carry_now, _ = lax.scan(
            one_block,
            carry_now,
            (
                jnp.arange(block_count, dtype=jnp.int32),
                keys_piece.reshape(block_count, block_rows, -1),
                values_piece.reshape(block_count, block_rows, -1),
            ),
        )
        return carry_now

    def forward_step(state_now, key_block, value_block, key_rows, key_start):
        running_max, running_sum, accum = state_now
        scores, visible = block_scores(key_block, key_rows)
        new_max = jnp.maximum(
            running_max, jnp.max(jnp.where(visible, scores, masked_score), axis=-1)
        )
        weights_p = jnp.where(visible, jnp.exp(scores - new_max[..., None]), 0.0)
        factor = jnp.exp(running_max - new_max)
        mixed_values = jnp.einsum(
            "gjtk,kgd->gjtd",
            weights_p.astype(jnp.bfloat16),
            value_block.reshape(-1, HEADS_KV, HEAD_DIM),
            preferred_element_type=jnp.float32,
        )
        return (
            new_max,
            running_sum * factor + jnp.sum(weights_p, axis=-1),
            accum * factor[..., None] + mixed_values,
        )

    head_shape = (HEADS_KV, group_ratio, rows_dev)
    initial = (
        jnp.full(head_shape, masked_score, jnp.float32),
        jnp.zeros(head_shape, jnp.float32),
        jnp.zeros(head_shape + (HEAD_DIM,), jnp.float32),
    )
    running_max, running_sum, accum = over_blocks(
        initial,
        (
            lax.all_gather(k_rot, span, axis=0, tiled=True),
            lax.all_gather(value_low, span, axis=0, tiled=True),
        ),
        forward_step,
    )
    attn_f32 = accum / running_sum[..., None]
    log_total = running_max + jnp.log(running_sum)
    attended = (
        attn_f32.transpose(2, 0, 1, 3).reshape(rows_dev, HEADS_Q * HEAD_DIM).astype(jnp.bfloat16)
    )
    attn_out = matmul(attended, weights[W_ATTN_OUT])
    gate_ssm = matmul(hidden, weights[W_GATE_SSM])
    xbc = jnp.concatenate(
        [matmul(hidden, weights[W_X_SSM]), matmul(hidden, weights[W_B_C])], axis=1
    )
    step_raw = matmul(hidden, weights[W_STEP])
    rim_rows = passed_along(xbc[rows_dev - (CONV - 1) :], span, 1)
    extended = jnp.concatenate([rim_rows, xbc], axis=0)

    def conv_local(extended_in, conv_weight, conv_bias):
        return conv_apply(extended_in, conv_weight, conv_bias, positions)

    conv_values, conv_back = jax.vjp(
        conv_local, extended, small_f32[CONV_WEIGHT], small_f32[CONV_BIAS]
    )

    def ssd_full(conv_in, step_in, step_bias, decay_log, skip_gain, state_in):
        x_ssm, b_in, c_in = split_conv(conv_in)
        step_size = jax.nn.softplus(step_in + step_bias[None, :])
        decay = -jnp.exp(decay_log)
        output = ssd_output(
            x_ssm, b_in, c_in, step_size, decay, skip_gain, seq_id, positions, state_in
        )
        carry_all, local_state = ssd_summary(x_ssm, b_in, step_size, decay, seq_id, positions)
        return (
            output.reshape(rows_dev, ssm_inner),
            carry_all[:, None, None] * state_in + local_state,
        )

    x_ssm, b_in, c_in = split_conv(conv_values)
    step_size = jax.nn.softplus(step_raw + small_f32[STEP_BIAS][None, :])
    decay = -jnp.exp(small_f32[DECAY_LOG])
    carry_all, local_state = ssd_summary(x_ssm, b_in, step_size, decay, seq_id, positions)
    state_ident = (jnp.ones_like(carry_all), jnp.zeros_like(local_state))
    _, state_in = prefix((carry_all, local_state), span, chain_states, state_ident)
    (ssm_y, _), ssd_back = jax.vjp(
        ssd_full,
        conv_values,
        step_raw,
        small_f32[STEP_BIAS],
        small_f32[DECAY_LOG],
        small_f32[SKIP_GAIN],
        state_in,
    )
    normed_ssm, gnorm_back = jax.vjp(gated_norm, ssm_y, gate_ssm, small_f32[NORM_SSM])
    ssm_low = normed_ssm.astype(jnp.bfloat16)
    ssm_out = matmul(ssm_low, weights[W_SSM_OUT])
    middle = x_rows + attn_out + ssm_out
    normed_two, norm_two_back = jax.vjp(rms_norm, middle, small_f32[NORM_FFN])
    hidden_two = normed_two.astype(jnp.bfloat16)
    gate_ffn = matmul(hidden_two, weights[W_GATE])
    upper = matmul(hidden_two, weights[W_UP_PROJ])
    activation_f32, swiglu_back = jax.vjp(swiglu, gate_ffn, upper)
    activation = activation_f32.astype(jnp.bfloat16)
    ffn_out = matmul(activation, weights[W_DOWN])
    result = middle + ffn_out
    squares = jnp.stack(
        [
            jnp.sum(result * result),
            jnp.sum(attn_out * attn_out),
            jnp.sum(ssm_out * ssm_out),
            jnp.sum(ffn_out * ffn_out),
        ]
    )
    totals = lax.psum(squares, group + span)
    stats = jnp.sqrt(totals / (all_rows * D))
    back_weights = weights
    grad_out = cotangent.astype(jnp.float32)
    grad_activation = matmul_right_t(cotangent, back_weights[W_DOWN])
    grad_gate_f32, grad_upper_f32 = swiglu_back(grad_activation)
    grad_gate = grad_gate_f32.astype(jnp.bfloat16)
    grad_upper = grad_upper_f32.astype(jnp.bfloat16)
    grad_hidden_two = matmul_right_t(grad_gate, back_weights[W_GATE]) + matmul_right_t(
        grad_upper, back_weights[W_UP_PROJ]
    )
    grad_middle_norm, grad_norm_ffn = norm_two_back(grad_hidden_two)
    grad_middle = grad_out + grad_middle_norm
    grad_branch = grad_middle.astype(jnp.bfloat16)
    grad_attended = matmul_right_t(grad_branch, back_weights[W_ATTN_OUT]).astype(jnp.bfloat16)
    grad_ssm_low = matmul_right_t(grad_branch, back_weights[W_SSM_OUT])
    grad_ssm_y, grad_gate_ssm_f32, grad_norm_ssm = gnorm_back(grad_ssm_low)
    cumul = jnp.cumsum(step_size * decay[None, :], axis=0)
    entry_decay = ssd_entry(cumul, seq_id, positions)
    grad_y_heads = grad_ssm_y.reshape(rows_dev, SSM_HEADS, SSM_DIM)
    grad_state_local = jnp.einsum(
        "thp,tn,th->hpn", grad_y_heads, c_in, entry_decay, precision=highest
    )
    _, grad_state_out = carried_in((carry_all, grad_state_local), span, chain_states, state_ident)
    grad_conv_values, grad_step_raw_f32, grad_step_bias, grad_decay_log, grad_skip_gain, _ = (
        ssd_back((grad_ssm_y, grad_state_out))
    )
    grad_extended, grad_conv_weight, grad_conv_bias = conv_back(grad_conv_values)
    rim_back = passed_along(grad_extended[: CONV - 1], span, -1)
    grad_xbc_f32 = grad_extended[CONV - 1 :]
    grad_xbc_f32 = grad_xbc_f32.at[rows_dev - (CONV - 1) :].add(rim_back)
    grad_xbc = grad_xbc_f32.astype(jnp.bfloat16)
    grad_gate_ssm = grad_gate_ssm_f32.astype(jnp.bfloat16)
    grad_step_raw = grad_step_raw_f32.astype(jnp.bfloat16)
    grad_w_step = matmul_left_t(hidden, grad_step_raw)
    grad_hidden_ssm = (
        matmul_right_t(grad_gate_ssm, back_weights[W_GATE_SSM])
        + matmul_right_t(grad_xbc[:, :ssm_inner], back_weights[W_X_SSM])
        + matmul_right_t(grad_xbc[:, ssm_inner:], back_weights[W_B_C])
        + matmul_right_t(grad_step_raw, back_weights[W_STEP])
    )
    grad_heads = grad_attended.reshape(rows_dev, HEADS_KV, group_ratio, HEAD_DIM).transpose(
        1, 2, 0, 3
    )
    delta = jnp.sum(grad_heads.astype(jnp.float32) * attn_f32, axis=-1)

    def backward_step(state_now, key_block, value_block, key_rows, key_start):
        grad_query, grad_keys, grad_values = state_now
        scores, visible = block_scores(key_block, key_rows)
        probs = jnp.where(visible, jnp.exp(scores - log_total[..., None]), 0.0)
        key_heads = key_block.reshape(-1, HEADS_KV, HEAD_DIM)
        value_heads = value_block.reshape(-1, HEADS_KV, HEAD_DIM)
        grad_probs = jnp.einsum(
            "gjtd,kgd->gjtk", grad_heads, value_heads, preferred_element_type=jnp.float32
        )
        grad_scores = (probs * (grad_probs - delta[..., None])).astype(jnp.bfloat16)
        grad_query = (
            grad_query
            + jnp.einsum(
                "gjtk,kgd->gjtd", grad_scores, key_heads, preferred_element_type=jnp.float32
            )
            * score_scale
        )
        key_part = (
            jnp.einsum("gjtk,tgjd->kgd", grad_scores, q_heads, preferred_element_type=jnp.float32)
            * score_scale
        )
        value_part = jnp.einsum(
            "gjtk,gjtd->kgd",
            probs.astype(jnp.bfloat16),
            grad_heads,
            preferred_element_type=jnp.float32,
        )
        block_rows = key_block.shape[0]
        grad_keys = add_rows(grad_keys, key_part.reshape(block_rows, -1), key_start)
        grad_values = add_rows(grad_values, value_part.reshape(block_rows, -1), key_start)
        return (grad_query, grad_keys, grad_values)

    initial_back = (
        jnp.zeros(head_shape + (HEAD_DIM,), jnp.float32),
        jnp.zeros((group_rows, HEADS_KV * HEAD_DIM), jnp.float32),
        jnp.zeros((group_rows, HEADS_KV * HEAD_DIM), jnp.float32),
    )
    grad_query_all, grad_keys_all, grad_values_all = over_blocks(
        initial_back,
        (
            lax.all_gather(k_rot, span, axis=0, tiled=True),
            lax.all_gather(value_low, span, axis=0, tiled=True),
        ),
        backward_step,
    )
    grad_keys_mine, grad_values_mine = (
        lax.psum_scatter(
            grad_keys_all.astype(jnp.bfloat16), span, scatter_dimension=0, tiled=True
        ).astype(jnp.float32),
        lax.psum_scatter(
            grad_values_all.astype(jnp.bfloat16), span, scatter_dimension=0, tiled=True
        ).astype(jnp.float32),
    )
    grad_q_rot = grad_query_all.transpose(2, 0, 1, 3).reshape(rows_dev, HEADS_Q * HEAD_DIM)
    grad_query_low = rotate(grad_q_rot, cosine, -sine, HEADS_Q).astype(jnp.bfloat16)
    grad_key_low = rotate(grad_keys_mine, cosine, -sine, HEADS_KV).astype(jnp.bfloat16)
    grad_value_low = grad_values_mine.astype(jnp.bfloat16)
    grad_hidden = (
        grad_hidden_ssm
        + matmul_right_t(grad_query_low, back_weights[W_QUERY])
        + matmul_right_t(grad_key_low, back_weights[W_KEY])
        + matmul_right_t(grad_value_low, back_weights[W_VALUE])
    )
    grad_x_norm, grad_norm_attn = norm_one_back(grad_hidden)
    grad_tokens = grad_middle + grad_x_norm
    small = {
        NORM_ATTN: grad_norm_attn,
        W_STEP: grad_w_step,
        CONV_WEIGHT: grad_conv_weight,
        CONV_BIAS: grad_conv_bias,
        STEP_BIAS: grad_step_bias,
        DECAY_LOG: grad_decay_log,
        SKIP_GAIN: grad_skip_gain,
        NORM_SSM: grad_norm_ssm,
        NORM_FFN: grad_norm_ffn,
    }
    pairs = {
        W_QUERY: (hidden, grad_query_low),
        W_KEY: (hidden, grad_key_low),
        W_VALUE: (hidden, grad_value_low),
        W_ATTN_OUT: (attended, grad_branch),
        W_GATE_SSM: (hidden, grad_gate_ssm),
        W_X_SSM: (hidden, grad_xbc[:, :ssm_inner]),
        W_B_C: (hidden, grad_xbc[:, ssm_inner:]),
        W_SSM_OUT: (ssm_low, grad_branch),
        W_GATE: (hidden_two, grad_gate),
        W_UP_PROJ: (hidden_two, grad_upper),
        W_DOWN: (activation, cotangent),
    }
    if fast:
        return (result.astype(jnp.bfloat16), grad_tokens, fast_gradients(small, pairs), stats)
    grad_dict = dict(small)
    for name_key, (left, right) in pairs.items():
        grad_dict[name_key] = matmul_left_t(left, right)
    flat_parts = [grad_dict[name_key].reshape(-1) for name_key, extent in layout()]
    used_entries = 0
    for part_array in flat_parts:
        used_entries += part_array.shape[0]
    flat_parts.append(jnp.zeros((params.shape[0] * lax.axis_size(group + span) - used_entries,), jnp.float32))
    grad_shard = lax.psum_scatter(
        jnp.concatenate(flat_parts), group + span, scatter_dimension=0, tiled=True
    )
    return (result.astype(jnp.bfloat16), grad_tokens, grad_shard, stats)


def solution(mesh):
    fast = (mesh.shape["group"], mesh.shape["span"]) == FAST
    if fast:
        mesh = Mesh(mesh.devices.reshape(4, 2, 2, 2), GRID)
        group, span = (GRID[:1], GRID[1:])
    else:
        group, span = (("group",), ("span",))

    def program(tokens, params, cotangent, offsets):
        return body(span, group, fast, tokens, params, cotangent, offsets)

    return jax.shard_map(
        program,
        mesh=mesh,
        in_specs=(P(group + span, None), P(group + span), P(group + span, None), P(group, None)),
        out_specs=(P(group + span, None), P(group + span, None), P(group + span), P()),
        check_vma=False,
    )
```

```python
import math

import jax
import jax.numpy as jnp
import numpy as np
from jax import lax
from jax.experimental import pallas as pl
from jax.experimental.pallas import tpu as pltpu
from jax.sharding import Mesh, PartitionSpec as P

D = 1024
HEADS_Q = 8
HEADS_KV = 2
HEAD_DIM = 64
SSM_HEADS = 24
SSM_DIM = 64
STATE = 128
CONV = 4
FF = 2048
(
    NORM_ATTN,
    W_QUERY,
    W_KEY,
    W_VALUE,
    W_ATTN_OUT,
    W_GATE_SSM,
    W_X_SSM,
    W_B_C,
    W_STEP,
    CONV_WEIGHT,
    CONV_BIAS,
    STEP_BIAS,
    DECAY_LOG,
    SKIP_GAIN,
    NORM_SSM,
    W_SSM_OUT,
    NORM_FFN,
    W_GATE,
    W_UP_PROJ,
    W_DOWN,
) = range(20)


epsilon = 1e-05
rope_base = 100000000000.0
masked_score = -1e30
highest = lax.Precision.HIGHEST
small_names = (
    NORM_ATTN,
    CONV_WEIGHT,
    CONV_BIAS,
    STEP_BIAS,
    DECAY_LOG,
    SKIP_GAIN,
    NORM_SSM,
    NORM_FFN,
)


def passed_along(value, axis, steps):
    count = lax.axis_size(axis)
    first, last = (max(0, -steps), min(count, count - steps))
    return lax.ppermute(value, axis, [(source, source + steps) for source in range(first, last)])


def prefix(value, axis, combine, identity):
    peers, place = (lax.axis_size(axis), lax.axis_index(axis))
    everything = jax.tree.map(
        lambda part, kind: lax.all_gather(part.astype(kind), axis),
        value,
        (jnp.bfloat16, jnp.bfloat16),
    )
    start = jax.tree.map(
        lambda part, zero: jnp.broadcast_to(jnp.asarray(zero, part.dtype), part.shape),
        value,
        identity,
    )

    def prefix_turn(k, before):
        reached = k < place
        new = combine(
            before, jax.tree.map(lambda part, own: part[k].astype(own.dtype), everything, value)
        )
        return jax.tree.map(lambda a, b: jnp.where(reached, a, b), new, before)

    return lax.fori_loop(0, peers, prefix_turn, start)


def carried_in(value, axis, combine, identity):
    peers, place = (lax.axis_size(axis), lax.axis_index(axis))
    everything = jax.tree.map(
        lambda part, kind: lax.all_gather(part.astype(kind), axis),
        value,
        jax.tree.map(lambda a: jnp.bfloat16 if a.dtype == jnp.float32 else a.dtype, value),
    )
    start = jax.tree.map(
        lambda part, zero: jnp.broadcast_to(jnp.asarray(zero, part.dtype), part.shape),
        value,
        identity,
    )

    def carried_turn(k, before):
        at = peers - 1 - k
        reached = at > place
        new = combine(
            before, jax.tree.map(lambda part, own: part[at].astype(own.dtype), everything, value)
        )
        return jax.tree.map(lambda a, b: jnp.where(reached, a, b), new, before)

    return lax.fori_loop(0, peers, carried_turn, start)


def layout():
    ssm_inner = SSM_HEADS * SSM_DIM
    channels = ssm_inner + 2 * STATE
    return [
        (NORM_ATTN, (D,)),
        (W_QUERY, (D, HEADS_Q * HEAD_DIM)),
        (W_KEY, (D, HEADS_KV * HEAD_DIM)),
        (W_VALUE, (D, HEADS_KV * HEAD_DIM)),
        (W_ATTN_OUT, (HEADS_Q * HEAD_DIM, D)),
        (W_GATE_SSM, (D, ssm_inner)),
        (W_X_SSM, (D, ssm_inner)),
        (W_B_C, (D, 2 * STATE)),
        (W_STEP, (D, SSM_HEADS)),
        (CONV_WEIGHT, (CONV, channels)),
        (CONV_BIAS, (channels,)),
        (STEP_BIAS, (SSM_HEADS,)),
        (DECAY_LOG, (SSM_HEADS,)),
        (SKIP_GAIN, (SSM_HEADS,)),
        (NORM_SSM, (ssm_inner,)),
        (W_SSM_OUT, (ssm_inner, D)),
        (NORM_FFN, (D,)),
        (W_GATE, (D, FF)),
        (W_UP_PROJ, (D, FF)),
        (W_DOWN, (FF, D)),
    ]


def unpack(flat_vector):
    unpacked = {}
    offset = 0
    for name_key, extent in layout():
        amount = math.prod(extent)
        unpacked[name_key] = flat_vector[offset : offset + amount].reshape(extent)
        offset += amount
    return unpacked


def matmul(left, right):
    return jnp.dot(left, right, preferred_element_type=jnp.float32)


def matmul_left_t(left, right):
    return lax.dot_general(
        left, right, (((0,), (0,)), ((), ())), preferred_element_type=jnp.float32
    )


def matmul_right_t(left, right):
    return lax.dot_general(
        left, right, (((1,), (1,)), ((), ())), preferred_element_type=jnp.float32
    )


def rms_norm(values, gain):
    return values * lax.rsqrt(jnp.mean(values * values, axis=-1, keepdims=True) + epsilon) * gain


def gated_norm(ssm_y, gate_ssm, gain):
    return rms_norm(ssm_y * jax.nn.silu(gate_ssm), gain)


def swiglu(gate_ffn, upper):
    return jax.nn.silu(gate_ffn) * upper


def sequence_info(row_index, bounds):
    starts = bounds[:-1]
    inside = row_index[:, None] >= starts[None, :]
    seq_id = jnp.sum(inside.astype(jnp.int32), axis=1) - 1
    seq_start = jnp.max(jnp.where(inside, starts[None, :], 0), axis=1)
    return (seq_id, row_index - seq_start)


def rotary_tables(positions):
    half_dim = HEAD_DIM // 2
    freqs = jnp.exp(
        -jnp.arange(half_dim, dtype=jnp.float32) * (2.0 * math.log(rope_base) / HEAD_DIM)
    )
    angles = positions.astype(jnp.float32)[:, None] * freqs[None, :]
    return (jnp.cos(angles), jnp.sin(angles))


def rotate(values, cosine, sine, heads):
    row_count = values.shape[0]
    half_dim = HEAD_DIM // 2
    split_heads = values.reshape(row_count, heads, HEAD_DIM)
    first_half = split_heads[..., :half_dim]
    second_half = split_heads[..., half_dim:]
    cos_b = cosine[:, None, :]
    sin_b = sine[:, None, :]
    turned = jnp.concatenate(
        [first_half * cos_b - second_half * sin_b, second_half * cos_b + first_half * sin_b],
        axis=-1,
    )
    return turned.reshape(row_count, heads * HEAD_DIM)


def conv_apply(extended, conv_weight, conv_bias, positions):
    row_count = positions.shape[0]
    conv_total = conv_bias[None, :]
    for tap_index in range(CONV):
        window = extended[tap_index : tap_index + row_count]
        valid_rows = (positions >= CONV - 1 - tap_index)[:, None]
        conv_total = (
            conv_total + jnp.where(valid_rows, window, 0.0) * conv_weight[tap_index][None, :]
        )
    return jax.nn.silu(conv_total)


def split_conv(conv_values):
    ssm_inner = SSM_HEADS * SSM_DIM
    x_ssm = conv_values[:, :ssm_inner].reshape(conv_values.shape[0], SSM_HEADS, SSM_DIM)
    return (
        x_ssm,
        conv_values[:, ssm_inner : ssm_inner + STATE],
        conv_values[:, ssm_inner + STATE :],
    )


def ssd_entry(cumul, seq_id, positions):
    carried = (seq_id == seq_id[0]) & (positions[0] > 0)
    return jnp.where(carried[:, None], jnp.exp(cumul), 0.0)


def ssd_output(x_ssm, b_in, c_in, step_size, decay, skip_gain, seq_id, positions, state_in):
    row_count = seq_id.shape[0]
    cumul = jnp.cumsum(step_size * decay[None, :], axis=0)
    order_rows = jnp.arange(row_count)
    visible = (seq_id[:, None] == seq_id[None, :]) & (order_rows[:, None] >= order_rows[None, :])
    log_gaps = cumul.T[:, :, None] - cumul.T[:, None, :]
    kernel = jnp.exp(jnp.where(visible[None], log_gaps, masked_score))
    inner_products = jnp.dot(c_in, b_in.T, precision=highest)
    scaled_x = x_ssm * step_size[:, :, None]
    intra_part = jnp.einsum(
        "hts,shp->thp", kernel * inner_products[None], scaled_x, precision=highest
    )
    entry_decay = ssd_entry(cumul, seq_id, positions)
    from_state = (
        jnp.einsum("hpn,tn->thp", state_in, c_in, precision=highest) * entry_decay[:, :, None]
    )
    return intra_part + from_state + skip_gain[None, :, None] * x_ssm


def ssd_summary(x_ssm, b_in, step_size, decay, seq_id, positions):
    cumul = jnp.cumsum(step_size * decay[None, :], axis=0)
    carried_last = (seq_id[-1] == seq_id[0]) & (positions[0] > 0)
    carry_all = jnp.where(carried_last, jnp.exp(cumul[-1]), 0.0)
    tail_decay = jnp.exp(
        jnp.where((seq_id == seq_id[-1])[:, None], cumul[-1:] - cumul, masked_score)
    )
    local_state = jnp.einsum(
        "sh,shp,sn->hpn", tail_decay, x_ssm * step_size[:, :, None], b_in, precision=highest
    )
    return (carry_all, local_state)


def chain_states(earlier, later):
    return (earlier[0] * later[0], earlier[1] * later[0][:, None, None] + later[1])


def add_rows(target, addend, first_row):
    current = lax.dynamic_slice_in_dim(target, first_row, addend.shape[0], 0)
    return lax.dynamic_update_slice_in_dim(target, current + addend, first_row, 0)


FAST = (4, 8)
LINE = 128
SHARD = 3082
SPAD = 3088
WIN = 3104
PLANE = 8 * SHARD
DEPTH = 4
TALL = {1: 1024, 2: 1024, 4: 512, 8: 256, 12: 128, 16: 128}
GRID = ("z", "y", "x", "c")
ZC = ("z", "c")
SWAP = [(0, 1), (1, 0)]


def zc_pairs(*pairs):
    return [(2 * a + c, 2 * b + c) for a, b, c in pairs]


def gather_lines(params):
    z, y, x, c = (lax.axis_index(name) for name in GRID)
    lines = jnp.pad(params.reshape(SHARD, LINE), ((0, SPAD - SHARD), (0, 0)))
    sibling = lax.ppermute(lines, ZC, [(2 * k + 1 - k % 2, 2 * k + k % 2) for k in range(4)])
    batches = []
    for batch in range(2):
        buffers = []
        for part in range(2):
            here = jnp.where(c == part, lines, sibling)
            if batch == 0:
                one = lax.ppermute(here, ZC, zc_pairs((0, 1, 0), (1, 2, 1)))
                side = lax.ppermute(here, ZC, zc_pairs((1, 0, 1)))
                two = lax.ppermute(one, ZC, zc_pairs((1, 2, 0), (2, 3, 1)))
                three = lax.ppermute(two, ZC, zc_pairs((2, 3, 0)))
            else:
                one = lax.ppermute(here, ZC, zc_pairs((2, 1, 0), (3, 2, 1)))
                side = lax.ppermute(here, ZC, zc_pairs((2, 3, 0)))
                two = lax.ppermute(one, ZC, zc_pairs((1, 0, 0), (2, 1, 1)))
                three = lax.ppermute(two, ZC, zc_pairs((1, 0, 1)))
            mine = z == 2 * batch + c
            column = jnp.where(mine, here, one + side + two + three)
            over_x = lax.ppermute(column, "x", SWAP)
            over_y = lax.ppermute(column, "y", SWAP)
            if part == 0:
                corner = lax.ppermute(over_x, "y", SWAP)
            else:
                corner = lax.ppermute(over_y, "x", SWAP)
            local = [column, over_x, over_y, corner]
            buffers += local + [lax.ppermute(piece, "c", SWAP) for piece in local]
        batches.append(buffers)
    shard = np.arange(32)
    sz, sy, sx, sc = shard // 8, shard // 4 % 2, shard // 2 % 2, shard % 2
    away = jnp.where(sz % 2 == c, 0, 4)
    where = sc * 8 + away + 2 * (sy ^ y) + (sx ^ x) + 16 * (sz // 2)
    return batches, where.astype(jnp.int32)


def unpack_lines(buffers, first, where, segments):
    jobs, starts = [], []
    reach = 0
    for offset, rows, columns in segments:
        per_row = columns // LINE
        lane, base = offset % LINE, offset // LINE
        if per_row == 1 and rows < 1024:
            lane, tall = 0, rows
        else:
            tall = TALL[per_row]
        starts.append(len(jobs))
        for k in range(rows // tall):
            jobs.append((base + k * tall * per_row, tall * per_row, 1 if lane else 0))
    window = max(job[1] for job in jobs) + 32
    table = np.zeros((len(jobs), 5), np.int32)
    for k, (line, count, extra) in enumerate(jobs):
        owner = line // SHARD
        inside = line - owner * SHARD
        begin = min(inside // 16 * 16, SPAD - window)
        crosses = int(line + count + extra > (owner + 1) * SHARD)
        table[k] = (owner, begin, begin - inside, crosses, (owner + 1) * SHARD - line)
    base_row = (int(-table[:, 2].min()) + 7) // 8 * 8
    table[:, 2] += base_row
    table[:, 4] += base_row
    room = int(max((table[:, 2] + window).max(), ((table[:, 4] + window) * table[:, 3]).max()))
    room = (room + 15) // 8 * 8
    total = len(jobs)
    count_buffers = len(buffers)
    shapes = []
    for offset, rows, columns in segments:
        per_row = columns // LINE
        tall = rows if per_row == 1 and rows < 1024 else TALL[per_row]
        shapes.append((rows, columns, tall, per_row, offset % LINE if tall != rows or per_row != 1 else 0))
    sizes = sorted({(tall, columns) for _, columns, tall, _, _ in shapes})

    def kernel(table_ref, where_ref, *refs):
        sources = refs[:count_buffers]
        outs = refs[count_buffers : count_buffers + len(segments)]
        rest = refs[count_buffers + len(segments) :]
        stages = dict(zip(sizes, rest))
        raw, flat, in_sem, out_sem = rest[len(sizes) :]
        step = pl.program_id(0)

        def fetch(job, slot):
            owner = table_ref[job, 0]
            begin = pl.multiple_of(table_ref[job, 1], 16)
            for b in range(count_buffers):

                @pl.when(where_ref[owner] == first + b)
                def _():
                    pltpu.make_async_copy(
                        sources[b].at[pl.ds(begin, window), :], raw.at[slot, 0], in_sem.at[slot, 0]
                    ).start()

            @pl.when(table_ref[job, 3] == 1)
            def _():
                for b in range(count_buffers):

                    @pl.when(where_ref[owner + 1] == first + b)
                    def _():
                        pltpu.make_async_copy(
                            sources[b].at[pl.ds(0, window), :], raw.at[slot, 1], in_sem.at[slot, 1]
                        ).start()

        def fetched(slot, half):
            return pltpu.make_async_copy(
                sources[0].at[pl.ds(0, window), :], raw.at[slot, half], in_sem.at[slot, half]
            )

        @pl.when(step == 0)
        def _():
            for k in range(min(DEPTH - 1, total)):
                fetch(k, k)

        @pl.when(step + DEPTH - 1 < total)
        def _():
            fetch(step + DEPTH - 1, lax.rem(step + DEPTH - 1, DEPTH))

        slot = lax.rem(step, DEPTH)
        fetched(slot, 0).wait()
        flat[pl.ds(table_ref[step, 2], window), :] = raw[slot, 0].astype(jnp.float32)

        @pl.when(table_ref[step, 3] == 1)
        def _():
            fetched(slot, 1).wait()
            flat[pl.ds(table_ref[step, 4], window), :] = raw[slot, 1].astype(jnp.float32)

        for index, (rows, columns, tall, per_row, lane) in enumerate(shapes):
            begin = starts[index]
            blocks = rows // tall
            stage = stages[(tall, columns)]

            @pl.when((step >= begin) & (step < begin + blocks))
            def _():
                block = step - begin
                side = lax.rem(block, 2)

                def written(k, s):
                    return pltpu.make_async_copy(
                        stage.at[s],
                        outs[index].at[pl.ds(pl.multiple_of(k * tall, 16), tall), :],
                        out_sem.at[s],
                    )

                @pl.when(block >= 2)
                def _():
                    written(block - 2, side).wait()

                def tile(j):
                    picked = flat[pl.ds(base_row + j, tall, stride=per_row), :]
                    return pltpu.roll(picked, LINE - lane, 1) if lane else picked

                if lane:
                    lanes = lax.broadcasted_iota(jnp.int32, (tall, LINE), 1)
                    now = tile(0)
                    for j in range(per_row):
                        later = tile(j + 1)
                        stage[side, :, j * LINE : (j + 1) * LINE] = jnp.where(
                            lanes < LINE - lane, now, later
                        ).astype(jnp.bfloat16)
                        now = later
                else:
                    for j in range(per_row):
                        stage[side, :, j * LINE : (j + 1) * LINE] = tile(j).astype(jnp.bfloat16)
                written(block, side).start()

                @pl.when(block == blocks - 1)
                def _():
                    if blocks > 1:
                        written(block - 1, 1 - side).wait()
                    written(block, side).wait()

    return pl.pallas_call(
        kernel,
        grid_spec=pltpu.PrefetchScalarGridSpec(
            num_scalar_prefetch=2,
            grid=(total,),
            in_specs=[pl.BlockSpec(memory_space=pl.ANY)] * count_buffers,
            out_specs=[pl.BlockSpec(memory_space=pl.ANY)] * len(segments),
            scratch_shapes=[pltpu.VMEM((2,) + size, jnp.bfloat16) for size in sizes]
            + [
                pltpu.VMEM((DEPTH, 2, window, LINE), jnp.bfloat16),
                pltpu.VMEM((room, LINE), jnp.float32),
                pltpu.SemaphoreType.DMA((DEPTH, 2)),
                pltpu.SemaphoreType.DMA((2,)),
            ],
        ),
        out_shape=[jax.ShapeDtypeStruct((rows, columns), jnp.bfloat16) for _, rows, columns in segments],
        compiler_params=pltpu.CompilerParams(vmem_limit_bytes=48 * 2**20),
        cost_estimate=pl.CostEstimate(flops=0, bytes_accessed=total * window * LINE * 4, transcendentals=0),
        name="unpack",
    )(jnp.asarray(table), where, *buffers)


def pack_lines(target, target_rows, first_row, segments, lane, phase, extras, carry, tail_rows):
    tall = 256
    lefts, rights, plan = [], [], []
    left_of, right_of = {}, {}
    row = first_row
    begin = 0
    for left, right in segments:
        for value, seen, kept in ((left, left_of, lefts), (right, right_of, rights)):
            if id(value) not in seen:
                seen[id(value)] = len(kept)
                kept.append(value)
        blocks = left.shape[1] // tall
        plan.append((left_of[id(left)], right_of[id(right)], right.shape[1] // LINE, begin, blocks, row))
        begin += blocks
        row += left.shape[1] * right.shape[1] // LINE
    end_row = row
    total = begin
    biggest = max(entry[2] for entry in plan) * tall
    tokens = lefts[0].shape[0]
    count_left, count_right, count_extra = len(lefts), len(rights), len(extras)
    rolled = [jnp.roll(right, lane, axis=1) if lane else right for right in rights]
    carry_in = [carry] if lane else []
    targets = [] if target is None else [target]

    def left_spec(index):
        mine = [entry for entry in plan if entry[0] == index]

        def place(step):
            block = 0
            for _, _, _, start, blocks, _ in mine:
                block = jnp.where(step >= start, jnp.minimum(step - start, blocks - 1), block)
            return (0, block)

        return pl.BlockSpec((tokens, tall), place)

    def kernel(*refs):
        left_refs = refs[:count_left]
        right_refs = refs[count_left : count_left + count_right]
        at = count_left + count_right
        extra_refs = refs[at : at + count_extra]
        at += count_extra
        carry_refs = refs[at : at + len(carry_in)]
        at += len(carry_in) + len(targets)
        out = refs[at]
        flat, stage, shift, last, sems, extra_sems = refs[at + 1 :]
        step = pl.program_id(0)
        side = lax.rem(step, 2)

        def extra_copy(k):
            rows = extras[k][0].shape[0]
            return pltpu.make_async_copy(
                extra_refs[k], out.at[pl.ds(extras[k][1], rows), :], extra_sems.at[k]
            )

        @pl.when(step == 0)
        def _():
            for k in range(count_extra):
                extra_copy(k).start()
            if lane:
                shift[0:8, :] = carry_refs[0][...]
            if phase:
                flat[0:8, :] = jnp.zeros((8, LINE), jnp.float32)

        for left_at, right_at, per_row, start, blocks, row in plan:
            lines = per_row * tall

            def written(block, s, row=row, lines=lines):
                return pltpu.make_async_copy(
                    stage.at[s, pl.ds(0, lines), :],
                    out.at[pl.ds(pl.multiple_of(row + block * lines, 16), lines), :],
                    sems.at[s],
                )

            @pl.when((step >= start) & (step < start + blocks))
            def _():
                block = step - start
                if phase:

                    @pl.when(step > 0)
                    def _():
                        flat[0:8, :] = flat[lines : lines + 8, :]

                turned = left_refs[left_at][...].T
                lanes = lax.broadcasted_iota(jnp.int32, (tall, LINE), 1)
                for j0 in range(0, per_row, 2):
                    wide = min(2, per_row - j0)
                    tile = jnp.dot(
                        turned,
                        right_refs[right_at][:, j0 * LINE : (j0 + wide) * LINE],
                        preferred_element_type=jnp.float32,
                    )
                    for j in range(wide):
                        piece = tile[:, j * LINE : (j + 1) * LINE]
                        if lane and j0 + j == 0:
                            shift[8 : 8 + tall, :] = piece
                            piece = jnp.where(lanes < lane, shift[7 : 7 + tall, :], piece)
                            shift[0:8, :] = shift[tall : tall + 8, :]
                        if per_row == 1:
                            flat[phase : phase + tall, :] = piece
                        else:
                            flat[pl.ds(phase + j0 + j, tall, stride=per_row), :] = piece

                stage[side, 0:lines, :] = flat[0:lines, :].astype(jnp.bfloat16)
                written(block, side).start()

            @pl.when((step > start) & (step <= start + blocks))
            def _():
                written(step - start - 1, 1 - side).wait()

            if start + blocks == total:

                @pl.when(step == total - 1)
                def _():
                    written(blocks - 1, side).wait()

        @pl.when(step == total - 1)
        def _():
            if tail_rows:
                lanes = lax.broadcasted_iota(jnp.int32, (tail_rows, LINE), 1)
                rows_at = lax.broadcasted_iota(jnp.int32, (tail_rows, LINE), 0)
                final = jnp.broadcast_to(shift[7:8, :], (tail_rows, LINE))
                last[...] = jnp.where((rows_at == 0) & (lanes < lane), final, 0.0).astype(jnp.bfloat16)
                closing = pltpu.make_async_copy(
                    last, out.at[pl.ds(end_row, tail_rows), :], extra_sems.at[count_extra]
                )
                closing.start()
                closing.wait()
            for k in range(count_extra):
                extra_copy(k).wait()

    whole = [pl.BlockSpec(array.shape, lambda step: (0, 0)) for array in rolled]
    flops = sum(2 * tokens * entry[4] * tall * entry[2] * LINE for entry in plan)
    return pl.pallas_call(
        kernel,
        grid=(total,),
        in_specs=[left_spec(k) for k in range(count_left)]
        + whole
        + [pl.BlockSpec(array.shape, lambda step: (0, 0)) for array, _ in extras]
        + [pl.BlockSpec(array.shape, lambda step: (0, 0)) for array in carry_in]
        + [pl.BlockSpec(memory_space=pl.ANY)] * len(targets),
        out_specs=pl.BlockSpec(memory_space=pl.ANY),
        out_shape=jax.ShapeDtypeStruct((target_rows, LINE), jnp.bfloat16),
        scratch_shapes=[
            pltpu.VMEM((biggest + 16, LINE), jnp.float32),
            pltpu.VMEM((2, biggest, LINE), jnp.bfloat16),
            pltpu.VMEM((tall + 8, LINE), jnp.float32),
            pltpu.VMEM((max(tail_rows, 16), LINE), jnp.bfloat16),
            pltpu.SemaphoreType.DMA((2,)),
            pltpu.SemaphoreType.DMA((count_extra + 1,)),
        ],
        input_output_aliases={count_left + count_right + count_extra + len(carry_in): 0} if targets else {},
        compiler_params=pltpu.CompilerParams(vmem_limit_bytes=48 * 2**20),
        cost_estimate=pl.CostEstimate(flops=flops, bytes_accessed=total * biggest * LINE * 2, transcendentals=0),
        name="pack",
    )(*lefts, *rolled, *[array for array, _ in extras], *carry_in, *targets)


def added(*parts):
    total = parts[0].astype(jnp.float32)
    for part in parts[1:]:
        total = total + part.astype(jnp.float32)
    return total.astype(jnp.bfloat16)


def reduce_lines(flat, batch, shift):
    z, y, x, c = (lax.axis_index(name) for name in GRID)
    length = PLANE + 32
    keep = lax.dynamic_slice(flat, (c * PLANE, 0), (length, LINE))
    send = lax.dynamic_slice(flat, ((1 - c) * PLANE, 0), (length, LINE))
    chip = added(keep, lax.ppermute(send, "c", SWAP))

    def window(sy, sx, part):
        shard = sy * 4 + sx * 2 + part
        start = (shift + SHARD * shard) // 16 * 16
        return lax.dynamic_slice(chip, (start, 0), (WIN, LINE))

    ends = []
    for part in range(2):
        if part == 0:
            away = jnp.stack([window(1 - y, 0, part), window(1 - y, 1, part)])
            home = jnp.stack([window(y, 0, part), window(y, 1, part)])
            first_axis, second_axis, place = "y", "x", x
        else:
            away = jnp.stack([window(0, 1 - x, part), window(1, 1 - x, part)])
            home = jnp.stack([window(0, x, part), window(1, x, part)])
            first_axis, second_axis, place = "x", "y", y
        half = added(home, lax.ppermute(away, first_axis, SWAP))
        other = lax.dynamic_index_in_dim(half, 1 - place, 0, keepdims=False)
        mine = lax.dynamic_index_in_dim(half, place, 0, keepdims=False)
        column = added(mine, lax.ppermute(other, second_axis, SWAP))
        if batch == 0:
            one = added(column, lax.ppermute(column, ZC, zc_pairs((3, 2, 0), (3, 2, 1))))
            side = lax.ppermute(column, ZC, zc_pairs((0, 1, 1)))
            two = added(one, lax.ppermute(one, ZC, zc_pairs((2, 1, 0), (2, 1, 1))), side)
            end = added(two, lax.ppermute(two, ZC, zc_pairs((1, 0, 0))))
        else:
            one = added(column, lax.ppermute(column, ZC, zc_pairs((0, 1, 0), (0, 1, 1))))
            side = lax.ppermute(column, ZC, zc_pairs((3, 2, 0)))
            two = added(one, lax.ppermute(one, ZC, zc_pairs((1, 2, 0), (1, 2, 1))), side)
            end = added(two, lax.ppermute(two, ZC, zc_pairs((2, 3, 1))))
        ends.append(end)
    mine = jnp.where(c == 0, ends[0], ends[1])
    other = jnp.where(c == 0, ends[1], ends[0])
    holders = [(2 * k + k % 2, 2 * k + 1 - k % 2) for k in range(4)]
    handed = lax.ppermute(other, ZC, holders)
    return jnp.where(c == z % 2, mine, handed)


KEYS = 512
PAIR = 2 * HEAD_DIM
NT = (((1,), (1,)), ((), ()))


def attention_forward(q_wide, kv, meta, starts):
    rows = q_wide.shape[1]
    blocks = kv.shape[0]
    tall = min(256, rows)

    def kernel(meta_ref, q_ref, kv_ref, start_ref, o_ref, log_ref, top, total, mixed):
        top[...] = jnp.full(top.shape, masked_score, jnp.float32)
        total[...] = jnp.zeros(total.shape, jnp.float32)
        mixed[...] = jnp.zeros(mixed.shape, jnp.float32)

        def block(b, partial):
            pair = kv_ref[b, 0]
            for r in range(0, rows, tall):
                here = slice(r, r + tall)
                scores = lax.dot_general(q_ref[0, here, :], pair, NT, preferred_element_type=jnp.float32)
                if partial:
                    keys = b * KEYS + lax.broadcasted_iota(jnp.int32, scores.shape, 1)
                    mine = meta_ref[2] + r + lax.broadcasted_iota(jnp.int32, scores.shape, 0)
                    visible = (keys >= start_ref[here, :]) & (keys <= mine)
                    scores = jnp.where(visible, scores, masked_score)
                before = top[here, :]
                peak = jnp.maximum(before, jnp.max(scores, axis=1, keepdims=True))
                part = jnp.exp(scores - peak[:, :1])
                if partial:
                    part = jnp.where(visible, part, 0.0)
                fade = jnp.exp(before - peak)
                top[here, :] = peak
                total[here, :] = total[here, :] * fade + jnp.sum(part, axis=1, keepdims=True)
                mixed[here, :] = mixed[here, :] * fade + jnp.dot(
                    part.astype(jnp.bfloat16), pair, preferred_element_type=jnp.float32
                )

        def turn(b, nothing):
            partial = ((b + 1) * KEYS > meta_ref[2]) | (b * KEYS < meta_ref[3])

            @pl.when(partial)
            def _():
                block(b, True)

            @pl.when(jnp.logical_not(partial))
            def _():
                block(b, False)

            return nothing

        lax.fori_loop(meta_ref[0], meta_ref[1], turn, 0)
        o_ref[0] = mixed[...] / total[...]
        log_ref[0] = (top[...] + jnp.log(total[...])).T[:8, :]

    ratio = HEADS_Q // HEADS_KV
    return pl.pallas_call(
        kernel,
        grid_spec=pltpu.PrefetchScalarGridSpec(
            num_scalar_prefetch=1,
            grid=(HEADS_Q,),
            in_specs=[
                pl.BlockSpec((1, rows, PAIR), lambda h, m: (h, 0, 0)),
                pl.BlockSpec((blocks, 1, KEYS, PAIR), lambda h, m: (0, h // ratio, 0, 0)),
                pl.BlockSpec((rows, 1), lambda h, m: (0, 0)),
            ],
            out_specs=[
                pl.BlockSpec((1, rows, PAIR), lambda h, m: (h, 0, 0)),
                pl.BlockSpec((1, 8, rows), lambda h, m: (h, 0, 0)),
            ],
            scratch_shapes=[pltpu.VMEM((rows, PAIR), jnp.float32)] * 3,
        ),
        out_shape=[
            jax.ShapeDtypeStruct((HEADS_Q, rows, PAIR), jnp.float32),
            jax.ShapeDtypeStruct((HEADS_Q, 8, rows), jnp.float32),
        ],
        compiler_params=pltpu.CompilerParams(vmem_limit_bytes=48 * 2**20),
        cost_estimate=pl.CostEstimate(flops=2 * 10**9, bytes_accessed=2**23, transcendentals=2**23),
        name="attend",
    )(meta, q_wide, kv, starts)


def attention_backward(q_wide, g_wide, kv, logs, mixed, meta, starts):
    rows = q_wide.shape[1]
    blocks = kv.shape[0]
    ratio = HEADS_Q // HEADS_KV
    wide = min(256, rows)

    def kernel(meta_ref, q_ref, g_ref, kv_ref, log_ref, o_ref, start_ref, dkv_ref, dq_ref, delta, sums):
        b = pl.program_id(1)

        @pl.when(b == 0)
        def _():
            dq_ref[...] = jnp.zeros(dq_ref.shape, jnp.float32)
            for h in range(ratio):
                both = g_ref[h].astype(jnp.float32) * o_ref[h]
                delta[h] = jnp.broadcast_to(jnp.sum(both.T, axis=0, keepdims=True), (8, rows))

        def block(partial):
            pair = kv_ref[0, 0]
            turned = pair.T[:HEAD_DIM, :]
            for h in range(ratio):
                for r in range(0, rows, wide):
                    here = slice(r, r + wide)
                    q_now = q_ref[h, here, :]
                    g_now = g_ref[h, here, :]
                    scores = lax.dot_general(pair, q_now, NT, preferred_element_type=jnp.float32)
                    probs = jnp.exp(scores - log_ref[h, 0:1, here])
                    if partial:
                        keys = b * KEYS + lax.broadcasted_iota(jnp.int32, scores.shape, 0)
                        mine = meta_ref[2] + r + lax.broadcasted_iota(jnp.int32, scores.shape, 1)
                        visible = (keys >= start_ref[0:1, here]) & (keys <= mine)
                        probs = jnp.where(visible, probs, 0.0)
                    grads = lax.dot_general(pair, g_now, NT, preferred_element_type=jnp.float32)
                    low_grads = (probs * (grads - delta[h, 0:1, here])).astype(jnp.bfloat16)
                    change = jnp.dot(
                        probs.astype(jnp.bfloat16), g_now, preferred_element_type=jnp.float32
                    ) + jnp.dot(low_grads, q_now, preferred_element_type=jnp.float32)
                    if h == 0 and r == 0:
                        sums[...] = change
                    else:
                        sums[...] += change
                    dq_ref[h, :, here] += jnp.dot(turned, low_grads, preferred_element_type=jnp.float32)
            dkv_ref[0, 0] = sums[...].astype(jnp.bfloat16)

        needed = (b >= meta_ref[0]) & (b < meta_ref[1])
        partial = ((b + 1) * KEYS > meta_ref[2]) | (b * KEYS < meta_ref[3])

        @pl.when(needed & partial)
        def _():
            block(True)

        @pl.when(needed & jnp.logical_not(partial))
        def _():
            block(False)

        @pl.when(jnp.logical_not(needed))
        def _():
            dkv_ref[0, 0] = jnp.zeros((KEYS, PAIR), jnp.bfloat16)

    heads = lambda g, b, m: (g, 0, 0)
    return pl.pallas_call(
        kernel,
        grid_spec=pltpu.PrefetchScalarGridSpec(
            num_scalar_prefetch=1,
            grid=(HEADS_KV, blocks),
            in_specs=[
                pl.BlockSpec((ratio, rows, PAIR), heads),
                pl.BlockSpec((ratio, rows, PAIR), heads),
                pl.BlockSpec((1, 1, KEYS, PAIR), lambda g, b, m: (b, g, 0, 0)),
                pl.BlockSpec((ratio, 8, rows), heads),
                pl.BlockSpec((ratio, rows, PAIR), heads),
                pl.BlockSpec((8, rows), lambda g, b, m: (0, 0)),
            ],
            out_specs=[
                pl.BlockSpec((1, 1, KEYS, PAIR), lambda g, b, m: (b, g, 0, 0)),
                pl.BlockSpec((ratio, HEAD_DIM, rows), heads),
            ],
            scratch_shapes=[
                pltpu.VMEM((ratio, 8, rows), jnp.float32),
                pltpu.VMEM((KEYS, PAIR), jnp.float32),
            ],
        ),
        out_shape=[
            jax.ShapeDtypeStruct((blocks, HEADS_KV, KEYS, PAIR), jnp.bfloat16),
            jax.ShapeDtypeStruct((HEADS_Q, HEAD_DIM, rows), jnp.float32),
        ],
        compiler_params=pltpu.CompilerParams(vmem_limit_bytes=48 * 2**20),
        cost_estimate=pl.CostEstimate(flops=5 * 10**9, bytes_accessed=2**23, transcendentals=2**23),
        name="attend_back",
    )(meta, q_wide, g_wide, kv, logs, mixed, starts)


def ordered(place, own, other, axis):
    first = jnp.where(place == 0, own, other)
    second = jnp.where(place == 0, other, own)
    return jnp.stack([first, second], axis=axis)


def gather_span(value, span, fast):
    if not fast:
        return lax.all_gather(value, span)
    _, y, x, c = (lax.axis_index(name) for name in GRID)
    two = ordered(x, value, lax.ppermute(value, "x", SWAP), 0)
    four = ordered(y, two, lax.ppermute(two, "y", SWAP), 0)
    eight = ordered(c, four, lax.ppermute(four, "c", SWAP), 2)
    return eight.reshape((8,) + value.shape)


def scatter_span(value, span, fast):
    if not fast:
        return lax.psum_scatter(value, span, scatter_dimension=0).astype(jnp.float32)
    _, y, x, c = (lax.axis_index(name) for name in GRID)
    value = value.reshape((2, 2, 2) + value.shape[1:])
    for name, place, axis in (("c", c, 2), ("y", y, 0), ("x", x, 0)):
        keep = lax.dynamic_index_in_dim(value, place, axis, keepdims=False)
        send = lax.dynamic_index_in_dim(value, 1 - place, axis, keepdims=False)
        value = keep.astype(jnp.float32) + lax.ppermute(send, name, SWAP).astype(jnp.float32)
        if name != "x":
            value = value.astype(jnp.bfloat16)
    return value


def sum_all(value, axes, fast):
    if not fast:
        return lax.psum(value, axes)
    for name in GRID[1:]:
        value = value + lax.ppermute(value, name, SWAP)
    for pairs in ([(0, 1), (1, 0), (2, 3), (3, 2)], [(0, 2), (2, 0), (1, 3), (3, 1)]):
        value = value + lax.ppermute(value, "z", pairs)
    return value


def offsets_of():
    places, at = {}, 0
    for name_key, extent in layout():
        places[name_key] = (at, extent)
        at += math.prod(extent)
    return places


def fast_weights(params):
    places = offsets_of()
    (early, late), where = gather_lines(params)
    early_names = (W_QUERY, W_KEY, W_VALUE, W_ATTN_OUT, W_GATE_SSM, W_X_SSM, W_B_C)
    late_names = (W_SSM_OUT, W_GATE, W_UP_PROJ, W_DOWN)

    def segment(name_key):
        at, extent = places[name_key]
        return (at, extent[0], extent[1])

    misc_at = places[W_STEP][0]
    first = unpack_lines(
        early, 0, where,
        [segment(name_key) for name_key in early_names] + [(0, 16, LINE), (misc_at, 288, LINE)],
    )
    second = unpack_lines(
        early + late, 0, where,
        [segment(name_key) for name_key in late_names] + [(places[NORM_FFN][0], 16, LINE)],
    )
    weights = dict(zip(early_names, first))
    weights.update(zip(late_names, second))
    weights[NORM_ATTN] = first[-2].reshape(-1)[:D]
    misc = first[-1].reshape(-1)
    for name_key in (W_STEP,) + small_names[1:-1]:
        at, extent = places[name_key]
        weights[name_key] = misc[at - misc_at : at - misc_at + math.prod(extent)].reshape(extent)
    lane = places[NORM_FFN][0] % LINE
    weights[NORM_FFN] = second[-1].reshape(-1)[lane : lane + D]
    return weights


def fast_gradients(small, pairs):
    places = offsets_of()
    z, y, x, c = (lax.axis_index(name) for name in GRID)
    ssm_low, grad_branch = pairs[W_SSM_OUT]
    out_at = places[W_SSM_OUT][0]
    lane = places[W_GATE][0] % LINE
    boundary = 2 * PLANE * LINE
    tail_from = (boundary - out_at) // D
    tail = matmul_left_t(ssm_low[:, tail_from:], grad_branch).reshape(-1)
    tail = tail[boundary - out_at - tail_from * D :]
    head = jnp.concatenate([jnp.zeros((14 * LINE,), jnp.float32), tail, small[NORM_FFN]])
    head_rows = head.shape[0] // LINE
    carry = jnp.zeros((8, LINE), jnp.float32).at[7, :lane].set(head[head_rows * LINE :])
    head = head[: head_rows * LINE].reshape(head_rows, LINE).astype(jnp.bfloat16)
    length = 2 * PLANE + 32
    late = pack_lines(
        None, length, head_rows,
        [pairs[W_GATE], pairs[W_UP_PROJ], pairs[W_DOWN]],
        lane, 0, [(head, 0)], carry, 48,
    )
    late_sum = reduce_lines(late, 1, 14)
    first_row = (8 + out_at // LINE) // 16 * 16
    early_rows = first_row + SSM_HEADS * SSM_DIM * D // LINE
    early = pack_lines(
        None, early_rows, first_row, [pairs[W_SSM_OUT]],
        lane, (8 + out_at // LINE) % 8, [], jnp.zeros((8, LINE), jnp.float32), 0,
    )
    names = (W_STEP,) + small_names[1:-1]
    misc = [small[name_key].reshape(-1) for name_key in names]
    count = sum(part.shape[0] for part in misc)
    misc_rows = (count // LINE + 16) // 16 * 16
    opening = matmul_left_t(ssm_low[:, :16], grad_branch).reshape(-1)
    misc = jnp.concatenate(misc + [opening[: misc_rows * LINE - count]])
    misc = misc.reshape(misc_rows, LINE).astype(jnp.bfloat16)
    first = jnp.concatenate([jnp.zeros((8 * LINE,), jnp.float32), small[NORM_ATTN]])
    first = first.reshape(16, LINE).astype(jnp.bfloat16)
    early = pack_lines(
        early, early_rows, 16,
        [pairs[k] for k in (W_QUERY, W_KEY, W_VALUE, W_ATTN_OUT, W_GATE_SSM, W_X_SSM, W_B_C)],
        0, 0, [(first, 0), (misc, 8 + places[W_STEP][0] // LINE)], None, 0,
    )
    early_sum = reduce_lines(early, 0, 8)
    shard = SHARD * (4 * y + 2 * x + c)
    start = jnp.where(z < 2, (8 + shard) % 16, (14 + shard) % 16)
    lines = jnp.where(z < 2, early_sum, late_sum)
    return lax.dynamic_slice(lines, (start, 0), (SHARD, LINE)).astype(jnp.float32).reshape(-1)


def body(span, group, fast, tokens, params, cotangent, offsets):
    rows_dev = tokens.shape[0]
    group_rows = rows_dev * lax.axis_size(span)
    all_rows = group_rows * lax.axis_size(group)
    ssm_inner = SSM_HEADS * SSM_DIM
    score_scale = HEAD_DIM ** (-0.5)
    bounds = offsets[0]
    my_start = lax.axis_index(span) * rows_dev
    row_index = my_start + jnp.arange(rows_dev, dtype=jnp.int32)
    seq_id, positions = sequence_info(row_index, bounds)
    first_start = row_index[0] - positions[0]
    last_row = my_start + rows_dev - 1
    cosine, sine = rotary_tables(positions)
    if fast:
        weights = fast_weights(params)
    else:
        weights = unpack(lax.all_gather(params, group + span, axis=0, tiled=True))
    small_f32 = {name_key: weights[name_key].astype(jnp.float32) for name_key in small_names}
    x_rows = tokens.astype(jnp.float32)
    normed_one, norm_one_back = jax.vjp(rms_norm, x_rows, small_f32[NORM_ATTN])
    hidden = normed_one.astype(jnp.bfloat16)
    query = matmul(hidden, weights[W_QUERY])
    key_raw = matmul(hidden, weights[W_KEY])
    value_low = matmul(hidden, weights[W_VALUE]).astype(jnp.bfloat16)
    q_rot = rotate(query, cosine, sine, HEADS_Q).astype(jnp.bfloat16)
    k_rot = rotate(key_raw, cosine, sine, HEADS_KV).astype(jnp.bfloat16)
    k_heads = k_rot.reshape(rows_dev, HEADS_KV, HEAD_DIM)
    v_heads = value_low.reshape(rows_dev, HEADS_KV, HEAD_DIM)
    kv_mine = jnp.concatenate([k_heads, v_heads], axis=2).transpose(1, 0, 2)
    key_blocks = gather_span(kv_mine.reshape(HEADS_KV, rows_dev, PAIR), span, fast)
    if rows_dev != KEYS:
        key_blocks = key_blocks.transpose(1, 0, 2, 3).reshape(HEADS_KV, -1, KEYS, PAIR).transpose(1, 0, 2, 3)
    row_starts = row_index - positions
    meta = jnp.stack(
        [first_start // KEYS, last_row // KEYS + 1, my_start, row_starts[rows_dev - 1]]
    ).astype(jnp.int32)
    q_low = (q_rot * jnp.bfloat16(score_scale)).reshape(rows_dev, HEADS_Q, HEAD_DIM).transpose(1, 0, 2)
    q_wide = jnp.pad(q_low, ((0, 0), (0, 0), (0, HEAD_DIM)))
    mixed, logs = attention_forward(q_wide, key_blocks, meta, row_starts[:, None])
    attended = (
        mixed[:, :, HEAD_DIM:].transpose(1, 0, 2).reshape(rows_dev, HEADS_Q * HEAD_DIM).astype(jnp.bfloat16)
    )
    attn_out = matmul(attended, weights[W_ATTN_OUT])
    gate_ssm = matmul(hidden, weights[W_GATE_SSM])
    xbc = jnp.concatenate(
        [matmul(hidden, weights[W_X_SSM]), matmul(hidden, weights[W_B_C])], axis=1
    )
    step_raw = matmul(hidden, weights[W_STEP])
    rim_rows = passed_along(xbc[rows_dev - (CONV - 1) :], span, 1)
    extended = jnp.concatenate([rim_rows, xbc], axis=0)

    def conv_local(extended_in, conv_weight, conv_bias):
        return conv_apply(extended_in, conv_weight, conv_bias, positions)

    conv_values, conv_back = jax.vjp(
        conv_local, extended, small_f32[CONV_WEIGHT], small_f32[CONV_BIAS]
    )

    def ssd_full(conv_in, step_in, step_bias, decay_log, skip_gain, state_in):
        x_ssm, b_in, c_in = split_conv(conv_in)
        step_size = jax.nn.softplus(step_in + step_bias[None, :])
        decay = -jnp.exp(decay_log)
        output = ssd_output(
            x_ssm, b_in, c_in, step_size, decay, skip_gain, seq_id, positions, state_in
        )
        carry_all, local_state = ssd_summary(x_ssm, b_in, step_size, decay, seq_id, positions)
        return (
            output.reshape(rows_dev, ssm_inner),
            carry_all[:, None, None] * state_in + local_state,
        )

    x_ssm, b_in, c_in = split_conv(conv_values)
    step_size = jax.nn.softplus(step_raw + small_f32[STEP_BIAS][None, :])
    decay = -jnp.exp(small_f32[DECAY_LOG])
    carry_all, local_state = ssd_summary(x_ssm, b_in, step_size, decay, seq_id, positions)
    state_ident = (jnp.ones_like(carry_all), jnp.zeros_like(local_state))
    _, state_in = prefix((carry_all, local_state), span, chain_states, state_ident)
    (ssm_y, _), ssd_back = jax.vjp(
        ssd_full,
        conv_values,
        step_raw,
        small_f32[STEP_BIAS],
        small_f32[DECAY_LOG],
        small_f32[SKIP_GAIN],
        state_in,
    )
    normed_ssm, gnorm_back = jax.vjp(gated_norm, ssm_y, gate_ssm, small_f32[NORM_SSM])
    ssm_low = normed_ssm.astype(jnp.bfloat16)
    ssm_out = matmul(ssm_low, weights[W_SSM_OUT])
    middle = x_rows + attn_out + ssm_out
    normed_two, norm_two_back = jax.vjp(rms_norm, middle, small_f32[NORM_FFN])
    hidden_two = normed_two.astype(jnp.bfloat16)
    gate_ffn = matmul(hidden_two, weights[W_GATE])
    upper = matmul(hidden_two, weights[W_UP_PROJ])
    activation_f32, swiglu_back = jax.vjp(swiglu, gate_ffn, upper)
    activation = activation_f32.astype(jnp.bfloat16)
    ffn_out = matmul(activation, weights[W_DOWN])
    result = middle + ffn_out
    squares = jnp.stack(
        [
            jnp.sum(result * result),
            jnp.sum(attn_out * attn_out),
            jnp.sum(ssm_out * ssm_out),
            jnp.sum(ffn_out * ffn_out),
        ]
    )
    totals = sum_all(squares, group + span, fast)
    stats = jnp.sqrt(totals / (all_rows * D))
    back_weights = weights
    grad_out = cotangent.astype(jnp.float32)
    grad_activation = matmul_right_t(cotangent, back_weights[W_DOWN])
    grad_gate_f32, grad_upper_f32 = swiglu_back(grad_activation)
    grad_gate = grad_gate_f32.astype(jnp.bfloat16)
    grad_upper = grad_upper_f32.astype(jnp.bfloat16)
    grad_hidden_two = matmul_right_t(grad_gate, back_weights[W_GATE]) + matmul_right_t(
        grad_upper, back_weights[W_UP_PROJ]
    )
    grad_middle_norm, grad_norm_ffn = norm_two_back(grad_hidden_two)
    grad_middle = grad_out + grad_middle_norm
    grad_branch = grad_middle.astype(jnp.bfloat16)
    grad_attended = matmul_right_t(grad_branch, back_weights[W_ATTN_OUT]).astype(jnp.bfloat16)
    grad_ssm_low = matmul_right_t(grad_branch, back_weights[W_SSM_OUT])
    grad_ssm_y, grad_gate_ssm_f32, grad_norm_ssm = gnorm_back(grad_ssm_low)
    cumul = jnp.cumsum(step_size * decay[None, :], axis=0)
    entry_decay = ssd_entry(cumul, seq_id, positions)
    grad_y_heads = grad_ssm_y.reshape(rows_dev, SSM_HEADS, SSM_DIM)
    grad_state_local = jnp.einsum(
        "thp,tn,th->hpn", grad_y_heads, c_in, entry_decay, precision=highest
    )
    _, grad_state_out = carried_in((carry_all, grad_state_local), span, chain_states, state_ident)
    grad_conv_values, grad_step_raw_f32, grad_step_bias, grad_decay_log, grad_skip_gain, _ = (
        ssd_back((grad_ssm_y, grad_state_out))
    )
    grad_extended, grad_conv_weight, grad_conv_bias = conv_back(grad_conv_values)
    rim_back = passed_along(grad_extended[: CONV - 1], span, -1)
    grad_xbc_f32 = grad_extended[CONV - 1 :]
    grad_xbc_f32 = grad_xbc_f32.at[rows_dev - (CONV - 1) :].add(rim_back)
    grad_xbc = grad_xbc_f32.astype(jnp.bfloat16)
    grad_gate_ssm = grad_gate_ssm_f32.astype(jnp.bfloat16)
    grad_step_raw = grad_step_raw_f32.astype(jnp.bfloat16)
    grad_w_step = matmul_left_t(hidden, grad_step_raw)
    grad_hidden_ssm = (
        matmul_right_t(grad_gate_ssm, back_weights[W_GATE_SSM])
        + matmul_right_t(grad_xbc[:, :ssm_inner], back_weights[W_X_SSM])
        + matmul_right_t(grad_xbc[:, ssm_inner:], back_weights[W_B_C])
        + matmul_right_t(grad_step_raw, back_weights[W_STEP])
    )
    g_low = grad_attended.reshape(rows_dev, HEADS_Q, HEAD_DIM).transpose(1, 0, 2)
    g_wide = jnp.pad(g_low, ((0, 0), (0, 0), (HEAD_DIM, 0)))
    grad_kv, grad_q_turned = attention_backward(
        q_wide, g_wide, key_blocks, logs, mixed, meta, jnp.broadcast_to(row_starts[None, :], (8, rows_dev))
    )
    if rows_dev != KEYS:
        grad_kv = grad_kv.transpose(1, 0, 2, 3).reshape(HEADS_KV, -1, rows_dev, PAIR).transpose(1, 0, 2, 3)
    grad_kv_mine = scatter_span(grad_kv, span, fast)
    grad_keys_mine = grad_kv_mine[:, :, :HEAD_DIM].transpose(1, 0, 2).reshape(rows_dev, -1)
    grad_values_mine = grad_kv_mine[:, :, HEAD_DIM:].transpose(1, 0, 2).reshape(rows_dev, -1)
    grad_q_rot = grad_q_turned.transpose(2, 0, 1).reshape(rows_dev, HEADS_Q * HEAD_DIM) * score_scale
    grad_query_low = rotate(grad_q_rot, cosine, -sine, HEADS_Q).astype(jnp.bfloat16)
    grad_key_low = rotate(grad_keys_mine, cosine, -sine, HEADS_KV).astype(jnp.bfloat16)
    grad_value_low = grad_values_mine.astype(jnp.bfloat16)
    grad_hidden = (
        grad_hidden_ssm
        + matmul_right_t(grad_query_low, back_weights[W_QUERY])
        + matmul_right_t(grad_key_low, back_weights[W_KEY])
        + matmul_right_t(grad_value_low, back_weights[W_VALUE])
    )
    grad_x_norm, grad_norm_attn = norm_one_back(grad_hidden)
    grad_tokens = grad_middle + grad_x_norm
    small = {
        NORM_ATTN: grad_norm_attn,
        W_STEP: grad_w_step,
        CONV_WEIGHT: grad_conv_weight,
        CONV_BIAS: grad_conv_bias,
        STEP_BIAS: grad_step_bias,
        DECAY_LOG: grad_decay_log,
        SKIP_GAIN: grad_skip_gain,
        NORM_SSM: grad_norm_ssm,
        NORM_FFN: grad_norm_ffn,
    }
    pairs = {
        W_QUERY: (hidden, grad_query_low),
        W_KEY: (hidden, grad_key_low),
        W_VALUE: (hidden, grad_value_low),
        W_ATTN_OUT: (attended, grad_branch),
        W_GATE_SSM: (hidden, grad_gate_ssm),
        W_X_SSM: (hidden, grad_xbc[:, :ssm_inner]),
        W_B_C: (hidden, grad_xbc[:, ssm_inner:]),
        W_SSM_OUT: (ssm_low, grad_branch),
        W_GATE: (hidden_two, grad_gate),
        W_UP_PROJ: (hidden_two, grad_upper),
        W_DOWN: (activation, cotangent),
    }
    if fast:
        return (result.astype(jnp.bfloat16), grad_tokens, fast_gradients(small, pairs), stats)
    grad_dict = dict(small)
    for name_key, (left, right) in pairs.items():
        grad_dict[name_key] = matmul_left_t(left, right)
    flat_parts = [grad_dict[name_key].reshape(-1) for name_key, extent in layout()]
    used_entries = 0
    for part_array in flat_parts:
        used_entries += part_array.shape[0]
    flat_parts.append(jnp.zeros((params.shape[0] * lax.axis_size(group + span) - used_entries,), jnp.float32))
    grad_shard = lax.psum_scatter(
        jnp.concatenate(flat_parts), group + span, scatter_dimension=0, tiled=True
    )
    return (result.astype(jnp.bfloat16), grad_tokens, grad_shard, stats)


def solution(mesh):
    fast = (mesh.shape["group"], mesh.shape["span"]) == FAST
    if fast:
        mesh = Mesh(mesh.devices.reshape(4, 2, 2, 2), GRID)
        group, span = (GRID[:1], GRID[1:])
    else:
        group, span = (("group",), ("span",))

    def program(tokens, params, cotangent, offsets):
        return body(span, group, fast, tokens, params, cotangent, offsets)

    return jax.shard_map(
        program,
        mesh=mesh,
        in_specs=(P(group + span, None), P(group + span), P(group + span, None), P(group, None)),
        out_specs=(P(group + span, None), P(group + span, None), P(group + span), P()),
        check_vma=False,
    )
```

```python
import math

import jax
import jax.numpy as jnp
import numpy as np
from jax import lax
from jax.experimental import pallas as pl
from jax.experimental.pallas import tpu as pltpu
from jax.sharding import Mesh, PartitionSpec as P

D = 1024
HEADS_Q = 8
HEADS_KV = 2
HEAD_DIM = 64
SSM_HEADS = 24
SSM_DIM = 64
STATE = 128
CONV = 4
FF = 2048
(
    NORM_ATTN,
    W_QUERY,
    W_KEY,
    W_VALUE,
    W_ATTN_OUT,
    W_GATE_SSM,
    W_X_SSM,
    W_B_C,
    W_STEP,
    CONV_WEIGHT,
    CONV_BIAS,
    STEP_BIAS,
    DECAY_LOG,
    SKIP_GAIN,
    NORM_SSM,
    W_SSM_OUT,
    NORM_FFN,
    W_GATE,
    W_UP_PROJ,
    W_DOWN,
) = range(20)


epsilon = 1e-05
rope_base = 100000000000.0
masked_score = -1e30
highest = lax.Precision.HIGHEST
small_names = (
    NORM_ATTN,
    CONV_WEIGHT,
    CONV_BIAS,
    STEP_BIAS,
    DECAY_LOG,
    SKIP_GAIN,
    NORM_SSM,
    NORM_FFN,
)


def passed_along(value, axis, steps):
    count = lax.axis_size(axis)
    first, last = (max(0, -steps), min(count, count - steps))
    return lax.ppermute(value, axis, [(source, source + steps) for source in range(first, last)])


def prefix(value, axis, combine, identity):
    peers, place = (lax.axis_size(axis), lax.axis_index(axis))
    everything = jax.tree.map(
        lambda part, kind: lax.all_gather(part.astype(kind), axis),
        value,
        (jnp.bfloat16, jnp.bfloat16),
    )
    start = jax.tree.map(
        lambda part, zero: jnp.broadcast_to(jnp.asarray(zero, part.dtype), part.shape),
        value,
        identity,
    )

    def prefix_turn(k, before):
        reached = k < place
        new = combine(
            before, jax.tree.map(lambda part, own: part[k].astype(own.dtype), everything, value)
        )
        return jax.tree.map(lambda a, b: jnp.where(reached, a, b), new, before)

    return lax.fori_loop(0, peers, prefix_turn, start)


def carried_in(value, axis, combine, identity):
    peers, place = (lax.axis_size(axis), lax.axis_index(axis))
    everything = jax.tree.map(
        lambda part, kind: lax.all_gather(part.astype(kind), axis),
        value,
        jax.tree.map(lambda a: jnp.bfloat16 if a.dtype == jnp.float32 else a.dtype, value),
    )
    start = jax.tree.map(
        lambda part, zero: jnp.broadcast_to(jnp.asarray(zero, part.dtype), part.shape),
        value,
        identity,
    )

    def carried_turn(k, before):
        at = peers - 1 - k
        reached = at > place
        new = combine(
            before, jax.tree.map(lambda part, own: part[at].astype(own.dtype), everything, value)
        )
        return jax.tree.map(lambda a, b: jnp.where(reached, a, b), new, before)

    return lax.fori_loop(0, peers, carried_turn, start)


def layout():
    ssm_inner = SSM_HEADS * SSM_DIM
    channels = ssm_inner + 2 * STATE
    return [
        (NORM_ATTN, (D,)),
        (W_QUERY, (D, HEADS_Q * HEAD_DIM)),
        (W_KEY, (D, HEADS_KV * HEAD_DIM)),
        (W_VALUE, (D, HEADS_KV * HEAD_DIM)),
        (W_ATTN_OUT, (HEADS_Q * HEAD_DIM, D)),
        (W_GATE_SSM, (D, ssm_inner)),
        (W_X_SSM, (D, ssm_inner)),
        (W_B_C, (D, 2 * STATE)),
        (W_STEP, (D, SSM_HEADS)),
        (CONV_WEIGHT, (CONV, channels)),
        (CONV_BIAS, (channels,)),
        (STEP_BIAS, (SSM_HEADS,)),
        (DECAY_LOG, (SSM_HEADS,)),
        (SKIP_GAIN, (SSM_HEADS,)),
        (NORM_SSM, (ssm_inner,)),
        (W_SSM_OUT, (ssm_inner, D)),
        (NORM_FFN, (D,)),
        (W_GATE, (D, FF)),
        (W_UP_PROJ, (D, FF)),
        (W_DOWN, (FF, D)),
    ]


def unpack(flat_vector):
    unpacked = {}
    offset = 0
    for name_key, extent in layout():
        amount = math.prod(extent)
        unpacked[name_key] = flat_vector[offset : offset + amount].reshape(extent)
        offset += amount
    return unpacked


def matmul(left, right):
    return jnp.dot(left, right, preferred_element_type=jnp.float32)


def matmul_left_t(left, right):
    return lax.dot_general(
        left, right, (((0,), (0,)), ((), ())), preferred_element_type=jnp.float32
    )


def matmul_right_t(left, right):
    return lax.dot_general(
        left, right, (((1,), (1,)), ((), ())), preferred_element_type=jnp.float32
    )


def rms_norm(values, gain):
    return values * lax.rsqrt(jnp.mean(values * values, axis=-1, keepdims=True) + epsilon) * gain


def gated_norm(ssm_y, gate_ssm, gain):
    return rms_norm(ssm_y * jax.nn.silu(gate_ssm), gain)


def swiglu(gate_ffn, upper):
    return jax.nn.silu(gate_ffn) * upper


def sequence_info(row_index, bounds):
    starts = bounds[:-1]
    inside = row_index[:, None] >= starts[None, :]
    seq_id = jnp.sum(inside.astype(jnp.int32), axis=1) - 1
    seq_start = jnp.max(jnp.where(inside, starts[None, :], 0), axis=1)
    return (seq_id, row_index - seq_start)


def rotary_tables(positions):
    half_dim = HEAD_DIM // 2
    freqs = jnp.exp(
        -jnp.arange(half_dim, dtype=jnp.float32) * (2.0 * math.log(rope_base) / HEAD_DIM)
    )
    angles = positions.astype(jnp.float32)[:, None] * freqs[None, :]
    return (jnp.cos(angles), jnp.sin(angles))


def rotate(values, cosine, sine, heads):
    row_count = values.shape[0]
    half_dim = HEAD_DIM // 2
    split_heads = values.reshape(row_count, heads, HEAD_DIM)
    first_half = split_heads[..., :half_dim]
    second_half = split_heads[..., half_dim:]
    cos_b = cosine[:, None, :]
    sin_b = sine[:, None, :]
    turned = jnp.concatenate(
        [first_half * cos_b - second_half * sin_b, second_half * cos_b + first_half * sin_b],
        axis=-1,
    )
    return turned.reshape(row_count, heads * HEAD_DIM)


def conv_apply(extended, conv_weight, conv_bias, positions):
    row_count = positions.shape[0]
    conv_total = conv_bias[None, :]
    for tap_index in range(CONV):
        window = extended[tap_index : tap_index + row_count]
        valid_rows = (positions >= CONV - 1 - tap_index)[:, None]
        conv_total = (
            conv_total + jnp.where(valid_rows, window, 0.0) * conv_weight[tap_index][None, :]
        )
    return jax.nn.silu(conv_total)


def add_rows(target, addend, first_row):
    current = lax.dynamic_slice_in_dim(target, first_row, addend.shape[0], 0)
    return lax.dynamic_update_slice_in_dim(target, current + addend, first_row, 0)


FAST = (4, 8)
LINE = 128
SHARD = 3082
SPAD = 3088
WIN = 3104
PLANE = 8 * SHARD
DEPTH = 4
TALL = {1: 1024, 2: 1024, 4: 512, 8: 256, 12: 128, 16: 128}
GRID = ("z", "y", "x", "c")
ZC = ("z", "c")
SWAP = [(0, 1), (1, 0)]


def zc_pairs(*pairs):
    return [(2 * a + c, 2 * b + c) for a, b, c in pairs]


def gather_lines(params):
    z, y, x, c = (lax.axis_index(name) for name in GRID)
    lines = jnp.pad(params.reshape(SHARD, LINE), ((0, SPAD - SHARD), (0, 0)))
    sibling = lax.ppermute(lines, ZC, [(2 * k + 1 - k % 2, 2 * k + k % 2) for k in range(4)])
    batches = []
    for batch in range(2):
        buffers = []
        for part in range(2):
            here = jnp.where(c == part, lines, sibling)
            if batch == 0:
                one = lax.ppermute(here, ZC, zc_pairs((0, 1, 0), (1, 2, 1)))
                side = lax.ppermute(here, ZC, zc_pairs((1, 0, 1)))
                two = lax.ppermute(one, ZC, zc_pairs((1, 2, 0), (2, 3, 1)))
                three = lax.ppermute(two, ZC, zc_pairs((2, 3, 0)))
            else:
                one = lax.ppermute(here, ZC, zc_pairs((2, 1, 0), (3, 2, 1)))
                side = lax.ppermute(here, ZC, zc_pairs((2, 3, 0)))
                two = lax.ppermute(one, ZC, zc_pairs((1, 0, 0), (2, 1, 1)))
                three = lax.ppermute(two, ZC, zc_pairs((1, 0, 1)))
            mine = z == 2 * batch + c
            column = jnp.where(mine, here, one + side + two + three)
            over_x = lax.ppermute(column, "x", SWAP)
            over_y = lax.ppermute(column, "y", SWAP)
            if part == 0:
                corner = lax.ppermute(over_x, "y", SWAP)
            else:
                corner = lax.ppermute(over_y, "x", SWAP)
            local = [column, over_x, over_y, corner]
            buffers += local + [lax.ppermute(piece, "c", SWAP) for piece in local]
        batches.append(buffers)
    shard = np.arange(32)
    sz, sy, sx, sc = shard // 8, shard // 4 % 2, shard // 2 % 2, shard % 2
    away = jnp.where(sz % 2 == c, 0, 4)
    where = sc * 8 + away + 2 * (sy ^ y) + (sx ^ x) + 16 * (sz // 2)
    return batches, where.astype(jnp.int32)


def unpack_lines(buffers, first, where, segments):
    jobs, starts = [], []
    reach = 0
    for offset, rows, columns in segments:
        per_row = columns // LINE
        lane, base = offset % LINE, offset // LINE
        if per_row == 1 and rows < 1024:
            lane, tall = 0, rows
        else:
            tall = TALL[per_row]
        starts.append(len(jobs))
        for k in range(rows // tall):
            jobs.append((base + k * tall * per_row, tall * per_row, 1 if lane else 0))
    window = max(job[1] for job in jobs) + 32
    table = np.zeros((len(jobs), 5), np.int32)
    for k, (line, count, extra) in enumerate(jobs):
        owner = line // SHARD
        inside = line - owner * SHARD
        begin = min(inside // 16 * 16, SPAD - window)
        crosses = int(line + count + extra > (owner + 1) * SHARD)
        table[k] = (owner, begin, begin - inside, crosses, (owner + 1) * SHARD - line)
    base_row = (int(-table[:, 2].min()) + 7) // 8 * 8
    table[:, 2] += base_row
    table[:, 4] += base_row
    room = int(max((table[:, 2] + window).max(), ((table[:, 4] + window) * table[:, 3]).max()))
    room = (room + 15) // 8 * 8
    total = len(jobs)
    count_buffers = len(buffers)
    shapes = []
    for offset, rows, columns in segments:
        per_row = columns // LINE
        tall = rows if per_row == 1 and rows < 1024 else TALL[per_row]
        shapes.append((rows, columns, tall, per_row, offset % LINE if tall != rows or per_row != 1 else 0))
    sizes = sorted({(tall, columns) for _, columns, tall, _, _ in shapes})

    def kernel(table_ref, where_ref, *refs):
        sources = refs[:count_buffers]
        outs = refs[count_buffers : count_buffers + len(segments)]
        rest = refs[count_buffers + len(segments) :]
        stages = dict(zip(sizes, rest))
        raw, flat, in_sem, out_sem = rest[len(sizes) :]
        step = pl.program_id(0)

        def fetch(job, slot):
            owner = table_ref[job, 0]
            begin = pl.multiple_of(table_ref[job, 1], 16)
            for b in range(count_buffers):

                @pl.when(where_ref[owner] == first + b)
                def _():
                    pltpu.make_async_copy(
                        sources[b].at[pl.ds(begin, window), :], raw.at[slot, 0], in_sem.at[slot, 0]
                    ).start()

            @pl.when(table_ref[job, 3] == 1)
            def _():
                for b in range(count_buffers):

                    @pl.when(where_ref[owner + 1] == first + b)
                    def _():
                        pltpu.make_async_copy(
                            sources[b].at[pl.ds(0, window), :], raw.at[slot, 1], in_sem.at[slot, 1]
                        ).start()

        def fetched(slot, half):
            return pltpu.make_async_copy(
                sources[0].at[pl.ds(0, window), :], raw.at[slot, half], in_sem.at[slot, half]
            )

        @pl.when(step == 0)
        def _():
            for k in range(min(DEPTH - 1, total)):
                fetch(k, k)

        @pl.when(step + DEPTH - 1 < total)
        def _():
            fetch(step + DEPTH - 1, lax.rem(step + DEPTH - 1, DEPTH))

        slot = lax.rem(step, DEPTH)
        fetched(slot, 0).wait()
        flat[pl.ds(table_ref[step, 2], window), :] = raw[slot, 0].astype(jnp.float32)

        @pl.when(table_ref[step, 3] == 1)
        def _():
            fetched(slot, 1).wait()
            flat[pl.ds(table_ref[step, 4], window), :] = raw[slot, 1].astype(jnp.float32)

        for index, (rows, columns, tall, per_row, lane) in enumerate(shapes):
            begin = starts[index]
            blocks = rows // tall
            stage = stages[(tall, columns)]

            @pl.when((step >= begin) & (step < begin + blocks))
            def _():
                block = step - begin
                side = lax.rem(block, 2)

                def written(k, s):
                    return pltpu.make_async_copy(
                        stage.at[s],
                        outs[index].at[pl.ds(pl.multiple_of(k * tall, 16), tall), :],
                        out_sem.at[s],
                    )

                @pl.when(block >= 2)
                def _():
                    written(block - 2, side).wait()

                def tile(j):
                    picked = flat[pl.ds(base_row + j, tall, stride=per_row), :]
                    return pltpu.roll(picked, LINE - lane, 1) if lane else picked

                if lane:
                    lanes = lax.broadcasted_iota(jnp.int32, (tall, LINE), 1)
                    now = tile(0)
                    for j in range(per_row):
                        later = tile(j + 1)
                        stage[side, :, j * LINE : (j + 1) * LINE] = jnp.where(
                            lanes < LINE - lane, now, later
                        ).astype(jnp.bfloat16)
                        now = later
                else:
                    for j in range(per_row):
                        stage[side, :, j * LINE : (j + 1) * LINE] = tile(j).astype(jnp.bfloat16)
                written(block, side).start()

                @pl.when(block == blocks - 1)
                def _():
                    if blocks > 1:
                        written(block - 1, 1 - side).wait()
                    written(block, side).wait()

    return pl.pallas_call(
        kernel,
        grid_spec=pltpu.PrefetchScalarGridSpec(
            num_scalar_prefetch=2,
            grid=(total,),
            in_specs=[pl.BlockSpec(memory_space=pl.ANY)] * count_buffers,
            out_specs=[pl.BlockSpec(memory_space=pl.ANY)] * len(segments),
            scratch_shapes=[pltpu.VMEM((2,) + size, jnp.bfloat16) for size in sizes]
            + [
                pltpu.VMEM((DEPTH, 2, window, LINE), jnp.bfloat16),
                pltpu.VMEM((room, LINE), jnp.float32),
                pltpu.SemaphoreType.DMA((DEPTH, 2)),
                pltpu.SemaphoreType.DMA((2,)),
            ],
        ),
        out_shape=[jax.ShapeDtypeStruct((rows, columns), jnp.bfloat16) for _, rows, columns in segments],
        compiler_params=pltpu.CompilerParams(vmem_limit_bytes=48 * 2**20),
        cost_estimate=pl.CostEstimate(flops=0, bytes_accessed=total * window * LINE * 4, transcendentals=0),
        name="unpack",
    )(jnp.asarray(table), where, *buffers)


def pack_lines(target, target_rows, first_row, segments, lane, phase, extras, carry, tail_rows):
    tall = 256
    lefts, rights, plan = [], [], []
    left_of, right_of = {}, {}
    row = first_row
    begin = 0
    for left, right in segments:
        for value, seen, kept in ((left, left_of, lefts), (right, right_of, rights)):
            if id(value) not in seen:
                seen[id(value)] = len(kept)
                kept.append(value)
        blocks = left.shape[1] // tall
        plan.append((left_of[id(left)], right_of[id(right)], right.shape[1] // LINE, begin, blocks, row))
        begin += blocks
        row += left.shape[1] * right.shape[1] // LINE
    end_row = row
    total = begin
    biggest = max(entry[2] for entry in plan) * tall
    tokens = lefts[0].shape[0]
    count_left, count_right, count_extra = len(lefts), len(rights), len(extras)
    rolled = [jnp.roll(right, lane, axis=1) if lane else right for right in rights]
    carry_in = [carry] if lane else []
    targets = [] if target is None else [target]

    def left_spec(index):
        mine = [entry for entry in plan if entry[0] == index]

        def place(step):
            block = 0
            for _, _, _, start, blocks, _ in mine:
                block = jnp.where(step >= start, jnp.minimum(step - start, blocks - 1), block)
            return (0, block)

        return pl.BlockSpec((tokens, tall), place)

    def kernel(*refs):
        left_refs = refs[:count_left]
        right_refs = refs[count_left : count_left + count_right]
        at = count_left + count_right
        extra_refs = refs[at : at + count_extra]
        at += count_extra
        carry_refs = refs[at : at + len(carry_in)]
        at += len(carry_in) + len(targets)
        out = refs[at]
        flat, stage, shift, last, sems, extra_sems = refs[at + 1 :]
        step = pl.program_id(0)
        side = lax.rem(step, 2)

        def extra_copy(k):
            rows = extras[k][0].shape[0]
            return pltpu.make_async_copy(
                extra_refs[k], out.at[pl.ds(extras[k][1], rows), :], extra_sems.at[k]
            )

        @pl.when(step == 0)
        def _():
            for k in range(count_extra):
                extra_copy(k).start()
            if lane:
                shift[0:8, :] = carry_refs[0][...]
            if phase:
                flat[0:8, :] = jnp.zeros((8, LINE), jnp.float32)

        for left_at, right_at, per_row, start, blocks, row in plan:
            lines = per_row * tall

            def written(block, s, row=row, lines=lines):
                return pltpu.make_async_copy(
                    stage.at[s, pl.ds(0, lines), :],
                    out.at[pl.ds(pl.multiple_of(row + block * lines, 16), lines), :],
                    sems.at[s],
                )

            @pl.when((step >= start) & (step < start + blocks))
            def _():
                block = step - start
                if phase:

                    @pl.when(step > 0)
                    def _():
                        flat[0:8, :] = flat[lines : lines + 8, :]

                turned = left_refs[left_at][...].T
                lanes = lax.broadcasted_iota(jnp.int32, (tall, LINE), 1)
                for j0 in range(0, per_row, 2):
                    wide = min(2, per_row - j0)
                    tile = jnp.dot(
                        turned,
                        right_refs[right_at][:, j0 * LINE : (j0 + wide) * LINE],
                        preferred_element_type=jnp.float32,
                    )
                    for j in range(wide):
                        piece = tile[:, j * LINE : (j + 1) * LINE]
                        if lane and j0 + j == 0:
                            shift[8 : 8 + tall, :] = piece
                            piece = jnp.where(lanes < lane, shift[7 : 7 + tall, :], piece)
                            shift[0:8, :] = shift[tall : tall + 8, :]
                        if per_row == 1:
                            flat[phase : phase + tall, :] = piece
                        else:
                            flat[pl.ds(phase + j0 + j, tall, stride=per_row), :] = piece

                stage[side, 0:lines, :] = flat[0:lines, :].astype(jnp.bfloat16)
                written(block, side).start()

            @pl.when((step > start) & (step <= start + blocks))
            def _():
                written(step - start - 1, 1 - side).wait()

            if start + blocks == total:

                @pl.when(step == total - 1)
                def _():
                    written(blocks - 1, side).wait()

        @pl.when(step == total - 1)
        def _():
            if tail_rows:
                lanes = lax.broadcasted_iota(jnp.int32, (tail_rows, LINE), 1)
                rows_at = lax.broadcasted_iota(jnp.int32, (tail_rows, LINE), 0)
                final = jnp.broadcast_to(shift[7:8, :], (tail_rows, LINE))
                last[...] = jnp.where((rows_at == 0) & (lanes < lane), final, 0.0).astype(jnp.bfloat16)
                closing = pltpu.make_async_copy(
                    last, out.at[pl.ds(end_row, tail_rows), :], extra_sems.at[count_extra]
                )
                closing.start()
                closing.wait()
            for k in range(count_extra):
                extra_copy(k).wait()

    whole = [pl.BlockSpec(array.shape, lambda step: (0, 0)) for array in rolled]
    flops = sum(2 * tokens * entry[4] * tall * entry[2] * LINE for entry in plan)
    return pl.pallas_call(
        kernel,
        grid=(total,),
        in_specs=[left_spec(k) for k in range(count_left)]
        + whole
        + [pl.BlockSpec(array.shape, lambda step: (0, 0)) for array, _ in extras]
        + [pl.BlockSpec(array.shape, lambda step: (0, 0)) for array in carry_in]
        + [pl.BlockSpec(memory_space=pl.ANY)] * len(targets),
        out_specs=pl.BlockSpec(memory_space=pl.ANY),
        out_shape=jax.ShapeDtypeStruct((target_rows, LINE), jnp.bfloat16),
        scratch_shapes=[
            pltpu.VMEM((biggest + 16, LINE), jnp.float32),
            pltpu.VMEM((2, biggest, LINE), jnp.bfloat16),
            pltpu.VMEM((tall + 8, LINE), jnp.float32),
            pltpu.VMEM((max(tail_rows, 16), LINE), jnp.bfloat16),
            pltpu.SemaphoreType.DMA((2,)),
            pltpu.SemaphoreType.DMA((count_extra + 1,)),
        ],
        input_output_aliases={count_left + count_right + count_extra + len(carry_in): 0} if targets else {},
        compiler_params=pltpu.CompilerParams(vmem_limit_bytes=48 * 2**20),
        cost_estimate=pl.CostEstimate(flops=flops, bytes_accessed=total * biggest * LINE * 2, transcendentals=0),
        name="pack",
    )(*lefts, *rolled, *[array for array, _ in extras], *carry_in, *targets)


def added(*parts):
    total = parts[0].astype(jnp.float32)
    for part in parts[1:]:
        total = total + part.astype(jnp.float32)
    return total.astype(jnp.bfloat16)


def reduce_lines(flat, batch, shift):
    z, y, x, c = (lax.axis_index(name) for name in GRID)
    length = PLANE + 32
    keep = lax.dynamic_slice(flat, (c * PLANE, 0), (length, LINE))
    send = lax.dynamic_slice(flat, ((1 - c) * PLANE, 0), (length, LINE))
    chip = added(keep, lax.ppermute(send, "c", SWAP))

    def window(sy, sx, part):
        shard = sy * 4 + sx * 2 + part
        start = (shift + SHARD * shard) // 16 * 16
        return lax.dynamic_slice(chip, (start, 0), (WIN, LINE))

    ends = []
    for part in range(2):
        if part == 0:
            away = jnp.stack([window(1 - y, 0, part), window(1 - y, 1, part)])
            home = jnp.stack([window(y, 0, part), window(y, 1, part)])
            first_axis, second_axis, place = "y", "x", x
        else:
            away = jnp.stack([window(0, 1 - x, part), window(1, 1 - x, part)])
            home = jnp.stack([window(0, x, part), window(1, x, part)])
            first_axis, second_axis, place = "x", "y", y
        half = added(home, lax.ppermute(away, first_axis, SWAP))
        other = lax.dynamic_index_in_dim(half, 1 - place, 0, keepdims=False)
        mine = lax.dynamic_index_in_dim(half, place, 0, keepdims=False)
        column = added(mine, lax.ppermute(other, second_axis, SWAP))
        if batch == 0:
            one = added(column, lax.ppermute(column, ZC, zc_pairs((3, 2, 0), (3, 2, 1))))
            side = lax.ppermute(column, ZC, zc_pairs((0, 1, 1)))
            two = added(one, lax.ppermute(one, ZC, zc_pairs((2, 1, 0), (2, 1, 1))), side)
            end = added(two, lax.ppermute(two, ZC, zc_pairs((1, 0, 0))))
        else:
            one = added(column, lax.ppermute(column, ZC, zc_pairs((0, 1, 0), (0, 1, 1))))
            side = lax.ppermute(column, ZC, zc_pairs((3, 2, 0)))
            two = added(one, lax.ppermute(one, ZC, zc_pairs((1, 2, 0), (1, 2, 1))), side)
            end = added(two, lax.ppermute(two, ZC, zc_pairs((2, 3, 1))))
        ends.append(end)
    mine = jnp.where(c == 0, ends[0], ends[1])
    other = jnp.where(c == 0, ends[1], ends[0])
    holders = [(2 * k + k % 2, 2 * k + 1 - k % 2) for k in range(4)]
    handed = lax.ppermute(other, ZC, holders)
    return jnp.where(c == z % 2, mine, handed)


CHUNK = 128
NT = (((1,), (1,)), ((), ()))
TN = (((0,), (0,)), ((), ()))
INNER = SSM_HEADS * SSM_DIM
PAIRS = SSM_HEADS // 2


def spread(rows_a, rows_b):
    length = rows_a.shape[1]
    tall = jnp.concatenate(
        [jnp.broadcast_to(rows_a, (SSM_DIM, length)), jnp.broadcast_to(rows_b, (SSM_DIM, length))], axis=0
    )
    return tall.T


def weighted_state(left, values, weight_rows):
    rows = left.shape[0]

    def kernel(left_ref, value_ref, weight_ref, out_ref):
        wide = spread(weight_ref[0, 0:1, :], weight_ref[0, 1:2, :])
        scaled = (value_ref[...] * wide).astype(jnp.bfloat16)
        out_ref[...] = lax.dot_general(
            left_ref[...].astype(jnp.bfloat16), scaled, TN, preferred_element_type=jnp.float32
        )

    return pl.pallas_call(
        kernel,
        grid=(PAIRS,),
        in_specs=[
            pl.BlockSpec((rows, STATE), lambda i: (0, 0)),
            pl.BlockSpec((rows, 2 * SSM_DIM), lambda i: (0, i)),
            pl.BlockSpec((1, 2, rows), lambda i: (i, 0, 0)),
        ],
        out_specs=pl.BlockSpec((STATE, 2 * SSM_DIM), lambda i: (0, i)),
        out_shape=jax.ShapeDtypeStruct((STATE, INNER), jnp.float32),
        cost_estimate=pl.CostEstimate(flops=2 * rows * STATE * INNER, bytes_accessed=rows * INNER * 4, transcendentals=0),
        name="state",
    )(left, values, weight_rows.reshape(PAIRS, 2, rows))


def chunk_rows(k, meta_ref, cum_ref, start_ref):
    here = slice(k * CHUNK, (k + 1) * CHUNK)
    first = meta_ref[0] + k * CHUNK
    index = first + lax.broadcasted_iota(jnp.int32, (1, CHUNK), 1)
    entering = start_ref[0:1, here] < first
    ending = index >= meta_ref[1 + k]
    cums, entries, tails = [], [], []
    for e in range(2):
        cum = cum_ref[0, e : e + 1, here]
        cums.append(cum)
        entries.append(jnp.where(entering, jnp.exp(cum), 0.0))
        gap = jnp.where(ending, cum[:, CHUNK - 1 :] - cum, masked_score)
        tails.append(jnp.exp(gap))
    return cums, entries, tails


def ssm_forward(x, b_in, c_in, cum, step, state_in, skip, meta, start_column, start_row):
    rows = x.shape[0]
    chunks = rows // CHUNK

    def kernel(meta_ref, x_ref, b_ref, c_ref, cum_ref, step_ref, state_ref, skip_ref, col_ref, row_ref,
               y_ref, inner, hide, state):
        @pl.when(pl.program_id(0) == 0)
        def _():
            for k in range(chunks):
                here = slice(k * CHUNK, (k + 1) * CHUNK)
                inner[k] = lax.dot_general(
                    c_ref[here, :], b_ref[here, :], NT, precision=highest, preferred_element_type=jnp.float32
                )
                t = lax.broadcasted_iota(jnp.int32, (CHUNK, CHUNK), 0)
                s = lax.broadcasted_iota(jnp.int32, (CHUNK, CHUNK), 1)
                shown = (s <= t) & (meta_ref[0] + k * CHUNK + s >= col_ref[here, :])
                hide[k] = jnp.where(shown, 0.0, masked_score)

        low_lane = lax.broadcasted_iota(jnp.int32, (CHUNK, 2 * SSM_DIM), 1) < SSM_DIM
        state[...] = state_ref[...]
        for k in range(chunks):
            here = slice(k * CHUNK, (k + 1) * CHUNK)
            cums, entries, tails = chunk_rows(k, meta_ref, cum_ref, row_ref)
            x_now = x_ref[here, :]
            x_low = x_now.astype(jnp.bfloat16)
            entry = spread(*entries)
            weight = spread(*[tails[e] * step_ref[0, e : e + 1, here] for e in range(2)])
            parts = []
            for e in range(2):
                across = jnp.broadcast_to(cums[e], (CHUNK, CHUNK))
                decays = jnp.exp(across.T - across + hide[k])
                mix = (inner[k] * decays * step_ref[0, e : e + 1, here]).astype(jnp.bfloat16)
                parts.append(jnp.dot(mix, x_low, preferred_element_type=jnp.float32))
            carried = jnp.dot(
                c_ref[here, :].astype(jnp.bfloat16), state[...].astype(jnp.bfloat16),
                preferred_element_type=jnp.float32,
            )
            y_ref[here, :] = jnp.where(low_lane, parts[0], parts[1]) + entry * carried + skip_ref[...] * x_now
            fresh = lax.dot_general(
                b_ref[here, :].astype(jnp.bfloat16), (x_now * weight).astype(jnp.bfloat16), TN,
                preferred_element_type=jnp.float32,
            )
            state[...] = entry[CHUNK - 1 :, :] * state[...] + fresh

    whole = lambda i, m: (0, 0)
    lanes = lambda i, m: (0, i)
    return pl.pallas_call(
        kernel,
        grid_spec=pltpu.PrefetchScalarGridSpec(
            num_scalar_prefetch=1,
            grid=(PAIRS,),
            in_specs=[
                pl.BlockSpec((rows, 2 * SSM_DIM), lanes),
                pl.BlockSpec((rows, STATE), whole),
                pl.BlockSpec((rows, STATE), whole),
                pl.BlockSpec((1, 2, rows), lambda i, m: (i, 0, 0)),
                pl.BlockSpec((1, 2, rows), lambda i, m: (i, 0, 0)),
                pl.BlockSpec((STATE, 2 * SSM_DIM), lanes),
                pl.BlockSpec((1, 2 * SSM_DIM), lanes),
                pl.BlockSpec((rows, 1), whole),
                pl.BlockSpec((8, rows), whole),
            ],
            out_specs=pl.BlockSpec((rows, 2 * SSM_DIM), lanes),
            scratch_shapes=[
                pltpu.VMEM((chunks, CHUNK, CHUNK), jnp.float32),
                pltpu.VMEM((chunks, CHUNK, CHUNK), jnp.float32),
                pltpu.VMEM((STATE, 2 * SSM_DIM), jnp.float32),
            ],
        ),
        out_shape=jax.ShapeDtypeStruct((rows, INNER), jnp.float32),
        compiler_params=pltpu.CompilerParams(vmem_limit_bytes=40 * 2**20),
        cost_estimate=pl.CostEstimate(flops=10**9, bytes_accessed=rows * INNER * 8, transcendentals=2**21),
        name="ssm",
    )(meta, x, b_in, c_in, cum.reshape(PAIRS, 2, rows), step.reshape(PAIRS, 2, rows), state_in, skip,
      start_column, start_row)


def ssm_backward(x, dy, b_in, c_in, cum, step, state_in, state_grad, skip, meta, start_row):
    rows = x.shape[0]
    chunks = rows // CHUNK

    def kernel(meta_ref, x_ref, dy_ref, b_ref, c_ref, cum_ref, step_ref, state_ref, grad_ref, skip_ref, row_ref,
               dx_ref, db_ref, dc_ref, small_ref, inner, hide, inner_grad, states, flow):
        low = lambda v: v.astype(jnp.bfloat16)
        dot = lambda p, q, dims=(((1,), (0,)), ((), ())): lax.dot_general(
            p, q, dims, preferred_element_type=jnp.float32
        )
        exact = lambda p, q, dims=(((1,), (0,)), ((), ())): lax.dot_general(
            p, q, dims, precision=highest, preferred_element_type=jnp.float32
        )
        s = lax.broadcasted_iota(jnp.int32, (CHUNK, CHUNK), 0)
        t = lax.broadcasted_iota(jnp.int32, (CHUNK, CHUNK), 1)

        @pl.when(pl.program_id(0) == 0)
        def _():
            db_ref[...] = jnp.zeros(db_ref.shape, jnp.float32)
            dc_ref[...] = jnp.zeros(dc_ref.shape, jnp.float32)
            inner_grad[...] = jnp.zeros(inner_grad.shape, jnp.float32)
            for k in range(chunks):
                here = slice(k * CHUNK, (k + 1) * CHUNK)
                inner[k] = exact(b_ref[here, :], c_ref[here, :], NT)
                shown = (s <= t) & (meta_ref[0] + k * CHUNK + s >= row_ref[0:1, here])
                hide[k] = jnp.where(shown, 0.0, masked_score)

        before = (s < t).astype(jnp.float32)
        until = low((s >= t).astype(jnp.float32))
        low_lane = t < SSM_DIM
        pick_row = lax.broadcasted_iota(jnp.int32, (8, 2 * SSM_DIM), 0)
        pick_lane = lax.broadcasted_iota(jnp.int32, (8, 2 * SSM_DIM), 1) // SSM_DIM
        pick = low((pick_row == pick_lane).astype(jnp.float32))
        spreads = []
        states[0] = state_ref[...]
        for k in range(chunks):
            here = slice(k * CHUNK, (k + 1) * CHUNK)
            cums, entries, tails = chunk_rows(k, meta_ref, cum_ref, row_ref)
            entry, tail = spread(*entries), spread(*tails)
            steps = spread(step_ref[0, 0:1, here], step_ref[0, 1:2, here])
            spreads.append((cums, entry, tail, steps))
            if k < chunks - 1:
                fresh = dot(low(b_ref[here, :]), low(x_ref[here, :] * steps * tail), TN)
                states[k + 1] = entry[CHUNK - 1 :, :] * states[k] + fresh
        flow[...] = grad_ref[...]
        skip_sum = jnp.zeros((1, 2 * SSM_DIM), jnp.float32)
        for k in reversed(range(chunks)):
            here = slice(k * CHUNK, (k + 1) * CHUNK)
            cums, entry, tail, steps = spreads[k]
            x_now, dy_now = x_ref[here, :], dy_ref[here, :]
            b_low, c_low = low(b_ref[here, :]), low(c_ref[here, :])
            scaled = x_now * steps
            dy_low = low(dy_now)
            flow_low, state_low = low(flow[...]), low(states[k])
            mixed, within = [], []
            for e in range(2):
                across = jnp.broadcast_to(cums[e], (CHUNK, CHUNK))
                decays = jnp.exp(across - across.T + hide[k])
                own = low(jnp.where(low_lane == (e == 0), scaled, 0.0))
                reach = decays * dot(own, dy_low, NT)
                inner_grad[k] += reach
                sums = dot(low(inner[k] * reach), until)
                within.append(jnp.sum(sums * before, axis=0, keepdims=True))
                mixed.append(dot(low(inner[k] * decays), dy_low))
            back = tail * dot(b_low, flow_low)
            dxs = jnp.where(low_lane, mixed[0], mixed[1]) + back
            db_ref[here, :] += dot(low(scaled * tail), flow_low, NT)
            entered = low(dy_now * entry)
            dc_ref[here, :] += dot(entered, state_low, NT)
            brought = dy_now * entry * dot(c_low, state_low)
            ends = dot(pick, low(brought), NT)
            begins = dot(pick, low(scaled * back), NT)
            direct = dot(pick, low(x_now * dxs), NT)
            through = jnp.sum(flow[...] * states[k], axis=0, keepdims=True) * entry[CHUNK - 1 :, :]
            log_grad = exact(ends, until.astype(jnp.float32)) + exact(begins, before)
            for e in range(2):
                lanes = slice(e * SSM_DIM, (e + 1) * SSM_DIM)
                kept = jnp.sum(through[:, lanes], axis=1, keepdims=True)
                small_ref[0, e : e + 1, here] = direct[e : e + 1, :]
                small_ref[0, 2 + e : 3 + e, here] = log_grad[e : e + 1, :] + within[e] + kept
            dx_ref[here, :] = dxs * steps + skip_ref[...] * dy_now
            skip_sum += jnp.sum(x_now * dy_now, axis=0, keepdims=True)
            flow[...] = entry[CHUNK - 1 :, :] * flow[...] + dot(c_low, entered, TN)
        small_ref[0, 4:8, :] = jnp.zeros((4, rows), jnp.float32)
        small_ref[0, 4:5, 0 : 2 * SSM_DIM] = skip_sum

        @pl.when(pl.program_id(0) == PAIRS - 1)
        def _():
            for k in range(chunks):
                here = slice(k * CHUNK, (k + 1) * CHUNK)
                grads = low(inner_grad[k])
                db_ref[here, :] += dot(grads, low(c_ref[here, :]))
                dc_ref[here, :] += dot(grads, low(b_ref[here, :]), TN)

    whole = lambda i, m: (0, 0)
    lanes = lambda i, m: (0, i)
    pair = lambda i, m: (i, 0, 0)
    return pl.pallas_call(
        kernel,
        grid_spec=pltpu.PrefetchScalarGridSpec(
            num_scalar_prefetch=1,
            grid=(PAIRS,),
            in_specs=[
                pl.BlockSpec((rows, 2 * SSM_DIM), lanes),
                pl.BlockSpec((rows, 2 * SSM_DIM), lanes),
                pl.BlockSpec((rows, STATE), whole),
                pl.BlockSpec((rows, STATE), whole),
                pl.BlockSpec((1, 2, rows), pair),
                pl.BlockSpec((1, 2, rows), pair),
                pl.BlockSpec((STATE, 2 * SSM_DIM), lanes),
                pl.BlockSpec((STATE, 2 * SSM_DIM), lanes),
                pl.BlockSpec((1, 2 * SSM_DIM), lanes),
                pl.BlockSpec((8, rows), whole),
            ],
            out_specs=[
                pl.BlockSpec((rows, 2 * SSM_DIM), lanes),
                pl.BlockSpec((rows, STATE), whole),
                pl.BlockSpec((rows, STATE), whole),
                pl.BlockSpec((1, 8, rows), pair),
            ],
            scratch_shapes=[
                pltpu.VMEM((chunks, CHUNK, CHUNK), jnp.float32),
                pltpu.VMEM((chunks, CHUNK, CHUNK), jnp.float32),
                pltpu.VMEM((chunks, CHUNK, CHUNK), jnp.float32),
                pltpu.VMEM((chunks, STATE, 2 * SSM_DIM), jnp.float32),
                pltpu.VMEM((STATE, 2 * SSM_DIM), jnp.float32),
            ],
        ),
        out_shape=[
            jax.ShapeDtypeStruct((rows, INNER), jnp.float32),
            jax.ShapeDtypeStruct((rows, STATE), jnp.float32),
            jax.ShapeDtypeStruct((rows, STATE), jnp.float32),
            jax.ShapeDtypeStruct((PAIRS, 8, rows), jnp.float32),
        ],
        compiler_params=pltpu.CompilerParams(vmem_limit_bytes=40 * 2**20),
        cost_estimate=pl.CostEstimate(flops=3 * 10**9, bytes_accessed=rows * INNER * 12, transcendentals=2**21),
        name="ssm_back",
    )(meta, x, dy, b_in, c_in, cum.reshape(PAIRS, 2, rows), step.reshape(PAIRS, 2, rows), state_in, state_grad,
      skip, start_row)


def chain_states(earlier, later):
    return (earlier[0] * later[0], earlier[1] * later[0] + later[1])


def scan_states(carry, state, span, fast, backward):
    wide = jnp.repeat(carry, SSM_DIM)[None, :]
    if not fast:
        ident = (jnp.ones_like(wide), jnp.zeros_like(state))
        return (carried_in if backward else prefix)((wide, state), span, chain_states, ident)[1]
    total = (wide, state)
    start = None
    for name in ("c", "x", "y"):
        place = lax.axis_index(name)
        packed = jnp.concatenate([total[1], jnp.broadcast_to(total[0], (16, INNER))], axis=0)
        packed = lax.ppermute(packed.astype(jnp.bfloat16), name, SWAP).astype(jnp.float32)
        other = (packed[STATE : STATE + 1], packed[:STATE])
        leads = place == (0 if backward else 1)
        seen = (jnp.where(leads, other[0], 1.0), jnp.where(leads, other[1], 0.0))
        start = seen if start is None else chain_states(seen, start)
        if name != "y":
            forward = chain_states(other, total)
            reverse = chain_states(total, other)
            total = jax.tree.map(lambda p, q: jnp.where(leads, p, q), forward, reverse)
    return start[1]


KEYS = 512
PAIR = 2 * HEAD_DIM


def attention_forward(q_wide, kv, meta, starts):
    rows = q_wide.shape[1]
    blocks = kv.shape[0]
    wide = min(256, rows)

    def kernel(meta_ref, q_ref, kv_ref, start_ref, o_ref, log_ref, top, total, mixed):
        top[...] = jnp.full(top.shape, masked_score, jnp.float32)
        total[...] = jnp.zeros(total.shape, jnp.float32)
        mixed[...] = jnp.zeros(mixed.shape, jnp.float32)

        def block(b, partial):
            pair = kv_ref[b, 0]
            turned = pair.T[HEAD_DIM:, :]
            for r in range(0, rows, wide):
                here = slice(r, r + wide)
                scores = lax.dot_general(pair, q_ref[0, here, :], NT, preferred_element_type=jnp.float32)
                if partial:
                    keys = b * KEYS + lax.broadcasted_iota(jnp.int32, scores.shape, 0)
                    mine = meta_ref[2] + r + lax.broadcasted_iota(jnp.int32, scores.shape, 1)
                    visible = (keys >= start_ref[0:1, here]) & (keys <= mine)
                    scores = jnp.where(visible, scores, masked_score)
                before = top[0:1, here]
                peak = jnp.maximum(before, jnp.max(scores, axis=0, keepdims=True))
                part = jnp.exp(scores - peak)
                if partial:
                    part = jnp.where(visible, part, 0.0)
                fade = jnp.exp(before - peak)
                top[0:1, here] = peak
                total[0:1, here] = total[0:1, here] * fade + jnp.sum(part, axis=0, keepdims=True)
                mixed[:, here] = mixed[:, here] * fade + jnp.dot(
                    turned, part.astype(jnp.bfloat16), preferred_element_type=jnp.float32
                )

        def turn(b, nothing):
            partial = ((b + 1) * KEYS > meta_ref[2]) | (b * KEYS < meta_ref[3])

            @pl.when(partial)
            def _():
                block(b, True)

            @pl.when(jnp.logical_not(partial))
            def _():
                block(b, False)

            return nothing

        lax.fori_loop(meta_ref[0], meta_ref[1], turn, 0)
        o_ref[0] = mixed[...] / total[0:1, :]
        log_ref[0] = jnp.broadcast_to(top[0:1, :] + jnp.log(total[0:1, :]), (8, rows))

    ratio = HEADS_Q // HEADS_KV
    return pl.pallas_call(
        kernel,
        grid_spec=pltpu.PrefetchScalarGridSpec(
            num_scalar_prefetch=1,
            grid=(HEADS_Q,),
            in_specs=[
                pl.BlockSpec((1, rows, PAIR), lambda h, m: (h, 0, 0)),
                pl.BlockSpec((blocks, 1, KEYS, PAIR), lambda h, m: (0, h // ratio, 0, 0)),
                pl.BlockSpec((8, rows), lambda h, m: (0, 0)),
            ],
            out_specs=[
                pl.BlockSpec((1, HEAD_DIM, rows), lambda h, m: (h, 0, 0)),
                pl.BlockSpec((1, 8, rows), lambda h, m: (h, 0, 0)),
            ],
            scratch_shapes=[
                pltpu.VMEM((8, rows), jnp.float32),
                pltpu.VMEM((8, rows), jnp.float32),
                pltpu.VMEM((HEAD_DIM, rows), jnp.float32),
            ],
        ),
        out_shape=[
            jax.ShapeDtypeStruct((HEADS_Q, HEAD_DIM, rows), jnp.float32),
            jax.ShapeDtypeStruct((HEADS_Q, 8, rows), jnp.float32),
        ],
        compiler_params=pltpu.CompilerParams(vmem_limit_bytes=48 * 2**20),
        cost_estimate=pl.CostEstimate(flops=4 * 10**9, bytes_accessed=2**23, transcendentals=2**23),
        name="attend",
    )(meta, q_wide, kv, starts)


def attention_backward(q_wide, g_wide, kv, logs, mixed, meta, starts):
    rows = q_wide.shape[1]
    blocks = kv.shape[0]
    ratio = HEADS_Q // HEADS_KV
    wide = min(256, rows)

    def kernel(meta_ref, q_ref, g_ref, kv_ref, log_ref, o_ref, start_ref, dkv_ref, dq_ref, delta, sums):
        b = pl.program_id(1)

        @pl.when(b == 0)
        def _():
            dq_ref[...] = jnp.zeros(dq_ref.shape, jnp.float32)
            for h in range(ratio):
                both = g_ref[h].astype(jnp.float32).T[HEAD_DIM:, :] * o_ref[h]
                delta[h] = jnp.broadcast_to(jnp.sum(both, axis=0, keepdims=True), (8, rows))

        def block(partial):
            pair = kv_ref[0, 0]
            turned = pair.T[:HEAD_DIM, :]
            for h in range(ratio):
                for r in range(0, rows, wide):
                    here = slice(r, r + wide)
                    q_now = q_ref[h, here, :]
                    g_now = g_ref[h, here, :]
                    scores = lax.dot_general(pair, q_now, NT, preferred_element_type=jnp.float32)
                    probs = jnp.exp(scores - log_ref[h, 0:1, here])
                    if partial:
                        keys = b * KEYS + lax.broadcasted_iota(jnp.int32, scores.shape, 0)
                        mine = meta_ref[2] + r + lax.broadcasted_iota(jnp.int32, scores.shape, 1)
                        visible = (keys >= start_ref[0:1, here]) & (keys <= mine)
                        probs = jnp.where(visible, probs, 0.0)
                    grads = lax.dot_general(pair, g_now, NT, preferred_element_type=jnp.float32)
                    low_grads = (probs * (grads - delta[h, 0:1, here])).astype(jnp.bfloat16)
                    change = jnp.dot(
                        probs.astype(jnp.bfloat16), g_now, preferred_element_type=jnp.float32
                    ) + jnp.dot(low_grads, q_now, preferred_element_type=jnp.float32)
                    if h == 0 and r == 0:
                        sums[...] = change
                    else:
                        sums[...] += change
                    dq_ref[h, :, here] += jnp.dot(turned, low_grads, preferred_element_type=jnp.float32)
            dkv_ref[0, 0] = sums[...].astype(jnp.bfloat16)

        needed = (b >= meta_ref[0]) & (b < meta_ref[1])
        partial = ((b + 1) * KEYS > meta_ref[2]) | (b * KEYS < meta_ref[3])

        @pl.when(needed & partial)
        def _():
            block(True)

        @pl.when(needed & jnp.logical_not(partial))
        def _():
            block(False)

        @pl.when(jnp.logical_not(needed))
        def _():
            dkv_ref[0, 0] = jnp.zeros((KEYS, PAIR), jnp.bfloat16)

    heads = lambda g, b, m: (g, 0, 0)
    return pl.pallas_call(
        kernel,
        grid_spec=pltpu.PrefetchScalarGridSpec(
            num_scalar_prefetch=1,
            grid=(HEADS_KV, blocks),
            in_specs=[
                pl.BlockSpec((ratio, rows, PAIR), heads),
                pl.BlockSpec((ratio, rows, PAIR), heads),
                pl.BlockSpec((1, 1, KEYS, PAIR), lambda g, b, m: (b, g, 0, 0)),
                pl.BlockSpec((ratio, 8, rows), heads),
                pl.BlockSpec((ratio, HEAD_DIM, rows), heads),
                pl.BlockSpec((8, rows), lambda g, b, m: (0, 0)),
            ],
            out_specs=[
                pl.BlockSpec((1, 1, KEYS, PAIR), lambda g, b, m: (b, g, 0, 0)),
                pl.BlockSpec((ratio, HEAD_DIM, rows), heads),
            ],
            scratch_shapes=[
                pltpu.VMEM((ratio, 8, rows), jnp.float32),
                pltpu.VMEM((KEYS, PAIR), jnp.float32),
            ],
        ),
        out_shape=[
            jax.ShapeDtypeStruct((blocks, HEADS_KV, KEYS, PAIR), jnp.bfloat16),
            jax.ShapeDtypeStruct((HEADS_Q, HEAD_DIM, rows), jnp.float32),
        ],
        compiler_params=pltpu.CompilerParams(vmem_limit_bytes=48 * 2**20),
        cost_estimate=pl.CostEstimate(flops=5 * 10**9, bytes_accessed=2**23, transcendentals=2**23),
        name="attend_back",
    )(meta, q_wide, g_wide, kv, logs, mixed, starts)


def ordered(place, own, other, axis):
    first = jnp.where(place == 0, own, other)
    second = jnp.where(place == 0, other, own)
    return jnp.stack([first, second], axis=axis)


def gather_span(value, span, fast):
    if not fast:
        return lax.all_gather(value, span)
    _, y, x, c = (lax.axis_index(name) for name in GRID)
    two = ordered(x, value, lax.ppermute(value, "x", SWAP), 0)
    four = ordered(y, two, lax.ppermute(two, "y", SWAP), 0)
    eight = ordered(c, four, lax.ppermute(four, "c", SWAP), 2)
    return eight.reshape((8,) + value.shape)


def scatter_span(value, span, fast):
    if not fast:
        return lax.psum_scatter(value, span, scatter_dimension=0).astype(jnp.float32)
    _, y, x, c = (lax.axis_index(name) for name in GRID)
    value = value.reshape((2, 2, 2) + value.shape[1:])
    for name, place, axis in (("c", c, 2), ("y", y, 0), ("x", x, 0)):
        keep = lax.dynamic_index_in_dim(value, place, axis, keepdims=False)
        send = lax.dynamic_index_in_dim(value, 1 - place, axis, keepdims=False)
        value = keep.astype(jnp.float32) + lax.ppermute(send, name, SWAP).astype(jnp.float32)
        if name != "x":
            value = value.astype(jnp.bfloat16)
    return value


def sum_all(value, axes, fast):
    if not fast:
        return lax.psum(value, axes)
    for name in GRID[1:]:
        value = value + lax.ppermute(value, name, SWAP)
    for pairs in ([(0, 1), (1, 0), (2, 3), (3, 2)], [(0, 2), (2, 0), (1, 3), (3, 1)]):
        value = value + lax.ppermute(value, "z", pairs)
    return value


def offsets_of():
    places, at = {}, 0
    for name_key, extent in layout():
        places[name_key] = (at, extent)
        at += math.prod(extent)
    return places


def fast_weights(params):
    places = offsets_of()
    (early, late), where = gather_lines(params)
    early_names = (W_QUERY, W_KEY, W_VALUE, W_ATTN_OUT, W_GATE_SSM, W_X_SSM, W_B_C)
    late_names = (W_SSM_OUT, W_GATE, W_UP_PROJ, W_DOWN)

    def segment(name_key):
        at, extent = places[name_key]
        return (at, extent[0], extent[1])

    misc_at = places[W_STEP][0]
    first = unpack_lines(
        early, 0, where,
        [segment(name_key) for name_key in early_names] + [(0, 16, LINE), (misc_at, 288, LINE)],
    )
    second = unpack_lines(
        early + late, 0, where,
        [segment(name_key) for name_key in late_names] + [(places[NORM_FFN][0], 16, LINE)],
    )
    weights = dict(zip(early_names, first))
    weights.update(zip(late_names, second))
    weights[NORM_ATTN] = first[-2].reshape(-1)[:D]
    misc = first[-1].reshape(-1)
    for name_key in (W_STEP,) + small_names[1:-1]:
        at, extent = places[name_key]
        weights[name_key] = misc[at - misc_at : at - misc_at + math.prod(extent)].reshape(extent)
    lane = places[NORM_FFN][0] % LINE
    weights[NORM_FFN] = second[-1].reshape(-1)[lane : lane + D]
    return weights


def fast_gradients(small, pairs):
    places = offsets_of()
    z, y, x, c = (lax.axis_index(name) for name in GRID)
    ssm_low, grad_branch = pairs[W_SSM_OUT]
    out_at = places[W_SSM_OUT][0]
    lane = places[W_GATE][0] % LINE
    boundary = 2 * PLANE * LINE
    tail_from = (boundary - out_at) // D
    tail = matmul_left_t(ssm_low[:, tail_from:], grad_branch).reshape(-1)
    tail = tail[boundary - out_at - tail_from * D :]
    head = jnp.concatenate([jnp.zeros((14 * LINE,), jnp.float32), tail, small[NORM_FFN]])
    head_rows = head.shape[0] // LINE
    carry = jnp.zeros((8, LINE), jnp.float32).at[7, :lane].set(head[head_rows * LINE :])
    head = head[: head_rows * LINE].reshape(head_rows, LINE).astype(jnp.bfloat16)
    length = 2 * PLANE + 32
    late = pack_lines(
        None, length, head_rows,
        [pairs[W_GATE], pairs[W_UP_PROJ], pairs[W_DOWN]],
        lane, 0, [(head, 0)], carry, 48,
    )
    late_sum = reduce_lines(late, 1, 14)
    first_row = (8 + out_at // LINE) // 16 * 16
    early_rows = first_row + SSM_HEADS * SSM_DIM * D // LINE
    early = pack_lines(
        None, early_rows, first_row, [pairs[W_SSM_OUT]],
        lane, (8 + out_at // LINE) % 8, [], jnp.zeros((8, LINE), jnp.float32), 0,
    )
    names = (W_STEP,) + small_names[1:-1]
    misc = [small[name_key].reshape(-1) for name_key in names]
    count = sum(part.shape[0] for part in misc)
    misc_rows = (count // LINE + 16) // 16 * 16
    opening = matmul_left_t(ssm_low[:, :16], grad_branch).reshape(-1)
    misc = jnp.concatenate(misc + [opening[: misc_rows * LINE - count]])
    misc = misc.reshape(misc_rows, LINE).astype(jnp.bfloat16)
    first = jnp.concatenate([jnp.zeros((8 * LINE,), jnp.float32), small[NORM_ATTN]])
    first = first.reshape(16, LINE).astype(jnp.bfloat16)
    early = pack_lines(
        early, early_rows, 16,
        [pairs[k] for k in (W_QUERY, W_KEY, W_VALUE, W_ATTN_OUT, W_GATE_SSM, W_X_SSM, W_B_C)],
        0, 0, [(first, 0), (misc, 8 + places[W_STEP][0] // LINE)], None, 0,
    )
    early_sum = reduce_lines(early, 0, 8)
    shard = SHARD * (4 * y + 2 * x + c)
    start = jnp.where(z < 2, (8 + shard) % 16, (14 + shard) % 16)
    lines = jnp.where(z < 2, early_sum, late_sum)
    return lax.dynamic_slice(lines, (start, 0), (SHARD, LINE)).astype(jnp.float32).reshape(-1)


def body(span, group, fast, tokens, params, cotangent, offsets):
    rows_dev = tokens.shape[0]
    group_rows = rows_dev * lax.axis_size(span)
    all_rows = group_rows * lax.axis_size(group)
    ssm_inner = SSM_HEADS * SSM_DIM
    score_scale = HEAD_DIM ** (-0.5)
    bounds = offsets[0]
    my_start = lax.axis_index(span) * rows_dev
    row_index = my_start + jnp.arange(rows_dev, dtype=jnp.int32)
    seq_id, positions = sequence_info(row_index, bounds)
    first_start = row_index[0] - positions[0]
    last_row = my_start + rows_dev - 1
    cosine, sine = rotary_tables(positions)
    if fast:
        weights = fast_weights(params)
    else:
        weights = unpack(lax.all_gather(params, group + span, axis=0, tiled=True))
    small_f32 = {name_key: weights[name_key].astype(jnp.float32) for name_key in small_names}
    x_rows = tokens.astype(jnp.float32)
    normed_one, norm_one_back = jax.vjp(rms_norm, x_rows, small_f32[NORM_ATTN])
    hidden = normed_one.astype(jnp.bfloat16)
    query = matmul(hidden, weights[W_QUERY])
    key_raw = matmul(hidden, weights[W_KEY])
    value_low = matmul(hidden, weights[W_VALUE]).astype(jnp.bfloat16)
    q_rot = rotate(query, cosine, sine, HEADS_Q).astype(jnp.bfloat16)
    k_rot = rotate(key_raw, cosine, sine, HEADS_KV).astype(jnp.bfloat16)
    k_heads = k_rot.reshape(rows_dev, HEADS_KV, HEAD_DIM)
    v_heads = value_low.reshape(rows_dev, HEADS_KV, HEAD_DIM)
    kv_mine = jnp.concatenate([k_heads, v_heads], axis=2).transpose(1, 0, 2)
    key_blocks = gather_span(kv_mine.reshape(HEADS_KV, rows_dev, PAIR), span, fast)
    if rows_dev != KEYS:
        key_blocks = key_blocks.transpose(1, 0, 2, 3).reshape(HEADS_KV, -1, KEYS, PAIR).transpose(1, 0, 2, 3)
    row_starts = row_index - positions
    meta = jnp.stack(
        [first_start // KEYS, last_row // KEYS + 1, my_start, row_starts[rows_dev - 1]]
    ).astype(jnp.int32)
    q_low = (q_rot * jnp.bfloat16(score_scale)).reshape(rows_dev, HEADS_Q, HEAD_DIM).transpose(1, 0, 2)
    q_wide = jnp.pad(q_low, ((0, 0), (0, 0), (0, HEAD_DIM)))
    start_row = jnp.broadcast_to(row_starts[None, :], (8, rows_dev))
    mixed, logs = attention_forward(q_wide, key_blocks, meta, start_row)
    attended = mixed.astype(jnp.bfloat16).reshape(HEADS_Q * HEAD_DIM, rows_dev).T
    attn_out = matmul(attended, weights[W_ATTN_OUT])
    gate_ssm = matmul(hidden, weights[W_GATE_SSM])
    xbc = jnp.concatenate(
        [matmul(hidden, weights[W_X_SSM]), matmul(hidden, weights[W_B_C])], axis=1
    )
    step_raw = matmul(hidden, weights[W_STEP])
    rim_rows = passed_along(xbc[rows_dev - (CONV - 1) :], span, 1)
    extended = jnp.concatenate([rim_rows, xbc], axis=0)

    def conv_local(extended_in, conv_weight, conv_bias):
        return conv_apply(extended_in, conv_weight, conv_bias, positions)

    conv_values, conv_back = jax.vjp(
        conv_local, extended, small_f32[CONV_WEIGHT], small_f32[CONV_BIAS]
    )

    x_ssm = conv_values[:, :ssm_inner]
    b_in = conv_values[:, ssm_inner : ssm_inner + STATE]
    c_in = conv_values[:, ssm_inner + STATE :]
    step_in = step_raw.T + small_f32[STEP_BIAS][:, None]
    step_rows = jax.nn.softplus(step_in)
    decay = -jnp.exp(small_f32[DECAY_LOG])
    logs_step = step_rows * decay[:, None]
    order = jnp.arange(rows_dev)
    upto = (order[:, None] <= order[None, :]).astype(jnp.float32)
    cumul = jnp.dot(logs_step, upto, precision=highest)
    chunk_cum = jnp.dot(
        logs_step.reshape(-1, CHUNK), upto[:CHUNK, :CHUNK], precision=highest
    ).reshape(SSM_HEADS, rows_dev)
    went_on = row_starts < my_start
    entry_rows = jnp.where(went_on[None, :], jnp.exp(cumul), 0.0)
    in_last = row_index >= row_starts[rows_dev - 1]
    tail_rows = jnp.exp(jnp.where(in_last[None, :], cumul[:, -1:] - cumul, masked_score))
    carry_all = entry_rows[:, -1]
    local_state = weighted_state(b_in, x_ssm, tail_rows * step_rows)
    state_in = scan_states(carry_all, local_state, span, fast, False)
    skip_wide = jnp.repeat(small_f32[SKIP_GAIN], SSM_DIM)[None, :]
    ssm_meta = jnp.concatenate([my_start[None], row_starts[CHUNK - 1 :: CHUNK]]).astype(jnp.int32)
    ssm_y = ssm_forward(
        x_ssm, b_in, c_in, chunk_cum, step_rows, state_in, skip_wide, ssm_meta, row_starts[:, None], start_row
    )
    normed_ssm, gnorm_back = jax.vjp(gated_norm, ssm_y, gate_ssm, small_f32[NORM_SSM])
    ssm_low = normed_ssm.astype(jnp.bfloat16)
    ssm_out = matmul(ssm_low, weights[W_SSM_OUT])
    middle = x_rows + attn_out + ssm_out
    normed_two, norm_two_back = jax.vjp(rms_norm, middle, small_f32[NORM_FFN])
    hidden_two = normed_two.astype(jnp.bfloat16)
    gate_ffn = matmul(hidden_two, weights[W_GATE])
    upper = matmul(hidden_two, weights[W_UP_PROJ])
    activation_f32, swiglu_back = jax.vjp(swiglu, gate_ffn, upper)
    activation = activation_f32.astype(jnp.bfloat16)
    ffn_out = matmul(activation, weights[W_DOWN])
    result = middle + ffn_out
    squares = jnp.stack(
        [
            jnp.sum(result * result),
            jnp.sum(attn_out * attn_out),
            jnp.sum(ssm_out * ssm_out),
            jnp.sum(ffn_out * ffn_out),
        ]
    )
    totals = sum_all(squares, group + span, fast)
    stats = jnp.sqrt(totals / (all_rows * D))
    back_weights = weights
    grad_out = cotangent.astype(jnp.float32)
    grad_activation = matmul_right_t(cotangent, back_weights[W_DOWN])
    grad_gate_f32, grad_upper_f32 = swiglu_back(grad_activation)
    grad_gate = grad_gate_f32.astype(jnp.bfloat16)
    grad_upper = grad_upper_f32.astype(jnp.bfloat16)
    grad_hidden_two = matmul_right_t(grad_gate, back_weights[W_GATE]) + matmul_right_t(
        grad_upper, back_weights[W_UP_PROJ]
    )
    grad_middle_norm, grad_norm_ffn = norm_two_back(grad_hidden_two)
    grad_middle = grad_out + grad_middle_norm
    grad_branch = grad_middle.astype(jnp.bfloat16)
    grad_attended = matmul_right_t(grad_branch, back_weights[W_ATTN_OUT]).astype(jnp.bfloat16)
    grad_ssm_low = matmul_right_t(grad_branch, back_weights[W_SSM_OUT])
    grad_ssm_y, grad_gate_ssm_f32, grad_norm_ssm = gnorm_back(grad_ssm_low)
    grad_state_local = weighted_state(c_in, grad_ssm_y, entry_rows)
    grad_state_out = scan_states(carry_all, grad_state_local, span, fast, True)
    grad_x, grad_b, grad_c, grad_small = ssm_backward(
        x_ssm, grad_ssm_y, b_in, c_in, chunk_cum, step_rows, state_in, grad_state_out, skip_wide, ssm_meta, start_row
    )
    grad_conv_values = jnp.concatenate([grad_x, grad_b, grad_c], axis=1)
    grad_direct = grad_small[:, 0:2].reshape(SSM_HEADS, rows_dev)
    grad_logs = grad_small[:, 2:4].reshape(SSM_HEADS, rows_dev)
    grad_decay_log = decay * jnp.sum(step_rows * grad_logs, axis=1)
    grad_step_rows = (grad_direct + decay[:, None] * grad_logs) * jax.nn.sigmoid(step_in)
    grad_step_bias = jnp.sum(grad_step_rows, axis=1)
    grad_step_raw_f32 = grad_step_rows.T
    grad_skip_gain = jnp.sum(grad_small[:, 4, : 2 * SSM_DIM].reshape(SSM_HEADS, SSM_DIM), axis=1)
    grad_extended, grad_conv_weight, grad_conv_bias = conv_back(grad_conv_values)
    rim_back = passed_along(grad_extended[: CONV - 1], span, -1)
    grad_xbc_f32 = grad_extended[CONV - 1 :]
    grad_xbc_f32 = grad_xbc_f32.at[rows_dev - (CONV - 1) :].add(rim_back)
    grad_xbc = grad_xbc_f32.astype(jnp.bfloat16)
    grad_gate_ssm = grad_gate_ssm_f32.astype(jnp.bfloat16)
    grad_step_raw = grad_step_raw_f32.astype(jnp.bfloat16)
    grad_w_step = matmul_left_t(hidden, grad_step_raw)
    grad_hidden_ssm = (
        matmul_right_t(grad_gate_ssm, back_weights[W_GATE_SSM])
        + matmul_right_t(grad_xbc[:, :ssm_inner], back_weights[W_X_SSM])
        + matmul_right_t(grad_xbc[:, ssm_inner:], back_weights[W_B_C])
        + matmul_right_t(grad_step_raw, back_weights[W_STEP])
    )
    g_low = grad_attended.reshape(rows_dev, HEADS_Q, HEAD_DIM).transpose(1, 0, 2)
    g_wide = jnp.pad(g_low, ((0, 0), (0, 0), (HEAD_DIM, 0)))
    grad_kv, grad_q_turned = attention_backward(
        q_wide, g_wide, key_blocks, logs, mixed, meta, start_row
    )
    if rows_dev != KEYS:
        grad_kv = grad_kv.transpose(1, 0, 2, 3).reshape(HEADS_KV, -1, rows_dev, PAIR).transpose(1, 0, 2, 3)
    grad_kv_mine = scatter_span(grad_kv, span, fast)
    grad_keys_mine = grad_kv_mine[:, :, :HEAD_DIM].transpose(1, 0, 2).reshape(rows_dev, -1)
    grad_values_mine = grad_kv_mine[:, :, HEAD_DIM:].transpose(1, 0, 2).reshape(rows_dev, -1)
    grad_q_rot = grad_q_turned.reshape(HEADS_Q * HEAD_DIM, rows_dev).T * score_scale
    grad_query_low = rotate(grad_q_rot, cosine, -sine, HEADS_Q).astype(jnp.bfloat16)
    grad_key_low = rotate(grad_keys_mine, cosine, -sine, HEADS_KV).astype(jnp.bfloat16)
    grad_value_low = grad_values_mine.astype(jnp.bfloat16)
    grad_hidden = (
        grad_hidden_ssm
        + matmul_right_t(grad_query_low, back_weights[W_QUERY])
        + matmul_right_t(grad_key_low, back_weights[W_KEY])
        + matmul_right_t(grad_value_low, back_weights[W_VALUE])
    )
    grad_x_norm, grad_norm_attn = norm_one_back(grad_hidden)
    grad_tokens = grad_middle + grad_x_norm
    small = {
        NORM_ATTN: grad_norm_attn,
        W_STEP: grad_w_step,
        CONV_WEIGHT: grad_conv_weight,
        CONV_BIAS: grad_conv_bias,
        STEP_BIAS: grad_step_bias,
        DECAY_LOG: grad_decay_log,
        SKIP_GAIN: grad_skip_gain,
        NORM_SSM: grad_norm_ssm,
        NORM_FFN: grad_norm_ffn,
    }
    pairs = {
        W_QUERY: (hidden, grad_query_low),
        W_KEY: (hidden, grad_key_low),
        W_VALUE: (hidden, grad_value_low),
        W_ATTN_OUT: (attended, grad_branch),
        W_GATE_SSM: (hidden, grad_gate_ssm),
        W_X_SSM: (hidden, grad_xbc[:, :ssm_inner]),
        W_B_C: (hidden, grad_xbc[:, ssm_inner:]),
        W_SSM_OUT: (ssm_low, grad_branch),
        W_GATE: (hidden_two, grad_gate),
        W_UP_PROJ: (hidden_two, grad_upper),
        W_DOWN: (activation, cotangent),
    }
    if fast:
        return (result.astype(jnp.bfloat16), grad_tokens, fast_gradients(small, pairs), stats)
    grad_dict = dict(small)
    for name_key, (left, right) in pairs.items():
        grad_dict[name_key] = matmul_left_t(left, right)
    flat_parts = [grad_dict[name_key].reshape(-1) for name_key, extent in layout()]
    used_entries = 0
    for part_array in flat_parts:
        used_entries += part_array.shape[0]
    flat_parts.append(jnp.zeros((params.shape[0] * lax.axis_size(group + span) - used_entries,), jnp.float32))
    grad_shard = lax.psum_scatter(
        jnp.concatenate(flat_parts), group + span, scatter_dimension=0, tiled=True
    )
    return (result.astype(jnp.bfloat16), grad_tokens, grad_shard, stats)


def solution(mesh):
    fast = (mesh.shape["group"], mesh.shape["span"]) == FAST
    if fast:
        mesh = Mesh(mesh.devices.reshape(4, 2, 2, 2), GRID)
        group, span = (GRID[:1], GRID[1:])
    else:
        group, span = (("group",), ("span",))

    def program(tokens, params, cotangent, offsets):
        return body(span, group, fast, tokens, params, cotangent, offsets)

    return jax.shard_map(
        program,
        mesh=mesh,
        in_specs=(P(group + span, None), P(group + span), P(group + span, None), P(group, None)),
        out_specs=(P(group + span, None), P(group + span, None), P(group + span), P()),
        check_vma=False,
    )
```

```python
import math

import jax
import jax.numpy as jnp
import numpy as np
from jax import lax
from jax.experimental import pallas as pl
from jax.experimental.pallas import tpu as pltpu
from jax.sharding import Mesh, PartitionSpec as P

D = 1024
HEADS_Q = 8
HEADS_KV = 2
HEAD_DIM = 64
SSM_HEADS = 24
SSM_DIM = 64
STATE = 128
CONV = 4
FF = 2048
(
    NORM_ATTN,
    W_QUERY,
    W_KEY,
    W_VALUE,
    W_ATTN_OUT,
    W_GATE_SSM,
    W_X_SSM,
    W_B_C,
    W_STEP,
    CONV_WEIGHT,
    CONV_BIAS,
    STEP_BIAS,
    DECAY_LOG,
    SKIP_GAIN,
    NORM_SSM,
    W_SSM_OUT,
    NORM_FFN,
    W_GATE,
    W_UP_PROJ,
    W_DOWN,
) = range(20)


epsilon = 1e-05
rope_base = 100000000000.0
masked_score = -1e30
highest = lax.Precision.HIGHEST
small_names = (
    NORM_ATTN,
    CONV_WEIGHT,
    CONV_BIAS,
    STEP_BIAS,
    DECAY_LOG,
    SKIP_GAIN,
    NORM_SSM,
    NORM_FFN,
)


def passed_along(value, axis, steps):
    count = lax.axis_size(axis)
    first, last = (max(0, -steps), min(count, count - steps))
    return lax.ppermute(value, axis, [(source, source + steps) for source in range(first, last)])


def prefix(value, axis, combine, identity):
    peers, place = (lax.axis_size(axis), lax.axis_index(axis))
    everything = jax.tree.map(
        lambda part, kind: lax.all_gather(part.astype(kind), axis),
        value,
        (jnp.bfloat16, jnp.bfloat16),
    )
    start = jax.tree.map(
        lambda part, zero: jnp.broadcast_to(jnp.asarray(zero, part.dtype), part.shape),
        value,
        identity,
    )

    def prefix_turn(k, before):
        reached = k < place
        new = combine(
            before, jax.tree.map(lambda part, own: part[k].astype(own.dtype), everything, value)
        )
        return jax.tree.map(lambda a, b: jnp.where(reached, a, b), new, before)

    return lax.fori_loop(0, peers, prefix_turn, start)


def carried_in(value, axis, combine, identity):
    peers, place = (lax.axis_size(axis), lax.axis_index(axis))
    everything = jax.tree.map(
        lambda part, kind: lax.all_gather(part.astype(kind), axis),
        value,
        jax.tree.map(lambda a: jnp.bfloat16 if a.dtype == jnp.float32 else a.dtype, value),
    )
    start = jax.tree.map(
        lambda part, zero: jnp.broadcast_to(jnp.asarray(zero, part.dtype), part.shape),
        value,
        identity,
    )

    def carried_turn(k, before):
        at = peers - 1 - k
        reached = at > place
        new = combine(
            before, jax.tree.map(lambda part, own: part[at].astype(own.dtype), everything, value)
        )
        return jax.tree.map(lambda a, b: jnp.where(reached, a, b), new, before)

    return lax.fori_loop(0, peers, carried_turn, start)


def layout():
    ssm_inner = SSM_HEADS * SSM_DIM
    channels = ssm_inner + 2 * STATE
    return [
        (NORM_ATTN, (D,)),
        (W_QUERY, (D, HEADS_Q * HEAD_DIM)),
        (W_KEY, (D, HEADS_KV * HEAD_DIM)),
        (W_VALUE, (D, HEADS_KV * HEAD_DIM)),
        (W_ATTN_OUT, (HEADS_Q * HEAD_DIM, D)),
        (W_GATE_SSM, (D, ssm_inner)),
        (W_X_SSM, (D, ssm_inner)),
        (W_B_C, (D, 2 * STATE)),
        (W_STEP, (D, SSM_HEADS)),
        (CONV_WEIGHT, (CONV, channels)),
        (CONV_BIAS, (channels,)),
        (STEP_BIAS, (SSM_HEADS,)),
        (DECAY_LOG, (SSM_HEADS,)),
        (SKIP_GAIN, (SSM_HEADS,)),
        (NORM_SSM, (ssm_inner,)),
        (W_SSM_OUT, (ssm_inner, D)),
        (NORM_FFN, (D,)),
        (W_GATE, (D, FF)),
        (W_UP_PROJ, (D, FF)),
        (W_DOWN, (FF, D)),
    ]


def unpack(flat_vector):
    unpacked = {}
    offset = 0
    for name_key, extent in layout():
        amount = math.prod(extent)
        unpacked[name_key] = flat_vector[offset : offset + amount].reshape(extent)
        offset += amount
    return unpacked


def matmul(left, right):
    return jnp.dot(left, right, preferred_element_type=jnp.float32)


def matmul_left_t(left, right):
    return lax.dot_general(
        left, right, (((0,), (0,)), ((), ())), preferred_element_type=jnp.float32
    )


def matmul_right_t(left, right):
    return lax.dot_general(
        left, right, (((1,), (1,)), ((), ())), preferred_element_type=jnp.float32
    )


def rms_norm(values, gain):
    return values * lax.rsqrt(jnp.mean(values * values, axis=-1, keepdims=True) + epsilon) * gain


def gated_norm(ssm_y, gate_ssm, gain):
    return rms_norm(ssm_y * jax.nn.silu(gate_ssm), gain)


def swiglu(gate_ffn, upper):
    return jax.nn.silu(gate_ffn) * upper


def sequence_info(row_index, bounds):
    starts = bounds[:-1]
    inside = row_index[:, None] >= starts[None, :]
    seq_id = jnp.sum(inside.astype(jnp.int32), axis=1) - 1
    seq_start = jnp.max(jnp.where(inside, starts[None, :], 0), axis=1)
    return (seq_id, row_index - seq_start)


def rotary_tables(positions):
    half_dim = HEAD_DIM // 2
    freqs = jnp.exp(
        -jnp.arange(half_dim, dtype=jnp.float32) * (2.0 * math.log(rope_base) / HEAD_DIM)
    )
    angles = positions.astype(jnp.float32)[:, None] * freqs[None, :]
    return (jnp.cos(angles), jnp.sin(angles))


def rotate(values, cosine, sine, heads):
    row_count = values.shape[0]
    half_dim = HEAD_DIM // 2
    split_heads = values.reshape(row_count, heads, HEAD_DIM)
    first_half = split_heads[..., :half_dim]
    second_half = split_heads[..., half_dim:]
    cos_b = cosine[:, None, :]
    sin_b = sine[:, None, :]
    turned = jnp.concatenate(
        [first_half * cos_b - second_half * sin_b, second_half * cos_b + first_half * sin_b],
        axis=-1,
    )
    return turned.reshape(row_count, heads * HEAD_DIM)


def conv_apply(extended, conv_weight, conv_bias, positions):
    row_count = positions.shape[0]
    conv_total = conv_bias[None, :]
    for tap_index in range(CONV):
        window = extended[tap_index : tap_index + row_count]
        valid_rows = (positions >= CONV - 1 - tap_index)[:, None]
        conv_total = (
            conv_total + jnp.where(valid_rows, window, 0.0) * conv_weight[tap_index][None, :]
        )
    return jax.nn.silu(conv_total)


def add_rows(target, addend, first_row):
    current = lax.dynamic_slice_in_dim(target, first_row, addend.shape[0], 0)
    return lax.dynamic_update_slice_in_dim(target, current + addend, first_row, 0)


FAST = (4, 8)
LINE = 128
SHARD = 3082
SPAD = 3088
WIN = 3104
PLANE = 8 * SHARD
DEPTH = 4
TALL = {1: 1024, 2: 1024, 4: 512, 8: 256, 12: 128, 16: 128}
GRID = ("z", "y", "x", "c")
ZC = ("z", "c")
SWAP = [(0, 1), (1, 0)]


def zc_pairs(*pairs):
    return [(2 * a + c, 2 * b + c) for a, b, c in pairs]


def pinned(kernel, count, after):
    return lambda *refs: kernel(*refs[:count], *refs[count + len(after) :])


def pins(after):
    return [pl.BlockSpec(memory_space=pltpu.HBM)] * len(after)


def gather_lines(params):
    z, y, x, c = (lax.axis_index(name) for name in GRID)
    lines = jnp.pad(params.reshape(SHARD, LINE), ((0, SPAD - SHARD), (0, 0)))
    sibling = lax.ppermute(lines, ZC, [(2 * k + 1 - k % 2, 2 * k + k % 2) for k in range(4)])
    batches = []
    for batch in range(2):
        buffers = []
        for part in range(2):
            here = jnp.where(c == part, lines, sibling)
            if batch == 0:
                one = lax.ppermute(here, ZC, zc_pairs((0, 1, 0), (1, 2, 1)))
                side = lax.ppermute(here, ZC, zc_pairs((1, 0, 1)))
                two = lax.ppermute(one, ZC, zc_pairs((1, 2, 0), (2, 3, 1)))
                three = lax.ppermute(two, ZC, zc_pairs((2, 3, 0)))
            else:
                one = lax.ppermute(here, ZC, zc_pairs((2, 1, 0), (3, 2, 1)))
                side = lax.ppermute(here, ZC, zc_pairs((2, 3, 0)))
                two = lax.ppermute(one, ZC, zc_pairs((1, 0, 0), (2, 1, 1)))
                three = lax.ppermute(two, ZC, zc_pairs((1, 0, 1)))
            mine = z == 2 * batch + c
            column = jnp.where(mine, here, one + side + two + three)
            over_x = lax.ppermute(column, "x", SWAP)
            over_y = lax.ppermute(column, "y", SWAP)
            if part == 0:
                corner = lax.ppermute(over_x, "y", SWAP)
            else:
                corner = lax.ppermute(over_y, "x", SWAP)
            local = [column, over_x, over_y, corner]
            buffers += local + [lax.ppermute(piece, "c", SWAP) for piece in local]
        batches.append(buffers)
    shard = np.arange(32)
    sz, sy, sx, sc = shard // 8, shard // 4 % 2, shard // 2 % 2, shard % 2
    away = jnp.where(sz % 2 == c, 0, 4)
    where = sc * 8 + away + 2 * (sy ^ y) + (sx ^ x) + 16 * (sz // 2)
    return batches, where.astype(jnp.int32)


def unpack_lines(buffers, first, where, segments, after=()):
    jobs, starts = [], []
    reach = 0
    for offset, rows, columns in segments:
        per_row = columns // LINE
        lane, base = offset % LINE, offset // LINE
        if per_row == 1 and rows < 1024:
            lane, tall = 0, rows
        else:
            tall = TALL[per_row]
        starts.append(len(jobs))
        for k in range(rows // tall):
            jobs.append((base + k * tall * per_row, tall * per_row, 1 if lane else 0))
    window = max(job[1] for job in jobs) + 32
    table = np.zeros((len(jobs), 5), np.int32)
    for k, (line, count, extra) in enumerate(jobs):
        owner = line // SHARD
        inside = line - owner * SHARD
        begin = min(inside // 16 * 16, SPAD - window)
        crosses = int(line + count + extra > (owner + 1) * SHARD)
        table[k] = (owner, begin, begin - inside, crosses, (owner + 1) * SHARD - line)
    base_row = (int(-table[:, 2].min()) + 7) // 8 * 8
    table[:, 2] += base_row
    table[:, 4] += base_row
    room = int(max((table[:, 2] + window).max(), ((table[:, 4] + window) * table[:, 3]).max()))
    room = (room + 15) // 8 * 8
    total = len(jobs)
    count_buffers = len(buffers)
    shapes = []
    for offset, rows, columns in segments:
        per_row = columns // LINE
        tall = rows if per_row == 1 and rows < 1024 else TALL[per_row]
        shapes.append((rows, columns, tall, per_row, offset % LINE if tall != rows or per_row != 1 else 0))
    sizes = sorted({(tall, columns) for _, columns, tall, _, _ in shapes})

    def kernel(table_ref, where_ref, *refs):
        sources = refs[:count_buffers]
        outs = refs[count_buffers : count_buffers + len(segments)]
        rest = refs[count_buffers + len(segments) :]
        stages = dict(zip(sizes, rest))
        raw, flat, in_sem, out_sem = rest[len(sizes) :]
        step = pl.program_id(0)

        def fetch(job, slot):
            owner = table_ref[job, 0]
            begin = pl.multiple_of(table_ref[job, 1], 16)
            for b in range(count_buffers):

                @pl.when(where_ref[owner] == first + b)
                def _():
                    pltpu.make_async_copy(
                        sources[b].at[pl.ds(begin, window), :], raw.at[slot, 0], in_sem.at[slot, 0]
                    ).start()

            @pl.when(table_ref[job, 3] == 1)
            def _():
                for b in range(count_buffers):

                    @pl.when(where_ref[owner + 1] == first + b)
                    def _():
                        pltpu.make_async_copy(
                            sources[b].at[pl.ds(0, window), :], raw.at[slot, 1], in_sem.at[slot, 1]
                        ).start()

        def fetched(slot, half):
            return pltpu.make_async_copy(
                sources[0].at[pl.ds(0, window), :], raw.at[slot, half], in_sem.at[slot, half]
            )

        @pl.when(step == 0)
        def _():
            for k in range(min(DEPTH - 1, total)):
                fetch(k, k)

        @pl.when(step + DEPTH - 1 < total)
        def _():
            fetch(step + DEPTH - 1, lax.rem(step + DEPTH - 1, DEPTH))

        slot = lax.rem(step, DEPTH)
        fetched(slot, 0).wait()
        flat[pl.ds(table_ref[step, 2], window), :] = raw[slot, 0].astype(jnp.float32)

        @pl.when(table_ref[step, 3] == 1)
        def _():
            fetched(slot, 1).wait()
            flat[pl.ds(table_ref[step, 4], window), :] = raw[slot, 1].astype(jnp.float32)

        for index, (rows, columns, tall, per_row, lane) in enumerate(shapes):
            begin = starts[index]
            blocks = rows // tall
            stage = stages[(tall, columns)]

            @pl.when((step >= begin) & (step < begin + blocks))
            def _():
                block = step - begin
                side = lax.rem(block, 2)

                def written(k, s):
                    return pltpu.make_async_copy(
                        stage.at[s],
                        outs[index].at[pl.ds(pl.multiple_of(k * tall, 16), tall), :],
                        out_sem.at[s],
                    )

                @pl.when(block >= 2)
                def _():
                    written(block - 2, side).wait()

                def tile(j):
                    picked = flat[pl.ds(base_row + j, tall, stride=per_row), :]
                    return pltpu.roll(picked, LINE - lane, 1) if lane else picked

                if lane:
                    lanes = lax.broadcasted_iota(jnp.int32, (tall, LINE), 1)
                    now = tile(0)
                    for j in range(per_row):
                        later = tile(j + 1)
                        stage[side, :, j * LINE : (j + 1) * LINE] = jnp.where(
                            lanes < LINE - lane, now, later
                        ).astype(jnp.bfloat16)
                        now = later
                else:
                    for j in range(per_row):
                        stage[side, :, j * LINE : (j + 1) * LINE] = tile(j).astype(jnp.bfloat16)
                written(block, side).start()

                @pl.when(block == blocks - 1)
                def _():
                    if blocks > 1:
                        written(block - 1, 1 - side).wait()
                    written(block, side).wait()

    return pl.pallas_call(
        pinned(kernel, 2 + count_buffers, after),
        grid_spec=pltpu.PrefetchScalarGridSpec(
            num_scalar_prefetch=2,
            grid=(total,),
            in_specs=[pl.BlockSpec(memory_space=pl.ANY)] * count_buffers + pins(after),
            out_specs=[pl.BlockSpec(memory_space=pl.ANY)] * len(segments),
            scratch_shapes=[pltpu.VMEM((2,) + size, jnp.bfloat16) for size in sizes]
            + [
                pltpu.VMEM((DEPTH, 2, window, LINE), jnp.bfloat16),
                pltpu.VMEM((room, LINE), jnp.float32),
                pltpu.SemaphoreType.DMA((DEPTH, 2)),
                pltpu.SemaphoreType.DMA((2,)),
            ],
        ),
        out_shape=[jax.ShapeDtypeStruct((rows, columns), jnp.bfloat16) for _, rows, columns in segments],
        compiler_params=pltpu.CompilerParams(vmem_limit_bytes=48 * 2**20),
        cost_estimate=pl.CostEstimate(flops=0, bytes_accessed=total * window * LINE * 4, transcendentals=0),
        name="unpack",
    )(jnp.asarray(table), where, *buffers, *after)


def pack_lines(target, target_rows, first_row, segments, lane, phase, extras, carry, tail_rows, after=()):
    tall = 256
    lefts, rights, plan = [], [], []
    left_of, right_of = {}, {}
    row = first_row
    begin = 0
    for left, right in segments:
        for value, seen, kept in ((left, left_of, lefts), (right, right_of, rights)):
            if id(value) not in seen:
                seen[id(value)] = len(kept)
                kept.append(value)
        blocks = left.shape[1] // tall
        plan.append((left_of[id(left)], right_of[id(right)], right.shape[1] // LINE, begin, blocks, row))
        begin += blocks
        row += left.shape[1] * right.shape[1] // LINE
    end_row = row
    total = begin
    biggest = max(entry[2] for entry in plan) * tall
    tokens = lefts[0].shape[0]
    count_left, count_right, count_extra = len(lefts), len(rights), len(extras)
    rolled = [jnp.roll(right, lane, axis=1) if lane else right for right in rights]
    carry_in = [carry] if lane else []
    targets = [] if target is None else [target]

    def left_spec(index):
        mine = [entry for entry in plan if entry[0] == index]

        def place(step):
            block = 0
            for _, _, _, start, blocks, _ in mine:
                block = jnp.where(step >= start, jnp.minimum(step - start, blocks - 1), block)
            return (0, block)

        return pl.BlockSpec((tokens, tall), place)

    def kernel(*refs):
        left_refs = refs[:count_left]
        right_refs = refs[count_left : count_left + count_right]
        at = count_left + count_right
        extra_refs = refs[at : at + count_extra]
        at += count_extra
        carry_refs = refs[at : at + len(carry_in)]
        at += len(carry_in) + len(targets)
        out = refs[at]
        flat, stage, shift, last, sems, extra_sems = refs[at + 1 :]
        step = pl.program_id(0)
        side = lax.rem(step, 2)

        def extra_copy(k):
            rows = extras[k][0].shape[0]
            return pltpu.make_async_copy(
                extra_refs[k], out.at[pl.ds(extras[k][1], rows), :], extra_sems.at[k]
            )

        @pl.when(step == 0)
        def _():
            for k in range(count_extra):
                extra_copy(k).start()
            if lane:
                shift[0:8, :] = carry_refs[0][...]
            if phase:
                flat[0:8, :] = jnp.zeros((8, LINE), jnp.float32)

        for left_at, right_at, per_row, start, blocks, row in plan:
            lines = per_row * tall

            def written(block, s, row=row, lines=lines):
                return pltpu.make_async_copy(
                    stage.at[s, pl.ds(0, lines), :],
                    out.at[pl.ds(pl.multiple_of(row + block * lines, 16), lines), :],
                    sems.at[s],
                )

            @pl.when((step >= start) & (step < start + blocks))
            def _():
                block = step - start
                if phase:

                    @pl.when(step > 0)
                    def _():
                        flat[0:8, :] = flat[lines : lines + 8, :]

                turned = left_refs[left_at][...].T
                lanes = lax.broadcasted_iota(jnp.int32, (tall, LINE), 1)
                for j0 in range(0, per_row, 2):
                    wide = min(2, per_row - j0)
                    tile = jnp.dot(
                        turned,
                        right_refs[right_at][:, j0 * LINE : (j0 + wide) * LINE],
                        preferred_element_type=jnp.float32,
                    )
                    for j in range(wide):
                        piece = tile[:, j * LINE : (j + 1) * LINE]
                        if lane and j0 + j == 0:
                            shift[8 : 8 + tall, :] = piece
                            piece = jnp.where(lanes < lane, shift[7 : 7 + tall, :], piece)
                            shift[0:8, :] = shift[tall : tall + 8, :]
                        if per_row == 1:
                            flat[phase : phase + tall, :] = piece
                        else:
                            flat[pl.ds(phase + j0 + j, tall, stride=per_row), :] = piece

                stage[side, 0:lines, :] = flat[0:lines, :].astype(jnp.bfloat16)
                written(block, side).start()

            @pl.when((step > start) & (step <= start + blocks))
            def _():
                written(step - start - 1, 1 - side).wait()

            if start + blocks == total:

                @pl.when(step == total - 1)
                def _():
                    written(blocks - 1, side).wait()

        @pl.when(step == total - 1)
        def _():
            if tail_rows:
                lanes = lax.broadcasted_iota(jnp.int32, (tail_rows, LINE), 1)
                rows_at = lax.broadcasted_iota(jnp.int32, (tail_rows, LINE), 0)
                final = jnp.broadcast_to(shift[7:8, :], (tail_rows, LINE))
                last[...] = jnp.where((rows_at == 0) & (lanes < lane), final, 0.0).astype(jnp.bfloat16)
                closing = pltpu.make_async_copy(
                    last, out.at[pl.ds(end_row, tail_rows), :], extra_sems.at[count_extra]
                )
                closing.start()
                closing.wait()
            for k in range(count_extra):
                extra_copy(k).wait()

    whole = [pl.BlockSpec(array.shape, lambda step: (0, 0)) for array in rolled]
    flops = sum(2 * tokens * entry[4] * tall * entry[2] * LINE for entry in plan)
    inputs = count_left + count_right + count_extra + len(carry_in) + len(targets)
    return pl.pallas_call(
        pinned(kernel, inputs, after),
        grid=(total,),
        in_specs=[left_spec(k) for k in range(count_left)]
        + whole
        + [pl.BlockSpec(array.shape, lambda step: (0, 0)) for array, _ in extras]
        + [pl.BlockSpec(array.shape, lambda step: (0, 0)) for array in carry_in]
        + [pl.BlockSpec(memory_space=pl.ANY)] * len(targets)
        + pins(after),
        out_specs=pl.BlockSpec(memory_space=pl.ANY),
        out_shape=jax.ShapeDtypeStruct((target_rows, LINE), jnp.bfloat16),
        scratch_shapes=[
            pltpu.VMEM((biggest + 16, LINE), jnp.float32),
            pltpu.VMEM((2, biggest, LINE), jnp.bfloat16),
            pltpu.VMEM((tall + 8, LINE), jnp.float32),
            pltpu.VMEM((max(tail_rows, 16), LINE), jnp.bfloat16),
            pltpu.SemaphoreType.DMA((2,)),
            pltpu.SemaphoreType.DMA((count_extra + 1,)),
        ],
        input_output_aliases={count_left + count_right + count_extra + len(carry_in): 0} if targets else {},
        compiler_params=pltpu.CompilerParams(vmem_limit_bytes=48 * 2**20),
        cost_estimate=pl.CostEstimate(flops=flops, bytes_accessed=total * biggest * LINE * 2, transcendentals=0),
        name="pack",
    )(*lefts, *rolled, *[array for array, _ in extras], *carry_in, *targets, *after)


def added(*parts):
    total = parts[0].astype(jnp.float32)
    for part in parts[1:]:
        total = total + part.astype(jnp.float32)
    return total.astype(jnp.bfloat16)


class Flow:
    def __init__(self, stages):
        self.stages = stages
        self.sends = next(stages)
        self.result = None

    def values(self):
        return [value for value, _, _ in self.sends]

    def go(self):
        arrived = [lax.ppermute(value, axis, pairs) for value, axis, pairs in self.sends]
        try:
            self.sends = self.stages.send(arrived)
        except StopIteration as stop:
            self.sends, self.result = [], stop.value
        return self


def reduce_stages(flat, batch, shift):
    z, y, x, c = (lax.axis_index(name) for name in GRID)
    length = PLANE + 32
    send = lax.dynamic_slice(flat, ((1 - c) * PLANE, 0), (length, LINE))
    (arrived,) = yield [(send, "c", SWAP)]
    chip = added(lax.dynamic_slice(flat, (c * PLANE, 0), (length, LINE)), arrived)

    def window(sy, sx, part):
        shard = sy * 4 + sx * 2 + part
        start = (shift + SHARD * shard) // 16 * 16
        return lax.dynamic_slice(chip, (start, 0), (WIN, LINE))

    away_0 = jnp.stack([window(1 - y, 0, 0), window(1 - y, 1, 0)])
    away_1 = jnp.stack([window(0, 1 - x, 1), window(1, 1 - x, 1)])
    home_0 = jnp.stack([window(y, 0, 0), window(y, 1, 0)])
    home_1 = jnp.stack([window(0, x, 1), window(1, x, 1)])
    got_0, got_1 = yield [(away_0, "y", SWAP), (away_1, "x", SWAP)]
    half_0, half_1 = added(home_0, got_0), added(home_1, got_1)
    pick = lambda value, at: lax.dynamic_index_in_dim(value, at, 0, keepdims=False)
    got_0, got_1 = yield [(pick(half_0, 1 - x), "x", SWAP), (pick(half_1, 1 - y), "y", SWAP)]
    columns = [added(pick(half_0, x), got_0), added(pick(half_1, y), got_1)]
    if batch == 0:
        hops = [((1, 0, 0), (2, 1, 1)), ((2, 0, 0), (3, 1, 1)), ((3, 0, 0), (0, 1, 1))]
    else:
        hops = [((1, 2, 0), (2, 3, 1)), ((0, 2, 0), (1, 3, 1)), ((3, 2, 0), (0, 3, 1))]
    got = yield [(column, ZC, zc_pairs(*hop)) for column in columns for hop in hops]
    ends = [added(columns[0], *got[:3]), added(columns[1], *got[3:])]
    mine = jnp.where(c == 0, ends[0], ends[1])
    other = jnp.where(c == 0, ends[1], ends[0])
    (handed,) = yield [(other, ZC, [(2 * k + k % 2, 2 * k + 1 - k % 2) for k in range(4)])]
    return jnp.where(c == z % 2, mine, handed)


PIECE = 400


def corner_stages(flat):
    z, y, x, c = (lax.axis_index(name) for name in GRID)
    length = 8 * PIECE
    second = (8 + SHARD) // 16 * 16
    take = lambda at: lax.dynamic_slice(flat, (at * second, 0), (length, LINE))
    (arrived,) = yield [(take(1 - c), "c", SWAP)]
    chip = added(take(c), arrived).reshape(2, 2, 2, PIECE, LINE)
    pick = lambda value, at: lax.dynamic_index_in_dim(value, at, 0, keepdims=False)
    got = yield [(pick(chip[0], 1 - x), "x", SWAP), (pick(chip[1], 1 - y), "y", SWAP)]
    halves = [added(pick(chip[0], x), got[0]), added(pick(chip[1], y), got[1])]
    got = yield [(pick(halves[0], 1 - y), "y", SWAP), (pick(halves[1], 1 - x), "x", SWAP)]
    pieces = jnp.stack([added(pick(halves[0], y), got[0]), added(pick(halves[1], x), got[1])])
    got = yield [(pieces, "z", [(k, 0)]) for k in (1, 2, 3)]
    pieces = added(pieces, *got)
    got = yield [(pieces[0], "y", [(1, 0)]), (pieces[1], "x", [(1, 0)])]
    halves = [jnp.stack([pieces[0], got[0]]), jnp.stack([pieces[1], got[1]])]
    got = yield [(halves[0], "x", [(1, 0)]), (halves[1], "y", [(1, 0)])]
    return jnp.stack([halves[0], got[0], halves[1], got[1]]).reshape(length, LINE)


CHUNK = 128
NT = (((1,), (1,)), ((), ()))
TN = (((0,), (0,)), ((), ()))
INNER = SSM_HEADS * SSM_DIM
PAIRS = SSM_HEADS // 2


def spread(rows_a, rows_b):
    length = rows_a.shape[1]
    tall = jnp.concatenate(
        [jnp.broadcast_to(rows_a, (SSM_DIM, length)), jnp.broadcast_to(rows_b, (SSM_DIM, length))], axis=0
    )
    return tall.T


def weighted_state(left, values, weight_rows, after=()):
    rows = left.shape[0]

    def kernel(left_ref, value_ref, weight_ref, out_ref, turned):
        @pl.when(pl.program_id(0) == 0)
        def _():
            turned[...] = left_ref[...].T.astype(jnp.bfloat16)

        wide = spread(weight_ref[0, 0:1, :], weight_ref[0, 1:2, :])
        scaled = (value_ref[...] * wide).astype(jnp.bfloat16)
        out_ref[...] = jnp.dot(turned[...], scaled, preferred_element_type=jnp.float32)

    return pl.pallas_call(
        pinned(kernel, 3, after),
        grid=(PAIRS,),
        in_specs=[
            pl.BlockSpec((rows, STATE), lambda i: (0, 0)),
            pl.BlockSpec((rows, 2 * SSM_DIM), lambda i: (0, i)),
            pl.BlockSpec((1, 2, rows), lambda i: (i, 0, 0)),
        ] + pins(after),
        out_specs=pl.BlockSpec((STATE, 2 * SSM_DIM), lambda i: (0, i)),
        out_shape=jax.ShapeDtypeStruct((STATE, INNER), jnp.float32),
        scratch_shapes=[pltpu.VMEM((STATE, rows), jnp.bfloat16)],
        cost_estimate=pl.CostEstimate(flops=2 * rows * STATE * INNER, bytes_accessed=rows * INNER * 4, transcendentals=0),
        name="state",
    )(left, values, weight_rows.reshape(PAIRS, 2, rows), *after)


def chunk_rows(k, meta_ref, cum_ref, start_ref):
    here = slice(k * CHUNK, (k + 1) * CHUNK)
    first = meta_ref[0] + k * CHUNK
    index = first + lax.broadcasted_iota(jnp.int32, (1, CHUNK), 1)
    entering = start_ref[0:1, here] < first
    ending = index >= meta_ref[1 + k]
    cums, entries, tails = [], [], []
    for e in range(2):
        cum = cum_ref[0, e : e + 1, here]
        cums.append(cum)
        entries.append(jnp.where(entering, jnp.exp(cum), 0.0))
        gap = jnp.where(ending, cum[:, CHUNK - 1 :] - cum, masked_score)
        tails.append(jnp.exp(gap))
    return cums, entries, tails


def ssm_forward(x, b_in, c_in, cum, step, state_in, skip, meta, start_column, start_row):
    rows = x.shape[0]
    chunks = rows // CHUNK

    def kernel(meta_ref, x_ref, b_ref, c_ref, cum_ref, step_ref, state_ref, skip_ref, col_ref, row_ref,
               y_ref, inner, hide, state, b_turned):
        @pl.when(pl.program_id(0) == 0)
        def _():
            for k in range(chunks):
                here = slice(k * CHUNK, (k + 1) * CHUNK)
                b_turned[:, here] = b_ref[here, :].T.astype(jnp.bfloat16)
                inner[k] = lax.dot_general(
                    c_ref[here, :], b_ref[here, :], NT, precision=highest, preferred_element_type=jnp.float32
                )
                t = lax.broadcasted_iota(jnp.int32, (CHUNK, CHUNK), 0)
                s = lax.broadcasted_iota(jnp.int32, (CHUNK, CHUNK), 1)
                shown = (s <= t) & (meta_ref[0] + k * CHUNK + s >= col_ref[here, :])
                hide[k] = jnp.where(shown, 0.0, masked_score)

        low_lane = lax.broadcasted_iota(jnp.int32, (CHUNK, 2 * SSM_DIM), 1) < SSM_DIM
        state[...] = state_ref[...]
        for k in range(chunks):
            here = slice(k * CHUNK, (k + 1) * CHUNK)
            cums, entries, tails = chunk_rows(k, meta_ref, cum_ref, row_ref)
            x_now = x_ref[here, :]
            x_low = x_now.astype(jnp.bfloat16)
            entry = spread(*entries)
            weight = spread(*[tails[e] * step_ref[0, e : e + 1, here] for e in range(2)])
            parts = []
            for e in range(2):
                across = jnp.broadcast_to(cums[e], (CHUNK, CHUNK))
                decays = jnp.exp(across.T - across + hide[k])
                mix = (inner[k] * decays * step_ref[0, e : e + 1, here]).astype(jnp.bfloat16)
                parts.append(jnp.dot(mix, x_low, preferred_element_type=jnp.float32))
            carried = jnp.dot(
                c_ref[here, :].astype(jnp.bfloat16), state[...].astype(jnp.bfloat16),
                preferred_element_type=jnp.float32,
            )
            y_ref[here, :] = jnp.where(low_lane, parts[0], parts[1]) + entry * carried + skip_ref[...] * x_now
            fresh = jnp.dot(
                b_turned[:, here], (x_now * weight).astype(jnp.bfloat16), preferred_element_type=jnp.float32
            )
            state[...] = entry[CHUNK - 1 :, :] * state[...] + fresh

    whole = lambda i, m: (0, 0)
    lanes = lambda i, m: (0, i)
    return pl.pallas_call(
        kernel,
        grid_spec=pltpu.PrefetchScalarGridSpec(
            num_scalar_prefetch=1,
            grid=(PAIRS,),
            in_specs=[
                pl.BlockSpec((rows, 2 * SSM_DIM), lanes),
                pl.BlockSpec((rows, STATE), whole),
                pl.BlockSpec((rows, STATE), whole),
                pl.BlockSpec((1, 2, rows), lambda i, m: (i, 0, 0)),
                pl.BlockSpec((1, 2, rows), lambda i, m: (i, 0, 0)),
                pl.BlockSpec((STATE, 2 * SSM_DIM), lanes),
                pl.BlockSpec((1, 2 * SSM_DIM), lanes),
                pl.BlockSpec((rows, 1), whole),
                pl.BlockSpec((8, rows), whole),
            ],
            out_specs=pl.BlockSpec((rows, 2 * SSM_DIM), lanes),
            scratch_shapes=[
                pltpu.VMEM((chunks, CHUNK, CHUNK), jnp.float32),
                pltpu.VMEM((chunks, CHUNK, CHUNK), jnp.float32),
                pltpu.VMEM((STATE, 2 * SSM_DIM), jnp.float32),
                pltpu.VMEM((STATE, rows), jnp.bfloat16),
            ],
        ),
        out_shape=jax.ShapeDtypeStruct((rows, INNER), jnp.float32),
        compiler_params=pltpu.CompilerParams(vmem_limit_bytes=40 * 2**20),
        cost_estimate=pl.CostEstimate(flops=10**9, bytes_accessed=rows * INNER * 8, transcendentals=2**21),
        name="ssm",
    )(meta, x, b_in, c_in, cum.reshape(PAIRS, 2, rows), step.reshape(PAIRS, 2, rows), state_in, skip,
      start_column, start_row)


def ssm_backward(x, dy, b_in, c_in, cum, step, state_in, state_grad, skip, meta, start_row, after=()):
    rows = x.shape[0]
    chunks = rows // CHUNK

    def kernel(meta_ref, x_ref, dy_ref, b_ref, c_ref, cum_ref, step_ref, state_ref, grad_ref, skip_ref, row_ref,
               dx_ref, db_ref, dc_ref, small_ref, inner, hide, inner_grad, states, flow,
               b_turned, c_turned):
        low = lambda v: v.astype(jnp.bfloat16)
        dot = lambda p, q, dims=(((1,), (0,)), ((), ())): lax.dot_general(
            p, q, dims, preferred_element_type=jnp.float32
        )
        exact = lambda p, q, dims=(((1,), (0,)), ((), ())): lax.dot_general(
            p, q, dims, precision=highest, preferred_element_type=jnp.float32
        )
        s = lax.broadcasted_iota(jnp.int32, (CHUNK, CHUNK), 0)
        t = lax.broadcasted_iota(jnp.int32, (CHUNK, CHUNK), 1)

        @pl.when(pl.program_id(0) == 0)
        def _():
            db_ref[...] = jnp.zeros(db_ref.shape, jnp.float32)
            dc_ref[...] = jnp.zeros(dc_ref.shape, jnp.float32)
            inner_grad[...] = jnp.zeros(inner_grad.shape, jnp.float32)
            for k in range(chunks):
                here = slice(k * CHUNK, (k + 1) * CHUNK)
                b_turned[:, here] = low(b_ref[here, :].T)
                c_turned[:, here] = low(c_ref[here, :].T)
                inner[k] = exact(b_ref[here, :], c_ref[here, :], NT)
                shown = (s <= t) & (meta_ref[0] + k * CHUNK + s >= row_ref[0:1, here])
                hide[k] = jnp.where(shown, 0.0, masked_score)

        before = (s < t).astype(jnp.float32)
        until = low((s >= t).astype(jnp.float32))
        low_lane = t < SSM_DIM
        pick_row = lax.broadcasted_iota(jnp.int32, (8, 2 * SSM_DIM), 0)
        pick_lane = lax.broadcasted_iota(jnp.int32, (8, 2 * SSM_DIM), 1) // SSM_DIM
        pick = low((pick_row == pick_lane).astype(jnp.float32))
        spreads = []
        states[0] = state_ref[...]
        for k in range(chunks):
            here = slice(k * CHUNK, (k + 1) * CHUNK)
            cums, entries, tails = chunk_rows(k, meta_ref, cum_ref, row_ref)
            entry, tail = spread(*entries), spread(*tails)
            steps = spread(step_ref[0, 0:1, here], step_ref[0, 1:2, here])
            spreads.append((cums, entry, tail, steps))
            if k < chunks - 1:
                fresh = dot(b_turned[:, here], low(x_ref[here, :] * steps * tail))
                states[k + 1] = entry[CHUNK - 1 :, :] * states[k] + fresh
        flow[...] = grad_ref[...]
        skip_sum = jnp.zeros((1, 2 * SSM_DIM), jnp.float32)
        for k in reversed(range(chunks)):
            here = slice(k * CHUNK, (k + 1) * CHUNK)
            cums, entry, tail, steps = spreads[k]
            x_now, dy_now = x_ref[here, :], dy_ref[here, :]
            b_low, c_low = low(b_ref[here, :]), low(c_ref[here, :])
            scaled = x_now * steps
            dy_low = low(dy_now)
            flow_low, state_low = low(flow[...]), low(states[k])
            mixed, within = [], []
            for e in range(2):
                across = jnp.broadcast_to(cums[e], (CHUNK, CHUNK))
                decays = jnp.exp(across - across.T + hide[k])
                own = low(jnp.where(low_lane == (e == 0), scaled, 0.0))
                reach = decays * dot(own, dy_low, NT)
                inner_grad[k] += reach
                sums = dot(low(inner[k] * reach), until)
                within.append(jnp.sum(sums * before, axis=0, keepdims=True))
                mixed.append(dot(low(inner[k] * decays), dy_low))
            back = tail * dot(b_low, flow_low)
            dxs = jnp.where(low_lane, mixed[0], mixed[1]) + back
            db_ref[here, :] += dot(low(scaled * tail), flow_low, NT)
            entered = low(dy_now * entry)
            dc_ref[here, :] += dot(entered, state_low, NT)
            brought = dy_now * entry * dot(c_low, state_low)
            ends = dot(pick, low(brought), NT)
            begins = dot(pick, low(scaled * back), NT)
            direct = dot(pick, low(x_now * dxs), NT)
            through = jnp.sum(flow[...] * states[k], axis=0, keepdims=True) * entry[CHUNK - 1 :, :]
            log_grad = exact(ends, until.astype(jnp.float32)) + exact(begins, before)
            for e in range(2):
                lanes = slice(e * SSM_DIM, (e + 1) * SSM_DIM)
                kept = jnp.sum(through[:, lanes], axis=1, keepdims=True)
                small_ref[0, e : e + 1, here] = direct[e : e + 1, :]
                small_ref[0, 2 + e : 3 + e, here] = log_grad[e : e + 1, :] + within[e] + kept
            dx_ref[here, :] = dxs * steps + skip_ref[...] * dy_now
            skip_sum += jnp.sum(x_now * dy_now, axis=0, keepdims=True)
            flow[...] = entry[CHUNK - 1 :, :] * flow[...] + dot(c_turned[:, here], entered)
        small_ref[0, 4:8, :] = jnp.zeros((4, rows), jnp.float32)
        small_ref[0, 4:5, 0 : 2 * SSM_DIM] = skip_sum

        @pl.when(pl.program_id(0) == PAIRS - 1)
        def _():
            for k in range(chunks):
                here = slice(k * CHUNK, (k + 1) * CHUNK)
                grads = low(inner_grad[k])
                db_ref[here, :] += dot(grads, low(c_ref[here, :]))
                dc_ref[here, :] += dot(grads, low(b_ref[here, :]), TN)

    whole = lambda i, m: (0, 0)
    lanes = lambda i, m: (0, i)
    pair = lambda i, m: (i, 0, 0)
    return pl.pallas_call(
        pinned(kernel, 11, after),
        grid_spec=pltpu.PrefetchScalarGridSpec(
            num_scalar_prefetch=1,
            grid=(PAIRS,),
            in_specs=[
                pl.BlockSpec((rows, 2 * SSM_DIM), lanes),
                pl.BlockSpec((rows, 2 * SSM_DIM), lanes),
                pl.BlockSpec((rows, STATE), whole),
                pl.BlockSpec((rows, STATE), whole),
                pl.BlockSpec((1, 2, rows), pair),
                pl.BlockSpec((1, 2, rows), pair),
                pl.BlockSpec((STATE, 2 * SSM_DIM), lanes),
                pl.BlockSpec((STATE, 2 * SSM_DIM), lanes),
                pl.BlockSpec((1, 2 * SSM_DIM), lanes),
                pl.BlockSpec((8, rows), whole),
            ] + pins(after),
            out_specs=[
                pl.BlockSpec((rows, 2 * SSM_DIM), lanes),
                pl.BlockSpec((rows, STATE), whole),
                pl.BlockSpec((rows, STATE), whole),
                pl.BlockSpec((1, 8, rows), pair),
            ],
            scratch_shapes=[
                pltpu.VMEM((chunks, CHUNK, CHUNK), jnp.float32),
                pltpu.VMEM((chunks, CHUNK, CHUNK), jnp.float32),
                pltpu.VMEM((chunks, CHUNK, CHUNK), jnp.float32),
                pltpu.VMEM((chunks, STATE, 2 * SSM_DIM), jnp.float32),
                pltpu.VMEM((STATE, 2 * SSM_DIM), jnp.float32),
                pltpu.VMEM((STATE, rows), jnp.bfloat16),
                pltpu.VMEM((STATE, rows), jnp.bfloat16),
            ],
        ),
        out_shape=[
            jax.ShapeDtypeStruct((rows, INNER), jnp.float32),
            jax.ShapeDtypeStruct((rows, STATE), jnp.float32),
            jax.ShapeDtypeStruct((rows, STATE), jnp.float32),
            jax.ShapeDtypeStruct((PAIRS, 8, rows), jnp.float32),
        ],
        compiler_params=pltpu.CompilerParams(vmem_limit_bytes=40 * 2**20),
        cost_estimate=pl.CostEstimate(flops=3 * 10**9, bytes_accessed=rows * INNER * 12, transcendentals=2**21),
        name="ssm_back",
    )(meta, x, dy, b_in, c_in, cum.reshape(PAIRS, 2, rows), step.reshape(PAIRS, 2, rows), state_in, state_grad,
      skip, start_row, *after)


def chain_states(earlier, later):
    return (earlier[0] * later[0], earlier[1] * later[0] + later[1])


def scan_states(carry, state, span, fast, backward):
    wide = jnp.repeat(carry, SSM_DIM)[None, :]
    if not fast:
        ident = (jnp.ones_like(wide), jnp.zeros_like(state))
        return (carried_in if backward else prefix)((wide, state), span, chain_states, ident)[1]
    total = (wide, state)
    start = None
    for name in ("c", "x", "y"):
        place = lax.axis_index(name)
        packed = jnp.concatenate([total[1], jnp.broadcast_to(total[0], (16, INNER))], axis=0)
        packed = lax.ppermute(packed.astype(jnp.bfloat16), name, SWAP).astype(jnp.float32)
        other = (packed[STATE : STATE + 1], packed[:STATE])
        leads = place == (0 if backward else 1)
        seen = (jnp.where(leads, other[0], 1.0), jnp.where(leads, other[1], 0.0))
        start = seen if start is None else chain_states(seen, start)
        if name != "y":
            forward = chain_states(other, total)
            reverse = chain_states(total, other)
            total = jax.tree.map(lambda p, q: jnp.where(leads, p, q), forward, reverse)
    return start[1]


KEYS = 512
PAIR = 2 * HEAD_DIM


def attention_forward(q_wide, kv, meta, starts, after=()):
    rows = q_wide.shape[1]
    blocks = kv.shape[0]
    ratio = HEADS_Q // HEADS_KV
    wide = min(256, rows)

    def kernel(meta_ref, q_ref, kv_ref, start_ref, o_ref, log_ref, top, total):
        b = pl.program_id(1)

        @pl.when(b == 0)
        def _():
            top[...] = jnp.full(top.shape, masked_score, jnp.float32)
            total[...] = jnp.zeros(total.shape, jnp.float32)
            o_ref[...] = jnp.zeros(o_ref.shape, jnp.float32)

        def block(partial):
            pair = kv_ref[0, 0]
            turned = pair.T[HEAD_DIM:, :]
            for h in range(ratio):
                for r in range(0, rows, wide):
                    here = slice(r, r + wide)
                    scores = lax.dot_general(pair, q_ref[h, here, :], NT, preferred_element_type=jnp.float32)
                    if partial:
                        keys = b * KEYS + lax.broadcasted_iota(jnp.int32, scores.shape, 0)
                        mine = meta_ref[2] + r + lax.broadcasted_iota(jnp.int32, scores.shape, 1)
                        visible = (keys >= start_ref[0:1, here]) & (keys <= mine)
                        scores = jnp.where(visible, scores, masked_score)
                    before = top[h, 0:1, here]
                    peak = jnp.maximum(before, jnp.max(scores, axis=0, keepdims=True))
                    part = jnp.exp(scores - peak)
                    if partial:
                        part = jnp.where(visible, part, 0.0)
                    fade = jnp.exp(before - peak)
                    top[h, 0:1, here] = peak
                    total[h, 0:1, here] = total[h, 0:1, here] * fade + jnp.sum(part, axis=0, keepdims=True)
                    o_ref[h, :, here] = o_ref[h, :, here] * fade + jnp.dot(
                        turned, part.astype(jnp.bfloat16), preferred_element_type=jnp.float32
                    )

        needed = (b >= meta_ref[0]) & (b < meta_ref[1])
        partial = ((b + 1) * KEYS > meta_ref[2]) | (b * KEYS < meta_ref[3])

        @pl.when(needed & partial)
        def _():
            block(True)

        @pl.when(needed & jnp.logical_not(partial))
        def _():
            block(False)

        @pl.when(b == blocks - 1)
        def _():
            for h in range(ratio):
                sums = total[h, 0:1, :]
                o_ref[h] = o_ref[h] / sums
                log_ref[h] = jnp.broadcast_to(top[h, 0:1, :] + jnp.log(sums), (8, rows))

    heads = lambda g, b, m: (g, 0, 0)
    return pl.pallas_call(
        pinned(kernel, 4, after),
        grid_spec=pltpu.PrefetchScalarGridSpec(
            num_scalar_prefetch=1,
            grid=(HEADS_KV, blocks),
            in_specs=[
                pl.BlockSpec((ratio, rows, PAIR), heads),
                pl.BlockSpec((1, 1, KEYS, PAIR), lambda g, b, m: (b, g, 0, 0)),
                pl.BlockSpec((8, rows), lambda g, b, m: (0, 0)),
            ] + pins(after),
            out_specs=[
                pl.BlockSpec((ratio, HEAD_DIM, rows), heads),
                pl.BlockSpec((ratio, 8, rows), heads),
            ],
            scratch_shapes=[
                pltpu.VMEM((ratio, 8, rows), jnp.float32),
                pltpu.VMEM((ratio, 8, rows), jnp.float32),
            ],
        ),
        out_shape=[
            jax.ShapeDtypeStruct((HEADS_Q, HEAD_DIM, rows), jnp.float32),
            jax.ShapeDtypeStruct((HEADS_Q, 8, rows), jnp.float32),
        ],
        compiler_params=pltpu.CompilerParams(vmem_limit_bytes=48 * 2**20),
        cost_estimate=pl.CostEstimate(flops=2 * 10**10, bytes_accessed=2**23, transcendentals=2**23),
        name="attend",
    )(meta, q_wide, kv, starts, *after)


def attention_backward(q_wide, g_wide, kv, logs, mixed, meta, starts, group, after=()):
    rows = q_wide.shape[1]
    blocks = kv.shape[0]
    ratio = HEADS_Q // HEADS_KV
    wide = min(256, rows)

    def kernel(meta_ref, q_ref, g_ref, kv_ref, log_ref, o_ref, start_ref, dkv_ref, dq_ref, delta, sums):
        b = pl.program_id(0)

        @pl.when(b == 0)
        def _():
            dq_ref[...] = jnp.zeros(dq_ref.shape, jnp.float32)
            for h in range(ratio):
                both = g_ref[h].astype(jnp.float32).T[HEAD_DIM:, :] * o_ref[h]
                delta[h] = jnp.broadcast_to(jnp.sum(both, axis=0, keepdims=True), (8, rows))

        def block(partial):
            pair = kv_ref[0, 0]
            turned = pair.T[:HEAD_DIM, :]
            for h in range(ratio):
                for r in range(0, rows, wide):
                    here = slice(r, r + wide)
                    q_now = q_ref[h, here, :]
                    g_now = g_ref[h, here, :]
                    scores = lax.dot_general(pair, q_now, NT, preferred_element_type=jnp.float32)
                    probs = jnp.exp(scores - log_ref[h, 0:1, here])
                    if partial:
                        keys = b * KEYS + lax.broadcasted_iota(jnp.int32, scores.shape, 0)
                        mine = meta_ref[2] + r + lax.broadcasted_iota(jnp.int32, scores.shape, 1)
                        visible = (keys >= start_ref[0:1, here]) & (keys <= mine)
                        probs = jnp.where(visible, probs, 0.0)
                    grads = lax.dot_general(pair, g_now, NT, preferred_element_type=jnp.float32)
                    low_grads = (probs * (grads - delta[h, 0:1, here])).astype(jnp.bfloat16)
                    change = jnp.dot(
                        probs.astype(jnp.bfloat16), g_now, preferred_element_type=jnp.float32
                    ) + jnp.dot(low_grads, q_now, preferred_element_type=jnp.float32)
                    if h == 0 and r == 0:
                        sums[...] = change
                    else:
                        sums[...] += change
                    dq_ref[h, :, here] += jnp.dot(turned, low_grads, preferred_element_type=jnp.float32)
            dkv_ref[0, 0] = sums[...].astype(jnp.bfloat16)

        needed = (b >= meta_ref[0]) & (b < meta_ref[1])
        partial = ((b + 1) * KEYS > meta_ref[2]) | (b * KEYS < meta_ref[3])

        @pl.when(needed & partial)
        def _():
            block(True)

        @pl.when(needed & jnp.logical_not(partial))
        def _():
            block(False)

        @pl.when(jnp.logical_not(needed))
        def _():
            dkv_ref[0, 0] = jnp.zeros((KEYS, PAIR), jnp.bfloat16)

    heads = lambda b, m: (group, 0, 0)
    return pl.pallas_call(
        pinned(kernel, 7, after),
        grid_spec=pltpu.PrefetchScalarGridSpec(
            num_scalar_prefetch=1,
            grid=(blocks,),
            in_specs=[
                pl.BlockSpec((ratio, rows, PAIR), heads),
                pl.BlockSpec((ratio, rows, PAIR), heads),
                pl.BlockSpec((1, 1, KEYS, PAIR), lambda b, m: (b, group, 0, 0)),
                pl.BlockSpec((ratio, 8, rows), heads),
                pl.BlockSpec((ratio, HEAD_DIM, rows), heads),
                pl.BlockSpec((8, rows), lambda b, m: (0, 0)),
            ] + pins(after),
            out_specs=[
                pl.BlockSpec((1, 1, KEYS, PAIR), lambda b, m: (b, 0, 0, 0)),
                pl.BlockSpec((ratio, HEAD_DIM, rows), lambda b, m: (0, 0, 0)),
            ],
            scratch_shapes=[
                pltpu.VMEM((ratio, 8, rows), jnp.float32),
                pltpu.VMEM((KEYS, PAIR), jnp.float32),
            ],
        ),
        out_shape=[
            jax.ShapeDtypeStruct((blocks, 1, KEYS, PAIR), jnp.bfloat16),
            jax.ShapeDtypeStruct((ratio, HEAD_DIM, rows), jnp.float32),
        ],
        compiler_params=pltpu.CompilerParams(vmem_limit_bytes=48 * 2**20),
        cost_estimate=pl.CostEstimate(flops=2 * 10**10, bytes_accessed=2**23, transcendentals=2**23),
        name="attend_back",
    )(meta, q_wide, g_wide, kv, logs, mixed, starts, *after)


def ordered(place, own, other, axis):
    first = jnp.where(place == 0, own, other)
    second = jnp.where(place == 0, other, own)
    return jnp.stack([first, second], axis=axis)


def gather_span(value, span, fast):
    if not fast:
        return lax.all_gather(value, span)
    _, y, x, c = (lax.axis_index(name) for name in GRID)
    two = ordered(x, value, lax.ppermute(value, "x", SWAP), 0)
    four = ordered(y, two, lax.ppermute(two, "y", SWAP), 0)
    eight = ordered(c, four, lax.ppermute(four, "c", SWAP), 2)
    return eight.reshape((8,) + value.shape)


def scatter_span(value, span, fast):
    if not fast:
        return lax.psum_scatter(value, span, scatter_dimension=0).astype(jnp.float32)
    _, y, x, c = (lax.axis_index(name) for name in GRID)
    value = value.reshape((2, 2, 2) + value.shape[1:])
    for name, place, axis in (("c", c, 2), ("y", y, 0), ("x", x, 0)):
        keep = lax.dynamic_index_in_dim(value, place, axis, keepdims=False)
        send = lax.dynamic_index_in_dim(value, 1 - place, axis, keepdims=False)
        value = keep.astype(jnp.float32) + lax.ppermute(send, name, SWAP).astype(jnp.float32)
        if name != "x":
            value = value.astype(jnp.bfloat16)
    return value


def sum_all(value, axes, fast):
    if not fast:
        return lax.psum(value, axes)
    for name in GRID[1:]:
        value = value + lax.ppermute(value, name, SWAP)
    for pairs in ([(0, 1), (1, 0), (2, 3), (3, 2)], [(0, 2), (2, 0), (1, 3), (3, 1)]):
        value = value + lax.ppermute(value, "z", pairs)
    return value


def offsets_of():
    places, at = {}, 0
    for name_key, extent in layout():
        places[name_key] = (at, extent)
        at += math.prod(extent)
    return places


def early_weights(params):
    places = offsets_of()
    (early, late), where = gather_lines(params)
    names = (W_QUERY, W_KEY, W_VALUE, W_ATTN_OUT, W_GATE_SSM, W_X_SSM, W_B_C)
    misc_at = places[W_STEP][0]
    first = unpack_lines(
        early, 0, where, [flat_segment(name_key) for name_key in names] + [(0, 16, LINE), (misc_at, 288, LINE)]
    )
    weights = dict(zip(names, first))
    weights[NORM_ATTN] = first[-2].reshape(-1)[:D]
    misc = first[-1].reshape(-1)
    for name_key in (W_STEP,) + small_names[1:-1]:
        at, extent = places[name_key]
        weights[name_key] = misc[at - misc_at : at - misc_at + math.prod(extent)].reshape(extent)
    return weights, (early + late, where)


def flat_segment(name_key):
    at, extent = offsets_of()[name_key]
    return (at, extent[0], extent[1])


def late_weights(held, after):
    buffers, where = held
    names = (W_SSM_OUT, W_GATE, W_UP_PROJ, W_DOWN)
    norm_at = offsets_of()[NORM_FFN][0]
    second = unpack_lines(
        buffers, 0, where, [flat_segment(name_key) for name_key in names] + [(norm_at, 16, LINE)], after
    )
    weights = dict(zip(names, second))
    weights[NORM_FFN] = second[-1].reshape(-1)[norm_at % LINE : norm_at % LINE + D]
    return weights


def pack_late(gate, up, down, ssm_low, grad_branch, grad_norm_ffn, after):
    places = offsets_of()
    out_at = places[W_SSM_OUT][0]
    lane = places[W_GATE][0] % LINE
    boundary = 2 * PLANE * LINE
    tail_from = (boundary - out_at) // D
    tail = matmul_left_t(ssm_low[:, tail_from:], grad_branch).reshape(-1)
    tail = tail[boundary - out_at - tail_from * D :]
    head = jnp.concatenate([jnp.zeros((14 * LINE,), jnp.float32), tail, grad_norm_ffn])
    head_rows = head.shape[0] // LINE
    carry = jnp.zeros((8, LINE), jnp.float32).at[7, :lane].set(head[head_rows * LINE :])
    head = head[: head_rows * LINE].reshape(head_rows, LINE).astype(jnp.bfloat16)
    return pack_lines(
        None, 2 * PLANE + 32, head_rows, [gate, up, down], lane, 0, [(head, 0)], carry, 48, after
    )


def pack_out(ssm_low, grad_branch, after):
    out_at = offsets_of()[W_SSM_OUT][0]
    first_row = (8 + out_at // LINE) // 16 * 16
    rows = first_row + SSM_HEADS * SSM_DIM * D // LINE
    return pack_lines(
        None, rows, first_row, [(ssm_low, grad_branch)], out_at % LINE, (8 + out_at // LINE) % 8, [],
        jnp.zeros((8, LINE), jnp.float32), 0, after,
    )


def pack_ssm(target, segments, small, ssm_low, grad_branch, after):
    places = offsets_of()
    misc = [small[name_key].reshape(-1) for name_key in (W_STEP,) + small_names[1:-1]]
    count = sum(part.shape[0] for part in misc)
    misc_rows = (count // LINE + 16) // 16 * 16
    opening = matmul_left_t(ssm_low[:, :16], grad_branch).reshape(-1)
    misc = jnp.concatenate(misc + [opening[: misc_rows * LINE - count]])
    misc = misc.reshape(misc_rows, LINE).astype(jnp.bfloat16)
    first_row = 8 + places[W_ATTN_OUT][0] // LINE
    return pack_lines(
        target, target.shape[0], first_row, segments, 0, 0, [(misc, 8 + places[W_STEP][0] // LINE)], None, 0, after
    )


def pack_qkv(segments, attended, grad_branch, after):
    places = offsets_of()
    out_row = 8 + places[W_ATTN_OUT][0] // LINE
    rows = (8 + SHARD) // 16 * 16 + 8 * PIECE
    closing = matmul_left_t(attended[:, :16], grad_branch).reshape(-1, LINE)
    closing = closing[: rows - out_row].astype(jnp.bfloat16)
    return pack_lines(
        None, rows, 16, segments, 0, 0, [(jnp.zeros((16, LINE), jnp.bfloat16), 0), (closing, out_row)], None, 0, after
    )


def own_lines(early, late, corner, grad_norm_attn):
    z, y, x, c = (lax.axis_index(name) for name in GRID)
    place = 4 * y + 2 * x + c
    shard = SHARD * place
    start = jnp.where(z < 2, (8 + shard) % 16, (14 + shard) % 16)
    lines = jnp.where(z < 2, early, late)
    lines = jnp.where((z == 0) & (place < 2), corner[:WIN], lines)
    lines = lax.dynamic_slice(lines, (start, 0), (SHARD, LINE)).astype(jnp.float32)
    norms = jnp.where((z == 0) & (place == 0), grad_norm_attn.reshape(-1, LINE), lines[: D // LINE])
    return jnp.concatenate([norms, lines[D // LINE :]]).reshape(-1)


def body(span, group, fast, tokens, params, cotangent, offsets):
    rows_dev = tokens.shape[0]
    group_rows = rows_dev * lax.axis_size(span)
    all_rows = group_rows * lax.axis_size(group)
    ssm_inner = SSM_HEADS * SSM_DIM
    score_scale = HEAD_DIM ** (-0.5)
    bounds = offsets[0]
    my_start = lax.axis_index(span) * rows_dev
    row_index = my_start + jnp.arange(rows_dev, dtype=jnp.int32)
    seq_id, positions = sequence_info(row_index, bounds)
    first_start = row_index[0] - positions[0]
    last_row = my_start + rows_dev - 1
    cosine, sine = rotary_tables(positions)
    if fast:
        weights, held = early_weights(params)
    else:
        weights = unpack(lax.all_gather(params, group + span, axis=0, tiled=True))
    small_f32 = {name_key: weights[name_key].astype(jnp.float32) for name_key in small_names[:-1]}
    x_rows = tokens.astype(jnp.float32)
    normed_one, norm_one_back = jax.vjp(rms_norm, x_rows, small_f32[NORM_ATTN])
    hidden = normed_one.astype(jnp.bfloat16)
    query = matmul(hidden, weights[W_QUERY])
    key_raw = matmul(hidden, weights[W_KEY])
    value_low = matmul(hidden, weights[W_VALUE]).astype(jnp.bfloat16)
    q_rot = rotate(query, cosine, sine, HEADS_Q).astype(jnp.bfloat16)
    k_rot = rotate(key_raw, cosine, sine, HEADS_KV).astype(jnp.bfloat16)
    k_heads = k_rot.reshape(rows_dev, HEADS_KV, HEAD_DIM)
    v_heads = value_low.reshape(rows_dev, HEADS_KV, HEAD_DIM)
    kv_mine = jnp.concatenate([k_heads, v_heads], axis=2).transpose(1, 0, 2)
    key_blocks = gather_span(kv_mine.reshape(HEADS_KV, rows_dev, PAIR), span, fast)
    if rows_dev != KEYS:
        key_blocks = key_blocks.transpose(1, 0, 2, 3).reshape(HEADS_KV, -1, KEYS, PAIR).transpose(1, 0, 2, 3)
    row_starts = row_index - positions
    meta = jnp.stack(
        [first_start // KEYS, last_row // KEYS + 1, my_start, row_starts[rows_dev - 1]]
    ).astype(jnp.int32)
    q_low = (q_rot * jnp.bfloat16(score_scale)).reshape(rows_dev, HEADS_Q, HEAD_DIM).transpose(1, 0, 2)
    q_wide = jnp.pad(q_low, ((0, 0), (0, 0), (0, HEAD_DIM)))
    start_row = jnp.broadcast_to(row_starts[None, :], (8, rows_dev))
    mixed, logs = attention_forward(q_wide, key_blocks, meta, start_row)
    attended = mixed.astype(jnp.bfloat16).reshape(HEADS_Q * HEAD_DIM, rows_dev).T
    attn_out = matmul(attended, weights[W_ATTN_OUT])
    gate_ssm = matmul(hidden, weights[W_GATE_SSM])
    xbc = jnp.concatenate(
        [matmul(hidden, weights[W_X_SSM]), matmul(hidden, weights[W_B_C])], axis=1
    )
    step_raw = matmul(hidden, weights[W_STEP])
    rim_rows = passed_along(xbc[rows_dev - (CONV - 1) :], span, 1)
    extended = jnp.concatenate([rim_rows, xbc], axis=0)

    def conv_local(extended_in, conv_weight, conv_bias):
        return conv_apply(extended_in, conv_weight, conv_bias, positions)

    conv_values, conv_back = jax.vjp(
        conv_local, extended, small_f32[CONV_WEIGHT], small_f32[CONV_BIAS]
    )

    x_ssm = conv_values[:, :ssm_inner]
    b_in = conv_values[:, ssm_inner : ssm_inner + STATE]
    c_in = conv_values[:, ssm_inner + STATE :]
    step_in = step_raw.T + small_f32[STEP_BIAS][:, None]
    step_rows = jax.nn.softplus(step_in)
    decay = -jnp.exp(small_f32[DECAY_LOG])
    logs_step = step_rows * decay[:, None]
    order = jnp.arange(rows_dev)
    upto = (order[:, None] <= order[None, :]).astype(jnp.float32)
    cumul = jnp.dot(logs_step, upto, precision=highest)
    chunk_cum = jnp.dot(
        logs_step.reshape(-1, CHUNK), upto[:CHUNK, :CHUNK], precision=highest
    ).reshape(SSM_HEADS, rows_dev)
    went_on = row_starts < my_start
    entry_rows = jnp.where(went_on[None, :], jnp.exp(cumul), 0.0)
    in_last = row_index >= row_starts[rows_dev - 1]
    tail_rows = jnp.exp(jnp.where(in_last[None, :], cumul[:, -1:] - cumul, masked_score))
    carry_all = entry_rows[:, -1]
    local_state = weighted_state(b_in, x_ssm, tail_rows * step_rows)
    state_in = scan_states(carry_all, local_state, span, fast, False)
    skip_wide = jnp.repeat(small_f32[SKIP_GAIN], SSM_DIM)[None, :]
    ssm_meta = jnp.concatenate([my_start[None], row_starts[CHUNK - 1 :: CHUNK]]).astype(jnp.int32)
    ssm_y = ssm_forward(
        x_ssm, b_in, c_in, chunk_cum, step_rows, state_in, skip_wide, ssm_meta, row_starts[:, None], start_row
    )
    normed_ssm, gnorm_back = jax.vjp(gated_norm, ssm_y, gate_ssm, small_f32[NORM_SSM])
    ssm_low = normed_ssm.astype(jnp.bfloat16)
    if fast:
        weights.update(late_weights(held, [mixed]))
    small_f32[NORM_FFN] = weights[NORM_FFN].astype(jnp.float32)
    ssm_out = matmul(ssm_low, weights[W_SSM_OUT])
    middle = x_rows + attn_out + ssm_out
    normed_two, norm_two_back = jax.vjp(rms_norm, middle, small_f32[NORM_FFN])
    hidden_two = normed_two.astype(jnp.bfloat16)
    gate_ffn = matmul(hidden_two, weights[W_GATE])
    upper = matmul(hidden_two, weights[W_UP_PROJ])
    activation_f32, swiglu_back = jax.vjp(swiglu, gate_ffn, upper)
    activation = activation_f32.astype(jnp.bfloat16)
    ffn_out = matmul(activation, weights[W_DOWN])
    result = middle + ffn_out
    squares = jnp.stack(
        [
            jnp.sum(result * result),
            jnp.sum(attn_out * attn_out),
            jnp.sum(ssm_out * ssm_out),
            jnp.sum(ffn_out * ffn_out),
        ]
    )
    totals = sum_all(squares, group + span, fast)
    stats = jnp.sqrt(totals / (all_rows * D))
    grad_out = cotangent.astype(jnp.float32)
    grad_activation = matmul_right_t(cotangent, weights[W_DOWN])
    grad_gate_f32, grad_upper_f32 = swiglu_back(grad_activation)
    grad_gate = grad_gate_f32.astype(jnp.bfloat16)
    grad_upper = grad_upper_f32.astype(jnp.bfloat16)
    grad_hidden_two = matmul_right_t(grad_gate, weights[W_GATE]) + matmul_right_t(
        grad_upper, weights[W_UP_PROJ]
    )
    grad_middle_norm, grad_norm_ffn = norm_two_back(grad_hidden_two)
    grad_middle = grad_out + grad_middle_norm
    grad_branch = grad_middle.astype(jnp.bfloat16)
    grad_attended = matmul_right_t(grad_branch, weights[W_ATTN_OUT]).astype(jnp.bfloat16)
    grad_ssm_low = matmul_right_t(grad_branch, weights[W_SSM_OUT])
    grad_ssm_y, grad_gate_ssm_f32, grad_norm_ssm = gnorm_back(grad_ssm_low)
    grad_state_local = weighted_state(c_in, grad_ssm_y, entry_rows)
    pinned_by = ()
    if fast:
        late = pack_late(
            (hidden_two, grad_gate), (hidden_two, grad_upper), (activation, cotangent),
            ssm_low, grad_branch, grad_norm_ffn, [grad_state_local],
        )
        late_flow = Flow(reduce_stages(late, 1, 14))
        early = pack_out(ssm_low, grad_branch, late_flow.values())
        late_flow.go()
        pinned_by = late_flow.values()
    grad_state_out = scan_states(carry_all, grad_state_local, span, fast, True)
    grad_x, grad_b, grad_c, grad_small = ssm_backward(
        x_ssm, grad_ssm_y, b_in, c_in, chunk_cum, step_rows, state_in, grad_state_out, skip_wide, ssm_meta, start_row, pinned_by
    )
    grad_conv_values = jnp.concatenate([grad_x, grad_b, grad_c], axis=1)
    grad_direct = grad_small[:, 0:2].reshape(SSM_HEADS, rows_dev)
    grad_logs = grad_small[:, 2:4].reshape(SSM_HEADS, rows_dev)
    grad_decay_log = decay * jnp.sum(step_rows * grad_logs, axis=1)
    grad_step_rows = (grad_direct + decay[:, None] * grad_logs) * jax.nn.sigmoid(step_in)
    grad_step_bias = jnp.sum(grad_step_rows, axis=1)
    grad_step_raw_f32 = grad_step_rows.T
    grad_skip_gain = jnp.sum(grad_small[:, 4, : 2 * SSM_DIM].reshape(SSM_HEADS, SSM_DIM), axis=1)
    grad_extended, grad_conv_weight, grad_conv_bias = conv_back(grad_conv_values)
    rim_back = passed_along(grad_extended[: CONV - 1], span, -1)
    grad_xbc_f32 = grad_extended[CONV - 1 :]
    grad_xbc_f32 = grad_xbc_f32.at[rows_dev - (CONV - 1) :].add(rim_back)
    grad_xbc = grad_xbc_f32.astype(jnp.bfloat16)
    grad_gate_ssm = grad_gate_ssm_f32.astype(jnp.bfloat16)
    grad_step_raw = grad_step_raw_f32.astype(jnp.bfloat16)
    grad_w_step = matmul_left_t(hidden, grad_step_raw)
    grad_hidden_ssm = (
        matmul_right_t(grad_gate_ssm, weights[W_GATE_SSM])
        + matmul_right_t(grad_xbc[:, :ssm_inner], weights[W_X_SSM])
        + matmul_right_t(grad_xbc[:, ssm_inner:], weights[W_B_C])
        + matmul_right_t(grad_step_raw, weights[W_STEP])
    )
    small = {
        W_STEP: grad_w_step,
        CONV_WEIGHT: grad_conv_weight,
        CONV_BIAS: grad_conv_bias,
        STEP_BIAS: grad_step_bias,
        DECAY_LOG: grad_decay_log,
        SKIP_GAIN: grad_skip_gain,
        NORM_SSM: grad_norm_ssm,
        NORM_FFN: grad_norm_ffn,
    }
    g_low = grad_attended.reshape(rows_dev, HEADS_Q, HEAD_DIM).transpose(1, 0, 2)
    g_wide = jnp.pad(g_low, ((0, 0), (0, 0), (HEAD_DIM, 0)))
    if fast:
        late_flow.go()
        early = pack_ssm(
            early,
            [
                (attended, grad_branch), (hidden, grad_gate_ssm),
                (hidden, grad_xbc[:, :ssm_inner]), (hidden, grad_xbc[:, ssm_inner:]),
            ],
            small, ssm_low, grad_branch, late_flow.values(),
        )
        late_flow.go()
        early_flow = Flow(reduce_stages(early, 0, 8))
        pinned_by = late_flow.values() + early_flow.values()
    parts = []
    for group_at in range(HEADS_KV):
        parts.append(
            attention_backward(q_wide, g_wide, key_blocks, logs, mixed, meta, start_row, group_at, pinned_by)
        )
        if fast:
            early_flow.go()
            pinned_by = early_flow.values() + [parts[-1][1]]
    grad_kv = jnp.concatenate([part[0] for part in parts], axis=1)
    grad_q_turned = jnp.concatenate([part[1] for part in parts], axis=0)
    if rows_dev != KEYS:
        grad_kv = grad_kv.transpose(1, 0, 2, 3).reshape(HEADS_KV, -1, rows_dev, PAIR).transpose(1, 0, 2, 3)
    grad_kv_mine = scatter_span(grad_kv, span, fast)
    grad_keys_mine = grad_kv_mine[:, :, :HEAD_DIM].transpose(1, 0, 2).reshape(rows_dev, -1)
    grad_values_mine = grad_kv_mine[:, :, HEAD_DIM:].transpose(1, 0, 2).reshape(rows_dev, -1)
    grad_q_rot = grad_q_turned.reshape(HEADS_Q * HEAD_DIM, rows_dev).T * score_scale
    grad_query_low = rotate(grad_q_rot, cosine, -sine, HEADS_Q).astype(jnp.bfloat16)
    grad_key_low = rotate(grad_keys_mine, cosine, -sine, HEADS_KV).astype(jnp.bfloat16)
    grad_value_low = grad_values_mine.astype(jnp.bfloat16)
    if fast:
        corner = pack_qkv(
            [(hidden, grad_query_low), (hidden, grad_key_low), (hidden, grad_value_low)],
            attended, grad_branch, early_flow.values(),
        )
        early_flow.go()
        late_flow.go()
        corner_flow = Flow(corner_stages(corner))
        for flow in (early_flow, late_flow, corner_flow):
            while flow.sends:
                flow.go()
    grad_hidden = (
        grad_hidden_ssm
        + matmul_right_t(grad_query_low, weights[W_QUERY])
        + matmul_right_t(grad_key_low, weights[W_KEY])
        + matmul_right_t(grad_value_low, weights[W_VALUE])
    )
    grad_x_norm, grad_norm_attn = norm_one_back(grad_hidden)
    grad_tokens = grad_middle + grad_x_norm
    if fast:
        norms = sum_all(grad_norm_attn, group + span, fast)
        grad_shard = own_lines(early_flow.result, late_flow.result, corner_flow.result, norms)
        return (result.astype(jnp.bfloat16), grad_tokens, grad_shard, stats)
    small[NORM_ATTN] = grad_norm_attn
    pairs = {
        W_QUERY: (hidden, grad_query_low),
        W_KEY: (hidden, grad_key_low),
        W_VALUE: (hidden, grad_value_low),
        W_ATTN_OUT: (attended, grad_branch),
        W_GATE_SSM: (hidden, grad_gate_ssm),
        W_X_SSM: (hidden, grad_xbc[:, :ssm_inner]),
        W_B_C: (hidden, grad_xbc[:, ssm_inner:]),
        W_SSM_OUT: (ssm_low, grad_branch),
        W_GATE: (hidden_two, grad_gate),
        W_UP_PROJ: (hidden_two, grad_upper),
        W_DOWN: (activation, cotangent),
    }
    grad_dict = dict(small)
    for name_key, (left, right) in pairs.items():
        grad_dict[name_key] = matmul_left_t(left, right)
    flat_parts = [grad_dict[name_key].reshape(-1) for name_key, extent in layout()]
    used_entries = 0
    for part_array in flat_parts:
        used_entries += part_array.shape[0]
    flat_parts.append(jnp.zeros((params.shape[0] * lax.axis_size(group + span) - used_entries,), jnp.float32))
    grad_shard = lax.psum_scatter(
        jnp.concatenate(flat_parts), group + span, scatter_dimension=0, tiled=True
    )
    return (result.astype(jnp.bfloat16), grad_tokens, grad_shard, stats)


def solution(mesh):
    fast = (mesh.shape["group"], mesh.shape["span"]) == FAST
    if fast:
        mesh = Mesh(mesh.devices.reshape(4, 2, 2, 2), GRID)
        group, span = (GRID[:1], GRID[1:])
    else:
        group, span = (("group",), ("span",))

    def program(tokens, params, cotangent, offsets):
        return body(span, group, fast, tokens, params, cotangent, offsets)

    return jax.shard_map(
        program,
        mesh=mesh,
        in_specs=(P(group + span, None), P(group + span), P(group + span, None), P(group, None)),
        out_specs=(P(group + span, None), P(group + span, None), P(group + span), P()),
        check_vma=False,
    )
```

```python
import math

import jax
import jax.numpy as jnp
import numpy as np
from jax import lax
from jax.experimental import pallas as pl
from jax.experimental.pallas import tpu as pltpu
from jax.sharding import Mesh, PartitionSpec as P

D = 1024
HEADS_Q = 8
HEADS_KV = 2
HEAD_DIM = 64
SSM_HEADS = 24
SSM_DIM = 64
STATE = 128
CONV = 4
FF = 2048
(
    NORM_ATTN,
    W_QUERY,
    W_KEY,
    W_VALUE,
    W_ATTN_OUT,
    W_GATE_SSM,
    W_X_SSM,
    W_B_C,
    W_STEP,
    CONV_WEIGHT,
    CONV_BIAS,
    STEP_BIAS,
    DECAY_LOG,
    SKIP_GAIN,
    NORM_SSM,
    W_SSM_OUT,
    NORM_FFN,
    W_GATE,
    W_UP_PROJ,
    W_DOWN,
) = range(20)


epsilon = 1e-05
rope_base = 100000000000.0
masked_score = -1e30
highest = lax.Precision.HIGHEST
small_names = (
    NORM_ATTN,
    CONV_WEIGHT,
    CONV_BIAS,
    STEP_BIAS,
    DECAY_LOG,
    SKIP_GAIN,
    NORM_SSM,
    NORM_FFN,
)


def passed_along(value, axis, steps):
    count = lax.axis_size(axis)
    first, last = (max(0, -steps), min(count, count - steps))
    return lax.ppermute(value, axis, [(source, source + steps) for source in range(first, last)])


def prefix(value, axis, combine, identity):
    peers, place = (lax.axis_size(axis), lax.axis_index(axis))
    everything = jax.tree.map(
        lambda part, kind: lax.all_gather(part.astype(kind), axis),
        value,
        (jnp.bfloat16, jnp.bfloat16),
    )
    start = jax.tree.map(
        lambda part, zero: jnp.broadcast_to(jnp.asarray(zero, part.dtype), part.shape),
        value,
        identity,
    )

    def prefix_turn(k, before):
        reached = k < place
        new = combine(
            before, jax.tree.map(lambda part, own: part[k].astype(own.dtype), everything, value)
        )
        return jax.tree.map(lambda a, b: jnp.where(reached, a, b), new, before)

    return lax.fori_loop(0, peers, prefix_turn, start)


def carried_in(value, axis, combine, identity):
    peers, place = (lax.axis_size(axis), lax.axis_index(axis))
    everything = jax.tree.map(
        lambda part, kind: lax.all_gather(part.astype(kind), axis),
        value,
        jax.tree.map(lambda a: jnp.bfloat16 if a.dtype == jnp.float32 else a.dtype, value),
    )
    start = jax.tree.map(
        lambda part, zero: jnp.broadcast_to(jnp.asarray(zero, part.dtype), part.shape),
        value,
        identity,
    )

    def carried_turn(k, before):
        at = peers - 1 - k
        reached = at > place
        new = combine(
            before, jax.tree.map(lambda part, own: part[at].astype(own.dtype), everything, value)
        )
        return jax.tree.map(lambda a, b: jnp.where(reached, a, b), new, before)

    return lax.fori_loop(0, peers, carried_turn, start)


def layout():
    ssm_inner = SSM_HEADS * SSM_DIM
    channels = ssm_inner + 2 * STATE
    return [
        (NORM_ATTN, (D,)),
        (W_QUERY, (D, HEADS_Q * HEAD_DIM)),
        (W_KEY, (D, HEADS_KV * HEAD_DIM)),
        (W_VALUE, (D, HEADS_KV * HEAD_DIM)),
        (W_ATTN_OUT, (HEADS_Q * HEAD_DIM, D)),
        (W_GATE_SSM, (D, ssm_inner)),
        (W_X_SSM, (D, ssm_inner)),
        (W_B_C, (D, 2 * STATE)),
        (W_STEP, (D, SSM_HEADS)),
        (CONV_WEIGHT, (CONV, channels)),
        (CONV_BIAS, (channels,)),
        (STEP_BIAS, (SSM_HEADS,)),
        (DECAY_LOG, (SSM_HEADS,)),
        (SKIP_GAIN, (SSM_HEADS,)),
        (NORM_SSM, (ssm_inner,)),
        (W_SSM_OUT, (ssm_inner, D)),
        (NORM_FFN, (D,)),
        (W_GATE, (D, FF)),
        (W_UP_PROJ, (D, FF)),
        (W_DOWN, (FF, D)),
    ]


def unpack(flat_vector):
    unpacked = {}
    offset = 0
    for name_key, extent in layout():
        amount = math.prod(extent)
        unpacked[name_key] = flat_vector[offset : offset + amount].reshape(extent)
        offset += amount
    return unpacked


def matmul(left, right):
    return jnp.dot(left, right, preferred_element_type=jnp.float32)


def matmul_left_t(left, right):
    return lax.dot_general(
        left, right, (((0,), (0,)), ((), ())), preferred_element_type=jnp.float32
    )


def matmul_right_t(left, right):
    return lax.dot_general(
        left, right, (((1,), (1,)), ((), ())), preferred_element_type=jnp.float32
    )


def rms_norm(values, gain):
    return values * lax.rsqrt(jnp.mean(values * values, axis=-1, keepdims=True) + epsilon) * gain


def gated_norm(ssm_y, gate_ssm, gain):
    return rms_norm(ssm_y * jax.nn.silu(gate_ssm), gain)


def swiglu(gate_ffn, upper):
    return jax.nn.silu(gate_ffn) * upper


def sequence_info(row_index, bounds):
    starts = bounds[:-1]
    inside = row_index[:, None] >= starts[None, :]
    seq_id = jnp.sum(inside.astype(jnp.int32), axis=1) - 1
    seq_start = jnp.max(jnp.where(inside, starts[None, :], 0), axis=1)
    return (seq_id, row_index - seq_start)


def rotary_tables(positions):
    half_dim = HEAD_DIM // 2
    freqs = jnp.exp(
        -jnp.arange(half_dim, dtype=jnp.float32) * (2.0 * math.log(rope_base) / HEAD_DIM)
    )
    angles = positions.astype(jnp.float32)[:, None] * freqs[None, :]
    return (jnp.cos(angles), jnp.sin(angles))


def rotate(values, cosine, sine, heads):
    row_count = values.shape[0]
    half_dim = HEAD_DIM // 2
    split_heads = values.reshape(row_count, heads, HEAD_DIM)
    first_half = split_heads[..., :half_dim]
    second_half = split_heads[..., half_dim:]
    cos_b = cosine[:, None, :]
    sin_b = sine[:, None, :]
    turned = jnp.concatenate(
        [first_half * cos_b - second_half * sin_b, second_half * cos_b + first_half * sin_b],
        axis=-1,
    )
    return turned.reshape(row_count, heads * HEAD_DIM)


def add_rows(target, addend, first_row):
    current = lax.dynamic_slice_in_dim(target, first_row, addend.shape[0], 0)
    return lax.dynamic_update_slice_in_dim(target, current + addend, first_row, 0)


FAST = (4, 8)
LINE = 128
SHARD = 3082
SPAD = 3088
WIN = 3104
PLANE = 8 * SHARD
DEPTH = 4
TALL = {1: 1024, 2: 1024, 4: 512, 8: 256, 12: 128, 16: 128}
GRID = ("z", "y", "x", "c")
ZC = ("z", "c")
SWAP = [(0, 1), (1, 0)]


def zc_pairs(*pairs):
    return [(2 * a + c, 2 * b + c) for a, b, c in pairs]


def pinned(kernel, count, after):
    return lambda *refs: kernel(*refs[:count], *refs[count + len(after) :])


def pins(after):
    return [pl.BlockSpec(memory_space=pltpu.HBM)] * len(after)


def gather_lines(params):
    z, y, x, c = (lax.axis_index(name) for name in GRID)
    lines = jnp.pad(params.reshape(SHARD, LINE), ((0, SPAD - SHARD), (0, 0)))
    sibling = lax.ppermute(lines, ZC, [(2 * k + 1 - k % 2, 2 * k + k % 2) for k in range(4)])
    batches = []
    for batch in range(2):
        buffers = []
        for part in range(2):
            here = jnp.where(c == part, lines, sibling)
            if batch == 0:
                one = lax.ppermute(here, ZC, zc_pairs((0, 1, 0), (1, 2, 1)))
                side = lax.ppermute(here, ZC, zc_pairs((1, 0, 1)))
                two = lax.ppermute(one, ZC, zc_pairs((1, 2, 0), (2, 3, 1)))
                three = lax.ppermute(two, ZC, zc_pairs((2, 3, 0)))
            else:
                one = lax.ppermute(here, ZC, zc_pairs((2, 1, 0), (3, 2, 1)))
                side = lax.ppermute(here, ZC, zc_pairs((2, 3, 0)))
                two = lax.ppermute(one, ZC, zc_pairs((1, 0, 0), (2, 1, 1)))
                three = lax.ppermute(two, ZC, zc_pairs((1, 0, 1)))
            mine = z == 2 * batch + c
            column = jnp.where(mine, here, one + side + two + three)
            over_x = lax.ppermute(column, "x", SWAP)
            over_y = lax.ppermute(column, "y", SWAP)
            if part == 0:
                corner = lax.ppermute(over_x, "y", SWAP)
            else:
                corner = lax.ppermute(over_y, "x", SWAP)
            local = [column, over_x, over_y, corner]
            buffers += local + [lax.ppermute(piece, "c", SWAP) for piece in local]
        batches.append(buffers)
    shard = np.arange(32)
    sz, sy, sx, sc = shard // 8, shard // 4 % 2, shard // 2 % 2, shard % 2
    away = jnp.where(sz % 2 == c, 0, 4)
    where = sc * 8 + away + 2 * (sy ^ y) + (sx ^ x) + 16 * (sz // 2)
    return batches, where.astype(jnp.int32)


def unpack_lines(buffers, first, where, segments, after=()):
    jobs, starts = [], []
    reach = 0
    for offset, rows, columns in segments:
        per_row = columns // LINE
        lane, base = offset % LINE, offset // LINE
        if per_row == 1 and rows < 1024:
            lane, tall = 0, rows
        else:
            tall = TALL[per_row]
        starts.append(len(jobs))
        for k in range(rows // tall):
            jobs.append((base + k * tall * per_row, tall * per_row, 1 if lane else 0))
    window = max(job[1] for job in jobs) + 32
    table = np.zeros((len(jobs), 5), np.int32)
    for k, (line, count, extra) in enumerate(jobs):
        owner = line // SHARD
        inside = line - owner * SHARD
        begin = min(inside // 16 * 16, SPAD - window)
        crosses = int(line + count + extra > (owner + 1) * SHARD)
        table[k] = (owner, begin, begin - inside, crosses, (owner + 1) * SHARD - line)
    base_row = (int(-table[:, 2].min()) + 7) // 8 * 8
    table[:, 2] += base_row
    table[:, 4] += base_row
    room = int(max((table[:, 2] + window).max(), ((table[:, 4] + window) * table[:, 3]).max()))
    room = (room + 15) // 8 * 8
    total = len(jobs)
    count_buffers = len(buffers)
    shapes = []
    for offset, rows, columns in segments:
        per_row = columns // LINE
        tall = rows if per_row == 1 and rows < 1024 else TALL[per_row]
        shapes.append((rows, columns, tall, per_row, offset % LINE if tall != rows or per_row != 1 else 0))
    sizes = sorted({(tall, columns) for _, columns, tall, _, _ in shapes})

    def kernel(table_ref, where_ref, *refs):
        sources = refs[:count_buffers]
        outs = refs[count_buffers : count_buffers + len(segments)]
        rest = refs[count_buffers + len(segments) :]
        stages = dict(zip(sizes, rest))
        raw, flat, in_sem, out_sem = rest[len(sizes) :]
        step = pl.program_id(0)

        def fetch(job, slot):
            owner = table_ref[job, 0]
            begin = pl.multiple_of(table_ref[job, 1], 16)
            for b in range(count_buffers):

                @pl.when(where_ref[owner] == first + b)
                def _():
                    pltpu.make_async_copy(
                        sources[b].at[pl.ds(begin, window), :], raw.at[slot, 0], in_sem.at[slot, 0]
                    ).start()

            @pl.when(table_ref[job, 3] == 1)
            def _():
                for b in range(count_buffers):

                    @pl.when(where_ref[owner + 1] == first + b)
                    def _():
                        pltpu.make_async_copy(
                            sources[b].at[pl.ds(0, window), :], raw.at[slot, 1], in_sem.at[slot, 1]
                        ).start()

        def fetched(slot, half):
            return pltpu.make_async_copy(
                sources[0].at[pl.ds(0, window), :], raw.at[slot, half], in_sem.at[slot, half]
            )

        @pl.when(step == 0)
        def _():
            for k in range(min(DEPTH - 1, total)):
                fetch(k, k)

        @pl.when(step + DEPTH - 1 < total)
        def _():
            fetch(step + DEPTH - 1, lax.rem(step + DEPTH - 1, DEPTH))

        slot = lax.rem(step, DEPTH)
        fetched(slot, 0).wait()
        flat[pl.ds(table_ref[step, 2], window), :] = raw[slot, 0].astype(jnp.float32)

        @pl.when(table_ref[step, 3] == 1)
        def _():
            fetched(slot, 1).wait()
            flat[pl.ds(table_ref[step, 4], window), :] = raw[slot, 1].astype(jnp.float32)

        for index, (rows, columns, tall, per_row, lane) in enumerate(shapes):
            begin = starts[index]
            blocks = rows // tall
            stage = stages[(tall, columns)]

            @pl.when((step >= begin) & (step < begin + blocks))
            def _():
                block = step - begin
                side = lax.rem(block, 2)

                def written(k, s):
                    return pltpu.make_async_copy(
                        stage.at[s],
                        outs[index].at[pl.ds(pl.multiple_of(k * tall, 16), tall), :],
                        out_sem.at[s],
                    )

                @pl.when(block >= 2)
                def _():
                    written(block - 2, side).wait()

                def tile(j):
                    picked = flat[pl.ds(base_row + j, tall, stride=per_row), :]
                    return pltpu.roll(picked, LINE - lane, 1) if lane else picked

                if lane:
                    lanes = lax.broadcasted_iota(jnp.int32, (tall, LINE), 1)
                    now = tile(0)
                    for j in range(per_row):
                        later = tile(j + 1)
                        stage[side, :, j * LINE : (j + 1) * LINE] = jnp.where(
                            lanes < LINE - lane, now, later
                        ).astype(jnp.bfloat16)
                        now = later
                else:
                    for j in range(per_row):
                        stage[side, :, j * LINE : (j + 1) * LINE] = tile(j).astype(jnp.bfloat16)
                written(block, side).start()

                @pl.when(block == blocks - 1)
                def _():
                    if blocks > 1:
                        written(block - 1, 1 - side).wait()
                    written(block, side).wait()

    return pl.pallas_call(
        pinned(kernel, 2 + count_buffers, after),
        grid_spec=pltpu.PrefetchScalarGridSpec(
            num_scalar_prefetch=2,
            grid=(total,),
            in_specs=[pl.BlockSpec(memory_space=pl.ANY)] * count_buffers + pins(after),
            out_specs=[pl.BlockSpec(memory_space=pl.ANY)] * len(segments),
            scratch_shapes=[pltpu.VMEM((2,) + size, jnp.bfloat16) for size in sizes]
            + [
                pltpu.VMEM((DEPTH, 2, window, LINE), jnp.bfloat16),
                pltpu.VMEM((room, LINE), jnp.float32),
                pltpu.SemaphoreType.DMA((DEPTH, 2)),
                pltpu.SemaphoreType.DMA((2,)),
            ],
        ),
        out_shape=[jax.ShapeDtypeStruct((rows, columns), jnp.bfloat16) for _, rows, columns in segments],
        compiler_params=pltpu.CompilerParams(vmem_limit_bytes=48 * 2**20),
        cost_estimate=pl.CostEstimate(flops=0, bytes_accessed=total * window * LINE * 4, transcendentals=0),
        name="unpack",
    )(jnp.asarray(table), where, *buffers, *after)


def pack_lines(target, target_rows, first_row, segments, lane, phase, extras, carry, tail_rows, after=()):
    tall = 256
    lefts, rights, plan = [], [], []
    left_of, right_of = {}, {}
    row = first_row
    begin = 0
    for left, right in segments:
        for value, seen, kept in ((left, left_of, lefts), (right, right_of, rights)):
            if id(value) not in seen:
                seen[id(value)] = len(kept)
                kept.append(value)
        blocks = left.shape[1] // tall
        plan.append((left_of[id(left)], right_of[id(right)], right.shape[1] // LINE, begin, blocks, row))
        begin += blocks
        row += left.shape[1] * right.shape[1] // LINE
    end_row = row
    total = begin
    biggest = max(entry[2] for entry in plan) * tall
    tokens = lefts[0].shape[0]
    count_left, count_right, count_extra = len(lefts), len(rights), len(extras)
    rolled = [jnp.roll(right, lane, axis=1) if lane else right for right in rights]
    carry_in = [carry] if lane else []
    targets = [] if target is None else [target]

    def left_spec(index):
        mine = [entry for entry in plan if entry[0] == index]

        def place(step):
            block = 0
            for _, _, _, start, blocks, _ in mine:
                block = jnp.where(step >= start, jnp.minimum(step - start, blocks - 1), block)
            return (0, block)

        return pl.BlockSpec((tokens, tall), place)

    def kernel(*refs):
        left_refs = refs[:count_left]
        right_refs = refs[count_left : count_left + count_right]
        at = count_left + count_right
        extra_refs = refs[at : at + count_extra]
        at += count_extra
        carry_refs = refs[at : at + len(carry_in)]
        at += len(carry_in) + len(targets)
        out = refs[at]
        flat, stage, shift, last, sems, extra_sems = refs[at + 1 :]
        step = pl.program_id(0)
        side = lax.rem(step, 2)

        def extra_copy(k):
            rows = extras[k][0].shape[0]
            return pltpu.make_async_copy(
                extra_refs[k], out.at[pl.ds(extras[k][1], rows), :], extra_sems.at[k]
            )

        @pl.when(step == 0)
        def _():
            for k in range(count_extra):
                extra_copy(k).start()
            if lane:
                shift[0:8, :] = carry_refs[0][...]
            if phase:
                flat[0:8, :] = jnp.zeros((8, LINE), jnp.float32)

        for left_at, right_at, per_row, start, blocks, row in plan:
            lines = per_row * tall

            def written(block, s, row=row, lines=lines):
                return pltpu.make_async_copy(
                    stage.at[s, pl.ds(0, lines), :],
                    out.at[pl.ds(pl.multiple_of(row + block * lines, 16), lines), :],
                    sems.at[s],
                )

            @pl.when((step >= start) & (step < start + blocks))
            def _():
                block = step - start
                if phase:

                    @pl.when(step > 0)
                    def _():
                        flat[0:8, :] = flat[lines : lines + 8, :]

                turned = left_refs[left_at][...].T
                lanes = lax.broadcasted_iota(jnp.int32, (tall, LINE), 1)
                for j0 in range(0, per_row, 2):
                    wide = min(2, per_row - j0)
                    tile = jnp.dot(
                        turned,
                        right_refs[right_at][:, j0 * LINE : (j0 + wide) * LINE],
                        preferred_element_type=jnp.float32,
                    )
                    for j in range(wide):
                        piece = tile[:, j * LINE : (j + 1) * LINE]
                        if lane and j0 + j == 0:
                            shift[8 : 8 + tall, :] = piece
                            piece = jnp.where(lanes < lane, shift[7 : 7 + tall, :], piece)
                            shift[0:8, :] = shift[tall : tall + 8, :]
                        if per_row == 1:
                            flat[phase : phase + tall, :] = piece
                        else:
                            flat[pl.ds(phase + j0 + j, tall, stride=per_row), :] = piece

                stage[side, 0:lines, :] = flat[0:lines, :].astype(jnp.bfloat16)
                written(block, side).start()

            @pl.when((step > start) & (step <= start + blocks))
            def _():
                written(step - start - 1, 1 - side).wait()

            if start + blocks == total:

                @pl.when(step == total - 1)
                def _():
                    written(blocks - 1, side).wait()

        @pl.when(step == total - 1)
        def _():
            if tail_rows:
                lanes = lax.broadcasted_iota(jnp.int32, (tail_rows, LINE), 1)
                rows_at = lax.broadcasted_iota(jnp.int32, (tail_rows, LINE), 0)
                final = jnp.broadcast_to(shift[7:8, :], (tail_rows, LINE))
                last[...] = jnp.where((rows_at == 0) & (lanes < lane), final, 0.0).astype(jnp.bfloat16)
                closing = pltpu.make_async_copy(
                    last, out.at[pl.ds(end_row, tail_rows), :], extra_sems.at[count_extra]
                )
                closing.start()
                closing.wait()
            for k in range(count_extra):
                extra_copy(k).wait()

    whole = [pl.BlockSpec(array.shape, lambda step: (0, 0)) for array in rolled]
    flops = sum(2 * tokens * entry[4] * tall * entry[2] * LINE for entry in plan)
    inputs = count_left + count_right + count_extra + len(carry_in) + len(targets)
    return pl.pallas_call(
        pinned(kernel, inputs, after),
        grid=(total,),
        in_specs=[left_spec(k) for k in range(count_left)]
        + whole
        + [pl.BlockSpec(array.shape, lambda step: (0, 0)) for array, _ in extras]
        + [pl.BlockSpec(array.shape, lambda step: (0, 0)) for array in carry_in]
        + [pl.BlockSpec(memory_space=pl.ANY)] * len(targets)
        + pins(after),
        out_specs=pl.BlockSpec(memory_space=pl.ANY),
        out_shape=jax.ShapeDtypeStruct((target_rows, LINE), jnp.bfloat16),
        scratch_shapes=[
            pltpu.VMEM((biggest + 16, LINE), jnp.float32),
            pltpu.VMEM((2, biggest, LINE), jnp.bfloat16),
            pltpu.VMEM((tall + 8, LINE), jnp.float32),
            pltpu.VMEM((max(tail_rows, 16), LINE), jnp.bfloat16),
            pltpu.SemaphoreType.DMA((2,)),
            pltpu.SemaphoreType.DMA((count_extra + 1,)),
        ],
        input_output_aliases={count_left + count_right + count_extra + len(carry_in): 0} if targets else {},
        compiler_params=pltpu.CompilerParams(vmem_limit_bytes=48 * 2**20),
        cost_estimate=pl.CostEstimate(flops=flops, bytes_accessed=total * biggest * LINE * 2, transcendentals=0),
        name="pack",
    )(*lefts, *rolled, *[array for array, _ in extras], *carry_in, *targets, *after)


def added(*parts):
    total = parts[0].astype(jnp.float32)
    for part in parts[1:]:
        total = total + part.astype(jnp.float32)
    return total.astype(jnp.bfloat16)


class Flow:
    def __init__(self, stages):
        self.stages = stages
        self.sends = next(stages)
        self.result = None

    def values(self):
        return [value for value, _, _ in self.sends]

    def go(self):
        arrived = [lax.ppermute(value, axis, pairs) for value, axis, pairs in self.sends]
        try:
            self.sends = self.stages.send(arrived)
        except StopIteration as stop:
            self.sends, self.result = [], stop.value
        return self


def reduce_stages(flat, batch, shift):
    z, y, x, c = (lax.axis_index(name) for name in GRID)
    length = PLANE + 32
    send = lax.dynamic_slice(flat, ((1 - c) * PLANE, 0), (length, LINE))
    (arrived,) = yield [(send, "c", SWAP)]
    chip = added(lax.dynamic_slice(flat, (c * PLANE, 0), (length, LINE)), arrived)

    def window(sy, sx, part):
        shard = sy * 4 + sx * 2 + part
        start = (shift + SHARD * shard) // 16 * 16
        return lax.dynamic_slice(chip, (start, 0), (WIN, LINE))

    away_0 = jnp.stack([window(1 - y, 0, 0), window(1 - y, 1, 0)])
    away_1 = jnp.stack([window(0, 1 - x, 1), window(1, 1 - x, 1)])
    home_0 = jnp.stack([window(y, 0, 0), window(y, 1, 0)])
    home_1 = jnp.stack([window(0, x, 1), window(1, x, 1)])
    got_0, got_1 = yield [(away_0, "y", SWAP), (away_1, "x", SWAP)]
    half_0, half_1 = added(home_0, got_0), added(home_1, got_1)
    pick = lambda value, at: lax.dynamic_index_in_dim(value, at, 0, keepdims=False)
    got_0, got_1 = yield [(pick(half_0, 1 - x), "x", SWAP), (pick(half_1, 1 - y), "y", SWAP)]
    columns = [added(pick(half_0, x), got_0), added(pick(half_1, y), got_1)]
    if batch == 0:
        hops = [((1, 0, 0), (2, 1, 1)), ((2, 0, 0), (3, 1, 1)), ((3, 0, 0), (0, 1, 1))]
    else:
        hops = [((1, 2, 0), (2, 3, 1)), ((0, 2, 0), (1, 3, 1)), ((3, 2, 0), (0, 3, 1))]
    got = yield [(column, ZC, zc_pairs(*hop)) for column in columns for hop in hops]
    ends = [added(columns[0], *got[:3]), added(columns[1], *got[3:])]
    mine = jnp.where(c == 0, ends[0], ends[1])
    other = jnp.where(c == 0, ends[1], ends[0])
    (handed,) = yield [(other, ZC, [(2 * k + k % 2, 2 * k + 1 - k % 2) for k in range(4)])]
    return jnp.where(c == z % 2, mine, handed)


PIECE = 400


def corner_stages(flat):
    z, y, x, c = (lax.axis_index(name) for name in GRID)
    length = 8 * PIECE
    second = (8 + SHARD) // 16 * 16
    take = lambda at: lax.dynamic_slice(flat, (at * second, 0), (length, LINE))
    (arrived,) = yield [(take(1 - c), "c", SWAP)]
    chip = added(take(c), arrived).reshape(2, 2, 2, PIECE, LINE)
    pick = lambda value, at: lax.dynamic_index_in_dim(value, at, 0, keepdims=False)
    got = yield [(pick(chip[0], 1 - x), "x", SWAP), (pick(chip[1], 1 - y), "y", SWAP)]
    halves = [added(pick(chip[0], x), got[0]), added(pick(chip[1], y), got[1])]
    got = yield [(pick(halves[0], 1 - y), "y", SWAP), (pick(halves[1], 1 - x), "x", SWAP)]
    pieces = jnp.stack([added(pick(halves[0], y), got[0]), added(pick(halves[1], x), got[1])])
    got = yield [(pieces, "z", [(k, 0)]) for k in (1, 2, 3)]
    pieces = added(pieces, *got)
    got = yield [(pieces[0], "y", [(1, 0)]), (pieces[1], "x", [(1, 0)])]
    halves = [jnp.stack([pieces[0], got[0]]), jnp.stack([pieces[1], got[1]])]
    got = yield [(halves[0], "x", [(1, 0)]), (halves[1], "y", [(1, 0)])]
    return jnp.stack([halves[0], got[0], halves[1], got[1]]).reshape(length, LINE)


CHUNK = 128
NT = (((1,), (1,)), ((), ()))
TN = (((0,), (0,)), ((), ()))
INNER = SSM_HEADS * SSM_DIM
PAIRS = SSM_HEADS // 2


def spread(rows_a, rows_b):
    length = rows_a.shape[1]
    tall = jnp.concatenate(
        [jnp.broadcast_to(rows_a, (SSM_DIM, length)), jnp.broadcast_to(rows_b, (SSM_DIM, length))], axis=0
    )
    return tall.T


CHANNELS = INNER + 2 * STATE
LANES = 2 * SSM_DIM
COLUMNS = CHANNELS // LANES


def conv_parts(ext, weight_ref, bias_ref, start_ref, first, rows):
    place = first + lax.broadcasted_iota(jnp.int32, (rows, 1), 0) - start_ref[...]
    windows = []
    total = bias_ref[...]
    for tap in range(CONV):
        reach = CONV - 1 - tap
        window = jnp.where(place >= reach, ext[8 - reach : 8 - reach + rows, :], 0.0)
        windows.append(window)
        total = total + window * weight_ref[tap : tap + 1, :]
    return place, windows, total


def conv_forward(xbc, rim, weight, bias, meta, start_column):
    rows = xbc.shape[0]

    def kernel(meta_ref, x_ref, rim_ref, weight_ref, bias_ref, start_ref, out_ref, ext):
        ext[0:8, :] = rim_ref[...]
        ext[8:, :] = x_ref[...]
        _, _, total = conv_parts(ext, weight_ref, bias_ref, start_ref, meta_ref[0], rows)
        out_ref[...] = total * jax.nn.sigmoid(total)

    lanes = lambda i, m: (0, i)
    return pl.pallas_call(
        kernel,
        grid_spec=pltpu.PrefetchScalarGridSpec(
            num_scalar_prefetch=1,
            grid=(COLUMNS,),
            in_specs=[
                pl.BlockSpec((rows, LANES), lanes),
                pl.BlockSpec((8, LANES), lanes),
                pl.BlockSpec((CONV, LANES), lanes),
                pl.BlockSpec((1, LANES), lanes),
                pl.BlockSpec((rows, 1), lambda i, m: (0, 0)),
            ],
            out_specs=pl.BlockSpec((rows, LANES), lanes),
            scratch_shapes=[pltpu.VMEM((rows + 8, LANES), jnp.float32)],
        ),
        out_shape=jax.ShapeDtypeStruct((rows, CHANNELS), jnp.float32),
        cost_estimate=pl.CostEstimate(flops=10**9, bytes_accessed=rows * CHANNELS * 8, transcendentals=0),
        name="conv",
    )(meta, xbc, rim, weight, bias, start_column)


def conv_backward(dx, db, dc, xbc, rim, weight, bias, meta, start_column, after=()):
    rows = xbc.shape[0]

    def kernel(meta_ref, dx_ref, db_ref, dc_ref, x_ref, rim_ref, weight_ref, bias_ref, start_ref,
               low_ref, tail_ref, edge_ref, small_ref, ext, upper):
        ext[0:8, :] = rim_ref[...]
        ext[8:, :] = x_ref[...]
        at = pl.program_id(0)
        arrived = jnp.where(at < PAIRS, dx_ref[...], jnp.where(at == PAIRS, db_ref[...], dc_ref[...]))
        place, windows, total = conv_parts(ext, weight_ref, bias_ref, start_ref, meta_ref[0], rows)
        gate = jax.nn.sigmoid(total)
        change = arrived * gate * (1.0 + total * (1.0 - gate))
        upper[0:8, :] = jnp.zeros((8, LANES), jnp.float32)
        upper[8 + rows :, :] = jnp.zeros((8, LANES), jnp.float32)
        main = jnp.zeros((rows, LANES), jnp.float32)
        edge = jnp.zeros((8, LANES), jnp.float32)
        small_ref[...] = jnp.zeros((8, LANES), jnp.float32)
        small_ref[CONV : CONV + 1, :] = jnp.sum(change, axis=0, keepdims=True)
        for tap in range(CONV):
            reach = CONV - 1 - tap
            small_ref[tap : tap + 1, :] = jnp.sum(change * windows[tap], axis=0, keepdims=True)
            upper[8 : 8 + rows, :] = jnp.where(place >= reach, change, 0.0) * weight_ref[tap : tap + 1, :]
            main = main + upper[8 + reach : 8 + reach + rows, :]
            edge = edge + upper[reach : reach + 8, :]
        low_ref[...] = main.astype(jnp.bfloat16)
        tail_ref[...] = main[rows - 16 :, :]
        edge_ref[...] = edge

    lanes = lambda i, m: (0, i)
    whole = lambda i, m: (0, 0)
    return pl.pallas_call(
        pinned(kernel, 9, after),
        grid_spec=pltpu.PrefetchScalarGridSpec(
            num_scalar_prefetch=1,
            grid=(COLUMNS,),
            in_specs=[
                pl.BlockSpec((rows, LANES), lambda i, m: (0, jnp.minimum(i, PAIRS - 1))),
                pl.BlockSpec((rows, STATE), whole),
                pl.BlockSpec((rows, STATE), whole),
                pl.BlockSpec((rows, LANES), lanes),
                pl.BlockSpec((8, LANES), lanes),
                pl.BlockSpec((CONV, LANES), lanes),
                pl.BlockSpec((1, LANES), lanes),
                pl.BlockSpec((rows, 1), whole),
            ] + pins(after),
            out_specs=[
                pl.BlockSpec((rows, LANES), lanes),
                pl.BlockSpec((16, LANES), lanes),
                pl.BlockSpec((8, LANES), lanes),
                pl.BlockSpec((8, LANES), lanes),
            ],
            scratch_shapes=[
                pltpu.VMEM((rows + 8, LANES), jnp.float32),
                pltpu.VMEM((rows + 16, LANES), jnp.float32),
            ],
        ),
        out_shape=[
            jax.ShapeDtypeStruct((rows, CHANNELS), jnp.bfloat16),
            jax.ShapeDtypeStruct((16, CHANNELS), jnp.float32),
            jax.ShapeDtypeStruct((8, CHANNELS), jnp.float32),
            jax.ShapeDtypeStruct((8, CHANNELS), jnp.float32),
        ],
        cost_estimate=pl.CostEstimate(flops=2 * 10**9, bytes_accessed=rows * CHANNELS * 10, transcendentals=0),
        name="conv_back",
    )(meta, dx, db, dc, xbc, rim, weight, bias, start_column, *after)


def weighted_state(left, left_block, values, weight_rows, after=()):
    rows = left.shape[0]

    def kernel(left_ref, value_ref, weight_ref, out_ref, turned):
        @pl.when(pl.program_id(0) == 0)
        def _():
            turned[...] = left_ref[...].T.astype(jnp.bfloat16)

        wide = spread(weight_ref[0, 0:1, :], weight_ref[0, 1:2, :])
        scaled = (value_ref[...] * wide).astype(jnp.bfloat16)
        out_ref[...] = jnp.dot(turned[...], scaled, preferred_element_type=jnp.float32)

    return pl.pallas_call(
        pinned(kernel, 3, after),
        grid=(PAIRS,),
        in_specs=[
            pl.BlockSpec((rows, STATE), lambda i: (0, left_block)),
            pl.BlockSpec((rows, 2 * SSM_DIM), lambda i: (0, i)),
            pl.BlockSpec((1, 2, rows), lambda i: (i, 0, 0)),
        ] + pins(after),
        out_specs=pl.BlockSpec((STATE, 2 * SSM_DIM), lambda i: (0, i)),
        out_shape=jax.ShapeDtypeStruct((STATE, INNER), jnp.float32),
        scratch_shapes=[pltpu.VMEM((STATE, rows), jnp.bfloat16)],
        cost_estimate=pl.CostEstimate(flops=2 * rows * STATE * INNER, bytes_accessed=rows * INNER * 4, transcendentals=0),
        name="state",
    )(left, values, weight_rows.reshape(PAIRS, 2, rows), *after)


def chunk_rows(k, meta_ref, cum_ref, start_ref):
    here = slice(k * CHUNK, (k + 1) * CHUNK)
    first = meta_ref[0] + k * CHUNK
    index = first + lax.broadcasted_iota(jnp.int32, (1, CHUNK), 1)
    entering = start_ref[0:1, here] < first
    ending = index >= meta_ref[1 + k]
    cums, entries, tails = [], [], []
    for e in range(2):
        cum = cum_ref[0, e : e + 1, here]
        cums.append(cum)
        entries.append(jnp.where(entering, jnp.exp(cum), 0.0))
        gap = jnp.where(ending, cum[:, CHUNK - 1 :] - cum, masked_score)
        tails.append(jnp.exp(gap))
    return cums, entries, tails


def ssm_forward(conv, cum, step, state_in, skip, meta, start_column, start_row):
    rows = conv.shape[0]
    chunks = rows // CHUNK

    def kernel(meta_ref, x_ref, b_ref, c_ref, cum_ref, step_ref, state_ref, skip_ref, col_ref, row_ref,
               y_ref, inner, hide, state, b_turned):
        @pl.when(pl.program_id(0) == 0)
        def _():
            for k in range(chunks):
                here = slice(k * CHUNK, (k + 1) * CHUNK)
                b_turned[:, here] = b_ref[here, :].T.astype(jnp.bfloat16)
                inner[k] = lax.dot_general(
                    c_ref[here, :], b_ref[here, :], NT, precision=highest, preferred_element_type=jnp.float32
                )
                t = lax.broadcasted_iota(jnp.int32, (CHUNK, CHUNK), 0)
                s = lax.broadcasted_iota(jnp.int32, (CHUNK, CHUNK), 1)
                shown = (s <= t) & (meta_ref[0] + k * CHUNK + s >= col_ref[here, :])
                hide[k] = jnp.where(shown, 0.0, masked_score)

        low_lane = lax.broadcasted_iota(jnp.int32, (CHUNK, 2 * SSM_DIM), 1) < SSM_DIM
        state[...] = state_ref[...]
        for k in range(chunks):
            here = slice(k * CHUNK, (k + 1) * CHUNK)
            cums, entries, tails = chunk_rows(k, meta_ref, cum_ref, row_ref)
            x_now = x_ref[here, :]
            x_low = x_now.astype(jnp.bfloat16)
            entry = spread(*entries)
            weight = spread(*[tails[e] * step_ref[0, e : e + 1, here] for e in range(2)])
            parts = []
            for e in range(2):
                across = jnp.broadcast_to(cums[e], (CHUNK, CHUNK))
                decays = jnp.exp(across.T - across + hide[k])
                mix = (inner[k] * decays * step_ref[0, e : e + 1, here]).astype(jnp.bfloat16)
                parts.append(jnp.dot(mix, x_low, preferred_element_type=jnp.float32))
            carried = jnp.dot(
                c_ref[here, :].astype(jnp.bfloat16), state[...].astype(jnp.bfloat16),
                preferred_element_type=jnp.float32,
            )
            y_ref[here, :] = jnp.where(low_lane, parts[0], parts[1]) + entry * carried + skip_ref[...] * x_now
            fresh = jnp.dot(
                b_turned[:, here], (x_now * weight).astype(jnp.bfloat16), preferred_element_type=jnp.float32
            )
            state[...] = entry[CHUNK - 1 :, :] * state[...] + fresh

    whole = lambda i, m: (0, 0)
    lanes = lambda i, m: (0, i)
    return pl.pallas_call(
        kernel,
        grid_spec=pltpu.PrefetchScalarGridSpec(
            num_scalar_prefetch=1,
            grid=(PAIRS,),
            in_specs=[
                pl.BlockSpec((rows, 2 * SSM_DIM), lanes),
                pl.BlockSpec((rows, STATE), lambda i, m: (0, PAIRS)),
                pl.BlockSpec((rows, STATE), lambda i, m: (0, PAIRS + 1)),
                pl.BlockSpec((1, 2, rows), lambda i, m: (i, 0, 0)),
                pl.BlockSpec((1, 2, rows), lambda i, m: (i, 0, 0)),
                pl.BlockSpec((STATE, 2 * SSM_DIM), lanes),
                pl.BlockSpec((1, 2 * SSM_DIM), lanes),
                pl.BlockSpec((rows, 1), whole),
                pl.BlockSpec((8, rows), whole),
            ],
            out_specs=pl.BlockSpec((rows, 2 * SSM_DIM), lanes),
            scratch_shapes=[
                pltpu.VMEM((chunks, CHUNK, CHUNK), jnp.float32),
                pltpu.VMEM((chunks, CHUNK, CHUNK), jnp.float32),
                pltpu.VMEM((STATE, 2 * SSM_DIM), jnp.float32),
                pltpu.VMEM((STATE, rows), jnp.bfloat16),
            ],
        ),
        out_shape=jax.ShapeDtypeStruct((rows, INNER), jnp.float32),
        compiler_params=pltpu.CompilerParams(vmem_limit_bytes=40 * 2**20),
        cost_estimate=pl.CostEstimate(flops=10**9, bytes_accessed=rows * INNER * 8, transcendentals=2**21),
        name="ssm",
    )(meta, conv, conv, conv, cum.reshape(PAIRS, 2, rows), step.reshape(PAIRS, 2, rows), state_in, skip,
      start_column, start_row)


def ssm_backward(conv, dy, cum, step, state_in, state_grad, skip, meta, start_row, after=()):
    rows = conv.shape[0]
    chunks = rows // CHUNK

    def kernel(meta_ref, x_ref, dy_ref, b_ref, c_ref, cum_ref, step_ref, state_ref, grad_ref, skip_ref, row_ref,
               dx_ref, db_ref, dc_ref, small_ref, inner, hide, inner_grad, states, flow,
               b_turned, c_turned):
        low = lambda v: v.astype(jnp.bfloat16)
        dot = lambda p, q, dims=(((1,), (0,)), ((), ())): lax.dot_general(
            p, q, dims, preferred_element_type=jnp.float32
        )
        exact = lambda p, q, dims=(((1,), (0,)), ((), ())): lax.dot_general(
            p, q, dims, precision=highest, preferred_element_type=jnp.float32
        )
        s = lax.broadcasted_iota(jnp.int32, (CHUNK, CHUNK), 0)
        t = lax.broadcasted_iota(jnp.int32, (CHUNK, CHUNK), 1)

        @pl.when(pl.program_id(0) == 0)
        def _():
            db_ref[...] = jnp.zeros(db_ref.shape, jnp.float32)
            dc_ref[...] = jnp.zeros(dc_ref.shape, jnp.float32)
            inner_grad[...] = jnp.zeros(inner_grad.shape, jnp.float32)
            for k in range(chunks):
                here = slice(k * CHUNK, (k + 1) * CHUNK)
                b_turned[:, here] = low(b_ref[here, :].T)
                c_turned[:, here] = low(c_ref[here, :].T)
                inner[k] = exact(b_ref[here, :], c_ref[here, :], NT)
                shown = (s <= t) & (meta_ref[0] + k * CHUNK + s >= row_ref[0:1, here])
                hide[k] = jnp.where(shown, 0.0, masked_score)

        before = (s < t).astype(jnp.float32)
        until = low((s >= t).astype(jnp.float32))
        low_lane = t < SSM_DIM
        pick_row = lax.broadcasted_iota(jnp.int32, (8, 2 * SSM_DIM), 0)
        pick_lane = lax.broadcasted_iota(jnp.int32, (8, 2 * SSM_DIM), 1) // SSM_DIM
        pick = low((pick_row == pick_lane).astype(jnp.float32))
        spreads = []
        states[0] = state_ref[...]
        for k in range(chunks):
            here = slice(k * CHUNK, (k + 1) * CHUNK)
            cums, entries, tails = chunk_rows(k, meta_ref, cum_ref, row_ref)
            entry, tail = spread(*entries), spread(*tails)
            steps = spread(step_ref[0, 0:1, here], step_ref[0, 1:2, here])
            spreads.append((cums, entry, tail, steps))
            if k < chunks - 1:
                fresh = dot(b_turned[:, here], low(x_ref[here, :] * steps * tail))
                states[k + 1] = entry[CHUNK - 1 :, :] * states[k] + fresh
        flow[...] = grad_ref[...]
        skip_sum = jnp.zeros((1, 2 * SSM_DIM), jnp.float32)
        for k in reversed(range(chunks)):
            here = slice(k * CHUNK, (k + 1) * CHUNK)
            cums, entry, tail, steps = spreads[k]
            x_now, dy_now = x_ref[here, :], dy_ref[here, :]
            b_low, c_low = low(b_ref[here, :]), low(c_ref[here, :])
            scaled = x_now * steps
            dy_low = low(dy_now)
            flow_low, state_low = low(flow[...]), low(states[k])
            mixed, within = [], []
            for e in range(2):
                across = jnp.broadcast_to(cums[e], (CHUNK, CHUNK))
                decays = jnp.exp(across - across.T + hide[k])
                own = low(jnp.where(low_lane == (e == 0), scaled, 0.0))
                reach = decays * dot(own, dy_low, NT)
                inner_grad[k] += reach
                sums = dot(low(inner[k] * reach), until)
                within.append(jnp.sum(sums * before, axis=0, keepdims=True))
                mixed.append(dot(low(inner[k] * decays), dy_low))
            back = tail * dot(b_low, flow_low)
            dxs = jnp.where(low_lane, mixed[0], mixed[1]) + back
            db_ref[here, :] += dot(low(scaled * tail), flow_low, NT)
            entered = low(dy_now * entry)
            dc_ref[here, :] += dot(entered, state_low, NT)
            brought = dy_now * entry * dot(c_low, state_low)
            ends = dot(pick, low(brought), NT)
            begins = dot(pick, low(scaled * back), NT)
            direct = dot(pick, low(x_now * dxs), NT)
            through = jnp.sum(flow[...] * states[k], axis=0, keepdims=True) * entry[CHUNK - 1 :, :]
            log_grad = exact(ends, until.astype(jnp.float32)) + exact(begins, before)
            for e in range(2):
                lanes = slice(e * SSM_DIM, (e + 1) * SSM_DIM)
                kept = jnp.sum(through[:, lanes], axis=1, keepdims=True)
                small_ref[0, e : e + 1, here] = direct[e : e + 1, :]
                small_ref[0, 2 + e : 3 + e, here] = log_grad[e : e + 1, :] + within[e] + kept
            dx_ref[here, :] = dxs * steps + skip_ref[...] * dy_now
            skip_sum += jnp.sum(x_now * dy_now, axis=0, keepdims=True)
            flow[...] = entry[CHUNK - 1 :, :] * flow[...] + dot(c_turned[:, here], entered)
        small_ref[0, 4:8, :] = jnp.zeros((4, rows), jnp.float32)
        small_ref[0, 4:5, 0 : 2 * SSM_DIM] = skip_sum

        @pl.when(pl.program_id(0) == PAIRS - 1)
        def _():
            for k in range(chunks):
                here = slice(k * CHUNK, (k + 1) * CHUNK)
                grads = low(inner_grad[k])
                db_ref[here, :] += dot(grads, low(c_ref[here, :]))
                dc_ref[here, :] += dot(grads, low(b_ref[here, :]), TN)

    whole = lambda i, m: (0, 0)
    lanes = lambda i, m: (0, i)
    pair = lambda i, m: (i, 0, 0)
    return pl.pallas_call(
        pinned(kernel, 11, after),
        grid_spec=pltpu.PrefetchScalarGridSpec(
            num_scalar_prefetch=1,
            grid=(PAIRS,),
            in_specs=[
                pl.BlockSpec((rows, 2 * SSM_DIM), lanes),
                pl.BlockSpec((rows, 2 * SSM_DIM), lanes),
                pl.BlockSpec((rows, STATE), lambda i, m: (0, PAIRS)),
                pl.BlockSpec((rows, STATE), lambda i, m: (0, PAIRS + 1)),
                pl.BlockSpec((1, 2, rows), pair),
                pl.BlockSpec((1, 2, rows), pair),
                pl.BlockSpec((STATE, 2 * SSM_DIM), lanes),
                pl.BlockSpec((STATE, 2 * SSM_DIM), lanes),
                pl.BlockSpec((1, 2 * SSM_DIM), lanes),
                pl.BlockSpec((8, rows), whole),
            ] + pins(after),
            out_specs=[
                pl.BlockSpec((rows, 2 * SSM_DIM), lanes),
                pl.BlockSpec((rows, STATE), whole),
                pl.BlockSpec((rows, STATE), whole),
                pl.BlockSpec((1, 8, rows), pair),
            ],
            scratch_shapes=[
                pltpu.VMEM((chunks, CHUNK, CHUNK), jnp.float32),
                pltpu.VMEM((chunks, CHUNK, CHUNK), jnp.float32),
                pltpu.VMEM((chunks, CHUNK, CHUNK), jnp.float32),
                pltpu.VMEM((chunks, STATE, 2 * SSM_DIM), jnp.float32),
                pltpu.VMEM((STATE, 2 * SSM_DIM), jnp.float32),
                pltpu.VMEM((STATE, rows), jnp.bfloat16),
                pltpu.VMEM((STATE, rows), jnp.bfloat16),
            ],
        ),
        out_shape=[
            jax.ShapeDtypeStruct((rows, INNER), jnp.float32),
            jax.ShapeDtypeStruct((rows, STATE), jnp.float32),
            jax.ShapeDtypeStruct((rows, STATE), jnp.float32),
            jax.ShapeDtypeStruct((PAIRS, 8, rows), jnp.float32),
        ],
        compiler_params=pltpu.CompilerParams(vmem_limit_bytes=40 * 2**20),
        cost_estimate=pl.CostEstimate(flops=3 * 10**9, bytes_accessed=rows * INNER * 12, transcendentals=2**21),
        name="ssm_back",
    )(meta, conv, dy, conv, conv, cum.reshape(PAIRS, 2, rows), step.reshape(PAIRS, 2, rows), state_in, state_grad,
      skip, start_row, *after)


def chain_states(earlier, later):
    return (earlier[0] * later[0], earlier[1] * later[0] + later[1])


def scan_states(carry, state, span, fast, backward):
    wide = jnp.repeat(carry, SSM_DIM)[None, :]
    if not fast:
        ident = (jnp.ones_like(wide), jnp.zeros_like(state))
        return (carried_in if backward else prefix)((wide, state), span, chain_states, ident)[1]
    total = (wide, state)
    start = None
    for name in ("c", "x", "y"):
        place = lax.axis_index(name)
        packed = jnp.concatenate([total[1], jnp.broadcast_to(total[0], (16, INNER))], axis=0)
        packed = lax.ppermute(packed.astype(jnp.bfloat16), name, SWAP).astype(jnp.float32)
        other = (packed[STATE : STATE + 1], packed[:STATE])
        leads = place == (0 if backward else 1)
        seen = (jnp.where(leads, other[0], 1.0), jnp.where(leads, other[1], 0.0))
        start = seen if start is None else chain_states(seen, start)
        if name != "y":
            forward = chain_states(other, total)
            reverse = chain_states(total, other)
            total = jax.tree.map(lambda p, q: jnp.where(leads, p, q), forward, reverse)
    return start[1]


KEYS = 512
PAIR = 2 * HEAD_DIM


def attention_forward(q_wide, kv, meta, starts, after=()):
    rows = q_wide.shape[1]
    blocks = kv.shape[0]
    ratio = HEADS_Q // HEADS_KV
    wide = min(512, rows)

    def kernel(meta_ref, q_ref, kv_ref, start_ref, o_ref, log_ref, top, total):
        b = pl.program_id(1)

        @pl.when(b == 0)
        def _():
            top[...] = jnp.full(top.shape, masked_score, jnp.float32)
            total[...] = jnp.zeros(total.shape, jnp.float32)
            o_ref[...] = jnp.zeros(o_ref.shape, jnp.float32)

        def block(partial):
            pair = kv_ref[0, 0]
            turned = pair.T[HEAD_DIM:, :]
            for h in range(ratio):
                for r in range(0, rows, wide):
                    here = slice(r, r + wide)
                    scores = lax.dot_general(pair, q_ref[h, here, :], NT, preferred_element_type=jnp.float32)
                    if partial:
                        keys = b * KEYS + lax.broadcasted_iota(jnp.int32, scores.shape, 0)
                        mine = meta_ref[2] + r + lax.broadcasted_iota(jnp.int32, scores.shape, 1)
                        visible = (keys >= start_ref[0:1, here]) & (keys <= mine)
                        scores = jnp.where(visible, scores, masked_score)
                    before = top[h, 0:1, here]
                    peak = jnp.maximum(before, jnp.max(scores, axis=0, keepdims=True))
                    part = jnp.exp(scores - peak)
                    if partial:
                        part = jnp.where(visible, part, 0.0)
                    fade = jnp.exp(before - peak)
                    top[h, 0:1, here] = peak
                    total[h, 0:1, here] = total[h, 0:1, here] * fade + jnp.sum(part, axis=0, keepdims=True)
                    o_ref[h, :, here] = o_ref[h, :, here] * fade + jnp.dot(
                        turned, part.astype(jnp.bfloat16), preferred_element_type=jnp.float32
                    )

        needed = (b >= meta_ref[0]) & (b < meta_ref[1])
        partial = ((b + 1) * KEYS > meta_ref[2]) | (b * KEYS < meta_ref[3])

        @pl.when(needed & partial)
        def _():
            block(True)

        @pl.when(needed & jnp.logical_not(partial))
        def _():
            block(False)

        @pl.when(b == blocks - 1)
        def _():
            for h in range(ratio):
                sums = total[h, 0:1, :]
                o_ref[h] = o_ref[h] / sums
                log_ref[h] = jnp.broadcast_to(top[h, 0:1, :] + jnp.log(sums), (8, rows))

    heads = lambda g, b, m: (g, 0, 0)
    return pl.pallas_call(
        pinned(kernel, 4, after),
        grid_spec=pltpu.PrefetchScalarGridSpec(
            num_scalar_prefetch=1,
            grid=(HEADS_KV, blocks),
            in_specs=[
                pl.BlockSpec((ratio, rows, PAIR), heads),
                pl.BlockSpec((1, 1, KEYS, PAIR), lambda g, b, m: (b, g, 0, 0)),
                pl.BlockSpec((8, rows), lambda g, b, m: (0, 0)),
            ] + pins(after),
            out_specs=[
                pl.BlockSpec((ratio, HEAD_DIM, rows), heads),
                pl.BlockSpec((ratio, 8, rows), heads),
            ],
            scratch_shapes=[
                pltpu.VMEM((ratio, 8, rows), jnp.float32),
                pltpu.VMEM((ratio, 8, rows), jnp.float32),
            ],
        ),
        out_shape=[
            jax.ShapeDtypeStruct((HEADS_Q, HEAD_DIM, rows), jnp.float32),
            jax.ShapeDtypeStruct((HEADS_Q, 8, rows), jnp.float32),
        ],
        compiler_params=pltpu.CompilerParams(vmem_limit_bytes=48 * 2**20),
        cost_estimate=pl.CostEstimate(flops=2 * 10**10, bytes_accessed=2**23, transcendentals=2**23),
        name="attend",
    )(meta, q_wide, kv, starts, *after)


def attention_backward(q_wide, g_wide, kv, logs, mixed, meta, starts, group, after=()):
    rows = q_wide.shape[1]
    blocks = kv.shape[0]
    ratio = HEADS_Q // HEADS_KV
    wide = min(512, rows)

    def kernel(meta_ref, q_ref, g_ref, kv_ref, log_ref, o_ref, start_ref, dkv_ref, dq_ref, delta, sums):
        b = pl.program_id(0)

        @pl.when(b == 0)
        def _():
            dq_ref[...] = jnp.zeros(dq_ref.shape, jnp.float32)
            for h in range(ratio):
                both = g_ref[h].astype(jnp.float32).T[HEAD_DIM:, :] * o_ref[h]
                delta[h] = jnp.broadcast_to(jnp.sum(both, axis=0, keepdims=True), (8, rows))

        def block(partial):
            pair = kv_ref[0, 0]
            turned = pair.T[:HEAD_DIM, :]
            for h in range(ratio):
                for r in range(0, rows, wide):
                    here = slice(r, r + wide)
                    q_now = q_ref[h, here, :]
                    g_now = g_ref[h, here, :]
                    scores = lax.dot_general(pair, q_now, NT, preferred_element_type=jnp.float32)
                    probs = jnp.exp(scores - log_ref[h, 0:1, here])
                    if partial:
                        keys = b * KEYS + lax.broadcasted_iota(jnp.int32, scores.shape, 0)
                        mine = meta_ref[2] + r + lax.broadcasted_iota(jnp.int32, scores.shape, 1)
                        visible = (keys >= start_ref[0:1, here]) & (keys <= mine)
                        probs = jnp.where(visible, probs, 0.0)
                    grads = lax.dot_general(pair, g_now, NT, preferred_element_type=jnp.float32)
                    low_grads = (probs * (grads - delta[h, 0:1, here])).astype(jnp.bfloat16)
                    change = jnp.dot(
                        probs.astype(jnp.bfloat16), g_now, preferred_element_type=jnp.float32
                    ) + jnp.dot(low_grads, q_now, preferred_element_type=jnp.float32)
                    if h == 0 and r == 0:
                        sums[...] = change
                    else:
                        sums[...] += change
                    dq_ref[h, :, here] += jnp.dot(turned, low_grads, preferred_element_type=jnp.float32)
            dkv_ref[0, 0] = sums[...].astype(jnp.bfloat16)

        needed = (b >= meta_ref[0]) & (b < meta_ref[1])
        partial = ((b + 1) * KEYS > meta_ref[2]) | (b * KEYS < meta_ref[3])

        @pl.when(needed & partial)
        def _():
            block(True)

        @pl.when(needed & jnp.logical_not(partial))
        def _():
            block(False)

        @pl.when(jnp.logical_not(needed))
        def _():
            dkv_ref[0, 0] = jnp.zeros((KEYS, PAIR), jnp.bfloat16)

    heads = lambda b, m: (group, 0, 0)
    return pl.pallas_call(
        pinned(kernel, 7, after),
        grid_spec=pltpu.PrefetchScalarGridSpec(
            num_scalar_prefetch=1,
            grid=(blocks,),
            in_specs=[
                pl.BlockSpec((ratio, rows, PAIR), heads),
                pl.BlockSpec((ratio, rows, PAIR), heads),
                pl.BlockSpec((1, 1, KEYS, PAIR), lambda b, m: (b, group, 0, 0)),
                pl.BlockSpec((ratio, 8, rows), heads),
                pl.BlockSpec((ratio, HEAD_DIM, rows), heads),
                pl.BlockSpec((8, rows), lambda b, m: (0, 0)),
            ] + pins(after),
            out_specs=[
                pl.BlockSpec((1, 1, KEYS, PAIR), lambda b, m: (b, 0, 0, 0)),
                pl.BlockSpec((ratio, HEAD_DIM, rows), lambda b, m: (0, 0, 0)),
            ],
            scratch_shapes=[
                pltpu.VMEM((ratio, 8, rows), jnp.float32),
                pltpu.VMEM((KEYS, PAIR), jnp.float32),
            ],
        ),
        out_shape=[
            jax.ShapeDtypeStruct((blocks, 1, KEYS, PAIR), jnp.bfloat16),
            jax.ShapeDtypeStruct((ratio, HEAD_DIM, rows), jnp.float32),
        ],
        compiler_params=pltpu.CompilerParams(vmem_limit_bytes=48 * 2**20),
        cost_estimate=pl.CostEstimate(flops=2 * 10**10, bytes_accessed=2**23, transcendentals=2**23),
        name="attend_back",
    )(meta, q_wide, g_wide, kv, logs, mixed, starts, *after)


def ordered(place, own, other, axis):
    first = jnp.where(place == 0, own, other)
    second = jnp.where(place == 0, other, own)
    return jnp.stack([first, second], axis=axis)


def gather_span(value, span, fast):
    if not fast:
        return lax.all_gather(value, span)
    _, y, x, c = (lax.axis_index(name) for name in GRID)
    two = ordered(x, value, lax.ppermute(value, "x", SWAP), 0)
    four = ordered(y, two, lax.ppermute(two, "y", SWAP), 0)
    eight = ordered(c, four, lax.ppermute(four, "c", SWAP), 2)
    return eight.reshape((8,) + value.shape)


def scatter_span(value, span, fast):
    if not fast:
        return lax.psum_scatter(value, span, scatter_dimension=0).astype(jnp.float32)
    _, y, x, c = (lax.axis_index(name) for name in GRID)
    value = value.reshape((2, 2, 2) + value.shape[1:])
    for name, place, axis in (("c", c, 2), ("y", y, 0), ("x", x, 0)):
        keep = lax.dynamic_index_in_dim(value, place, axis, keepdims=False)
        send = lax.dynamic_index_in_dim(value, 1 - place, axis, keepdims=False)
        value = keep.astype(jnp.float32) + lax.ppermute(send, name, SWAP).astype(jnp.float32)
        if name != "x":
            value = value.astype(jnp.bfloat16)
    return value


def sum_all(value, axes, fast):
    if not fast:
        return lax.psum(value, axes)
    for name in GRID[1:]:
        value = value + lax.ppermute(value, name, SWAP)
    for pairs in ([(0, 1), (1, 0), (2, 3), (3, 2)], [(0, 2), (2, 0), (1, 3), (3, 1)]):
        value = value + lax.ppermute(value, "z", pairs)
    return value


def offsets_of():
    places, at = {}, 0
    for name_key, extent in layout():
        places[name_key] = (at, extent)
        at += math.prod(extent)
    return places


def early_weights(params):
    places = offsets_of()
    (early, late), where = gather_lines(params)
    names = (W_QUERY, W_KEY, W_VALUE, W_ATTN_OUT, W_GATE_SSM, W_X_SSM, W_B_C)
    misc_at = places[W_STEP][0]
    first = unpack_lines(
        early, 0, where, [flat_segment(name_key) for name_key in names] + [(0, 16, LINE), (misc_at, 288, LINE)]
    )
    weights = dict(zip(names, first))
    weights[NORM_ATTN] = first[-2].reshape(-1)[:D]
    misc = first[-1].reshape(-1)
    for name_key in (W_STEP,) + small_names[1:-1]:
        at, extent = places[name_key]
        weights[name_key] = misc[at - misc_at : at - misc_at + math.prod(extent)].reshape(extent)
    return weights, (early + late, where)


def flat_segment(name_key):
    at, extent = offsets_of()[name_key]
    return (at, extent[0], extent[1])


def late_weights(held, after):
    buffers, where = held
    names = (W_SSM_OUT, W_GATE, W_UP_PROJ, W_DOWN)
    norm_at = offsets_of()[NORM_FFN][0]
    second = unpack_lines(
        buffers, 0, where, [flat_segment(name_key) for name_key in names] + [(norm_at, 16, LINE)], after
    )
    weights = dict(zip(names, second))
    weights[NORM_FFN] = second[-1].reshape(-1)[norm_at % LINE : norm_at % LINE + D]
    return weights


def pack_late(gate, up, down, ssm_low, grad_branch, grad_norm_ffn, after):
    places = offsets_of()
    out_at = places[W_SSM_OUT][0]
    lane = places[W_GATE][0] % LINE
    boundary = 2 * PLANE * LINE
    tail_from = (boundary - out_at) // D
    tail = matmul_left_t(ssm_low[:, tail_from:], grad_branch).reshape(-1)
    tail = tail[boundary - out_at - tail_from * D :]
    head = jnp.concatenate([jnp.zeros((14 * LINE,), jnp.float32), tail, grad_norm_ffn])
    head_rows = head.shape[0] // LINE
    carry = jnp.zeros((8, LINE), jnp.float32).at[7, :lane].set(head[head_rows * LINE :])
    head = head[: head_rows * LINE].reshape(head_rows, LINE).astype(jnp.bfloat16)
    return pack_lines(
        None, 2 * PLANE + 32, head_rows, [gate, up, down], lane, 0, [(head, 0)], carry, 48, after
    )


def pack_out(ssm_low, grad_branch, after):
    out_at = offsets_of()[W_SSM_OUT][0]
    first_row = (8 + out_at // LINE) // 16 * 16
    rows = first_row + SSM_HEADS * SSM_DIM * D // LINE
    return pack_lines(
        None, rows, first_row, [(ssm_low, grad_branch)], out_at % LINE, (8 + out_at // LINE) % 8, [],
        jnp.zeros((8, LINE), jnp.float32), 0, after,
    )


def pack_ssm(target, segments, small, ssm_low, grad_branch, after):
    places = offsets_of()
    misc = [small[name_key].reshape(-1) for name_key in (W_STEP,) + small_names[1:-1]]
    count = sum(part.shape[0] for part in misc)
    misc_rows = (count // LINE + 16) // 16 * 16
    opening = matmul_left_t(ssm_low[:, :16], grad_branch).reshape(-1)
    misc = jnp.concatenate(misc + [opening[: misc_rows * LINE - count]])
    misc = misc.reshape(misc_rows, LINE).astype(jnp.bfloat16)
    first_row = 8 + places[W_ATTN_OUT][0] // LINE
    return pack_lines(
        target, target.shape[0], first_row, segments, 0, 0, [(misc, 8 + places[W_STEP][0] // LINE)], None, 0, after
    )


def pack_qkv(segments, attended, grad_branch, after):
    places = offsets_of()
    out_row = 8 + places[W_ATTN_OUT][0] // LINE
    rows = (8 + SHARD) // 16 * 16 + 8 * PIECE
    closing = matmul_left_t(attended[:, :16], grad_branch).reshape(-1, LINE)
    closing = closing[: rows - out_row].astype(jnp.bfloat16)
    return pack_lines(
        None, rows, 16, segments, 0, 0, [(jnp.zeros((16, LINE), jnp.bfloat16), 0), (closing, out_row)], None, 0, after
    )


def own_lines(early, late, corner, grad_norm_attn):
    z, y, x, c = (lax.axis_index(name) for name in GRID)
    place = 4 * y + 2 * x + c
    shard = SHARD * place
    start = jnp.where(z < 2, (8 + shard) % 16, (14 + shard) % 16)
    lines = jnp.where(z < 2, early, late)
    lines = jnp.where((z == 0) & (place < 2), corner[:WIN], lines)
    lines = lax.dynamic_slice(lines, (start, 0), (SHARD, LINE)).astype(jnp.float32)
    norms = jnp.where((z == 0) & (place == 0), grad_norm_attn.reshape(-1, LINE), lines[: D // LINE])
    return jnp.concatenate([norms, lines[D // LINE :]]).reshape(-1)


def body(span, group, fast, tokens, params, cotangent, offsets):
    rows_dev = tokens.shape[0]
    group_rows = rows_dev * lax.axis_size(span)
    all_rows = group_rows * lax.axis_size(group)
    ssm_inner = SSM_HEADS * SSM_DIM
    score_scale = HEAD_DIM ** (-0.5)
    bounds = offsets[0]
    my_start = lax.axis_index(span) * rows_dev
    row_index = my_start + jnp.arange(rows_dev, dtype=jnp.int32)
    seq_id, positions = sequence_info(row_index, bounds)
    first_start = row_index[0] - positions[0]
    last_row = my_start + rows_dev - 1
    cosine, sine = rotary_tables(positions)
    if fast:
        weights, held = early_weights(params)
    else:
        weights = unpack(lax.all_gather(params, group + span, axis=0, tiled=True))
    small_f32 = {name_key: weights[name_key].astype(jnp.float32) for name_key in small_names[:-1]}
    x_rows = tokens.astype(jnp.float32)
    normed_one, norm_one_back = jax.vjp(rms_norm, x_rows, small_f32[NORM_ATTN])
    hidden = normed_one.astype(jnp.bfloat16)
    query = matmul(hidden, weights[W_QUERY])
    key_raw = matmul(hidden, weights[W_KEY])
    value_low = matmul(hidden, weights[W_VALUE]).astype(jnp.bfloat16)
    q_rot = rotate(query, cosine, sine, HEADS_Q).astype(jnp.bfloat16)
    k_rot = rotate(key_raw, cosine, sine, HEADS_KV).astype(jnp.bfloat16)
    k_heads = k_rot.reshape(rows_dev, HEADS_KV, HEAD_DIM)
    v_heads = value_low.reshape(rows_dev, HEADS_KV, HEAD_DIM)
    kv_mine = jnp.concatenate([k_heads, v_heads], axis=2).transpose(1, 0, 2)
    key_blocks = gather_span(kv_mine.reshape(HEADS_KV, rows_dev, PAIR), span, fast)
    if rows_dev != KEYS:
        key_blocks = key_blocks.transpose(1, 0, 2, 3).reshape(HEADS_KV, -1, KEYS, PAIR).transpose(1, 0, 2, 3)
    row_starts = row_index - positions
    meta = jnp.stack(
        [first_start // KEYS, last_row // KEYS + 1, my_start, row_starts[rows_dev - 1]]
    ).astype(jnp.int32)
    q_low = (q_rot * jnp.bfloat16(score_scale)).reshape(rows_dev, HEADS_Q, HEAD_DIM).transpose(1, 0, 2)
    q_wide = jnp.pad(q_low, ((0, 0), (0, 0), (0, HEAD_DIM)))
    start_row = jnp.broadcast_to(row_starts[None, :], (8, rows_dev))
    mixed, logs = attention_forward(q_wide, key_blocks, meta, start_row)
    attended = mixed.astype(jnp.bfloat16).reshape(HEADS_Q * HEAD_DIM, rows_dev).T
    attn_out = matmul(attended, weights[W_ATTN_OUT])
    gate_ssm = matmul(hidden, weights[W_GATE_SSM])
    xbc = jnp.concatenate(
        [matmul(hidden, weights[W_X_SSM]), matmul(hidden, weights[W_B_C])], axis=1
    )
    step_raw = matmul(hidden, weights[W_STEP])
    rim_rows = passed_along(xbc[rows_dev - 8 :], span, 1)
    ssm_meta = jnp.concatenate([my_start[None], row_starts[CHUNK - 1 :: CHUNK]]).astype(jnp.int32)
    conv_bias = small_f32[CONV_BIAS][None, :]
    conv_values = conv_forward(xbc, rim_rows, small_f32[CONV_WEIGHT], conv_bias, ssm_meta, row_starts[:, None])
    step_in = step_raw.T + small_f32[STEP_BIAS][:, None]
    step_rows = jax.nn.softplus(step_in)
    decay = -jnp.exp(small_f32[DECAY_LOG])
    logs_step = step_rows * decay[:, None]
    order = jnp.arange(rows_dev)
    upto = (order[:, None] <= order[None, :]).astype(jnp.float32)
    cumul = jnp.dot(logs_step, upto, precision=highest)
    chunk_cum = jnp.dot(
        logs_step.reshape(-1, CHUNK), upto[:CHUNK, :CHUNK], precision=highest
    ).reshape(SSM_HEADS, rows_dev)
    went_on = row_starts < my_start
    entry_rows = jnp.where(went_on[None, :], jnp.exp(cumul), 0.0)
    in_last = row_index >= row_starts[rows_dev - 1]
    tail_rows = jnp.exp(jnp.where(in_last[None, :], cumul[:, -1:] - cumul, masked_score))
    carry_all = entry_rows[:, -1]
    local_state = weighted_state(conv_values, PAIRS, conv_values, tail_rows * step_rows)
    state_in = scan_states(carry_all, local_state, span, fast, False)
    skip_wide = jnp.repeat(small_f32[SKIP_GAIN], SSM_DIM)[None, :]
    ssm_y = ssm_forward(
        conv_values, chunk_cum, step_rows, state_in, skip_wide, ssm_meta, row_starts[:, None], start_row
    )
    normed_ssm, gnorm_back = jax.vjp(gated_norm, ssm_y, gate_ssm, small_f32[NORM_SSM])
    ssm_low = normed_ssm.astype(jnp.bfloat16)
    if fast:
        weights.update(late_weights(held, [mixed]))
    small_f32[NORM_FFN] = weights[NORM_FFN].astype(jnp.float32)
    ssm_out = matmul(ssm_low, weights[W_SSM_OUT])
    middle = x_rows + attn_out + ssm_out
    normed_two, norm_two_back = jax.vjp(rms_norm, middle, small_f32[NORM_FFN])
    hidden_two = normed_two.astype(jnp.bfloat16)
    gate_ffn = matmul(hidden_two, weights[W_GATE])
    upper = matmul(hidden_two, weights[W_UP_PROJ])
    activation_f32, swiglu_back = jax.vjp(swiglu, gate_ffn, upper)
    activation = activation_f32.astype(jnp.bfloat16)
    ffn_out = matmul(activation, weights[W_DOWN])
    result = middle + ffn_out
    squares = jnp.stack(
        [
            jnp.sum(result * result),
            jnp.sum(attn_out * attn_out),
            jnp.sum(ssm_out * ssm_out),
            jnp.sum(ffn_out * ffn_out),
        ]
    )
    totals = sum_all(squares, group + span, fast)
    stats = jnp.sqrt(totals / (all_rows * D))
    grad_out = cotangent.astype(jnp.float32)
    grad_activation = matmul_right_t(cotangent, weights[W_DOWN])
    grad_gate_f32, grad_upper_f32 = swiglu_back(grad_activation)
    grad_gate = grad_gate_f32.astype(jnp.bfloat16)
    grad_upper = grad_upper_f32.astype(jnp.bfloat16)
    grad_hidden_two = matmul_right_t(grad_gate, weights[W_GATE]) + matmul_right_t(
        grad_upper, weights[W_UP_PROJ]
    )
    grad_middle_norm, grad_norm_ffn = norm_two_back(grad_hidden_two)
    grad_middle = grad_out + grad_middle_norm
    grad_branch = grad_middle.astype(jnp.bfloat16)
    grad_attended = matmul_right_t(grad_branch, weights[W_ATTN_OUT]).astype(jnp.bfloat16)
    grad_ssm_low = matmul_right_t(grad_branch, weights[W_SSM_OUT])
    grad_ssm_y, grad_gate_ssm_f32, grad_norm_ssm = gnorm_back(grad_ssm_low)
    grad_state_local = weighted_state(conv_values, PAIRS + 1, grad_ssm_y, entry_rows)
    pinned_by = ()
    if fast:
        late = pack_late(
            (hidden_two, grad_gate), (hidden_two, grad_upper), (activation, cotangent),
            ssm_low, grad_branch, grad_norm_ffn, [grad_state_local],
        )
        late_flow = Flow(reduce_stages(late, 1, 14))
        early = pack_out(ssm_low, grad_branch, late_flow.values())
        late_flow.go()
        pinned_by = late_flow.values()
    grad_state_out = scan_states(carry_all, grad_state_local, span, fast, True)
    grad_x, grad_b, grad_c, grad_small = ssm_backward(
        conv_values, grad_ssm_y, chunk_cum, step_rows, state_in, grad_state_out, skip_wide, ssm_meta, start_row, pinned_by
    )
    grad_direct = grad_small[:, 0:2].reshape(SSM_HEADS, rows_dev)
    grad_logs = grad_small[:, 2:4].reshape(SSM_HEADS, rows_dev)
    grad_decay_log = decay * jnp.sum(step_rows * grad_logs, axis=1)
    grad_step_rows = (grad_direct + decay[:, None] * grad_logs) * jax.nn.sigmoid(step_in)
    grad_step_bias = jnp.sum(grad_step_rows, axis=1)
    grad_step_raw_f32 = grad_step_rows.T
    grad_skip_gain = jnp.sum(grad_small[:, 4, : 2 * SSM_DIM].reshape(SSM_HEADS, SSM_DIM), axis=1)
    if fast:
        late_flow.go()
        pinned_by = late_flow.values()
    grad_main, grad_tail, grad_edge, grad_taps = conv_backward(
        grad_x, grad_b, grad_c, xbc, rim_rows, small_f32[CONV_WEIGHT], conv_bias, ssm_meta,
        row_starts[:, None], pinned_by,
    )
    grad_conv_weight = grad_taps[:CONV]
    grad_conv_bias = grad_taps[CONV]
    rim_back = passed_along(grad_edge, span, -1)
    grad_tail = grad_tail + jnp.pad(rim_back, ((8, 0), (0, 0)))
    grad_xbc = lax.dynamic_update_slice(grad_main, grad_tail.astype(jnp.bfloat16), (rows_dev - 16, 0))
    grad_gate_ssm = grad_gate_ssm_f32.astype(jnp.bfloat16)
    grad_step_raw = grad_step_raw_f32.astype(jnp.bfloat16)
    grad_w_step = matmul_left_t(hidden, grad_step_raw)
    grad_hidden_ssm = (
        matmul_right_t(grad_gate_ssm, weights[W_GATE_SSM])
        + matmul_right_t(grad_xbc[:, :ssm_inner], weights[W_X_SSM])
        + matmul_right_t(grad_xbc[:, ssm_inner:], weights[W_B_C])
        + matmul_right_t(grad_step_raw, weights[W_STEP])
    )
    small = {
        W_STEP: grad_w_step,
        CONV_WEIGHT: grad_conv_weight,
        CONV_BIAS: grad_conv_bias,
        STEP_BIAS: grad_step_bias,
        DECAY_LOG: grad_decay_log,
        SKIP_GAIN: grad_skip_gain,
        NORM_SSM: grad_norm_ssm,
        NORM_FFN: grad_norm_ffn,
    }
    g_low = grad_attended.reshape(rows_dev, HEADS_Q, HEAD_DIM).transpose(1, 0, 2)
    g_wide = jnp.pad(g_low, ((0, 0), (0, 0), (HEAD_DIM, 0)))
    if fast:
        late_flow.go()
        early = pack_ssm(
            early,
            [
                (attended, grad_branch), (hidden, grad_gate_ssm),
                (hidden, grad_xbc[:, :ssm_inner]), (hidden, grad_xbc[:, ssm_inner:]),
            ],
            small, ssm_low, grad_branch, late_flow.values(),
        )
        late_flow.go()
        early_flow = Flow(reduce_stages(early, 0, 8))
        pinned_by = early_flow.values()
    parts = []
    for group_at in range(HEADS_KV):
        parts.append(
            attention_backward(q_wide, g_wide, key_blocks, logs, mixed, meta, start_row, group_at, pinned_by)
        )
        if fast:
            early_flow.go()
            pinned_by = early_flow.values() + late_flow.values() + [parts[-1][1]]
    grad_kv = jnp.concatenate([part[0] for part in parts], axis=1)
    grad_q_turned = jnp.concatenate([part[1] for part in parts], axis=0)
    if rows_dev != KEYS:
        grad_kv = grad_kv.transpose(1, 0, 2, 3).reshape(HEADS_KV, -1, rows_dev, PAIR).transpose(1, 0, 2, 3)
    grad_kv_mine = scatter_span(grad_kv, span, fast)
    grad_keys_mine = grad_kv_mine[:, :, :HEAD_DIM].transpose(1, 0, 2).reshape(rows_dev, -1)
    grad_values_mine = grad_kv_mine[:, :, HEAD_DIM:].transpose(1, 0, 2).reshape(rows_dev, -1)
    grad_q_rot = grad_q_turned.reshape(HEADS_Q * HEAD_DIM, rows_dev).T * score_scale
    grad_query_low = rotate(grad_q_rot, cosine, -sine, HEADS_Q).astype(jnp.bfloat16)
    grad_key_low = rotate(grad_keys_mine, cosine, -sine, HEADS_KV).astype(jnp.bfloat16)
    grad_value_low = grad_values_mine.astype(jnp.bfloat16)
    if fast:
        corner = pack_qkv(
            [(hidden, grad_query_low), (hidden, grad_key_low), (hidden, grad_value_low)],
            attended, grad_branch, early_flow.values(),
        )
        early_flow.go()
        corner_flow = Flow(corner_stages(corner))
        for flow in (early_flow, late_flow, corner_flow):
            while flow.sends:
                flow.go()
    grad_hidden = (
        grad_hidden_ssm
        + matmul_right_t(grad_query_low, weights[W_QUERY])
        + matmul_right_t(grad_key_low, weights[W_KEY])
        + matmul_right_t(grad_value_low, weights[W_VALUE])
    )
    grad_x_norm, grad_norm_attn = norm_one_back(grad_hidden)
    grad_tokens = grad_middle + grad_x_norm
    if fast:
        norms = sum_all(grad_norm_attn, group + span, fast)
        grad_shard = own_lines(early_flow.result, late_flow.result, corner_flow.result, norms)
        return (result.astype(jnp.bfloat16), grad_tokens, grad_shard, stats)
    small[NORM_ATTN] = grad_norm_attn
    pairs = {
        W_QUERY: (hidden, grad_query_low),
        W_KEY: (hidden, grad_key_low),
        W_VALUE: (hidden, grad_value_low),
        W_ATTN_OUT: (attended, grad_branch),
        W_GATE_SSM: (hidden, grad_gate_ssm),
        W_X_SSM: (hidden, grad_xbc[:, :ssm_inner]),
        W_B_C: (hidden, grad_xbc[:, ssm_inner:]),
        W_SSM_OUT: (ssm_low, grad_branch),
        W_GATE: (hidden_two, grad_gate),
        W_UP_PROJ: (hidden_two, grad_upper),
        W_DOWN: (activation, cotangent),
    }
    grad_dict = dict(small)
    for name_key, (left, right) in pairs.items():
        grad_dict[name_key] = matmul_left_t(left, right)
    flat_parts = [grad_dict[name_key].reshape(-1) for name_key, extent in layout()]
    used_entries = 0
    for part_array in flat_parts:
        used_entries += part_array.shape[0]
    flat_parts.append(jnp.zeros((params.shape[0] * lax.axis_size(group + span) - used_entries,), jnp.float32))
    grad_shard = lax.psum_scatter(
        jnp.concatenate(flat_parts), group + span, scatter_dimension=0, tiled=True
    )
    return (result.astype(jnp.bfloat16), grad_tokens, grad_shard, stats)


def solution(mesh):
    fast = (mesh.shape["group"], mesh.shape["span"]) == FAST
    if fast:
        mesh = Mesh(mesh.devices.reshape(4, 2, 2, 2), GRID)
        group, span = (GRID[:1], GRID[1:])
    else:
        group, span = (("group",), ("span",))

    def program(tokens, params, cotangent, offsets):
        return body(span, group, fast, tokens, params, cotangent, offsets)

    return jax.shard_map(
        program,
        mesh=mesh,
        in_specs=(P(group + span, None), P(group + span), P(group + span, None), P(group, None)),
        out_specs=(P(group + span, None), P(group + span, None), P(group + span), P()),
        check_vma=False,
    )
```

```python
import math

import jax
import jax.numpy as jnp
import numpy as np
from jax import lax
from jax.experimental import pallas as pl
from jax.experimental.pallas import tpu as pltpu
from jax.sharding import Mesh, PartitionSpec as P

D = 1024
HEADS_Q = 8
HEADS_KV = 2
HEAD_DIM = 64
SSM_HEADS = 24
SSM_DIM = 64
STATE = 128
CONV = 4
FF = 2048
(
    NORM_ATTN,
    W_QUERY,
    W_KEY,
    W_VALUE,
    W_ATTN_OUT,
    W_GATE_SSM,
    W_X_SSM,
    W_B_C,
    W_STEP,
    CONV_WEIGHT,
    CONV_BIAS,
    STEP_BIAS,
    DECAY_LOG,
    SKIP_GAIN,
    NORM_SSM,
    W_SSM_OUT,
    NORM_FFN,
    W_GATE,
    W_UP_PROJ,
    W_DOWN,
) = range(20)


epsilon = 1e-05
rope_base = 100000000000.0
masked_score = -1e30
highest = lax.Precision.HIGHEST
small_names = (
    NORM_ATTN,
    CONV_WEIGHT,
    CONV_BIAS,
    STEP_BIAS,
    DECAY_LOG,
    SKIP_GAIN,
    NORM_SSM,
    NORM_FFN,
)


def passed_along(value, axis, steps):
    count = lax.axis_size(axis)
    first, last = (max(0, -steps), min(count, count - steps))
    return lax.ppermute(value, axis, [(source, source + steps) for source in range(first, last)])


def prefix(value, axis, combine, identity):
    peers, place = (lax.axis_size(axis), lax.axis_index(axis))
    everything = jax.tree.map(
        lambda part, kind: lax.all_gather(part.astype(kind), axis),
        value,
        (jnp.bfloat16, jnp.bfloat16),
    )
    start = jax.tree.map(
        lambda part, zero: jnp.broadcast_to(jnp.asarray(zero, part.dtype), part.shape),
        value,
        identity,
    )

    def prefix_turn(k, before):
        reached = k < place
        new = combine(
            before, jax.tree.map(lambda part, own: part[k].astype(own.dtype), everything, value)
        )
        return jax.tree.map(lambda a, b: jnp.where(reached, a, b), new, before)

    return lax.fori_loop(0, peers, prefix_turn, start)


def carried_in(value, axis, combine, identity):
    peers, place = (lax.axis_size(axis), lax.axis_index(axis))
    everything = jax.tree.map(
        lambda part, kind: lax.all_gather(part.astype(kind), axis),
        value,
        jax.tree.map(lambda a: jnp.bfloat16 if a.dtype == jnp.float32 else a.dtype, value),
    )
    start = jax.tree.map(
        lambda part, zero: jnp.broadcast_to(jnp.asarray(zero, part.dtype), part.shape),
        value,
        identity,
    )

    def carried_turn(k, before):
        at = peers - 1 - k
        reached = at > place
        new = combine(
            before, jax.tree.map(lambda part, own: part[at].astype(own.dtype), everything, value)
        )
        return jax.tree.map(lambda a, b: jnp.where(reached, a, b), new, before)

    return lax.fori_loop(0, peers, carried_turn, start)


def layout():
    ssm_inner = SSM_HEADS * SSM_DIM
    channels = ssm_inner + 2 * STATE
    return [
        (NORM_ATTN, (D,)),
        (W_QUERY, (D, HEADS_Q * HEAD_DIM)),
        (W_KEY, (D, HEADS_KV * HEAD_DIM)),
        (W_VALUE, (D, HEADS_KV * HEAD_DIM)),
        (W_ATTN_OUT, (HEADS_Q * HEAD_DIM, D)),
        (W_GATE_SSM, (D, ssm_inner)),
        (W_X_SSM, (D, ssm_inner)),
        (W_B_C, (D, 2 * STATE)),
        (W_STEP, (D, SSM_HEADS)),
        (CONV_WEIGHT, (CONV, channels)),
        (CONV_BIAS, (channels,)),
        (STEP_BIAS, (SSM_HEADS,)),
        (DECAY_LOG, (SSM_HEADS,)),
        (SKIP_GAIN, (SSM_HEADS,)),
        (NORM_SSM, (ssm_inner,)),
        (W_SSM_OUT, (ssm_inner, D)),
        (NORM_FFN, (D,)),
        (W_GATE, (D, FF)),
        (W_UP_PROJ, (D, FF)),
        (W_DOWN, (FF, D)),
    ]


def unpack(flat_vector):
    unpacked = {}
    offset = 0
    for name_key, extent in layout():
        amount = math.prod(extent)
        unpacked[name_key] = flat_vector[offset : offset + amount].reshape(extent)
        offset += amount
    return unpacked


def matmul(left, right):
    return jnp.dot(left, right, preferred_element_type=jnp.float32)


def matmul_left_t(left, right):
    return lax.dot_general(
        left, right, (((0,), (0,)), ((), ())), preferred_element_type=jnp.float32
    )


def matmul_right_t(left, right):
    return lax.dot_general(
        left, right, (((1,), (1,)), ((), ())), preferred_element_type=jnp.float32
    )


def rms_norm(values, gain):
    return values * lax.rsqrt(jnp.mean(values * values, axis=-1, keepdims=True) + epsilon) * gain


def gated_norm(ssm_y, gate_ssm, gain):
    return rms_norm(ssm_y * jax.nn.silu(gate_ssm), gain)


def swiglu(gate_ffn, upper):
    return jax.nn.silu(gate_ffn) * upper


def sequence_info(row_index, bounds):
    starts = bounds[:-1]
    inside = row_index[:, None] >= starts[None, :]
    seq_id = jnp.sum(inside.astype(jnp.int32), axis=1) - 1
    seq_start = jnp.max(jnp.where(inside, starts[None, :], 0), axis=1)
    return (seq_id, row_index - seq_start)


def rotary_tables(positions):
    half_dim = HEAD_DIM // 2
    freqs = jnp.exp(
        -jnp.arange(half_dim, dtype=jnp.float32) * (2.0 * math.log(rope_base) / HEAD_DIM)
    )
    angles = positions.astype(jnp.float32)[:, None] * freqs[None, :]
    return (jnp.cos(angles), jnp.sin(angles))


def rotate(values, cosine, sine, heads):
    row_count = values.shape[0]
    half_dim = HEAD_DIM // 2
    split_heads = values.reshape(row_count, heads, HEAD_DIM)
    first_half = split_heads[..., :half_dim]
    second_half = split_heads[..., half_dim:]
    cos_b = cosine[:, None, :]
    sin_b = sine[:, None, :]
    turned = jnp.concatenate(
        [first_half * cos_b - second_half * sin_b, second_half * cos_b + first_half * sin_b],
        axis=-1,
    )
    return turned.reshape(row_count, heads * HEAD_DIM)


def add_rows(target, addend, first_row):
    current = lax.dynamic_slice_in_dim(target, first_row, addend.shape[0], 0)
    return lax.dynamic_update_slice_in_dim(target, current + addend, first_row, 0)


FAST = (4, 8)
LINE = 128
SHARD = 3082
SPAD = 3088
WIN = 3104
PLANE = 8 * SHARD
DEPTH = 4
TALL = {1: 1024, 2: 1024, 4: 512, 8: 256, 12: 128, 16: 128}
GRID = ("z", "y", "x", "c")
ZC = ("z", "c")
SWAP = [(0, 1), (1, 0)]


def zc_pairs(*pairs):
    return [(2 * a + c, 2 * b + c) for a, b, c in pairs]


def pinned(kernel, count, after):
    return lambda *refs: kernel(*refs[:count], *refs[count + len(after) :])


def pins(after):
    return [pl.BlockSpec(memory_space=pltpu.HBM)] * len(after)


def fence(values, after):
    def kernel(*refs):
        del refs

    return pl.pallas_call(
        kernel,
        in_specs=pins(values) + pins(after),
        out_specs=pins(values),
        out_shape=[jax.ShapeDtypeStruct(value.shape, value.dtype) for value in values],
        input_output_aliases={k: k for k in range(len(values))},
        name="fence",
    )(*values, *after)


def bracket(call, flows):
    out = call([value for flow in flows for value in flow.values()])
    for flow in flows:
        flow.go()
    return fence(out if isinstance(out, (list, tuple)) else [out], [v for flow in flows for v in flow.values()])


def gather_lines(params):
    z, y, x, c = (lax.axis_index(name) for name in GRID)
    lines = jnp.pad(params.reshape(SHARD, LINE), ((0, SPAD - SHARD), (0, 0)))
    sibling = lax.ppermute(lines, ZC, [(2 * k + 1 - k % 2, 2 * k + k % 2) for k in range(4)])
    buffers = []
    for part in range(2):
        here = jnp.where(c == part, lines, sibling)
        one = lax.ppermute(here, ZC, zc_pairs((0, 1, 0), (1, 2, 1)))
        side = lax.ppermute(here, ZC, zc_pairs((1, 0, 1)))
        two = lax.ppermute(one, ZC, zc_pairs((1, 2, 0), (2, 3, 1)))
        three = lax.ppermute(two, ZC, zc_pairs((2, 3, 0)))
        column = jnp.where(z == c, here, one + side + two + three)
        over_x = lax.ppermute(column, "x", SWAP)
        over_y = lax.ppermute(column, "y", SWAP)
        corner = lax.ppermute(over_y if part else over_x, "x" if part else "y", SWAP)
        local = [column, over_x, over_y, corner]
        buffers += [piece[None] for piece in local]
        buffers += [lax.ppermute(piece, "c", SWAP)[None] for piece in local]
    early = [(k, 0) for k in range(16)]
    here = jnp.where(c == 0, jnp.stack([lines, sibling]), jnp.stack([sibling, lines]))
    one = lax.ppermute(here, ZC, zc_pairs((2, 1, 0), (3, 2, 1)))
    side = lax.ppermute(here, ZC, zc_pairs((2, 3, 0)))
    two = lax.ppermute(one, ZC, zc_pairs((1, 0, 0), (2, 1, 1)))
    three = lax.ppermute(two, ZC, zc_pairs((1, 0, 1)))
    column = jnp.where(z == 2 + c, here, one + side + two + three)
    over_x = lax.ppermute(column, "x", SWAP)
    over_y = lax.ppermute(column, "y", SWAP)
    corners = [lax.ppermute(over_x[:1], "y", SWAP), lax.ppermute(over_y[1:], "x", SWAP)]
    local = [column, over_x, over_y] + corners
    buffers += local + [lax.ppermute(piece, "c", SWAP) for piece in local]
    late = []
    for part in range(2):
        for first in (16, 21):
            late += [(first, part), (first + 1, part), (first + 2, part), (first + 3 + part, 0)]
    shard = np.arange(32)
    sz, sy, sx, sc = shard // 8, shard // 4 % 2, shard // 2 % 2, shard % 2
    away = jnp.where(sz % 2 == c, 0, 4)
    where = sc * 8 + away + 2 * (sy ^ y) + (sx ^ x) + 16 * (sz // 2)
    return buffers, (early, early + late), where.astype(jnp.int32)


def unpack_lines(buffers, slots, where, segments, after=()):
    jobs, starts = [], []
    reach = 0
    for offset, rows, columns in segments:
        per_row = columns // LINE
        lane, base = offset % LINE, offset // LINE
        if per_row == 1 and rows < 1024:
            lane, tall = 0, rows
        else:
            tall = TALL[per_row]
        starts.append(len(jobs))
        for k in range(rows // tall):
            jobs.append((base + k * tall * per_row, tall * per_row, 1 if lane else 0))
    window = max(job[1] for job in jobs) + 32
    table = np.zeros((len(jobs), 5), np.int32)
    for k, (line, count, extra) in enumerate(jobs):
        owner = line // SHARD
        inside = line - owner * SHARD
        begin = min(inside // 16 * 16, SPAD - window)
        crosses = int(line + count + extra > (owner + 1) * SHARD)
        table[k] = (owner, begin, begin - inside, crosses, (owner + 1) * SHARD - line)
    base_row = (int(-table[:, 2].min()) + 7) // 8 * 8
    table[:, 2] += base_row
    table[:, 4] += base_row
    room = int(max((table[:, 2] + window).max(), ((table[:, 4] + window) * table[:, 3]).max()))
    room = (room + 15) // 8 * 8
    total = len(jobs)
    count_buffers = len(buffers)
    shapes = []
    for offset, rows, columns in segments:
        per_row = columns // LINE
        tall = rows if per_row == 1 and rows < 1024 else TALL[per_row]
        shapes.append((rows, columns, tall, per_row, offset % LINE if tall != rows or per_row != 1 else 0))
    sizes = sorted({(tall, columns) for _, columns, tall, _, _ in shapes})

    def kernel(table_ref, where_ref, *refs):
        sources = refs[:count_buffers]
        outs = refs[count_buffers : count_buffers + len(segments)]
        rest = refs[count_buffers + len(segments) :]
        stages = dict(zip(sizes, rest))
        raw, flat, in_sem, out_sem = rest[len(sizes) :]
        step = pl.program_id(0)

        def fetch(job, slot):
            owner = table_ref[job, 0]
            begin = pl.multiple_of(table_ref[job, 1], 16)
            for b, (source, part) in enumerate(slots):

                @pl.when(where_ref[owner] == b)
                def _():
                    pltpu.make_async_copy(
                        sources[source].at[part, pl.ds(begin, window), :], raw.at[slot, 0], in_sem.at[slot, 0]
                    ).start()

            @pl.when(table_ref[job, 3] == 1)
            def _():
                for b, (source, part) in enumerate(slots):

                    @pl.when(where_ref[owner + 1] == b)
                    def _():
                        pltpu.make_async_copy(
                            sources[source].at[part, pl.ds(0, window), :], raw.at[slot, 1], in_sem.at[slot, 1]
                        ).start()

        def fetched(slot, half):
            return pltpu.make_async_copy(
                sources[0].at[0, pl.ds(0, window), :], raw.at[slot, half], in_sem.at[slot, half]
            )

        @pl.when(step == 0)
        def _():
            for k in range(min(DEPTH - 1, total)):
                fetch(k, k)

        @pl.when(step + DEPTH - 1 < total)
        def _():
            fetch(step + DEPTH - 1, lax.rem(step + DEPTH - 1, DEPTH))

        slot = lax.rem(step, DEPTH)
        fetched(slot, 0).wait()
        flat[pl.ds(table_ref[step, 2], window), :] = raw[slot, 0].astype(jnp.float32)

        @pl.when(table_ref[step, 3] == 1)
        def _():
            fetched(slot, 1).wait()
            flat[pl.ds(table_ref[step, 4], window), :] = raw[slot, 1].astype(jnp.float32)

        for index, (rows, columns, tall, per_row, lane) in enumerate(shapes):
            begin = starts[index]
            blocks = rows // tall
            stage = stages[(tall, columns)]

            @pl.when((step >= begin) & (step < begin + blocks))
            def _():
                block = step - begin
                side = lax.rem(block, 2)

                def written(k, s):
                    return pltpu.make_async_copy(
                        stage.at[s],
                        outs[index].at[pl.ds(pl.multiple_of(k * tall, 16), tall), :],
                        out_sem.at[s],
                    )

                @pl.when(block >= 2)
                def _():
                    written(block - 2, side).wait()

                def tile(j):
                    picked = flat[pl.ds(base_row + j, tall, stride=per_row), :]
                    return pltpu.roll(picked, LINE - lane, 1) if lane else picked

                if lane:
                    lanes = lax.broadcasted_iota(jnp.int32, (tall, LINE), 1)
                    now = tile(0)
                    for j in range(per_row):
                        later = tile(j + 1)
                        stage[side, :, j * LINE : (j + 1) * LINE] = jnp.where(
                            lanes < LINE - lane, now, later
                        ).astype(jnp.bfloat16)
                        now = later
                else:
                    for j in range(per_row):
                        stage[side, :, j * LINE : (j + 1) * LINE] = tile(j).astype(jnp.bfloat16)
                written(block, side).start()

                @pl.when(block == blocks - 1)
                def _():
                    if blocks > 1:
                        written(block - 1, 1 - side).wait()
                    written(block, side).wait()

    return pl.pallas_call(
        pinned(kernel, 2 + count_buffers, after),
        grid_spec=pltpu.PrefetchScalarGridSpec(
            num_scalar_prefetch=2,
            grid=(total,),
            in_specs=[pl.BlockSpec(memory_space=pl.ANY)] * count_buffers + pins(after),
            out_specs=[pl.BlockSpec(memory_space=pl.ANY)] * len(segments),
            scratch_shapes=[pltpu.VMEM((2,) + size, jnp.bfloat16) for size in sizes]
            + [
                pltpu.VMEM((DEPTH, 2, window, LINE), jnp.bfloat16),
                pltpu.VMEM((room, LINE), jnp.float32),
                pltpu.SemaphoreType.DMA((DEPTH, 2)),
                pltpu.SemaphoreType.DMA((2,)),
            ],
        ),
        out_shape=[jax.ShapeDtypeStruct((rows, columns), jnp.bfloat16) for _, rows, columns in segments],
        compiler_params=pltpu.CompilerParams(vmem_limit_bytes=48 * 2**20),
        cost_estimate=pl.CostEstimate(flops=0, bytes_accessed=total * window * LINE * 4, transcendentals=0),
        name="unpack",
    )(jnp.asarray(table), where, *buffers, *after)


def pack_lines(target, target_rows, first_row, segments, lane, phase, extras, carry, tail_rows, after=()):
    tall = 256
    lefts, rights, plan = [], [], []
    left_of, right_of = {}, {}
    row = first_row
    begin = 0
    for left, right in segments:
        for value, seen, kept in ((left, left_of, lefts), (right, right_of, rights)):
            if id(value) not in seen:
                seen[id(value)] = len(kept)
                kept.append(value)
        blocks = left.shape[1] // tall
        plan.append((left_of[id(left)], right_of[id(right)], right.shape[1] // LINE, begin, blocks, row))
        begin += blocks
        row += left.shape[1] * right.shape[1] // LINE
    end_row = row
    total = begin
    biggest = max(entry[2] for entry in plan) * tall
    tokens = lefts[0].shape[0]
    count_left, count_right, count_extra = len(lefts), len(rights), len(extras)
    rolled = [jnp.roll(right, lane, axis=1) if lane else right for right in rights]
    carry_in = [carry] if lane else []
    targets = [] if target is None else [target]

    def left_spec(index):
        mine = [entry for entry in plan if entry[0] == index]

        def place(step):
            block = 0
            for _, _, _, start, blocks, _ in mine:
                block = jnp.where(step >= start, jnp.minimum(step - start, blocks - 1), block)
            return (0, block)

        return pl.BlockSpec((tokens, tall), place)

    def kernel(*refs):
        left_refs = refs[:count_left]
        right_refs = refs[count_left : count_left + count_right]
        at = count_left + count_right
        extra_refs = refs[at : at + count_extra]
        at += count_extra
        carry_refs = refs[at : at + len(carry_in)]
        at += len(carry_in) + len(targets)
        out = refs[at]
        flat, stage, shift, last, sems, extra_sems = refs[at + 1 :]
        step = pl.program_id(0)
        side = lax.rem(step, 2)

        def extra_copy(k):
            rows = extras[k][0].shape[0]
            return pltpu.make_async_copy(
                extra_refs[k], out.at[pl.ds(extras[k][1], rows), :], extra_sems.at[k]
            )

        @pl.when(step == 0)
        def _():
            for k in range(count_extra):
                extra_copy(k).start()
            if lane:
                shift[0:8, :] = carry_refs[0][...]
            if phase:
                flat[0:8, :] = jnp.zeros((8, LINE), jnp.float32)

        for left_at, right_at, per_row, start, blocks, row in plan:
            lines = per_row * tall

            def written(block, s, row=row, lines=lines):
                return pltpu.make_async_copy(
                    stage.at[s, pl.ds(0, lines), :],
                    out.at[pl.ds(pl.multiple_of(row + block * lines, 16), lines), :],
                    sems.at[s],
                )

            @pl.when((step >= start) & (step < start + blocks))
            def _():
                block = step - start
                if phase:

                    @pl.when(step > 0)
                    def _():
                        flat[0:8, :] = flat[lines : lines + 8, :]

                turned = left_refs[left_at][...].T
                lanes = lax.broadcasted_iota(jnp.int32, (tall, LINE), 1)
                for j0 in range(0, per_row, 2):
                    wide = min(2, per_row - j0)
                    tile = jnp.dot(
                        turned,
                        right_refs[right_at][:, j0 * LINE : (j0 + wide) * LINE],
                        preferred_element_type=jnp.float32,
                    )
                    for j in range(wide):
                        piece = tile[:, j * LINE : (j + 1) * LINE]
                        if lane and j0 + j == 0:
                            shift[8 : 8 + tall, :] = piece
                            piece = jnp.where(lanes < lane, shift[7 : 7 + tall, :], piece)
                            shift[0:8, :] = shift[tall : tall + 8, :]
                        if per_row == 1:
                            flat[phase : phase + tall, :] = piece
                        else:
                            flat[pl.ds(phase + j0 + j, tall, stride=per_row), :] = piece

                stage[side, 0:lines, :] = flat[0:lines, :].astype(jnp.bfloat16)
                written(block, side).start()

            @pl.when((step > start) & (step <= start + blocks))
            def _():
                written(step - start - 1, 1 - side).wait()

            if start + blocks == total:

                @pl.when(step == total - 1)
                def _():
                    written(blocks - 1, side).wait()

        @pl.when(step == total - 1)
        def _():
            if tail_rows:
                lanes = lax.broadcasted_iota(jnp.int32, (tail_rows, LINE), 1)
                rows_at = lax.broadcasted_iota(jnp.int32, (tail_rows, LINE), 0)
                final = jnp.broadcast_to(shift[7:8, :], (tail_rows, LINE))
                last[...] = jnp.where((rows_at == 0) & (lanes < lane), final, 0.0).astype(jnp.bfloat16)
                closing = pltpu.make_async_copy(
                    last, out.at[pl.ds(end_row, tail_rows), :], extra_sems.at[count_extra]
                )
                closing.start()
                closing.wait()
            for k in range(count_extra):
                extra_copy(k).wait()

    whole = [pl.BlockSpec(array.shape, lambda step: (0, 0)) for array in rolled]
    flops = sum(2 * tokens * entry[4] * tall * entry[2] * LINE for entry in plan)
    inputs = count_left + count_right + count_extra + len(carry_in) + len(targets)
    return pl.pallas_call(
        pinned(kernel, inputs, after),
        grid=(total,),
        in_specs=[left_spec(k) for k in range(count_left)]
        + whole
        + [pl.BlockSpec(array.shape, lambda step: (0, 0)) for array, _ in extras]
        + [pl.BlockSpec(array.shape, lambda step: (0, 0)) for array in carry_in]
        + [pl.BlockSpec(memory_space=pl.ANY)] * len(targets)
        + pins(after),
        out_specs=pl.BlockSpec(memory_space=pl.ANY),
        out_shape=jax.ShapeDtypeStruct((target_rows, LINE), jnp.bfloat16),
        scratch_shapes=[
            pltpu.VMEM((biggest + 16, LINE), jnp.float32),
            pltpu.VMEM((2, biggest, LINE), jnp.bfloat16),
            pltpu.VMEM((tall + 8, LINE), jnp.float32),
            pltpu.VMEM((max(tail_rows, 16), LINE), jnp.bfloat16),
            pltpu.SemaphoreType.DMA((2,)),
            pltpu.SemaphoreType.DMA((count_extra + 1,)),
        ],
        input_output_aliases={count_left + count_right + count_extra + len(carry_in): 0} if targets else {},
        compiler_params=pltpu.CompilerParams(vmem_limit_bytes=48 * 2**20),
        cost_estimate=pl.CostEstimate(flops=flops, bytes_accessed=total * biggest * LINE * 2, transcendentals=0),
        name="pack",
    )(*lefts, *rolled, *[array for array, _ in extras], *carry_in, *targets, *after)


def added(*parts):
    total = parts[0].astype(jnp.float32)
    for part in parts[1:]:
        total = total + part.astype(jnp.float32)
    return total.astype(jnp.bfloat16)


class Flow:
    def __init__(self, stages):
        self.stages = stages
        self.sends = next(stages)
        self.result = None

    def values(self):
        return [value for value, _, _ in self.sends] or [self.result]

    def go(self):
        arrived = [lax.ppermute(value, axis, pairs) for value, axis, pairs in self.sends]
        try:
            self.sends = self.stages.send(arrived)
        except StopIteration as stop:
            self.sends, self.result = [], stop.value
        return self


def reduce_stages(flat, batch, shift):
    z, y, x, c = (lax.axis_index(name) for name in GRID)
    length = PLANE + 32
    send = lax.dynamic_slice(flat, ((1 - c) * PLANE, 0), (length, LINE))
    (arrived,) = yield [(send, "c", SWAP)]
    chip = added(lax.dynamic_slice(flat, (c * PLANE, 0), (length, LINE)), arrived)

    def window(sy, sx, part):
        shard = sy * 4 + sx * 2 + part
        start = (shift + SHARD * shard) // 16 * 16
        return lax.dynamic_slice(chip, (start, 0), (WIN, LINE))

    away_0 = jnp.stack([window(1 - y, 0, 0), window(1 - y, 1, 0)])
    away_1 = jnp.stack([window(0, 1 - x, 1), window(1, 1 - x, 1)])
    home_0 = jnp.stack([window(y, 0, 0), window(y, 1, 0)])
    home_1 = jnp.stack([window(0, x, 1), window(1, x, 1)])
    got_0, got_1 = yield [(away_0, "y", SWAP), (away_1, "x", SWAP)]
    half_0, half_1 = added(home_0, got_0), added(home_1, got_1)
    pick = lambda value, at: lax.dynamic_index_in_dim(value, at, 0, keepdims=False)
    got_0, got_1 = yield [(pick(half_0, 1 - x), "x", SWAP), (pick(half_1, 1 - y), "y", SWAP)]
    columns = [added(pick(half_0, x), got_0), added(pick(half_1, y), got_1)]
    if batch == 0:
        hops = [((1, 0, 0), (2, 1, 1)), ((2, 0, 0), (3, 1, 1)), ((3, 0, 0), (0, 1, 1))]
    else:
        hops = [((1, 2, 0), (2, 3, 1)), ((0, 2, 0), (1, 3, 1)), ((3, 2, 0), (0, 3, 1))]
    columns = jnp.stack(columns)
    got = yield [(columns, ZC, zc_pairs(*hop)) for hop in hops]
    ends = added(columns, *got)
    mine = jnp.where(c == 0, ends[0], ends[1])
    other = jnp.where(c == 0, ends[1], ends[0])
    (handed,) = yield [(other, ZC, [(2 * k + k % 2, 2 * k + 1 - k % 2) for k in range(4)])]
    return jnp.where(c == z % 2, mine, handed)


PIECE = 400


def corner_stages(flat):
    z, y, x, c = (lax.axis_index(name) for name in GRID)
    length = 8 * PIECE
    second = (8 + SHARD) // 16 * 16
    take = lambda at: lax.dynamic_slice(flat, (at * second, 0), (length, LINE))
    (arrived,) = yield [(take(1 - c), "c", SWAP)]
    chip = added(take(c), arrived).reshape(2, 2, 2, PIECE, LINE)
    pick = lambda value, at: lax.dynamic_index_in_dim(value, at, 0, keepdims=False)
    got = yield [(pick(chip[0], 1 - x), "x", SWAP), (pick(chip[1], 1 - y), "y", SWAP)]
    halves = [added(pick(chip[0], x), got[0]), added(pick(chip[1], y), got[1])]
    got = yield [(pick(halves[0], 1 - y), "y", SWAP), (pick(halves[1], 1 - x), "x", SWAP)]
    pieces = jnp.stack([added(pick(halves[0], y), got[0]), added(pick(halves[1], x), got[1])])
    got = yield [(pieces, "z", [(k, 0)]) for k in (1, 2, 3)]
    pieces = added(pieces, *got)
    got = yield [(pieces[0], "y", [(1, 0)]), (pieces[1], "x", [(1, 0)])]
    halves = [jnp.stack([pieces[0], got[0]]), jnp.stack([pieces[1], got[1]])]
    got = yield [(halves[0], "x", [(1, 0)]), (halves[1], "y", [(1, 0)])]
    return jnp.stack([halves[0], got[0], halves[1], got[1]]).reshape(length, LINE)


CHUNK = 128
NT = (((1,), (1,)), ((), ()))
TN = (((0,), (0,)), ((), ()))
INNER = SSM_HEADS * SSM_DIM
PAIRS = SSM_HEADS // 2


def spread(rows_a, rows_b):
    length = rows_a.shape[1]
    tall = jnp.concatenate(
        [jnp.broadcast_to(rows_a, (SSM_DIM, length)), jnp.broadcast_to(rows_b, (SSM_DIM, length))], axis=0
    )
    return tall.T


CHANNELS = INNER + 2 * STATE
LANES = 2 * SSM_DIM
COLUMNS = CHANNELS // LANES


def conv_parts(ext, weight_ref, bias_ref, start_ref, first, rows):
    place = first + lax.broadcasted_iota(jnp.int32, (rows, 1), 0) - start_ref[...]
    windows = []
    total = bias_ref[...]
    for tap in range(CONV):
        reach = CONV - 1 - tap
        window = jnp.where(place >= reach, ext[8 - reach : 8 - reach + rows, :], 0.0)
        windows.append(window)
        total = total + window * weight_ref[tap : tap + 1, :]
    return place, windows, total


def conv_forward(xbc, rim, weight, bias, meta, start_column):
    rows = xbc.shape[0]

    def kernel(meta_ref, x_ref, rim_ref, weight_ref, bias_ref, start_ref, out_ref, ext):
        ext[0:8, :] = rim_ref[...]
        ext[8:, :] = x_ref[...]
        _, _, total = conv_parts(ext, weight_ref, bias_ref, start_ref, meta_ref[0], rows)
        out_ref[...] = total * jax.nn.sigmoid(total)

    lanes = lambda i, m: (0, i)
    return pl.pallas_call(
        kernel,
        grid_spec=pltpu.PrefetchScalarGridSpec(
            num_scalar_prefetch=1,
            grid=(COLUMNS,),
            in_specs=[
                pl.BlockSpec((rows, LANES), lanes),
                pl.BlockSpec((8, LANES), lanes),
                pl.BlockSpec((CONV, LANES), lanes),
                pl.BlockSpec((1, LANES), lanes),
                pl.BlockSpec((rows, 1), lambda i, m: (0, 0)),
            ],
            out_specs=pl.BlockSpec((rows, LANES), lanes),
            scratch_shapes=[pltpu.VMEM((rows + 8, LANES), jnp.float32)],
        ),
        out_shape=jax.ShapeDtypeStruct((rows, CHANNELS), jnp.float32),
        cost_estimate=pl.CostEstimate(flops=10**9, bytes_accessed=rows * CHANNELS * 8, transcendentals=0),
        name="conv",
    )(meta, xbc, rim, weight, bias, start_column)


def conv_backward(dx, db, dc, xbc, rim, weight, bias, meta, start_column, after=()):
    rows = xbc.shape[0]

    def kernel(meta_ref, dx_ref, db_ref, dc_ref, x_ref, rim_ref, weight_ref, bias_ref, start_ref,
               low_ref, tail_ref, edge_ref, small_ref, ext, upper):
        ext[0:8, :] = rim_ref[...]
        ext[8:, :] = x_ref[...]
        at = pl.program_id(0)
        arrived = jnp.where(at < PAIRS, dx_ref[...], jnp.where(at == PAIRS, db_ref[...], dc_ref[...]))
        place, windows, total = conv_parts(ext, weight_ref, bias_ref, start_ref, meta_ref[0], rows)
        gate = jax.nn.sigmoid(total)
        change = arrived * gate * (1.0 + total * (1.0 - gate))
        upper[0:8, :] = jnp.zeros((8, LANES), jnp.float32)
        upper[8 + rows :, :] = jnp.zeros((8, LANES), jnp.float32)
        main = jnp.zeros((rows, LANES), jnp.float32)
        edge = jnp.zeros((8, LANES), jnp.float32)
        small_ref[...] = jnp.zeros((8, LANES), jnp.float32)
        small_ref[CONV : CONV + 1, :] = jnp.sum(change, axis=0, keepdims=True)
        for tap in range(CONV):
            reach = CONV - 1 - tap
            small_ref[tap : tap + 1, :] = jnp.sum(change * windows[tap], axis=0, keepdims=True)
            upper[8 : 8 + rows, :] = jnp.where(place >= reach, change, 0.0) * weight_ref[tap : tap + 1, :]
            main = main + upper[8 + reach : 8 + reach + rows, :]
            edge = edge + upper[reach : reach + 8, :]
        low_ref[...] = main.astype(jnp.bfloat16)
        tail_ref[...] = main[rows - 16 :, :]
        edge_ref[...] = edge

    lanes = lambda i, m: (0, i)
    whole = lambda i, m: (0, 0)
    return pl.pallas_call(
        pinned(kernel, 9, after),
        grid_spec=pltpu.PrefetchScalarGridSpec(
            num_scalar_prefetch=1,
            grid=(COLUMNS,),
            in_specs=[
                pl.BlockSpec((rows, LANES), lambda i, m: (0, jnp.minimum(i, PAIRS - 1))),
                pl.BlockSpec((rows, STATE), whole),
                pl.BlockSpec((rows, STATE), whole),
                pl.BlockSpec((rows, LANES), lanes),
                pl.BlockSpec((8, LANES), lanes),
                pl.BlockSpec((CONV, LANES), lanes),
                pl.BlockSpec((1, LANES), lanes),
                pl.BlockSpec((rows, 1), whole),
            ] + pins(after),
            out_specs=[
                pl.BlockSpec((rows, LANES), lanes),
                pl.BlockSpec((16, LANES), lanes),
                pl.BlockSpec((8, LANES), lanes),
                pl.BlockSpec((8, LANES), lanes),
            ],
            scratch_shapes=[
                pltpu.VMEM((rows + 8, LANES), jnp.float32),
                pltpu.VMEM((rows + 16, LANES), jnp.float32),
            ],
        ),
        out_shape=[
            jax.ShapeDtypeStruct((rows, CHANNELS), jnp.bfloat16),
            jax.ShapeDtypeStruct((16, CHANNELS), jnp.float32),
            jax.ShapeDtypeStruct((8, CHANNELS), jnp.float32),
            jax.ShapeDtypeStruct((8, CHANNELS), jnp.float32),
        ],
        cost_estimate=pl.CostEstimate(flops=2 * 10**9, bytes_accessed=rows * CHANNELS * 10, transcendentals=0),
        name="conv_back",
    )(meta, dx, db, dc, xbc, rim, weight, bias, start_column, *after)


def weighted_state(left, left_block, values, weight_rows, after=()):
    rows = left.shape[0]

    def kernel(left_ref, value_ref, weight_ref, out_ref, turned):
        @pl.when(pl.program_id(0) == 0)
        def _():
            turned[...] = left_ref[...].T.astype(jnp.bfloat16)

        wide = spread(weight_ref[0, 0:1, :], weight_ref[0, 1:2, :])
        scaled = (value_ref[...] * wide).astype(jnp.bfloat16)
        out_ref[...] = jnp.dot(turned[...], scaled, preferred_element_type=jnp.float32)

    return pl.pallas_call(
        pinned(kernel, 3, after),
        grid=(PAIRS,),
        in_specs=[
            pl.BlockSpec((rows, STATE), lambda i: (0, left_block)),
            pl.BlockSpec((rows, 2 * SSM_DIM), lambda i: (0, i)),
            pl.BlockSpec((1, 2, rows), lambda i: (i, 0, 0)),
        ] + pins(after),
        out_specs=pl.BlockSpec((STATE, 2 * SSM_DIM), lambda i: (0, i)),
        out_shape=jax.ShapeDtypeStruct((STATE, INNER), jnp.float32),
        scratch_shapes=[pltpu.VMEM((STATE, rows), jnp.bfloat16)],
        cost_estimate=pl.CostEstimate(flops=2 * rows * STATE * INNER, bytes_accessed=rows * INNER * 4, transcendentals=0),
        name="state",
    )(left, values, weight_rows.reshape(PAIRS, 2, rows), *after)


def chunk_rows(k, meta_ref, cum_ref, start_ref):
    here = slice(k * CHUNK, (k + 1) * CHUNK)
    first = meta_ref[0] + k * CHUNK
    index = first + lax.broadcasted_iota(jnp.int32, (1, CHUNK), 1)
    entering = start_ref[0:1, here] < first
    ending = index >= meta_ref[1 + k]
    cums, entries, tails = [], [], []
    for e in range(2):
        cum = cum_ref[0, e : e + 1, here]
        cums.append(cum)
        entries.append(jnp.where(entering, jnp.exp(cum), 0.0))
        gap = jnp.where(ending, cum[:, CHUNK - 1 :] - cum, masked_score)
        tails.append(jnp.exp(gap))
    return cums, entries, tails


def ssm_forward(conv, cum, step, state_in, skip, meta, start_column, start_row):
    rows = conv.shape[0]
    chunks = rows // CHUNK

    def kernel(meta_ref, x_ref, b_ref, c_ref, cum_ref, step_ref, state_ref, skip_ref, col_ref, row_ref,
               y_ref, inner, hide, state, b_turned):
        @pl.when(pl.program_id(0) == 0)
        def _():
            for k in range(chunks):
                here = slice(k * CHUNK, (k + 1) * CHUNK)
                b_turned[:, here] = b_ref[here, :].T.astype(jnp.bfloat16)
                inner[k] = lax.dot_general(
                    c_ref[here, :], b_ref[here, :], NT, precision=highest, preferred_element_type=jnp.float32
                )
                t = lax.broadcasted_iota(jnp.int32, (CHUNK, CHUNK), 0)
                s = lax.broadcasted_iota(jnp.int32, (CHUNK, CHUNK), 1)
                shown = (s <= t) & (meta_ref[0] + k * CHUNK + s >= col_ref[here, :])
                hide[k] = jnp.where(shown, 0.0, masked_score)

        low_lane = lax.broadcasted_iota(jnp.int32, (CHUNK, 2 * SSM_DIM), 1) < SSM_DIM
        state[...] = state_ref[...]
        for k in range(chunks):
            here = slice(k * CHUNK, (k + 1) * CHUNK)
            cums, entries, tails = chunk_rows(k, meta_ref, cum_ref, row_ref)
            x_now = x_ref[here, :]
            x_low = x_now.astype(jnp.bfloat16)
            entry = spread(*entries)
            weight = spread(*[tails[e] * step_ref[0, e : e + 1, here] for e in range(2)])
            parts = []
            for e in range(2):
                across = jnp.broadcast_to(cums[e], (CHUNK, CHUNK))
                decays = jnp.exp(across.T - across + hide[k])
                mix = (inner[k] * decays * step_ref[0, e : e + 1, here]).astype(jnp.bfloat16)
                parts.append(jnp.dot(mix, x_low, preferred_element_type=jnp.float32))
            carried = jnp.dot(
                c_ref[here, :].astype(jnp.bfloat16), state[...].astype(jnp.bfloat16),
                preferred_element_type=jnp.float32,
            )
            y_ref[here, :] = jnp.where(low_lane, parts[0], parts[1]) + entry * carried + skip_ref[...] * x_now
            fresh = jnp.dot(
                b_turned[:, here], (x_now * weight).astype(jnp.bfloat16), preferred_element_type=jnp.float32
            )
            state[...] = entry[CHUNK - 1 :, :] * state[...] + fresh

    whole = lambda i, m: (0, 0)
    lanes = lambda i, m: (0, i)
    return pl.pallas_call(
        kernel,
        grid_spec=pltpu.PrefetchScalarGridSpec(
            num_scalar_prefetch=1,
            grid=(PAIRS,),
            in_specs=[
                pl.BlockSpec((rows, 2 * SSM_DIM), lanes),
                pl.BlockSpec((rows, STATE), lambda i, m: (0, PAIRS)),
                pl.BlockSpec((rows, STATE), lambda i, m: (0, PAIRS + 1)),
                pl.BlockSpec((1, 2, rows), lambda i, m: (i, 0, 0)),
                pl.BlockSpec((1, 2, rows), lambda i, m: (i, 0, 0)),
                pl.BlockSpec((STATE, 2 * SSM_DIM), lanes),
                pl.BlockSpec((1, 2 * SSM_DIM), lanes),
                pl.BlockSpec((rows, 1), whole),
                pl.BlockSpec((8, rows), whole),
            ],
            out_specs=pl.BlockSpec((rows, 2 * SSM_DIM), lanes),
            scratch_shapes=[
                pltpu.VMEM((chunks, CHUNK, CHUNK), jnp.float32),
                pltpu.VMEM((chunks, CHUNK, CHUNK), jnp.float32),
                pltpu.VMEM((STATE, 2 * SSM_DIM), jnp.float32),
                pltpu.VMEM((STATE, rows), jnp.bfloat16),
            ],
        ),
        out_shape=jax.ShapeDtypeStruct((rows, INNER), jnp.float32),
        compiler_params=pltpu.CompilerParams(vmem_limit_bytes=40 * 2**20),
        cost_estimate=pl.CostEstimate(flops=10**9, bytes_accessed=rows * INNER * 8, transcendentals=2**21),
        name="ssm",
    )(meta, conv, conv, conv, cum.reshape(PAIRS, 2, rows), step.reshape(PAIRS, 2, rows), state_in, skip,
      start_column, start_row)


def ssm_backward(conv, dy, cum, step, state_in, state_grad, skip, meta, start_row, after=()):
    rows = conv.shape[0]
    chunks = rows // CHUNK

    def kernel(meta_ref, x_ref, dy_ref, b_ref, c_ref, cum_ref, step_ref, state_ref, grad_ref, skip_ref, row_ref,
               dx_ref, db_ref, dc_ref, small_ref, inner, hide, inner_grad, states, flow,
               b_turned, c_turned):
        low = lambda v: v.astype(jnp.bfloat16)
        dot = lambda p, q, dims=(((1,), (0,)), ((), ())): lax.dot_general(
            p, q, dims, preferred_element_type=jnp.float32
        )
        exact = lambda p, q, dims=(((1,), (0,)), ((), ())): lax.dot_general(
            p, q, dims, precision=highest, preferred_element_type=jnp.float32
        )
        s = lax.broadcasted_iota(jnp.int32, (CHUNK, CHUNK), 0)
        t = lax.broadcasted_iota(jnp.int32, (CHUNK, CHUNK), 1)

        @pl.when(pl.program_id(0) == 0)
        def _():
            db_ref[...] = jnp.zeros(db_ref.shape, jnp.float32)
            dc_ref[...] = jnp.zeros(dc_ref.shape, jnp.float32)
            inner_grad[...] = jnp.zeros(inner_grad.shape, jnp.float32)
            for k in range(chunks):
                here = slice(k * CHUNK, (k + 1) * CHUNK)
                b_turned[:, here] = low(b_ref[here, :].T)
                c_turned[:, here] = low(c_ref[here, :].T)
                inner[k] = exact(b_ref[here, :], c_ref[here, :], NT)
                shown = (s <= t) & (meta_ref[0] + k * CHUNK + s >= row_ref[0:1, here])
                hide[k] = jnp.where(shown, 0.0, masked_score)

        before = (s < t).astype(jnp.float32)
        until = low((s >= t).astype(jnp.float32))
        low_lane = t < SSM_DIM
        pick_row = lax.broadcasted_iota(jnp.int32, (8, 2 * SSM_DIM), 0)
        pick_lane = lax.broadcasted_iota(jnp.int32, (8, 2 * SSM_DIM), 1) // SSM_DIM
        pick = low((pick_row == pick_lane).astype(jnp.float32))
        spreads = []
        states[0] = state_ref[...]
        for k in range(chunks):
            here = slice(k * CHUNK, (k + 1) * CHUNK)
            cums, entries, tails = chunk_rows(k, meta_ref, cum_ref, row_ref)
            entry, tail = spread(*entries), spread(*tails)
            steps = spread(step_ref[0, 0:1, here], step_ref[0, 1:2, here])
            spreads.append((cums, entry, tail, steps))
            if k < chunks - 1:
                fresh = dot(b_turned[:, here], low(x_ref[here, :] * steps * tail))
                states[k + 1] = entry[CHUNK - 1 :, :] * states[k] + fresh
        flow[...] = grad_ref[...]
        skip_sum = jnp.zeros((1, 2 * SSM_DIM), jnp.float32)
        for k in reversed(range(chunks)):
            here = slice(k * CHUNK, (k + 1) * CHUNK)
            cums, entry, tail, steps = spreads[k]
            x_now, dy_now = x_ref[here, :], dy_ref[here, :]
            b_low, c_low = low(b_ref[here, :]), low(c_ref[here, :])
            scaled = x_now * steps
            dy_low = low(dy_now)
            flow_low, state_low = low(flow[...]), low(states[k])
            mixed, within = [], []
            for e in range(2):
                across = jnp.broadcast_to(cums[e], (CHUNK, CHUNK))
                decays = jnp.exp(across - across.T + hide[k])
                own = low(jnp.where(low_lane == (e == 0), scaled, 0.0))
                reach = decays * dot(own, dy_low, NT)
                inner_grad[k] += reach
                sums = dot(low(inner[k] * reach), until)
                within.append(jnp.sum(sums * before, axis=0, keepdims=True))
                mixed.append(dot(low(inner[k] * decays), dy_low))
            back = tail * dot(b_low, flow_low)
            dxs = jnp.where(low_lane, mixed[0], mixed[1]) + back
            db_ref[here, :] += dot(low(scaled * tail), flow_low, NT)
            entered = low(dy_now * entry)
            dc_ref[here, :] += dot(entered, state_low, NT)
            brought = dy_now * entry * dot(c_low, state_low)
            ends = dot(pick, low(brought), NT)
            begins = dot(pick, low(scaled * back), NT)
            direct = dot(pick, low(x_now * dxs), NT)
            through = jnp.sum(flow[...] * states[k], axis=0, keepdims=True) * entry[CHUNK - 1 :, :]
            log_grad = exact(ends, until.astype(jnp.float32)) + exact(begins, before)
            for e in range(2):
                lanes = slice(e * SSM_DIM, (e + 1) * SSM_DIM)
                kept = jnp.sum(through[:, lanes], axis=1, keepdims=True)
                small_ref[0, e : e + 1, here] = direct[e : e + 1, :]
                small_ref[0, 2 + e : 3 + e, here] = log_grad[e : e + 1, :] + within[e] + kept
            dx_ref[here, :] = dxs * steps + skip_ref[...] * dy_now
            skip_sum += jnp.sum(x_now * dy_now, axis=0, keepdims=True)
            flow[...] = entry[CHUNK - 1 :, :] * flow[...] + dot(c_turned[:, here], entered)
        small_ref[0, 4:8, :] = jnp.zeros((4, rows), jnp.float32)
        small_ref[0, 4:5, 0 : 2 * SSM_DIM] = skip_sum

        @pl.when(pl.program_id(0) == PAIRS - 1)
        def _():
            for k in range(chunks):
                here = slice(k * CHUNK, (k + 1) * CHUNK)
                grads = low(inner_grad[k])
                db_ref[here, :] += dot(grads, low(c_ref[here, :]))
                dc_ref[here, :] += dot(grads, low(b_ref[here, :]), TN)

    whole = lambda i, m: (0, 0)
    lanes = lambda i, m: (0, i)
    pair = lambda i, m: (i, 0, 0)
    return pl.pallas_call(
        pinned(kernel, 11, after),
        grid_spec=pltpu.PrefetchScalarGridSpec(
            num_scalar_prefetch=1,
            grid=(PAIRS,),
            in_specs=[
                pl.BlockSpec((rows, 2 * SSM_DIM), lanes),
                pl.BlockSpec((rows, 2 * SSM_DIM), lanes),
                pl.BlockSpec((rows, STATE), lambda i, m: (0, PAIRS)),
                pl.BlockSpec((rows, STATE), lambda i, m: (0, PAIRS + 1)),
                pl.BlockSpec((1, 2, rows), pair),
                pl.BlockSpec((1, 2, rows), pair),
                pl.BlockSpec((STATE, 2 * SSM_DIM), lanes),
                pl.BlockSpec((STATE, 2 * SSM_DIM), lanes),
                pl.BlockSpec((1, 2 * SSM_DIM), lanes),
                pl.BlockSpec((8, rows), whole),
            ] + pins(after),
            out_specs=[
                pl.BlockSpec((rows, 2 * SSM_DIM), lanes),
                pl.BlockSpec((rows, STATE), whole),
                pl.BlockSpec((rows, STATE), whole),
                pl.BlockSpec((1, 8, rows), pair),
            ],
            scratch_shapes=[
                pltpu.VMEM((chunks, CHUNK, CHUNK), jnp.float32),
                pltpu.VMEM((chunks, CHUNK, CHUNK), jnp.float32),
                pltpu.VMEM((chunks, CHUNK, CHUNK), jnp.float32),
                pltpu.VMEM((chunks, STATE, 2 * SSM_DIM), jnp.float32),
                pltpu.VMEM((STATE, 2 * SSM_DIM), jnp.float32),
                pltpu.VMEM((STATE, rows), jnp.bfloat16),
                pltpu.VMEM((STATE, rows), jnp.bfloat16),
            ],
        ),
        out_shape=[
            jax.ShapeDtypeStruct((rows, INNER), jnp.float32),
            jax.ShapeDtypeStruct((rows, STATE), jnp.float32),
            jax.ShapeDtypeStruct((rows, STATE), jnp.float32),
            jax.ShapeDtypeStruct((PAIRS, 8, rows), jnp.float32),
        ],
        compiler_params=pltpu.CompilerParams(vmem_limit_bytes=40 * 2**20),
        cost_estimate=pl.CostEstimate(flops=3 * 10**9, bytes_accessed=rows * INNER * 12, transcendentals=2**21),
        name="ssm_back",
    )(meta, conv, dy, conv, conv, cum.reshape(PAIRS, 2, rows), step.reshape(PAIRS, 2, rows), state_in, state_grad,
      skip, start_row, *after)


def chain_states(earlier, later):
    return (earlier[0] * later[0], earlier[1] * later[0] + later[1])


def scan_states(carry, state, span, fast, backward):
    wide = jnp.repeat(carry, SSM_DIM)[None, :]
    if not fast:
        ident = (jnp.ones_like(wide), jnp.zeros_like(state))
        return (carried_in if backward else prefix)((wide, state), span, chain_states, ident)[1]
    flow = Flow(scan_stages(carry, state, backward))
    while flow.sends:
        flow.go()
    return flow.result


def scan_stages(carry, state, backward):
    total = (jnp.repeat(carry, SSM_DIM)[None, :], state)
    start = None
    for name in ("c", "x", "y"):
        place = lax.axis_index(name)
        packed = jnp.concatenate([total[1], jnp.broadcast_to(total[0], (16, INNER))], axis=0)
        (packed,) = yield [(packed.astype(jnp.bfloat16), name, SWAP)]
        packed = packed.astype(jnp.float32)
        other = (packed[STATE : STATE + 1], packed[:STATE])
        leads = place == (0 if backward else 1)
        seen = (jnp.where(leads, other[0], 1.0), jnp.where(leads, other[1], 0.0))
        start = seen if start is None else chain_states(seen, start)
        if name != "y":
            forward = chain_states(other, total)
            reverse = chain_states(total, other)
            total = jax.tree.map(lambda p, q: jnp.where(leads, p, q), forward, reverse)
    return start[1]


KEYS = 512
PAIR = 2 * HEAD_DIM


def attention_forward(q_wide, kv, meta, starts, after=()):
    rows = q_wide.shape[1]
    blocks = kv.shape[0]
    ratio = HEADS_Q // HEADS_KV
    wide = min(512, rows)

    def kernel(meta_ref, q_ref, kv_ref, start_ref, o_ref, log_ref, top, total):
        b = pl.program_id(1)

        @pl.when(b == 0)
        def _():
            top[...] = jnp.full(top.shape, masked_score, jnp.float32)
            total[...] = jnp.zeros(total.shape, jnp.float32)
            o_ref[...] = jnp.zeros(o_ref.shape, jnp.float32)

        def block(partial):
            pair = kv_ref[0, 0]
            turned = pair.T[HEAD_DIM:, :]
            for h in range(ratio):
                for r in range(0, rows, wide):
                    here = slice(r, r + wide)
                    scores = lax.dot_general(pair, q_ref[h, here, :], NT, preferred_element_type=jnp.float32)
                    if partial:
                        keys = b * KEYS + lax.broadcasted_iota(jnp.int32, scores.shape, 0)
                        mine = meta_ref[2] + r + lax.broadcasted_iota(jnp.int32, scores.shape, 1)
                        visible = (keys >= start_ref[0:1, here]) & (keys <= mine)
                        scores = jnp.where(visible, scores, masked_score)
                    before = top[h, 0:1, here]
                    peak = jnp.maximum(before, jnp.max(scores, axis=0, keepdims=True))
                    part = jnp.exp(scores - peak)
                    if partial:
                        part = jnp.where(visible, part, 0.0)
                    fade = jnp.exp(before - peak)
                    top[h, 0:1, here] = peak
                    total[h, 0:1, here] = total[h, 0:1, here] * fade + jnp.sum(part, axis=0, keepdims=True)
                    o_ref[h, :, here] = o_ref[h, :, here] * fade + jnp.dot(
                        turned, part.astype(jnp.bfloat16), preferred_element_type=jnp.float32
                    )

        needed = (b >= meta_ref[0]) & (b < meta_ref[1])
        partial = ((b + 1) * KEYS > meta_ref[2]) | (b * KEYS < meta_ref[3])

        @pl.when(needed & partial)
        def _():
            block(True)

        @pl.when(needed & jnp.logical_not(partial))
        def _():
            block(False)

        @pl.when(b == blocks - 1)
        def _():
            for h in range(ratio):
                sums = total[h, 0:1, :]
                o_ref[h] = o_ref[h] / sums
                log_ref[h] = jnp.broadcast_to(top[h, 0:1, :] + jnp.log(sums), (8, rows))

    heads = lambda g, b, m: (g, 0, 0)
    return pl.pallas_call(
        pinned(kernel, 4, after),
        grid_spec=pltpu.PrefetchScalarGridSpec(
            num_scalar_prefetch=1,
            grid=(HEADS_KV, blocks),
            in_specs=[
                pl.BlockSpec((ratio, rows, PAIR), heads),
                pl.BlockSpec((1, 1, KEYS, PAIR), lambda g, b, m: (b, g, 0, 0)),
                pl.BlockSpec((8, rows), lambda g, b, m: (0, 0)),
            ] + pins(after),
            out_specs=[
                pl.BlockSpec((ratio, HEAD_DIM, rows), heads),
                pl.BlockSpec((ratio, 8, rows), heads),
            ],
            scratch_shapes=[
                pltpu.VMEM((ratio, 8, rows), jnp.float32),
                pltpu.VMEM((ratio, 8, rows), jnp.float32),
            ],
        ),
        out_shape=[
            jax.ShapeDtypeStruct((HEADS_Q, HEAD_DIM, rows), jnp.float32),
            jax.ShapeDtypeStruct((HEADS_Q, 8, rows), jnp.float32),
        ],
        compiler_params=pltpu.CompilerParams(vmem_limit_bytes=48 * 2**20),
        cost_estimate=pl.CostEstimate(flops=2 * 10**10, bytes_accessed=2**23, transcendentals=2**23),
        name="attend",
    )(meta, q_wide, kv, starts, *after)


def attention_backward(q_wide, g_wide, kv, logs, mixed, meta, starts, group, after=()):
    rows = q_wide.shape[1]
    blocks = kv.shape[0]
    ratio = HEADS_Q // HEADS_KV
    wide = min(512, rows)

    def kernel(meta_ref, q_ref, g_ref, kv_ref, log_ref, o_ref, start_ref, dkv_ref, dq_ref, delta, sums):
        b = pl.program_id(0)

        @pl.when(b == 0)
        def _():
            dq_ref[...] = jnp.zeros(dq_ref.shape, jnp.float32)
            for h in range(ratio):
                both = g_ref[h].astype(jnp.float32).T[HEAD_DIM:, :] * o_ref[h]
                delta[h] = jnp.broadcast_to(jnp.sum(both, axis=0, keepdims=True), (8, rows))

        def block(partial):
            pair = kv_ref[0, 0]
            turned = pair.T[:HEAD_DIM, :]
            for h in range(ratio):
                for r in range(0, rows, wide):
                    here = slice(r, r + wide)
                    q_now = q_ref[h, here, :]
                    g_now = g_ref[h, here, :]
                    scores = lax.dot_general(pair, q_now, NT, preferred_element_type=jnp.float32)
                    probs = jnp.exp(scores - log_ref[h, 0:1, here])
                    if partial:
                        keys = b * KEYS + lax.broadcasted_iota(jnp.int32, scores.shape, 0)
                        mine = meta_ref[2] + r + lax.broadcasted_iota(jnp.int32, scores.shape, 1)
                        visible = (keys >= start_ref[0:1, here]) & (keys <= mine)
                        probs = jnp.where(visible, probs, 0.0)
                    grads = lax.dot_general(pair, g_now, NT, preferred_element_type=jnp.float32)
                    low_grads = (probs * (grads - delta[h, 0:1, here])).astype(jnp.bfloat16)
                    change = jnp.dot(
                        probs.astype(jnp.bfloat16), g_now, preferred_element_type=jnp.float32
                    ) + jnp.dot(low_grads, q_now, preferred_element_type=jnp.float32)
                    if h == 0 and r == 0:
                        sums[...] = change
                    else:
                        sums[...] += change
                    dq_ref[h, :, here] += jnp.dot(turned, low_grads, preferred_element_type=jnp.float32)
            dkv_ref[0, 0] = sums[...].astype(jnp.bfloat16)

        needed = (b >= meta_ref[0]) & (b < meta_ref[1])
        partial = ((b + 1) * KEYS > meta_ref[2]) | (b * KEYS < meta_ref[3])

        @pl.when(needed & partial)
        def _():
            block(True)

        @pl.when(needed & jnp.logical_not(partial))
        def _():
            block(False)

        @pl.when(jnp.logical_not(needed))
        def _():
            dkv_ref[0, 0] = jnp.zeros((KEYS, PAIR), jnp.bfloat16)

    heads = lambda b, m: (group, 0, 0)
    return pl.pallas_call(
        pinned(kernel, 7, after),
        grid_spec=pltpu.PrefetchScalarGridSpec(
            num_scalar_prefetch=1,
            grid=(blocks,),
            in_specs=[
                pl.BlockSpec((ratio, rows, PAIR), heads),
                pl.BlockSpec((ratio, rows, PAIR), heads),
                pl.BlockSpec((1, 1, KEYS, PAIR), lambda b, m: (b, group, 0, 0)),
                pl.BlockSpec((ratio, 8, rows), heads),
                pl.BlockSpec((ratio, HEAD_DIM, rows), heads),
                pl.BlockSpec((8, rows), lambda b, m: (0, 0)),
            ] + pins(after),
            out_specs=[
                pl.BlockSpec((1, 1, KEYS, PAIR), lambda b, m: (b, 0, 0, 0)),
                pl.BlockSpec((ratio, HEAD_DIM, rows), lambda b, m: (0, 0, 0)),
            ],
            scratch_shapes=[
                pltpu.VMEM((ratio, 8, rows), jnp.float32),
                pltpu.VMEM((KEYS, PAIR), jnp.float32),
            ],
        ),
        out_shape=[
            jax.ShapeDtypeStruct((blocks, 1, KEYS, PAIR), jnp.bfloat16),
            jax.ShapeDtypeStruct((ratio, HEAD_DIM, rows), jnp.float32),
        ],
        compiler_params=pltpu.CompilerParams(vmem_limit_bytes=48 * 2**20),
        cost_estimate=pl.CostEstimate(flops=2 * 10**10, bytes_accessed=2**23, transcendentals=2**23),
        name="attend_back",
    )(meta, q_wide, g_wide, kv, logs, mixed, starts, *after)


def ordered(place, own, other, axis):
    first = jnp.where(place == 0, own, other)
    second = jnp.where(place == 0, other, own)
    return jnp.stack([first, second], axis=axis)


def gather_span(value, span, fast):
    if not fast:
        return lax.all_gather(value, span)
    _, y, x, c = (lax.axis_index(name) for name in GRID)
    two = ordered(x, value, lax.ppermute(value, "x", SWAP), 0)
    four = ordered(y, two, lax.ppermute(two, "y", SWAP), 0)
    eight = ordered(c, four, lax.ppermute(four, "c", SWAP), 2)
    return eight.reshape((8,) + value.shape)


def scatter_span(value, span, fast):
    if not fast:
        return lax.psum_scatter(value, span, scatter_dimension=0).astype(jnp.float32)
    flow = Flow(scatter_stages(value))
    while flow.sends:
        flow.go()
    return flow.result


def scatter_stages(value):
    _, y, x, c = (lax.axis_index(name) for name in GRID)
    value = value.reshape((2, 2, 2) + value.shape[1:])
    for name, place, axis in (("c", c, 2), ("y", y, 0), ("x", x, 0)):
        send = lax.dynamic_index_in_dim(value, 1 - place, axis, keepdims=False)
        (arrived,) = yield [(send, name, SWAP)]
        keep = lax.dynamic_index_in_dim(value, place, axis, keepdims=False)
        value = keep.astype(jnp.float32) + arrived.astype(jnp.float32)
        if name != "x":
            value = value.astype(jnp.bfloat16)
    return value


def sum_all(value, axes, fast):
    if not fast:
        return lax.psum(value, axes)
    for name in GRID[1:]:
        value = value + lax.ppermute(value, name, SWAP)
    for pairs in ([(0, 1), (1, 0), (2, 3), (3, 2)], [(0, 2), (2, 0), (1, 3), (3, 1)]):
        value = value + lax.ppermute(value, "z", pairs)
    return value


def offsets_of():
    places, at = {}, 0
    for name_key, extent in layout():
        places[name_key] = (at, extent)
        at += math.prod(extent)
    return places


def early_weights(params):
    places = offsets_of()
    buffers, (slots, all_slots), where = gather_lines(params)
    names = (W_QUERY, W_KEY, W_VALUE, W_ATTN_OUT, W_GATE_SSM, W_X_SSM, W_B_C)
    misc_at = places[W_STEP][0]
    first = unpack_lines(
        buffers[:16], slots, where, [flat_segment(name_key) for name_key in names] + [(0, 16, LINE), (misc_at, 288, LINE)]
    )
    weights = dict(zip(names, first))
    weights[NORM_ATTN] = first[-2].reshape(-1)[:D]
    misc = first[-1].reshape(-1)
    for name_key in (W_STEP,) + small_names[1:-1]:
        at, extent = places[name_key]
        weights[name_key] = misc[at - misc_at : at - misc_at + math.prod(extent)].reshape(extent)
    return weights, (buffers, all_slots, where)


def flat_segment(name_key):
    at, extent = offsets_of()[name_key]
    return (at, extent[0], extent[1])


def late_weights(held, after):
    buffers, slots, where = held
    names = (W_SSM_OUT, W_GATE, W_UP_PROJ, W_DOWN)
    norm_at = offsets_of()[NORM_FFN][0]
    second = unpack_lines(
        buffers, slots, where, [flat_segment(name_key) for name_key in names] + [(norm_at, 16, LINE)], after
    )
    weights = dict(zip(names, second))
    weights[NORM_FFN] = second[-1].reshape(-1)[norm_at % LINE : norm_at % LINE + D]
    return weights


def pack_late(gate, up, down, ssm_low, grad_branch, grad_norm_ffn, after):
    places = offsets_of()
    out_at = places[W_SSM_OUT][0]
    lane = places[W_GATE][0] % LINE
    boundary = 2 * PLANE * LINE
    tail_from = (boundary - out_at) // D
    tail = matmul_left_t(ssm_low[:, tail_from:], grad_branch).reshape(-1)
    tail = tail[boundary - out_at - tail_from * D :]
    head = jnp.concatenate([jnp.zeros((14 * LINE,), jnp.float32), tail, grad_norm_ffn])
    head_rows = head.shape[0] // LINE
    carry = jnp.zeros((8, LINE), jnp.float32).at[7, :lane].set(head[head_rows * LINE :])
    head = head[: head_rows * LINE].reshape(head_rows, LINE).astype(jnp.bfloat16)
    return pack_lines(
        None, 2 * PLANE + 32, head_rows, [gate, up, down], lane, 0, [(head, 0)], carry, 48, after
    )


def pack_out(ssm_low, grad_branch, after):
    out_at = offsets_of()[W_SSM_OUT][0]
    first_row = (8 + out_at // LINE) // 16 * 16
    rows = first_row + SSM_HEADS * SSM_DIM * D // LINE
    return pack_lines(
        None, rows, first_row, [(ssm_low, grad_branch)], out_at % LINE, (8 + out_at // LINE) % 8, [],
        jnp.zeros((8, LINE), jnp.float32), 0, after,
    )


def pack_ssm(target, segments, small, ssm_low, grad_branch, after):
    places = offsets_of()
    misc = [small[name_key].reshape(-1) for name_key in (W_STEP,) + small_names[1:-1]]
    count = sum(part.shape[0] for part in misc)
    misc_rows = (count // LINE + 16) // 16 * 16
    opening = matmul_left_t(ssm_low[:, :16], grad_branch).reshape(-1)
    misc = jnp.concatenate(misc + [opening[: misc_rows * LINE - count]])
    misc = misc.reshape(misc_rows, LINE).astype(jnp.bfloat16)
    first_row = 8 + places[W_ATTN_OUT][0] // LINE
    return pack_lines(
        target, target.shape[0], first_row, segments, 0, 0, [(misc, 8 + places[W_STEP][0] // LINE)], None, 0, after
    )


def pack_qkv(segments, attended, grad_branch, after):
    places = offsets_of()
    out_row = 8 + places[W_ATTN_OUT][0] // LINE
    rows = (8 + SHARD) // 16 * 16 + 8 * PIECE
    closing = matmul_left_t(attended[:, :16], grad_branch).reshape(-1, LINE)
    closing = closing[: rows - out_row].astype(jnp.bfloat16)
    return pack_lines(
        None, rows, 16, segments, 0, 0, [(jnp.zeros((16, LINE), jnp.bfloat16), 0), (closing, out_row)], None, 0, after
    )


def own_lines(early, late, corner, grad_norm_attn):
    z, y, x, c = (lax.axis_index(name) for name in GRID)
    place = 4 * y + 2 * x + c
    shard = SHARD * place
    start = jnp.where(z < 2, (8 + shard) % 16, (14 + shard) % 16)
    lines = jnp.where(z < 2, early, late)
    lines = jnp.where((z == 0) & (place < 2), corner[:WIN], lines)
    lines = lax.dynamic_slice(lines, (start, 0), (SHARD, LINE)).astype(jnp.float32)
    norms = jnp.where((z == 0) & (place == 0), grad_norm_attn.reshape(-1, LINE), lines[: D // LINE])
    return jnp.concatenate([norms, lines[D // LINE :]]).reshape(-1)


def body(span, group, fast, tokens, params, cotangent, offsets):
    rows_dev = tokens.shape[0]
    group_rows = rows_dev * lax.axis_size(span)
    all_rows = group_rows * lax.axis_size(group)
    ssm_inner = SSM_HEADS * SSM_DIM
    score_scale = HEAD_DIM ** (-0.5)
    bounds = offsets[0]
    my_start = lax.axis_index(span) * rows_dev
    row_index = my_start + jnp.arange(rows_dev, dtype=jnp.int32)
    seq_id, positions = sequence_info(row_index, bounds)
    first_start = row_index[0] - positions[0]
    last_row = my_start + rows_dev - 1
    cosine, sine = rotary_tables(positions)
    if fast:
        weights, held = early_weights(params)
    else:
        weights = unpack(lax.all_gather(params, group + span, axis=0, tiled=True))
    small_f32 = {name_key: weights[name_key].astype(jnp.float32) for name_key in small_names[:-1]}
    x_rows = tokens.astype(jnp.float32)
    normed_one, norm_one_back = jax.vjp(rms_norm, x_rows, small_f32[NORM_ATTN])
    hidden = normed_one.astype(jnp.bfloat16)
    query = matmul(hidden, weights[W_QUERY])
    key_raw = matmul(hidden, weights[W_KEY])
    value_low = matmul(hidden, weights[W_VALUE]).astype(jnp.bfloat16)
    q_rot = rotate(query, cosine, sine, HEADS_Q).astype(jnp.bfloat16)
    k_rot = rotate(key_raw, cosine, sine, HEADS_KV).astype(jnp.bfloat16)
    k_heads = k_rot.reshape(rows_dev, HEADS_KV, HEAD_DIM)
    v_heads = value_low.reshape(rows_dev, HEADS_KV, HEAD_DIM)
    kv_mine = jnp.concatenate([k_heads, v_heads], axis=2).transpose(1, 0, 2)
    key_blocks = gather_span(kv_mine.reshape(HEADS_KV, rows_dev, PAIR), span, fast)
    if rows_dev != KEYS:
        key_blocks = key_blocks.transpose(1, 0, 2, 3).reshape(HEADS_KV, -1, KEYS, PAIR).transpose(1, 0, 2, 3)
    row_starts = row_index - positions
    meta = jnp.stack(
        [first_start // KEYS, last_row // KEYS + 1, my_start, row_starts[rows_dev - 1]]
    ).astype(jnp.int32)
    q_low = (q_rot * jnp.bfloat16(score_scale)).reshape(rows_dev, HEADS_Q, HEAD_DIM).transpose(1, 0, 2)
    q_wide = jnp.pad(q_low, ((0, 0), (0, 0), (0, HEAD_DIM)))
    start_row = jnp.broadcast_to(row_starts[None, :], (8, rows_dev))
    mixed, logs = attention_forward(q_wide, key_blocks, meta, start_row)
    attended = mixed.astype(jnp.bfloat16).reshape(HEADS_Q * HEAD_DIM, rows_dev).T
    attn_out = matmul(attended, weights[W_ATTN_OUT])
    gate_ssm = matmul(hidden, weights[W_GATE_SSM])
    xbc = jnp.concatenate(
        [matmul(hidden, weights[W_X_SSM]), matmul(hidden, weights[W_B_C])], axis=1
    )
    step_raw = matmul(hidden, weights[W_STEP])
    rim_rows = passed_along(xbc[rows_dev - 8 :], span, 1)
    ssm_meta = jnp.concatenate([my_start[None], row_starts[CHUNK - 1 :: CHUNK]]).astype(jnp.int32)
    conv_bias = small_f32[CONV_BIAS][None, :]
    conv_values = conv_forward(xbc, rim_rows, small_f32[CONV_WEIGHT], conv_bias, ssm_meta, row_starts[:, None])
    step_in = step_raw.T + small_f32[STEP_BIAS][:, None]
    step_rows = jax.nn.softplus(step_in)
    decay = -jnp.exp(small_f32[DECAY_LOG])
    logs_step = step_rows * decay[:, None]
    order = jnp.arange(rows_dev)
    upto = (order[:, None] <= order[None, :]).astype(jnp.float32)
    cumul = jnp.dot(logs_step, upto, precision=highest)
    chunk_cum = jnp.dot(
        logs_step.reshape(-1, CHUNK), upto[:CHUNK, :CHUNK], precision=highest
    ).reshape(SSM_HEADS, rows_dev)
    went_on = row_starts < my_start
    entry_rows = jnp.where(went_on[None, :], jnp.exp(cumul), 0.0)
    in_last = row_index >= row_starts[rows_dev - 1]
    tail_rows = jnp.exp(jnp.where(in_last[None, :], cumul[:, -1:] - cumul, masked_score))
    carry_all = entry_rows[:, -1]
    local_state = weighted_state(conv_values, PAIRS, conv_values, tail_rows * step_rows)
    state_in = scan_states(carry_all, local_state, span, fast, False)
    skip_wide = jnp.repeat(small_f32[SKIP_GAIN], SSM_DIM)[None, :]
    ssm_y = ssm_forward(
        conv_values, chunk_cum, step_rows, state_in, skip_wide, ssm_meta, row_starts[:, None], start_row
    )
    normed_ssm, gnorm_back = jax.vjp(gated_norm, ssm_y, gate_ssm, small_f32[NORM_SSM])
    ssm_low = normed_ssm.astype(jnp.bfloat16)
    if fast:
        weights.update(late_weights(held, [mixed]))
    small_f32[NORM_FFN] = weights[NORM_FFN].astype(jnp.float32)
    ssm_out = matmul(ssm_low, weights[W_SSM_OUT])
    middle = x_rows + attn_out + ssm_out
    normed_two, norm_two_back = jax.vjp(rms_norm, middle, small_f32[NORM_FFN])
    hidden_two = normed_two.astype(jnp.bfloat16)
    gate_ffn = matmul(hidden_two, weights[W_GATE])
    upper = matmul(hidden_two, weights[W_UP_PROJ])
    activation_f32, swiglu_back = jax.vjp(swiglu, gate_ffn, upper)
    activation = activation_f32.astype(jnp.bfloat16)
    ffn_out = matmul(activation, weights[W_DOWN])
    result = middle + ffn_out
    squares = jnp.stack(
        [
            jnp.sum(result * result),
            jnp.sum(attn_out * attn_out),
            jnp.sum(ssm_out * ssm_out),
            jnp.sum(ffn_out * ffn_out),
        ]
    )
    grad_out = cotangent.astype(jnp.float32)
    grad_activation = matmul_right_t(cotangent, weights[W_DOWN])
    grad_gate_f32, grad_upper_f32 = swiglu_back(grad_activation)
    grad_gate = grad_gate_f32.astype(jnp.bfloat16)
    grad_upper = grad_upper_f32.astype(jnp.bfloat16)
    grad_hidden_two = matmul_right_t(grad_gate, weights[W_GATE]) + matmul_right_t(
        grad_upper, weights[W_UP_PROJ]
    )
    grad_middle_norm, grad_norm_ffn = norm_two_back(grad_hidden_two)
    grad_middle = grad_out + grad_middle_norm
    grad_branch = grad_middle.astype(jnp.bfloat16)
    grad_attended = matmul_right_t(grad_branch, weights[W_ATTN_OUT]).astype(jnp.bfloat16)
    grad_ssm_low = matmul_right_t(grad_branch, weights[W_SSM_OUT])
    grad_ssm_y, grad_gate_ssm_f32, grad_norm_ssm = gnorm_back(grad_ssm_low)
    grad_state_local = weighted_state(conv_values, PAIRS + 1, grad_ssm_y, entry_rows)
    if fast:
        scan = Flow(scan_stages(carry_all, grad_state_local, True))
        (late,) = bracket(
            lambda after: pack_late(
                (hidden_two, grad_gate), (hidden_two, grad_upper), (activation, cotangent),
                ssm_low, grad_branch, grad_norm_ffn, after,
            ),
            [scan],
        )
        late_flow = Flow(reduce_stages(late, 1, 14))
        (early,) = bracket(lambda after: pack_out(ssm_low, grad_branch, after + late_flow.values()), [scan])
        scan.go()
        late_flow.go()
        grad_state_out = scan.result
        around = lambda call: bracket(call, [late_flow])
    else:
        grad_state_out = scan_states(carry_all, grad_state_local, span, fast, True)
        around = lambda call: call(())
    grad_x, grad_b, grad_c, grad_small = around(
        lambda after: ssm_backward(
            conv_values, grad_ssm_y, chunk_cum, step_rows, state_in, grad_state_out, skip_wide, ssm_meta, start_row,
            after,
        )
    )
    grad_direct = grad_small[:, 0:2].reshape(SSM_HEADS, rows_dev)
    grad_logs = grad_small[:, 2:4].reshape(SSM_HEADS, rows_dev)
    grad_decay_log = decay * jnp.sum(step_rows * grad_logs, axis=1)
    grad_step_rows = (grad_direct + decay[:, None] * grad_logs) * jax.nn.sigmoid(step_in)
    grad_step_bias = jnp.sum(grad_step_rows, axis=1)
    grad_step_raw_f32 = grad_step_rows.T
    grad_skip_gain = jnp.sum(grad_small[:, 4, : 2 * SSM_DIM].reshape(SSM_HEADS, SSM_DIM), axis=1)
    grad_main, grad_tail, grad_edge, grad_taps = around(
        lambda after: conv_backward(
            grad_x, grad_b, grad_c, xbc, rim_rows, small_f32[CONV_WEIGHT], conv_bias, ssm_meta,
            row_starts[:, None], after,
        )
    )
    grad_conv_weight = grad_taps[:CONV]
    grad_conv_bias = grad_taps[CONV]
    rim_back = passed_along(grad_edge, span, -1)
    grad_tail = grad_tail + jnp.pad(rim_back, ((8, 0), (0, 0)))
    grad_xbc = lax.dynamic_update_slice(grad_main, grad_tail.astype(jnp.bfloat16), (rows_dev - 16, 0))
    grad_gate_ssm = grad_gate_ssm_f32.astype(jnp.bfloat16)
    grad_step_raw = grad_step_raw_f32.astype(jnp.bfloat16)
    grad_w_step = matmul_left_t(hidden, grad_step_raw)
    grad_hidden_ssm = (
        matmul_right_t(grad_gate_ssm, weights[W_GATE_SSM])
        + matmul_right_t(grad_xbc[:, :ssm_inner], weights[W_X_SSM])
        + matmul_right_t(grad_xbc[:, ssm_inner:], weights[W_B_C])
        + matmul_right_t(grad_step_raw, weights[W_STEP])
    )
    small = {
        W_STEP: grad_w_step,
        CONV_WEIGHT: grad_conv_weight,
        CONV_BIAS: grad_conv_bias,
        STEP_BIAS: grad_step_bias,
        DECAY_LOG: grad_decay_log,
        SKIP_GAIN: grad_skip_gain,
        NORM_SSM: grad_norm_ssm,
        NORM_FFN: grad_norm_ffn,
    }
    g_low = grad_attended.reshape(rows_dev, HEADS_Q, HEAD_DIM).transpose(1, 0, 2)
    g_wide = jnp.pad(g_low, ((0, 0), (0, 0), (HEAD_DIM, 0)))
    parts = []
    if fast:
        early = pack_ssm(
            early,
            [
                (attended, grad_branch), (hidden, grad_gate_ssm),
                (hidden, grad_xbc[:, :ssm_inner]), (hidden, grad_xbc[:, ssm_inner:]),
            ],
            small, ssm_low, grad_branch, late_flow.values(),
        )
        early_flow = Flow(reduce_stages(early, 0, 8))
        around = lambda call: bracket(call, [early_flow])
    for group_at in range(HEADS_KV):
        after_part = [part[1] for part in parts]
        if fast and group_at == 0:
            after_part = late_flow.values()
        parts.append(
            around(
                lambda after: attention_backward(
                    q_wide, g_wide, key_blocks, logs, mixed, meta, start_row, group_at, (*after, *after_part)
                )
            )
        )
    grad_kv = jnp.concatenate([part[0] for part in parts], axis=1)
    grad_q_turned = jnp.concatenate([part[1] for part in parts], axis=0)
    if rows_dev != KEYS:
        grad_kv = grad_kv.transpose(1, 0, 2, 3).reshape(HEADS_KV, -1, rows_dev, PAIR).transpose(1, 0, 2, 3)
    if fast:
        late_flow.go()
        scatter = Flow(scatter_stages(grad_kv))
        (grad_q_turned,) = fence([grad_q_turned], scatter.values() + early_flow.values() + late_flow.values())
    grad_q_rot = grad_q_turned.reshape(HEADS_Q * HEAD_DIM, rows_dev).T * score_scale
    grad_query_low = rotate(grad_q_rot, cosine, -sine, HEADS_Q).astype(jnp.bfloat16)
    if fast:
        scatter.go()
        (grad_query_low,) = fence([grad_query_low], scatter.values())
    grad_hidden = grad_hidden_ssm + matmul_right_t(grad_query_low, weights[W_QUERY])
    if fast:
        scatter.go()
        early_flow.go()
        (grad_hidden,) = fence([grad_hidden], scatter.values() + early_flow.values())
        scatter.go()
        grad_kv_mine = scatter.result
    else:
        grad_kv_mine = scatter_span(grad_kv, span, fast)
    grad_keys_mine = grad_kv_mine[:, :, :HEAD_DIM].transpose(1, 0, 2).reshape(rows_dev, -1)
    grad_values_mine = grad_kv_mine[:, :, HEAD_DIM:].transpose(1, 0, 2).reshape(rows_dev, -1)
    grad_key_low = rotate(grad_keys_mine, cosine, -sine, HEADS_KV).astype(jnp.bfloat16)
    grad_value_low = grad_values_mine.astype(jnp.bfloat16)
    if fast:
        corner = pack_qkv(
            [(hidden, grad_query_low), (hidden, grad_key_low), (hidden, grad_value_low)],
            attended, grad_branch, early_flow.values(),
        )
        corner_flow = Flow(corner_stages(corner))
        for flow in (early_flow, late_flow, corner_flow):
            while flow.sends:
                flow.go()
    grad_hidden = (
        grad_hidden
        + matmul_right_t(grad_key_low, weights[W_KEY])
        + matmul_right_t(grad_value_low, weights[W_VALUE])
    )
    grad_x_norm, grad_norm_attn = norm_one_back(grad_hidden)
    grad_tokens = grad_middle + grad_x_norm
    if fast:
        ends = sum_all(jnp.concatenate([grad_norm_attn, squares]), group + span, fast)
        norms, totals = ends[:D], ends[D:]
        stats = jnp.sqrt(totals / (all_rows * D))
        grad_shard = own_lines(early_flow.result, late_flow.result, corner_flow.result, norms)
        return (result.astype(jnp.bfloat16), grad_tokens, grad_shard, stats)
    small[NORM_ATTN] = grad_norm_attn
    stats = jnp.sqrt(sum_all(squares, group + span, fast) / (all_rows * D))
    pairs = {
        W_QUERY: (hidden, grad_query_low),
        W_KEY: (hidden, grad_key_low),
        W_VALUE: (hidden, grad_value_low),
        W_ATTN_OUT: (attended, grad_branch),
        W_GATE_SSM: (hidden, grad_gate_ssm),
        W_X_SSM: (hidden, grad_xbc[:, :ssm_inner]),
        W_B_C: (hidden, grad_xbc[:, ssm_inner:]),
        W_SSM_OUT: (ssm_low, grad_branch),
        W_GATE: (hidden_two, grad_gate),
        W_UP_PROJ: (hidden_two, grad_upper),
        W_DOWN: (activation, cotangent),
    }
    grad_dict = dict(small)
    for name_key, (left, right) in pairs.items():
        grad_dict[name_key] = matmul_left_t(left, right)
    flat_parts = [grad_dict[name_key].reshape(-1) for name_key, extent in layout()]
    used_entries = 0
    for part_array in flat_parts:
        used_entries += part_array.shape[0]
    flat_parts.append(jnp.zeros((params.shape[0] * lax.axis_size(group + span) - used_entries,), jnp.float32))
    grad_shard = lax.psum_scatter(
        jnp.concatenate(flat_parts), group + span, scatter_dimension=0, tiled=True
    )
    return (result.astype(jnp.bfloat16), grad_tokens, grad_shard, stats)


def solution(mesh):
    fast = (mesh.shape["group"], mesh.shape["span"]) == FAST
    if fast:
        mesh = Mesh(mesh.devices.reshape(4, 2, 2, 2), GRID)
        group, span = (GRID[:1], GRID[1:])
    else:
        group, span = (("group",), ("span",))

    def program(tokens, params, cotangent, offsets):
        return body(span, group, fast, tokens, params, cotangent, offsets)

    return jax.shard_map(
        program,
        mesh=mesh,
        in_specs=(P(group + span, None), P(group + span), P(group + span, None), P(group, None)),
        out_specs=(P(group + span, None), P(group + span, None), P(group + span), P()),
        check_vma=False,
    )
```

```python
import math

import jax
import jax.numpy as jnp
import numpy as np
from jax import lax
from jax.experimental import pallas as pl
from jax.experimental.pallas import tpu as pltpu
from jax.sharding import Mesh, PartitionSpec as P

D = 1024
HEADS_Q = 8
HEADS_KV = 2
HEAD_DIM = 64
SSM_HEADS = 24
SSM_DIM = 64
STATE = 128
CONV = 4
FF = 2048
(
    NORM_ATTN,
    W_QUERY,
    W_KEY,
    W_VALUE,
    W_ATTN_OUT,
    W_GATE_SSM,
    W_X_SSM,
    W_B_C,
    W_STEP,
    CONV_WEIGHT,
    CONV_BIAS,
    STEP_BIAS,
    DECAY_LOG,
    SKIP_GAIN,
    NORM_SSM,
    W_SSM_OUT,
    NORM_FFN,
    W_GATE,
    W_UP_PROJ,
    W_DOWN,
) = range(20)


epsilon = 1e-05
rope_base = 100000000000.0
masked_score = -1e30
highest = lax.Precision.HIGHEST
small_names = (
    NORM_ATTN,
    CONV_WEIGHT,
    CONV_BIAS,
    STEP_BIAS,
    DECAY_LOG,
    SKIP_GAIN,
    NORM_SSM,
    NORM_FFN,
)


def passed_along(value, axis, steps):
    count = lax.axis_size(axis)
    first, last = (max(0, -steps), min(count, count - steps))
    return lax.ppermute(value, axis, [(source, source + steps) for source in range(first, last)])


def prefix(value, axis, combine, identity):
    peers, place = (lax.axis_size(axis), lax.axis_index(axis))
    everything = jax.tree.map(
        lambda part, kind: lax.all_gather(part.astype(kind), axis),
        value,
        (jnp.bfloat16, jnp.bfloat16),
    )
    start = jax.tree.map(
        lambda part, zero: jnp.broadcast_to(jnp.asarray(zero, part.dtype), part.shape),
        value,
        identity,
    )

    def prefix_turn(k, before):
        reached = k < place
        new = combine(
            before, jax.tree.map(lambda part, own: part[k].astype(own.dtype), everything, value)
        )
        return jax.tree.map(lambda a, b: jnp.where(reached, a, b), new, before)

    return lax.fori_loop(0, peers, prefix_turn, start)


def carried_in(value, axis, combine, identity):
    peers, place = (lax.axis_size(axis), lax.axis_index(axis))
    everything = jax.tree.map(
        lambda part, kind: lax.all_gather(part.astype(kind), axis),
        value,
        jax.tree.map(lambda a: jnp.bfloat16 if a.dtype == jnp.float32 else a.dtype, value),
    )
    start = jax.tree.map(
        lambda part, zero: jnp.broadcast_to(jnp.asarray(zero, part.dtype), part.shape),
        value,
        identity,
    )

    def carried_turn(k, before):
        at = peers - 1 - k
        reached = at > place
        new = combine(
            before, jax.tree.map(lambda part, own: part[at].astype(own.dtype), everything, value)
        )
        return jax.tree.map(lambda a, b: jnp.where(reached, a, b), new, before)

    return lax.fori_loop(0, peers, carried_turn, start)


def layout():
    ssm_inner = SSM_HEADS * SSM_DIM
    channels = ssm_inner + 2 * STATE
    return [
        (NORM_ATTN, (D,)),
        (W_QUERY, (D, HEADS_Q * HEAD_DIM)),
        (W_KEY, (D, HEADS_KV * HEAD_DIM)),
        (W_VALUE, (D, HEADS_KV * HEAD_DIM)),
        (W_ATTN_OUT, (HEADS_Q * HEAD_DIM, D)),
        (W_GATE_SSM, (D, ssm_inner)),
        (W_X_SSM, (D, ssm_inner)),
        (W_B_C, (D, 2 * STATE)),
        (W_STEP, (D, SSM_HEADS)),
        (CONV_WEIGHT, (CONV, channels)),
        (CONV_BIAS, (channels,)),
        (STEP_BIAS, (SSM_HEADS,)),
        (DECAY_LOG, (SSM_HEADS,)),
        (SKIP_GAIN, (SSM_HEADS,)),
        (NORM_SSM, (ssm_inner,)),
        (W_SSM_OUT, (ssm_inner, D)),
        (NORM_FFN, (D,)),
        (W_GATE, (D, FF)),
        (W_UP_PROJ, (D, FF)),
        (W_DOWN, (FF, D)),
    ]


def unpack(flat_vector):
    unpacked = {}
    offset = 0
    for name_key, extent in layout():
        amount = math.prod(extent)
        unpacked[name_key] = flat_vector[offset : offset + amount].reshape(extent)
        offset += amount
    return unpacked


def matmul(left, right):
    return jnp.dot(left, right, preferred_element_type=jnp.float32)


def matmul_left_t(left, right):
    return lax.dot_general(
        left, right, (((0,), (0,)), ((), ())), preferred_element_type=jnp.float32
    )


def matmul_right_t(left, right):
    return lax.dot_general(
        left, right, (((1,), (1,)), ((), ())), preferred_element_type=jnp.float32
    )


def rms_norm(values, gain):
    return values * lax.rsqrt(jnp.mean(values * values, axis=-1, keepdims=True) + epsilon) * gain


def gated_norm(ssm_y, gate_ssm, gain):
    return rms_norm(ssm_y * jax.nn.silu(gate_ssm), gain)


def swiglu(gate_ffn, upper):
    return jax.nn.silu(gate_ffn) * upper


def sequence_info(row_index, bounds):
    starts = bounds[:-1]
    inside = row_index[:, None] >= starts[None, :]
    seq_id = jnp.sum(inside.astype(jnp.int32), axis=1) - 1
    seq_start = jnp.max(jnp.where(inside, starts[None, :], 0), axis=1)
    return (seq_id, row_index - seq_start)


def rotary_tables(positions):
    half_dim = HEAD_DIM // 2
    freqs = jnp.exp(
        -jnp.arange(half_dim, dtype=jnp.float32) * (2.0 * math.log(rope_base) / HEAD_DIM)
    )
    angles = positions.astype(jnp.float32)[:, None] * freqs[None, :]
    return (jnp.cos(angles), jnp.sin(angles))


def rotate(values, cosine, sine, heads):
    row_count = values.shape[0]
    half_dim = HEAD_DIM // 2
    split_heads = values.reshape(row_count, heads, HEAD_DIM)
    first_half = split_heads[..., :half_dim]
    second_half = split_heads[..., half_dim:]
    cos_b = cosine[:, None, :]
    sin_b = sine[:, None, :]
    turned = jnp.concatenate(
        [first_half * cos_b - second_half * sin_b, second_half * cos_b + first_half * sin_b],
        axis=-1,
    )
    return turned.reshape(row_count, heads * HEAD_DIM)


def add_rows(target, addend, first_row):
    current = lax.dynamic_slice_in_dim(target, first_row, addend.shape[0], 0)
    return lax.dynamic_update_slice_in_dim(target, current + addend, first_row, 0)


FAST = (4, 8)
LINE = 128
SHARD = 3082
SPAD = 3088
WIN = 3104
PLANE = 8 * SHARD
DEPTH = 4
TALL = {1: 1024, 2: 1024, 4: 512, 8: 256, 12: 128, 16: 128}
GRID = ("z", "y", "x", "c")
ZC = ("z", "c")
SWAP = [(0, 1), (1, 0)]


def zc_pairs(*pairs):
    return [(2 * a + c, 2 * b + c) for a, b, c in pairs]


def pinned(kernel, count, after):
    return lambda *refs: kernel(*refs[:count], *refs[count + len(after) :])


def pins(after):
    return [pl.BlockSpec(memory_space=pltpu.HBM)] * len(after)


class Flow:
    def __init__(self, stages):
        self.stages = stages
        self.sends = next(stages)
        self.result = None

    def values(self):
        return [value for value, _, _ in self.sends] or (list(self.result) if isinstance(self.result, list) else [self.result])

    def go(self, after=()):
        arrived = [lax.ppermute(value, axis, pairs) for value, axis, pairs in self.sends]
        if after:
            arrived = fence(arrived, after)
        try:
            self.sends = self.stages.send(arrived)
        except StopIteration as stop:
            self.sends, self.result = [], stop.value
        return self


def fence(values, after):
    def kernel(*refs):
        del refs

    return pl.pallas_call(
        kernel,
        in_specs=pins(values) + pins(after),
        out_specs=pins(values),
        out_shape=[jax.ShapeDtypeStruct(value.shape, value.dtype) for value in values],
        input_output_aliases={k: k for k in range(len(values))},
        name="fence",
    )(*values, *after)


def bracket(call, flows):
    out = call([value for flow in flows for value in flow.values()])
    for flow in flows:
        flow.go()
    return fence(out if isinstance(out, (list, tuple)) else [out], [v for flow in flows for v in flow.values()])


def gather_lines(params):
    z, y, x, c = (lax.axis_index(name) for name in GRID)
    lines = jnp.pad(params.reshape(SHARD, LINE), ((0, SPAD - SHARD), (0, 0)))
    sibling = lax.ppermute(lines, ZC, [(2 * k + 1 - k % 2, 2 * k + k % 2) for k in range(4)])
    buffers = []
    for part in range(2):
        here = jnp.where(c == part, lines, sibling)
        one = lax.ppermute(here, ZC, zc_pairs((0, 1, 0), (1, 2, 1)))
        side = lax.ppermute(here, ZC, zc_pairs((1, 0, 1)))
        two = lax.ppermute(one, ZC, zc_pairs((1, 2, 0), (2, 3, 1)))
        three = lax.ppermute(two, ZC, zc_pairs((2, 3, 0)))
        column = jnp.where(z == c, here, one + side + two + three)
        over_x = lax.ppermute(column, "x", SWAP)
        over_y = lax.ppermute(column, "y", SWAP)
        corner = lax.ppermute(over_y if part else over_x, "x" if part else "y", SWAP)
        local = [column, over_x, over_y, corner]
        buffers += [piece[None] for piece in local]
        buffers += [lax.ppermute(piece, "c", SWAP)[None] for piece in local]
    early = [(k, 0) for k in range(16)]
    here = jnp.where(c == 0, jnp.stack([lines, sibling]), jnp.stack([sibling, lines]))
    one = lax.ppermute(here, ZC, zc_pairs((2, 1, 0), (3, 2, 1)))
    side = lax.ppermute(here, ZC, zc_pairs((2, 3, 0)))
    two = lax.ppermute(one, ZC, zc_pairs((1, 0, 0), (2, 1, 1)))
    three = lax.ppermute(two, ZC, zc_pairs((1, 0, 1)))
    column = jnp.where(z == 2 + c, here, one + side + two + three)
    late = []
    for part in range(2):
        for first in (16, 21):
            late += [(first, part), (first + 1, part), (first + 2, part), (first + 3 + part, 0)]
    shard = np.arange(32)
    sz, sy, sx, sc = shard // 8, shard // 4 % 2, shard // 2 % 2, shard % 2
    away = jnp.where(sz % 2 == c, 0, 4)
    where = sc * 8 + away + 2 * (sy ^ y) + (sx ^ x) + 16 * (sz // 2)
    return buffers, Flow(spread_stages(column)), (early, early + late), where.astype(jnp.int32)


def spread_stages(column):
    over_x, over_y = yield [(column, "x", SWAP), (column, "y", SWAP)]
    corners = yield [(over_x[:1], "y", SWAP), (over_y[1:], "x", SWAP)]
    local = [column, over_x, over_y] + list(corners)
    return local + list((yield [(piece, "c", SWAP) for piece in local]))


def unpack_lines(buffers, slots, where, segments, after=()):
    jobs, starts = [], []
    reach = 0
    for offset, rows, columns in segments:
        per_row = columns // LINE
        lane, base = offset % LINE, offset // LINE
        if per_row == 1 and rows < 1024:
            lane, tall = 0, rows
        else:
            tall = TALL[per_row]
        starts.append(len(jobs))
        for k in range(rows // tall):
            jobs.append((base + k * tall * per_row, tall * per_row, 1 if lane else 0))
    window = max(job[1] for job in jobs) + 32
    table = np.zeros((len(jobs), 5), np.int32)
    for k, (line, count, extra) in enumerate(jobs):
        owner = line // SHARD
        inside = line - owner * SHARD
        begin = min(inside // 16 * 16, SPAD - window)
        crosses = int(line + count + extra > (owner + 1) * SHARD)
        table[k] = (owner, begin, begin - inside, crosses, (owner + 1) * SHARD - line)
    base_row = (int(-table[:, 2].min()) + 7) // 8 * 8
    table[:, 2] += base_row
    table[:, 4] += base_row
    room = int(max((table[:, 2] + window).max(), ((table[:, 4] + window) * table[:, 3]).max()))
    room = (room + 15) // 8 * 8
    total = len(jobs)
    count_buffers = len(buffers)
    shapes = []
    for offset, rows, columns in segments:
        per_row = columns // LINE
        tall = rows if per_row == 1 and rows < 1024 else TALL[per_row]
        shapes.append((rows, columns, tall, per_row, offset % LINE if tall != rows or per_row != 1 else 0))
    sizes = sorted({(tall, columns) for _, columns, tall, _, _ in shapes})

    def kernel(table_ref, where_ref, *refs):
        sources = refs[:count_buffers]
        outs = refs[count_buffers : count_buffers + len(segments)]
        rest = refs[count_buffers + len(segments) :]
        stages = dict(zip(sizes, rest))
        raw, flat, in_sem, out_sem = rest[len(sizes) :]
        step = pl.program_id(0)

        def fetch(job, slot):
            owner = table_ref[job, 0]
            begin = pl.multiple_of(table_ref[job, 1], 16)
            for b, (source, part) in enumerate(slots):

                @pl.when(where_ref[owner] == b)
                def _():
                    pltpu.make_async_copy(
                        sources[source].at[part, pl.ds(begin, window), :], raw.at[slot, 0], in_sem.at[slot, 0]
                    ).start()

            @pl.when(table_ref[job, 3] == 1)
            def _():
                for b, (source, part) in enumerate(slots):

                    @pl.when(where_ref[owner + 1] == b)
                    def _():
                        pltpu.make_async_copy(
                            sources[source].at[part, pl.ds(0, window), :], raw.at[slot, 1], in_sem.at[slot, 1]
                        ).start()

        def fetched(slot, half):
            return pltpu.make_async_copy(
                sources[0].at[0, pl.ds(0, window), :], raw.at[slot, half], in_sem.at[slot, half]
            )

        @pl.when(step == 0)
        def _():
            for k in range(min(DEPTH - 1, total)):
                fetch(k, k)

        @pl.when(step + DEPTH - 1 < total)
        def _():
            fetch(step + DEPTH - 1, lax.rem(step + DEPTH - 1, DEPTH))

        slot = lax.rem(step, DEPTH)
        fetched(slot, 0).wait()
        flat[pl.ds(table_ref[step, 2], window), :] = raw[slot, 0].astype(jnp.float32)

        @pl.when(table_ref[step, 3] == 1)
        def _():
            fetched(slot, 1).wait()
            flat[pl.ds(table_ref[step, 4], window), :] = raw[slot, 1].astype(jnp.float32)

        for index, (rows, columns, tall, per_row, lane) in enumerate(shapes):
            begin = starts[index]
            blocks = rows // tall
            stage = stages[(tall, columns)]

            @pl.when((step >= begin) & (step < begin + blocks))
            def _():
                block = step - begin
                side = lax.rem(block, 2)

                def written(k, s):
                    return pltpu.make_async_copy(
                        stage.at[s],
                        outs[index].at[pl.ds(pl.multiple_of(k * tall, 16), tall), :],
                        out_sem.at[s],
                    )

                @pl.when(block >= 2)
                def _():
                    written(block - 2, side).wait()

                def tile(j):
                    picked = flat[pl.ds(base_row + j, tall, stride=per_row), :]
                    return pltpu.roll(picked, LINE - lane, 1) if lane else picked

                if lane:
                    lanes = lax.broadcasted_iota(jnp.int32, (tall, LINE), 1)
                    now = tile(0)
                    for j in range(per_row):
                        later = tile(j + 1)
                        stage[side, :, j * LINE : (j + 1) * LINE] = jnp.where(
                            lanes < LINE - lane, now, later
                        ).astype(jnp.bfloat16)
                        now = later
                else:
                    for j in range(per_row):
                        stage[side, :, j * LINE : (j + 1) * LINE] = tile(j).astype(jnp.bfloat16)
                written(block, side).start()

                @pl.when(block == blocks - 1)
                def _():
                    if blocks > 1:
                        written(block - 1, 1 - side).wait()
                    written(block, side).wait()

    return pl.pallas_call(
        pinned(kernel, 2 + count_buffers, after),
        grid_spec=pltpu.PrefetchScalarGridSpec(
            num_scalar_prefetch=2,
            grid=(total,),
            in_specs=[pl.BlockSpec(memory_space=pl.ANY)] * count_buffers + pins(after),
            out_specs=[pl.BlockSpec(memory_space=pl.ANY)] * len(segments),
            scratch_shapes=[pltpu.VMEM((2,) + size, jnp.bfloat16) for size in sizes]
            + [
                pltpu.VMEM((DEPTH, 2, window, LINE), jnp.bfloat16),
                pltpu.VMEM((room, LINE), jnp.float32),
                pltpu.SemaphoreType.DMA((DEPTH, 2)),
                pltpu.SemaphoreType.DMA((2,)),
            ],
        ),
        out_shape=[jax.ShapeDtypeStruct((rows, columns), jnp.bfloat16) for _, rows, columns in segments],
        compiler_params=pltpu.CompilerParams(vmem_limit_bytes=48 * 2**20),
        cost_estimate=pl.CostEstimate(flops=0, bytes_accessed=total * window * LINE * 4, transcendentals=0),
        name="unpack",
    )(jnp.asarray(table), where, *buffers, *after)


def pack_lines(target, target_rows, first_row, segments, lane, phase, extras, carry, tail_rows, after=()):
    tall = 256
    lefts, rights, plan = [], [], []
    left_of, right_of = {}, {}
    row = first_row
    begin = 0
    for left, right in segments:
        for value, seen, kept in ((left, left_of, lefts), (right, right_of, rights)):
            if id(value) not in seen:
                seen[id(value)] = len(kept)
                kept.append(value)
        blocks = left.shape[1] // tall
        plan.append((left_of[id(left)], right_of[id(right)], right.shape[1] // LINE, begin, blocks, row))
        begin += blocks
        row += left.shape[1] * right.shape[1] // LINE
    end_row = row
    total = begin
    biggest = max(entry[2] for entry in plan) * tall
    tokens = lefts[0].shape[0]
    count_left, count_right, count_extra = len(lefts), len(rights), len(extras)
    rolled = [jnp.roll(right, lane, axis=1) if lane else right for right in rights]
    carry_in = [carry] if lane else []
    targets = [] if target is None else [target]

    def left_spec(index):
        mine = [entry for entry in plan if entry[0] == index]

        def place(step):
            block = 0
            for _, _, _, start, blocks, _ in mine:
                block = jnp.where(step >= start, jnp.minimum(step - start, blocks - 1), block)
            return (0, block)

        return pl.BlockSpec((tokens, tall), place)

    def kernel(*refs):
        left_refs = refs[:count_left]
        right_refs = refs[count_left : count_left + count_right]
        at = count_left + count_right
        extra_refs = refs[at : at + count_extra]
        at += count_extra
        carry_refs = refs[at : at + len(carry_in)]
        at += len(carry_in) + len(targets)
        out = refs[at]
        flat, stage, shift, last, sems, extra_sems = refs[at + 1 :]
        step = pl.program_id(0)
        side = lax.rem(step, 2)

        def extra_copy(k):
            rows = extras[k][0].shape[0]
            return pltpu.make_async_copy(
                extra_refs[k], out.at[pl.ds(extras[k][1], rows), :], extra_sems.at[k]
            )

        @pl.when(step == 0)
        def _():
            for k in range(count_extra):
                extra_copy(k).start()
            if lane:
                shift[0:8, :] = carry_refs[0][...]
            if phase:
                flat[0:8, :] = jnp.zeros((8, LINE), jnp.float32)

        for left_at, right_at, per_row, start, blocks, row in plan:
            lines = per_row * tall

            def written(block, s, row=row, lines=lines):
                return pltpu.make_async_copy(
                    stage.at[s, pl.ds(0, lines), :],
                    out.at[pl.ds(pl.multiple_of(row + block * lines, 16), lines), :],
                    sems.at[s],
                )

            @pl.when((step >= start) & (step < start + blocks))
            def _():
                block = step - start
                if phase:

                    @pl.when(step > 0)
                    def _():
                        flat[0:8, :] = flat[lines : lines + 8, :]

                turned = left_refs[left_at][...].T
                lanes = lax.broadcasted_iota(jnp.int32, (tall, LINE), 1)
                for j0 in range(0, per_row, 2):
                    wide = min(2, per_row - j0)
                    tile = jnp.dot(
                        turned,
                        right_refs[right_at][:, j0 * LINE : (j0 + wide) * LINE],
                        preferred_element_type=jnp.float32,
                    )
                    for j in range(wide):
                        piece = tile[:, j * LINE : (j + 1) * LINE]
                        if lane and j0 + j == 0:
                            shift[8 : 8 + tall, :] = piece
                            piece = jnp.where(lanes < lane, shift[7 : 7 + tall, :], piece)
                            shift[0:8, :] = shift[tall : tall + 8, :]
                        if per_row == 1:
                            flat[phase : phase + tall, :] = piece
                        else:
                            flat[pl.ds(phase + j0 + j, tall, stride=per_row), :] = piece

                stage[side, 0:lines, :] = flat[0:lines, :].astype(jnp.bfloat16)
                written(block, side).start()

            @pl.when((step > start) & (step <= start + blocks))
            def _():
                written(step - start - 1, 1 - side).wait()

            if start + blocks == total:

                @pl.when(step == total - 1)
                def _():
                    written(blocks - 1, side).wait()

        @pl.when(step == total - 1)
        def _():
            if tail_rows:
                lanes = lax.broadcasted_iota(jnp.int32, (tail_rows, LINE), 1)
                rows_at = lax.broadcasted_iota(jnp.int32, (tail_rows, LINE), 0)
                final = jnp.broadcast_to(shift[7:8, :], (tail_rows, LINE))
                last[...] = jnp.where((rows_at == 0) & (lanes < lane), final, 0.0).astype(jnp.bfloat16)
                closing = pltpu.make_async_copy(
                    last, out.at[pl.ds(end_row, tail_rows), :], extra_sems.at[count_extra]
                )
                closing.start()
                closing.wait()
            for k in range(count_extra):
                extra_copy(k).wait()

    whole = [pl.BlockSpec(array.shape, lambda step: (0, 0)) for array in rolled]
    flops = sum(2 * tokens * entry[4] * tall * entry[2] * LINE for entry in plan)
    inputs = count_left + count_right + count_extra + len(carry_in) + len(targets)
    return pl.pallas_call(
        pinned(kernel, inputs, after),
        grid=(total,),
        in_specs=[left_spec(k) for k in range(count_left)]
        + whole
        + [pl.BlockSpec(array.shape, lambda step: (0, 0)) for array, _ in extras]
        + [pl.BlockSpec(array.shape, lambda step: (0, 0)) for array in carry_in]
        + [pl.BlockSpec(memory_space=pl.ANY)] * len(targets)
        + pins(after),
        out_specs=pl.BlockSpec(memory_space=pl.ANY),
        out_shape=jax.ShapeDtypeStruct((target_rows, LINE), jnp.bfloat16),
        scratch_shapes=[
            pltpu.VMEM((biggest + 16, LINE), jnp.float32),
            pltpu.VMEM((2, biggest, LINE), jnp.bfloat16),
            pltpu.VMEM((tall + 8, LINE), jnp.float32),
            pltpu.VMEM((max(tail_rows, 16), LINE), jnp.bfloat16),
            pltpu.SemaphoreType.DMA((2,)),
            pltpu.SemaphoreType.DMA((count_extra + 1,)),
        ],
        input_output_aliases={count_left + count_right + count_extra + len(carry_in): 0} if targets else {},
        compiler_params=pltpu.CompilerParams(vmem_limit_bytes=48 * 2**20),
        cost_estimate=pl.CostEstimate(flops=flops, bytes_accessed=total * biggest * LINE * 2, transcendentals=0),
        name="pack",
    )(*lefts, *rolled, *[array for array, _ in extras], *carry_in, *targets, *after)


def added(*parts):
    total = parts[0].astype(jnp.float32)
    for part in parts[1:]:
        total = total + part.astype(jnp.float32)
    return total.astype(jnp.bfloat16)


def reduce_stages(flat, batch, shift):
    z, y, x, c = (lax.axis_index(name) for name in GRID)
    length = PLANE + 32
    send = lax.dynamic_slice(flat, ((1 - c) * PLANE, 0), (length, LINE))
    (arrived,) = yield [(send, "c", SWAP)]
    chip = added(lax.dynamic_slice(flat, (c * PLANE, 0), (length, LINE)), arrived)

    def window(sy, sx, part):
        shard = sy * 4 + sx * 2 + part
        start = (shift + SHARD * shard) // 16 * 16
        return lax.dynamic_slice(chip, (start, 0), (WIN, LINE))

    away_0 = jnp.stack([window(1 - y, 0, 0), window(1 - y, 1, 0)])
    away_1 = jnp.stack([window(0, 1 - x, 1), window(1, 1 - x, 1)])
    home_0 = jnp.stack([window(y, 0, 0), window(y, 1, 0)])
    home_1 = jnp.stack([window(0, x, 1), window(1, x, 1)])
    got_0, got_1 = yield [(away_0, "y", SWAP), (away_1, "x", SWAP)]
    half_0, half_1 = added(home_0, got_0), added(home_1, got_1)
    pick = lambda value, at: lax.dynamic_index_in_dim(value, at, 0, keepdims=False)
    got_0, got_1 = yield [(pick(half_0, 1 - x), "x", SWAP), (pick(half_1, 1 - y), "y", SWAP)]
    columns = [added(pick(half_0, x), got_0), added(pick(half_1, y), got_1)]
    if batch == 0:
        hops = [((1, 0, 0), (2, 1, 1)), ((2, 0, 0), (3, 1, 1)), ((3, 0, 0), (0, 1, 1))]
    else:
        hops = [((1, 2, 0), (2, 3, 1)), ((0, 2, 0), (1, 3, 1)), ((3, 2, 0), (0, 3, 1))]
    if batch == 0:
        got = yield [(columns[0], ZC, zc_pairs(*hop)) for hop in hops]
        end = added(columns[0], *got)
        (column,) = fence(columns[1:], [end])
        got = yield [(column, ZC, zc_pairs(*hop)) for hop in hops]
        ends = [end, added(column, *got)]
    else:
        columns = jnp.stack(columns)
        got = yield [(columns, ZC, zc_pairs(*hop)) for hop in hops]
        ends = added(columns, *got)
    mine = jnp.where(c == 0, ends[0], ends[1])
    other = jnp.where(c == 0, ends[1], ends[0])
    (handed,) = yield [(other, ZC, [(2 * k + k % 2, 2 * k + 1 - k % 2) for k in range(4)])]
    return jnp.where(c == z % 2, mine, handed)


PIECE = 400


def corner_stages(flat):
    z, y, x, c = (lax.axis_index(name) for name in GRID)
    length = 8 * PIECE
    second = (8 + SHARD) // 16 * 16
    take = lambda at: lax.dynamic_slice(flat, (at * second, 0), (length, LINE))
    (arrived,) = yield [(take(1 - c), "c", SWAP)]
    chip = added(take(c), arrived).reshape(2, 2, 2, PIECE, LINE)
    pick = lambda value, at: lax.dynamic_index_in_dim(value, at, 0, keepdims=False)
    got = yield [(pick(chip[0], 1 - x), "x", SWAP), (pick(chip[1], 1 - y), "y", SWAP)]
    halves = [added(pick(chip[0], x), got[0]), added(pick(chip[1], y), got[1])]
    got = yield [(pick(halves[0], 1 - y), "y", SWAP), (pick(halves[1], 1 - x), "x", SWAP)]
    pieces = jnp.stack([added(pick(halves[0], y), got[0]), added(pick(halves[1], x), got[1])])
    got = yield [(pieces, "z", [(k, 0)]) for k in (1, 2, 3)]
    pieces = added(pieces, *got)
    got = yield [(pieces[0], "y", [(1, 0)]), (pieces[1], "x", [(1, 0)])]
    halves = [jnp.stack([pieces[0], got[0]]), jnp.stack([pieces[1], got[1]])]
    got = yield [(halves[0], "x", [(1, 0)]), (halves[1], "y", [(1, 0)])]
    return jnp.stack([halves[0], got[0], halves[1], got[1]]).reshape(length, LINE)


CHUNK = 128
NT = (((1,), (1,)), ((), ()))
TN = (((0,), (0,)), ((), ()))
INNER = SSM_HEADS * SSM_DIM
PAIRS = SSM_HEADS // 2


def spread(rows_a, rows_b):
    length = rows_a.shape[1]
    tall = jnp.concatenate(
        [jnp.broadcast_to(rows_a, (SSM_DIM, length)), jnp.broadcast_to(rows_b, (SSM_DIM, length))], axis=0
    )
    return tall.T


CHANNELS = INNER + 2 * STATE
LANES = 2 * SSM_DIM
COLUMNS = CHANNELS // LANES


def conv_parts(ext, weight_ref, bias_ref, start_ref, first, rows):
    place = first + lax.broadcasted_iota(jnp.int32, (rows, 1), 0) - start_ref[...]
    windows = []
    total = bias_ref[...]
    for tap in range(CONV):
        reach = CONV - 1 - tap
        window = jnp.where(place >= reach, ext[8 - reach : 8 - reach + rows, :], 0.0)
        windows.append(window)
        total = total + window * weight_ref[tap : tap + 1, :]
    return place, windows, total


def conv_forward(xbc, rim, weight, bias, meta, start_column, after=()):
    rows = xbc.shape[0]

    def kernel(meta_ref, x_ref, rim_ref, weight_ref, bias_ref, start_ref, out_ref, ext):
        ext[0:8, :] = rim_ref[...]
        ext[8:, :] = x_ref[...]
        _, _, total = conv_parts(ext, weight_ref, bias_ref, start_ref, meta_ref[0], rows)
        out_ref[...] = total * jax.nn.sigmoid(total)

    lanes = lambda i, m: (0, i)
    return pl.pallas_call(
        pinned(kernel, 6, after),
        grid_spec=pltpu.PrefetchScalarGridSpec(
            num_scalar_prefetch=1,
            grid=(COLUMNS,),
            in_specs=[
                pl.BlockSpec((rows, LANES), lanes),
                pl.BlockSpec((8, LANES), lanes),
                pl.BlockSpec((CONV, LANES), lanes),
                pl.BlockSpec((1, LANES), lanes),
                pl.BlockSpec((rows, 1), lambda i, m: (0, 0)),
            ] + pins(after),
            out_specs=pl.BlockSpec((rows, LANES), lanes),
            scratch_shapes=[pltpu.VMEM((rows + 8, LANES), jnp.float32)],
        ),
        out_shape=jax.ShapeDtypeStruct((rows, CHANNELS), jnp.float32),
        cost_estimate=pl.CostEstimate(flops=10**9, bytes_accessed=rows * CHANNELS * 8, transcendentals=0),
        name="conv",
    )(meta, xbc, rim, weight, bias, start_column, *after)


def conv_backward(dx, db, dc, xbc, rim, weight, bias, meta, start_column, after=()):
    rows = xbc.shape[0]

    def kernel(meta_ref, dx_ref, db_ref, dc_ref, x_ref, rim_ref, weight_ref, bias_ref, start_ref,
               low_ref, tail_ref, edge_ref, small_ref, ext, upper):
        ext[0:8, :] = rim_ref[...]
        ext[8:, :] = x_ref[...]
        at = pl.program_id(0)
        arrived = jnp.where(at < PAIRS, dx_ref[...], jnp.where(at == PAIRS, db_ref[...], dc_ref[...]))
        place, windows, total = conv_parts(ext, weight_ref, bias_ref, start_ref, meta_ref[0], rows)
        gate = jax.nn.sigmoid(total)
        change = arrived * gate * (1.0 + total * (1.0 - gate))
        upper[0:8, :] = jnp.zeros((8, LANES), jnp.float32)
        upper[8 + rows :, :] = jnp.zeros((8, LANES), jnp.float32)
        main = jnp.zeros((rows, LANES), jnp.float32)
        edge = jnp.zeros((8, LANES), jnp.float32)
        small_ref[...] = jnp.zeros((8, LANES), jnp.float32)
        small_ref[CONV : CONV + 1, :] = jnp.sum(change, axis=0, keepdims=True)
        for tap in range(CONV):
            reach = CONV - 1 - tap
            small_ref[tap : tap + 1, :] = jnp.sum(change * windows[tap], axis=0, keepdims=True)
            upper[8 : 8 + rows, :] = jnp.where(place >= reach, change, 0.0) * weight_ref[tap : tap + 1, :]
            main = main + upper[8 + reach : 8 + reach + rows, :]
            edge = edge + upper[reach : reach + 8, :]
        low_ref[...] = main.astype(jnp.bfloat16)
        tail_ref[...] = main[rows - 16 :, :]
        edge_ref[...] = edge

    lanes = lambda i, m: (0, i)
    whole = lambda i, m: (0, 0)
    return pl.pallas_call(
        pinned(kernel, 9, after),
        grid_spec=pltpu.PrefetchScalarGridSpec(
            num_scalar_prefetch=1,
            grid=(COLUMNS,),
            in_specs=[
                pl.BlockSpec((rows, LANES), lambda i, m: (0, jnp.minimum(i, PAIRS - 1))),
                pl.BlockSpec((rows, STATE), whole),
                pl.BlockSpec((rows, STATE), whole),
                pl.BlockSpec((rows, LANES), lanes),
                pl.BlockSpec((8, LANES), lanes),
                pl.BlockSpec((CONV, LANES), lanes),
                pl.BlockSpec((1, LANES), lanes),
                pl.BlockSpec((rows, 1), whole),
            ] + pins(after),
            out_specs=[
                pl.BlockSpec((rows, LANES), lanes),
                pl.BlockSpec((16, LANES), lanes),
                pl.BlockSpec((8, LANES), lanes),
                pl.BlockSpec((8, LANES), lanes),
            ],
            scratch_shapes=[
                pltpu.VMEM((rows + 8, LANES), jnp.float32),
                pltpu.VMEM((rows + 16, LANES), jnp.float32),
            ],
        ),
        out_shape=[
            jax.ShapeDtypeStruct((rows, CHANNELS), jnp.bfloat16),
            jax.ShapeDtypeStruct((16, CHANNELS), jnp.float32),
            jax.ShapeDtypeStruct((8, CHANNELS), jnp.float32),
            jax.ShapeDtypeStruct((8, CHANNELS), jnp.float32),
        ],
        cost_estimate=pl.CostEstimate(flops=2 * 10**9, bytes_accessed=rows * CHANNELS * 10, transcendentals=0),
        name="conv_back",
    )(meta, dx, db, dc, xbc, rim, weight, bias, start_column, *after)


def weighted_state(left, left_block, values, weight_rows, after=()):
    rows = left.shape[0]

    def kernel(left_ref, value_ref, weight_ref, out_ref, turned):
        @pl.when(pl.program_id(0) == 0)
        def _():
            turned[...] = left_ref[...].T.astype(jnp.bfloat16)

        wide = spread(weight_ref[0, 0:1, :], weight_ref[0, 1:2, :])
        scaled = (value_ref[...] * wide).astype(jnp.bfloat16)
        out_ref[...] = jnp.dot(turned[...], scaled, preferred_element_type=jnp.float32)

    return pl.pallas_call(
        pinned(kernel, 3, after),
        grid=(PAIRS,),
        in_specs=[
            pl.BlockSpec((rows, STATE), lambda i: (0, left_block)),
            pl.BlockSpec((rows, 2 * SSM_DIM), lambda i: (0, i)),
            pl.BlockSpec((1, 2, rows), lambda i: (i, 0, 0)),
        ] + pins(after),
        out_specs=pl.BlockSpec((STATE, 2 * SSM_DIM), lambda i: (0, i)),
        out_shape=jax.ShapeDtypeStruct((STATE, INNER), jnp.float32),
        scratch_shapes=[pltpu.VMEM((STATE, rows), jnp.bfloat16)],
        cost_estimate=pl.CostEstimate(flops=2 * rows * STATE * INNER, bytes_accessed=rows * INNER * 4, transcendentals=0),
        name="state",
    )(left, values, weight_rows.reshape(PAIRS, 2, rows), *after)


def chunk_rows(k, meta_ref, cum_ref, start_ref):
    here = slice(k * CHUNK, (k + 1) * CHUNK)
    first = meta_ref[0] + k * CHUNK
    index = first + lax.broadcasted_iota(jnp.int32, (1, CHUNK), 1)
    entering = start_ref[0:1, here] < first
    ending = index >= meta_ref[1 + k]
    cums, entries, tails = [], [], []
    for e in range(2):
        cum = cum_ref[0, e : e + 1, here]
        cums.append(cum)
        entries.append(jnp.where(entering, jnp.exp(cum), 0.0))
        gap = jnp.where(ending, cum[:, CHUNK - 1 :] - cum, masked_score)
        tails.append(jnp.exp(gap))
    return cums, entries, tails


def ssm_forward(conv, cum, step, state_in, skip, meta, start_column, start_row):
    rows = conv.shape[0]
    chunks = rows // CHUNK

    def kernel(meta_ref, x_ref, b_ref, c_ref, cum_ref, step_ref, state_ref, skip_ref, col_ref, row_ref,
               y_ref, inner, hide, state, b_turned):
        @pl.when(pl.program_id(0) == 0)
        def _():
            for k in range(chunks):
                here = slice(k * CHUNK, (k + 1) * CHUNK)
                b_turned[:, here] = b_ref[here, :].T.astype(jnp.bfloat16)
                inner[k] = lax.dot_general(
                    c_ref[here, :], b_ref[here, :], NT, precision=highest, preferred_element_type=jnp.float32
                )
                t = lax.broadcasted_iota(jnp.int32, (CHUNK, CHUNK), 0)
                s = lax.broadcasted_iota(jnp.int32, (CHUNK, CHUNK), 1)
                shown = (s <= t) & (meta_ref[0] + k * CHUNK + s >= col_ref[here, :])
                hide[k] = jnp.where(shown, 0.0, masked_score)

        low_lane = lax.broadcasted_iota(jnp.int32, (CHUNK, 2 * SSM_DIM), 1) < SSM_DIM
        state[...] = state_ref[...]
        for k in range(chunks):
            here = slice(k * CHUNK, (k + 1) * CHUNK)
            cums, entries, tails = chunk_rows(k, meta_ref, cum_ref, row_ref)
            x_now = x_ref[here, :]
            x_low = x_now.astype(jnp.bfloat16)
            entry = spread(*entries)
            weight = spread(*[tails[e] * step_ref[0, e : e + 1, here] for e in range(2)])
            parts = []
            for e in range(2):
                across = jnp.broadcast_to(cums[e], (CHUNK, CHUNK))
                decays = jnp.exp(across.T - across + hide[k])
                mix = (inner[k] * decays * step_ref[0, e : e + 1, here]).astype(jnp.bfloat16)
                parts.append(jnp.dot(mix, x_low, preferred_element_type=jnp.float32))
            carried = jnp.dot(
                c_ref[here, :].astype(jnp.bfloat16), state[...].astype(jnp.bfloat16),
                preferred_element_type=jnp.float32,
            )
            y_ref[here, :] = jnp.where(low_lane, parts[0], parts[1]) + entry * carried + skip_ref[...] * x_now
            fresh = jnp.dot(
                b_turned[:, here], (x_now * weight).astype(jnp.bfloat16), preferred_element_type=jnp.float32
            )
            state[...] = entry[CHUNK - 1 :, :] * state[...] + fresh

    whole = lambda i, m: (0, 0)
    lanes = lambda i, m: (0, i)
    return pl.pallas_call(
        kernel,
        grid_spec=pltpu.PrefetchScalarGridSpec(
            num_scalar_prefetch=1,
            grid=(PAIRS,),
            in_specs=[
                pl.BlockSpec((rows, 2 * SSM_DIM), lanes),
                pl.BlockSpec((rows, STATE), lambda i, m: (0, PAIRS)),
                pl.BlockSpec((rows, STATE), lambda i, m: (0, PAIRS + 1)),
                pl.BlockSpec((1, 2, rows), lambda i, m: (i, 0, 0)),
                pl.BlockSpec((1, 2, rows), lambda i, m: (i, 0, 0)),
                pl.BlockSpec((STATE, 2 * SSM_DIM), lanes),
                pl.BlockSpec((1, 2 * SSM_DIM), lanes),
                pl.BlockSpec((rows, 1), whole),
                pl.BlockSpec((8, rows), whole),
            ],
            out_specs=pl.BlockSpec((rows, 2 * SSM_DIM), lanes),
            scratch_shapes=[
                pltpu.VMEM((chunks, CHUNK, CHUNK), jnp.float32),
                pltpu.VMEM((chunks, CHUNK, CHUNK), jnp.float32),
                pltpu.VMEM((STATE, 2 * SSM_DIM), jnp.float32),
                pltpu.VMEM((STATE, rows), jnp.bfloat16),
            ],
        ),
        out_shape=jax.ShapeDtypeStruct((rows, INNER), jnp.float32),
        compiler_params=pltpu.CompilerParams(vmem_limit_bytes=40 * 2**20),
        cost_estimate=pl.CostEstimate(flops=10**9, bytes_accessed=rows * INNER * 8, transcendentals=2**21),
        name="ssm",
    )(meta, conv, conv, conv, cum.reshape(PAIRS, 2, rows), step.reshape(PAIRS, 2, rows), state_in, skip,
      start_column, start_row)


def ssm_backward(conv, dy, cum, step, state_in, state_grad, skip, meta, start_row, after=()):
    rows = conv.shape[0]
    chunks = rows // CHUNK

    def kernel(meta_ref, x_ref, dy_ref, b_ref, c_ref, cum_ref, step_ref, state_ref, grad_ref, skip_ref, row_ref,
               dx_ref, db_ref, dc_ref, small_ref, inner, hide, inner_grad, states, flow,
               b_turned, c_turned):
        low = lambda v: v.astype(jnp.bfloat16)
        dot = lambda p, q, dims=(((1,), (0,)), ((), ())): lax.dot_general(
            p, q, dims, preferred_element_type=jnp.float32
        )
        exact = lambda p, q, dims=(((1,), (0,)), ((), ())): lax.dot_general(
            p, q, dims, precision=highest, preferred_element_type=jnp.float32
        )
        s = lax.broadcasted_iota(jnp.int32, (CHUNK, CHUNK), 0)
        t = lax.broadcasted_iota(jnp.int32, (CHUNK, CHUNK), 1)

        @pl.when(pl.program_id(0) == 0)
        def _():
            db_ref[...] = jnp.zeros(db_ref.shape, jnp.float32)
            dc_ref[...] = jnp.zeros(dc_ref.shape, jnp.float32)
            inner_grad[...] = jnp.zeros(inner_grad.shape, jnp.float32)
            for k in range(chunks):
                here = slice(k * CHUNK, (k + 1) * CHUNK)
                b_turned[:, here] = low(b_ref[here, :].T)
                c_turned[:, here] = low(c_ref[here, :].T)
                inner[k] = exact(b_ref[here, :], c_ref[here, :], NT)
                shown = (s <= t) & (meta_ref[0] + k * CHUNK + s >= row_ref[0:1, here])
                hide[k] = jnp.where(shown, 0.0, masked_score)

        before = (s < t).astype(jnp.float32)
        until = low((s >= t).astype(jnp.float32))
        low_lane = t < SSM_DIM
        pick_row = lax.broadcasted_iota(jnp.int32, (8, 2 * SSM_DIM), 0)
        pick_lane = lax.broadcasted_iota(jnp.int32, (8, 2 * SSM_DIM), 1) // SSM_DIM
        pick = low((pick_row == pick_lane).astype(jnp.float32))
        spreads = []
        states[0] = state_ref[...]
        for k in range(chunks):
            here = slice(k * CHUNK, (k + 1) * CHUNK)
            cums, entries, tails = chunk_rows(k, meta_ref, cum_ref, row_ref)
            entry, tail = spread(*entries), spread(*tails)
            steps = spread(step_ref[0, 0:1, here], step_ref[0, 1:2, here])
            spreads.append((cums, entry, tail, steps))
            if k < chunks - 1:
                fresh = dot(b_turned[:, here], low(x_ref[here, :] * steps * tail))
                states[k + 1] = entry[CHUNK - 1 :, :] * states[k] + fresh
        flow[...] = grad_ref[...]
        skip_sum = jnp.zeros((1, 2 * SSM_DIM), jnp.float32)
        for k in reversed(range(chunks)):
            here = slice(k * CHUNK, (k + 1) * CHUNK)
            cums, entry, tail, steps = spreads[k]
            x_now, dy_now = x_ref[here, :], dy_ref[here, :]
            b_low, c_low = low(b_ref[here, :]), low(c_ref[here, :])
            scaled = x_now * steps
            dy_low = low(dy_now)
            flow_low, state_low = low(flow[...]), low(states[k])
            mixed, within = [], []
            for e in range(2):
                across = jnp.broadcast_to(cums[e], (CHUNK, CHUNK))
                decays = jnp.exp(across - across.T + hide[k])
                own = low(jnp.where(low_lane == (e == 0), scaled, 0.0))
                reach = decays * dot(own, dy_low, NT)
                inner_grad[k] += reach
                sums = dot(low(inner[k] * reach), until)
                within.append(jnp.sum(sums * before, axis=0, keepdims=True))
                mixed.append(dot(low(inner[k] * decays), dy_low))
            back = tail * dot(b_low, flow_low)
            dxs = jnp.where(low_lane, mixed[0], mixed[1]) + back
            db_ref[here, :] += dot(low(scaled * tail), flow_low, NT)
            entered = low(dy_now * entry)
            dc_ref[here, :] += dot(entered, state_low, NT)
            brought = dy_now * entry * dot(c_low, state_low)
            ends = dot(pick, low(brought), NT)
            begins = dot(pick, low(scaled * back), NT)
            direct = dot(pick, low(x_now * dxs), NT)
            through = jnp.sum(flow[...] * states[k], axis=0, keepdims=True) * entry[CHUNK - 1 :, :]
            log_grad = exact(ends, until.astype(jnp.float32)) + exact(begins, before)
            for e in range(2):
                lanes = slice(e * SSM_DIM, (e + 1) * SSM_DIM)
                kept = jnp.sum(through[:, lanes], axis=1, keepdims=True)
                small_ref[0, e : e + 1, here] = direct[e : e + 1, :]
                small_ref[0, 2 + e : 3 + e, here] = log_grad[e : e + 1, :] + within[e] + kept
            dx_ref[here, :] = dxs * steps + skip_ref[...] * dy_now
            skip_sum += jnp.sum(x_now * dy_now, axis=0, keepdims=True)
            flow[...] = entry[CHUNK - 1 :, :] * flow[...] + dot(c_turned[:, here], entered)
        small_ref[0, 4:8, :] = jnp.zeros((4, rows), jnp.float32)
        small_ref[0, 4:5, 0 : 2 * SSM_DIM] = skip_sum

        @pl.when(pl.program_id(0) == PAIRS - 1)
        def _():
            for k in range(chunks):
                here = slice(k * CHUNK, (k + 1) * CHUNK)
                grads = low(inner_grad[k])
                db_ref[here, :] += dot(grads, low(c_ref[here, :]))
                dc_ref[here, :] += dot(grads, low(b_ref[here, :]), TN)

    whole = lambda i, m: (0, 0)
    lanes = lambda i, m: (0, i)
    pair = lambda i, m: (i, 0, 0)
    return pl.pallas_call(
        pinned(kernel, 11, after),
        grid_spec=pltpu.PrefetchScalarGridSpec(
            num_scalar_prefetch=1,
            grid=(PAIRS,),
            in_specs=[
                pl.BlockSpec((rows, 2 * SSM_DIM), lanes),
                pl.BlockSpec((rows, 2 * SSM_DIM), lanes),
                pl.BlockSpec((rows, STATE), lambda i, m: (0, PAIRS)),
                pl.BlockSpec((rows, STATE), lambda i, m: (0, PAIRS + 1)),
                pl.BlockSpec((1, 2, rows), pair),
                pl.BlockSpec((1, 2, rows), pair),
                pl.BlockSpec((STATE, 2 * SSM_DIM), lanes),
                pl.BlockSpec((STATE, 2 * SSM_DIM), lanes),
                pl.BlockSpec((1, 2 * SSM_DIM), lanes),
                pl.BlockSpec((8, rows), whole),
            ] + pins(after),
            out_specs=[
                pl.BlockSpec((rows, 2 * SSM_DIM), lanes),
                pl.BlockSpec((rows, STATE), whole),
                pl.BlockSpec((rows, STATE), whole),
                pl.BlockSpec((1, 8, rows), pair),
            ],
            scratch_shapes=[
                pltpu.VMEM((chunks, CHUNK, CHUNK), jnp.float32),
                pltpu.VMEM((chunks, CHUNK, CHUNK), jnp.float32),
                pltpu.VMEM((chunks, CHUNK, CHUNK), jnp.float32),
                pltpu.VMEM((chunks, STATE, 2 * SSM_DIM), jnp.float32),
                pltpu.VMEM((STATE, 2 * SSM_DIM), jnp.float32),
                pltpu.VMEM((STATE, rows), jnp.bfloat16),
                pltpu.VMEM((STATE, rows), jnp.bfloat16),
            ],
        ),
        out_shape=[
            jax.ShapeDtypeStruct((rows, INNER), jnp.float32),
            jax.ShapeDtypeStruct((rows, STATE), jnp.float32),
            jax.ShapeDtypeStruct((rows, STATE), jnp.float32),
            jax.ShapeDtypeStruct((PAIRS, 8, rows), jnp.float32),
        ],
        compiler_params=pltpu.CompilerParams(vmem_limit_bytes=40 * 2**20),
        cost_estimate=pl.CostEstimate(flops=3 * 10**9, bytes_accessed=rows * INNER * 12, transcendentals=2**21),
        name="ssm_back",
    )(meta, conv, dy, conv, conv, cum.reshape(PAIRS, 2, rows), step.reshape(PAIRS, 2, rows), state_in, state_grad,
      skip, start_row, *after)


def chain_states(earlier, later):
    return (earlier[0] * later[0], earlier[1] * later[0] + later[1])


def scan_states(carry, state, span, fast, backward):
    wide = jnp.repeat(carry, SSM_DIM)[None, :]
    if not fast:
        ident = (jnp.ones_like(wide), jnp.zeros_like(state))
        return (carried_in if backward else prefix)((wide, state), span, chain_states, ident)[1]
    flow = Flow(scan_stages(carry, state, backward))
    while flow.sends:
        flow.go()
    return flow.result


def scan_stages(carry, state, backward):
    total = (jnp.repeat(carry, SSM_DIM)[None, :], state)
    start = None
    for name in ("c", "x", "y"):
        place = lax.axis_index(name)
        packed = jnp.concatenate([total[1], jnp.broadcast_to(total[0], (16, INNER))], axis=0)
        (packed,) = yield [(packed.astype(jnp.bfloat16), name, SWAP)]
        packed = packed.astype(jnp.float32)
        other = (packed[STATE : STATE + 1], packed[:STATE])
        leads = place == (0 if backward else 1)
        seen = (jnp.where(leads, other[0], 1.0), jnp.where(leads, other[1], 0.0))
        start = seen if start is None else chain_states(seen, start)
        if name != "y":
            forward = chain_states(other, total)
            reverse = chain_states(total, other)
            total = jax.tree.map(lambda p, q: jnp.where(leads, p, q), forward, reverse)
    return start[1]


KEYS = 512
PAIR = 2 * HEAD_DIM


def attention_forward(q_wide, kv, meta, starts, after=()):
    rows = q_wide.shape[1]
    blocks = kv.shape[0]
    ratio = HEADS_Q // HEADS_KV
    wide = min(512, rows)

    def kernel(meta_ref, q_ref, kv_ref, start_ref, o_ref, log_ref, top, total):
        b = pl.program_id(1)

        @pl.when(b == 0)
        def _():
            top[...] = jnp.full(top.shape, masked_score, jnp.float32)
            total[...] = jnp.zeros(total.shape, jnp.float32)
            o_ref[...] = jnp.zeros(o_ref.shape, jnp.float32)

        def block(partial):
            pair = kv_ref[0, 0]
            turned = pair.T[HEAD_DIM:, :]
            for h in range(ratio):
                for r in range(0, rows, wide):
                    here = slice(r, r + wide)
                    scores = lax.dot_general(pair, q_ref[h, here, :], NT, preferred_element_type=jnp.float32)
                    if partial:
                        keys = b * KEYS + lax.broadcasted_iota(jnp.int32, scores.shape, 0)
                        mine = meta_ref[2] + r + lax.broadcasted_iota(jnp.int32, scores.shape, 1)
                        visible = (keys >= start_ref[0:1, here]) & (keys <= mine)
                        scores = jnp.where(visible, scores, masked_score)
                    before = top[h, 0:1, here]
                    peak = jnp.maximum(before, jnp.max(scores, axis=0, keepdims=True))
                    part = jnp.exp(scores - peak)
                    if partial:
                        part = jnp.where(visible, part, 0.0)
                    fade = jnp.exp(before - peak)
                    top[h, 0:1, here] = peak
                    total[h, 0:1, here] = total[h, 0:1, here] * fade + jnp.sum(part, axis=0, keepdims=True)
                    o_ref[h, :, here] = o_ref[h, :, here] * fade + jnp.dot(
                        turned, part.astype(jnp.bfloat16), preferred_element_type=jnp.float32
                    )

        needed = (b >= meta_ref[0]) & (b < meta_ref[1])
        partial = ((b + 1) * KEYS > meta_ref[2]) | (b * KEYS < meta_ref[3])

        @pl.when(needed & partial)
        def _():
            block(True)

        @pl.when(needed & jnp.logical_not(partial))
        def _():
            block(False)

        @pl.when(b == blocks - 1)
        def _():
            for h in range(ratio):
                sums = total[h, 0:1, :]
                o_ref[h] = o_ref[h] / sums
                log_ref[h] = jnp.broadcast_to(top[h, 0:1, :] + jnp.log(sums), (8, rows))

    heads = lambda g, b, m: (g, 0, 0)
    return pl.pallas_call(
        pinned(kernel, 4, after),
        grid_spec=pltpu.PrefetchScalarGridSpec(
            num_scalar_prefetch=1,
            grid=(HEADS_KV, blocks),
            in_specs=[
                pl.BlockSpec((ratio, rows, PAIR), heads),
                pl.BlockSpec((1, 1, KEYS, PAIR), lambda g, b, m: (b, g, 0, 0)),
                pl.BlockSpec((8, rows), lambda g, b, m: (0, 0)),
            ] + pins(after),
            out_specs=[
                pl.BlockSpec((ratio, HEAD_DIM, rows), heads),
                pl.BlockSpec((ratio, 8, rows), heads),
            ],
            scratch_shapes=[
                pltpu.VMEM((ratio, 8, rows), jnp.float32),
                pltpu.VMEM((ratio, 8, rows), jnp.float32),
            ],
        ),
        out_shape=[
            jax.ShapeDtypeStruct((HEADS_Q, HEAD_DIM, rows), jnp.float32),
            jax.ShapeDtypeStruct((HEADS_Q, 8, rows), jnp.float32),
        ],
        compiler_params=pltpu.CompilerParams(vmem_limit_bytes=48 * 2**20),
        cost_estimate=pl.CostEstimate(flops=2 * 10**10, bytes_accessed=2**23, transcendentals=2**23),
        name="attend",
    )(meta, q_wide, kv, starts, *after)


def attention_backward(q_wide, g_wide, kv, logs, mixed, meta, starts, group, after=()):
    rows = q_wide.shape[1]
    blocks = kv.shape[0]
    ratio = HEADS_Q // HEADS_KV
    wide = min(512, rows)

    def kernel(meta_ref, q_ref, g_ref, kv_ref, log_ref, o_ref, start_ref, dkv_ref, dq_ref, delta, sums):
        b = pl.program_id(0)

        @pl.when(b == 0)
        def _():
            dq_ref[...] = jnp.zeros(dq_ref.shape, jnp.float32)
            for h in range(ratio):
                both = g_ref[h].astype(jnp.float32).T[HEAD_DIM:, :] * o_ref[h]
                delta[h] = jnp.broadcast_to(jnp.sum(both, axis=0, keepdims=True), (8, rows))

        def block(partial):
            pair = kv_ref[0, 0]
            turned = pair.T[:HEAD_DIM, :]
            for h in range(ratio):
                for r in range(0, rows, wide):
                    here = slice(r, r + wide)
                    q_now = q_ref[h, here, :]
                    g_now = g_ref[h, here, :]
                    scores = lax.dot_general(pair, q_now, NT, preferred_element_type=jnp.float32)
                    probs = jnp.exp(scores - log_ref[h, 0:1, here])
                    if partial:
                        keys = b * KEYS + lax.broadcasted_iota(jnp.int32, scores.shape, 0)
                        mine = meta_ref[2] + r + lax.broadcasted_iota(jnp.int32, scores.shape, 1)
                        visible = (keys >= start_ref[0:1, here]) & (keys <= mine)
                        probs = jnp.where(visible, probs, 0.0)
                    grads = lax.dot_general(pair, g_now, NT, preferred_element_type=jnp.float32)
                    low_grads = (probs * (grads - delta[h, 0:1, here])).astype(jnp.bfloat16)
                    change = jnp.dot(
                        probs.astype(jnp.bfloat16), g_now, preferred_element_type=jnp.float32
                    ) + jnp.dot(low_grads, q_now, preferred_element_type=jnp.float32)
                    if h == 0 and r == 0:
                        sums[...] = change
                    else:
                        sums[...] += change
                    dq_ref[h, :, here] += jnp.dot(turned, low_grads, preferred_element_type=jnp.float32)
            dkv_ref[0, 0] = sums[...].astype(jnp.bfloat16)

        needed = (b >= meta_ref[0]) & (b < meta_ref[1])
        partial = ((b + 1) * KEYS > meta_ref[2]) | (b * KEYS < meta_ref[3])

        @pl.when(needed & partial)
        def _():
            block(True)

        @pl.when(needed & jnp.logical_not(partial))
        def _():
            block(False)

        @pl.when(jnp.logical_not(needed))
        def _():
            dkv_ref[0, 0] = jnp.zeros((KEYS, PAIR), jnp.bfloat16)

    heads = lambda b, m: (group, 0, 0)
    return pl.pallas_call(
        pinned(kernel, 7, after),
        grid_spec=pltpu.PrefetchScalarGridSpec(
            num_scalar_prefetch=1,
            grid=(blocks,),
            in_specs=[
                pl.BlockSpec((ratio, rows, PAIR), heads),
                pl.BlockSpec((ratio, rows, PAIR), heads),
                pl.BlockSpec((1, 1, KEYS, PAIR), lambda b, m: (b, group, 0, 0)),
                pl.BlockSpec((ratio, 8, rows), heads),
                pl.BlockSpec((ratio, HEAD_DIM, rows), heads),
                pl.BlockSpec((8, rows), lambda b, m: (0, 0)),
            ] + pins(after),
            out_specs=[
                pl.BlockSpec((1, 1, KEYS, PAIR), lambda b, m: (b, 0, 0, 0)),
                pl.BlockSpec((ratio, HEAD_DIM, rows), lambda b, m: (0, 0, 0)),
            ],
            scratch_shapes=[
                pltpu.VMEM((ratio, 8, rows), jnp.float32),
                pltpu.VMEM((KEYS, PAIR), jnp.float32),
            ],
        ),
        out_shape=[
            jax.ShapeDtypeStruct((blocks, 1, KEYS, PAIR), jnp.bfloat16),
            jax.ShapeDtypeStruct((ratio, HEAD_DIM, rows), jnp.float32),
        ],
        compiler_params=pltpu.CompilerParams(vmem_limit_bytes=48 * 2**20),
        cost_estimate=pl.CostEstimate(flops=2 * 10**10, bytes_accessed=2**23, transcendentals=2**23),
        name="attend_back",
    )(meta, q_wide, g_wide, kv, logs, mixed, starts, *after)


def ordered(place, own, other, axis):
    first = jnp.where(place == 0, own, other)
    second = jnp.where(place == 0, other, own)
    return jnp.stack([first, second], axis=axis)


def gather_span(value, span, fast):
    if not fast:
        return lax.all_gather(value, span)
    flow = Flow(gather_stages(value))
    while flow.sends:
        flow.go()
    return flow.result


def gather_stages(value):
    _, y, x, c = (lax.axis_index(name) for name in GRID)
    (other,) = yield [(value, "x", SWAP)]
    two = ordered(x, value, other, 0)
    (other,) = yield [(two, "y", SWAP)]
    four = ordered(y, two, other, 0)
    (other,) = yield [(four, "c", SWAP)]
    return ordered(c, four, other, 2).reshape((8,) + value.shape)


def scatter_span(value, span, fast):
    if not fast:
        return lax.psum_scatter(value, span, scatter_dimension=0).astype(jnp.float32)
    flow = Flow(scatter_stages(value))
    while flow.sends:
        flow.go()
    return flow.result


def scatter_stages(value):
    _, y, x, c = (lax.axis_index(name) for name in GRID)
    value = value.reshape((2, 2, 2) + value.shape[1:])
    for name, place, axis in (("c", c, 2), ("y", y, 0), ("x", x, 0)):
        send = lax.dynamic_index_in_dim(value, 1 - place, axis, keepdims=False)
        (arrived,) = yield [(send, name, SWAP)]
        keep = lax.dynamic_index_in_dim(value, place, axis, keepdims=False)
        value = keep.astype(jnp.float32) + arrived.astype(jnp.float32)
        if name != "x":
            value = value.astype(jnp.bfloat16)
    return value


def sum_stages(value):
    for name in GRID[1:]:
        (other,) = yield [(value, name, SWAP)]
        value = value + other
    for pairs in ([(0, 1), (1, 0), (2, 3), (3, 2)], [(0, 2), (2, 0), (1, 3), (3, 1)]):
        (other,) = yield [(value, "z", pairs)]
        value = value + other
    return value


def offsets_of():
    places, at = {}, 0
    for name_key, extent in layout():
        places[name_key] = (at, extent)
        at += math.prod(extent)
    return places


def early_weights(params):
    places = offsets_of()
    buffers, spread_flow, (slots, all_slots), where = gather_lines(params)
    spread_flow.go()
    names = (W_QUERY, W_KEY, W_VALUE, W_ATTN_OUT, W_GATE_SSM, W_X_SSM, W_B_C)
    misc_at = places[W_STEP][0]
    first = unpack_lines(
        buffers[:16], slots, where, [flat_segment(name_key) for name_key in names] + [(0, 16, LINE), (misc_at, 288, LINE)]
    )
    weights = dict(zip(names, first))
    weights[NORM_ATTN] = first[-2].reshape(-1)[:D]
    misc = first[-1].reshape(-1)
    for name_key in (W_STEP,) + small_names[1:-1]:
        at, extent = places[name_key]
        weights[name_key] = misc[at - misc_at : at - misc_at + math.prod(extent)].reshape(extent)
    return weights, spread_flow, (buffers, all_slots, where)


def flat_segment(name_key):
    at, extent = offsets_of()[name_key]
    return (at, extent[0], extent[1])


def late_weights(held, after):
    buffers, slots, where = held
    names = (W_SSM_OUT, W_GATE, W_UP_PROJ, W_DOWN)
    norm_at = offsets_of()[NORM_FFN][0]
    second = unpack_lines(
        buffers, slots, where, [flat_segment(name_key) for name_key in names] + [(norm_at, 16, LINE)], after
    )
    weights = dict(zip(names, second))
    weights[NORM_FFN] = second[-1].reshape(-1)[norm_at % LINE : norm_at % LINE + D]
    return weights


def pack_late(gate, up, down, ssm_low, grad_branch, grad_norm_ffn, after):
    places = offsets_of()
    out_at = places[W_SSM_OUT][0]
    lane = places[W_GATE][0] % LINE
    boundary = 2 * PLANE * LINE
    tail_from = (boundary - out_at) // D
    tail = matmul_left_t(ssm_low[:, tail_from:], grad_branch).reshape(-1)
    tail = tail[boundary - out_at - tail_from * D :]
    head = jnp.concatenate([jnp.zeros((14 * LINE,), jnp.float32), tail, grad_norm_ffn])
    head_rows = head.shape[0] // LINE
    carry = jnp.zeros((8, LINE), jnp.float32).at[7, :lane].set(head[head_rows * LINE :])
    head = head[: head_rows * LINE].reshape(head_rows, LINE).astype(jnp.bfloat16)
    return pack_lines(
        None, 2 * PLANE + 32, head_rows, [gate, up, down], lane, 0, [(head, 0)], carry, 48, after
    )


def pack_out(ssm_low, grad_branch, after):
    out_at = offsets_of()[W_SSM_OUT][0]
    first_row = (8 + out_at // LINE) // 16 * 16
    rows = first_row + SSM_HEADS * SSM_DIM * D // LINE
    return pack_lines(
        None, rows, first_row, [(ssm_low, grad_branch)], out_at % LINE, (8 + out_at // LINE) % 8, [],
        jnp.zeros((8, LINE), jnp.float32), 0, after,
    )


def pack_ssm(target, segments, small, ssm_low, grad_branch, after):
    places = offsets_of()
    misc = [small[name_key].reshape(-1) for name_key in (W_STEP,) + small_names[1:-1]]
    count = sum(part.shape[0] for part in misc)
    misc_rows = (count // LINE + 16) // 16 * 16
    opening = matmul_left_t(ssm_low[:, :16], grad_branch).reshape(-1)
    misc = jnp.concatenate(misc + [opening[: misc_rows * LINE - count]])
    misc = misc.reshape(misc_rows, LINE).astype(jnp.bfloat16)
    first_row = 8 + places[W_ATTN_OUT][0] // LINE
    return pack_lines(
        target, target.shape[0], first_row, segments, 0, 0, [(misc, 8 + places[W_STEP][0] // LINE)], None, 0, after
    )


def pack_qkv(segments, attended, grad_branch, grad_norm_attn, after):
    places = offsets_of()
    out_row = 8 + places[W_ATTN_OUT][0] // LINE
    rows = (8 + SHARD) // 16 * 16 + 8 * PIECE
    closing = matmul_left_t(attended[:, :16], grad_branch).reshape(-1, LINE)
    closing = closing[: rows - out_row].astype(jnp.bfloat16)
    opening = jnp.concatenate([jnp.zeros((8, LINE), jnp.float32), grad_norm_attn.reshape(-1, LINE)]).astype(jnp.bfloat16)
    return pack_lines(
        None, rows, 16, segments, 0, 0, [(opening, 0), (closing, out_row)], None, 0, after
    )


def own_lines(early, late, corner):
    z, y, x, c = (lax.axis_index(name) for name in GRID)
    place = 4 * y + 2 * x + c
    shard = SHARD * place
    start = jnp.where(z < 2, (8 + shard) % 16, (14 + shard) % 16)
    lines = jnp.where(z < 2, early, late)
    lines = jnp.where((z == 0) & (place < 2), corner[:WIN], lines)
    lines = lax.dynamic_slice(lines, (start, 0), (SHARD, LINE)).astype(jnp.float32)
    return lines.reshape(-1)


def body(span, group, fast, tokens, params, cotangent, offsets):
    rows_dev = tokens.shape[0]
    group_rows = rows_dev * lax.axis_size(span)
    all_rows = group_rows * lax.axis_size(group)
    ssm_inner = SSM_HEADS * SSM_DIM
    score_scale = HEAD_DIM ** (-0.5)
    bounds = offsets[0]
    my_start = lax.axis_index(span) * rows_dev
    row_index = my_start + jnp.arange(rows_dev, dtype=jnp.int32)
    seq_id, positions = sequence_info(row_index, bounds)
    first_start = row_index[0] - positions[0]
    last_row = my_start + rows_dev - 1
    cosine, sine = rotary_tables(positions)
    if fast:
        weights, spread_flow, held = early_weights(params)
    else:
        weights = unpack(lax.all_gather(params, group + span, axis=0, tiled=True))
    small_f32 = {name_key: weights[name_key].astype(jnp.float32) for name_key in small_names[:-1]}
    x_rows = tokens.astype(jnp.float32)
    normed_one, norm_one_back = jax.vjp(rms_norm, x_rows, small_f32[NORM_ATTN])
    hidden = normed_one.astype(jnp.bfloat16)
    query = matmul(hidden, weights[W_QUERY])
    key_raw = matmul(hidden, weights[W_KEY])
    value_low = matmul(hidden, weights[W_VALUE]).astype(jnp.bfloat16)
    q_rot = rotate(query, cosine, sine, HEADS_Q).astype(jnp.bfloat16)
    k_rot = rotate(key_raw, cosine, sine, HEADS_KV).astype(jnp.bfloat16)
    k_heads = k_rot.reshape(rows_dev, HEADS_KV, HEAD_DIM)
    v_heads = value_low.reshape(rows_dev, HEADS_KV, HEAD_DIM)
    kv_mine = jnp.concatenate([k_heads, v_heads], axis=2).transpose(1, 0, 2)
    row_starts = row_index - positions
    kv_local = kv_mine.reshape(HEADS_KV, rows_dev, PAIR)
    xbc = jnp.concatenate(
        [matmul(hidden, weights[W_X_SSM]), matmul(hidden, weights[W_B_C])], axis=1
    )
    step_raw = matmul(hidden, weights[W_STEP])
    rim_rows = passed_along(xbc[rows_dev - 8 :], span, 1)
    ssm_meta = jnp.concatenate([my_start[None], row_starts[CHUNK - 1 :: CHUNK]]).astype(jnp.int32)
    conv_bias = small_f32[CONV_BIAS][None, :]
    convolve = lambda after: conv_forward(
        xbc, rim_rows, small_f32[CONV_WEIGHT], conv_bias, ssm_meta, row_starts[:, None], after
    )
    if fast:
        keys_flow = Flow(gather_stages(kv_local))
        (conv_values,) = bracket(convolve, [keys_flow, spread_flow])
    else:
        conv_values = convolve(())
    step_in = step_raw.T + small_f32[STEP_BIAS][:, None]
    step_rows = jax.nn.softplus(step_in)
    decay = -jnp.exp(small_f32[DECAY_LOG])
    logs_step = step_rows * decay[:, None]
    order = jnp.arange(rows_dev)
    upto = (order[:, None] <= order[None, :]).astype(jnp.float32)
    cumul = jnp.dot(logs_step, upto, precision=highest)
    chunk_cum = jnp.dot(
        logs_step.reshape(-1, CHUNK), upto[:CHUNK, :CHUNK], precision=highest
    ).reshape(SSM_HEADS, rows_dev)
    went_on = row_starts < my_start
    entry_rows = jnp.where(went_on[None, :], jnp.exp(cumul), 0.0)
    in_last = row_index >= row_starts[rows_dev - 1]
    tail_rows = jnp.exp(jnp.where(in_last[None, :], cumul[:, -1:] - cumul, masked_score))
    carry_all = entry_rows[:, -1]
    summarize = lambda after: weighted_state(conv_values, PAIRS, conv_values, tail_rows * step_rows, after)
    meta = jnp.stack(
        [first_start // KEYS, last_row // KEYS + 1, my_start, row_starts[rows_dev - 1]]
    ).astype(jnp.int32)
    q_low = (q_rot * jnp.bfloat16(score_scale)).reshape(rows_dev, HEADS_Q, HEAD_DIM).transpose(1, 0, 2)
    q_wide = jnp.pad(q_low, ((0, 0), (0, 0), (0, HEAD_DIM)))
    start_row = jnp.broadcast_to(row_starts[None, :], (8, rows_dev))
    if fast:
        (local_state,) = bracket(lambda after: summarize((*after, *spread_flow.values())), [keys_flow])
        scan = Flow(scan_stages(carry_all, local_state, False))
        (gate_in,) = fence([hidden], scan.values() + keys_flow.values())
        gate_ssm = matmul(gate_in, weights[W_GATE_SSM])
        scan.go()
        keys_flow.go()
        key_blocks = keys_flow.result
        (gate_ssm,) = fence([gate_ssm], scan.values() + keys_flow.values())
        scan.go()
        mixed, logs = bracket(
            lambda after: attention_forward(
                q_wide, key_blocks, meta, start_row, (*after, gate_ssm, *spread_flow.values())
            ),
            [scan],
        )
        spread_flow.go()
        state_in = scan.result
    else:
        gate_ssm = matmul(hidden, weights[W_GATE_SSM])
        key_blocks = lax.all_gather(kv_local, span)
        if rows_dev != KEYS:
            key_blocks = key_blocks.transpose(1, 0, 2, 3).reshape(HEADS_KV, -1, KEYS, PAIR).transpose(1, 0, 2, 3)
        state_in = scan_states(carry_all, summarize(()), span, fast, False)
        mixed, logs = attention_forward(q_wide, key_blocks, meta, start_row)
    attended = mixed.astype(jnp.bfloat16).reshape(HEADS_Q * HEAD_DIM, rows_dev).T
    attn_out = matmul(attended, weights[W_ATTN_OUT])
    skip_wide = jnp.repeat(small_f32[SKIP_GAIN], SSM_DIM)[None, :]
    ssm_y = ssm_forward(
        conv_values, chunk_cum, step_rows, state_in, skip_wide, ssm_meta, row_starts[:, None], start_row
    )
    normed_ssm, gnorm_back = jax.vjp(gated_norm, ssm_y, gate_ssm, small_f32[NORM_SSM])
    ssm_low = normed_ssm.astype(jnp.bfloat16)
    if fast:
        held = (held[0] + spread_flow.result,) + held[1:]
        weights.update(late_weights(held, [ssm_y]))
    small_f32[NORM_FFN] = weights[NORM_FFN].astype(jnp.float32)
    ssm_out = matmul(ssm_low, weights[W_SSM_OUT])
    middle = x_rows + attn_out + ssm_out
    normed_two, norm_two_back = jax.vjp(rms_norm, middle, small_f32[NORM_FFN])
    hidden_two = normed_two.astype(jnp.bfloat16)
    gate_ffn = matmul(hidden_two, weights[W_GATE])
    upper = matmul(hidden_two, weights[W_UP_PROJ])
    activation_f32, swiglu_back = jax.vjp(swiglu, gate_ffn, upper)
    activation = activation_f32.astype(jnp.bfloat16)
    ffn_out = matmul(activation, weights[W_DOWN])
    result = middle + ffn_out
    squares = jnp.stack(
        [
            jnp.sum(result * result),
            jnp.sum(attn_out * attn_out),
            jnp.sum(ssm_out * ssm_out),
            jnp.sum(ffn_out * ffn_out),
        ]
    )
    grad_out = cotangent.astype(jnp.float32)
    grad_activation = matmul_right_t(cotangent, weights[W_DOWN])
    grad_gate_f32, grad_upper_f32 = swiglu_back(grad_activation)
    grad_gate = grad_gate_f32.astype(jnp.bfloat16)
    grad_upper = grad_upper_f32.astype(jnp.bfloat16)
    grad_hidden_two = matmul_right_t(grad_gate, weights[W_GATE]) + matmul_right_t(
        grad_upper, weights[W_UP_PROJ]
    )
    grad_middle_norm, grad_norm_ffn = norm_two_back(grad_hidden_two)
    grad_middle = grad_out + grad_middle_norm
    grad_branch = grad_middle.astype(jnp.bfloat16)
    grad_attended = matmul_right_t(grad_branch, weights[W_ATTN_OUT]).astype(jnp.bfloat16)
    grad_ssm_low = matmul_right_t(grad_branch, weights[W_SSM_OUT])
    grad_ssm_y, grad_gate_ssm_f32, grad_norm_ssm = gnorm_back(grad_ssm_low)
    grad_state_local = weighted_state(conv_values, PAIRS + 1, grad_ssm_y, entry_rows)
    if fast:
        scan = Flow(scan_stages(carry_all, grad_state_local, True))
        stats_flow = Flow(sum_stages(squares))
        (late,) = bracket(
            lambda after: pack_late(
                (hidden_two, grad_gate), (hidden_two, grad_upper), (activation, cotangent),
                ssm_low, grad_branch, grad_norm_ffn, after,
            ),
            [scan, stats_flow],
        )
        late_flow = Flow(reduce_stages(late, 1, 14))
        (early,) = bracket(lambda after: pack_out(ssm_low, grad_branch, after + late_flow.values()), [scan, stats_flow])
        scan.go()
        late_flow.go()
        grad_state_out = scan.result
        around = lambda call: bracket(call, [late_flow, stats_flow])
    else:
        grad_state_out = scan_states(carry_all, grad_state_local, span, fast, True)
        around = lambda call: call(())
    grad_x, grad_b, grad_c, grad_small = around(
        lambda after: ssm_backward(
            conv_values, grad_ssm_y, chunk_cum, step_rows, state_in, grad_state_out, skip_wide, ssm_meta, start_row,
            after,
        )
    )
    grad_direct = grad_small[:, 0:2].reshape(SSM_HEADS, rows_dev)
    grad_logs = grad_small[:, 2:4].reshape(SSM_HEADS, rows_dev)
    grad_decay_log = decay * jnp.sum(step_rows * grad_logs, axis=1)
    grad_step_rows = (grad_direct + decay[:, None] * grad_logs) * jax.nn.sigmoid(step_in)
    grad_step_bias = jnp.sum(grad_step_rows, axis=1)
    grad_step_raw_f32 = grad_step_rows.T
    grad_skip_gain = jnp.sum(grad_small[:, 4, : 2 * SSM_DIM].reshape(SSM_HEADS, SSM_DIM), axis=1)
    grad_main, grad_tail, grad_edge, grad_taps = around(
        lambda after: conv_backward(
            grad_x, grad_b, grad_c, xbc, rim_rows, small_f32[CONV_WEIGHT], conv_bias, ssm_meta,
            row_starts[:, None], after,
        )
    )
    grad_conv_weight = grad_taps[:CONV]
    grad_conv_bias = grad_taps[CONV]
    rim_back = passed_along(grad_edge, span, -1)
    grad_tail = grad_tail + jnp.pad(rim_back, ((8, 0), (0, 0)))
    grad_xbc = lax.dynamic_update_slice(grad_main, grad_tail.astype(jnp.bfloat16), (rows_dev - 16, 0))
    grad_gate_ssm = grad_gate_ssm_f32.astype(jnp.bfloat16)
    grad_step_raw = grad_step_raw_f32.astype(jnp.bfloat16)
    grad_w_step = matmul_left_t(hidden, grad_step_raw)
    grad_hidden_ssm = (
        matmul_right_t(grad_gate_ssm, weights[W_GATE_SSM])
        + matmul_right_t(grad_xbc[:, :ssm_inner], weights[W_X_SSM])
        + matmul_right_t(grad_xbc[:, ssm_inner:], weights[W_B_C])
        + matmul_right_t(grad_step_raw, weights[W_STEP])
    )
    small = {
        W_STEP: grad_w_step,
        CONV_WEIGHT: grad_conv_weight,
        CONV_BIAS: grad_conv_bias,
        STEP_BIAS: grad_step_bias,
        DECAY_LOG: grad_decay_log,
        SKIP_GAIN: grad_skip_gain,
        NORM_SSM: grad_norm_ssm,
        NORM_FFN: grad_norm_ffn,
    }
    parts = []
    if fast:
        (early,) = bracket(lambda after: pack_ssm(
            early,
            [
                (attended, grad_branch), (hidden, grad_gate_ssm),
                (hidden, grad_xbc[:, :ssm_inner]), (hidden, grad_xbc[:, ssm_inner:]),
            ],
            small, ssm_low, grad_branch, (*after, *late_flow.values()),
        ), [stats_flow])
        early_flow = Flow(reduce_stages(early, 0, 8))
        (grad_attended,) = fence([grad_attended], early_flow.values() + late_flow.values())
        around = lambda call: bracket(call, [early_flow])
    g_low = grad_attended.reshape(rows_dev, HEADS_Q, HEAD_DIM).transpose(1, 0, 2)
    g_wide = jnp.pad(g_low, ((0, 0), (0, 0), (HEAD_DIM, 0)))
    if fast:
        early_flow.go()
        (g_wide,) = fence([g_wide], early_flow.values())
    for group_at in range(HEADS_KV):
        after_part = [part[1] for part in parts]
        if fast and group_at == 0:
            after_part = late_flow.values()
        parts.append(
            around(
                lambda after: attention_backward(
                    q_wide, g_wide, key_blocks, logs, mixed, meta, start_row, group_at, (*after, *after_part)
                )
            )
        )
    grad_kv = jnp.concatenate([part[0] for part in parts], axis=1)
    grad_q_turned = jnp.concatenate([part[1] for part in parts], axis=0)
    if rows_dev != KEYS:
        grad_kv = grad_kv.transpose(1, 0, 2, 3).reshape(HEADS_KV, -1, rows_dev, PAIR).transpose(1, 0, 2, 3)
    if fast:
        late_flow.go([parts[-1][1]])
        scatter = Flow(scatter_stages(grad_kv))
        (grad_q_turned,) = fence([grad_q_turned], scatter.values() + early_flow.values() + late_flow.values())
    grad_q_rot = grad_q_turned.reshape(HEADS_Q * HEAD_DIM, rows_dev).T * score_scale
    grad_query_low = rotate(grad_q_rot, cosine, -sine, HEADS_Q).astype(jnp.bfloat16)
    if fast:
        scatter.go()
        early_flow.go()
        (grad_query_low,) = fence([grad_query_low], scatter.values() + early_flow.values())
    grad_hidden = grad_hidden_ssm + matmul_right_t(grad_query_low, weights[W_QUERY])
    if fast:
        scatter.go()
        (grad_hidden,) = fence([grad_hidden], scatter.values())
        scatter.go()
        grad_kv_mine = scatter.result
    else:
        grad_kv_mine = scatter_span(grad_kv, span, fast)
    grad_keys_mine = grad_kv_mine[:, :, :HEAD_DIM].transpose(1, 0, 2).reshape(rows_dev, -1)
    grad_values_mine = grad_kv_mine[:, :, HEAD_DIM:].transpose(1, 0, 2).reshape(rows_dev, -1)
    grad_key_low = rotate(grad_keys_mine, cosine, -sine, HEADS_KV).astype(jnp.bfloat16)
    grad_value_low = grad_values_mine.astype(jnp.bfloat16)
    grad_hidden = (
        grad_hidden
        + matmul_right_t(grad_key_low, weights[W_KEY])
        + matmul_right_t(grad_value_low, weights[W_VALUE])
    )
    grad_x_norm, grad_norm_attn = norm_one_back(grad_hidden)
    grad_tokens = grad_middle + grad_x_norm
    if fast:
        corner = pack_qkv(
            [(hidden, grad_query_low), (hidden, grad_key_low), (hidden, grad_value_low)],
            attended, grad_branch, grad_norm_attn, early_flow.values(),
        )
        corner_flow = Flow(corner_stages(corner))
        for _ in range(3):
            corner_flow.go()
        early_flow.go()
        ((pieces, _, _), *_) = corner_flow.sends
        (pieces,) = fence([pieces], early_flow.values())
        corner_flow.sends = [(pieces, axis, pairs) for _, axis, pairs in corner_flow.sends]
        for flow in (early_flow, late_flow, corner_flow):
            while flow.sends:
                flow.go()
        stats = jnp.sqrt(stats_flow.result / (all_rows * D))
        grad_shard = own_lines(early_flow.result, late_flow.result, corner_flow.result)
        return (result.astype(jnp.bfloat16), grad_tokens, grad_shard, stats)
    small[NORM_ATTN] = grad_norm_attn
    stats = jnp.sqrt(lax.psum(squares, group + span) / (all_rows * D))
    pairs = {
        W_QUERY: (hidden, grad_query_low),
        W_KEY: (hidden, grad_key_low),
        W_VALUE: (hidden, grad_value_low),
        W_ATTN_OUT: (attended, grad_branch),
        W_GATE_SSM: (hidden, grad_gate_ssm),
        W_X_SSM: (hidden, grad_xbc[:, :ssm_inner]),
        W_B_C: (hidden, grad_xbc[:, ssm_inner:]),
        W_SSM_OUT: (ssm_low, grad_branch),
        W_GATE: (hidden_two, grad_gate),
        W_UP_PROJ: (hidden_two, grad_upper),
        W_DOWN: (activation, cotangent),
    }
    grad_dict = dict(small)
    for name_key, (left, right) in pairs.items():
        grad_dict[name_key] = matmul_left_t(left, right)
    flat_parts = [grad_dict[name_key].reshape(-1) for name_key, extent in layout()]
    used_entries = 0
    for part_array in flat_parts:
        used_entries += part_array.shape[0]
    flat_parts.append(jnp.zeros((params.shape[0] * lax.axis_size(group + span) - used_entries,), jnp.float32))
    grad_shard = lax.psum_scatter(
        jnp.concatenate(flat_parts), group + span, scatter_dimension=0, tiled=True
    )
    return (result.astype(jnp.bfloat16), grad_tokens, grad_shard, stats)


def solution(mesh):
    fast = (mesh.shape["group"], mesh.shape["span"]) == FAST
    if fast:
        mesh = Mesh(mesh.devices.reshape(4, 2, 2, 2), GRID)
        group, span = (GRID[:1], GRID[1:])
    else:
        group, span = (("group",), ("span",))

    def program(tokens, params, cotangent, offsets):
        return body(span, group, fast, tokens, params, cotangent, offsets)

    return jax.shard_map(
        program,
        mesh=mesh,
        in_specs=(P(group + span, None), P(group + span), P(group + span, None), P(group, None)),
        out_specs=(P(group + span, None), P(group + span, None), P(group + span), P()),
        check_vma=False,
    )
```

```python
import math

import jax
import jax.numpy as jnp
import numpy as np
from jax import lax
from jax.experimental import pallas as pl
from jax.experimental.pallas import tpu as pltpu
from jax.sharding import Mesh, PartitionSpec as P

D = 1024
HEADS_Q = 8
HEADS_KV = 2
HEAD_DIM = 64
SSM_HEADS = 24
SSM_DIM = 64
STATE = 128
CONV = 4
FF = 2048
(
    NORM_ATTN,
    W_QUERY,
    W_KEY,
    W_VALUE,
    W_ATTN_OUT,
    W_GATE_SSM,
    W_X_SSM,
    W_B_C,
    W_STEP,
    CONV_WEIGHT,
    CONV_BIAS,
    STEP_BIAS,
    DECAY_LOG,
    SKIP_GAIN,
    NORM_SSM,
    W_SSM_OUT,
    NORM_FFN,
    W_GATE,
    W_UP_PROJ,
    W_DOWN,
) = range(20)


epsilon = 1e-05
rope_base = 100000000000.0
masked_score = -1e30
highest = lax.Precision.HIGHEST
small_names = (
    NORM_ATTN,
    CONV_WEIGHT,
    CONV_BIAS,
    STEP_BIAS,
    DECAY_LOG,
    SKIP_GAIN,
    NORM_SSM,
    NORM_FFN,
)


def passed_along(value, axis, steps):
    count = lax.axis_size(axis)
    first, last = (max(0, -steps), min(count, count - steps))
    return lax.ppermute(value, axis, [(source, source + steps) for source in range(first, last)])


def prefix(value, axis, combine, identity):
    peers, place = (lax.axis_size(axis), lax.axis_index(axis))
    everything = jax.tree.map(
        lambda part, kind: lax.all_gather(part.astype(kind), axis),
        value,
        (jnp.bfloat16, jnp.bfloat16),
    )
    start = jax.tree.map(
        lambda part, zero: jnp.broadcast_to(jnp.asarray(zero, part.dtype), part.shape),
        value,
        identity,
    )

    def prefix_turn(k, before):
        reached = k < place
        new = combine(
            before, jax.tree.map(lambda part, own: part[k].astype(own.dtype), everything, value)
        )
        return jax.tree.map(lambda a, b: jnp.where(reached, a, b), new, before)

    return lax.fori_loop(0, peers, prefix_turn, start)


def carried_in(value, axis, combine, identity):
    peers, place = (lax.axis_size(axis), lax.axis_index(axis))
    everything = jax.tree.map(
        lambda part, kind: lax.all_gather(part.astype(kind), axis),
        value,
        jax.tree.map(lambda a: jnp.bfloat16 if a.dtype == jnp.float32 else a.dtype, value),
    )
    start = jax.tree.map(
        lambda part, zero: jnp.broadcast_to(jnp.asarray(zero, part.dtype), part.shape),
        value,
        identity,
    )

    def carried_turn(k, before):
        at = peers - 1 - k
        reached = at > place
        new = combine(
            before, jax.tree.map(lambda part, own: part[at].astype(own.dtype), everything, value)
        )
        return jax.tree.map(lambda a, b: jnp.where(reached, a, b), new, before)

    return lax.fori_loop(0, peers, carried_turn, start)


def layout():
    ssm_inner = SSM_HEADS * SSM_DIM
    channels = ssm_inner + 2 * STATE
    return [
        (NORM_ATTN, (D,)),
        (W_QUERY, (D, HEADS_Q * HEAD_DIM)),
        (W_KEY, (D, HEADS_KV * HEAD_DIM)),
        (W_VALUE, (D, HEADS_KV * HEAD_DIM)),
        (W_ATTN_OUT, (HEADS_Q * HEAD_DIM, D)),
        (W_GATE_SSM, (D, ssm_inner)),
        (W_X_SSM, (D, ssm_inner)),
        (W_B_C, (D, 2 * STATE)),
        (W_STEP, (D, SSM_HEADS)),
        (CONV_WEIGHT, (CONV, channels)),
        (CONV_BIAS, (channels,)),
        (STEP_BIAS, (SSM_HEADS,)),
        (DECAY_LOG, (SSM_HEADS,)),
        (SKIP_GAIN, (SSM_HEADS,)),
        (NORM_SSM, (ssm_inner,)),
        (W_SSM_OUT, (ssm_inner, D)),
        (NORM_FFN, (D,)),
        (W_GATE, (D, FF)),
        (W_UP_PROJ, (D, FF)),
        (W_DOWN, (FF, D)),
    ]


def unpack(flat_vector):
    unpacked = {}
    offset = 0
    for name_key, extent in layout():
        amount = math.prod(extent)
        unpacked[name_key] = flat_vector[offset : offset + amount].reshape(extent)
        offset += amount
    return unpacked


def matmul(left, right):
    return jnp.dot(left, right, preferred_element_type=jnp.float32)


def matmul_left_t(left, right):
    return lax.dot_general(
        left, right, (((0,), (0,)), ((), ())), preferred_element_type=jnp.float32
    )


def matmul_right_t(left, right):
    return lax.dot_general(
        left, right, (((1,), (1,)), ((), ())), preferred_element_type=jnp.float32
    )


def rms_norm(values, gain):
    return values * lax.rsqrt(jnp.mean(values * values, axis=-1, keepdims=True) + epsilon) * gain


def gated_norm(ssm_y, gate_ssm, gain):
    return rms_norm(ssm_y * jax.nn.silu(gate_ssm), gain)


def swiglu(gate_ffn, upper):
    return jax.nn.silu(gate_ffn) * upper


def sequence_info(row_index, bounds):
    starts = bounds[:-1]
    inside = row_index[:, None] >= starts[None, :]
    seq_id = jnp.sum(inside.astype(jnp.int32), axis=1) - 1
    seq_start = jnp.max(jnp.where(inside, starts[None, :], 0), axis=1)
    return (seq_id, row_index - seq_start)


def rotary_tables(positions):
    half_dim = HEAD_DIM // 2
    freqs = jnp.exp(
        -jnp.arange(half_dim, dtype=jnp.float32) * (2.0 * math.log(rope_base) / HEAD_DIM)
    )
    angles = positions.astype(jnp.float32)[:, None] * freqs[None, :]
    return (jnp.cos(angles), jnp.sin(angles))


def rotate(values, cosine, sine, heads):
    row_count = values.shape[0]
    half_dim = HEAD_DIM // 2
    split_heads = values.reshape(row_count, heads, HEAD_DIM)
    first_half = split_heads[..., :half_dim]
    second_half = split_heads[..., half_dim:]
    cos_b = cosine[:, None, :]
    sin_b = sine[:, None, :]
    turned = jnp.concatenate(
        [first_half * cos_b - second_half * sin_b, second_half * cos_b + first_half * sin_b],
        axis=-1,
    )
    return turned.reshape(row_count, heads * HEAD_DIM)


def add_rows(target, addend, first_row):
    current = lax.dynamic_slice_in_dim(target, first_row, addend.shape[0], 0)
    return lax.dynamic_update_slice_in_dim(target, current + addend, first_row, 0)


FAST = (4, 8)
LINE = 128
SHARD = 3082
SPAD = 3088
WIN = 3104
PLANE = 8 * SHARD
DEPTH = 4
TALL = {1: 1024, 2: 1024, 4: 512, 8: 256, 12: 128, 16: 128}
GRID = ("z", "y", "x", "c")
ZC = ("z", "c")
SWAP = [(0, 1), (1, 0)]


def zc_pairs(*pairs):
    return [(2 * a + c, 2 * b + c) for a, b, c in pairs]


def pinned(kernel, count, after):
    return lambda *refs: kernel(*refs[:count], *refs[count + len(after) :])


def pins(after):
    return [pl.BlockSpec(memory_space=pltpu.HBM)] * len(after)


class Flow:
    def __init__(self, stages):
        self.stages = stages
        self.sends = next(stages)
        self.result = None

    def values(self):
        return [value for value, _, _ in self.sends] or (list(self.result) if isinstance(self.result, list) else [self.result])

    def go(self, after=()):
        arrived = [lax.ppermute(value, axis, pairs) for value, axis, pairs in self.sends]
        if after:
            arrived = fence(arrived, after)
        try:
            self.sends = self.stages.send(arrived)
        except StopIteration as stop:
            self.sends, self.result = [], stop.value
        return self


def fence(values, after):
    def kernel(*refs):
        del refs

    return pl.pallas_call(
        kernel,
        in_specs=pins(values) + pins(after),
        out_specs=pins(values),
        out_shape=[jax.ShapeDtypeStruct(value.shape, value.dtype) for value in values],
        input_output_aliases={k: k for k in range(len(values))},
        name="fence",
    )(*values, *after)


def bracket(call, flows):
    out = call([value for flow in flows for value in flow.values()])
    out = list(out) if isinstance(out, (list, tuple)) else [out]
    for flow in flows:
        flow.go(out[-1:])
    return fence(out, [v for flow in flows for v in flow.values()])


def gather_lines(params):
    z, y, x, c = (lax.axis_index(name) for name in GRID)
    lines = jnp.pad(params.reshape(SHARD, LINE), ((0, SPAD - SHARD), (0, 0)))
    sibling = lax.ppermute(lines, ZC, [(2 * k + 1 - k % 2, 2 * k + k % 2) for k in range(4)])
    buffers = []
    for part in range(2):
        here = jnp.where(c == part, lines, sibling)
        one = lax.ppermute(here, ZC, zc_pairs((0, 1, 0), (1, 2, 1)))
        side = lax.ppermute(here, ZC, zc_pairs((1, 0, 1)))
        two = lax.ppermute(one, ZC, zc_pairs((1, 2, 0), (2, 3, 1)))
        three = lax.ppermute(two, ZC, zc_pairs((2, 3, 0)))
        column = jnp.where(z == c, here, one + side + two + three)
        over_x = lax.ppermute(column, "x", SWAP)
        over_y = lax.ppermute(column, "y", SWAP)
        corner = lax.ppermute(over_y if part else over_x, "x" if part else "y", SWAP)
        local = [column, over_x, over_y, corner]
        buffers += [piece[None] for piece in local]
        buffers += [lax.ppermute(piece, "c", SWAP)[None] for piece in local]
    early = [(k, 0) for k in range(16)]
    here = jnp.where(c == 0, jnp.stack([lines, sibling]), jnp.stack([sibling, lines]))
    one = lax.ppermute(here, ZC, zc_pairs((2, 1, 0), (3, 2, 1)))
    side = lax.ppermute(here, ZC, zc_pairs((2, 3, 0)))
    two = lax.ppermute(one, ZC, zc_pairs((1, 0, 0), (2, 1, 1)))
    three = lax.ppermute(two, ZC, zc_pairs((1, 0, 1)))
    column = jnp.where(z == 2 + c, here, one + side + two + three)
    late = []
    for part in range(2):
        for first in (16, 20):
            late += [(first + k, part) for k in range(4)]
    shard = np.arange(32)
    sz, sy, sx, sc = shard // 8, shard // 4 % 2, shard // 2 % 2, shard % 2
    away = jnp.where(sz % 2 == c, 0, 4)
    where = sc * 8 + away + 2 * (sy ^ y) + (sx ^ x) + 16 * (sz // 2)
    return buffers, Flow(spread_stages(column)), (early, early + late), where.astype(jnp.int32)


def spread_stages(column):
    over_x, over_y = yield [(column, "x", SWAP), (column, "y", SWAP)]
    corners = yield [(over_x[:1], "y", SWAP), (over_y[1:], "x", SWAP)]
    local = [column, over_x, over_y, jnp.concatenate(corners)]
    return local + list((yield [(piece, "c", SWAP) for piece in local]))


def unpack_lines(buffers, slots, where, segments, after=()):
    jobs, starts = [], []
    reach = 0
    for offset, rows, columns in segments:
        per_row = columns // LINE
        lane, base = offset % LINE, offset // LINE
        if per_row == 1 and rows < 1024:
            lane, tall = 0, rows
        else:
            tall = TALL[per_row]
        starts.append(len(jobs))
        for k in range(rows // tall):
            jobs.append((base + k * tall * per_row, tall * per_row, 1 if lane else 0))
    window = max(job[1] for job in jobs) + 32
    table = np.zeros((len(jobs), 5), np.int32)
    for k, (line, count, extra) in enumerate(jobs):
        owner = line // SHARD
        inside = line - owner * SHARD
        begin = min(inside // 16 * 16, SPAD - window)
        crosses = int(line + count + extra > (owner + 1) * SHARD)
        table[k] = (owner, begin, begin - inside, crosses, (owner + 1) * SHARD - line)
    base_row = (int(-table[:, 2].min()) + 7) // 8 * 8
    table[:, 2] += base_row
    table[:, 4] += base_row
    room = int(max((table[:, 2] + window).max(), ((table[:, 4] + window) * table[:, 3]).max()))
    room = (room + 15) // 8 * 8
    total = len(jobs)
    count_buffers = len(buffers)
    shapes = []
    for offset, rows, columns in segments:
        per_row = columns // LINE
        tall = rows if per_row == 1 and rows < 1024 else TALL[per_row]
        shapes.append((rows, columns, tall, per_row, offset % LINE if tall != rows or per_row != 1 else 0))
    sizes = sorted({(tall, columns) for _, columns, tall, _, _ in shapes})

    def kernel(table_ref, where_ref, *refs):
        sources = refs[:count_buffers]
        outs = refs[count_buffers : count_buffers + len(segments)]
        rest = refs[count_buffers + len(segments) :]
        stages = dict(zip(sizes, rest))
        raw, flat, in_sem, out_sem = rest[len(sizes) :]
        step = pl.program_id(0)

        def fetch(job, slot):
            owner = table_ref[job, 0]
            begin = pl.multiple_of(table_ref[job, 1], 16)
            for b, (source, part) in enumerate(slots):

                @pl.when(where_ref[owner] == b)
                def _():
                    pltpu.make_async_copy(
                        sources[source].at[part, pl.ds(begin, window), :], raw.at[slot, 0], in_sem.at[slot, 0]
                    ).start()

            @pl.when(table_ref[job, 3] == 1)
            def _():
                for b, (source, part) in enumerate(slots):

                    @pl.when(where_ref[owner + 1] == b)
                    def _():
                        pltpu.make_async_copy(
                            sources[source].at[part, pl.ds(0, window), :], raw.at[slot, 1], in_sem.at[slot, 1]
                        ).start()

        def fetched(slot, half):
            return pltpu.make_async_copy(
                sources[0].at[0, pl.ds(0, window), :], raw.at[slot, half], in_sem.at[slot, half]
            )

        @pl.when(step == 0)
        def _():
            for k in range(min(DEPTH - 1, total)):
                fetch(k, k)

        @pl.when(step + DEPTH - 1 < total)
        def _():
            fetch(step + DEPTH - 1, lax.rem(step + DEPTH - 1, DEPTH))

        slot = lax.rem(step, DEPTH)
        fetched(slot, 0).wait()
        flat[pl.ds(table_ref[step, 2], window), :] = raw[slot, 0].astype(jnp.float32)

        @pl.when(table_ref[step, 3] == 1)
        def _():
            fetched(slot, 1).wait()
            flat[pl.ds(table_ref[step, 4], window), :] = raw[slot, 1].astype(jnp.float32)

        for index, (rows, columns, tall, per_row, lane) in enumerate(shapes):
            begin = starts[index]
            blocks = rows // tall
            stage = stages[(tall, columns)]

            @pl.when((step >= begin) & (step < begin + blocks))
            def _():
                block = step - begin
                side = lax.rem(block, DEPTH)

                def written(k, s):
                    return pltpu.make_async_copy(
                        stage.at[s],
                        outs[index].at[pl.ds(pl.multiple_of(k * tall, 16), tall), :],
                        out_sem.at[s],
                    )

                @pl.when(block >= DEPTH)
                def _():
                    written(block - DEPTH, side).wait()

                def tile(j):
                    picked = flat[pl.ds(base_row + j, tall, stride=per_row), :]
                    return pltpu.roll(picked, LINE - lane, 1) if lane else picked

                if lane:
                    lanes = lax.broadcasted_iota(jnp.int32, (tall, LINE), 1)
                    now = tile(0)
                    for j in range(per_row):
                        later = tile(j + 1)
                        stage[side, :, j * LINE : (j + 1) * LINE] = jnp.where(
                            lanes < LINE - lane, now, later
                        ).astype(jnp.bfloat16)
                        now = later
                else:
                    for j in range(per_row):
                        stage[side, :, j * LINE : (j + 1) * LINE] = tile(j).astype(jnp.bfloat16)
                written(block, side).start()

                @pl.when(block == blocks - 1)
                def _():
                    for back in reversed(range(min(DEPTH, blocks))):
                        written(block - back, lax.rem(block - back, DEPTH)).wait()

    return pl.pallas_call(
        pinned(kernel, 2 + count_buffers, after),
        grid_spec=pltpu.PrefetchScalarGridSpec(
            num_scalar_prefetch=2,
            grid=(total,),
            in_specs=[pl.BlockSpec(memory_space=pl.ANY)] * count_buffers + pins(after),
            out_specs=[pl.BlockSpec(memory_space=pl.ANY)] * len(segments),
            scratch_shapes=[pltpu.VMEM((DEPTH,) + size, jnp.bfloat16) for size in sizes]
            + [
                pltpu.VMEM((DEPTH, 2, window, LINE), jnp.bfloat16),
                pltpu.VMEM((room, LINE), jnp.float32),
                pltpu.SemaphoreType.DMA((DEPTH, 2)),
                pltpu.SemaphoreType.DMA((DEPTH,)),
            ],
        ),
        out_shape=[jax.ShapeDtypeStruct((rows, columns), jnp.bfloat16) for _, rows, columns in segments],
        compiler_params=pltpu.CompilerParams(vmem_limit_bytes=48 * 2**20),
        cost_estimate=pl.CostEstimate(flops=0, bytes_accessed=total * window * LINE * 4, transcendentals=0),
        name="unpack",
    )(jnp.asarray(table), where, *buffers, *after)


def pack_lines(target, target_rows, first_row, segments, lane, phase, extras, carry, tail_rows, after=()):
    tall = 256
    lefts, rights, plan = [], [], []
    left_of, right_of = {}, {}
    row = first_row
    begin = 0
    for left, right in segments:
        for value, seen, kept in ((left, left_of, lefts), (right, right_of, rights)):
            if id(value) not in seen:
                seen[id(value)] = len(kept)
                kept.append(value)
        blocks = left.shape[1] // tall
        plan.append((left_of[id(left)], right_of[id(right)], right.shape[1] // LINE, begin, blocks, row))
        begin += blocks
        row += left.shape[1] * right.shape[1] // LINE
    end_row = row
    total = begin
    biggest = max(entry[2] for entry in plan) * tall
    tokens = lefts[0].shape[0]
    count_left, count_right, count_extra = len(lefts), len(rights), len(extras)
    rolled = [jnp.roll(right, lane, axis=1) if lane else right for right in rights]
    carry_in = [carry] if lane else []
    targets = [] if target is None else [target]

    def left_spec(index):
        mine = [entry for entry in plan if entry[0] == index]

        def place(step):
            block = 0
            for _, _, _, start, blocks, _ in mine:
                block = jnp.where(step >= start, jnp.minimum(step - start, blocks - 1), block)
            return (0, block)

        return pl.BlockSpec((tokens, tall), place)

    def kernel(*refs):
        left_refs = refs[:count_left]
        right_refs = refs[count_left : count_left + count_right]
        at = count_left + count_right
        extra_refs = refs[at : at + count_extra]
        at += count_extra
        carry_refs = refs[at : at + len(carry_in)]
        at += len(carry_in) + len(targets)
        out = refs[at]
        flat, stage, shift, last, sems, extra_sems = refs[at + 1 :]
        step = pl.program_id(0)
        side = lax.rem(step, 2)

        def extra_copy(k):
            rows = extras[k][0].shape[0]
            return pltpu.make_async_copy(
                extra_refs[k], out.at[pl.ds(extras[k][1], rows), :], extra_sems.at[k]
            )

        @pl.when(step == 0)
        def _():
            for k in range(count_extra):
                extra_copy(k).start()
            if lane:
                shift[0:8, :] = carry_refs[0][...]
            if phase:
                flat[0:8, :] = jnp.zeros((8, LINE), jnp.float32)

        for left_at, right_at, per_row, start, blocks, row in plan:
            lines = per_row * tall

            def written(block, s, row=row, lines=lines):
                return pltpu.make_async_copy(
                    stage.at[s, pl.ds(0, lines), :],
                    out.at[pl.ds(pl.multiple_of(row + block * lines, 16), lines), :],
                    sems.at[s],
                )

            @pl.when((step >= start) & (step < start + blocks))
            def _():
                block = step - start
                if phase:

                    @pl.when(step > 0)
                    def _():
                        flat[0:8, :] = flat[lines : lines + 8, :]

                turned = left_refs[left_at][...].T
                lanes = lax.broadcasted_iota(jnp.int32, (tall, LINE), 1)
                for j0 in range(0, per_row, 2):
                    wide = min(2, per_row - j0)
                    tile = jnp.dot(
                        turned,
                        right_refs[right_at][:, j0 * LINE : (j0 + wide) * LINE],
                        preferred_element_type=jnp.float32,
                    )
                    for j in range(wide):
                        piece = tile[:, j * LINE : (j + 1) * LINE]
                        if lane and j0 + j == 0:
                            shift[8 : 8 + tall, :] = piece
                            piece = jnp.where(lanes < lane, shift[7 : 7 + tall, :], piece)
                            shift[0:8, :] = shift[tall : tall + 8, :]
                        if per_row == 1:
                            flat[phase : phase + tall, :] = piece
                        else:
                            flat[pl.ds(phase + j0 + j, tall, stride=per_row), :] = piece

                stage[side, 0:lines, :] = flat[0:lines, :].astype(jnp.bfloat16)
                written(block, side).start()

            @pl.when((step > start) & (step <= start + blocks))
            def _():
                written(step - start - 1, 1 - side).wait()

            if start + blocks == total:

                @pl.when(step == total - 1)
                def _():
                    written(blocks - 1, side).wait()

        @pl.when(step == total - 1)
        def _():
            if tail_rows:
                lanes = lax.broadcasted_iota(jnp.int32, (tail_rows, LINE), 1)
                rows_at = lax.broadcasted_iota(jnp.int32, (tail_rows, LINE), 0)
                final = jnp.broadcast_to(shift[7:8, :], (tail_rows, LINE))
                last[...] = jnp.where((rows_at == 0) & (lanes < lane), final, 0.0).astype(jnp.bfloat16)
                closing = pltpu.make_async_copy(
                    last, out.at[pl.ds(end_row, tail_rows), :], extra_sems.at[count_extra]
                )
                closing.start()
                closing.wait()
            for k in range(count_extra):
                extra_copy(k).wait()

    whole = [pl.BlockSpec(array.shape, lambda step: (0, 0)) for array in rolled]
    flops = sum(2 * tokens * entry[4] * tall * entry[2] * LINE for entry in plan)
    inputs = count_left + count_right + count_extra + len(carry_in) + len(targets)
    return pl.pallas_call(
        pinned(kernel, inputs, after),
        grid=(total,),
        in_specs=[left_spec(k) for k in range(count_left)]
        + whole
        + [pl.BlockSpec(array.shape, lambda step: (0, 0)) for array, _ in extras]
        + [pl.BlockSpec(array.shape, lambda step: (0, 0)) for array in carry_in]
        + [pl.BlockSpec(memory_space=pl.ANY)] * len(targets)
        + pins(after),
        out_specs=pl.BlockSpec(memory_space=pl.ANY),
        out_shape=jax.ShapeDtypeStruct((target_rows, LINE), jnp.bfloat16),
        scratch_shapes=[
            pltpu.VMEM((biggest + 16, LINE), jnp.float32),
            pltpu.VMEM((2, biggest, LINE), jnp.bfloat16),
            pltpu.VMEM((tall + 8, LINE), jnp.float32),
            pltpu.VMEM((max(tail_rows, 16), LINE), jnp.bfloat16),
            pltpu.SemaphoreType.DMA((2,)),
            pltpu.SemaphoreType.DMA((count_extra + 1,)),
        ],
        input_output_aliases={count_left + count_right + count_extra + len(carry_in): 0} if targets else {},
        compiler_params=pltpu.CompilerParams(vmem_limit_bytes=48 * 2**20),
        cost_estimate=pl.CostEstimate(flops=flops, bytes_accessed=total * biggest * LINE * 2, transcendentals=0),
        name="pack",
    )(*lefts, *rolled, *[array for array, _ in extras], *carry_in, *targets, *after)


def added(*parts):
    total = parts[0].astype(jnp.float32)
    for part in parts[1:]:
        total = total + part.astype(jnp.float32)
    return total.astype(jnp.bfloat16)


def reduce_stages(flat, batch, shift):
    z, y, x, c = (lax.axis_index(name) for name in GRID)
    length = PLANE + 32
    send = lax.dynamic_slice(flat, ((1 - c) * PLANE, 0), (length, LINE))
    (arrived,) = yield [(send, "c", SWAP)]
    chip = added(lax.dynamic_slice(flat, (c * PLANE, 0), (length, LINE)), arrived)

    def window(sy, sx, part):
        shard = sy * 4 + sx * 2 + part
        start = (shift + SHARD * shard) // 16 * 16
        return lax.dynamic_slice(chip, (start, 0), (WIN, LINE))

    away_0 = jnp.stack([window(1 - y, 0, 0), window(1 - y, 1, 0)])
    away_1 = jnp.stack([window(0, 1 - x, 1), window(1, 1 - x, 1)])
    home_0 = jnp.stack([window(y, 0, 0), window(y, 1, 0)])
    home_1 = jnp.stack([window(0, x, 1), window(1, x, 1)])
    got_0, got_1 = yield [(away_0, "y", SWAP), (away_1, "x", SWAP)]
    half_0, half_1 = added(home_0, got_0), added(home_1, got_1)
    pick = lambda value, at: lax.dynamic_index_in_dim(value, at, 0, keepdims=False)
    got_0, got_1 = yield [(pick(half_0, 1 - x), "x", SWAP), (pick(half_1, 1 - y), "y", SWAP)]
    columns = [added(pick(half_0, x), got_0), added(pick(half_1, y), got_1)]
    if batch == 0:
        hops = [((1, 0, 0), (2, 1, 1)), ((2, 0, 0), (3, 1, 1)), ((3, 0, 0), (0, 1, 1))]
    else:
        hops = [((1, 2, 0), (2, 3, 1)), ((0, 2, 0), (1, 3, 1)), ((3, 2, 0), (0, 3, 1))]
    if batch == 0:
        got = yield [(columns[0], ZC, zc_pairs(*hop)) for hop in hops]
        end = added(columns[0], *got)
        (column,) = fence(columns[1:], [end])
        got = yield [(column, ZC, zc_pairs(*hop)) for hop in hops]
        ends = [end, added(column, *got)]
    else:
        columns = jnp.stack(columns)
        got = yield [(columns, ZC, zc_pairs(*hop)) for hop in hops]
        ends = added(columns, *got)
    mine = jnp.where(c == 0, ends[0], ends[1])
    other = jnp.where(c == 0, ends[1], ends[0])
    (handed,) = yield [(other, ZC, [(2 * k + k % 2, 2 * k + 1 - k % 2) for k in range(4)])]
    return jnp.where(c == z % 2, mine, handed)


PIECE = 400


def corner_stages(flat):
    z, y, x, c = (lax.axis_index(name) for name in GRID)
    length = 8 * PIECE
    second = (8 + SHARD) // 16 * 16
    take = lambda at: lax.dynamic_slice(flat, (at * second, 0), (length, LINE))
    (arrived,) = yield [(take(1 - c), "c", SWAP)]
    chip = added(take(c), arrived).reshape(2, 2, 2, PIECE, LINE)
    pick = lambda value, at: lax.dynamic_index_in_dim(value, at, 0, keepdims=False)
    got = yield [(pick(chip[0], 1 - x), "x", SWAP), (pick(chip[1], 1 - y), "y", SWAP)]
    halves = [added(pick(chip[0], x), got[0]), added(pick(chip[1], y), got[1])]
    got = yield [(pick(halves[0], 1 - y), "y", SWAP), (pick(halves[1], 1 - x), "x", SWAP)]
    pieces = jnp.stack([added(pick(halves[0], y), got[0]), added(pick(halves[1], x), got[1])])
    got = yield [(pieces, "z", [(k, 0)]) for k in (1, 2, 3)]
    pieces = added(pieces, *got)
    got = yield [(pieces[0], "y", [(1, 0)]), (pieces[1], "x", [(1, 0)])]
    halves = [jnp.stack([pieces[0], got[0]]), jnp.stack([pieces[1], got[1]])]
    got = yield [(halves[0], "x", [(1, 0)]), (halves[1], "y", [(1, 0)])]
    return jnp.stack([halves[0], got[0], halves[1], got[1]]).reshape(length, LINE)


CHUNK = 128
NT = (((1,), (1,)), ((), ()))
TN = (((0,), (0,)), ((), ()))
INNER = SSM_HEADS * SSM_DIM
PAIRS = SSM_HEADS // 2


def spread(rows_a, rows_b):
    length = rows_a.shape[1]
    tall = jnp.concatenate(
        [jnp.broadcast_to(rows_a, (SSM_DIM, length)), jnp.broadcast_to(rows_b, (SSM_DIM, length))], axis=0
    )
    return tall.T


CHANNELS = INNER + 2 * STATE
LANES = 2 * SSM_DIM
COLUMNS = CHANNELS // LANES


def conv_parts(ext, weight_ref, bias_ref, start_ref, first, rows):
    place = first + lax.broadcasted_iota(jnp.int32, (rows, 1), 0) - start_ref[...]
    windows = []
    total = bias_ref[...]
    for tap in range(CONV):
        reach = CONV - 1 - tap
        window = jnp.where(place >= reach, ext[8 - reach : 8 - reach + rows, :], 0.0)
        windows.append(window)
        total = total + window * weight_ref[tap : tap + 1, :]
    return place, windows, total


def conv_forward(xbc, rim, weight, bias, meta, start_column, after=()):
    rows = xbc.shape[0]

    def kernel(meta_ref, x_ref, rim_ref, weight_ref, bias_ref, start_ref, out_ref, ext):
        ext[0:8, :] = rim_ref[...]
        ext[8:, :] = x_ref[...]
        _, _, total = conv_parts(ext, weight_ref, bias_ref, start_ref, meta_ref[0], rows)
        out_ref[...] = total * jax.nn.sigmoid(total)

    lanes = lambda i, m: (0, i)
    return pl.pallas_call(
        pinned(kernel, 6, after),
        grid_spec=pltpu.PrefetchScalarGridSpec(
            num_scalar_prefetch=1,
            grid=(COLUMNS,),
            in_specs=[
                pl.BlockSpec((rows, LANES), lanes),
                pl.BlockSpec((8, LANES), lanes),
                pl.BlockSpec((CONV, LANES), lanes),
                pl.BlockSpec((1, LANES), lanes),
                pl.BlockSpec((rows, 1), lambda i, m: (0, 0)),
            ] + pins(after),
            out_specs=pl.BlockSpec((rows, LANES), lanes),
            scratch_shapes=[pltpu.VMEM((rows + 8, LANES), jnp.float32)],
        ),
        out_shape=jax.ShapeDtypeStruct((rows, CHANNELS), jnp.float32),
        cost_estimate=pl.CostEstimate(flops=10**9, bytes_accessed=rows * CHANNELS * 8, transcendentals=0),
        name="conv",
    )(meta, xbc, rim, weight, bias, start_column, *after)


def conv_backward(dx, db, dc, xbc, rim, weight, bias, meta, start_column, after=()):
    rows = xbc.shape[0]

    def kernel(meta_ref, dx_ref, db_ref, dc_ref, x_ref, rim_ref, weight_ref, bias_ref, start_ref,
               low_ref, tail_ref, edge_ref, small_ref, ext, upper):
        ext[0:8, :] = rim_ref[...]
        ext[8:, :] = x_ref[...]
        at = pl.program_id(0)
        arrived = jnp.where(at < PAIRS, dx_ref[...], jnp.where(at == PAIRS, db_ref[...], dc_ref[...]))
        place, windows, total = conv_parts(ext, weight_ref, bias_ref, start_ref, meta_ref[0], rows)
        gate = jax.nn.sigmoid(total)
        change = arrived * gate * (1.0 + total * (1.0 - gate))
        upper[0:8, :] = jnp.zeros((8, LANES), jnp.float32)
        upper[8 + rows :, :] = jnp.zeros((8, LANES), jnp.float32)
        main = jnp.zeros((rows, LANES), jnp.float32)
        edge = jnp.zeros((8, LANES), jnp.float32)
        small_ref[...] = jnp.zeros((8, LANES), jnp.float32)
        small_ref[CONV : CONV + 1, :] = jnp.sum(change, axis=0, keepdims=True)
        for tap in range(CONV):
            reach = CONV - 1 - tap
            small_ref[tap : tap + 1, :] = jnp.sum(change * windows[tap], axis=0, keepdims=True)
            upper[8 : 8 + rows, :] = jnp.where(place >= reach, change, 0.0) * weight_ref[tap : tap + 1, :]
            main = main + upper[8 + reach : 8 + reach + rows, :]
            edge = edge + upper[reach : reach + 8, :]
        low_ref[...] = main.astype(jnp.bfloat16)
        tail_ref[...] = main[rows - 16 :, :]
        edge_ref[...] = edge

    lanes = lambda i, m: (0, i)
    whole = lambda i, m: (0, 0)
    return pl.pallas_call(
        pinned(kernel, 9, after),
        grid_spec=pltpu.PrefetchScalarGridSpec(
            num_scalar_prefetch=1,
            grid=(COLUMNS,),
            in_specs=[
                pl.BlockSpec((rows, LANES), lambda i, m: (0, jnp.minimum(i, PAIRS - 1))),
                pl.BlockSpec((rows, STATE), whole),
                pl.BlockSpec((rows, STATE), whole),
                pl.BlockSpec((rows, LANES), lanes),
                pl.BlockSpec((8, LANES), lanes),
                pl.BlockSpec((CONV, LANES), lanes),
                pl.BlockSpec((1, LANES), lanes),
                pl.BlockSpec((rows, 1), whole),
            ] + pins(after),
            out_specs=[
                pl.BlockSpec((rows, LANES), lanes),
                pl.BlockSpec((16, LANES), lanes),
                pl.BlockSpec((8, LANES), lanes),
                pl.BlockSpec((8, LANES), lanes),
            ],
            scratch_shapes=[
                pltpu.VMEM((rows + 8, LANES), jnp.float32),
                pltpu.VMEM((rows + 16, LANES), jnp.float32),
            ],
        ),
        out_shape=[
            jax.ShapeDtypeStruct((rows, CHANNELS), jnp.bfloat16),
            jax.ShapeDtypeStruct((16, CHANNELS), jnp.float32),
            jax.ShapeDtypeStruct((8, CHANNELS), jnp.float32),
            jax.ShapeDtypeStruct((8, CHANNELS), jnp.float32),
        ],
        cost_estimate=pl.CostEstimate(flops=2 * 10**9, bytes_accessed=rows * CHANNELS * 10, transcendentals=0),
        name="conv_back",
    )(meta, dx, db, dc, xbc, rim, weight, bias, start_column, *after)


def weighted_state(left, left_block, values, weight_rows, after=()):
    rows = left.shape[0]

    def kernel(left_ref, value_ref, weight_ref, out_ref, turned):
        @pl.when(pl.program_id(0) == 0)
        def _():
            turned[...] = left_ref[...].T.astype(jnp.bfloat16)

        wide = spread(weight_ref[0, 0:1, :], weight_ref[0, 1:2, :])
        scaled = (value_ref[...] * wide).astype(jnp.bfloat16)
        out_ref[...] = jnp.dot(turned[...], scaled, preferred_element_type=jnp.float32)

    return pl.pallas_call(
        pinned(kernel, 3, after),
        grid=(PAIRS,),
        in_specs=[
            pl.BlockSpec((rows, STATE), lambda i: (0, left_block)),
            pl.BlockSpec((rows, 2 * SSM_DIM), lambda i: (0, i)),
            pl.BlockSpec((1, 2, rows), lambda i: (i, 0, 0)),
        ] + pins(after),
        out_specs=pl.BlockSpec((STATE, 2 * SSM_DIM), lambda i: (0, i)),
        out_shape=jax.ShapeDtypeStruct((STATE, INNER), jnp.float32),
        scratch_shapes=[pltpu.VMEM((STATE, rows), jnp.bfloat16)],
        cost_estimate=pl.CostEstimate(flops=2 * rows * STATE * INNER, bytes_accessed=rows * INNER * 4, transcendentals=0),
        name="state",
    )(left, values, weight_rows.reshape(PAIRS, 2, rows), *after)


def chunk_rows(k, meta_ref, cum_ref, start_ref):
    here = slice(k * CHUNK, (k + 1) * CHUNK)
    first = meta_ref[0] + k * CHUNK
    index = first + lax.broadcasted_iota(jnp.int32, (1, CHUNK), 1)
    entering = start_ref[0:1, here] < first
    ending = index >= meta_ref[1 + k]
    cums, entries, tails = [], [], []
    for e in range(2):
        cum = cum_ref[0, e : e + 1, here]
        cums.append(cum)
        entries.append(jnp.where(entering, jnp.exp(cum), 0.0))
        gap = jnp.where(ending, cum[:, CHUNK - 1 :] - cum, masked_score)
        tails.append(jnp.exp(gap))
    return cums, entries, tails


def ssm_forward(conv, cum, step, state_in, skip, meta, start_column, start_row):
    rows = conv.shape[0]
    chunks = rows // CHUNK

    def kernel(meta_ref, x_ref, b_ref, c_ref, cum_ref, step_ref, state_ref, skip_ref, col_ref, row_ref,
               y_ref, inner, hide, state, b_turned):
        @pl.when(pl.program_id(0) == 0)
        def _():
            for k in range(chunks):
                here = slice(k * CHUNK, (k + 1) * CHUNK)
                b_turned[:, here] = b_ref[here, :].T.astype(jnp.bfloat16)
                inner[k] = lax.dot_general(
                    c_ref[here, :], b_ref[here, :], NT, precision=highest, preferred_element_type=jnp.float32
                )
                t = lax.broadcasted_iota(jnp.int32, (CHUNK, CHUNK), 0)
                s = lax.broadcasted_iota(jnp.int32, (CHUNK, CHUNK), 1)
                shown = (s <= t) & (meta_ref[0] + k * CHUNK + s >= col_ref[here, :])
                hide[k] = jnp.where(shown, 0.0, masked_score)

        low_lane = lax.broadcasted_iota(jnp.int32, (CHUNK, 2 * SSM_DIM), 1) < SSM_DIM
        state[...] = state_ref[...]
        for k in range(chunks):
            here = slice(k * CHUNK, (k + 1) * CHUNK)
            cums, entries, tails = chunk_rows(k, meta_ref, cum_ref, row_ref)
            x_now = x_ref[here, :]
            x_low = x_now.astype(jnp.bfloat16)
            entry = spread(*entries)
            weight = spread(*[tails[e] * step_ref[0, e : e + 1, here] for e in range(2)])
            parts = []
            for e in range(2):
                across = jnp.broadcast_to(cums[e], (CHUNK, CHUNK))
                decays = jnp.exp(across.T - across + hide[k])
                mix = (inner[k] * decays * step_ref[0, e : e + 1, here]).astype(jnp.bfloat16)
                parts.append(jnp.dot(mix, x_low, preferred_element_type=jnp.float32))
            carried = jnp.dot(
                c_ref[here, :].astype(jnp.bfloat16), state[...].astype(jnp.bfloat16),
                preferred_element_type=jnp.float32,
            )
            y_ref[here, :] = jnp.where(low_lane, parts[0], parts[1]) + entry * carried + skip_ref[...] * x_now
            fresh = jnp.dot(
                b_turned[:, here], (x_now * weight).astype(jnp.bfloat16), preferred_element_type=jnp.float32
            )
            state[...] = entry[CHUNK - 1 :, :] * state[...] + fresh

    whole = lambda i, m: (0, 0)
    lanes = lambda i, m: (0, i)
    return pl.pallas_call(
        kernel,
        grid_spec=pltpu.PrefetchScalarGridSpec(
            num_scalar_prefetch=1,
            grid=(PAIRS,),
            in_specs=[
                pl.BlockSpec((rows, 2 * SSM_DIM), lanes),
                pl.BlockSpec((rows, STATE), lambda i, m: (0, PAIRS)),
                pl.BlockSpec((rows, STATE), lambda i, m: (0, PAIRS + 1)),
                pl.BlockSpec((1, 2, rows), lambda i, m: (i, 0, 0)),
                pl.BlockSpec((1, 2, rows), lambda i, m: (i, 0, 0)),
                pl.BlockSpec((STATE, 2 * SSM_DIM), lanes),
                pl.BlockSpec((1, 2 * SSM_DIM), lanes),
                pl.BlockSpec((rows, 1), whole),
                pl.BlockSpec((8, rows), whole),
            ],
            out_specs=pl.BlockSpec((rows, 2 * SSM_DIM), lanes),
            scratch_shapes=[
                pltpu.VMEM((chunks, CHUNK, CHUNK), jnp.float32),
                pltpu.VMEM((chunks, CHUNK, CHUNK), jnp.float32),
                pltpu.VMEM((STATE, 2 * SSM_DIM), jnp.float32),
                pltpu.VMEM((STATE, rows), jnp.bfloat16),
            ],
        ),
        out_shape=jax.ShapeDtypeStruct((rows, INNER), jnp.float32),
        compiler_params=pltpu.CompilerParams(vmem_limit_bytes=40 * 2**20),
        cost_estimate=pl.CostEstimate(flops=10**9, bytes_accessed=rows * INNER * 8, transcendentals=2**21),
        name="ssm",
    )(meta, conv, conv, conv, cum.reshape(PAIRS, 2, rows), step.reshape(PAIRS, 2, rows), state_in, skip,
      start_column, start_row)


def ssm_backward(conv, dy, cum, step, state_in, state_grad, skip, meta, start_row, after=()):
    rows = conv.shape[0]
    chunks = rows // CHUNK

    def kernel(meta_ref, x_ref, dy_ref, b_ref, c_ref, cum_ref, step_ref, state_ref, grad_ref, skip_ref, row_ref,
               dx_ref, db_ref, dc_ref, small_ref, inner, hide, inner_grad, states, flow,
               b_turned, c_turned):
        low = lambda v: v.astype(jnp.bfloat16)
        dot = lambda p, q, dims=(((1,), (0,)), ((), ())): lax.dot_general(
            p, q, dims, preferred_element_type=jnp.float32
        )
        exact = lambda p, q, dims=(((1,), (0,)), ((), ())): lax.dot_general(
            p, q, dims, precision=highest, preferred_element_type=jnp.float32
        )
        s = lax.broadcasted_iota(jnp.int32, (CHUNK, CHUNK), 0)
        t = lax.broadcasted_iota(jnp.int32, (CHUNK, CHUNK), 1)

        @pl.when(pl.program_id(0) == 0)
        def _():
            db_ref[...] = jnp.zeros(db_ref.shape, jnp.float32)
            dc_ref[...] = jnp.zeros(dc_ref.shape, jnp.float32)
            inner_grad[...] = jnp.zeros(inner_grad.shape, jnp.float32)
            for k in range(chunks):
                here = slice(k * CHUNK, (k + 1) * CHUNK)
                b_turned[:, here] = low(b_ref[here, :].T)
                c_turned[:, here] = low(c_ref[here, :].T)
                inner[k] = exact(b_ref[here, :], c_ref[here, :], NT)
                shown = (s <= t) & (meta_ref[0] + k * CHUNK + s >= row_ref[0:1, here])
                hide[k] = jnp.where(shown, 0.0, masked_score)

        before = (s < t).astype(jnp.float32)
        until = low((s >= t).astype(jnp.float32))
        low_lane = t < SSM_DIM
        pick_row = lax.broadcasted_iota(jnp.int32, (8, 2 * SSM_DIM), 0)
        pick_lane = lax.broadcasted_iota(jnp.int32, (8, 2 * SSM_DIM), 1) // SSM_DIM
        pick = low((pick_row == pick_lane).astype(jnp.float32))
        spreads = []
        states[0] = state_ref[...]
        for k in range(chunks):
            here = slice(k * CHUNK, (k + 1) * CHUNK)
            cums, entries, tails = chunk_rows(k, meta_ref, cum_ref, row_ref)
            entry, tail = spread(*entries), spread(*tails)
            steps = spread(step_ref[0, 0:1, here], step_ref[0, 1:2, here])
            spreads.append((cums, entry, tail, steps))
            if k < chunks - 1:
                fresh = dot(b_turned[:, here], low(x_ref[here, :] * steps * tail))
                states[k + 1] = entry[CHUNK - 1 :, :] * states[k] + fresh
        flow[...] = grad_ref[...]
        skip_sum = jnp.zeros((1, 2 * SSM_DIM), jnp.float32)
        for k in reversed(range(chunks)):
            here = slice(k * CHUNK, (k + 1) * CHUNK)
            cums, entry, tail, steps = spreads[k]
            x_now, dy_now = x_ref[here, :], dy_ref[here, :]
            b_low, c_low = low(b_ref[here, :]), low(c_ref[here, :])
            scaled = x_now * steps
            dy_low = low(dy_now)
            flow_low, state_low = low(flow[...]), low(states[k])
            mixed, within = [], []
            for e in range(2):
                across = jnp.broadcast_to(cums[e], (CHUNK, CHUNK))
                decays = jnp.exp(across - across.T + hide[k])
                own = low(jnp.where(low_lane == (e == 0), scaled, 0.0))
                reach = decays * dot(own, dy_low, NT)
                inner_grad[k] += reach
                sums = dot(low(inner[k] * reach), until)
                within.append(jnp.sum(sums * before, axis=0, keepdims=True))
                mixed.append(dot(low(inner[k] * decays), dy_low))
            back = tail * dot(b_low, flow_low)
            dxs = jnp.where(low_lane, mixed[0], mixed[1]) + back
            db_ref[here, :] += dot(low(scaled * tail), flow_low, NT)
            entered = low(dy_now * entry)
            dc_ref[here, :] += dot(entered, state_low, NT)
            brought = dy_now * entry * dot(c_low, state_low)
            ends = dot(pick, low(brought), NT)
            begins = dot(pick, low(scaled * back), NT)
            direct = dot(pick, low(x_now * dxs), NT)
            through = jnp.sum(flow[...] * states[k], axis=0, keepdims=True) * entry[CHUNK - 1 :, :]
            log_grad = exact(ends, until.astype(jnp.float32)) + exact(begins, before)
            for e in range(2):
                lanes = slice(e * SSM_DIM, (e + 1) * SSM_DIM)
                kept = jnp.sum(through[:, lanes], axis=1, keepdims=True)
                small_ref[0, e : e + 1, here] = direct[e : e + 1, :]
                small_ref[0, 2 + e : 3 + e, here] = log_grad[e : e + 1, :] + within[e] + kept
            dx_ref[here, :] = dxs * steps + skip_ref[...] * dy_now
            skip_sum += jnp.sum(x_now * dy_now, axis=0, keepdims=True)
            flow[...] = entry[CHUNK - 1 :, :] * flow[...] + dot(c_turned[:, here], entered)
        small_ref[0, 4:8, :] = jnp.zeros((4, rows), jnp.float32)
        small_ref[0, 4:5, 0 : 2 * SSM_DIM] = skip_sum

        @pl.when(pl.program_id(0) == PAIRS - 1)
        def _():
            for k in range(chunks):
                here = slice(k * CHUNK, (k + 1) * CHUNK)
                grads = low(inner_grad[k])
                db_ref[here, :] += dot(grads, low(c_ref[here, :]))
                dc_ref[here, :] += dot(grads, low(b_ref[here, :]), TN)

    whole = lambda i, m: (0, 0)
    lanes = lambda i, m: (0, i)
    pair = lambda i, m: (i, 0, 0)
    return pl.pallas_call(
        pinned(kernel, 11, after),
        grid_spec=pltpu.PrefetchScalarGridSpec(
            num_scalar_prefetch=1,
            grid=(PAIRS,),
            in_specs=[
                pl.BlockSpec((rows, 2 * SSM_DIM), lanes),
                pl.BlockSpec((rows, 2 * SSM_DIM), lanes),
                pl.BlockSpec((rows, STATE), lambda i, m: (0, PAIRS)),
                pl.BlockSpec((rows, STATE), lambda i, m: (0, PAIRS + 1)),
                pl.BlockSpec((1, 2, rows), pair),
                pl.BlockSpec((1, 2, rows), pair),
                pl.BlockSpec((STATE, 2 * SSM_DIM), lanes),
                pl.BlockSpec((STATE, 2 * SSM_DIM), lanes),
                pl.BlockSpec((1, 2 * SSM_DIM), lanes),
                pl.BlockSpec((8, rows), whole),
            ] + pins(after),
            out_specs=[
                pl.BlockSpec((rows, 2 * SSM_DIM), lanes),
                pl.BlockSpec((rows, STATE), whole),
                pl.BlockSpec((rows, STATE), whole),
                pl.BlockSpec((1, 8, rows), pair),
            ],
            scratch_shapes=[
                pltpu.VMEM((chunks, CHUNK, CHUNK), jnp.float32),
                pltpu.VMEM((chunks, CHUNK, CHUNK), jnp.float32),
                pltpu.VMEM((chunks, CHUNK, CHUNK), jnp.float32),
                pltpu.VMEM((chunks, STATE, 2 * SSM_DIM), jnp.float32),
                pltpu.VMEM((STATE, 2 * SSM_DIM), jnp.float32),
                pltpu.VMEM((STATE, rows), jnp.bfloat16),
                pltpu.VMEM((STATE, rows), jnp.bfloat16),
            ],
        ),
        out_shape=[
            jax.ShapeDtypeStruct((rows, INNER), jnp.float32),
            jax.ShapeDtypeStruct((rows, STATE), jnp.float32),
            jax.ShapeDtypeStruct((rows, STATE), jnp.float32),
            jax.ShapeDtypeStruct((PAIRS, 8, rows), jnp.float32),
        ],
        compiler_params=pltpu.CompilerParams(vmem_limit_bytes=40 * 2**20),
        cost_estimate=pl.CostEstimate(flops=3 * 10**9, bytes_accessed=rows * INNER * 12, transcendentals=2**21),
        name="ssm_back",
    )(meta, conv, dy, conv, conv, cum.reshape(PAIRS, 2, rows), step.reshape(PAIRS, 2, rows), state_in, state_grad,
      skip, start_row, *after)


def chain_states(earlier, later):
    return (earlier[0] * later[0], earlier[1] * later[0] + later[1])


def scan_states(carry, state, span, fast, backward):
    wide = jnp.repeat(carry, SSM_DIM)[None, :]
    if not fast:
        ident = (jnp.ones_like(wide), jnp.zeros_like(state))
        return (carried_in if backward else prefix)((wide, state), span, chain_states, ident)[1]
    flow = Flow(scan_stages(carry, state, backward))
    while flow.sends:
        flow.go()
    return flow.result


def scan_stages(carry, state, backward):
    total = (jnp.repeat(carry, SSM_DIM)[None, :], state)
    start = None
    for name in ("c", "x", "y"):
        place = lax.axis_index(name)
        packed = jnp.concatenate([total[1], jnp.broadcast_to(total[0], (16, INNER))], axis=0)
        (packed,) = yield [(packed.astype(jnp.bfloat16), name, SWAP)]
        packed = packed.astype(jnp.float32)
        other = (packed[STATE : STATE + 1], packed[:STATE])
        leads = place == (0 if backward else 1)
        seen = (jnp.where(leads, other[0], 1.0), jnp.where(leads, other[1], 0.0))
        start = seen if start is None else chain_states(seen, start)
        if name != "y":
            forward = chain_states(other, total)
            reverse = chain_states(total, other)
            total = jax.tree.map(lambda p, q: jnp.where(leads, p, q), forward, reverse)
    return start[1]


KEYS = 512
PAIR = 2 * HEAD_DIM


def attention_forward(q_wide, kv, meta, starts, after=()):
    rows = q_wide.shape[1]
    blocks = kv.shape[0]
    ratio = HEADS_Q // HEADS_KV
    wide = min(512, rows)

    def kernel(meta_ref, q_ref, kv_ref, start_ref, o_ref, log_ref, top, total):
        b = pl.program_id(1)

        @pl.when(b == 0)
        def _():
            top[...] = jnp.full(top.shape, masked_score, jnp.float32)
            total[...] = jnp.zeros(total.shape, jnp.float32)
            o_ref[...] = jnp.zeros(o_ref.shape, jnp.float32)

        def block(partial):
            pair = kv_ref[0, 0]
            turned = pair.T[HEAD_DIM:, :]
            for h in range(ratio):
                for r in range(0, rows, wide):
                    here = slice(r, r + wide)
                    scores = lax.dot_general(pair, q_ref[h, here, :], NT, preferred_element_type=jnp.float32)
                    if partial:
                        keys = b * KEYS + lax.broadcasted_iota(jnp.int32, scores.shape, 0)
                        mine = meta_ref[2] + r + lax.broadcasted_iota(jnp.int32, scores.shape, 1)
                        visible = (keys >= start_ref[0:1, here]) & (keys <= mine)
                        scores = jnp.where(visible, scores, masked_score)
                    before = top[h, 0:1, here]
                    peak = jnp.maximum(before, jnp.max(scores, axis=0, keepdims=True))
                    part = jnp.exp(scores - peak)
                    if partial:
                        part = jnp.where(visible, part, 0.0)
                    fade = jnp.exp(before - peak)
                    top[h, 0:1, here] = peak
                    total[h, 0:1, here] = total[h, 0:1, here] * fade + jnp.sum(part, axis=0, keepdims=True)
                    o_ref[h, :, here] = o_ref[h, :, here] * fade + jnp.dot(
                        turned, part.astype(jnp.bfloat16), preferred_element_type=jnp.float32
                    )

        needed = (b >= meta_ref[0]) & (b < meta_ref[1])
        partial = ((b + 1) * KEYS > meta_ref[2]) | (b * KEYS < meta_ref[3])

        @pl.when(needed & partial)
        def _():
            block(True)

        @pl.when(needed & jnp.logical_not(partial))
        def _():
            block(False)

        @pl.when(b == blocks - 1)
        def _():
            for h in range(ratio):
                sums = total[h, 0:1, :]
                o_ref[h] = o_ref[h] / sums
                log_ref[h] = jnp.broadcast_to(top[h, 0:1, :] + jnp.log(sums), (8, rows))

    heads = lambda g, b, m: (g, 0, 0)
    return pl.pallas_call(
        pinned(kernel, 4, after),
        grid_spec=pltpu.PrefetchScalarGridSpec(
            num_scalar_prefetch=1,
            grid=(HEADS_KV, blocks),
            in_specs=[
                pl.BlockSpec((ratio, rows, PAIR), heads),
                pl.BlockSpec((1, 1, KEYS, PAIR), lambda g, b, m: (b, g, 0, 0)),
                pl.BlockSpec((8, rows), lambda g, b, m: (0, 0)),
            ] + pins(after),
            out_specs=[
                pl.BlockSpec((ratio, HEAD_DIM, rows), heads),
                pl.BlockSpec((ratio, 8, rows), heads),
            ],
            scratch_shapes=[
                pltpu.VMEM((ratio, 8, rows), jnp.float32),
                pltpu.VMEM((ratio, 8, rows), jnp.float32),
            ],
        ),
        out_shape=[
            jax.ShapeDtypeStruct((HEADS_Q, HEAD_DIM, rows), jnp.float32),
            jax.ShapeDtypeStruct((HEADS_Q, 8, rows), jnp.float32),
        ],
        compiler_params=pltpu.CompilerParams(vmem_limit_bytes=48 * 2**20),
        cost_estimate=pl.CostEstimate(flops=2 * 10**10, bytes_accessed=2**23, transcendentals=2**23),
        name="attend",
    )(meta, q_wide, kv, starts, *after)


def attention_backward(q_wide, g_wide, kv, logs, mixed, meta, starts, group, after=()):
    rows = q_wide.shape[1]
    blocks = kv.shape[0]
    ratio = HEADS_Q // HEADS_KV
    wide = min(512, rows)

    def kernel(meta_ref, q_ref, g_ref, kv_ref, log_ref, o_ref, start_ref, dkv_ref, dq_ref, delta, sums):
        b = pl.program_id(0)

        @pl.when(b == 0)
        def _():
            dq_ref[...] = jnp.zeros(dq_ref.shape, jnp.float32)
            for h in range(ratio):
                both = g_ref[h].astype(jnp.float32).T[HEAD_DIM:, :] * o_ref[h]
                delta[h] = jnp.broadcast_to(jnp.sum(both, axis=0, keepdims=True), (8, rows))

        def block(partial):
            pair = kv_ref[0, 0]
            turned = pair.T[:HEAD_DIM, :]
            for h in range(ratio):
                for r in range(0, rows, wide):
                    here = slice(r, r + wide)
                    q_now = q_ref[h, here, :]
                    g_now = g_ref[h, here, :]
                    scores = lax.dot_general(pair, q_now, NT, preferred_element_type=jnp.float32)
                    probs = jnp.exp(scores - log_ref[h, 0:1, here])
                    if partial:
                        keys = b * KEYS + lax.broadcasted_iota(jnp.int32, scores.shape, 0)
                        mine = meta_ref[2] + r + lax.broadcasted_iota(jnp.int32, scores.shape, 1)
                        visible = (keys >= start_ref[0:1, here]) & (keys <= mine)
                        probs = jnp.where(visible, probs, 0.0)
                    grads = lax.dot_general(pair, g_now, NT, preferred_element_type=jnp.float32)
                    low_grads = (probs * (grads - delta[h, 0:1, here])).astype(jnp.bfloat16)
                    change = jnp.dot(
                        probs.astype(jnp.bfloat16), g_now, preferred_element_type=jnp.float32
                    ) + jnp.dot(low_grads, q_now, preferred_element_type=jnp.float32)
                    if h == 0 and r == 0:
                        sums[...] = change
                    else:
                        sums[...] += change
                    dq_ref[h, :, here] += jnp.dot(turned, low_grads, preferred_element_type=jnp.float32)
            dkv_ref[0, 0] = sums[...].astype(jnp.bfloat16)

        needed = (b >= meta_ref[0]) & (b < meta_ref[1])
        partial = ((b + 1) * KEYS > meta_ref[2]) | (b * KEYS < meta_ref[3])

        @pl.when(needed & partial)
        def _():
            block(True)

        @pl.when(needed & jnp.logical_not(partial))
        def _():
            block(False)

        @pl.when(jnp.logical_not(needed))
        def _():
            dkv_ref[0, 0] = jnp.zeros((KEYS, PAIR), jnp.bfloat16)

    heads = lambda b, m: (group, 0, 0)
    return pl.pallas_call(
        pinned(kernel, 7, after),
        grid_spec=pltpu.PrefetchScalarGridSpec(
            num_scalar_prefetch=1,
            grid=(blocks,),
            in_specs=[
                pl.BlockSpec((ratio, rows, PAIR), heads),
                pl.BlockSpec((ratio, rows, PAIR), heads),
                pl.BlockSpec((1, 1, KEYS, PAIR), lambda b, m: (b, group, 0, 0)),
                pl.BlockSpec((ratio, 8, rows), heads),
                pl.BlockSpec((ratio, HEAD_DIM, rows), heads),
                pl.BlockSpec((8, rows), lambda b, m: (0, 0)),
            ] + pins(after),
            out_specs=[
                pl.BlockSpec((1, 1, KEYS, PAIR), lambda b, m: (b, 0, 0, 0)),
                pl.BlockSpec((ratio, HEAD_DIM, rows), lambda b, m: (0, 0, 0)),
            ],
            scratch_shapes=[
                pltpu.VMEM((ratio, 8, rows), jnp.float32),
                pltpu.VMEM((KEYS, PAIR), jnp.float32),
            ],
        ),
        out_shape=[
            jax.ShapeDtypeStruct((blocks, 1, KEYS, PAIR), jnp.bfloat16),
            jax.ShapeDtypeStruct((ratio, HEAD_DIM, rows), jnp.float32),
        ],
        compiler_params=pltpu.CompilerParams(vmem_limit_bytes=48 * 2**20),
        cost_estimate=pl.CostEstimate(flops=2 * 10**10, bytes_accessed=2**23, transcendentals=2**23),
        name="attend_back",
    )(meta, q_wide, g_wide, kv, logs, mixed, starts, *after)


def ordered(place, own, other, axis):
    first = jnp.where(place == 0, own, other)
    second = jnp.where(place == 0, other, own)
    return jnp.stack([first, second], axis=axis)


def gather_span(value, span, fast):
    if not fast:
        return lax.all_gather(value, span)
    flow = Flow(gather_stages(value))
    while flow.sends:
        flow.go()
    return flow.result


def gather_stages(value):
    _, y, x, c = (lax.axis_index(name) for name in GRID)
    (other,) = yield [(value, "x", SWAP)]
    two = ordered(x, value, other, 0)
    (other,) = yield [(two, "y", SWAP)]
    four = ordered(y, two, other, 0)
    (other,) = yield [(four, "c", SWAP)]
    return ordered(c, four, other, 2).reshape((8,) + value.shape)


def scatter_span(value, span, fast):
    if not fast:
        return lax.psum_scatter(value, span, scatter_dimension=0).astype(jnp.float32)
    flow = Flow(scatter_stages(value))
    while flow.sends:
        flow.go()
    return flow.result


def scatter_stages(value):
    _, y, x, c = (lax.axis_index(name) for name in GRID)
    value = value.reshape((2, 2, 2) + value.shape[1:])
    for name, place, axis in (("c", c, 2), ("y", y, 0), ("x", x, 0)):
        send = lax.dynamic_index_in_dim(value, 1 - place, axis, keepdims=False)
        (arrived,) = yield [(send, name, SWAP)]
        keep = lax.dynamic_index_in_dim(value, place, axis, keepdims=False)
        value = keep.astype(jnp.float32) + arrived.astype(jnp.float32)
        if name != "x":
            value = value.astype(jnp.bfloat16)
    return value


def sum_stages(value):
    for name in GRID[1:]:
        (other,) = yield [(value, name, SWAP)]
        value = value + other
    for pairs in ([(0, 1), (1, 0), (2, 3), (3, 2)], [(0, 2), (2, 0), (1, 3), (3, 1)]):
        (other,) = yield [(value, "z", pairs)]
        value = value + other
    return value


def offsets_of():
    places, at = {}, 0
    for name_key, extent in layout():
        places[name_key] = (at, extent)
        at += math.prod(extent)
    return places


def early_weights(params):
    places = offsets_of()
    buffers, spread_flow, (slots, all_slots), where = gather_lines(params)
    spread_flow.go()
    names = (W_QUERY, W_KEY, W_VALUE, W_ATTN_OUT, W_GATE_SSM, W_X_SSM, W_B_C)
    misc_at = places[W_STEP][0]
    first = unpack_lines(
        buffers[:16], slots, where, [flat_segment(name_key) for name_key in names] + [(0, 16, LINE), (misc_at, 288, LINE)]
    )
    weights = dict(zip(names, first))
    weights[NORM_ATTN] = first[-2].reshape(-1)[:D]
    misc = first[-1].reshape(-1)
    for name_key in (W_STEP,) + small_names[1:-1]:
        at, extent = places[name_key]
        weights[name_key] = misc[at - misc_at : at - misc_at + math.prod(extent)].reshape(extent)
    return weights, spread_flow, (buffers, all_slots, where)


def flat_segment(name_key):
    at, extent = offsets_of()[name_key]
    return (at, extent[0], extent[1])


def late_weights(held, after):
    buffers, slots, where = held
    names = (W_SSM_OUT, W_GATE, W_UP_PROJ, W_DOWN)
    norm_at = offsets_of()[NORM_FFN][0]
    second = unpack_lines(
        buffers, slots, where, [flat_segment(name_key) for name_key in names] + [(norm_at, 16, LINE)], after
    )
    weights = dict(zip(names, second))
    weights[NORM_FFN] = second[-1].reshape(-1)[norm_at % LINE : norm_at % LINE + D]
    return weights


def pack_late(gate, up, down, ssm_low, grad_branch, grad_norm_ffn, after):
    places = offsets_of()
    out_at = places[W_SSM_OUT][0]
    lane = places[W_GATE][0] % LINE
    boundary = 2 * PLANE * LINE
    tail_from = (boundary - out_at) // D
    tail = matmul_left_t(ssm_low[:, tail_from:], grad_branch).reshape(-1)
    tail = tail[boundary - out_at - tail_from * D :]
    head = jnp.concatenate([jnp.zeros((14 * LINE,), jnp.float32), tail, grad_norm_ffn])
    head_rows = head.shape[0] // LINE
    carry = jnp.zeros((8, LINE), jnp.float32).at[7, :lane].set(head[head_rows * LINE :])
    head = head[: head_rows * LINE].reshape(head_rows, LINE).astype(jnp.bfloat16)
    return pack_lines(
        None, 2 * PLANE + 32, head_rows, [gate, up, down], lane, 0, [(head, 0)], carry, 48, after
    )


def pack_out(ssm_low, grad_branch, after):
    out_at = offsets_of()[W_SSM_OUT][0]
    first_row = (8 + out_at // LINE) // 16 * 16
    rows = first_row + SSM_HEADS * SSM_DIM * D // LINE
    return pack_lines(
        None, rows, first_row, [(ssm_low, grad_branch)], out_at % LINE, (8 + out_at // LINE) % 8, [],
        jnp.zeros((8, LINE), jnp.float32), 0, after,
    )


def pack_ssm(target, segments, small, ssm_low, grad_branch, after):
    places = offsets_of()
    misc = [small[name_key].reshape(-1) for name_key in (W_STEP,) + small_names[1:-1]]
    count = sum(part.shape[0] for part in misc)
    misc_rows = (count // LINE + 16) // 16 * 16
    opening = matmul_left_t(ssm_low[:, :16], grad_branch).reshape(-1)
    misc = jnp.concatenate(misc + [opening[: misc_rows * LINE - count]])
    misc = misc.reshape(misc_rows, LINE).astype(jnp.bfloat16)
    first_row = 8 + places[W_ATTN_OUT][0] // LINE
    return pack_lines(
        target, target.shape[0], first_row, segments, 0, 0, [(misc, 8 + places[W_STEP][0] // LINE)], None, 0, after
    )


def pack_qkv(segments, attended, grad_branch, grad_norm_attn, after):
    places = offsets_of()
    out_row = 8 + places[W_ATTN_OUT][0] // LINE
    rows = (8 + SHARD) // 16 * 16 + 8 * PIECE
    closing = matmul_left_t(attended[:, :16], grad_branch).reshape(-1, LINE)
    closing = closing[: rows - out_row].astype(jnp.bfloat16)
    opening = jnp.concatenate([jnp.zeros((8, LINE), jnp.float32), grad_norm_attn.reshape(-1, LINE)]).astype(jnp.bfloat16)
    return pack_lines(
        None, rows, 16, segments, 0, 0, [(opening, 0), (closing, out_row)], None, 0, after
    )


def own_lines(early, late, corner):
    z, y, x, c = (lax.axis_index(name) for name in GRID)
    place = 4 * y + 2 * x + c
    shard = SHARD * place
    start = jnp.where(z < 2, (8 + shard) % 16, (14 + shard) % 16)
    lines = jnp.where(z < 2, early, late)
    lines = jnp.where((z == 0) & (place < 2), corner[:WIN], lines)
    lines = lax.dynamic_slice(lines, (start, 0), (SHARD, LINE)).astype(jnp.float32)
    return lines.reshape(-1)


def body(span, group, fast, tokens, params, cotangent, offsets):
    rows_dev = tokens.shape[0]
    group_rows = rows_dev * lax.axis_size(span)
    all_rows = group_rows * lax.axis_size(group)
    ssm_inner = SSM_HEADS * SSM_DIM
    score_scale = HEAD_DIM ** (-0.5)
    bounds = offsets[0]
    my_start = lax.axis_index(span) * rows_dev
    row_index = my_start + jnp.arange(rows_dev, dtype=jnp.int32)
    seq_id, positions = sequence_info(row_index, bounds)
    first_start = row_index[0] - positions[0]
    last_row = my_start + rows_dev - 1
    cosine, sine = rotary_tables(positions)
    if fast:
        weights, spread_flow, held = early_weights(params)
    else:
        weights = unpack(lax.all_gather(params, group + span, axis=0, tiled=True))
    small_f32 = {name_key: weights[name_key].astype(jnp.float32) for name_key in small_names[:-1]}
    x_rows = tokens.astype(jnp.float32)
    normed_one, norm_one_back = jax.vjp(rms_norm, x_rows, small_f32[NORM_ATTN])
    hidden = normed_one.astype(jnp.bfloat16)
    query = matmul(hidden, weights[W_QUERY])
    key_raw = matmul(hidden, weights[W_KEY])
    value_low = matmul(hidden, weights[W_VALUE]).astype(jnp.bfloat16)
    q_rot = rotate(query, cosine, sine, HEADS_Q).astype(jnp.bfloat16)
    k_rot = rotate(key_raw, cosine, sine, HEADS_KV).astype(jnp.bfloat16)
    k_heads = k_rot.reshape(rows_dev, HEADS_KV, HEAD_DIM)
    v_heads = value_low.reshape(rows_dev, HEADS_KV, HEAD_DIM)
    kv_mine = jnp.concatenate([k_heads, v_heads], axis=2).transpose(1, 0, 2)
    row_starts = row_index - positions
    kv_local = kv_mine.reshape(HEADS_KV, rows_dev, PAIR)
    xbc = jnp.concatenate(
        [matmul(hidden, weights[W_X_SSM]), matmul(hidden, weights[W_B_C])], axis=1
    )
    step_raw = matmul(hidden, weights[W_STEP])
    rim_rows = passed_along(xbc[rows_dev - 8 :], span, 1)
    ssm_meta = jnp.concatenate([my_start[None], row_starts[CHUNK - 1 :: CHUNK]]).astype(jnp.int32)
    conv_bias = small_f32[CONV_BIAS][None, :]
    convolve = lambda after: conv_forward(
        xbc, rim_rows, small_f32[CONV_WEIGHT], conv_bias, ssm_meta, row_starts[:, None], after
    )
    if fast:
        keys_flow = Flow(gather_stages(kv_local))
        keys_flow.go()
        (conv_values,) = bracket(convolve, [keys_flow, spread_flow])
    else:
        conv_values = convolve(())
    step_in = step_raw.T + small_f32[STEP_BIAS][:, None]
    step_rows = jax.nn.softplus(step_in)
    decay = -jnp.exp(small_f32[DECAY_LOG])
    logs_step = step_rows * decay[:, None]
    order = jnp.arange(rows_dev)
    upto = (order[:, None] <= order[None, :]).astype(jnp.float32)
    cumul = jnp.dot(logs_step, upto, precision=highest)
    chunk_cum = jnp.dot(
        logs_step.reshape(-1, CHUNK), upto[:CHUNK, :CHUNK], precision=highest
    ).reshape(SSM_HEADS, rows_dev)
    went_on = row_starts < my_start
    entry_rows = jnp.where(went_on[None, :], jnp.exp(cumul), 0.0)
    in_last = row_index >= row_starts[rows_dev - 1]
    tail_rows = jnp.exp(jnp.where(in_last[None, :], cumul[:, -1:] - cumul, masked_score))
    carry_all = entry_rows[:, -1]
    summarize = lambda after: weighted_state(conv_values, PAIRS, conv_values, tail_rows * step_rows, after)
    meta = jnp.stack(
        [first_start // KEYS, last_row // KEYS + 1, my_start, row_starts[rows_dev - 1]]
    ).astype(jnp.int32)
    q_low = (q_rot * jnp.bfloat16(score_scale)).reshape(rows_dev, HEADS_Q, HEAD_DIM).transpose(1, 0, 2)
    q_wide = jnp.pad(q_low, ((0, 0), (0, 0), (0, HEAD_DIM)))
    start_row = jnp.broadcast_to(row_starts[None, :], (8, rows_dev))
    if fast:
        (local_state,) = bracket(lambda after: summarize((*after, *spread_flow.values())), [keys_flow])
        scan = Flow(scan_stages(carry_all, local_state, False))
        key_blocks = keys_flow.result
        (gate_in,) = fence([hidden], scan.values())
        gate_ssm = matmul(gate_in, weights[W_GATE_SSM])
        scan.go()
        (gate_ssm,) = fence([gate_ssm], scan.values())
        scan.go()
        mixed, logs = bracket(
            lambda after: attention_forward(
                q_wide, key_blocks, meta, start_row, (*after, gate_ssm, *spread_flow.values())
            ),
            [scan],
        )
        spread_flow.go()
        state_in = scan.result
    else:
        gate_ssm = matmul(hidden, weights[W_GATE_SSM])
        key_blocks = lax.all_gather(kv_local, span)
        if rows_dev != KEYS:
            key_blocks = key_blocks.transpose(1, 0, 2, 3).reshape(HEADS_KV, -1, KEYS, PAIR).transpose(1, 0, 2, 3)
        state_in = scan_states(carry_all, summarize(()), span, fast, False)
        mixed, logs = attention_forward(q_wide, key_blocks, meta, start_row)
    attended = mixed.astype(jnp.bfloat16).reshape(HEADS_Q * HEAD_DIM, rows_dev).T
    attn_out = matmul(attended, weights[W_ATTN_OUT])
    skip_wide = jnp.repeat(small_f32[SKIP_GAIN], SSM_DIM)[None, :]
    ssm_y = ssm_forward(
        conv_values, chunk_cum, step_rows, state_in, skip_wide, ssm_meta, row_starts[:, None], start_row
    )
    normed_ssm, gnorm_back = jax.vjp(gated_norm, ssm_y, gate_ssm, small_f32[NORM_SSM])
    ssm_low = normed_ssm.astype(jnp.bfloat16)
    if fast:
        held = (held[0] + spread_flow.result,) + held[1:]
        weights.update(late_weights(held, [ssm_y]))
    small_f32[NORM_FFN] = weights[NORM_FFN].astype(jnp.float32)
    ssm_out = matmul(ssm_low, weights[W_SSM_OUT])
    middle = x_rows + attn_out + ssm_out
    normed_two, norm_two_back = jax.vjp(rms_norm, middle, small_f32[NORM_FFN])
    hidden_two = normed_two.astype(jnp.bfloat16)
    gate_ffn = matmul(hidden_two, weights[W_GATE])
    upper = matmul(hidden_two, weights[W_UP_PROJ])
    activation_f32, swiglu_back = jax.vjp(swiglu, gate_ffn, upper)
    activation = activation_f32.astype(jnp.bfloat16)
    ffn_out = matmul(activation, weights[W_DOWN])
    result = middle + ffn_out
    squares = jnp.stack(
        [
            jnp.sum(result * result),
            jnp.sum(attn_out * attn_out),
            jnp.sum(ssm_out * ssm_out),
            jnp.sum(ffn_out * ffn_out),
        ]
    )
    grad_out = cotangent.astype(jnp.float32)
    grad_activation = matmul_right_t(cotangent, weights[W_DOWN])
    grad_gate_f32, grad_upper_f32 = swiglu_back(grad_activation)
    grad_gate = grad_gate_f32.astype(jnp.bfloat16)
    grad_upper = grad_upper_f32.astype(jnp.bfloat16)
    grad_hidden_two = matmul_right_t(grad_gate, weights[W_GATE]) + matmul_right_t(
        grad_upper, weights[W_UP_PROJ]
    )
    grad_middle_norm, grad_norm_ffn = norm_two_back(grad_hidden_two)
    grad_middle = grad_out + grad_middle_norm
    grad_branch = grad_middle.astype(jnp.bfloat16)
    grad_attended = matmul_right_t(grad_branch, weights[W_ATTN_OUT]).astype(jnp.bfloat16)
    grad_ssm_low = matmul_right_t(grad_branch, weights[W_SSM_OUT])
    grad_ssm_y, grad_gate_ssm_f32, grad_norm_ssm = gnorm_back(grad_ssm_low)
    grad_state_local = weighted_state(conv_values, PAIRS + 1, grad_ssm_y, entry_rows)
    if fast:
        scan = Flow(scan_stages(carry_all, grad_state_local, True))
        (late,) = bracket(
            lambda after: pack_late(
                (hidden_two, grad_gate), (hidden_two, grad_upper), (activation, cotangent),
                ssm_low, grad_branch, grad_norm_ffn, after,
            ),
            [scan],
        )
        late_flow = Flow(reduce_stages(late, 1, 14))
        (early,) = bracket(lambda after: pack_out(ssm_low, grad_branch, after + late_flow.values()), [scan])
        scan.go()
        late_flow.go()
        grad_state_out = scan.result
        around = lambda call: bracket(call, [late_flow])
    else:
        grad_state_out = scan_states(carry_all, grad_state_local, span, fast, True)
        around = lambda call: call(())
    grad_x, grad_b, grad_c, grad_small = around(
        lambda after: ssm_backward(
            conv_values, grad_ssm_y, chunk_cum, step_rows, state_in, grad_state_out, skip_wide, ssm_meta, start_row,
            after,
        )
    )
    grad_direct = grad_small[:, 0:2].reshape(SSM_HEADS, rows_dev)
    grad_logs = grad_small[:, 2:4].reshape(SSM_HEADS, rows_dev)
    grad_decay_log = decay * jnp.sum(step_rows * grad_logs, axis=1)
    grad_step_rows = (grad_direct + decay[:, None] * grad_logs) * jax.nn.sigmoid(step_in)
    grad_step_bias = jnp.sum(grad_step_rows, axis=1)
    grad_step_raw_f32 = grad_step_rows.T
    grad_skip_gain = jnp.sum(grad_small[:, 4, : 2 * SSM_DIM].reshape(SSM_HEADS, SSM_DIM), axis=1)
    grad_main, grad_tail, grad_edge, grad_taps = around(
        lambda after: conv_backward(
            grad_x, grad_b, grad_c, xbc, rim_rows, small_f32[CONV_WEIGHT], conv_bias, ssm_meta,
            row_starts[:, None], after,
        )
    )
    grad_conv_weight = grad_taps[:CONV]
    grad_conv_bias = grad_taps[CONV]
    rim_back = passed_along(grad_edge, span, -1)
    grad_tail = grad_tail + jnp.pad(rim_back, ((8, 0), (0, 0)))
    grad_xbc = lax.dynamic_update_slice(grad_main, grad_tail.astype(jnp.bfloat16), (rows_dev - 16, 0))
    grad_gate_ssm = grad_gate_ssm_f32.astype(jnp.bfloat16)
    grad_step_raw = grad_step_raw_f32.astype(jnp.bfloat16)
    grad_w_step = matmul_left_t(hidden, grad_step_raw)
    grad_hidden_ssm = (
        matmul_right_t(grad_gate_ssm, weights[W_GATE_SSM])
        + matmul_right_t(grad_xbc[:, :ssm_inner], weights[W_X_SSM])
        + matmul_right_t(grad_xbc[:, ssm_inner:], weights[W_B_C])
        + matmul_right_t(grad_step_raw, weights[W_STEP])
    )
    small = {
        W_STEP: grad_w_step,
        CONV_WEIGHT: grad_conv_weight,
        CONV_BIAS: grad_conv_bias,
        STEP_BIAS: grad_step_bias,
        DECAY_LOG: grad_decay_log,
        SKIP_GAIN: grad_skip_gain,
        NORM_SSM: grad_norm_ssm,
        NORM_FFN: grad_norm_ffn,
    }
    parts = []
    if fast:
        early = pack_ssm(
            early,
            [
                (attended, grad_branch), (hidden, grad_gate_ssm),
                (hidden, grad_xbc[:, :ssm_inner]), (hidden, grad_xbc[:, ssm_inner:]),
            ],
            small, ssm_low, grad_branch, late_flow.values(),
        )
        early_flow = Flow(reduce_stages(early, 0, 8))
        (grad_attended,) = fence([grad_attended], early_flow.values() + late_flow.values())
        around = lambda call: bracket(call, [early_flow])
    g_low = grad_attended.reshape(rows_dev, HEADS_Q, HEAD_DIM).transpose(1, 0, 2)
    g_wide = jnp.pad(g_low, ((0, 0), (0, 0), (HEAD_DIM, 0)))
    if fast:
        early_flow.go()
        (g_wide,) = fence([g_wide], early_flow.values())
    for group_at in range(HEADS_KV):
        after_part = [part[1] for part in parts]
        if fast and group_at == 0:
            after_part = late_flow.values()
        parts.append(
            around(
                lambda after: attention_backward(
                    q_wide, g_wide, key_blocks, logs, mixed, meta, start_row, group_at, (*after, *after_part)
                )
            )
        )
    grad_kv = jnp.concatenate([part[0] for part in parts], axis=1)
    grad_q_turned = jnp.concatenate([part[1] for part in parts], axis=0)
    if rows_dev != KEYS:
        grad_kv = grad_kv.transpose(1, 0, 2, 3).reshape(HEADS_KV, -1, rows_dev, PAIR).transpose(1, 0, 2, 3)
    if fast:
        late_flow.go([parts[-1][1]])
        scatter = Flow(scatter_stages(grad_kv))
        (grad_q_turned,) = fence([grad_q_turned], scatter.values() + early_flow.values() + late_flow.values())
    halves = grad_q_turned.reshape(HEADS_Q, 2, HEAD_DIM // 2, rows_dev) * score_scale
    cos_t, sin_t = cosine.T[None], sine.T[None]
    turned_back = jnp.stack(
        [halves[:, 0] * cos_t + halves[:, 1] * sin_t, halves[:, 1] * cos_t - halves[:, 0] * sin_t], axis=1
    ).astype(jnp.bfloat16)
    grad_query_low = turned_back.reshape(HEADS_Q * HEAD_DIM, rows_dev).T
    if fast:
        scatter.go()
        early_flow.go()
        (grad_query_low,) = fence([grad_query_low], scatter.values() + early_flow.values())
    grad_hidden = grad_hidden_ssm + matmul_right_t(grad_query_low, weights[W_QUERY])
    if fast:
        scatter.go()
        (grad_hidden,) = fence([grad_hidden], scatter.values())
        scatter.go()
        grad_kv_mine = scatter.result
    else:
        grad_kv_mine = scatter_span(grad_kv, span, fast)
    grad_keys_mine = grad_kv_mine[:, :, :HEAD_DIM].transpose(1, 0, 2).reshape(rows_dev, -1)
    grad_values_mine = grad_kv_mine[:, :, HEAD_DIM:].transpose(1, 0, 2).reshape(rows_dev, -1)
    grad_key_low = rotate(grad_keys_mine, cosine, -sine, HEADS_KV).astype(jnp.bfloat16)
    grad_value_low = grad_values_mine.astype(jnp.bfloat16)
    grad_hidden = (
        grad_hidden
        + matmul_right_t(grad_key_low, weights[W_KEY])
        + matmul_right_t(grad_value_low, weights[W_VALUE])
    )
    grad_x_norm, grad_norm_attn = norm_one_back(grad_hidden)
    grad_tokens = grad_middle + grad_x_norm
    if fast:
        corner = pack_qkv(
            [(hidden, grad_query_low), (hidden, grad_key_low), (hidden, grad_value_low)],
            attended, grad_branch, grad_norm_attn, early_flow.values(),
        )
        corner_flow = Flow(corner_stages(corner))
        (squares,) = fence([squares], corner_flow.values())
        stats_flow = Flow(sum_stages(squares))
        for _ in range(3):
            corner_flow.go()
            stats_flow.go()
        early_flow.go()
        ((pieces, _, _), *_) = corner_flow.sends
        (pieces,) = fence([pieces], early_flow.values())
        corner_flow.sends = [(pieces, axis, pairs) for _, axis, pairs in corner_flow.sends]
        for flow in (stats_flow, early_flow, late_flow, corner_flow):
            while flow.sends:
                flow.go()
        stats = jnp.sqrt(stats_flow.result / (all_rows * D))
        grad_shard = own_lines(early_flow.result, late_flow.result, corner_flow.result)
        return (result.astype(jnp.bfloat16), grad_tokens, grad_shard, stats)
    small[NORM_ATTN] = grad_norm_attn
    stats = jnp.sqrt(lax.psum(squares, group + span) / (all_rows * D))
    pairs = {
        W_QUERY: (hidden, grad_query_low),
        W_KEY: (hidden, grad_key_low),
        W_VALUE: (hidden, grad_value_low),
        W_ATTN_OUT: (attended, grad_branch),
        W_GATE_SSM: (hidden, grad_gate_ssm),
        W_X_SSM: (hidden, grad_xbc[:, :ssm_inner]),
        W_B_C: (hidden, grad_xbc[:, ssm_inner:]),
        W_SSM_OUT: (ssm_low, grad_branch),
        W_GATE: (hidden_two, grad_gate),
        W_UP_PROJ: (hidden_two, grad_upper),
        W_DOWN: (activation, cotangent),
    }
    grad_dict = dict(small)
    for name_key, (left, right) in pairs.items():
        grad_dict[name_key] = matmul_left_t(left, right)
    flat_parts = [grad_dict[name_key].reshape(-1) for name_key, extent in layout()]
    used_entries = 0
    for part_array in flat_parts:
        used_entries += part_array.shape[0]
    flat_parts.append(jnp.zeros((params.shape[0] * lax.axis_size(group + span) - used_entries,), jnp.float32))
    grad_shard = lax.psum_scatter(
        jnp.concatenate(flat_parts), group + span, scatter_dimension=0, tiled=True
    )
    return (result.astype(jnp.bfloat16), grad_tokens, grad_shard, stats)


def solution(mesh):
    fast = (mesh.shape["group"], mesh.shape["span"]) == FAST
    if fast:
        mesh = Mesh(mesh.devices.reshape(4, 2, 2, 2), GRID)
        group, span = (GRID[:1], GRID[1:])
    else:
        group, span = (("group",), ("span",))

    def program(tokens, params, cotangent, offsets):
        return body(span, group, fast, tokens, params, cotangent, offsets)

    return jax.shard_map(
        program,
        mesh=mesh,
        in_specs=(P(group + span, None), P(group + span), P(group + span, None), P(group, None)),
        out_specs=(P(group + span, None), P(group + span, None), P(group + span), P()),
        check_vma=False,
    )
```

```python
import math

import jax
import jax.numpy as jnp
import numpy as np
from jax import lax
from jax.experimental import pallas as pl
from jax.experimental.pallas import tpu as pltpu
from jax.sharding import Mesh, PartitionSpec as P

D = 1024
HEADS_Q = 8
HEADS_KV = 2
HEAD_DIM = 64
SSM_HEADS = 24
SSM_DIM = 64
STATE = 128
CONV = 4
FF = 2048
(
    NORM_ATTN,
    W_QUERY,
    W_KEY,
    W_VALUE,
    W_ATTN_OUT,
    W_GATE_SSM,
    W_X_SSM,
    W_B_C,
    W_STEP,
    CONV_WEIGHT,
    CONV_BIAS,
    STEP_BIAS,
    DECAY_LOG,
    SKIP_GAIN,
    NORM_SSM,
    W_SSM_OUT,
    NORM_FFN,
    W_GATE,
    W_UP_PROJ,
    W_DOWN,
) = range(20)


epsilon = 1e-05
rope_base = 100000000000.0
masked_score = -1e30
highest = lax.Precision.HIGHEST
small_names = (
    NORM_ATTN,
    CONV_WEIGHT,
    CONV_BIAS,
    STEP_BIAS,
    DECAY_LOG,
    SKIP_GAIN,
    NORM_SSM,
    NORM_FFN,
)


def passed_along(value, axis, steps):
    count = lax.axis_size(axis)
    first, last = (max(0, -steps), min(count, count - steps))
    return lax.ppermute(value, axis, [(source, source + steps) for source in range(first, last)])


def prefix(value, axis, combine, identity):
    peers, place = (lax.axis_size(axis), lax.axis_index(axis))
    everything = jax.tree.map(
        lambda part, kind: lax.all_gather(part.astype(kind), axis),
        value,
        (jnp.bfloat16, jnp.bfloat16),
    )
    start = jax.tree.map(
        lambda part, zero: jnp.broadcast_to(jnp.asarray(zero, part.dtype), part.shape),
        value,
        identity,
    )

    def prefix_turn(k, before):
        reached = k < place
        new = combine(
            before, jax.tree.map(lambda part, own: part[k].astype(own.dtype), everything, value)
        )
        return jax.tree.map(lambda a, b: jnp.where(reached, a, b), new, before)

    return lax.fori_loop(0, peers, prefix_turn, start)


def carried_in(value, axis, combine, identity):
    peers, place = (lax.axis_size(axis), lax.axis_index(axis))
    everything = jax.tree.map(
        lambda part, kind: lax.all_gather(part.astype(kind), axis),
        value,
        jax.tree.map(lambda a: jnp.bfloat16 if a.dtype == jnp.float32 else a.dtype, value),
    )
    start = jax.tree.map(
        lambda part, zero: jnp.broadcast_to(jnp.asarray(zero, part.dtype), part.shape),
        value,
        identity,
    )

    def carried_turn(k, before):
        at = peers - 1 - k
        reached = at > place
        new = combine(
            before, jax.tree.map(lambda part, own: part[at].astype(own.dtype), everything, value)
        )
        return jax.tree.map(lambda a, b: jnp.where(reached, a, b), new, before)

    return lax.fori_loop(0, peers, carried_turn, start)


def layout():
    ssm_inner = SSM_HEADS * SSM_DIM
    channels = ssm_inner + 2 * STATE
    return [
        (NORM_ATTN, (D,)),
        (W_QUERY, (D, HEADS_Q * HEAD_DIM)),
        (W_KEY, (D, HEADS_KV * HEAD_DIM)),
        (W_VALUE, (D, HEADS_KV * HEAD_DIM)),
        (W_ATTN_OUT, (HEADS_Q * HEAD_DIM, D)),
        (W_GATE_SSM, (D, ssm_inner)),
        (W_X_SSM, (D, ssm_inner)),
        (W_B_C, (D, 2 * STATE)),
        (W_STEP, (D, SSM_HEADS)),
        (CONV_WEIGHT, (CONV, channels)),
        (CONV_BIAS, (channels,)),
        (STEP_BIAS, (SSM_HEADS,)),
        (DECAY_LOG, (SSM_HEADS,)),
        (SKIP_GAIN, (SSM_HEADS,)),
        (NORM_SSM, (ssm_inner,)),
        (W_SSM_OUT, (ssm_inner, D)),
        (NORM_FFN, (D,)),
        (W_GATE, (D, FF)),
        (W_UP_PROJ, (D, FF)),
        (W_DOWN, (FF, D)),
    ]


def unpack(flat_vector):
    unpacked = {}
    offset = 0
    for name_key, extent in layout():
        amount = math.prod(extent)
        unpacked[name_key] = flat_vector[offset : offset + amount].reshape(extent)
        offset += amount
    return unpacked


def matmul(left, right):
    return jnp.dot(left, right, preferred_element_type=jnp.float32)


def matmul_left_t(left, right):
    return lax.dot_general(
        left, right, (((0,), (0,)), ((), ())), preferred_element_type=jnp.float32
    )


def matmul_right_t(left, right):
    return lax.dot_general(
        left, right, (((1,), (1,)), ((), ())), preferred_element_type=jnp.float32
    )


def rms_norm(values, gain):
    return values * lax.rsqrt(jnp.mean(values * values, axis=-1, keepdims=True) + epsilon) * gain


def gated_norm(ssm_y, gate_ssm, gain):
    return rms_norm(ssm_y * jax.nn.silu(gate_ssm), gain)


def swiglu(gate_ffn, upper):
    return jax.nn.silu(gate_ffn) * upper


def sequence_info(row_index, bounds):
    starts = bounds[:-1]
    inside = row_index[:, None] >= starts[None, :]
    seq_id = jnp.sum(inside.astype(jnp.int32), axis=1) - 1
    seq_start = jnp.max(jnp.where(inside, starts[None, :], 0), axis=1)
    return (seq_id, row_index - seq_start)


def rotary_tables(positions):
    half_dim = HEAD_DIM // 2
    freqs = jnp.exp(
        -jnp.arange(half_dim, dtype=jnp.float32) * (2.0 * math.log(rope_base) / HEAD_DIM)
    )
    angles = freqs[:, None] * positions.astype(jnp.float32)[None, :]
    return (jnp.cos(angles), jnp.sin(angles))


def rotate(values, cosine, sine, heads):
    halves = values.reshape(heads, 2, HEAD_DIM // 2, -1)
    first_half, second_half = halves[:, 0], halves[:, 1]
    turned = jnp.stack(
        [first_half * cosine - second_half * sine, second_half * cosine + first_half * sine], axis=1
    )
    return turned.reshape(heads, HEAD_DIM, -1)


def add_rows(target, addend, first_row):
    current = lax.dynamic_slice_in_dim(target, first_row, addend.shape[0], 0)
    return lax.dynamic_update_slice_in_dim(target, current + addend, first_row, 0)


FAST = (4, 8)
LINE = 128
SHARD = 3082
SPAD = 3088
WIN = 3104
PLANE = 8 * SHARD
DEPTH = 4
TALL = {1: 1024, 2: 1024, 4: 512, 8: 256, 12: 128, 16: 128}
GRID = ("z", "y", "x", "c")
ZC = ("z", "c")
SWAP = [(0, 1), (1, 0)]


def zc_pairs(*pairs):
    return [(2 * a + c, 2 * b + c) for a, b, c in pairs]


def pinned(kernel, count, after):
    return lambda *refs: kernel(*refs[:count], *refs[count + len(after) :])


def pins(after):
    return [pl.BlockSpec(memory_space=pltpu.HBM)] * len(after)


class Flow:
    def __init__(self, stages):
        self.stages = stages
        self.sends = next(stages)
        self.result = None

    def values(self):
        return [value for value, _, _ in self.sends] or (list(self.result) if isinstance(self.result, list) else [self.result])

    def hold(self, after):
        held = fence(self.values(), after)
        self.sends = [(value, axis, pairs) for value, (_, axis, pairs) in zip(held, self.sends)]

    def go(self, after=()):
        arrived = [lax.ppermute(value, axis, pairs) for value, axis, pairs in self.sends]
        if after:
            arrived = fence(arrived, after)
        try:
            self.sends = self.stages.send(arrived)
        except StopIteration as stop:
            self.sends, self.result = [], stop.value
        return self


def fence(values, after):
    def kernel(*refs):
        del refs

    return pl.pallas_call(
        kernel,
        in_specs=pins(values) + pins(after),
        out_specs=pins(values),
        out_shape=[jax.ShapeDtypeStruct(value.shape, value.dtype) for value in values],
        input_output_aliases={k: k for k in range(len(values))},
        name="fence",
    )(*values, *after)


def bracket(call, flows):
    out = call([value for flow in flows for value in flow.values()])
    out = list(out) if isinstance(out, (list, tuple)) else [out]
    for flow in flows:
        flow.go()
    return fence(out, [v for flow in flows for v in flow.values()])


def gather_lines(params):
    z, y, x, c = (lax.axis_index(name) for name in GRID)
    lines = jnp.pad(params.reshape(SHARD, LINE), ((0, SPAD - SHARD), (0, 0)))
    sibling = lax.ppermute(lines, ZC, [(2 * k + 1 - k % 2, 2 * k + k % 2) for k in range(4)])
    buffers = []
    for part in range(2):
        here = jnp.where(c == part, lines, sibling)
        one = lax.ppermute(here, ZC, zc_pairs((0, 1, 0), (1, 2, 1)))
        side = lax.ppermute(here, ZC, zc_pairs((1, 0, 1)))
        two = lax.ppermute(one, ZC, zc_pairs((1, 2, 0), (2, 3, 1)))
        three = lax.ppermute(two, ZC, zc_pairs((2, 3, 0)))
        column = jnp.where(z == c, here, one + side + two + three)
        over_x = lax.ppermute(column, "x", SWAP)
        over_y = lax.ppermute(column, "y", SWAP)
        corner = lax.ppermute(over_y if part else over_x, "x" if part else "y", SWAP)
        local = [column, over_x, over_y, corner]
        buffers += [piece[None] for piece in local]
        buffers += [lax.ppermute(piece, "c", SWAP)[None] for piece in local]
    early = [(k, 0) for k in range(16)]
    here = jnp.where(c == 0, jnp.stack([lines, sibling]), jnp.stack([sibling, lines]))
    one = lax.ppermute(here, ZC, zc_pairs((2, 1, 0), (3, 2, 1)))
    side = lax.ppermute(here, ZC, zc_pairs((2, 3, 0)))
    two = lax.ppermute(one, ZC, zc_pairs((1, 0, 0), (2, 1, 1)))
    three = lax.ppermute(two, ZC, zc_pairs((1, 0, 1)))
    column = jnp.where(z == 2 + c, here, one + side + two + three)
    late = []
    for part in range(2):
        for first in (16, 21):
            late += [(first, part), (first + 1, part), (first + 2, part), (first + 3 + part, 0)]
    shard = np.arange(32)
    sz, sy, sx, sc = shard // 8, shard // 4 % 2, shard // 2 % 2, shard % 2
    away = jnp.where(sz % 2 == c, 0, 4)
    where = sc * 8 + away + 2 * (sy ^ y) + (sx ^ x) + 16 * (sz // 2)
    return buffers, Flow(spread_stages(column)), (early, early + late), where.astype(jnp.int32)


def spread_stages(column):
    over_x, over_y = yield [(column, "x", SWAP), (column, "y", SWAP)]
    corners = yield [(over_x[:1], "y", SWAP), (over_y[1:], "x", SWAP)]
    local = [column, over_x, over_y] + list(corners)
    return local + list((yield [(piece, "c", SWAP) for piece in local]))


def unpack_lines(buffers, slots, where, segments, after=()):
    jobs, starts = [], []
    reach = 0
    for offset, rows, columns in segments:
        per_row = columns // LINE
        lane, base = offset % LINE, offset // LINE
        if per_row == 1 and rows < 1024:
            lane, tall = 0, rows
        else:
            tall = TALL[per_row]
        starts.append(len(jobs))
        for k in range(rows // tall):
            jobs.append((base + k * tall * per_row, tall * per_row, 1 if lane else 0))
    window = max(job[1] for job in jobs) + 32
    table = np.zeros((len(jobs), 5), np.int32)
    for k, (line, count, extra) in enumerate(jobs):
        owner = line // SHARD
        inside = line - owner * SHARD
        begin = min(inside // 16 * 16, SPAD - window)
        crosses = int(line + count + extra > (owner + 1) * SHARD)
        table[k] = (owner, begin, begin - inside, crosses, (owner + 1) * SHARD - line)
    base_row = (int(-table[:, 2].min()) + 7) // 8 * 8
    table[:, 2] += base_row
    table[:, 4] += base_row
    room = int(max((table[:, 2] + window).max(), ((table[:, 4] + window) * table[:, 3]).max()))
    room = (room + 15) // 8 * 8
    total = len(jobs)
    count_buffers = len(buffers)
    shapes = []
    for offset, rows, columns in segments:
        per_row = columns // LINE
        tall = rows if per_row == 1 and rows < 1024 else TALL[per_row]
        shapes.append((rows, columns, tall, per_row, offset % LINE if tall != rows or per_row != 1 else 0))
    sizes = sorted({(tall, columns) for _, columns, tall, _, _ in shapes})

    def kernel(table_ref, where_ref, *refs):
        sources = refs[:count_buffers]
        outs = refs[count_buffers : count_buffers + len(segments)]
        rest = refs[count_buffers + len(segments) :]
        stages = dict(zip(sizes, rest))
        raw, flat, in_sem, out_sem = rest[len(sizes) :]
        step = pl.program_id(0)

        def fetch(job, slot):
            owner = table_ref[job, 0]
            begin = pl.multiple_of(table_ref[job, 1], 16)
            for b, (source, part) in enumerate(slots):

                @pl.when(where_ref[owner] == b)
                def _():
                    pltpu.make_async_copy(
                        sources[source].at[part, pl.ds(begin, window), :], raw.at[slot, 0], in_sem.at[slot, 0]
                    ).start()

            @pl.when(table_ref[job, 3] == 1)
            def _():
                for b, (source, part) in enumerate(slots):

                    @pl.when(where_ref[owner + 1] == b)
                    def _():
                        pltpu.make_async_copy(
                            sources[source].at[part, pl.ds(0, window), :], raw.at[slot, 1], in_sem.at[slot, 1]
                        ).start()

        def fetched(slot, half):
            return pltpu.make_async_copy(
                sources[0].at[0, pl.ds(0, window), :], raw.at[slot, half], in_sem.at[slot, half]
            )

        @pl.when(step == 0)
        def _():
            for k in range(min(DEPTH - 1, total)):
                fetch(k, k)

        @pl.when(step + DEPTH - 1 < total)
        def _():
            fetch(step + DEPTH - 1, lax.rem(step + DEPTH - 1, DEPTH))

        slot = lax.rem(step, DEPTH)
        fetched(slot, 0).wait()
        flat[pl.ds(table_ref[step, 2], window), :] = raw[slot, 0].astype(jnp.float32)

        @pl.when(table_ref[step, 3] == 1)
        def _():
            fetched(slot, 1).wait()
            flat[pl.ds(table_ref[step, 4], window), :] = raw[slot, 1].astype(jnp.float32)

        for index, (rows, columns, tall, per_row, lane) in enumerate(shapes):
            begin = starts[index]
            blocks = rows // tall
            stage = stages[(tall, columns)]

            @pl.when((step >= begin) & (step < begin + blocks))
            def _():
                block = step - begin
                side = lax.rem(block, DEPTH)

                def written(k, s):
                    return pltpu.make_async_copy(
                        stage.at[s],
                        outs[index].at[pl.ds(pl.multiple_of(k * tall, 16), tall), :],
                        out_sem.at[s],
                    )

                @pl.when(block >= DEPTH)
                def _():
                    written(block - DEPTH, side).wait()

                def tile(j):
                    picked = flat[pl.ds(base_row + j, tall, stride=per_row), :]
                    return pltpu.roll(picked, LINE - lane, 1) if lane else picked

                if lane:
                    lanes = lax.broadcasted_iota(jnp.int32, (tall, LINE), 1)
                    now = tile(0)
                    for j in range(per_row):
                        later = tile(j + 1)
                        stage[side, :, j * LINE : (j + 1) * LINE] = jnp.where(
                            lanes < LINE - lane, now, later
                        ).astype(jnp.bfloat16)
                        now = later
                else:
                    for j in range(per_row):
                        stage[side, :, j * LINE : (j + 1) * LINE] = tile(j).astype(jnp.bfloat16)
                written(block, side).start()

                @pl.when(block == blocks - 1)
                def _():
                    for back in reversed(range(min(DEPTH, blocks))):
                        written(block - back, lax.rem(block - back, DEPTH)).wait()

    return pl.pallas_call(
        pinned(kernel, 2 + count_buffers, after),
        grid_spec=pltpu.PrefetchScalarGridSpec(
            num_scalar_prefetch=2,
            grid=(total,),
            in_specs=[pl.BlockSpec(memory_space=pl.ANY)] * count_buffers + pins(after),
            out_specs=[pl.BlockSpec(memory_space=pl.ANY)] * len(segments),
            scratch_shapes=[pltpu.VMEM((DEPTH,) + size, jnp.bfloat16) for size in sizes]
            + [
                pltpu.VMEM((DEPTH, 2, window, LINE), jnp.bfloat16),
                pltpu.VMEM((room, LINE), jnp.float32),
                pltpu.SemaphoreType.DMA((DEPTH, 2)),
                pltpu.SemaphoreType.DMA((DEPTH,)),
            ],
        ),
        out_shape=[jax.ShapeDtypeStruct((rows, columns), jnp.bfloat16) for _, rows, columns in segments],
        compiler_params=pltpu.CompilerParams(vmem_limit_bytes=48 * 2**20),
        cost_estimate=pl.CostEstimate(flops=0, bytes_accessed=total * window * LINE * 4, transcendentals=0),
        name="unpack",
    )(jnp.asarray(table), where, *buffers, *after)


def pack_lines(target, target_rows, first_row, segments, lane, phase, extras, carry, tail_rows, after=()):
    tall = 256
    lefts, rights, plan = [], [], []
    left_of, right_of = {}, {}
    row = first_row
    begin = 0
    for left, right in segments:
        for value, seen, kept in ((left, left_of, lefts), (right, right_of, rights)):
            if id(value) not in seen:
                seen[id(value)] = len(kept)
                kept.append(value)
        blocks = left.shape[1] // tall
        plan.append((left_of[id(left)], right_of[id(right)], right.shape[1] // LINE, begin, blocks, row))
        begin += blocks
        row += left.shape[1] * right.shape[1] // LINE
    end_row = row
    total = begin
    biggest = max(entry[2] for entry in plan) * tall
    tokens = lefts[0].shape[0]
    count_left, count_right, count_extra = len(lefts), len(rights), len(extras)
    rolled = [jnp.roll(right, lane, axis=1) if lane else right for right in rights]
    carry_in = [carry] if lane else []
    targets = [] if target is None else [target]

    def left_spec(index):
        mine = [entry for entry in plan if entry[0] == index]

        def place(step):
            block = 0
            for _, _, _, start, blocks, _ in mine:
                block = jnp.where(step >= start, jnp.minimum(step - start, blocks - 1), block)
            return (0, block)

        return pl.BlockSpec((tokens, tall), place)

    def kernel(*refs):
        left_refs = refs[:count_left]
        right_refs = refs[count_left : count_left + count_right]
        at = count_left + count_right
        extra_refs = refs[at : at + count_extra]
        at += count_extra
        carry_refs = refs[at : at + len(carry_in)]
        at += len(carry_in) + len(targets)
        out = refs[at]
        flat, stage, shift, last, sems, extra_sems = refs[at + 1 :]
        step = pl.program_id(0)
        side = lax.rem(step, 2)

        def extra_copy(k):
            rows = extras[k][0].shape[0]
            return pltpu.make_async_copy(
                extra_refs[k], out.at[pl.ds(extras[k][1], rows), :], extra_sems.at[k]
            )

        @pl.when(step == 0)
        def _():
            for k in range(count_extra):
                extra_copy(k).start()
            if lane:
                shift[0:8, :] = carry_refs[0][...]
            if phase:
                flat[0:8, :] = jnp.zeros((8, LINE), jnp.float32)

        for left_at, right_at, per_row, start, blocks, row in plan:
            lines = per_row * tall

            def written(block, s, row=row, lines=lines):
                return pltpu.make_async_copy(
                    stage.at[s, pl.ds(0, lines), :],
                    out.at[pl.ds(pl.multiple_of(row + block * lines, 16), lines), :],
                    sems.at[s],
                )

            @pl.when((step >= start) & (step < start + blocks))
            def _():
                block = step - start
                if phase:

                    @pl.when(step > 0)
                    def _():
                        flat[0:8, :] = flat[lines : lines + 8, :]

                turned = left_refs[left_at][...].T
                lanes = lax.broadcasted_iota(jnp.int32, (tall, LINE), 1)
                for j0 in range(0, per_row, 2):
                    wide = min(2, per_row - j0)
                    tile = jnp.dot(
                        turned,
                        right_refs[right_at][:, j0 * LINE : (j0 + wide) * LINE],
                        preferred_element_type=jnp.float32,
                    )
                    for j in range(wide):
                        piece = tile[:, j * LINE : (j + 1) * LINE]
                        if lane and j0 + j == 0:
                            shift[8 : 8 + tall, :] = piece
                            piece = jnp.where(lanes < lane, shift[7 : 7 + tall, :], piece)
                            shift[0:8, :] = shift[tall : tall + 8, :]
                        if per_row == 1:
                            flat[phase : phase + tall, :] = piece
                        else:
                            flat[pl.ds(phase + j0 + j, tall, stride=per_row), :] = piece

                stage[side, 0:lines, :] = flat[0:lines, :].astype(jnp.bfloat16)
                written(block, side).start()

            @pl.when((step > start) & (step <= start + blocks))
            def _():
                written(step - start - 1, 1 - side).wait()

            if start + blocks == total:

                @pl.when(step == total - 1)
                def _():
                    written(blocks - 1, side).wait()

        @pl.when(step == total - 1)
        def _():
            if tail_rows:
                lanes = lax.broadcasted_iota(jnp.int32, (tail_rows, LINE), 1)
                rows_at = lax.broadcasted_iota(jnp.int32, (tail_rows, LINE), 0)
                final = jnp.broadcast_to(shift[7:8, :], (tail_rows, LINE))
                last[...] = jnp.where((rows_at == 0) & (lanes < lane), final, 0.0).astype(jnp.bfloat16)
                closing = pltpu.make_async_copy(
                    last, out.at[pl.ds(end_row, tail_rows), :], extra_sems.at[count_extra]
                )
                closing.start()
                closing.wait()
            for k in range(count_extra):
                extra_copy(k).wait()

    whole = [pl.BlockSpec(array.shape, lambda step: (0, 0)) for array in rolled]
    flops = sum(2 * tokens * entry[4] * tall * entry[2] * LINE for entry in plan)
    inputs = count_left + count_right + count_extra + len(carry_in) + len(targets)
    return pl.pallas_call(
        pinned(kernel, inputs, after),
        grid=(total,),
        in_specs=[left_spec(k) for k in range(count_left)]
        + whole
        + [pl.BlockSpec(array.shape, lambda step: (0, 0)) for array, _ in extras]
        + [pl.BlockSpec(array.shape, lambda step: (0, 0)) for array in carry_in]
        + [pl.BlockSpec(memory_space=pl.ANY)] * len(targets)
        + pins(after),
        out_specs=pl.BlockSpec(memory_space=pl.ANY),
        out_shape=jax.ShapeDtypeStruct((target_rows, LINE), jnp.bfloat16),
        scratch_shapes=[
            pltpu.VMEM((biggest + 16, LINE), jnp.float32),
            pltpu.VMEM((2, biggest, LINE), jnp.bfloat16),
            pltpu.VMEM((tall + 8, LINE), jnp.float32),
            pltpu.VMEM((max(tail_rows, 16), LINE), jnp.bfloat16),
            pltpu.SemaphoreType.DMA((2,)),
            pltpu.SemaphoreType.DMA((count_extra + 1,)),
        ],
        input_output_aliases={count_left + count_right + count_extra + len(carry_in): 0} if targets else {},
        compiler_params=pltpu.CompilerParams(vmem_limit_bytes=48 * 2**20),
        cost_estimate=pl.CostEstimate(flops=flops, bytes_accessed=total * biggest * LINE * 2, transcendentals=0),
        name="pack",
    )(*lefts, *rolled, *[array for array, _ in extras], *carry_in, *targets, *after)


def added(*parts):
    total = parts[0].astype(jnp.float32)
    for part in parts[1:]:
        total = total + part.astype(jnp.float32)
    return total.astype(jnp.bfloat16)


def reduce_stages(flat, batch, shift):
    z, y, x, c = (lax.axis_index(name) for name in GRID)
    length = PLANE + 32
    send = lax.dynamic_slice(flat, ((1 - c) * PLANE, 0), (length, LINE))
    (arrived,) = yield [(send, "c", SWAP)]
    chip = added(lax.dynamic_slice(flat, (c * PLANE, 0), (length, LINE)), arrived)

    def window(sy, sx, part):
        shard = sy * 4 + sx * 2 + part
        start = (shift + SHARD * shard) // 16 * 16
        return lax.dynamic_slice(chip, (start, 0), (WIN, LINE))

    away_0 = jnp.stack([window(1 - y, 0, 0), window(1 - y, 1, 0)])
    away_1 = jnp.stack([window(0, 1 - x, 1), window(1, 1 - x, 1)])
    home_0 = jnp.stack([window(y, 0, 0), window(y, 1, 0)])
    home_1 = jnp.stack([window(0, x, 1), window(1, x, 1)])
    got_0, got_1 = yield [(away_0, "y", SWAP), (away_1, "x", SWAP)]
    half_0, half_1 = added(home_0, got_0), added(home_1, got_1)
    pick = lambda value, at: lax.dynamic_index_in_dim(value, at, 0, keepdims=False)
    got_0, got_1 = yield [(pick(half_0, 1 - x), "x", SWAP), (pick(half_1, 1 - y), "y", SWAP)]
    columns = [added(pick(half_0, x), got_0), added(pick(half_1, y), got_1)]
    if batch == 0:
        hops = [((1, 0, 0), (2, 1, 1)), ((2, 0, 0), (3, 1, 1)), ((3, 0, 0), (0, 1, 1))]
    else:
        hops = [((1, 2, 0), (2, 3, 1)), ((0, 2, 0), (1, 3, 1)), ((3, 2, 0), (0, 3, 1))]
    if batch == 0:
        got = yield [(columns[0], ZC, zc_pairs(*hop)) for hop in hops]
        end = added(columns[0], *got)
        (column,) = fence(columns[1:], [end])
        got = yield [(column, ZC, zc_pairs(*hop)) for hop in hops]
        ends = [end, added(column, *got)]
    else:
        columns = jnp.stack(columns)
        got = yield [(columns, ZC, zc_pairs(*hop)) for hop in hops]
        ends = added(columns, *got)
    mine = jnp.where(c == 0, ends[0], ends[1])
    other = jnp.where(c == 0, ends[1], ends[0])
    (handed,) = yield [(other, ZC, [(2 * k + k % 2, 2 * k + 1 - k % 2) for k in range(4)])]
    return jnp.where(c == z % 2, mine, handed)


PIECE = 400


def corner_stages(flat):
    z, y, x, c = (lax.axis_index(name) for name in GRID)
    length = 8 * PIECE
    second = (8 + SHARD) // 16 * 16
    take = lambda at: lax.dynamic_slice(flat, (at * second, 0), (length, LINE))
    (arrived,) = yield [(take(1 - c), "c", SWAP)]
    chip = added(take(c), arrived).reshape(2, 2, 2, PIECE, LINE)
    pick = lambda value, at: lax.dynamic_index_in_dim(value, at, 0, keepdims=False)
    got = yield [(pick(chip[0], 1 - x), "x", SWAP), (pick(chip[1], 1 - y), "y", SWAP)]
    halves = [added(pick(chip[0], x), got[0]), added(pick(chip[1], y), got[1])]
    got = yield [(pick(halves[0], 1 - y), "y", SWAP), (pick(halves[1], 1 - x), "x", SWAP)]
    pieces = jnp.stack([added(pick(halves[0], y), got[0]), added(pick(halves[1], x), got[1])])
    got = yield [(pieces, "z", [(k, 0)]) for k in (1, 2, 3)]
    pieces = added(pieces, *got)
    got = yield [(pieces[0], "y", [(1, 0)]), (pieces[1], "x", [(1, 0)])]
    halves = [jnp.stack([pieces[0], got[0]]), jnp.stack([pieces[1], got[1]])]
    got = yield [(halves[0], "x", [(1, 0)]), (halves[1], "y", [(1, 0)])]
    return jnp.stack([halves[0], got[0], halves[1], got[1]]).reshape(length, LINE)


CHUNK = 128
NT = (((1,), (1,)), ((), ()))
TN = (((0,), (0,)), ((), ()))
INNER = SSM_HEADS * SSM_DIM
PAIRS = SSM_HEADS // 2


def spread(rows_a, rows_b):
    length = rows_a.shape[1]
    tall = jnp.concatenate(
        [jnp.broadcast_to(rows_a, (SSM_DIM, length)), jnp.broadcast_to(rows_b, (SSM_DIM, length))], axis=0
    )
    return tall.T


CHANNELS = INNER + 2 * STATE
LANES = 2 * SSM_DIM
COLUMNS = CHANNELS // LANES


def conv_masks(masks, start_ref, first, rows):
    place = first + lax.broadcasted_iota(jnp.int32, (rows, LANES), 0) - start_ref[...]
    for reach in range(1, CONV):
        masks[reach - 1] = jnp.where(place >= reach, 1.0, 0.0)


def conv_parts(ext, weight_ref, bias_ref, masks, rows):
    windows = []
    total = bias_ref[...]
    for tap in range(CONV):
        reach = CONV - 1 - tap
        window = ext[8 - reach : 8 - reach + rows, :]
        if reach:
            window = window * masks[reach - 1]
        windows.append(window)
        total = total + window * weight_ref[tap : tap + 1, :]
    return windows, total


def conv_forward(xbc, rim, weight, bias, meta, start_column, after=()):
    rows = xbc.shape[0]

    def kernel(meta_ref, x_ref, rim_ref, weight_ref, bias_ref, start_ref, out_ref, ext, masks):
        @pl.when(pl.program_id(0) == 0)
        def _():
            conv_masks(masks, start_ref, meta_ref[0], rows)

        ext[0:8, :] = rim_ref[...]
        ext[8:, :] = x_ref[...]
        _, total = conv_parts(ext, weight_ref, bias_ref, masks, rows)
        out_ref[...] = total * jax.nn.sigmoid(total)

    lanes = lambda i, m: (0, i)
    return pl.pallas_call(
        pinned(kernel, 6, after),
        grid_spec=pltpu.PrefetchScalarGridSpec(
            num_scalar_prefetch=1,
            grid=(COLUMNS,),
            in_specs=[
                pl.BlockSpec((rows, LANES), lanes),
                pl.BlockSpec((8, LANES), lanes),
                pl.BlockSpec((CONV, LANES), lanes),
                pl.BlockSpec((1, LANES), lanes),
                pl.BlockSpec((rows, 1), lambda i, m: (0, 0)),
            ] + pins(after),
            out_specs=pl.BlockSpec((rows, LANES), lanes),
            scratch_shapes=[
                pltpu.VMEM((rows + 8, LANES), jnp.float32),
                pltpu.VMEM((CONV - 1, rows, LANES), jnp.float32),
            ],
        ),
        out_shape=jax.ShapeDtypeStruct((rows, CHANNELS), jnp.float32),
        cost_estimate=pl.CostEstimate(flops=10**9, bytes_accessed=rows * CHANNELS * 8, transcendentals=0),
        name="conv",
    )(meta, xbc, rim, weight, bias, start_column, *after)


def conv_backward(dx, db, dc, xbc, rim, weight, bias, meta, start_column, after=()):
    rows = xbc.shape[0]

    def kernel(meta_ref, dx_ref, db_ref, dc_ref, x_ref, rim_ref, weight_ref, bias_ref, start_ref,
               low_ref, tail_ref, edge_ref, small_ref, ext, upper, masks):
        @pl.when(pl.program_id(0) == 0)
        def _():
            conv_masks(masks, start_ref, meta_ref[0], rows)
            upper[0:8, :] = jnp.zeros((8, LANES), jnp.float32)
            upper[8 + rows :, :] = jnp.zeros((8, LANES), jnp.float32)

        ext[0:8, :] = rim_ref[...]
        ext[8:, :] = x_ref[...]
        at = pl.program_id(0)
        arrived = jnp.where(at < PAIRS, dx_ref[...], jnp.where(at == PAIRS, db_ref[...], dc_ref[...]))
        windows, total = conv_parts(ext, weight_ref, bias_ref, masks, rows)
        gate = jax.nn.sigmoid(total)
        change = arrived * gate * (1.0 + total * (1.0 - gate))
        main = jnp.zeros((rows, LANES), jnp.float32)
        edge = jnp.zeros((8, LANES), jnp.float32)
        small_ref[...] = jnp.zeros((8, LANES), jnp.float32)
        small_ref[CONV : CONV + 1, :] = jnp.sum(change, axis=0, keepdims=True)
        for tap in range(CONV):
            reach = CONV - 1 - tap
            small_ref[tap : tap + 1, :] = jnp.sum(change * windows[tap], axis=0, keepdims=True)
            masked = change * masks[reach - 1] if reach else change
            upper[8 : 8 + rows, :] = masked * weight_ref[tap : tap + 1, :]
            main = main + upper[8 + reach : 8 + reach + rows, :]
            edge = edge + upper[reach : reach + 8, :]
        low_ref[...] = main.astype(jnp.bfloat16)
        tail_ref[...] = main[rows - 16 :, :]
        edge_ref[...] = edge

    lanes = lambda i, m: (0, i)
    whole = lambda i, m: (0, 0)
    return pl.pallas_call(
        pinned(kernel, 9, after),
        grid_spec=pltpu.PrefetchScalarGridSpec(
            num_scalar_prefetch=1,
            grid=(COLUMNS,),
            in_specs=[
                pl.BlockSpec((rows, LANES), lambda i, m: (0, jnp.minimum(i, PAIRS - 1))),
                pl.BlockSpec((rows, STATE), whole),
                pl.BlockSpec((rows, STATE), whole),
                pl.BlockSpec((rows, LANES), lanes),
                pl.BlockSpec((8, LANES), lanes),
                pl.BlockSpec((CONV, LANES), lanes),
                pl.BlockSpec((1, LANES), lanes),
                pl.BlockSpec((rows, 1), whole),
            ] + pins(after),
            out_specs=[
                pl.BlockSpec((rows, LANES), lanes),
                pl.BlockSpec((16, LANES), lanes),
                pl.BlockSpec((8, LANES), lanes),
                pl.BlockSpec((8, LANES), lanes),
            ],
            scratch_shapes=[
                pltpu.VMEM((rows + 8, LANES), jnp.float32),
                pltpu.VMEM((rows + 16, LANES), jnp.float32),
                pltpu.VMEM((CONV - 1, rows, LANES), jnp.float32),
            ],
        ),
        out_shape=[
            jax.ShapeDtypeStruct((rows, CHANNELS), jnp.bfloat16),
            jax.ShapeDtypeStruct((16, CHANNELS), jnp.float32),
            jax.ShapeDtypeStruct((8, CHANNELS), jnp.float32),
            jax.ShapeDtypeStruct((8, CHANNELS), jnp.float32),
        ],
        cost_estimate=pl.CostEstimate(flops=2 * 10**9, bytes_accessed=rows * CHANNELS * 10, transcendentals=0),
        name="conv_back",
    )(meta, dx, db, dc, xbc, rim, weight, bias, start_column, *after)


def weighted_state(left, left_block, values, weight_rows, after=()):
    rows = left.shape[0]

    def kernel(left_ref, value_ref, weight_ref, out_ref, turned):
        @pl.when(pl.program_id(0) == 0)
        def _():
            turned[...] = left_ref[...].T

        scaled = [(turned[...] * weight_ref[0, e : e + 1, :]).astype(jnp.bfloat16) for e in range(2)]
        both = jnp.dot(
            jnp.concatenate(scaled, axis=0), value_ref[...].astype(jnp.bfloat16), preferred_element_type=jnp.float32
        )
        low_lane = lax.broadcasted_iota(jnp.int32, (STATE, 2 * SSM_DIM), 1) < SSM_DIM
        out_ref[...] = jnp.where(low_lane, both[:STATE], both[STATE:])

    return pl.pallas_call(
        pinned(kernel, 3, after),
        grid=(PAIRS,),
        in_specs=[
            pl.BlockSpec((rows, STATE), lambda i: (0, left_block)),
            pl.BlockSpec((rows, 2 * SSM_DIM), lambda i: (0, i)),
            pl.BlockSpec((1, 2, rows), lambda i: (i, 0, 0)),
        ] + pins(after),
        out_specs=pl.BlockSpec((STATE, 2 * SSM_DIM), lambda i: (0, i)),
        out_shape=jax.ShapeDtypeStruct((STATE, INNER), jnp.float32),
        scratch_shapes=[pltpu.VMEM((STATE, rows), jnp.float32)],
        cost_estimate=pl.CostEstimate(flops=2 * rows * STATE * INNER, bytes_accessed=rows * INNER * 4, transcendentals=0),
        name="state",
    )(left, values, weight_rows.reshape(PAIRS, 2, rows), *after)


def chunk_rows(k, meta_ref, cum_ref, start_ref):
    here = slice(k * CHUNK, (k + 1) * CHUNK)
    first = meta_ref[0] + k * CHUNK
    index = first + lax.broadcasted_iota(jnp.int32, (1, CHUNK), 1)
    entering = start_ref[0:1, here] < first
    ending = index >= meta_ref[1 + k]
    cums, entries, tails = [], [], []
    for e in range(2):
        cum = cum_ref[0, e : e + 1, here]
        cums.append(cum)
        entries.append(jnp.where(entering, jnp.exp(cum), 0.0))
        gap = jnp.where(ending, cum[:, CHUNK - 1 :] - cum, masked_score)
        tails.append(jnp.exp(gap))
    return cums, entries, tails


def ssm_forward(conv, cum, step, state_in, skip, meta, start_column, start_row):
    rows = conv.shape[0]
    chunks = rows // CHUNK

    def kernel(meta_ref, x_ref, b_ref, c_ref, cum_ref, step_ref, state_ref, skip_ref, col_ref, row_ref,
               y_ref, inner, hide, state, b_turned):
        @pl.when(pl.program_id(0) == 0)
        def _():
            for k in range(chunks):
                here = slice(k * CHUNK, (k + 1) * CHUNK)
                b_turned[:, here] = b_ref[here, :].T.astype(jnp.bfloat16)
                inner[k] = lax.dot_general(
                    c_ref[here, :], b_ref[here, :], NT, precision=highest, preferred_element_type=jnp.float32
                )
                t = lax.broadcasted_iota(jnp.int32, (CHUNK, CHUNK), 0)
                s = lax.broadcasted_iota(jnp.int32, (CHUNK, CHUNK), 1)
                shown = (s <= t) & (meta_ref[0] + k * CHUNK + s >= col_ref[here, :])
                hide[k] = jnp.where(shown, 0.0, masked_score)

        low_lane = lax.broadcasted_iota(jnp.int32, (CHUNK, 2 * SSM_DIM), 1) < SSM_DIM
        state[...] = state_ref[...]
        for k in range(chunks):
            here = slice(k * CHUNK, (k + 1) * CHUNK)
            cums, entries, tails = chunk_rows(k, meta_ref, cum_ref, row_ref)
            x_now = x_ref[here, :]
            x_low = x_now.astype(jnp.bfloat16)
            entry = spread(*entries)
            weight = spread(*[tails[e] * step_ref[0, e : e + 1, here] for e in range(2)])
            parts = []
            for e in range(2):
                across = jnp.broadcast_to(cums[e], (CHUNK, CHUNK))
                decays = jnp.exp(across.T - across + hide[k])
                mix = (inner[k] * decays * step_ref[0, e : e + 1, here]).astype(jnp.bfloat16)
                parts.append(jnp.dot(mix, x_low, preferred_element_type=jnp.float32))
            carried = jnp.dot(
                c_ref[here, :].astype(jnp.bfloat16), state[...].astype(jnp.bfloat16),
                preferred_element_type=jnp.float32,
            )
            y_ref[here, :] = jnp.where(low_lane, parts[0], parts[1]) + entry * carried + skip_ref[...] * x_now
            fresh = jnp.dot(
                b_turned[:, here], (x_now * weight).astype(jnp.bfloat16), preferred_element_type=jnp.float32
            )
            state[...] = entry[CHUNK - 1 :, :] * state[...] + fresh

    whole = lambda i, m: (0, 0)
    lanes = lambda i, m: (0, i)
    return pl.pallas_call(
        kernel,
        grid_spec=pltpu.PrefetchScalarGridSpec(
            num_scalar_prefetch=1,
            grid=(PAIRS,),
            in_specs=[
                pl.BlockSpec((rows, 2 * SSM_DIM), lanes),
                pl.BlockSpec((rows, STATE), lambda i, m: (0, PAIRS)),
                pl.BlockSpec((rows, STATE), lambda i, m: (0, PAIRS + 1)),
                pl.BlockSpec((1, 2, rows), lambda i, m: (i, 0, 0)),
                pl.BlockSpec((1, 2, rows), lambda i, m: (i, 0, 0)),
                pl.BlockSpec((STATE, 2 * SSM_DIM), lanes),
                pl.BlockSpec((1, 2 * SSM_DIM), lanes),
                pl.BlockSpec((rows, 1), whole),
                pl.BlockSpec((8, rows), whole),
            ],
            out_specs=pl.BlockSpec((rows, 2 * SSM_DIM), lanes),
            scratch_shapes=[
                pltpu.VMEM((chunks, CHUNK, CHUNK), jnp.float32),
                pltpu.VMEM((chunks, CHUNK, CHUNK), jnp.float32),
                pltpu.VMEM((STATE, 2 * SSM_DIM), jnp.float32),
                pltpu.VMEM((STATE, rows), jnp.bfloat16),
            ],
        ),
        out_shape=jax.ShapeDtypeStruct((rows, INNER), jnp.float32),
        compiler_params=pltpu.CompilerParams(vmem_limit_bytes=40 * 2**20),
        cost_estimate=pl.CostEstimate(flops=10**9, bytes_accessed=rows * INNER * 8, transcendentals=2**21),
        name="ssm",
    )(meta, conv, conv, conv, cum.reshape(PAIRS, 2, rows), step.reshape(PAIRS, 2, rows), state_in, skip,
      start_column, start_row)


def ssm_backward(conv, dy, cum, step, state_in, state_grad, skip, meta, start_row, after=()):
    rows = conv.shape[0]
    chunks = rows // CHUNK

    def kernel(meta_ref, x_ref, dy_ref, b_ref, c_ref, cum_ref, step_ref, state_ref, grad_ref, skip_ref, row_ref,
               dx_ref, db_ref, dc_ref, small_ref, inner, hide, inner_grad, states, flow,
               b_turned, c_turned):
        low = lambda v: v.astype(jnp.bfloat16)
        dot = lambda p, q, dims=(((1,), (0,)), ((), ())): lax.dot_general(
            p, q, dims, preferred_element_type=jnp.float32
        )
        exact = lambda p, q, dims=(((1,), (0,)), ((), ())): lax.dot_general(
            p, q, dims, precision=highest, preferred_element_type=jnp.float32
        )
        s = lax.broadcasted_iota(jnp.int32, (CHUNK, CHUNK), 0)
        t = lax.broadcasted_iota(jnp.int32, (CHUNK, CHUNK), 1)

        @pl.when(pl.program_id(0) == 0)
        def _():
            db_ref[...] = jnp.zeros(db_ref.shape, jnp.float32)
            dc_ref[...] = jnp.zeros(dc_ref.shape, jnp.float32)
            inner_grad[...] = jnp.zeros(inner_grad.shape, jnp.float32)
            for k in range(chunks):
                here = slice(k * CHUNK, (k + 1) * CHUNK)
                b_turned[:, here] = low(b_ref[here, :].T)
                c_turned[:, here] = low(c_ref[here, :].T)
                inner[k] = exact(b_ref[here, :], c_ref[here, :], NT)
                shown = (s <= t) & (meta_ref[0] + k * CHUNK + s >= row_ref[0:1, here])
                hide[k] = jnp.where(shown, 0.0, masked_score)

        before = (s < t).astype(jnp.float32)
        until = low((s >= t).astype(jnp.float32))
        low_lane = t < SSM_DIM
        pick_row = lax.broadcasted_iota(jnp.int32, (8, 2 * SSM_DIM), 0)
        pick_lane = lax.broadcasted_iota(jnp.int32, (8, 2 * SSM_DIM), 1) // SSM_DIM
        pick = low((pick_row == pick_lane).astype(jnp.float32))
        spreads = []
        states[0] = state_ref[...]
        for k in range(chunks):
            here = slice(k * CHUNK, (k + 1) * CHUNK)
            cums, entries, tails = chunk_rows(k, meta_ref, cum_ref, row_ref)
            entry, tail = spread(*entries), spread(*tails)
            steps = spread(step_ref[0, 0:1, here], step_ref[0, 1:2, here])
            spreads.append((cums, entry, tail, steps))
            if k < chunks - 1:
                fresh = dot(b_turned[:, here], low(x_ref[here, :] * steps * tail))
                states[k + 1] = entry[CHUNK - 1 :, :] * states[k] + fresh
        flow[...] = grad_ref[...]
        skip_sum = jnp.zeros((1, 2 * SSM_DIM), jnp.float32)
        for k in reversed(range(chunks)):
            here = slice(k * CHUNK, (k + 1) * CHUNK)
            cums, entry, tail, steps = spreads[k]
            x_now, dy_now = x_ref[here, :], dy_ref[here, :]
            b_low, c_low = low(b_ref[here, :]), low(c_ref[here, :])
            scaled = x_now * steps
            dy_low = low(dy_now)
            flow_low, state_low = low(flow[...]), low(states[k])
            both = low(
                jnp.concatenate([jnp.where(low_lane, scaled, 0.0), jnp.where(low_lane, 0.0, scaled)], axis=0)
            )
            reached = dot(both, dy_low, NT)
            mixes, weighed = [], []
            for e in range(2):
                across = jnp.broadcast_to(cums[e], (CHUNK, CHUNK))
                decays = jnp.exp(across - across.T + hide[k])
                reach = decays * reached[e * CHUNK : (e + 1) * CHUNK]
                inner_grad[k] += reach
                weighed.append(low(inner[k] * reach))
                mixes.append(low(inner[k] * decays))
            sums = dot(jnp.concatenate(weighed, axis=0), until)
            within = [
                jnp.sum(sums[e * CHUNK : (e + 1) * CHUNK] * before, axis=0, keepdims=True) for e in range(2)
            ]
            mixed = dot(jnp.concatenate(mixes, axis=0), dy_low)
            back = tail * dot(b_low, flow_low)
            dxs = jnp.where(low_lane, mixed[:CHUNK], mixed[CHUNK:]) + back
            db_ref[here, :] += dot(low(scaled * tail), flow_low, NT)
            entered = low(dy_now * entry)
            dc_ref[here, :] += dot(entered, state_low, NT)
            brought = dy_now * entry * dot(c_low, state_low)
            ends = dot(pick, low(brought), NT)
            begins = dot(pick, low(scaled * back), NT)
            direct = dot(pick, low(x_now * dxs), NT)
            through = jnp.sum(flow[...] * states[k], axis=0, keepdims=True) * entry[CHUNK - 1 :, :]
            log_grad = exact(ends, until.astype(jnp.float32)) + exact(begins, before)
            for e in range(2):
                lanes = slice(e * SSM_DIM, (e + 1) * SSM_DIM)
                kept = jnp.sum(through[:, lanes], axis=1, keepdims=True)
                small_ref[0, e : e + 1, here] = direct[e : e + 1, :]
                small_ref[0, 2 + e : 3 + e, here] = log_grad[e : e + 1, :] + within[e] + kept
            dx_ref[here, :] = dxs * steps + skip_ref[...] * dy_now
            skip_sum += jnp.sum(x_now * dy_now, axis=0, keepdims=True)
            flow[...] = entry[CHUNK - 1 :, :] * flow[...] + dot(c_turned[:, here], entered)
        small_ref[0, 4:8, :] = jnp.zeros((4, rows), jnp.float32)
        small_ref[0, 4:5, 0 : 2 * SSM_DIM] = skip_sum

        @pl.when(pl.program_id(0) == PAIRS - 1)
        def _():
            for k in range(chunks):
                here = slice(k * CHUNK, (k + 1) * CHUNK)
                grads = low(inner_grad[k])
                db_ref[here, :] += dot(grads, low(c_ref[here, :]))
                dc_ref[here, :] += dot(grads, low(b_ref[here, :]), TN)

    whole = lambda i, m: (0, 0)
    lanes = lambda i, m: (0, i)
    pair = lambda i, m: (i, 0, 0)
    return pl.pallas_call(
        pinned(kernel, 11, after),
        grid_spec=pltpu.PrefetchScalarGridSpec(
            num_scalar_prefetch=1,
            grid=(PAIRS,),
            in_specs=[
                pl.BlockSpec((rows, 2 * SSM_DIM), lanes),
                pl.BlockSpec((rows, 2 * SSM_DIM), lanes),
                pl.BlockSpec((rows, STATE), lambda i, m: (0, PAIRS)),
                pl.BlockSpec((rows, STATE), lambda i, m: (0, PAIRS + 1)),
                pl.BlockSpec((1, 2, rows), pair),
                pl.BlockSpec((1, 2, rows), pair),
                pl.BlockSpec((STATE, 2 * SSM_DIM), lanes),
                pl.BlockSpec((STATE, 2 * SSM_DIM), lanes),
                pl.BlockSpec((1, 2 * SSM_DIM), lanes),
                pl.BlockSpec((8, rows), whole),
            ] + pins(after),
            out_specs=[
                pl.BlockSpec((rows, 2 * SSM_DIM), lanes),
                pl.BlockSpec((rows, STATE), whole),
                pl.BlockSpec((rows, STATE), whole),
                pl.BlockSpec((1, 8, rows), pair),
            ],
            scratch_shapes=[
                pltpu.VMEM((chunks, CHUNK, CHUNK), jnp.float32),
                pltpu.VMEM((chunks, CHUNK, CHUNK), jnp.float32),
                pltpu.VMEM((chunks, CHUNK, CHUNK), jnp.float32),
                pltpu.VMEM((chunks, STATE, 2 * SSM_DIM), jnp.float32),
                pltpu.VMEM((STATE, 2 * SSM_DIM), jnp.float32),
                pltpu.VMEM((STATE, rows), jnp.bfloat16),
                pltpu.VMEM((STATE, rows), jnp.bfloat16),
            ],
        ),
        out_shape=[
            jax.ShapeDtypeStruct((rows, INNER), jnp.float32),
            jax.ShapeDtypeStruct((rows, STATE), jnp.float32),
            jax.ShapeDtypeStruct((rows, STATE), jnp.float32),
            jax.ShapeDtypeStruct((PAIRS, 8, rows), jnp.float32),
        ],
        compiler_params=pltpu.CompilerParams(vmem_limit_bytes=40 * 2**20),
        cost_estimate=pl.CostEstimate(flops=3 * 10**9, bytes_accessed=rows * INNER * 12, transcendentals=2**21),
        name="ssm_back",
    )(meta, conv, dy, conv, conv, cum.reshape(PAIRS, 2, rows), step.reshape(PAIRS, 2, rows), state_in, state_grad,
      skip, start_row, *after)


def chain_states(earlier, later):
    return (earlier[0] * later[0], earlier[1] * later[0] + later[1])


def scan_states(carry, state, span, fast, backward):
    wide = jnp.repeat(carry, SSM_DIM)[None, :]
    if not fast:
        ident = (jnp.ones_like(wide), jnp.zeros_like(state))
        return (carried_in if backward else prefix)((wide, state), span, chain_states, ident)[1]
    flow = Flow(scan_stages(carry, state, backward))
    while flow.sends:
        flow.go()
    return flow.result


def scan_stages(carry, state, backward, extra=None):
    total = (jnp.repeat(carry, SSM_DIM)[None, :], state)
    start = None
    for name in ("c", "x", "y"):
        place = lax.axis_index(name)
        rows = [total[1], total[0]]
        if extra is None:
            rows.append(jnp.zeros((15, INNER), jnp.float32))
        else:
            rest = extra
            for _ in range(3):
                term = lax.reduce_precision(rest, 8, 7)
                rows.append(jnp.pad(term, (0, INNER - term.shape[0]))[None, :])
                rest = rest - term
            rows.append(jnp.zeros((12, INNER), jnp.float32))
        packed = jnp.concatenate(rows, axis=0)
        (packed,) = yield [(packed.astype(jnp.bfloat16), name, SWAP)]
        packed = packed.astype(jnp.float32)
        other = (packed[STATE : STATE + 1], packed[:STATE])
        if extra is not None:
            extra = extra + jnp.sum(packed[STATE + 1 : STATE + 4, : extra.shape[0]], axis=0)
        leads = place == (0 if backward else 1)
        seen = (jnp.where(leads, other[0], 1.0), jnp.where(leads, other[1], 0.0))
        start = seen if start is None else chain_states(seen, start)
        if name != "y":
            forward = chain_states(other, total)
            reverse = chain_states(total, other)
            total = jax.tree.map(lambda p, q: jnp.where(leads, p, q), forward, reverse)
    return start[1] if extra is None else [start[1], extra]


KEYS = 512
PAIR = 2 * HEAD_DIM


def attention_forward(q_wide, kv, meta, starts, after=()):
    rows = q_wide.shape[2]
    blocks = kv.shape[0]
    ratio = HEADS_Q // HEADS_KV
    wide = min(512, rows)

    def kernel(meta_ref, q_ref, kv_ref, start_ref, o_ref, log_ref, top, total):
        b = pl.program_id(1)

        @pl.when(b == 0)
        def _():
            top[...] = jnp.full(top.shape, masked_score, jnp.float32)
            total[...] = jnp.zeros(total.shape, jnp.float32)
            o_ref[...] = jnp.zeros(o_ref.shape, jnp.float32)

        def block(partial):
            pair = kv_ref[0, 0]
            turned = pair.T[HEAD_DIM:, :]
            for h in range(ratio):
                for r in range(0, rows, wide):
                    here = slice(r, r + wide)
                    scores = jnp.dot(pair, q_ref[h, :, here], preferred_element_type=jnp.float32)
                    if partial:
                        keys = b * KEYS + lax.broadcasted_iota(jnp.int32, scores.shape, 0)
                        mine = meta_ref[2] + r + lax.broadcasted_iota(jnp.int32, scores.shape, 1)
                        visible = (keys >= start_ref[0:1, here]) & (keys <= mine)
                        scores = jnp.where(visible, scores, masked_score)
                    before = top[h, 0:1, here]
                    peak = jnp.maximum(before, jnp.max(scores, axis=0, keepdims=True))
                    part = jnp.exp(scores - peak)
                    if partial:
                        part = jnp.where(visible, part, 0.0)
                    fade = jnp.exp(before - peak)
                    top[h, 0:1, here] = peak
                    total[h, 0:1, here] = total[h, 0:1, here] * fade + jnp.sum(part, axis=0, keepdims=True)
                    o_ref[h, :, here] = o_ref[h, :, here] * fade + jnp.dot(
                        turned, part.astype(jnp.bfloat16), preferred_element_type=jnp.float32
                    )

        needed = (b >= meta_ref[0]) & (b < meta_ref[1])
        partial = ((b + 1) * KEYS > meta_ref[2]) | (b * KEYS < meta_ref[3])

        @pl.when(needed & partial)
        def _():
            block(True)

        @pl.when(needed & jnp.logical_not(partial))
        def _():
            block(False)

        @pl.when(b == blocks - 1)
        def _():
            for h in range(ratio):
                sums = total[h, 0:1, :]
                o_ref[h] = o_ref[h] / sums
                log_ref[h] = jnp.broadcast_to(top[h, 0:1, :] + jnp.log(sums), (8, rows))

    heads = lambda g, b, m: (g, 0, 0)
    return pl.pallas_call(
        pinned(kernel, 4, after),
        grid_spec=pltpu.PrefetchScalarGridSpec(
            num_scalar_prefetch=1,
            grid=(HEADS_KV, blocks),
            in_specs=[
                pl.BlockSpec((ratio, PAIR, rows), heads),
                pl.BlockSpec((1, 1, KEYS, PAIR), lambda g, b, m: (b, g, 0, 0)),
                pl.BlockSpec((8, rows), lambda g, b, m: (0, 0)),
            ] + pins(after),
            out_specs=[
                pl.BlockSpec((ratio, HEAD_DIM, rows), heads),
                pl.BlockSpec((ratio, 8, rows), heads),
            ],
            scratch_shapes=[
                pltpu.VMEM((ratio, 8, rows), jnp.float32),
                pltpu.VMEM((ratio, 8, rows), jnp.float32),
            ],
        ),
        out_shape=[
            jax.ShapeDtypeStruct((HEADS_Q, HEAD_DIM, rows), jnp.float32),
            jax.ShapeDtypeStruct((HEADS_Q, 8, rows), jnp.float32),
        ],
        compiler_params=pltpu.CompilerParams(vmem_limit_bytes=48 * 2**20),
        cost_estimate=pl.CostEstimate(flops=2 * 10**10, bytes_accessed=2**23, transcendentals=2**23),
        name="attend",
    )(meta, q_wide, kv, starts, *after)


def attention_backward(q_wide, g_wide, kv, logs, mixed, meta, starts, group, after=()):
    rows = q_wide.shape[2]
    blocks = kv.shape[0]
    ratio = HEADS_Q // HEADS_KV
    wide = min(512, rows)

    def kernel(meta_ref, q_ref, g_ref, kv_ref, log_ref, o_ref, start_ref, dkv_ref, dq_ref, delta, sums):
        b = pl.program_id(0)

        @pl.when(b == 0)
        def _():
            dq_ref[...] = jnp.zeros(dq_ref.shape, jnp.float32)
            for h in range(ratio):
                both = g_ref[h, HEAD_DIM:, :].astype(jnp.float32) * o_ref[h]
                delta[h] = jnp.broadcast_to(jnp.sum(both, axis=0, keepdims=True), (8, rows))

        def block(partial):
            pair = kv_ref[0, 0]
            turned = pair.T[:HEAD_DIM, :]
            for h in range(ratio):
                for r in range(0, rows, wide):
                    here = slice(r, r + wide)
                    q_now = q_ref[h, :, here]
                    g_now = g_ref[h, :, here]
                    scores = jnp.dot(pair, q_now, preferred_element_type=jnp.float32)
                    probs = jnp.exp(scores - log_ref[h, 0:1, here])
                    if partial:
                        keys = b * KEYS + lax.broadcasted_iota(jnp.int32, scores.shape, 0)
                        mine = meta_ref[2] + r + lax.broadcasted_iota(jnp.int32, scores.shape, 1)
                        visible = (keys >= start_ref[0:1, here]) & (keys <= mine)
                        probs = jnp.where(visible, probs, 0.0)
                    grads = jnp.dot(pair, g_now, preferred_element_type=jnp.float32)
                    low_grads = (probs * (grads - delta[h, 0:1, here])).astype(jnp.bfloat16)
                    change = lax.dot_general(
                        probs.astype(jnp.bfloat16), g_now, NT, preferred_element_type=jnp.float32
                    ) + lax.dot_general(low_grads, q_now, NT, preferred_element_type=jnp.float32)
                    if h == 0 and r == 0:
                        sums[...] = change
                    else:
                        sums[...] += change
                    dq_ref[h, :, here] += jnp.dot(turned, low_grads, preferred_element_type=jnp.float32)
            dkv_ref[0, 0] = sums[...].astype(jnp.bfloat16)

        needed = (b >= meta_ref[0]) & (b < meta_ref[1])
        partial = ((b + 1) * KEYS > meta_ref[2]) | (b * KEYS < meta_ref[3])

        @pl.when(needed & partial)
        def _():
            block(True)

        @pl.when(needed & jnp.logical_not(partial))
        def _():
            block(False)

        @pl.when(jnp.logical_not(needed))
        def _():
            dkv_ref[0, 0] = jnp.zeros((KEYS, PAIR), jnp.bfloat16)

    heads = lambda b, m: (group, 0, 0)
    return pl.pallas_call(
        pinned(kernel, 7, after),
        grid_spec=pltpu.PrefetchScalarGridSpec(
            num_scalar_prefetch=1,
            grid=(blocks,),
            in_specs=[
                pl.BlockSpec((ratio, PAIR, rows), heads),
                pl.BlockSpec((ratio, PAIR, rows), heads),
                pl.BlockSpec((1, 1, KEYS, PAIR), lambda b, m: (b, group, 0, 0)),
                pl.BlockSpec((ratio, 8, rows), heads),
                pl.BlockSpec((ratio, HEAD_DIM, rows), heads),
                pl.BlockSpec((8, rows), lambda b, m: (0, 0)),
            ] + pins(after),
            out_specs=[
                pl.BlockSpec((1, 1, KEYS, PAIR), lambda b, m: (b, 0, 0, 0)),
                pl.BlockSpec((ratio, HEAD_DIM, rows), lambda b, m: (0, 0, 0)),
            ],
            scratch_shapes=[
                pltpu.VMEM((ratio, 8, rows), jnp.float32),
                pltpu.VMEM((KEYS, PAIR), jnp.float32),
            ],
        ),
        out_shape=[
            jax.ShapeDtypeStruct((blocks, 1, KEYS, PAIR), jnp.bfloat16),
            jax.ShapeDtypeStruct((ratio, HEAD_DIM, rows), jnp.float32),
        ],
        compiler_params=pltpu.CompilerParams(vmem_limit_bytes=48 * 2**20),
        cost_estimate=pl.CostEstimate(flops=2 * 10**10, bytes_accessed=2**23, transcendentals=2**23),
        name="attend_back",
    )(meta, q_wide, g_wide, kv, logs, mixed, starts, *after)


def scatter_span(value, span, fast):
    if not fast:
        return lax.psum_scatter(value, span, scatter_dimension=0).astype(jnp.float32)
    flow = Flow(scatter_stages(value))
    while flow.sends:
        flow.go()
    return flow.result


def scatter_stages(value):
    _, y, x, c = (lax.axis_index(name) for name in GRID)
    value = value.reshape((2, 2, 2) + value.shape[1:])
    for name, place, axis in (("c", c, 2), ("y", y, 0), ("x", x, 0)):
        send = lax.dynamic_index_in_dim(value, 1 - place, axis, keepdims=False)
        (arrived,) = yield [(send, name, SWAP)]
        keep = lax.dynamic_index_in_dim(value, place, axis, keepdims=False)
        value = keep.astype(jnp.float32) + arrived.astype(jnp.float32)
        if name != "x":
            value = value.astype(jnp.bfloat16)
    return value


def plane_stages(value):
    for pairs in ([(0, 1), (1, 0), (2, 3), (3, 2)], [(0, 2), (2, 0), (1, 3), (3, 1)]):
        (other,) = yield [(value, "z", pairs)]
        value = value + other
    return value


def offsets_of():
    places, at = {}, 0
    for name_key, extent in layout():
        places[name_key] = (at, extent)
        at += math.prod(extent)
    return places


def early_weights(params):
    places = offsets_of()
    buffers, spread_flow, (slots, all_slots), where = gather_lines(params)
    spread_flow.go()
    names = (W_QUERY, W_KEY, W_VALUE, W_ATTN_OUT, W_GATE_SSM, W_X_SSM, W_B_C)
    misc_at = places[W_STEP][0]
    first = unpack_lines(
        buffers[:16], slots, where, [flat_segment(name_key) for name_key in names] + [(0, 16, LINE), (misc_at, 288, LINE)]
    )
    weights = dict(zip(names, first))
    weights[NORM_ATTN] = first[-2].reshape(-1)[:D]
    misc = first[-1].reshape(-1)
    for name_key in (W_STEP,) + small_names[1:-1]:
        at, extent = places[name_key]
        weights[name_key] = misc[at - misc_at : at - misc_at + math.prod(extent)].reshape(extent)
    return weights, spread_flow, (buffers, all_slots, where)


def flat_segment(name_key):
    at, extent = offsets_of()[name_key]
    return (at, extent[0], extent[1])


def late_weights(held, after):
    buffers, slots, where = held
    names = (W_SSM_OUT, W_GATE, W_UP_PROJ, W_DOWN)
    norm_at = offsets_of()[NORM_FFN][0]
    second = unpack_lines(
        buffers, slots, where, [flat_segment(name_key) for name_key in names] + [(norm_at, 16, LINE)], after
    )
    weights = dict(zip(names, second))
    weights[NORM_FFN] = second[-1].reshape(-1)[norm_at % LINE : norm_at % LINE + D]
    return weights


def pack_late(gate, up, down, ssm_low, grad_branch, grad_norm_ffn, after):
    places = offsets_of()
    out_at = places[W_SSM_OUT][0]
    lane = places[W_GATE][0] % LINE
    boundary = 2 * PLANE * LINE
    tail_from = (boundary - out_at) // D
    tail = matmul_left_t(ssm_low[:, tail_from:], grad_branch).reshape(-1)
    tail = tail[boundary - out_at - tail_from * D :]
    head = jnp.concatenate([jnp.zeros((14 * LINE,), jnp.float32), tail, grad_norm_ffn])
    head_rows = head.shape[0] // LINE
    carry = jnp.zeros((8, LINE), jnp.float32).at[7, :lane].set(head[head_rows * LINE :])
    head = head[: head_rows * LINE].reshape(head_rows, LINE).astype(jnp.bfloat16)
    return pack_lines(
        None, 2 * PLANE + 32, head_rows, [gate, up, down], lane, 0, [(head, 0)], carry, 48, after
    )


def pack_out(ssm_low, grad_branch, after):
    out_at = offsets_of()[W_SSM_OUT][0]
    first_row = (8 + out_at // LINE) // 16 * 16
    rows = first_row + SSM_HEADS * SSM_DIM * D // LINE
    return pack_lines(
        None, rows, first_row, [(ssm_low, grad_branch)], out_at % LINE, (8 + out_at // LINE) % 8, [],
        jnp.zeros((8, LINE), jnp.float32), 0, after,
    )


def pack_ssm(target, segments, small, ssm_low, grad_branch, after):
    places = offsets_of()
    misc = [small[name_key].reshape(-1) for name_key in (W_STEP,) + small_names[1:-1]]
    count = sum(part.shape[0] for part in misc)
    misc_rows = (count // LINE + 16) // 16 * 16
    opening = matmul_left_t(ssm_low[:, :16], grad_branch).reshape(-1)
    misc = jnp.concatenate(misc + [opening[: misc_rows * LINE - count]])
    misc = misc.reshape(misc_rows, LINE).astype(jnp.bfloat16)
    first_row = 8 + places[W_ATTN_OUT][0] // LINE
    return pack_lines(
        target, target.shape[0], first_row, segments, 0, 0, [(misc, 8 + places[W_STEP][0] // LINE)], None, 0, after
    )


def pack_qkv(segments, attended, grad_branch, grad_norm_attn, after):
    places = offsets_of()
    out_row = 8 + places[W_ATTN_OUT][0] // LINE
    rows = (8 + SHARD) // 16 * 16 + 8 * PIECE
    closing = matmul_left_t(attended[:, :16], grad_branch).reshape(-1, LINE)
    closing = closing[: rows - out_row].astype(jnp.bfloat16)
    opening = jnp.concatenate([jnp.zeros((8, LINE), jnp.float32), grad_norm_attn.reshape(-1, LINE)]).astype(jnp.bfloat16)
    return pack_lines(
        None, rows, 16, segments, 0, 0, [(opening, 0), (closing, out_row)], None, 0, after
    )


def own_lines(early, late, corner):
    z, y, x, c = (lax.axis_index(name) for name in GRID)
    place = 4 * y + 2 * x + c
    shard = SHARD * place
    start = jnp.where(z < 2, (8 + shard) % 16, (14 + shard) % 16)
    lines = jnp.where(z < 2, early, late)
    lines = jnp.where((z == 0) & (place < 2), corner[:WIN], lines)
    lines = lax.dynamic_slice(lines, (start, 0), (SHARD, LINE)).astype(jnp.float32)
    return lines.reshape(-1)


def body(span, group, fast, tokens, params, cotangent, offsets):
    rows_dev = tokens.shape[0]
    group_rows = rows_dev * lax.axis_size(span)
    all_rows = group_rows * lax.axis_size(group)
    ssm_inner = SSM_HEADS * SSM_DIM
    score_scale = HEAD_DIM ** (-0.5)
    bounds = offsets[0]
    my_start = lax.axis_index(span) * rows_dev
    row_index = my_start + jnp.arange(rows_dev, dtype=jnp.int32)
    seq_id, positions = sequence_info(row_index, bounds)
    first_start = row_index[0] - positions[0]
    last_row = my_start + rows_dev - 1
    cosine, sine = rotary_tables(positions)
    if fast:
        weights, spread_flow, held = early_weights(params)
    else:
        weights = unpack(lax.all_gather(params, group + span, axis=0, tiled=True))
    small_f32 = {name_key: weights[name_key].astype(jnp.float32) for name_key in small_names[:-1]}
    x_rows = tokens.astype(jnp.float32)
    normed_one, norm_one_back = jax.vjp(rms_norm, x_rows, small_f32[NORM_ATTN])
    hidden = normed_one.astype(jnp.bfloat16)
    across = lambda weight: lax.dot_general(
        weight, hidden, (((0,), (1,)), ((), ())), preferred_element_type=jnp.float32
    )
    q_rot = rotate(across(weights[W_QUERY]), cosine, sine, HEADS_Q).astype(jnp.bfloat16)
    k_rot = rotate(across(weights[W_KEY]), cosine, sine, HEADS_KV).astype(jnp.bfloat16)
    value_low = across(weights[W_VALUE]).astype(jnp.bfloat16).reshape(HEADS_KV, HEAD_DIM, rows_dev)
    kv_mine = jnp.concatenate([k_rot, value_low], axis=1).transpose(0, 2, 1)
    row_starts = row_index - positions
    kv_local = kv_mine.reshape(HEADS_KV, rows_dev, PAIR)
    xbc = jnp.concatenate(
        [matmul(hidden, weights[W_X_SSM]), matmul(hidden, weights[W_B_C])], axis=1
    )
    step_raw = matmul(hidden, weights[W_STEP])
    rim_rows = passed_along(xbc[rows_dev - 8 :], span, 1)
    ssm_meta = jnp.concatenate([my_start[None], row_starts[CHUNK - 1 :: CHUNK]]).astype(jnp.int32)
    conv_bias = small_f32[CONV_BIAS][None, :]
    convolve = lambda after: conv_forward(
        xbc, rim_rows, small_f32[CONV_WEIGHT], conv_bias, ssm_meta, row_starts[:, None], after
    )
    if fast:
        key_blocks = lax.all_gather(kv_local, span)
        (conv_values,) = bracket(convolve, [spread_flow])
    else:
        conv_values = convolve(())
    step_in = step_raw.T + small_f32[STEP_BIAS][:, None]
    step_rows = jax.nn.softplus(step_in)
    decay = -jnp.exp(small_f32[DECAY_LOG])
    logs_step = step_rows * decay[:, None]
    order = jnp.arange(rows_dev)
    upto = (order[:, None] <= order[None, :]).astype(jnp.float32)
    cumul = jnp.dot(logs_step, upto, precision=highest)
    chunk_cum = jnp.dot(
        logs_step.reshape(-1, CHUNK), upto[:CHUNK, :CHUNK], precision=highest
    ).reshape(SSM_HEADS, rows_dev)
    went_on = row_starts < my_start
    entry_rows = jnp.where(went_on[None, :], jnp.exp(cumul), 0.0)
    in_last = row_index >= row_starts[rows_dev - 1]
    tail_rows = jnp.exp(jnp.where(in_last[None, :], cumul[:, -1:] - cumul, masked_score))
    carry_all = entry_rows[:, -1]
    summarize = lambda after: weighted_state(conv_values, PAIRS, conv_values, tail_rows * step_rows, after)
    meta = jnp.stack(
        [first_start // KEYS, last_row // KEYS + 1, my_start, row_starts[rows_dev - 1]]
    ).astype(jnp.int32)
    q_wide = jnp.pad(q_rot * jnp.bfloat16(score_scale), ((0, 0), (0, HEAD_DIM), (0, 0)))
    start_row = jnp.broadcast_to(row_starts[None, :], (8, rows_dev))
    if fast:
        local_state = summarize(())
        scan = Flow(scan_stages(carry_all, local_state, False))
        (gate_in,) = fence([hidden], scan.values())
        gate_ssm = matmul(gate_in, weights[W_GATE_SSM])
        scan.go()
        (gate_ssm,) = fence([gate_ssm], scan.values())
        scan.go()
        mixed, logs = bracket(
            lambda after: attention_forward(
                q_wide, key_blocks, meta, start_row, (*after, gate_ssm, *spread_flow.values())
            ),
            [scan],
        )
        spread_flow.go()
        state_in = scan.result
    else:
        gate_ssm = matmul(hidden, weights[W_GATE_SSM])
        key_blocks = lax.all_gather(kv_local, span)
        if rows_dev != KEYS:
            key_blocks = key_blocks.transpose(1, 0, 2, 3).reshape(HEADS_KV, -1, KEYS, PAIR).transpose(1, 0, 2, 3)
        state_in = scan_states(carry_all, summarize(()), span, fast, False)
        mixed, logs = attention_forward(q_wide, key_blocks, meta, start_row)
    attended = mixed.astype(jnp.bfloat16).reshape(HEADS_Q * HEAD_DIM, rows_dev).T
    attn_out = matmul(attended, weights[W_ATTN_OUT])
    skip_wide = jnp.repeat(small_f32[SKIP_GAIN], SSM_DIM)[None, :]
    ssm_y = ssm_forward(
        conv_values, chunk_cum, step_rows, state_in, skip_wide, ssm_meta, row_starts[:, None], start_row
    )
    normed_ssm, gnorm_back = jax.vjp(gated_norm, ssm_y, gate_ssm, small_f32[NORM_SSM])
    ssm_low = normed_ssm.astype(jnp.bfloat16)
    if fast:
        held = (held[0] + spread_flow.result,) + held[1:]
        weights.update(late_weights(held, [ssm_y]))
    small_f32[NORM_FFN] = weights[NORM_FFN].astype(jnp.float32)
    ssm_out = matmul(ssm_low, weights[W_SSM_OUT])
    middle = x_rows + attn_out + ssm_out
    normed_two, norm_two_back = jax.vjp(rms_norm, middle, small_f32[NORM_FFN])
    hidden_two = normed_two.astype(jnp.bfloat16)
    gate_ffn = matmul(hidden_two, weights[W_GATE])
    upper = matmul(hidden_two, weights[W_UP_PROJ])
    activation_f32, swiglu_back = jax.vjp(swiglu, gate_ffn, upper)
    activation = activation_f32.astype(jnp.bfloat16)
    ffn_out = matmul(activation, weights[W_DOWN])
    result = middle + ffn_out
    squares = jnp.stack(
        [
            jnp.sum(result * result),
            jnp.sum(attn_out * attn_out),
            jnp.sum(ssm_out * ssm_out),
            jnp.sum(ffn_out * ffn_out),
        ]
    )
    grad_out = cotangent.astype(jnp.float32)
    grad_activation = matmul_right_t(cotangent, weights[W_DOWN])
    grad_gate_f32, grad_upper_f32 = swiglu_back(grad_activation)
    grad_gate = grad_gate_f32.astype(jnp.bfloat16)
    grad_upper = grad_upper_f32.astype(jnp.bfloat16)
    grad_hidden_two = matmul_right_t(grad_gate, weights[W_GATE]) + matmul_right_t(
        grad_upper, weights[W_UP_PROJ]
    )
    grad_middle_norm, grad_norm_ffn = norm_two_back(grad_hidden_two)
    grad_middle = grad_out + grad_middle_norm
    grad_branch = grad_middle.astype(jnp.bfloat16)
    grad_attended = matmul_right_t(weights[W_ATTN_OUT], grad_branch).astype(jnp.bfloat16)
    grad_ssm_low = matmul_right_t(grad_branch, weights[W_SSM_OUT])
    grad_ssm_y, grad_gate_ssm_f32, grad_norm_ssm = gnorm_back(grad_ssm_low)
    grad_state_local = weighted_state(conv_values, PAIRS + 1, grad_ssm_y, entry_rows)
    if fast:
        scan = Flow(scan_stages(carry_all, grad_state_local, True, squares)).go()
        (late,) = bracket(
            lambda after: pack_late(
                (hidden_two, grad_gate), (hidden_two, grad_upper), (activation, cotangent),
                ssm_low, grad_branch, grad_norm_ffn, after,
            ),
            [scan],
        )
        late_flow = Flow(reduce_stages(late, 1, 14))
        (grad_branch_low,) = fence([grad_branch], scan.values() + late_flow.values())
        early = pack_out(ssm_low, grad_branch_low, ())
        scan.go()
        grad_state_out, squares = scan.result
        (early,) = fence([early], [grad_state_out])
        late_flow.go()
        (early,) = fence([early], late_flow.values())
        stats_flow = Flow(plane_stages(squares))
        around = lambda call: bracket(call, [late_flow])
    else:
        grad_state_out = scan_states(carry_all, grad_state_local, span, fast, True)
        around = lambda call: call(())
    grad_x, grad_b, grad_c, grad_small = around(
        lambda after: ssm_backward(
            conv_values, grad_ssm_y, chunk_cum, step_rows, state_in, grad_state_out, skip_wide, ssm_meta, start_row,
            after,
        )
    )
    grad_direct = grad_small[:, 0:2].reshape(SSM_HEADS, rows_dev)
    grad_logs = grad_small[:, 2:4].reshape(SSM_HEADS, rows_dev)
    grad_decay_log = decay * jnp.sum(step_rows * grad_logs, axis=1)
    grad_step_rows = (grad_direct + decay[:, None] * grad_logs) * jax.nn.sigmoid(step_in)
    grad_step_bias = jnp.sum(grad_step_rows, axis=1)
    grad_step_raw_f32 = grad_step_rows.T
    grad_skip_gain = jnp.sum(grad_small[:, 4, : 2 * SSM_DIM].reshape(SSM_HEADS, SSM_DIM), axis=1)
    if fast:
        around = lambda call: bracket(call, [late_flow, stats_flow])
    grad_main, grad_tail, grad_edge, grad_taps = around(
        lambda after: conv_backward(
            grad_x, grad_b, grad_c, xbc, rim_rows, small_f32[CONV_WEIGHT], conv_bias, ssm_meta,
            row_starts[:, None], after,
        )
    )
    grad_conv_weight = grad_taps[:CONV]
    grad_conv_bias = grad_taps[CONV]
    rim_back = passed_along(grad_edge, span, -1)
    grad_tail = grad_tail + jnp.pad(rim_back, ((8, 0), (0, 0)))
    grad_xbc = lax.dynamic_update_slice(grad_main, grad_tail.astype(jnp.bfloat16), (rows_dev - 16, 0))
    grad_gate_ssm = grad_gate_ssm_f32.astype(jnp.bfloat16)
    grad_step_raw = grad_step_raw_f32.astype(jnp.bfloat16)
    grad_w_step = matmul_left_t(hidden, grad_step_raw)
    grad_hidden_ssm = (
        matmul_right_t(grad_gate_ssm, weights[W_GATE_SSM])
        + matmul_right_t(grad_xbc[:, :ssm_inner], weights[W_X_SSM])
        + matmul_right_t(grad_xbc[:, ssm_inner:], weights[W_B_C])
        + matmul_right_t(grad_step_raw, weights[W_STEP])
    )
    small = {
        W_STEP: grad_w_step,
        CONV_WEIGHT: grad_conv_weight,
        CONV_BIAS: grad_conv_bias,
        STEP_BIAS: grad_step_bias,
        DECAY_LOG: grad_decay_log,
        SKIP_GAIN: grad_skip_gain,
        NORM_SSM: grad_norm_ssm,
        NORM_FFN: grad_norm_ffn,
    }
    parts = []
    if fast:
        (early,) = bracket(lambda after: pack_ssm(
            early,
            [
                (attended, grad_branch), (hidden, grad_gate_ssm),
                (hidden, grad_xbc[:, :ssm_inner]), (hidden, grad_xbc[:, ssm_inner:]),
            ],
            small, ssm_low, grad_branch, (*after, *late_flow.values()),
        ), [stats_flow])
        early_flow = Flow(reduce_stages(early, 0, 8))
        (grad_attended,) = fence([grad_attended], early_flow.values() + late_flow.values())
        around = lambda call: bracket(call, [early_flow])
    g_wide = jnp.pad(grad_attended.reshape(HEADS_Q, HEAD_DIM, rows_dev), ((0, 0), (HEAD_DIM, 0), (0, 0)))
    if fast:
        early_flow.go()
        (g_wide,) = fence([g_wide], early_flow.values())
    for group_at in range(HEADS_KV):
        after_part = [part[1] for part in parts]
        if fast and group_at == 0:
            after_part = late_flow.values()
        parts.append(
            around(
                lambda after: attention_backward(
                    q_wide, g_wide, key_blocks, logs, mixed, meta, start_row, group_at, (*after, *after_part)
                )
            )
        )
    grad_kv = jnp.concatenate([part[0] for part in parts], axis=1)
    grad_q_turned = jnp.concatenate([part[1] for part in parts], axis=0)
    if rows_dev != KEYS:
        grad_kv = grad_kv.transpose(1, 0, 2, 3).reshape(HEADS_KV, -1, rows_dev, PAIR).transpose(1, 0, 2, 3)
    if fast:
        late_flow.go([parts[-1][1]])
        scatter = Flow(scatter_stages(grad_kv))
        (grad_q_turned,) = fence([grad_q_turned], scatter.values() + early_flow.values() + late_flow.values())
    turned_back = rotate(grad_q_turned * score_scale, cosine, -sine, HEADS_Q).astype(jnp.bfloat16)
    grad_query_low = turned_back.reshape(HEADS_Q * HEAD_DIM, rows_dev).T
    if fast:
        scatter.go()
        early_flow.go()
        (grad_query_low,) = fence([grad_query_low], scatter.values() + early_flow.values())
    grad_hidden = grad_hidden_ssm + matmul_right_t(grad_query_low, weights[W_QUERY])
    if fast:
        scatter.go()
        (grad_hidden,) = fence([grad_hidden], scatter.values())
        scatter.go()
        grad_kv_mine = scatter.result
    else:
        grad_kv_mine = scatter_span(grad_kv, span, fast)
    grad_kv_mine = grad_kv_mine.transpose(0, 2, 1)
    grad_key_low = rotate(grad_kv_mine[:, :HEAD_DIM], cosine, -sine, HEADS_KV).astype(jnp.bfloat16)
    grad_key_low = grad_key_low.reshape(HEADS_KV * HEAD_DIM, rows_dev).T
    grad_value_low = grad_kv_mine[:, HEAD_DIM:].astype(jnp.bfloat16).reshape(HEADS_KV * HEAD_DIM, rows_dev).T
    grad_hidden = (
        grad_hidden
        + matmul_right_t(grad_key_low, weights[W_KEY])
        + matmul_right_t(grad_value_low, weights[W_VALUE])
    )
    grad_x_norm, grad_norm_attn = norm_one_back(grad_hidden)
    grad_tokens = grad_middle + grad_x_norm
    if fast:
        corner = pack_qkv(
            [(hidden, grad_query_low), (hidden, grad_key_low), (hidden, grad_value_low)],
            attended, grad_branch, grad_norm_attn, early_flow.values(),
        )
        corner_flow = Flow(corner_stages(corner))
        for _ in range(3):
            corner_flow.go()
        early_flow.go()
        ((pieces, _, _), *_) = corner_flow.sends
        (pieces,) = fence([pieces], early_flow.values())
        corner_flow.sends = [(pieces, axis, pairs) for _, axis, pairs in corner_flow.sends]
        for flow in (early_flow, late_flow, corner_flow):
            while flow.sends:
                flow.go()
        stats = jnp.sqrt(stats_flow.result / (all_rows * D))
        grad_shard = own_lines(early_flow.result, late_flow.result, corner_flow.result)
        return (result.astype(jnp.bfloat16), grad_tokens, grad_shard, stats)
    small[NORM_ATTN] = grad_norm_attn
    stats = jnp.sqrt(lax.psum(squares, group + span) / (all_rows * D))
    pairs = {
        W_QUERY: (hidden, grad_query_low),
        W_KEY: (hidden, grad_key_low),
        W_VALUE: (hidden, grad_value_low),
        W_ATTN_OUT: (attended, grad_branch),
        W_GATE_SSM: (hidden, grad_gate_ssm),
        W_X_SSM: (hidden, grad_xbc[:, :ssm_inner]),
        W_B_C: (hidden, grad_xbc[:, ssm_inner:]),
        W_SSM_OUT: (ssm_low, grad_branch),
        W_GATE: (hidden_two, grad_gate),
        W_UP_PROJ: (hidden_two, grad_upper),
        W_DOWN: (activation, cotangent),
    }
    grad_dict = dict(small)
    for name_key, (left, right) in pairs.items():
        grad_dict[name_key] = matmul_left_t(left, right)
    flat_parts = [grad_dict[name_key].reshape(-1) for name_key, extent in layout()]
    used_entries = 0
    for part_array in flat_parts:
        used_entries += part_array.shape[0]
    flat_parts.append(jnp.zeros((params.shape[0] * lax.axis_size(group + span) - used_entries,), jnp.float32))
    grad_shard = lax.psum_scatter(
        jnp.concatenate(flat_parts), group + span, scatter_dimension=0, tiled=True
    )
    return (result.astype(jnp.bfloat16), grad_tokens, grad_shard, stats)


def solution(mesh):
    fast = (mesh.shape["group"], mesh.shape["span"]) == FAST
    if fast:
        mesh = Mesh(mesh.devices.reshape(4, 2, 2, 2), GRID)
        group, span = (GRID[:1], GRID[1:])
    else:
        group, span = (("group",), ("span",))

    def program(tokens, params, cotangent, offsets):
        return body(span, group, fast, tokens, params, cotangent, offsets)

    return jax.shard_map(
        program,
        mesh=mesh,
        in_specs=(P(group + span, None), P(group + span), P(group + span, None), P(group, None)),
        out_specs=(P(group + span, None), P(group + span, None), P(group + span), P()),
        check_vma=False,
    )
```

```python
import math

import jax
import jax.numpy as jnp
import numpy as np
from jax import lax
from jax.experimental import pallas as pl
from jax.experimental.pallas import tpu as pltpu
from jax.sharding import Mesh, PartitionSpec as P

D = 1024
HEADS_Q = 8
HEADS_KV = 2
HEAD_DIM = 64
SSM_HEADS = 24
SSM_DIM = 64
STATE = 128
CONV = 4
FF = 2048
(
    NORM_ATTN,
    W_QUERY,
    W_KEY,
    W_VALUE,
    W_ATTN_OUT,
    W_GATE_SSM,
    W_X_SSM,
    W_B_C,
    W_STEP,
    CONV_WEIGHT,
    CONV_BIAS,
    STEP_BIAS,
    DECAY_LOG,
    SKIP_GAIN,
    NORM_SSM,
    W_SSM_OUT,
    NORM_FFN,
    W_GATE,
    W_UP_PROJ,
    W_DOWN,
) = range(20)


epsilon = 1e-05
rope_base = 100000000000.0
masked_score = -1e30
highest = lax.Precision.HIGHEST
small_names = (
    NORM_ATTN,
    CONV_WEIGHT,
    CONV_BIAS,
    STEP_BIAS,
    DECAY_LOG,
    SKIP_GAIN,
    NORM_SSM,
    NORM_FFN,
)


def passed_along(value, axis, steps):
    count = lax.axis_size(axis)
    first, last = (max(0, -steps), min(count, count - steps))
    return lax.ppermute(value, axis, [(source, source + steps) for source in range(first, last)])


def prefix(value, axis, combine, identity):
    peers, place = (lax.axis_size(axis), lax.axis_index(axis))
    everything = jax.tree.map(
        lambda part, kind: lax.all_gather(part.astype(kind), axis),
        value,
        (jnp.bfloat16, jnp.bfloat16),
    )
    start = jax.tree.map(
        lambda part, zero: jnp.broadcast_to(jnp.asarray(zero, part.dtype), part.shape),
        value,
        identity,
    )

    def prefix_turn(k, before):
        reached = k < place
        new = combine(
            before, jax.tree.map(lambda part, own: part[k].astype(own.dtype), everything, value)
        )
        return jax.tree.map(lambda a, b: jnp.where(reached, a, b), new, before)

    return lax.fori_loop(0, peers, prefix_turn, start)


def carried_in(value, axis, combine, identity):
    peers, place = (lax.axis_size(axis), lax.axis_index(axis))
    everything = jax.tree.map(
        lambda part, kind: lax.all_gather(part.astype(kind), axis),
        value,
        jax.tree.map(lambda a: jnp.bfloat16 if a.dtype == jnp.float32 else a.dtype, value),
    )
    start = jax.tree.map(
        lambda part, zero: jnp.broadcast_to(jnp.asarray(zero, part.dtype), part.shape),
        value,
        identity,
    )

    def carried_turn(k, before):
        at = peers - 1 - k
        reached = at > place
        new = combine(
            before, jax.tree.map(lambda part, own: part[at].astype(own.dtype), everything, value)
        )
        return jax.tree.map(lambda a, b: jnp.where(reached, a, b), new, before)

    return lax.fori_loop(0, peers, carried_turn, start)


def layout():
    ssm_inner = SSM_HEADS * SSM_DIM
    channels = ssm_inner + 2 * STATE
    return [
        (NORM_ATTN, (D,)),
        (W_QUERY, (D, HEADS_Q * HEAD_DIM)),
        (W_KEY, (D, HEADS_KV * HEAD_DIM)),
        (W_VALUE, (D, HEADS_KV * HEAD_DIM)),
        (W_ATTN_OUT, (HEADS_Q * HEAD_DIM, D)),
        (W_GATE_SSM, (D, ssm_inner)),
        (W_X_SSM, (D, ssm_inner)),
        (W_B_C, (D, 2 * STATE)),
        (W_STEP, (D, SSM_HEADS)),
        (CONV_WEIGHT, (CONV, channels)),
        (CONV_BIAS, (channels,)),
        (STEP_BIAS, (SSM_HEADS,)),
        (DECAY_LOG, (SSM_HEADS,)),
        (SKIP_GAIN, (SSM_HEADS,)),
        (NORM_SSM, (ssm_inner,)),
        (W_SSM_OUT, (ssm_inner, D)),
        (NORM_FFN, (D,)),
        (W_GATE, (D, FF)),
        (W_UP_PROJ, (D, FF)),
        (W_DOWN, (FF, D)),
    ]


def unpack(flat_vector):
    unpacked = {}
    offset = 0
    for name_key, extent in layout():
        amount = math.prod(extent)
        unpacked[name_key] = flat_vector[offset : offset + amount].reshape(extent)
        offset += amount
    return unpacked


def matmul(left, right):
    return jnp.dot(left, right, preferred_element_type=jnp.float32)


def matmul_left_t(left, right):
    return lax.dot_general(
        left, right, (((0,), (0,)), ((), ())), preferred_element_type=jnp.float32
    )


def matmul_right_t(left, right):
    return lax.dot_general(
        left, right, (((1,), (1,)), ((), ())), preferred_element_type=jnp.float32
    )


def rms_norm(values, gain):
    return values * lax.rsqrt(jnp.mean(values * values, axis=-1, keepdims=True) + epsilon) * gain


def gated_norm(ssm_y, gate_ssm, gain):
    return rms_norm(ssm_y * jax.nn.silu(gate_ssm), gain)


def swiglu(gate_ffn, upper):
    return jax.nn.silu(gate_ffn) * upper


def sequence_info(row_index, bounds):
    starts = bounds[:-1]
    inside = row_index[:, None] >= starts[None, :]
    seq_id = jnp.sum(inside.astype(jnp.int32), axis=1) - 1
    seq_start = jnp.max(jnp.where(inside, starts[None, :], 0), axis=1)
    return (seq_id, row_index - seq_start)


def rotary_tables(positions):
    half_dim = HEAD_DIM // 2
    freqs = jnp.exp(
        -jnp.arange(half_dim, dtype=jnp.float32) * (2.0 * math.log(rope_base) / HEAD_DIM)
    )
    angles = freqs[:, None] * positions.astype(jnp.float32)[None, :]
    return (jnp.cos(angles), jnp.sin(angles))


def rotate(values, cosine, sine, heads):
    halves = values.reshape(heads, 2, HEAD_DIM // 2, -1)
    first_half, second_half = halves[:, 0], halves[:, 1]
    turned = jnp.stack(
        [first_half * cosine - second_half * sine, second_half * cosine + first_half * sine], axis=1
    )
    return turned.reshape(heads, HEAD_DIM, -1)


def add_rows(target, addend, first_row):
    current = lax.dynamic_slice_in_dim(target, first_row, addend.shape[0], 0)
    return lax.dynamic_update_slice_in_dim(target, current + addend, first_row, 0)


FAST = (4, 8)
LINE = 128
SHARD = 3082
SPAD = 3088
WIN = 3104
PLANE = 8 * SHARD
DEPTH = 4
TALL = {1: 1024, 2: 1024, 4: 512, 8: 256, 12: 128, 16: 128}
GRID = ("z", "y", "x", "c")
ZC = ("z", "c")
SWAP = [(0, 1), (1, 0)]


def zc_pairs(*pairs):
    return [(2 * a + c, 2 * b + c) for a, b, c in pairs]


def pinned(kernel, count, after):
    return lambda *refs: kernel(*refs[:count], *refs[count + len(after) :])


def pins(after):
    return [pl.BlockSpec(memory_space=pltpu.HBM)] * len(after)


class Flow:
    def __init__(self, stages):
        self.stages = stages
        self.sends = next(stages)
        self.result = None

    def values(self):
        return [value for value, _, _ in self.sends] or (list(self.result) if isinstance(self.result, list) else [self.result])

    def hold(self, after):
        held = fence(self.values(), after)
        self.sends = [(value, axis, pairs) for value, (_, axis, pairs) in zip(held, self.sends)]

    def go(self, after=()):
        arrived = [lax.ppermute(value, axis, pairs) for value, axis, pairs in self.sends]
        if after:
            arrived = fence(arrived, after)
        try:
            self.sends = self.stages.send(arrived)
        except StopIteration as stop:
            self.sends, self.result = [], stop.value
        return self


def fence(values, after):
    def kernel(*refs):
        del refs

    return pl.pallas_call(
        kernel,
        in_specs=pins(values) + pins(after),
        out_specs=pins(values),
        out_shape=[jax.ShapeDtypeStruct(value.shape, value.dtype) for value in values],
        input_output_aliases={k: k for k in range(len(values))},
        name="fence",
    )(*values, *after)


def bracket(call, flows):
    out = call([value for flow in flows for value in flow.values()])
    out = list(out) if isinstance(out, (list, tuple)) else [out]
    for flow in flows:
        flow.go()
    return fence(out, [v for flow in flows for v in flow.values()])


def gather_lines(params):
    z, y, x, c = (lax.axis_index(name) for name in GRID)
    lines = jnp.pad(params.reshape(SHARD, LINE), ((0, SPAD - SHARD), (0, 0)))
    sibling = lax.ppermute(lines, ZC, [(2 * k + 1 - k % 2, 2 * k + k % 2) for k in range(4)])
    buffers = []
    for part in range(2):
        here = jnp.where(c == part, lines, sibling)
        one = lax.ppermute(here, ZC, zc_pairs((0, 1, 0), (1, 2, 1)))
        side = lax.ppermute(here, ZC, zc_pairs((1, 0, 1)))
        two = lax.ppermute(one, ZC, zc_pairs((1, 2, 0), (2, 3, 1)))
        three = lax.ppermute(two, ZC, zc_pairs((2, 3, 0)))
        column = jnp.where(z == c, here, one + side + two + three)
        over_x = lax.ppermute(column, "x", SWAP)
        over_y = lax.ppermute(column, "y", SWAP)
        corner = lax.ppermute(over_y if part else over_x, "x" if part else "y", SWAP)
        local = [column, over_x, over_y, corner]
        buffers += [piece[None] for piece in local]
        buffers += [lax.ppermute(piece, "c", SWAP)[None] for piece in local]
    early = [(k, 0) for k in range(16)]
    here = jnp.where(c == 0, jnp.stack([lines, sibling]), jnp.stack([sibling, lines]))
    one = lax.ppermute(here, ZC, zc_pairs((2, 1, 0), (3, 2, 1)))
    side = lax.ppermute(here, ZC, zc_pairs((2, 3, 0)))
    two = lax.ppermute(one, ZC, zc_pairs((1, 0, 0), (2, 1, 1)))
    three = lax.ppermute(two, ZC, zc_pairs((1, 0, 1)))
    column = jnp.where(z == 2 + c, here, one + side + two + three)
    late = []
    for part in range(2):
        for first in (16, 21):
            late += [(first, part), (first + 1, part), (first + 2, part), (first + 3 + part, 0)]
    shard = np.arange(32)
    sz, sy, sx, sc = shard // 8, shard // 4 % 2, shard // 2 % 2, shard % 2
    away = jnp.where(sz % 2 == c, 0, 4)
    where = sc * 8 + away + 2 * (sy ^ y) + (sx ^ x) + 16 * (sz // 2)
    return buffers, Flow(spread_stages(column)), (early, early + late), where.astype(jnp.int32)


def spread_stages(column):
    over_x, over_y = yield [(column, "x", SWAP), (column, "y", SWAP)]
    corners = yield [(over_x[:1], "y", SWAP), (over_y[1:], "x", SWAP)]
    local = [column, over_x, over_y] + list(corners)
    return local + list((yield [(piece, "c", SWAP) for piece in local]))


def unpack_lines(buffers, slots, where, segments, after=()):
    jobs, starts = [], []
    reach = 0
    for offset, rows, columns in segments:
        per_row = columns // LINE
        lane, base = offset % LINE, offset // LINE
        if per_row == 1 and rows < 1024:
            lane, tall = 0, rows
        else:
            tall = TALL[per_row]
        starts.append(len(jobs))
        for k in range(rows // tall):
            jobs.append((base + k * tall * per_row, tall * per_row, 1 if lane else 0))
    window = max(job[1] for job in jobs) + 32
    table = np.zeros((len(jobs), 5), np.int32)
    for k, (line, count, extra) in enumerate(jobs):
        owner = line // SHARD
        inside = line - owner * SHARD
        begin = min(inside // 16 * 16, SPAD - window)
        crosses = int(line + count + extra > (owner + 1) * SHARD)
        table[k] = (owner, begin, begin - inside, crosses, (owner + 1) * SHARD - line)
    base_row = (int(-table[:, 2].min()) + 7) // 8 * 8
    table[:, 2] += base_row
    table[:, 4] += base_row
    room = int(max((table[:, 2] + window).max(), ((table[:, 4] + window) * table[:, 3]).max()))
    room = (room + 15) // 8 * 8
    total = len(jobs)
    count_buffers = len(buffers)
    shapes = []
    for offset, rows, columns in segments:
        per_row = columns // LINE
        tall = rows if per_row == 1 and rows < 1024 else TALL[per_row]
        shapes.append((rows, columns, tall, per_row, offset % LINE if tall != rows or per_row != 1 else 0))
    sizes = sorted({(tall, columns) for _, columns, tall, _, _ in shapes})

    def kernel(table_ref, where_ref, *refs):
        sources = refs[:count_buffers]
        outs = refs[count_buffers : count_buffers + len(segments)]
        rest = refs[count_buffers + len(segments) :]
        stages = dict(zip(sizes, rest))
        raw, flat, in_sem, out_sem = rest[len(sizes) :]
        step = pl.program_id(0)

        def fetch(job, slot):
            owner = table_ref[job, 0]
            begin = pl.multiple_of(table_ref[job, 1], 16)
            for b, (source, part) in enumerate(slots):

                @pl.when(where_ref[owner] == b)
                def _():
                    pltpu.make_async_copy(
                        sources[source].at[part, pl.ds(begin, window), :], raw.at[slot, 0], in_sem.at[slot, 0]
                    ).start()

            @pl.when(table_ref[job, 3] == 1)
            def _():
                for b, (source, part) in enumerate(slots):

                    @pl.when(where_ref[owner + 1] == b)
                    def _():
                        pltpu.make_async_copy(
                            sources[source].at[part, pl.ds(0, window), :], raw.at[slot, 1], in_sem.at[slot, 1]
                        ).start()

        def fetched(slot, half):
            return pltpu.make_async_copy(
                sources[0].at[0, pl.ds(0, window), :], raw.at[slot, half], in_sem.at[slot, half]
            )

        @pl.when(step == 0)
        def _():
            for k in range(min(DEPTH - 1, total)):
                fetch(k, k)

        @pl.when(step + DEPTH - 1 < total)
        def _():
            fetch(step + DEPTH - 1, lax.rem(step + DEPTH - 1, DEPTH))

        slot = lax.rem(step, DEPTH)
        fetched(slot, 0).wait()
        flat[pl.ds(table_ref[step, 2], window), :] = raw[slot, 0].astype(jnp.float32)

        @pl.when(table_ref[step, 3] == 1)
        def _():
            fetched(slot, 1).wait()
            flat[pl.ds(table_ref[step, 4], window), :] = raw[slot, 1].astype(jnp.float32)

        for index, (rows, columns, tall, per_row, lane) in enumerate(shapes):
            begin = starts[index]
            blocks = rows // tall
            stage = stages[(tall, columns)]

            @pl.when((step >= begin) & (step < begin + blocks))
            def _():
                block = step - begin
                side = lax.rem(block, DEPTH)

                def written(k, s):
                    return pltpu.make_async_copy(
                        stage.at[s],
                        outs[index].at[pl.ds(pl.multiple_of(k * tall, 16), tall), :],
                        out_sem.at[s],
                    )

                @pl.when(block >= DEPTH)
                def _():
                    written(block - DEPTH, side).wait()

                def tile(j):
                    picked = flat[pl.ds(base_row + j, tall, stride=per_row), :]
                    return pltpu.roll(picked, LINE - lane, 1) if lane else picked

                if lane:
                    lanes = lax.broadcasted_iota(jnp.int32, (tall, LINE), 1)
                    now = tile(0)
                    for j in range(per_row):
                        later = tile(j + 1)
                        stage[side, :, j * LINE : (j + 1) * LINE] = jnp.where(
                            lanes < LINE - lane, now, later
                        ).astype(jnp.bfloat16)
                        now = later
                else:
                    for j in range(per_row):
                        stage[side, :, j * LINE : (j + 1) * LINE] = tile(j).astype(jnp.bfloat16)
                written(block, side).start()

                @pl.when(block == blocks - 1)
                def _():
                    for back in reversed(range(min(DEPTH, blocks))):
                        written(block - back, lax.rem(block - back, DEPTH)).wait()

    return pl.pallas_call(
        pinned(kernel, 2 + count_buffers, after),
        grid_spec=pltpu.PrefetchScalarGridSpec(
            num_scalar_prefetch=2,
            grid=(total,),
            in_specs=[pl.BlockSpec(memory_space=pl.ANY)] * count_buffers + pins(after),
            out_specs=[pl.BlockSpec(memory_space=pl.ANY)] * len(segments),
            scratch_shapes=[pltpu.VMEM((DEPTH,) + size, jnp.bfloat16) for size in sizes]
            + [
                pltpu.VMEM((DEPTH, 2, window, LINE), jnp.bfloat16),
                pltpu.VMEM((room, LINE), jnp.float32),
                pltpu.SemaphoreType.DMA((DEPTH, 2)),
                pltpu.SemaphoreType.DMA((DEPTH,)),
            ],
        ),
        out_shape=[jax.ShapeDtypeStruct((rows, columns), jnp.bfloat16) for _, rows, columns in segments],
        compiler_params=pltpu.CompilerParams(vmem_limit_bytes=48 * 2**20),
        cost_estimate=pl.CostEstimate(flops=0, bytes_accessed=total * window * LINE * 4, transcendentals=0),
        name="unpack",
    )(jnp.asarray(table), where, *buffers, *after)


def pack_lines(target, target_rows, first_row, segments, lane, phase, extras, carry, tail_rows, after=()):
    tall = 256
    lefts, rights, plan = [], [], []
    left_of, right_of = {}, {}
    row = first_row
    begin = 0
    for left, right in segments:
        for value, seen, kept in ((left, left_of, lefts), (right, right_of, rights)):
            if id(value) not in seen:
                seen[id(value)] = len(kept)
                kept.append(value)
        blocks = left.shape[1] // tall
        plan.append((left_of[id(left)], right_of[id(right)], right.shape[1] // LINE, begin, blocks, row))
        begin += blocks
        row += left.shape[1] * right.shape[1] // LINE
    end_row = row
    total = begin
    biggest = max(entry[2] for entry in plan) * tall
    tokens = lefts[0].shape[0]
    count_left, count_right, count_extra = len(lefts), len(rights), len(extras)
    rolled = [jnp.roll(right, lane, axis=1) if lane else right for right in rights]
    carry_in = [carry] if lane else []
    targets = [] if target is None else [target]

    def left_spec(index):
        mine = [entry for entry in plan if entry[0] == index]

        def place(step):
            block = 0
            for _, _, _, start, blocks, _ in mine:
                block = jnp.where(step >= start, jnp.minimum(step - start, blocks - 1), block)
            return (0, block)

        return pl.BlockSpec((tokens, tall), place)

    def kernel(*refs):
        left_refs = refs[:count_left]
        right_refs = refs[count_left : count_left + count_right]
        at = count_left + count_right
        extra_refs = refs[at : at + count_extra]
        at += count_extra
        carry_refs = refs[at : at + len(carry_in)]
        at += len(carry_in) + len(targets)
        out = refs[at]
        flat, stage, shift, last, sems, extra_sems = refs[at + 1 :]
        step = pl.program_id(0)
        side = lax.rem(step, 2)

        def extra_copy(k):
            rows = extras[k][0].shape[0]
            return pltpu.make_async_copy(
                extra_refs[k], out.at[pl.ds(extras[k][1], rows), :], extra_sems.at[k]
            )

        @pl.when(step == 0)
        def _():
            for k in range(count_extra):
                extra_copy(k).start()
            if lane:
                shift[0:8, :] = carry_refs[0][...]
            if phase:
                flat[0:8, :] = jnp.zeros((8, LINE), jnp.float32)

        for left_at, right_at, per_row, start, blocks, row in plan:
            lines = per_row * tall

            def written(block, s, row=row, lines=lines):
                return pltpu.make_async_copy(
                    stage.at[s, pl.ds(0, lines), :],
                    out.at[pl.ds(pl.multiple_of(row + block * lines, 16), lines), :],
                    sems.at[s],
                )

            @pl.when((step >= start) & (step < start + blocks))
            def _():
                block = step - start
                if phase:

                    @pl.when(step > 0)
                    def _():
                        flat[0:8, :] = flat[lines : lines + 8, :]

                turned = left_refs[left_at][...].T
                lanes = lax.broadcasted_iota(jnp.int32, (tall, LINE), 1)
                for j0 in range(0, per_row, 2):
                    wide = min(2, per_row - j0)
                    tile = jnp.dot(
                        turned,
                        right_refs[right_at][:, j0 * LINE : (j0 + wide) * LINE],
                        preferred_element_type=jnp.float32,
                    )
                    for j in range(wide):
                        piece = tile[:, j * LINE : (j + 1) * LINE]
                        if lane and j0 + j == 0:
                            shift[8 : 8 + tall, :] = piece
                            piece = jnp.where(lanes < lane, shift[7 : 7 + tall, :], piece)
                            shift[0:8, :] = shift[tall : tall + 8, :]
                        if per_row == 1:
                            flat[phase : phase + tall, :] = piece
                        else:
                            flat[pl.ds(phase + j0 + j, tall, stride=per_row), :] = piece

                stage[side, 0:lines, :] = flat[0:lines, :].astype(jnp.bfloat16)
                written(block, side).start()

            @pl.when((step > start) & (step <= start + blocks))
            def _():
                written(step - start - 1, 1 - side).wait()

            if start + blocks == total:

                @pl.when(step == total - 1)
                def _():
                    written(blocks - 1, side).wait()

        @pl.when(step == total - 1)
        def _():
            if tail_rows:
                lanes = lax.broadcasted_iota(jnp.int32, (tail_rows, LINE), 1)
                rows_at = lax.broadcasted_iota(jnp.int32, (tail_rows, LINE), 0)
                final = jnp.broadcast_to(shift[7:8, :], (tail_rows, LINE))
                last[...] = jnp.where((rows_at == 0) & (lanes < lane), final, 0.0).astype(jnp.bfloat16)
                closing = pltpu.make_async_copy(
                    last, out.at[pl.ds(end_row, tail_rows), :], extra_sems.at[count_extra]
                )
                closing.start()
                closing.wait()
            for k in range(count_extra):
                extra_copy(k).wait()

    whole = [pl.BlockSpec(array.shape, lambda step: (0, 0)) for array in rolled]
    flops = sum(2 * tokens * entry[4] * tall * entry[2] * LINE for entry in plan)
    inputs = count_left + count_right + count_extra + len(carry_in) + len(targets)
    return pl.pallas_call(
        pinned(kernel, inputs, after),
        grid=(total,),
        in_specs=[left_spec(k) for k in range(count_left)]
        + whole
        + [pl.BlockSpec(array.shape, lambda step: (0, 0)) for array, _ in extras]
        + [pl.BlockSpec(array.shape, lambda step: (0, 0)) for array in carry_in]
        + [pl.BlockSpec(memory_space=pl.ANY)] * len(targets)
        + pins(after),
        out_specs=pl.BlockSpec(memory_space=pl.ANY),
        out_shape=jax.ShapeDtypeStruct((target_rows, LINE), jnp.bfloat16),
        scratch_shapes=[
            pltpu.VMEM((biggest + 16, LINE), jnp.float32),
            pltpu.VMEM((2, biggest, LINE), jnp.bfloat16),
            pltpu.VMEM((tall + 8, LINE), jnp.float32),
            pltpu.VMEM((max(tail_rows, 16), LINE), jnp.bfloat16),
            pltpu.SemaphoreType.DMA((2,)),
            pltpu.SemaphoreType.DMA((count_extra + 1,)),
        ],
        input_output_aliases={count_left + count_right + count_extra + len(carry_in): 0} if targets else {},
        compiler_params=pltpu.CompilerParams(vmem_limit_bytes=48 * 2**20),
        cost_estimate=pl.CostEstimate(flops=flops, bytes_accessed=total * biggest * LINE * 2, transcendentals=0),
        name="pack",
    )(*lefts, *rolled, *[array for array, _ in extras], *carry_in, *targets, *after)


def added(*parts):
    total = parts[0].astype(jnp.float32)
    for part in parts[1:]:
        total = total + part.astype(jnp.float32)
    return total.astype(jnp.bfloat16)


def reduce_stages(flat, batch, shift):
    z, y, x, c = (lax.axis_index(name) for name in GRID)
    length = PLANE + 32
    send = lax.dynamic_slice(flat, ((1 - c) * PLANE, 0), (length, LINE))
    (arrived,) = yield [(send, "c", SWAP)]
    chip = added(lax.dynamic_slice(flat, (c * PLANE, 0), (length, LINE)), arrived)

    def window(sy, sx, part):
        shard = sy * 4 + sx * 2 + part
        start = (shift + SHARD * shard) // 16 * 16
        return lax.dynamic_slice(chip, (start, 0), (WIN, LINE))

    away_0 = jnp.stack([window(1 - y, 0, 0), window(1 - y, 1, 0)])
    away_1 = jnp.stack([window(0, 1 - x, 1), window(1, 1 - x, 1)])
    home_0 = jnp.stack([window(y, 0, 0), window(y, 1, 0)])
    home_1 = jnp.stack([window(0, x, 1), window(1, x, 1)])
    got_0, got_1 = yield [(away_0, "y", SWAP), (away_1, "x", SWAP)]
    half_0, half_1 = added(home_0, got_0), added(home_1, got_1)
    pick = lambda value, at: lax.dynamic_index_in_dim(value, at, 0, keepdims=False)
    got_0, got_1 = yield [(pick(half_0, 1 - x), "x", SWAP), (pick(half_1, 1 - y), "y", SWAP)]
    columns = [added(pick(half_0, x), got_0), added(pick(half_1, y), got_1)]
    if batch == 0:
        hops = [((1, 0, 0), (2, 1, 1)), ((2, 0, 0), (3, 1, 1)), ((3, 0, 0), (0, 1, 1))]
    else:
        hops = [((1, 2, 0), (2, 3, 1)), ((0, 2, 0), (1, 3, 1)), ((3, 2, 0), (0, 3, 1))]
    if batch == 0:
        got = yield [(columns[0], ZC, zc_pairs(*hop)) for hop in hops]
        end = added(columns[0], *got)
        (column,) = fence(columns[1:], [end])
        got = yield [(column, ZC, zc_pairs(*hop)) for hop in hops]
        ends = [end, added(column, *got)]
    else:
        columns = jnp.stack(columns)
        got = yield [(columns, ZC, zc_pairs(*hop)) for hop in hops]
        ends = added(columns, *got)
    mine = jnp.where(c == 0, ends[0], ends[1])
    other = jnp.where(c == 0, ends[1], ends[0])
    (handed,) = yield [(other, ZC, [(2 * k + k % 2, 2 * k + 1 - k % 2) for k in range(4)])]
    return jnp.where(c == z % 2, mine, handed)


PIECE = 400


def corner_stages(flat):
    z, y, x, c = (lax.axis_index(name) for name in GRID)
    length = 8 * PIECE
    second = (8 + SHARD) // 16 * 16
    take = lambda at: lax.dynamic_slice(flat, (at * second, 0), (length, LINE))
    (arrived,) = yield [(take(1 - c), "c", SWAP)]
    chip = added(take(c), arrived).reshape(2, 2, 2, PIECE, LINE)
    pick = lambda value, at: lax.dynamic_index_in_dim(value, at, 0, keepdims=False)
    got = yield [(pick(chip[0], 1 - x), "x", SWAP), (pick(chip[1], 1 - y), "y", SWAP)]
    halves = [added(pick(chip[0], x), got[0]), added(pick(chip[1], y), got[1])]
    got = yield [(pick(halves[0], 1 - y), "y", SWAP), (pick(halves[1], 1 - x), "x", SWAP)]
    pieces = jnp.stack([added(pick(halves[0], y), got[0]), added(pick(halves[1], x), got[1])])
    got = yield [(pieces, "z", [(k, 0)]) for k in (1, 2, 3)]
    pieces = added(pieces, *got)
    got = yield [(pieces[0], "y", [(1, 0)]), (pieces[1], "x", [(1, 0)])]
    halves = [jnp.stack([pieces[0], got[0]]), jnp.stack([pieces[1], got[1]])]
    got = yield [(halves[0], "x", [(1, 0)]), (halves[1], "y", [(1, 0)])]
    return jnp.stack([halves[0], got[0], halves[1], got[1]]).reshape(length, LINE)


CHUNK = 128
NT = (((1,), (1,)), ((), ()))
TN = (((0,), (0,)), ((), ()))
INNER = SSM_HEADS * SSM_DIM
PAIRS = SSM_HEADS // 2


def spread(rows_a, rows_b):
    length = rows_a.shape[1]
    tall = jnp.concatenate(
        [jnp.broadcast_to(rows_a, (SSM_DIM, length)), jnp.broadcast_to(rows_b, (SSM_DIM, length))], axis=0
    )
    return tall.T


CHANNELS = INNER + 2 * STATE
LANES = 2 * SSM_DIM
COLUMNS = CHANNELS // LANES


def conv_masks(masks, start_ref, first, rows):
    place = first + lax.broadcasted_iota(jnp.int32, (rows, LANES), 0) - start_ref[...]
    for reach in range(1, CONV):
        masks[reach - 1] = jnp.where(place >= reach, 1.0, 0.0)


def conv_parts(ext, weight_ref, bias_ref, masks, rows):
    windows = []
    total = bias_ref[...]
    for tap in range(CONV):
        reach = CONV - 1 - tap
        window = ext[8 - reach : 8 - reach + rows, :]
        if reach:
            window = window * masks[reach - 1]
        windows.append(window)
        total = total + window * weight_ref[tap : tap + 1, :]
    return windows, total


def conv_forward(xbc, rim, weight, bias, meta, start_column, after=()):
    rows = xbc.shape[0]

    def kernel(meta_ref, x_ref, rim_ref, weight_ref, bias_ref, start_ref, out_ref, ext, masks):
        @pl.when(pl.program_id(0) == 0)
        def _():
            conv_masks(masks, start_ref, meta_ref[0], rows)

        ext[0:8, :] = rim_ref[...]
        ext[8:, :] = x_ref[...]
        _, total = conv_parts(ext, weight_ref, bias_ref, masks, rows)
        out_ref[...] = total * jax.nn.sigmoid(total)

    lanes = lambda i, m: (0, i)
    return pl.pallas_call(
        pinned(kernel, 6, after),
        grid_spec=pltpu.PrefetchScalarGridSpec(
            num_scalar_prefetch=1,
            grid=(COLUMNS,),
            in_specs=[
                pl.BlockSpec((rows, LANES), lanes),
                pl.BlockSpec((8, LANES), lanes),
                pl.BlockSpec((CONV, LANES), lanes),
                pl.BlockSpec((1, LANES), lanes),
                pl.BlockSpec((rows, 1), lambda i, m: (0, 0)),
            ] + pins(after),
            out_specs=pl.BlockSpec((rows, LANES), lanes),
            scratch_shapes=[
                pltpu.VMEM((rows + 8, LANES), jnp.float32),
                pltpu.VMEM((CONV - 1, rows, LANES), jnp.float32),
            ],
        ),
        out_shape=jax.ShapeDtypeStruct((rows, CHANNELS), jnp.float32),
        cost_estimate=pl.CostEstimate(flops=10**9, bytes_accessed=rows * CHANNELS * 8, transcendentals=0),
        name="conv",
    )(meta, xbc, rim, weight, bias, start_column, *after)


def conv_backward(dx, db, dc, xbc, rim, weight, bias, meta, start_column, after=()):
    rows = xbc.shape[0]

    def kernel(meta_ref, dx_ref, db_ref, dc_ref, x_ref, rim_ref, weight_ref, bias_ref, start_ref,
               low_ref, tail_ref, edge_ref, small_ref, ext, upper, masks):
        @pl.when(pl.program_id(0) == 0)
        def _():
            conv_masks(masks, start_ref, meta_ref[0], rows)
            upper[0:8, :] = jnp.zeros((8, LANES), jnp.float32)
            upper[8 + rows :, :] = jnp.zeros((8, LANES), jnp.float32)

        ext[0:8, :] = rim_ref[...]
        ext[8:, :] = x_ref[...]
        at = pl.program_id(0)
        arrived = jnp.where(at < PAIRS, dx_ref[...], jnp.where(at == PAIRS, db_ref[...], dc_ref[...]))
        windows, total = conv_parts(ext, weight_ref, bias_ref, masks, rows)
        gate = jax.nn.sigmoid(total)
        change = arrived * gate * (1.0 + total * (1.0 - gate))
        main = jnp.zeros((rows, LANES), jnp.float32)
        edge = jnp.zeros((8, LANES), jnp.float32)
        small_ref[...] = jnp.zeros((8, LANES), jnp.float32)
        small_ref[CONV : CONV + 1, :] = jnp.sum(change, axis=0, keepdims=True)
        for tap in range(CONV):
            reach = CONV - 1 - tap
            small_ref[tap : tap + 1, :] = jnp.sum(change * windows[tap], axis=0, keepdims=True)
            masked = change * masks[reach - 1] if reach else change
            upper[8 : 8 + rows, :] = masked * weight_ref[tap : tap + 1, :]
            main = main + upper[8 + reach : 8 + reach + rows, :]
            edge = edge + upper[reach : reach + 8, :]
        low_ref[...] = main.astype(jnp.bfloat16)
        tail_ref[...] = main[rows - 16 :, :]
        edge_ref[...] = edge

    lanes = lambda i, m: (0, i)
    whole = lambda i, m: (0, 0)
    return pl.pallas_call(
        pinned(kernel, 9, after),
        grid_spec=pltpu.PrefetchScalarGridSpec(
            num_scalar_prefetch=1,
            grid=(COLUMNS,),
            in_specs=[
                pl.BlockSpec((rows, LANES), lambda i, m: (0, jnp.minimum(i, PAIRS - 1))),
                pl.BlockSpec((rows, STATE), whole),
                pl.BlockSpec((rows, STATE), whole),
                pl.BlockSpec((rows, LANES), lanes),
                pl.BlockSpec((8, LANES), lanes),
                pl.BlockSpec((CONV, LANES), lanes),
                pl.BlockSpec((1, LANES), lanes),
                pl.BlockSpec((rows, 1), whole),
            ] + pins(after),
            out_specs=[
                pl.BlockSpec((rows, LANES), lanes),
                pl.BlockSpec((16, LANES), lanes),
                pl.BlockSpec((8, LANES), lanes),
                pl.BlockSpec((8, LANES), lanes),
            ],
            scratch_shapes=[
                pltpu.VMEM((rows + 8, LANES), jnp.float32),
                pltpu.VMEM((rows + 16, LANES), jnp.float32),
                pltpu.VMEM((CONV - 1, rows, LANES), jnp.float32),
            ],
        ),
        out_shape=[
            jax.ShapeDtypeStruct((rows, CHANNELS), jnp.bfloat16),
            jax.ShapeDtypeStruct((16, CHANNELS), jnp.float32),
            jax.ShapeDtypeStruct((8, CHANNELS), jnp.float32),
            jax.ShapeDtypeStruct((8, CHANNELS), jnp.float32),
        ],
        cost_estimate=pl.CostEstimate(flops=2 * 10**9, bytes_accessed=rows * CHANNELS * 10, transcendentals=0),
        name="conv_back",
    )(meta, dx, db, dc, xbc, rim, weight, bias, start_column, *after)


def weighted_state(left, left_block, values, weight_rows, after=()):
    rows = left.shape[0]

    def kernel(left_ref, value_ref, weight_ref, out_ref, turned):
        @pl.when(pl.program_id(0) == 0)
        def _():
            turned[...] = left_ref[...].T

        scaled = [(turned[...] * weight_ref[0, e : e + 1, :]).astype(jnp.bfloat16) for e in range(2)]
        both = jnp.dot(
            jnp.concatenate(scaled, axis=0), value_ref[...].astype(jnp.bfloat16), preferred_element_type=jnp.float32
        )
        low_lane = lax.broadcasted_iota(jnp.int32, (STATE, 2 * SSM_DIM), 1) < SSM_DIM
        out_ref[...] = jnp.where(low_lane, both[:STATE], both[STATE:])

    return pl.pallas_call(
        pinned(kernel, 3, after),
        grid=(PAIRS,),
        in_specs=[
            pl.BlockSpec((rows, STATE), lambda i: (0, left_block)),
            pl.BlockSpec((rows, 2 * SSM_DIM), lambda i: (0, i)),
            pl.BlockSpec((1, 2, rows), lambda i: (i, 0, 0)),
        ] + pins(after),
        out_specs=pl.BlockSpec((STATE, 2 * SSM_DIM), lambda i: (0, i)),
        out_shape=jax.ShapeDtypeStruct((STATE, INNER), jnp.float32),
        scratch_shapes=[pltpu.VMEM((STATE, rows), jnp.float32)],
        cost_estimate=pl.CostEstimate(flops=2 * rows * STATE * INNER, bytes_accessed=rows * INNER * 4, transcendentals=0),
        name="state",
    )(left, values, weight_rows.reshape(PAIRS, 2, rows), *after)


def chunk_rows(k, meta_ref, cum_ref, start_ref):
    here = slice(k * CHUNK, (k + 1) * CHUNK)
    first = meta_ref[0] + k * CHUNK
    index = first + lax.broadcasted_iota(jnp.int32, (1, CHUNK), 1)
    entering = start_ref[0:1, here] < first
    ending = index >= meta_ref[1 + k]
    cums, entries, tails = [], [], []
    for e in range(2):
        cum = cum_ref[0, e : e + 1, here]
        cums.append(cum)
        entries.append(jnp.where(entering, jnp.exp(cum), 0.0))
        gap = jnp.where(ending, cum[:, CHUNK - 1 :] - cum, masked_score)
        tails.append(jnp.exp(gap))
    return cums, entries, tails


def ssm_forward(conv, cum, step, state_in, skip, meta, start_column, start_row):
    rows = conv.shape[0]
    chunks = rows // CHUNK

    def kernel(meta_ref, x_ref, b_ref, c_ref, cum_ref, step_ref, state_ref, skip_ref, col_ref, row_ref,
               y_ref, inner, hide, state, b_turned):
        @pl.when(pl.program_id(0) == 0)
        def _():
            for k in range(chunks):
                here = slice(k * CHUNK, (k + 1) * CHUNK)
                b_turned[:, here] = b_ref[here, :].T.astype(jnp.bfloat16)
                inner[k] = lax.dot_general(
                    c_ref[here, :], b_ref[here, :], NT, precision=highest, preferred_element_type=jnp.float32
                )
                t = lax.broadcasted_iota(jnp.int32, (CHUNK, CHUNK), 0)
                s = lax.broadcasted_iota(jnp.int32, (CHUNK, CHUNK), 1)
                shown = (s <= t) & (meta_ref[0] + k * CHUNK + s >= col_ref[here, :])
                hide[k] = jnp.where(shown, 0.0, masked_score)

        low_lane = lax.broadcasted_iota(jnp.int32, (CHUNK, 2 * SSM_DIM), 1) < SSM_DIM
        state[...] = state_ref[...]
        for k in range(chunks):
            here = slice(k * CHUNK, (k + 1) * CHUNK)
            cums, entries, tails = chunk_rows(k, meta_ref, cum_ref, row_ref)
            x_now = x_ref[here, :]
            x_low = x_now.astype(jnp.bfloat16)
            entry = spread(*entries)
            weight = spread(*[tails[e] * step_ref[0, e : e + 1, here] for e in range(2)])
            parts = []
            for e in range(2):
                across = jnp.broadcast_to(cums[e], (CHUNK, CHUNK))
                decays = jnp.exp(across.T - across + hide[k])
                mix = (inner[k] * decays * step_ref[0, e : e + 1, here]).astype(jnp.bfloat16)
                parts.append(jnp.dot(mix, x_low, preferred_element_type=jnp.float32))
            carried = jnp.dot(
                c_ref[here, :].astype(jnp.bfloat16), state[...].astype(jnp.bfloat16),
                preferred_element_type=jnp.float32,
            )
            y_ref[here, :] = jnp.where(low_lane, parts[0], parts[1]) + entry * carried + skip_ref[...] * x_now
            fresh = jnp.dot(
                b_turned[:, here], (x_now * weight).astype(jnp.bfloat16), preferred_element_type=jnp.float32
            )
            state[...] = entry[CHUNK - 1 :, :] * state[...] + fresh

    whole = lambda i, m: (0, 0)
    lanes = lambda i, m: (0, i)
    return pl.pallas_call(
        kernel,
        grid_spec=pltpu.PrefetchScalarGridSpec(
            num_scalar_prefetch=1,
            grid=(PAIRS,),
            in_specs=[
                pl.BlockSpec((rows, 2 * SSM_DIM), lanes),
                pl.BlockSpec((rows, STATE), lambda i, m: (0, PAIRS)),
                pl.BlockSpec((rows, STATE), lambda i, m: (0, PAIRS + 1)),
                pl.BlockSpec((1, 2, rows), lambda i, m: (i, 0, 0)),
                pl.BlockSpec((1, 2, rows), lambda i, m: (i, 0, 0)),
                pl.BlockSpec((STATE, 2 * SSM_DIM), lanes),
                pl.BlockSpec((1, 2 * SSM_DIM), lanes),
                pl.BlockSpec((rows, 1), whole),
                pl.BlockSpec((8, rows), whole),
            ],
            out_specs=pl.BlockSpec((rows, 2 * SSM_DIM), lanes),
            scratch_shapes=[
                pltpu.VMEM((chunks, CHUNK, CHUNK), jnp.float32),
                pltpu.VMEM((chunks, CHUNK, CHUNK), jnp.float32),
                pltpu.VMEM((STATE, 2 * SSM_DIM), jnp.float32),
                pltpu.VMEM((STATE, rows), jnp.bfloat16),
            ],
        ),
        out_shape=jax.ShapeDtypeStruct((rows, INNER), jnp.float32),
        compiler_params=pltpu.CompilerParams(vmem_limit_bytes=40 * 2**20),
        cost_estimate=pl.CostEstimate(flops=10**9, bytes_accessed=rows * INNER * 8, transcendentals=2**21),
        name="ssm",
    )(meta, conv, conv, conv, cum.reshape(PAIRS, 2, rows), step.reshape(PAIRS, 2, rows), state_in, skip,
      start_column, start_row)


def ssm_backward(conv, dy, cum, step, state_in, state_grad, skip, meta, start_row, after=()):
    rows = conv.shape[0]
    chunks = rows // CHUNK

    def kernel(meta_ref, x_ref, dy_ref, b_ref, c_ref, cum_ref, step_ref, state_ref, grad_ref, skip_ref, row_ref,
               dx_ref, db_ref, dc_ref, small_ref, inner, hide, inner_grad, states, flow,
               b_turned, c_turned):
        low = lambda v: v.astype(jnp.bfloat16)
        dot = lambda p, q, dims=(((1,), (0,)), ((), ())): lax.dot_general(
            p, q, dims, preferred_element_type=jnp.float32
        )
        exact = lambda p, q, dims=(((1,), (0,)), ((), ())): lax.dot_general(
            p, q, dims, precision=highest, preferred_element_type=jnp.float32
        )
        s = lax.broadcasted_iota(jnp.int32, (CHUNK, CHUNK), 0)
        t = lax.broadcasted_iota(jnp.int32, (CHUNK, CHUNK), 1)

        @pl.when(pl.program_id(0) == 0)
        def _():
            db_ref[...] = jnp.zeros(db_ref.shape, jnp.float32)
            dc_ref[...] = jnp.zeros(dc_ref.shape, jnp.float32)
            inner_grad[...] = jnp.zeros(inner_grad.shape, jnp.float32)
            for k in range(chunks):
                here = slice(k * CHUNK, (k + 1) * CHUNK)
                b_turned[:, here] = low(b_ref[here, :].T)
                c_turned[:, here] = low(c_ref[here, :].T)
                inner[k] = exact(b_ref[here, :], c_ref[here, :], NT)
                shown = (s <= t) & (meta_ref[0] + k * CHUNK + s >= row_ref[0:1, here])
                hide[k] = jnp.where(shown, 0.0, masked_score)

        before = (s < t).astype(jnp.float32)
        until = low((s >= t).astype(jnp.float32))
        low_lane = t < SSM_DIM
        pick_row = lax.broadcasted_iota(jnp.int32, (8, 2 * SSM_DIM), 0)
        pick_lane = lax.broadcasted_iota(jnp.int32, (8, 2 * SSM_DIM), 1) // SSM_DIM
        pick = low((pick_row == pick_lane).astype(jnp.float32))
        spreads = []
        states[0] = state_ref[...]
        for k in range(chunks):
            here = slice(k * CHUNK, (k + 1) * CHUNK)
            cums, entries, tails = chunk_rows(k, meta_ref, cum_ref, row_ref)
            entry, tail = spread(*entries), spread(*tails)
            steps = spread(step_ref[0, 0:1, here], step_ref[0, 1:2, here])
            spreads.append((cums, entry, tail, steps))
            if k < chunks - 1:
                fresh = dot(b_turned[:, here], low(x_ref[here, :] * steps * tail))
                states[k + 1] = entry[CHUNK - 1 :, :] * states[k] + fresh
        flow[...] = grad_ref[...]
        skip_sum = jnp.zeros((1, 2 * SSM_DIM), jnp.float32)
        for k in reversed(range(chunks)):
            here = slice(k * CHUNK, (k + 1) * CHUNK)
            cums, entry, tail, steps = spreads[k]
            x_now, dy_now = x_ref[here, :], dy_ref[here, :]
            b_low, c_low = low(b_ref[here, :]), low(c_ref[here, :])
            scaled = x_now * steps
            dy_low = low(dy_now)
            flow_low, state_low = low(flow[...]), low(states[k])
            both = low(
                jnp.concatenate([jnp.where(low_lane, scaled, 0.0), jnp.where(low_lane, 0.0, scaled)], axis=0)
            )
            reached = dot(both, dy_low, NT)
            mixes, weighed = [], []
            for e in range(2):
                across = jnp.broadcast_to(cums[e], (CHUNK, CHUNK))
                decays = jnp.exp(across - across.T + hide[k])
                reach = decays * reached[e * CHUNK : (e + 1) * CHUNK]
                inner_grad[k] += reach
                weighed.append(low(inner[k] * reach))
                mixes.append(low(inner[k] * decays))
            sums = dot(jnp.concatenate(weighed, axis=0), until)
            within = [
                jnp.sum(sums[e * CHUNK : (e + 1) * CHUNK] * before, axis=0, keepdims=True) for e in range(2)
            ]
            mixed = dot(jnp.concatenate(mixes, axis=0), dy_low)
            back = tail * dot(b_low, flow_low)
            dxs = jnp.where(low_lane, mixed[:CHUNK], mixed[CHUNK:]) + back
            db_ref[here, :] += dot(low(scaled * tail), flow_low, NT)
            entered = low(dy_now * entry)
            dc_ref[here, :] += dot(entered, state_low, NT)
            brought = dy_now * entry * dot(c_low, state_low)
            ends = dot(pick, low(brought), NT)
            begins = dot(pick, low(scaled * back), NT)
            direct = dot(pick, low(x_now * dxs), NT)
            through = jnp.sum(flow[...] * states[k], axis=0, keepdims=True) * entry[CHUNK - 1 :, :]
            log_grad = exact(ends, until.astype(jnp.float32)) + exact(begins, before)
            for e in range(2):
                lanes = slice(e * SSM_DIM, (e + 1) * SSM_DIM)
                kept = jnp.sum(through[:, lanes], axis=1, keepdims=True)
                small_ref[0, e : e + 1, here] = direct[e : e + 1, :]
                small_ref[0, 2 + e : 3 + e, here] = log_grad[e : e + 1, :] + within[e] + kept
            dx_ref[here, :] = dxs * steps + skip_ref[...] * dy_now
            skip_sum += jnp.sum(x_now * dy_now, axis=0, keepdims=True)
            flow[...] = entry[CHUNK - 1 :, :] * flow[...] + dot(c_turned[:, here], entered)
        small_ref[0, 4:8, :] = jnp.zeros((4, rows), jnp.float32)
        small_ref[0, 4:5, 0 : 2 * SSM_DIM] = skip_sum

        @pl.when(pl.program_id(0) == PAIRS - 1)
        def _():
            for k in range(chunks):
                here = slice(k * CHUNK, (k + 1) * CHUNK)
                grads = low(inner_grad[k])
                db_ref[here, :] += dot(grads, low(c_ref[here, :]))
                dc_ref[here, :] += dot(grads, low(b_ref[here, :]), TN)

    whole = lambda i, m: (0, 0)
    lanes = lambda i, m: (0, i)
    pair = lambda i, m: (i, 0, 0)
    return pl.pallas_call(
        pinned(kernel, 11, after),
        grid_spec=pltpu.PrefetchScalarGridSpec(
            num_scalar_prefetch=1,
            grid=(PAIRS,),
            in_specs=[
                pl.BlockSpec((rows, 2 * SSM_DIM), lanes),
                pl.BlockSpec((rows, 2 * SSM_DIM), lanes),
                pl.BlockSpec((rows, STATE), lambda i, m: (0, PAIRS)),
                pl.BlockSpec((rows, STATE), lambda i, m: (0, PAIRS + 1)),
                pl.BlockSpec((1, 2, rows), pair),
                pl.BlockSpec((1, 2, rows), pair),
                pl.BlockSpec((STATE, 2 * SSM_DIM), lanes),
                pl.BlockSpec((STATE, 2 * SSM_DIM), lanes),
                pl.BlockSpec((1, 2 * SSM_DIM), lanes),
                pl.BlockSpec((8, rows), whole),
            ] + pins(after),
            out_specs=[
                pl.BlockSpec((rows, 2 * SSM_DIM), lanes),
                pl.BlockSpec((rows, STATE), whole),
                pl.BlockSpec((rows, STATE), whole),
                pl.BlockSpec((1, 8, rows), pair),
            ],
            scratch_shapes=[
                pltpu.VMEM((chunks, CHUNK, CHUNK), jnp.float32),
                pltpu.VMEM((chunks, CHUNK, CHUNK), jnp.float32),
                pltpu.VMEM((chunks, CHUNK, CHUNK), jnp.float32),
                pltpu.VMEM((chunks, STATE, 2 * SSM_DIM), jnp.float32),
                pltpu.VMEM((STATE, 2 * SSM_DIM), jnp.float32),
                pltpu.VMEM((STATE, rows), jnp.bfloat16),
                pltpu.VMEM((STATE, rows), jnp.bfloat16),
            ],
        ),
        out_shape=[
            jax.ShapeDtypeStruct((rows, INNER), jnp.float32),
            jax.ShapeDtypeStruct((rows, STATE), jnp.float32),
            jax.ShapeDtypeStruct((rows, STATE), jnp.float32),
            jax.ShapeDtypeStruct((PAIRS, 8, rows), jnp.float32),
        ],
        compiler_params=pltpu.CompilerParams(vmem_limit_bytes=40 * 2**20),
        cost_estimate=pl.CostEstimate(flops=3 * 10**9, bytes_accessed=rows * INNER * 12, transcendentals=2**21),
        name="ssm_back",
    )(meta, conv, dy, conv, conv, cum.reshape(PAIRS, 2, rows), step.reshape(PAIRS, 2, rows), state_in, state_grad,
      skip, start_row, *after)


def chain_states(earlier, later):
    return (earlier[0] * later[0], earlier[1] * later[0] + later[1])


def scan_states(carry, state, span, fast, backward):
    wide = jnp.repeat(carry, SSM_DIM)[None, :]
    if not fast:
        ident = (jnp.ones_like(wide), jnp.zeros_like(state))
        return (carried_in if backward else prefix)((wide, state), span, chain_states, ident)[1]
    flow = Flow(scan_stages(carry, state, backward))
    while flow.sends:
        flow.go()
    return flow.result


def scan_stages(carry, state, backward, extra=None):
    total = (jnp.repeat(carry, SSM_DIM)[None, :], state)
    start = None
    for name in ("c", "x", "y"):
        place = lax.axis_index(name)
        at = lax.broadcasted_iota(jnp.int32, (16, INNER), 0)
        block = jnp.where(at == 0, total[0], 0.0)
        if extra is not None:
            rest = jnp.pad(extra, (0, INNER - extra.shape[0]))[None, :]
            for place_at in range(1, 4):
                term = lax.reduce_precision(rest, 8, 7)
                block = jnp.where(at == place_at, term, block)
                rest = rest - term
        packed = jnp.concatenate([total[1].astype(jnp.bfloat16), block.astype(jnp.bfloat16)], axis=0)
        (packed,) = yield [(packed, name, SWAP)]
        packed = packed.astype(jnp.float32)
        other = (packed[STATE : STATE + 1], packed[:STATE])
        if extra is not None:
            extra = extra + jnp.sum(packed[STATE + 1 : STATE + 4, : extra.shape[0]], axis=0)
        leads = place == (0 if backward else 1)
        seen = (jnp.where(leads, other[0], 1.0), jnp.where(leads, other[1], 0.0))
        start = seen if start is None else chain_states(seen, start)
        if name != "y":
            forward = chain_states(other, total)
            reverse = chain_states(total, other)
            total = jax.tree.map(lambda p, q: jnp.where(leads, p, q), forward, reverse)
    return start[1] if extra is None else [start[1], extra]


KEYS = 512
PAIR = 2 * HEAD_DIM


def attention_forward(q_wide, kv, meta, starts, after=()):
    rows = q_wide.shape[2]
    blocks = kv.shape[0]
    ratio = HEADS_Q // HEADS_KV
    wide = min(512, rows)

    def kernel(meta_ref, q_ref, kv_ref, start_ref, o_ref, log_ref, top, total):
        b = pl.program_id(1)

        @pl.when(b == 0)
        def _():
            top[...] = jnp.full(top.shape, masked_score, jnp.float32)
            total[...] = jnp.zeros(total.shape, jnp.float32)
            o_ref[...] = jnp.zeros(o_ref.shape, jnp.float32)

        def block(partial):
            pair = kv_ref[0, 0]
            turned = pair.T[HEAD_DIM:, :]
            for h in range(ratio):
                for r in range(0, rows, wide):
                    here = slice(r, r + wide)
                    scores = jnp.dot(pair, q_ref[h, :, here], preferred_element_type=jnp.float32)
                    if partial:
                        keys = b * KEYS + lax.broadcasted_iota(jnp.int32, scores.shape, 0)
                        mine = meta_ref[2] + r + lax.broadcasted_iota(jnp.int32, scores.shape, 1)
                        visible = (keys >= start_ref[0:1, here]) & (keys <= mine)
                        scores = jnp.where(visible, scores, masked_score)
                    before = top[h, 0:1, here]
                    peak = jnp.maximum(before, jnp.max(scores, axis=0, keepdims=True))
                    part = jnp.exp(scores - peak)
                    if partial:
                        part = jnp.where(visible, part, 0.0)
                    fade = jnp.exp(before - peak)
                    top[h, 0:1, here] = peak
                    total[h, 0:1, here] = total[h, 0:1, here] * fade + jnp.sum(part, axis=0, keepdims=True)
                    o_ref[h, :, here] = o_ref[h, :, here] * fade + jnp.dot(
                        turned, part.astype(jnp.bfloat16), preferred_element_type=jnp.float32
                    )

        needed = (b >= meta_ref[0]) & (b < meta_ref[1])
        partial = ((b + 1) * KEYS > meta_ref[2]) | (b * KEYS < meta_ref[3])

        @pl.when(needed & partial)
        def _():
            block(True)

        @pl.when(needed & jnp.logical_not(partial))
        def _():
            block(False)

        @pl.when(b == blocks - 1)
        def _():
            for h in range(ratio):
                sums = total[h, 0:1, :]
                o_ref[h] = o_ref[h] / sums
                log_ref[h] = jnp.broadcast_to(top[h, 0:1, :] + jnp.log(sums), (8, rows))

    heads = lambda g, b, m: (g, 0, 0)
    return pl.pallas_call(
        pinned(kernel, 4, after),
        grid_spec=pltpu.PrefetchScalarGridSpec(
            num_scalar_prefetch=1,
            grid=(HEADS_KV, blocks),
            in_specs=[
                pl.BlockSpec((ratio, PAIR, rows), heads),
                pl.BlockSpec((1, 1, KEYS, PAIR), lambda g, b, m: (b, g, 0, 0)),
                pl.BlockSpec((8, rows), lambda g, b, m: (0, 0)),
            ] + pins(after),
            out_specs=[
                pl.BlockSpec((ratio, HEAD_DIM, rows), heads),
                pl.BlockSpec((ratio, 8, rows), heads),
            ],
            scratch_shapes=[
                pltpu.VMEM((ratio, 8, rows), jnp.float32),
                pltpu.VMEM((ratio, 8, rows), jnp.float32),
            ],
        ),
        out_shape=[
            jax.ShapeDtypeStruct((HEADS_Q, HEAD_DIM, rows), jnp.float32),
            jax.ShapeDtypeStruct((HEADS_Q, 8, rows), jnp.float32),
        ],
        compiler_params=pltpu.CompilerParams(vmem_limit_bytes=48 * 2**20),
        cost_estimate=pl.CostEstimate(flops=2 * 10**10, bytes_accessed=2**23, transcendentals=2**23),
        name="attend",
    )(meta, q_wide, kv, starts, *after)


def attention_backward(q_wide, g_wide, kv, logs, mixed, meta, starts, group, after=()):
    rows = q_wide.shape[2]
    blocks = kv.shape[0]
    ratio = HEADS_Q // HEADS_KV
    wide = min(512, rows)

    def kernel(meta_ref, q_ref, g_ref, kv_ref, log_ref, o_ref, start_ref, dkv_ref, dq_ref, delta, sums):
        b = pl.program_id(0)

        @pl.when(b == 0)
        def _():
            dq_ref[...] = jnp.zeros(dq_ref.shape, jnp.float32)
            for h in range(ratio):
                both = g_ref[h, HEAD_DIM:, :].astype(jnp.float32) * o_ref[h]
                delta[h] = jnp.broadcast_to(jnp.sum(both, axis=0, keepdims=True), (8, rows))

        def block(partial):
            pair = kv_ref[0, 0]
            turned = pair.T[:HEAD_DIM, :]
            for h in range(ratio):
                for r in range(0, rows, wide):
                    here = slice(r, r + wide)
                    q_now = q_ref[h, :, here]
                    g_now = g_ref[h, :, here]
                    scores = jnp.dot(pair, q_now, preferred_element_type=jnp.float32)
                    probs = jnp.exp(scores - log_ref[h, 0:1, here])
                    if partial:
                        keys = b * KEYS + lax.broadcasted_iota(jnp.int32, scores.shape, 0)
                        mine = meta_ref[2] + r + lax.broadcasted_iota(jnp.int32, scores.shape, 1)
                        visible = (keys >= start_ref[0:1, here]) & (keys <= mine)
                        probs = jnp.where(visible, probs, 0.0)
                    grads = jnp.dot(pair, g_now, preferred_element_type=jnp.float32)
                    low_grads = (probs * (grads - delta[h, 0:1, here])).astype(jnp.bfloat16)
                    change = lax.dot_general(
                        probs.astype(jnp.bfloat16), g_now, NT, preferred_element_type=jnp.float32
                    ) + lax.dot_general(low_grads, q_now, NT, preferred_element_type=jnp.float32)
                    if h == 0 and r == 0:
                        sums[...] = change
                    else:
                        sums[...] += change
                    dq_ref[h, :, here] += jnp.dot(turned, low_grads, preferred_element_type=jnp.float32)
            dkv_ref[0, 0] = sums[...].astype(jnp.bfloat16)

        needed = (b >= meta_ref[0]) & (b < meta_ref[1])
        partial = ((b + 1) * KEYS > meta_ref[2]) | (b * KEYS < meta_ref[3])

        @pl.when(needed & partial)
        def _():
            block(True)

        @pl.when(needed & jnp.logical_not(partial))
        def _():
            block(False)

        @pl.when(jnp.logical_not(needed))
        def _():
            dkv_ref[0, 0] = jnp.zeros((KEYS, PAIR), jnp.bfloat16)

    heads = lambda b, m: (group, 0, 0)
    return pl.pallas_call(
        pinned(kernel, 7, after),
        grid_spec=pltpu.PrefetchScalarGridSpec(
            num_scalar_prefetch=1,
            grid=(blocks,),
            in_specs=[
                pl.BlockSpec((ratio, PAIR, rows), heads),
                pl.BlockSpec((ratio, PAIR, rows), heads),
                pl.BlockSpec((1, 1, KEYS, PAIR), lambda b, m: (b, group, 0, 0)),
                pl.BlockSpec((ratio, 8, rows), heads),
                pl.BlockSpec((ratio, HEAD_DIM, rows), heads),
                pl.BlockSpec((8, rows), lambda b, m: (0, 0)),
            ] + pins(after),
            out_specs=[
                pl.BlockSpec((1, 1, KEYS, PAIR), lambda b, m: (b, 0, 0, 0)),
                pl.BlockSpec((ratio, HEAD_DIM, rows), lambda b, m: (0, 0, 0)),
            ],
            scratch_shapes=[
                pltpu.VMEM((ratio, 8, rows), jnp.float32),
                pltpu.VMEM((KEYS, PAIR), jnp.float32),
            ],
        ),
        out_shape=[
            jax.ShapeDtypeStruct((blocks, 1, KEYS, PAIR), jnp.bfloat16),
            jax.ShapeDtypeStruct((ratio, HEAD_DIM, rows), jnp.float32),
        ],
        compiler_params=pltpu.CompilerParams(vmem_limit_bytes=48 * 2**20),
        cost_estimate=pl.CostEstimate(flops=2 * 10**10, bytes_accessed=2**23, transcendentals=2**23),
        name="attend_back",
    )(meta, q_wide, g_wide, kv, logs, mixed, starts, *after)


def scatter_span(value, span, fast):
    if not fast:
        return lax.psum_scatter(value, span, scatter_dimension=0).astype(jnp.float32)
    flow = Flow(scatter_stages(value))
    while flow.sends:
        flow.go()
    return flow.result


def scatter_stages(value):
    _, y, x, c = (lax.axis_index(name) for name in GRID)
    value = value.reshape((2, 2, 2) + value.shape[1:])
    for name, place, axis in (("c", c, 2), ("y", y, 0), ("x", x, 0)):
        send = lax.dynamic_index_in_dim(value, 1 - place, axis, keepdims=False)
        (arrived,) = yield [(send, name, SWAP)]
        keep = lax.dynamic_index_in_dim(value, place, axis, keepdims=False)
        value = keep.astype(jnp.float32) + arrived.astype(jnp.float32)
        if name != "x":
            value = value.astype(jnp.bfloat16)
    return value


def plane_stages(value):
    for pairs in ([(0, 1), (1, 0), (2, 3), (3, 2)], [(0, 2), (2, 0), (1, 3), (3, 1)]):
        (other,) = yield [(value, "z", pairs)]
        value = value + other
    return value


def offsets_of():
    places, at = {}, 0
    for name_key, extent in layout():
        places[name_key] = (at, extent)
        at += math.prod(extent)
    return places


def early_weights(params):
    places = offsets_of()
    buffers, spread_flow, (slots, all_slots), where = gather_lines(params)
    spread_flow.go()
    names = (W_QUERY, W_KEY, W_VALUE, W_ATTN_OUT, W_GATE_SSM, W_X_SSM, W_B_C)
    misc_at = places[W_STEP][0]
    first = unpack_lines(
        buffers[:16], slots, where, [flat_segment(name_key) for name_key in names] + [(0, 16, LINE), (misc_at, 288, LINE)]
    )
    weights = dict(zip(names, first))
    weights[NORM_ATTN] = first[-2].reshape(-1)[:D]
    misc = first[-1].reshape(-1)
    for name_key in (W_STEP,) + small_names[1:-1]:
        at, extent = places[name_key]
        weights[name_key] = misc[at - misc_at : at - misc_at + math.prod(extent)].reshape(extent)
    return weights, spread_flow, (buffers, all_slots, where)


def flat_segment(name_key):
    at, extent = offsets_of()[name_key]
    return (at, extent[0], extent[1])


def late_weights(held, after):
    buffers, slots, where = held
    names = (W_SSM_OUT, W_GATE, W_UP_PROJ, W_DOWN)
    norm_at = offsets_of()[NORM_FFN][0]
    second = unpack_lines(
        buffers, slots, where, [flat_segment(name_key) for name_key in names] + [(norm_at, 16, LINE)], after
    )
    weights = dict(zip(names, second))
    weights[NORM_FFN] = second[-1].reshape(-1)[norm_at % LINE : norm_at % LINE + D]
    return weights


def pack_late(gate, up, down, ssm_low, grad_branch, grad_norm_ffn, after):
    places = offsets_of()
    out_at = places[W_SSM_OUT][0]
    lane = places[W_GATE][0] % LINE
    boundary = 2 * PLANE * LINE
    tail_from = (boundary - out_at) // D
    tail = matmul_left_t(ssm_low[:, tail_from:], grad_branch).reshape(-1)
    tail = tail[boundary - out_at - tail_from * D :]
    head = jnp.concatenate([jnp.zeros((14 * LINE,), jnp.float32), tail, grad_norm_ffn])
    head_rows = head.shape[0] // LINE
    carry = jnp.zeros((8, LINE), jnp.float32).at[7, :lane].set(head[head_rows * LINE :])
    head = head[: head_rows * LINE].reshape(head_rows, LINE).astype(jnp.bfloat16)
    return pack_lines(
        None, 2 * PLANE + 32, head_rows, [gate, up, down], lane, 0, [(head, 0)], carry, 48, after
    )


def pack_out(ssm_low, grad_branch, after):
    out_at = offsets_of()[W_SSM_OUT][0]
    first_row = (8 + out_at // LINE) // 16 * 16
    rows = first_row + SSM_HEADS * SSM_DIM * D // LINE
    return pack_lines(
        None, rows, first_row, [(ssm_low, grad_branch)], out_at % LINE, (8 + out_at // LINE) % 8, [],
        jnp.zeros((8, LINE), jnp.float32), 0, after,
    )


def pack_ssm(target, segments, small, ssm_low, grad_branch, after):
    places = offsets_of()
    misc = [small[name_key].reshape(-1) for name_key in (W_STEP,) + small_names[1:-1]]
    count = sum(part.shape[0] for part in misc)
    misc_rows = (count // LINE + 16) // 16 * 16
    opening = matmul_left_t(ssm_low[:, :16], grad_branch).reshape(-1)
    misc = jnp.concatenate(misc + [opening[: misc_rows * LINE - count]])
    misc = misc.reshape(misc_rows, LINE).astype(jnp.bfloat16)
    first_row = 8 + places[W_ATTN_OUT][0] // LINE
    return pack_lines(
        target, target.shape[0], first_row, segments, 0, 0, [(misc, 8 + places[W_STEP][0] // LINE)], None, 0, after
    )


def pack_qkv(segments, attended, grad_branch, grad_norm_attn, after):
    places = offsets_of()
    out_row = 8 + places[W_ATTN_OUT][0] // LINE
    rows = (8 + SHARD) // 16 * 16 + 8 * PIECE
    closing = matmul_left_t(attended[:, :16], grad_branch).reshape(-1, LINE)
    closing = closing[: rows - out_row].astype(jnp.bfloat16)
    opening = jnp.concatenate([jnp.zeros((8, LINE), jnp.float32), grad_norm_attn.reshape(-1, LINE)]).astype(jnp.bfloat16)
    return pack_lines(
        None, rows, 16, segments, 0, 0, [(opening, 0), (closing, out_row)], None, 0, after
    )


def own_lines(early, late, corner):
    z, y, x, c = (lax.axis_index(name) for name in GRID)
    place = 4 * y + 2 * x + c
    shard = SHARD * place
    start = jnp.where(z < 2, (8 + shard) % 16, (14 + shard) % 16)
    lines = jnp.where(z < 2, early, late)
    lines = jnp.where((z == 0) & (place < 2), corner[:WIN], lines)
    lines = lax.dynamic_slice(lines, (start, 0), (SHARD, LINE)).astype(jnp.float32)
    return lines.reshape(-1)


def body(span, group, fast, tokens, params, cotangent, offsets):
    rows_dev = tokens.shape[0]
    group_rows = rows_dev * lax.axis_size(span)
    all_rows = group_rows * lax.axis_size(group)
    ssm_inner = SSM_HEADS * SSM_DIM
    score_scale = HEAD_DIM ** (-0.5)
    bounds = offsets[0]
    my_start = lax.axis_index(span) * rows_dev
    row_index = my_start + jnp.arange(rows_dev, dtype=jnp.int32)
    seq_id, positions = sequence_info(row_index, bounds)
    first_start = row_index[0] - positions[0]
    last_row = my_start + rows_dev - 1
    cosine, sine = rotary_tables(positions)
    if fast:
        weights, spread_flow, held = early_weights(params)
    else:
        weights = unpack(lax.all_gather(params, group + span, axis=0, tiled=True))
    small_f32 = {name_key: weights[name_key].astype(jnp.float32) for name_key in small_names[:-1]}
    x_rows = tokens.astype(jnp.float32)
    normed_one, norm_one_back = jax.vjp(rms_norm, x_rows, small_f32[NORM_ATTN])
    hidden = normed_one.astype(jnp.bfloat16)
    across = lambda weight: lax.dot_general(
        weight, hidden, (((0,), (1,)), ((), ())), preferred_element_type=jnp.float32
    )
    q_rot = rotate(across(weights[W_QUERY]), cosine, sine, HEADS_Q).astype(jnp.bfloat16)
    k_rot = rotate(across(weights[W_KEY]), cosine, sine, HEADS_KV).astype(jnp.bfloat16)
    value_low = across(weights[W_VALUE]).astype(jnp.bfloat16).reshape(HEADS_KV, HEAD_DIM, rows_dev)
    kv_mine = jnp.concatenate([k_rot, value_low], axis=1).transpose(0, 2, 1)
    row_starts = row_index - positions
    kv_local = kv_mine.reshape(HEADS_KV, rows_dev, PAIR)
    xbc = jnp.concatenate(
        [matmul(hidden, weights[W_X_SSM]), matmul(hidden, weights[W_B_C])], axis=1
    )
    step_raw = matmul(hidden, weights[W_STEP])
    rim_rows = passed_along(xbc[rows_dev - 8 :], span, 1)
    ssm_meta = jnp.concatenate([my_start[None], row_starts[CHUNK - 1 :: CHUNK]]).astype(jnp.int32)
    conv_bias = small_f32[CONV_BIAS][None, :]
    convolve = lambda after: conv_forward(
        xbc, rim_rows, small_f32[CONV_WEIGHT], conv_bias, ssm_meta, row_starts[:, None], after
    )
    if fast:
        key_blocks = lax.all_gather(kv_local, span)
        conv_values = convolve(())
    else:
        conv_values = convolve(())
    step_in = step_raw.T + small_f32[STEP_BIAS][:, None]
    step_rows = jax.nn.softplus(step_in)
    decay = -jnp.exp(small_f32[DECAY_LOG])
    logs_step = step_rows * decay[:, None]
    order = jnp.arange(rows_dev)
    upto = (order[:, None] <= order[None, :]).astype(jnp.float32)
    cumul = jnp.dot(logs_step, upto, precision=highest)
    chunk_cum = jnp.dot(
        logs_step.reshape(-1, CHUNK), upto[:CHUNK, :CHUNK], precision=highest
    ).reshape(SSM_HEADS, rows_dev)
    went_on = row_starts < my_start
    entry_rows = jnp.where(went_on[None, :], jnp.exp(cumul), 0.0)
    in_last = row_index >= row_starts[rows_dev - 1]
    tail_rows = jnp.exp(jnp.where(in_last[None, :], cumul[:, -1:] - cumul, masked_score))
    carry_all = entry_rows[:, -1]
    summarize = lambda after: weighted_state(conv_values, PAIRS, conv_values, tail_rows * step_rows, after)
    meta = jnp.stack(
        [first_start // KEYS, last_row // KEYS + 1, my_start, row_starts[rows_dev - 1]]
    ).astype(jnp.int32)
    q_wide = jnp.pad(q_rot * jnp.bfloat16(score_scale), ((0, 0), (0, HEAD_DIM), (0, 0)))
    start_row = jnp.broadcast_to(row_starts[None, :], (8, rows_dev))
    if fast:
        (local_state,) = bracket(summarize, [spread_flow])
        scan = Flow(scan_stages(carry_all, local_state, False))
        (gate_in,) = fence([hidden], scan.values())
        gate_ssm = matmul(gate_in, weights[W_GATE_SSM])
        scan.go()
        (gate_ssm,) = fence([gate_ssm], scan.values())
        scan.go()
        mixed, logs = bracket(
            lambda after: attention_forward(
                q_wide, key_blocks, meta, start_row, (*after, gate_ssm, *spread_flow.values())
            ),
            [scan],
        )
        spread_flow.go()
        state_in = scan.result
    else:
        gate_ssm = matmul(hidden, weights[W_GATE_SSM])
        key_blocks = lax.all_gather(kv_local, span)
        if rows_dev != KEYS:
            key_blocks = key_blocks.transpose(1, 0, 2, 3).reshape(HEADS_KV, -1, KEYS, PAIR).transpose(1, 0, 2, 3)
        state_in = scan_states(carry_all, summarize(()), span, fast, False)
        mixed, logs = attention_forward(q_wide, key_blocks, meta, start_row)
    attended = mixed.astype(jnp.bfloat16).reshape(HEADS_Q * HEAD_DIM, rows_dev).T
    attn_out = matmul(attended, weights[W_ATTN_OUT])
    skip_wide = jnp.repeat(small_f32[SKIP_GAIN], SSM_DIM)[None, :]
    ssm_y = ssm_forward(
        conv_values, chunk_cum, step_rows, state_in, skip_wide, ssm_meta, row_starts[:, None], start_row
    )
    normed_ssm, gnorm_back = jax.vjp(gated_norm, ssm_y, gate_ssm, small_f32[NORM_SSM])
    ssm_low = normed_ssm.astype(jnp.bfloat16)
    if fast:
        held = (held[0] + spread_flow.result,) + held[1:]
        weights.update(late_weights(held, [ssm_y]))
    small_f32[NORM_FFN] = weights[NORM_FFN].astype(jnp.float32)
    ssm_out = matmul(ssm_low, weights[W_SSM_OUT])
    middle = x_rows + attn_out + ssm_out
    normed_two, norm_two_back = jax.vjp(rms_norm, middle, small_f32[NORM_FFN])
    hidden_two = normed_two.astype(jnp.bfloat16)
    gate_ffn = matmul(hidden_two, weights[W_GATE])
    upper = matmul(hidden_two, weights[W_UP_PROJ])
    activation_f32, swiglu_back = jax.vjp(swiglu, gate_ffn, upper)
    activation = activation_f32.astype(jnp.bfloat16)
    ffn_out = matmul(activation, weights[W_DOWN])
    result = middle + ffn_out
    squares = jnp.stack(
        [
            jnp.sum(result * result),
            jnp.sum(attn_out * attn_out),
            jnp.sum(ssm_out * ssm_out),
            jnp.sum(ffn_out * ffn_out),
        ]
    )
    grad_out = cotangent.astype(jnp.float32)
    grad_activation = matmul_right_t(cotangent, weights[W_DOWN])
    grad_gate_f32, grad_upper_f32 = swiglu_back(grad_activation)
    grad_gate = grad_gate_f32.astype(jnp.bfloat16)
    grad_upper = grad_upper_f32.astype(jnp.bfloat16)
    grad_hidden_two = matmul_right_t(grad_gate, weights[W_GATE]) + matmul_right_t(
        grad_upper, weights[W_UP_PROJ]
    )
    grad_middle_norm, grad_norm_ffn = norm_two_back(grad_hidden_two)
    grad_middle = grad_out + grad_middle_norm
    grad_branch = grad_middle.astype(jnp.bfloat16)
    grad_attended = matmul_right_t(weights[W_ATTN_OUT], grad_branch).astype(jnp.bfloat16)
    grad_ssm_low = matmul_right_t(grad_branch, weights[W_SSM_OUT])
    grad_ssm_y, grad_gate_ssm_f32, grad_norm_ssm = gnorm_back(grad_ssm_low)
    grad_state_local = weighted_state(conv_values, PAIRS + 1, grad_ssm_y, entry_rows)
    if fast:
        scan = Flow(scan_stages(carry_all, grad_state_local, True, squares)).go()
        (late,) = bracket(
            lambda after: pack_late(
                (hidden_two, grad_gate), (hidden_two, grad_upper), (activation, cotangent),
                ssm_low, grad_branch, grad_norm_ffn, after,
            ),
            [scan],
        )
        late_flow = Flow(reduce_stages(late, 1, 14))
        (grad_branch_low,) = fence([grad_branch], scan.values() + late_flow.values())
        early = pack_out(ssm_low, grad_branch_low, ())
        scan.go()
        grad_state_out, squares = scan.result
        (early,) = fence([early], [grad_state_out])
        late_flow.go()
        (early,) = fence([early], late_flow.values())
        stats_flow = Flow(plane_stages(squares))
        around = lambda call: bracket(call, [late_flow])
    else:
        grad_state_out = scan_states(carry_all, grad_state_local, span, fast, True)
        around = lambda call: call(())
    grad_x, grad_b, grad_c, grad_small = around(
        lambda after: ssm_backward(
            conv_values, grad_ssm_y, chunk_cum, step_rows, state_in, grad_state_out, skip_wide, ssm_meta, start_row,
            after,
        )
    )
    grad_direct = grad_small[:, 0:2].reshape(SSM_HEADS, rows_dev)
    grad_logs = grad_small[:, 2:4].reshape(SSM_HEADS, rows_dev)
    grad_decay_log = decay * jnp.sum(step_rows * grad_logs, axis=1)
    grad_step_rows = (grad_direct + decay[:, None] * grad_logs) * jax.nn.sigmoid(step_in)
    grad_step_bias = jnp.sum(grad_step_rows, axis=1)
    grad_step_raw_f32 = grad_step_rows.T
    grad_skip_gain = jnp.sum(grad_small[:, 4, : 2 * SSM_DIM].reshape(SSM_HEADS, SSM_DIM), axis=1)
    if fast:
        around = lambda call: bracket(call, [late_flow, stats_flow])
    grad_main, grad_tail, grad_edge, grad_taps = around(
        lambda after: conv_backward(
            grad_x, grad_b, grad_c, xbc, rim_rows, small_f32[CONV_WEIGHT], conv_bias, ssm_meta,
            row_starts[:, None], after,
        )
    )
    grad_conv_weight = grad_taps[:CONV]
    grad_conv_bias = grad_taps[CONV]
    rim_back = passed_along(grad_edge, span, -1)
    grad_tail = grad_tail + jnp.pad(rim_back, ((8, 0), (0, 0)))
    grad_xbc = lax.dynamic_update_slice(grad_main, grad_tail.astype(jnp.bfloat16), (rows_dev - 16, 0))
    grad_gate_ssm = grad_gate_ssm_f32.astype(jnp.bfloat16)
    grad_step_raw = grad_step_raw_f32.astype(jnp.bfloat16)
    grad_w_step = matmul_left_t(hidden, grad_step_raw)
    grad_hidden_ssm = (
        matmul_right_t(grad_gate_ssm, weights[W_GATE_SSM])
        + matmul_right_t(grad_xbc[:, :ssm_inner], weights[W_X_SSM])
        + matmul_right_t(grad_xbc[:, ssm_inner:], weights[W_B_C])
        + matmul_right_t(grad_step_raw, weights[W_STEP])
    )
    small = {
        W_STEP: grad_w_step,
        CONV_WEIGHT: grad_conv_weight,
        CONV_BIAS: grad_conv_bias,
        STEP_BIAS: grad_step_bias,
        DECAY_LOG: grad_decay_log,
        SKIP_GAIN: grad_skip_gain,
        NORM_SSM: grad_norm_ssm,
        NORM_FFN: grad_norm_ffn,
    }
    parts = []
    if fast:
        (early,) = bracket(lambda after: pack_ssm(
            early,
            [
                (attended, grad_branch), (hidden, grad_gate_ssm),
                (hidden, grad_xbc[:, :ssm_inner]), (hidden, grad_xbc[:, ssm_inner:]),
            ],
            small, ssm_low, grad_branch, (*after, *late_flow.values()),
        ), [stats_flow])
        early_flow = Flow(reduce_stages(early, 0, 8))
        (grad_attended,) = fence([grad_attended], early_flow.values() + late_flow.values())
        around = lambda call: bracket(call, [early_flow])
    g_wide = jnp.pad(grad_attended.reshape(HEADS_Q, HEAD_DIM, rows_dev), ((0, 0), (HEAD_DIM, 0), (0, 0)))
    if fast:
        early_flow.go()
        (g_wide,) = fence([g_wide], early_flow.values())
    for group_at in range(HEADS_KV):
        after_part = [part[1] for part in parts]
        if fast and group_at == 0:
            after_part = late_flow.values()
        parts.append(
            around(
                lambda after: attention_backward(
                    q_wide, g_wide, key_blocks, logs, mixed, meta, start_row, group_at, (*after, *after_part)
                )
            )
        )
    grad_kv = jnp.concatenate([part[0] for part in parts], axis=1)
    grad_q_turned = jnp.concatenate([part[1] for part in parts], axis=0)
    if rows_dev != KEYS:
        grad_kv = grad_kv.transpose(1, 0, 2, 3).reshape(HEADS_KV, -1, rows_dev, PAIR).transpose(1, 0, 2, 3)
    if fast:
        late_flow.go([parts[-1][1]])
        scatter = Flow(scatter_stages(grad_kv))
        (grad_q_turned,) = fence([grad_q_turned], scatter.values() + early_flow.values() + late_flow.values())
    turned_back = rotate(grad_q_turned * score_scale, cosine, -sine, HEADS_Q).astype(jnp.bfloat16)
    grad_query_low = turned_back.reshape(HEADS_Q * HEAD_DIM, rows_dev).T
    if fast:
        scatter.go()
        early_flow.go()
        (grad_query_low,) = fence([grad_query_low], scatter.values() + early_flow.values())
    grad_hidden = grad_hidden_ssm + matmul_right_t(grad_query_low, weights[W_QUERY])
    if fast:
        scatter.go()
        (grad_hidden,) = fence([grad_hidden], scatter.values())
        scatter.go()
        grad_kv_mine = scatter.result
    else:
        grad_kv_mine = scatter_span(grad_kv, span, fast)
    grad_kv_mine = grad_kv_mine.transpose(0, 2, 1)
    grad_key_low = rotate(grad_kv_mine[:, :HEAD_DIM], cosine, -sine, HEADS_KV).astype(jnp.bfloat16)
    grad_key_low = grad_key_low.reshape(HEADS_KV * HEAD_DIM, rows_dev).T
    grad_value_low = grad_kv_mine[:, HEAD_DIM:].astype(jnp.bfloat16).reshape(HEADS_KV * HEAD_DIM, rows_dev).T
    grad_hidden = (
        grad_hidden
        + matmul_right_t(grad_key_low, weights[W_KEY])
        + matmul_right_t(grad_value_low, weights[W_VALUE])
    )
    grad_x_norm, grad_norm_attn = norm_one_back(grad_hidden)
    grad_tokens = grad_middle + grad_x_norm
    if fast:
        corner = pack_qkv(
            [(hidden, grad_query_low), (hidden, grad_key_low), (hidden, grad_value_low)],
            attended, grad_branch, grad_norm_attn, early_flow.values(),
        )
        corner_flow = Flow(corner_stages(corner))
        for _ in range(3):
            corner_flow.go()
        early_flow.go()
        ((pieces, _, _), *_) = corner_flow.sends
        (pieces,) = fence([pieces], early_flow.values())
        corner_flow.sends = [(pieces, axis, pairs) for _, axis, pairs in corner_flow.sends]
        for flow in (early_flow, late_flow, corner_flow):
            while flow.sends:
                flow.go()
        stats = jnp.sqrt(stats_flow.result / (all_rows * D))
        grad_shard = own_lines(early_flow.result, late_flow.result, corner_flow.result)
        return (result.astype(jnp.bfloat16), grad_tokens, grad_shard, stats)
    small[NORM_ATTN] = grad_norm_attn
    stats = jnp.sqrt(lax.psum(squares, group + span) / (all_rows * D))
    pairs = {
        W_QUERY: (hidden, grad_query_low),
        W_KEY: (hidden, grad_key_low),
        W_VALUE: (hidden, grad_value_low),
        W_ATTN_OUT: (attended, grad_branch),
        W_GATE_SSM: (hidden, grad_gate_ssm),
        W_X_SSM: (hidden, grad_xbc[:, :ssm_inner]),
        W_B_C: (hidden, grad_xbc[:, ssm_inner:]),
        W_SSM_OUT: (ssm_low, grad_branch),
        W_GATE: (hidden_two, grad_gate),
        W_UP_PROJ: (hidden_two, grad_upper),
        W_DOWN: (activation, cotangent),
    }
    grad_dict = dict(small)
    for name_key, (left, right) in pairs.items():
        grad_dict[name_key] = matmul_left_t(left, right)
    flat_parts = [grad_dict[name_key].reshape(-1) for name_key, extent in layout()]
    used_entries = 0
    for part_array in flat_parts:
        used_entries += part_array.shape[0]
    flat_parts.append(jnp.zeros((params.shape[0] * lax.axis_size(group + span) - used_entries,), jnp.float32))
    grad_shard = lax.psum_scatter(
        jnp.concatenate(flat_parts), group + span, scatter_dimension=0, tiled=True
    )
    return (result.astype(jnp.bfloat16), grad_tokens, grad_shard, stats)


def solution(mesh):
    fast = (mesh.shape["group"], mesh.shape["span"]) == FAST
    if fast:
        mesh = Mesh(mesh.devices.reshape(4, 2, 2, 2), GRID)
        group, span = (GRID[:1], GRID[1:])
    else:
        group, span = (("group",), ("span",))

    def program(tokens, params, cotangent, offsets):
        return body(span, group, fast, tokens, params, cotangent, offsets)

    return jax.shard_map(
        program,
        mesh=mesh,
        in_specs=(P(group + span, None), P(group + span), P(group + span, None), P(group, None)),
        out_specs=(P(group + span, None), P(group + span, None), P(group + span), P()),
        check_vma=False,
    )
```

```python
import math

import jax
import jax.numpy as jnp
import numpy as np
from jax import lax
from jax.experimental import pallas as pl
from jax.experimental.pallas import tpu as pltpu
from jax.sharding import Mesh, PartitionSpec as P

D = 1024
HEADS_Q = 8
HEADS_KV = 2
HEAD_DIM = 64
SSM_HEADS = 24
SSM_DIM = 64
STATE = 128
CONV = 4
FF = 2048
(
    NORM_ATTN,
    W_QUERY,
    W_KEY,
    W_VALUE,
    W_ATTN_OUT,
    W_GATE_SSM,
    W_X_SSM,
    W_B_C,
    W_STEP,
    CONV_WEIGHT,
    CONV_BIAS,
    STEP_BIAS,
    DECAY_LOG,
    SKIP_GAIN,
    NORM_SSM,
    W_SSM_OUT,
    NORM_FFN,
    W_GATE,
    W_UP_PROJ,
    W_DOWN,
) = range(20)


epsilon = 1e-05
rope_base = 100000000000.0
masked_score = -1e30
highest = lax.Precision.HIGHEST
small_names = (
    NORM_ATTN,
    CONV_WEIGHT,
    CONV_BIAS,
    STEP_BIAS,
    DECAY_LOG,
    SKIP_GAIN,
    NORM_SSM,
    NORM_FFN,
)


def passed_along(value, axis, steps):
    count = lax.axis_size(axis)
    first, last = (max(0, -steps), min(count, count - steps))
    return lax.ppermute(value, axis, [(source, source + steps) for source in range(first, last)])


def prefix(value, axis, combine, identity):
    peers, place = (lax.axis_size(axis), lax.axis_index(axis))
    everything = jax.tree.map(
        lambda part, kind: lax.all_gather(part.astype(kind), axis),
        value,
        (jnp.bfloat16, jnp.bfloat16),
    )
    start = jax.tree.map(
        lambda part, zero: jnp.broadcast_to(jnp.asarray(zero, part.dtype), part.shape),
        value,
        identity,
    )

    def prefix_turn(k, before):
        reached = k < place
        new = combine(
            before, jax.tree.map(lambda part, own: part[k].astype(own.dtype), everything, value)
        )
        return jax.tree.map(lambda a, b: jnp.where(reached, a, b), new, before)

    return lax.fori_loop(0, peers, prefix_turn, start)


def carried_in(value, axis, combine, identity):
    peers, place = (lax.axis_size(axis), lax.axis_index(axis))
    everything = jax.tree.map(
        lambda part, kind: lax.all_gather(part.astype(kind), axis),
        value,
        jax.tree.map(lambda a: jnp.bfloat16 if a.dtype == jnp.float32 else a.dtype, value),
    )
    start = jax.tree.map(
        lambda part, zero: jnp.broadcast_to(jnp.asarray(zero, part.dtype), part.shape),
        value,
        identity,
    )

    def carried_turn(k, before):
        at = peers - 1 - k
        reached = at > place
        new = combine(
            before, jax.tree.map(lambda part, own: part[at].astype(own.dtype), everything, value)
        )
        return jax.tree.map(lambda a, b: jnp.where(reached, a, b), new, before)

    return lax.fori_loop(0, peers, carried_turn, start)


def layout():
    ssm_inner = SSM_HEADS * SSM_DIM
    channels = ssm_inner + 2 * STATE
    return [
        (NORM_ATTN, (D,)),
        (W_QUERY, (D, HEADS_Q * HEAD_DIM)),
        (W_KEY, (D, HEADS_KV * HEAD_DIM)),
        (W_VALUE, (D, HEADS_KV * HEAD_DIM)),
        (W_ATTN_OUT, (HEADS_Q * HEAD_DIM, D)),
        (W_GATE_SSM, (D, ssm_inner)),
        (W_X_SSM, (D, ssm_inner)),
        (W_B_C, (D, 2 * STATE)),
        (W_STEP, (D, SSM_HEADS)),
        (CONV_WEIGHT, (CONV, channels)),
        (CONV_BIAS, (channels,)),
        (STEP_BIAS, (SSM_HEADS,)),
        (DECAY_LOG, (SSM_HEADS,)),
        (SKIP_GAIN, (SSM_HEADS,)),
        (NORM_SSM, (ssm_inner,)),
        (W_SSM_OUT, (ssm_inner, D)),
        (NORM_FFN, (D,)),
        (W_GATE, (D, FF)),
        (W_UP_PROJ, (D, FF)),
        (W_DOWN, (FF, D)),
    ]


def unpack(flat_vector):
    unpacked = {}
    offset = 0
    for name_key, extent in layout():
        amount = math.prod(extent)
        unpacked[name_key] = flat_vector[offset : offset + amount].reshape(extent)
        offset += amount
    return unpacked


def matmul(left, right):
    return jnp.dot(left, right, preferred_element_type=jnp.float32)


def matmul_left_t(left, right):
    return lax.dot_general(
        left, right, (((0,), (0,)), ((), ())), preferred_element_type=jnp.float32
    )


def matmul_right_t(left, right):
    return lax.dot_general(
        left, right, (((1,), (1,)), ((), ())), preferred_element_type=jnp.float32
    )


def rms_norm(values, gain):
    return values * lax.rsqrt(jnp.mean(values * values, axis=-1, keepdims=True) + epsilon) * gain


def gated_norm(ssm_y, gate_ssm, gain):
    return rms_norm(ssm_y * jax.nn.silu(gate_ssm), gain)


def swiglu(gate_ffn, upper):
    return jax.nn.silu(gate_ffn) * upper


def sequence_info(row_index, bounds):
    starts = bounds[:-1]
    inside = row_index[:, None] >= starts[None, :]
    seq_id = jnp.sum(inside.astype(jnp.int32), axis=1) - 1
    seq_start = jnp.max(jnp.where(inside, starts[None, :], 0), axis=1)
    return (seq_id, row_index - seq_start)


def rotary_tables(positions):
    half_dim = HEAD_DIM // 2
    freqs = jnp.exp(
        -jnp.arange(half_dim, dtype=jnp.float32) * (2.0 * math.log(rope_base) / HEAD_DIM)
    )
    angles = freqs[:, None] * positions.astype(jnp.float32)[None, :]
    return (jnp.cos(angles), jnp.sin(angles))


def rotate(values, cosine, sine, heads):
    halves = values.reshape(heads, 2, HEAD_DIM // 2, -1)
    first_half, second_half = halves[:, 0], halves[:, 1]
    turned = jnp.stack(
        [first_half * cosine - second_half * sine, second_half * cosine + first_half * sine], axis=1
    )
    return turned.reshape(heads, HEAD_DIM, -1)


def add_rows(target, addend, first_row):
    current = lax.dynamic_slice_in_dim(target, first_row, addend.shape[0], 0)
    return lax.dynamic_update_slice_in_dim(target, current + addend, first_row, 0)


FAST = (4, 8)
LINE = 128
SHARD = 3082
SPAD = 3088
WIN = 3104
PLANE = 8 * SHARD
DEPTH = 4
TALL = {1: 1024, 2: 1024, 4: 512, 8: 256, 12: 128, 16: 128}
GRID = ("z", "y", "x", "c")
ZC = ("z", "c")
SWAP = [(0, 1), (1, 0)]


def zc_pairs(*pairs):
    return [(2 * a + c, 2 * b + c) for a, b, c in pairs]


def pinned(kernel, count, after):
    return lambda *refs: kernel(*refs[:count], *refs[count + len(after) :])


def pins(after):
    return [pl.BlockSpec(memory_space=pltpu.HBM)] * len(after)


class Flow:
    def __init__(self, stages):
        self.stages = stages
        self.sends = next(stages)
        self.result = None

    def values(self):
        return [value for value, _, _ in self.sends] or (list(self.result) if isinstance(self.result, list) else [self.result])

    def hold(self, after):
        held = fence(self.values(), after)
        self.sends = [(value, axis, pairs) for value, (_, axis, pairs) in zip(held, self.sends)]

    def go(self, after=()):
        arrived = [lax.ppermute(value, axis, pairs) for value, axis, pairs in self.sends]
        if after:
            arrived = fence(arrived, after)
        try:
            self.sends = self.stages.send(arrived)
        except StopIteration as stop:
            self.sends, self.result = [], stop.value
        return self


def fence(values, after):
    def kernel(*refs):
        del refs

    return pl.pallas_call(
        kernel,
        in_specs=pins(values) + pins(after),
        out_specs=pins(values),
        out_shape=[jax.ShapeDtypeStruct(value.shape, value.dtype) for value in values],
        input_output_aliases={k: k for k in range(len(values))},
        name="fence",
    )(*values, *after)


def bracket(call, flows):
    out = call([value for flow in flows for value in flow.values()])
    out = list(out) if isinstance(out, (list, tuple)) else [out]
    for flow in flows:
        flow.go()
    return fence(out, [v for flow in flows for v in flow.values()])


def gather_lines(params):
    z, y, x, c = (lax.axis_index(name) for name in GRID)
    lines = jnp.pad(params.reshape(SHARD, LINE), ((0, SPAD - SHARD), (0, 0)))
    sibling = lax.ppermute(lines, ZC, [(2 * k + 1 - k % 2, 2 * k + k % 2) for k in range(4)])
    buffers = []
    for part in range(2):
        here = jnp.where(c == part, lines, sibling)
        one = lax.ppermute(here, ZC, zc_pairs((0, 1, 0), (1, 2, 1)))
        side = lax.ppermute(here, ZC, zc_pairs((1, 0, 1)))
        two = lax.ppermute(one, ZC, zc_pairs((1, 2, 0), (2, 3, 1)))
        three = lax.ppermute(two, ZC, zc_pairs((2, 3, 0)))
        column = jnp.where(z == c, here, one + side + two + three)
        over_x = lax.ppermute(column, "x", SWAP)
        over_y = lax.ppermute(column, "y", SWAP)
        corner = lax.ppermute(over_y if part else over_x, "x" if part else "y", SWAP)
        local = [column, over_x, over_y, corner]
        buffers += [piece[None] for piece in local]
        buffers += [lax.ppermute(piece, "c", SWAP)[None] for piece in local]
    early = [(k, 0) for k in range(16)]
    here = jnp.where(c == 0, jnp.stack([lines, sibling]), jnp.stack([sibling, lines]))
    one = lax.ppermute(here, ZC, zc_pairs((2, 1, 0), (3, 2, 1)))
    side = lax.ppermute(here, ZC, zc_pairs((2, 3, 0)))
    two = lax.ppermute(one, ZC, zc_pairs((1, 0, 0), (2, 1, 1)))
    three = lax.ppermute(two, ZC, zc_pairs((1, 0, 1)))
    column = jnp.where(z == 2 + c, here, one + side + two + three)
    late = []
    for part in range(2):
        for first in (16, 21):
            late += [(first, part), (first + 1, part), (first + 2, part), (first + 3 + part, 0)]
    shard = np.arange(32)
    sz, sy, sx, sc = shard // 8, shard // 4 % 2, shard // 2 % 2, shard % 2
    away = jnp.where(sz % 2 == c, 0, 4)
    where = sc * 8 + away + 2 * (sy ^ y) + (sx ^ x) + 16 * (sz // 2)
    return buffers, Flow(spread_stages(column)), (early, early + late), where.astype(jnp.int32)


def spread_stages(column):
    over_x, over_y = yield [(column, "x", SWAP), (column, "y", SWAP)]
    corners = yield [(over_x[:1], "y", SWAP), (over_y[1:], "x", SWAP)]
    local = [column, over_x, over_y] + list(corners)
    return local + list((yield [(piece, "c", SWAP) for piece in local]))


def unpack_lines(buffers, slots, where, segments, after=()):
    jobs, starts = [], []
    reach = 0
    for offset, rows, columns in segments:
        per_row = columns // LINE
        lane, base = offset % LINE, offset // LINE
        if per_row == 1 and rows < 1024:
            lane, tall = 0, rows
        else:
            tall = TALL[per_row]
        starts.append(len(jobs))
        for k in range(rows // tall):
            jobs.append((base + k * tall * per_row, tall * per_row, 1 if lane else 0))
    window = max(job[1] for job in jobs) + 32
    table = np.zeros((len(jobs), 5), np.int32)
    for k, (line, count, extra) in enumerate(jobs):
        owner = line // SHARD
        inside = line - owner * SHARD
        begin = min(inside // 16 * 16, SPAD - window)
        crosses = int(line + count + extra > (owner + 1) * SHARD)
        table[k] = (owner, begin, begin - inside, crosses, (owner + 1) * SHARD - line)
    base_row = (int(-table[:, 2].min()) + 7) // 8 * 8
    table[:, 2] += base_row
    table[:, 4] += base_row
    room = int(max((table[:, 2] + window).max(), ((table[:, 4] + window) * table[:, 3]).max()))
    room = (room + 15) // 8 * 8
    total = len(jobs)
    count_buffers = len(buffers)
    shapes = []
    for offset, rows, columns in segments:
        per_row = columns // LINE
        tall = rows if per_row == 1 and rows < 1024 else TALL[per_row]
        shapes.append((rows, columns, tall, per_row, offset % LINE if tall != rows or per_row != 1 else 0))
    sizes = sorted({(tall, columns) for _, columns, tall, _, _ in shapes})

    def kernel(table_ref, where_ref, *refs):
        sources = refs[:count_buffers]
        outs = refs[count_buffers : count_buffers + len(segments)]
        rest = refs[count_buffers + len(segments) :]
        stages = dict(zip(sizes, rest))
        raw, flat, in_sem, out_sem = rest[len(sizes) :]
        step = pl.program_id(0)

        def fetch(job, slot):
            owner = table_ref[job, 0]
            begin = pl.multiple_of(table_ref[job, 1], 16)
            for b, (source, part) in enumerate(slots):

                @pl.when(where_ref[owner] == b)
                def _():
                    pltpu.make_async_copy(
                        sources[source].at[part, pl.ds(begin, window), :], raw.at[slot, 0], in_sem.at[slot, 0]
                    ).start()

            @pl.when(table_ref[job, 3] == 1)
            def _():
                for b, (source, part) in enumerate(slots):

                    @pl.when(where_ref[owner + 1] == b)
                    def _():
                        pltpu.make_async_copy(
                            sources[source].at[part, pl.ds(0, window), :], raw.at[slot, 1], in_sem.at[slot, 1]
                        ).start()

        def fetched(slot, half):
            return pltpu.make_async_copy(
                sources[0].at[0, pl.ds(0, window), :], raw.at[slot, half], in_sem.at[slot, half]
            )

        @pl.when(step == 0)
        def _():
            for k in range(min(DEPTH - 1, total)):
                fetch(k, k)

        @pl.when(step + DEPTH - 1 < total)
        def _():
            fetch(step + DEPTH - 1, lax.rem(step + DEPTH - 1, DEPTH))

        slot = lax.rem(step, DEPTH)
        fetched(slot, 0).wait()
        flat[pl.ds(table_ref[step, 2], window), :] = raw[slot, 0].astype(jnp.float32)

        @pl.when(table_ref[step, 3] == 1)
        def _():
            fetched(slot, 1).wait()
            flat[pl.ds(table_ref[step, 4], window), :] = raw[slot, 1].astype(jnp.float32)

        for index, (rows, columns, tall, per_row, lane) in enumerate(shapes):
            begin = starts[index]
            blocks = rows // tall
            stage = stages[(tall, columns)]

            @pl.when((step >= begin) & (step < begin + blocks))
            def _():
                block = step - begin
                side = lax.rem(block, DEPTH)

                def written(k, s):
                    return pltpu.make_async_copy(
                        stage.at[s],
                        outs[index].at[pl.ds(pl.multiple_of(k * tall, 16), tall), :],
                        out_sem.at[s],
                    )

                @pl.when(block >= DEPTH)
                def _():
                    written(block - DEPTH, side).wait()

                def tile(j):
                    picked = flat[pl.ds(base_row + j, tall, stride=per_row), :]
                    return pltpu.roll(picked, LINE - lane, 1) if lane else picked

                if lane:
                    lanes = lax.broadcasted_iota(jnp.int32, (tall, LINE), 1)
                    now = tile(0)
                    for j in range(per_row):
                        later = tile(j + 1)
                        stage[side, :, j * LINE : (j + 1) * LINE] = jnp.where(
                            lanes < LINE - lane, now, later
                        ).astype(jnp.bfloat16)
                        now = later
                else:
                    for j in range(per_row):
                        stage[side, :, j * LINE : (j + 1) * LINE] = tile(j).astype(jnp.bfloat16)
                written(block, side).start()

                @pl.when(block == blocks - 1)
                def _():
                    for back in reversed(range(min(DEPTH, blocks))):
                        written(block - back, lax.rem(block - back, DEPTH)).wait()

    return pl.pallas_call(
        pinned(kernel, 2 + count_buffers, after),
        grid_spec=pltpu.PrefetchScalarGridSpec(
            num_scalar_prefetch=2,
            grid=(total,),
            in_specs=[pl.BlockSpec(memory_space=pl.ANY)] * count_buffers + pins(after),
            out_specs=[pl.BlockSpec(memory_space=pl.ANY)] * len(segments),
            scratch_shapes=[pltpu.VMEM((DEPTH,) + size, jnp.bfloat16) for size in sizes]
            + [
                pltpu.VMEM((DEPTH, 2, window, LINE), jnp.bfloat16),
                pltpu.VMEM((room, LINE), jnp.float32),
                pltpu.SemaphoreType.DMA((DEPTH, 2)),
                pltpu.SemaphoreType.DMA((DEPTH,)),
            ],
        ),
        out_shape=[jax.ShapeDtypeStruct((rows, columns), jnp.bfloat16) for _, rows, columns in segments],
        compiler_params=pltpu.CompilerParams(vmem_limit_bytes=48 * 2**20),
        cost_estimate=pl.CostEstimate(flops=0, bytes_accessed=total * window * LINE * 4, transcendentals=0),
        name="unpack",
    )(jnp.asarray(table), where, *buffers, *after)


def pack_lines(target, target_rows, first_row, segments, lane, phase, extras, carry, tail_rows, after=()):
    tall = 256
    lefts, rights, plan = [], [], []
    left_of, right_of = {}, {}
    row = first_row
    begin = 0
    for left, right in segments:
        for value, seen, kept in ((left, left_of, lefts), (right, right_of, rights)):
            if id(value) not in seen:
                seen[id(value)] = len(kept)
                kept.append(value)
        blocks = left.shape[1] // tall
        plan.append((left_of[id(left)], right_of[id(right)], right.shape[1] // LINE, begin, blocks, row))
        begin += blocks
        row += left.shape[1] * right.shape[1] // LINE
    end_row = row
    total = begin
    biggest = max(entry[2] for entry in plan) * tall
    tokens = lefts[0].shape[0]
    count_left, count_right, count_extra = len(lefts), len(rights), len(extras)
    rolled = [jnp.roll(right, lane, axis=1) if lane else right for right in rights]
    carry_in = [carry] if lane else []
    targets = [] if target is None else [target]

    def left_spec(index):
        mine = [entry for entry in plan if entry[0] == index]

        def place(step):
            block = 0
            for _, _, _, start, blocks, _ in mine:
                block = jnp.where(step >= start, jnp.minimum(step - start, blocks - 1), block)
            return (0, block)

        return pl.BlockSpec((tokens, tall), place)

    def kernel(*refs):
        left_refs = refs[:count_left]
        right_refs = refs[count_left : count_left + count_right]
        at = count_left + count_right
        extra_refs = refs[at : at + count_extra]
        at += count_extra
        carry_refs = refs[at : at + len(carry_in)]
        at += len(carry_in) + len(targets)
        out = refs[at]
        flat, stage, shift, last, sems, extra_sems = refs[at + 1 :]
        step = pl.program_id(0)
        side = lax.rem(step, 2)

        def extra_copy(k):
            rows = extras[k][0].shape[0]
            return pltpu.make_async_copy(
                extra_refs[k], out.at[pl.ds(extras[k][1], rows), :], extra_sems.at[k]
            )

        @pl.when(step == 0)
        def _():
            for k in range(count_extra):
                extra_copy(k).start()
            if lane:
                shift[0:8, :] = carry_refs[0][...]
            if phase:
                flat[0:8, :] = jnp.zeros((8, LINE), jnp.float32)

        for left_at, right_at, per_row, start, blocks, row in plan:
            lines = per_row * tall

            def written(block, s, row=row, lines=lines):
                return pltpu.make_async_copy(
                    stage.at[s, pl.ds(0, lines), :],
                    out.at[pl.ds(pl.multiple_of(row + block * lines, 16), lines), :],
                    sems.at[s],
                )

            @pl.when((step >= start) & (step < start + blocks))
            def _():
                block = step - start
                if phase:

                    @pl.when(step > 0)
                    def _():
                        flat[0:8, :] = flat[lines : lines + 8, :]

                turned = left_refs[left_at][...].T
                lanes = lax.broadcasted_iota(jnp.int32, (tall, LINE), 1)
                for j0 in range(0, per_row, 2):
                    wide = min(2, per_row - j0)
                    tile = jnp.dot(
                        turned,
                        right_refs[right_at][:, j0 * LINE : (j0 + wide) * LINE],
                        preferred_element_type=jnp.float32,
                    )
                    for j in range(wide):
                        piece = tile[:, j * LINE : (j + 1) * LINE]
                        if lane and j0 + j == 0:
                            shift[8 : 8 + tall, :] = piece
                            piece = jnp.where(lanes < lane, shift[7 : 7 + tall, :], piece)
                            shift[0:8, :] = shift[tall : tall + 8, :]
                        if per_row == 1:
                            flat[phase : phase + tall, :] = piece
                        else:
                            flat[pl.ds(phase + j0 + j, tall, stride=per_row), :] = piece

                stage[side, 0:lines, :] = flat[0:lines, :].astype(jnp.bfloat16)
                written(block, side).start()

            @pl.when((step > start) & (step <= start + blocks))
            def _():
                written(step - start - 1, 1 - side).wait()

            if start + blocks == total:

                @pl.when(step == total - 1)
                def _():
                    written(blocks - 1, side).wait()

        @pl.when(step == total - 1)
        def _():
            if tail_rows:
                lanes = lax.broadcasted_iota(jnp.int32, (tail_rows, LINE), 1)
                rows_at = lax.broadcasted_iota(jnp.int32, (tail_rows, LINE), 0)
                final = jnp.broadcast_to(shift[7:8, :], (tail_rows, LINE))
                last[...] = jnp.where((rows_at == 0) & (lanes < lane), final, 0.0).astype(jnp.bfloat16)
                closing = pltpu.make_async_copy(
                    last, out.at[pl.ds(end_row, tail_rows), :], extra_sems.at[count_extra]
                )
                closing.start()
                closing.wait()
            for k in range(count_extra):
                extra_copy(k).wait()

    whole = [pl.BlockSpec(array.shape, lambda step: (0, 0)) for array in rolled]
    flops = sum(2 * tokens * entry[4] * tall * entry[2] * LINE for entry in plan)
    inputs = count_left + count_right + count_extra + len(carry_in) + len(targets)
    return pl.pallas_call(
        pinned(kernel, inputs, after),
        grid=(total,),
        in_specs=[left_spec(k) for k in range(count_left)]
        + whole
        + [pl.BlockSpec(array.shape, lambda step: (0, 0)) for array, _ in extras]
        + [pl.BlockSpec(array.shape, lambda step: (0, 0)) for array in carry_in]
        + [pl.BlockSpec(memory_space=pl.ANY)] * len(targets)
        + pins(after),
        out_specs=pl.BlockSpec(memory_space=pl.ANY),
        out_shape=jax.ShapeDtypeStruct((target_rows, LINE), jnp.bfloat16),
        scratch_shapes=[
            pltpu.VMEM((biggest + 16, LINE), jnp.float32),
            pltpu.VMEM((2, biggest, LINE), jnp.bfloat16),
            pltpu.VMEM((tall + 8, LINE), jnp.float32),
            pltpu.VMEM((max(tail_rows, 16), LINE), jnp.bfloat16),
            pltpu.SemaphoreType.DMA((2,)),
            pltpu.SemaphoreType.DMA((count_extra + 1,)),
        ],
        input_output_aliases={count_left + count_right + count_extra + len(carry_in): 0} if targets else {},
        compiler_params=pltpu.CompilerParams(vmem_limit_bytes=48 * 2**20),
        cost_estimate=pl.CostEstimate(flops=flops, bytes_accessed=total * biggest * LINE * 2, transcendentals=0),
        name="pack",
    )(*lefts, *rolled, *[array for array, _ in extras], *carry_in, *targets, *after)


def added(*parts):
    total = parts[0].astype(jnp.float32)
    for part in parts[1:]:
        total = total + part.astype(jnp.float32)
    return total.astype(jnp.bfloat16)


def reduce_stages(flat, batch, shift):
    z, y, x, c = (lax.axis_index(name) for name in GRID)
    length = PLANE + 32
    send = lax.dynamic_slice(flat, ((1 - c) * PLANE, 0), (length, LINE))
    (arrived,) = yield [(send, "c", SWAP)]
    chip = added(lax.dynamic_slice(flat, (c * PLANE, 0), (length, LINE)), arrived)

    def window(sy, sx, part):
        shard = sy * 4 + sx * 2 + part
        start = (shift + SHARD * shard) // 16 * 16
        return lax.dynamic_slice(chip, (start, 0), (WIN, LINE))

    away_0 = jnp.stack([window(1 - y, 0, 0), window(1 - y, 1, 0)])
    away_1 = jnp.stack([window(0, 1 - x, 1), window(1, 1 - x, 1)])
    home_0 = jnp.stack([window(y, 0, 0), window(y, 1, 0)])
    home_1 = jnp.stack([window(0, x, 1), window(1, x, 1)])
    got_0, got_1 = yield [(away_0, "y", SWAP), (away_1, "x", SWAP)]
    half_0, half_1 = added(home_0, got_0), added(home_1, got_1)
    pick = lambda value, at: lax.dynamic_index_in_dim(value, at, 0, keepdims=False)
    got_0, got_1 = yield [(pick(half_0, 1 - x), "x", SWAP), (pick(half_1, 1 - y), "y", SWAP)]
    columns = [added(pick(half_0, x), got_0), added(pick(half_1, y), got_1)]
    if batch == 0:
        hops = [((1, 0, 0), (2, 1, 1)), ((2, 0, 0), (3, 1, 1)), ((3, 0, 0), (0, 1, 1))]
    else:
        hops = [((1, 2, 0), (2, 3, 1)), ((0, 2, 0), (1, 3, 1)), ((3, 2, 0), (0, 3, 1))]
    if batch == 0:
        got = yield [(columns[0], ZC, zc_pairs(*hop)) for hop in hops]
        end = added(columns[0], *got)
        (column,) = fence(columns[1:], [end])
        got = yield [(column, ZC, zc_pairs(*hop)) for hop in hops]
        ends = [end, added(column, *got)]
    else:
        columns = jnp.stack(columns)
        got = yield [(columns, ZC, zc_pairs(*hop)) for hop in hops]
        ends = added(columns, *got)
    mine = jnp.where(c == 0, ends[0], ends[1])
    other = jnp.where(c == 0, ends[1], ends[0])
    (handed,) = yield [(other, ZC, [(2 * k + k % 2, 2 * k + 1 - k % 2) for k in range(4)])]
    return jnp.where(c == z % 2, mine, handed)


PIECE = 400


def corner_stages(flat):
    z, y, x, c = (lax.axis_index(name) for name in GRID)
    length = 8 * PIECE
    second = (8 + SHARD) // 16 * 16
    take = lambda at: lax.dynamic_slice(flat, (at * second, 0), (length, LINE))
    (arrived,) = yield [(take(1 - c), "c", SWAP)]
    chip = added(take(c), arrived).reshape(2, 2, 2, PIECE, LINE)
    pick = lambda value, at: lax.dynamic_index_in_dim(value, at, 0, keepdims=False)
    got = yield [(pick(chip[0], 1 - x), "x", SWAP), (pick(chip[1], 1 - y), "y", SWAP)]
    halves = [added(pick(chip[0], x), got[0]), added(pick(chip[1], y), got[1])]
    got = yield [(pick(halves[0], 1 - y), "y", SWAP), (pick(halves[1], 1 - x), "x", SWAP)]
    pieces = jnp.stack([added(pick(halves[0], y), got[0]), added(pick(halves[1], x), got[1])])
    got = yield [(pieces, "z", [(k, 0)]) for k in (1, 2, 3)]
    pieces = added(pieces, *got)
    got = yield [(pieces[0], "y", [(1, 0)]), (pieces[1], "x", [(1, 0)])]
    halves = [jnp.stack([pieces[0], got[0]]), jnp.stack([pieces[1], got[1]])]
    got = yield [(halves[0], "x", [(1, 0)]), (halves[1], "y", [(1, 0)])]
    return jnp.stack([halves[0], got[0], halves[1], got[1]]).reshape(length, LINE)


CHUNK = 128
NT = (((1,), (1,)), ((), ()))
TN = (((0,), (0,)), ((), ()))
INNER = SSM_HEADS * SSM_DIM
PAIRS = SSM_HEADS // 2


def spread(rows_a, rows_b):
    length = rows_a.shape[1]
    tall = jnp.concatenate(
        [jnp.broadcast_to(rows_a, (SSM_DIM, length)), jnp.broadcast_to(rows_b, (SSM_DIM, length))], axis=0
    )
    return tall.T


CHANNELS = INNER + 2 * STATE
LANES = 2 * SSM_DIM
COLUMNS = CHANNELS // LANES


def conv_masks(masks, start_ref, first, rows):
    place = first + lax.broadcasted_iota(jnp.int32, (rows, LANES), 0) - start_ref[...]
    for reach in range(1, CONV):
        masks[reach - 1] = jnp.where(place >= reach, 1.0, 0.0)


def conv_parts(ext, weight_ref, bias_ref, masks, rows):
    windows = []
    total = bias_ref[...]
    for tap in range(CONV):
        reach = CONV - 1 - tap
        window = ext[8 - reach : 8 - reach + rows, :]
        if reach:
            window = window * masks[reach - 1]
        windows.append(window)
        total = total + window * weight_ref[tap : tap + 1, :]
    return windows, total


def conv_forward(xbc, rim, weight, bias, meta, start_column, after=()):
    rows = xbc.shape[0]

    def kernel(meta_ref, x_ref, rim_ref, weight_ref, bias_ref, start_ref, out_ref, ext, masks):
        @pl.when(pl.program_id(0) == 0)
        def _():
            conv_masks(masks, start_ref, meta_ref[0], rows)

        ext[0:8, :] = rim_ref[...]
        ext[8:, :] = x_ref[...]
        _, total = conv_parts(ext, weight_ref, bias_ref, masks, rows)
        out_ref[...] = total * jax.nn.sigmoid(total)

    lanes = lambda i, m: (0, i)
    return pl.pallas_call(
        pinned(kernel, 6, after),
        grid_spec=pltpu.PrefetchScalarGridSpec(
            num_scalar_prefetch=1,
            grid=(COLUMNS,),
            in_specs=[
                pl.BlockSpec((rows, LANES), lanes),
                pl.BlockSpec((8, LANES), lanes),
                pl.BlockSpec((CONV, LANES), lanes),
                pl.BlockSpec((1, LANES), lanes),
                pl.BlockSpec((rows, 1), lambda i, m: (0, 0)),
            ] + pins(after),
            out_specs=pl.BlockSpec((rows, LANES), lanes),
            scratch_shapes=[
                pltpu.VMEM((rows + 8, LANES), jnp.float32),
                pltpu.VMEM((CONV - 1, rows, LANES), jnp.float32),
            ],
        ),
        out_shape=jax.ShapeDtypeStruct((rows, CHANNELS), jnp.float32),
        cost_estimate=pl.CostEstimate(flops=10**9, bytes_accessed=rows * CHANNELS * 8, transcendentals=0),
        name="conv",
    )(meta, xbc, rim, weight, bias, start_column, *after)


def conv_backward(dx, db, dc, xbc, rim, weight, bias, meta, start_column, after=()):
    rows = xbc.shape[0]

    def kernel(meta_ref, dx_ref, db_ref, dc_ref, x_ref, rim_ref, weight_ref, bias_ref, start_ref,
               low_ref, tail_ref, edge_ref, small_ref, ext, upper, masks):
        @pl.when(pl.program_id(0) == 0)
        def _():
            conv_masks(masks, start_ref, meta_ref[0], rows)
            upper[0:8, :] = jnp.zeros((8, LANES), jnp.float32)
            upper[8 + rows :, :] = jnp.zeros((8, LANES), jnp.float32)

        ext[0:8, :] = rim_ref[...]
        ext[8:, :] = x_ref[...]
        at = pl.program_id(0)
        arrived = jnp.where(at < PAIRS, dx_ref[...], jnp.where(at == PAIRS, db_ref[...], dc_ref[...]))
        windows, total = conv_parts(ext, weight_ref, bias_ref, masks, rows)
        gate = jax.nn.sigmoid(total)
        change = arrived * gate * (1.0 + total * (1.0 - gate))
        main = jnp.zeros((rows, LANES), jnp.float32)
        edge = jnp.zeros((8, LANES), jnp.float32)
        small_ref[...] = jnp.zeros((8, LANES), jnp.float32)
        small_ref[CONV : CONV + 1, :] = jnp.sum(change, axis=0, keepdims=True)
        for tap in range(CONV):
            reach = CONV - 1 - tap
            small_ref[tap : tap + 1, :] = jnp.sum(change * windows[tap], axis=0, keepdims=True)
            masked = change * masks[reach - 1] if reach else change
            upper[8 : 8 + rows, :] = masked * weight_ref[tap : tap + 1, :]
            main = main + upper[8 + reach : 8 + reach + rows, :]
            edge = edge + upper[reach : reach + 8, :]
        low_ref[...] = main.astype(jnp.bfloat16)
        tail_ref[...] = main[rows - 16 :, :]
        edge_ref[...] = edge

    lanes = lambda i, m: (0, i)
    whole = lambda i, m: (0, 0)
    return pl.pallas_call(
        pinned(kernel, 9, after),
        grid_spec=pltpu.PrefetchScalarGridSpec(
            num_scalar_prefetch=1,
            grid=(COLUMNS,),
            in_specs=[
                pl.BlockSpec((rows, LANES), lambda i, m: (0, jnp.minimum(i, PAIRS - 1))),
                pl.BlockSpec((rows, STATE), whole),
                pl.BlockSpec((rows, STATE), whole),
                pl.BlockSpec((rows, LANES), lanes),
                pl.BlockSpec((8, LANES), lanes),
                pl.BlockSpec((CONV, LANES), lanes),
                pl.BlockSpec((1, LANES), lanes),
                pl.BlockSpec((rows, 1), whole),
            ] + pins(after),
            out_specs=[
                pl.BlockSpec((rows, LANES), lanes),
                pl.BlockSpec((16, LANES), lanes),
                pl.BlockSpec((8, LANES), lanes),
                pl.BlockSpec((8, LANES), lanes),
            ],
            scratch_shapes=[
                pltpu.VMEM((rows + 8, LANES), jnp.float32),
                pltpu.VMEM((rows + 16, LANES), jnp.float32),
                pltpu.VMEM((CONV - 1, rows, LANES), jnp.float32),
            ],
        ),
        out_shape=[
            jax.ShapeDtypeStruct((rows, CHANNELS), jnp.bfloat16),
            jax.ShapeDtypeStruct((16, CHANNELS), jnp.float32),
            jax.ShapeDtypeStruct((8, CHANNELS), jnp.float32),
            jax.ShapeDtypeStruct((8, CHANNELS), jnp.float32),
        ],
        cost_estimate=pl.CostEstimate(flops=2 * 10**9, bytes_accessed=rows * CHANNELS * 10, transcendentals=0),
        name="conv_back",
    )(meta, dx, db, dc, xbc, rim, weight, bias, start_column, *after)


def weighted_state(left, left_block, values, weight_rows, after=()):
    rows = left.shape[0]

    def kernel(left_ref, value_ref, weight_ref, out_ref, turned):
        @pl.when(pl.program_id(0) == 0)
        def _():
            turned[...] = left_ref[...].T

        scaled = [(turned[...] * weight_ref[0, e : e + 1, :]).astype(jnp.bfloat16) for e in range(2)]
        both = jnp.dot(
            jnp.concatenate(scaled, axis=0), value_ref[...].astype(jnp.bfloat16), preferred_element_type=jnp.float32
        )
        low_lane = lax.broadcasted_iota(jnp.int32, (STATE, 2 * SSM_DIM), 1) < SSM_DIM
        out_ref[...] = jnp.where(low_lane, both[:STATE], both[STATE:])

    return pl.pallas_call(
        pinned(kernel, 3, after),
        grid=(PAIRS,),
        in_specs=[
            pl.BlockSpec((rows, STATE), lambda i: (0, left_block)),
            pl.BlockSpec((rows, 2 * SSM_DIM), lambda i: (0, i)),
            pl.BlockSpec((1, 2, rows), lambda i: (i, 0, 0)),
        ] + pins(after),
        out_specs=pl.BlockSpec((STATE, 2 * SSM_DIM), lambda i: (0, i)),
        out_shape=jax.ShapeDtypeStruct((STATE, INNER), jnp.float32),
        scratch_shapes=[pltpu.VMEM((STATE, rows), jnp.float32)],
        cost_estimate=pl.CostEstimate(flops=2 * rows * STATE * INNER, bytes_accessed=rows * INNER * 4, transcendentals=0),
        name="state",
    )(left, values, weight_rows.reshape(PAIRS, 2, rows), *after)


def chunk_rows(k, meta_ref, cum_ref, start_ref):
    here = slice(k * CHUNK, (k + 1) * CHUNK)
    first = meta_ref[0] + k * CHUNK
    index = first + lax.broadcasted_iota(jnp.int32, (1, CHUNK), 1)
    entering = start_ref[0:1, here] < first
    ending = index >= meta_ref[1 + k]
    cums, entries, tails = [], [], []
    for e in range(2):
        cum = cum_ref[0, e : e + 1, here]
        cums.append(cum)
        entries.append(jnp.where(entering, jnp.exp(cum), 0.0))
        gap = jnp.where(ending, cum[:, CHUNK - 1 :] - cum, masked_score)
        tails.append(jnp.exp(gap))
    return cums, entries, tails


def ssm_forward(conv, cum, step, state_in, skip, meta, start_column, start_row):
    rows = conv.shape[0]
    chunks = rows // CHUNK

    def kernel(meta_ref, x_ref, b_ref, c_ref, cum_ref, step_ref, state_ref, skip_ref, col_ref, row_ref,
               y_ref, inner, hide, state, b_turned):
        @pl.when(pl.program_id(0) == 0)
        def _():
            for k in range(chunks):
                here = slice(k * CHUNK, (k + 1) * CHUNK)
                b_turned[:, here] = b_ref[here, :].T.astype(jnp.bfloat16)
                inner[k] = lax.dot_general(
                    c_ref[here, :], b_ref[here, :], NT, precision=highest, preferred_element_type=jnp.float32
                )
                t = lax.broadcasted_iota(jnp.int32, (CHUNK, CHUNK), 0)
                s = lax.broadcasted_iota(jnp.int32, (CHUNK, CHUNK), 1)
                shown = (s <= t) & (meta_ref[0] + k * CHUNK + s >= col_ref[here, :])
                hide[k] = jnp.where(shown, 0.0, masked_score)

        low_lane = lax.broadcasted_iota(jnp.int32, (CHUNK, 2 * SSM_DIM), 1) < SSM_DIM
        state[...] = state_ref[...]
        for k in range(chunks):
            here = slice(k * CHUNK, (k + 1) * CHUNK)
            cums, entries, tails = chunk_rows(k, meta_ref, cum_ref, row_ref)
            x_now = x_ref[here, :]
            x_low = x_now.astype(jnp.bfloat16)
            entry = spread(*entries)
            weight = spread(*[tails[e] * step_ref[0, e : e + 1, here] for e in range(2)])
            parts = []
            for e in range(2):
                across = jnp.broadcast_to(cums[e], (CHUNK, CHUNK))
                decays = jnp.exp(across.T - across + hide[k])
                mix = (inner[k] * decays * step_ref[0, e : e + 1, here]).astype(jnp.bfloat16)
                parts.append(jnp.dot(mix, x_low, preferred_element_type=jnp.float32))
            carried = jnp.dot(
                c_ref[here, :].astype(jnp.bfloat16), state[...].astype(jnp.bfloat16),
                preferred_element_type=jnp.float32,
            )
            y_ref[here, :] = jnp.where(low_lane, parts[0], parts[1]) + entry * carried + skip_ref[...] * x_now
            fresh = jnp.dot(
                b_turned[:, here], (x_now * weight).astype(jnp.bfloat16), preferred_element_type=jnp.float32
            )
            state[...] = entry[CHUNK - 1 :, :] * state[...] + fresh

    whole = lambda i, m: (0, 0)
    lanes = lambda i, m: (0, i)
    return pl.pallas_call(
        kernel,
        grid_spec=pltpu.PrefetchScalarGridSpec(
            num_scalar_prefetch=1,
            grid=(PAIRS,),
            in_specs=[
                pl.BlockSpec((rows, 2 * SSM_DIM), lanes),
                pl.BlockSpec((rows, STATE), lambda i, m: (0, PAIRS)),
                pl.BlockSpec((rows, STATE), lambda i, m: (0, PAIRS + 1)),
                pl.BlockSpec((1, 2, rows), lambda i, m: (i, 0, 0)),
                pl.BlockSpec((1, 2, rows), lambda i, m: (i, 0, 0)),
                pl.BlockSpec((STATE, 2 * SSM_DIM), lanes),
                pl.BlockSpec((1, 2 * SSM_DIM), lanes),
                pl.BlockSpec((rows, 1), whole),
                pl.BlockSpec((8, rows), whole),
            ],
            out_specs=pl.BlockSpec((rows, 2 * SSM_DIM), lanes),
            scratch_shapes=[
                pltpu.VMEM((chunks, CHUNK, CHUNK), jnp.float32),
                pltpu.VMEM((chunks, CHUNK, CHUNK), jnp.float32),
                pltpu.VMEM((STATE, 2 * SSM_DIM), jnp.float32),
                pltpu.VMEM((STATE, rows), jnp.bfloat16),
            ],
        ),
        out_shape=jax.ShapeDtypeStruct((rows, INNER), jnp.float32),
        compiler_params=pltpu.CompilerParams(vmem_limit_bytes=40 * 2**20),
        cost_estimate=pl.CostEstimate(flops=10**9, bytes_accessed=rows * INNER * 8, transcendentals=2**21),
        name="ssm",
    )(meta, conv, conv, conv, cum.reshape(PAIRS, 2, rows), step.reshape(PAIRS, 2, rows), state_in, skip,
      start_column, start_row)


def ssm_backward(conv, dy, cum, step, state_in, state_grad, skip, meta, start_row, after=()):
    rows = conv.shape[0]
    chunks = rows // CHUNK

    def kernel(meta_ref, x_ref, dy_ref, b_ref, c_ref, cum_ref, step_ref, state_ref, grad_ref, skip_ref, row_ref,
               dx_ref, db_ref, dc_ref, small_ref, inner, hide, inner_grad, states, flow,
               b_turned, c_turned):
        low = lambda v: v.astype(jnp.bfloat16)
        dot = lambda p, q, dims=(((1,), (0,)), ((), ())): lax.dot_general(
            p, q, dims, preferred_element_type=jnp.float32
        )
        exact = lambda p, q, dims=(((1,), (0,)), ((), ())): lax.dot_general(
            p, q, dims, precision=highest, preferred_element_type=jnp.float32
        )
        s = lax.broadcasted_iota(jnp.int32, (CHUNK, CHUNK), 0)
        t = lax.broadcasted_iota(jnp.int32, (CHUNK, CHUNK), 1)

        @pl.when(pl.program_id(0) == 0)
        def _():
            db_ref[...] = jnp.zeros(db_ref.shape, jnp.float32)
            dc_ref[...] = jnp.zeros(dc_ref.shape, jnp.float32)
            inner_grad[...] = jnp.zeros(inner_grad.shape, jnp.float32)
            for k in range(chunks):
                here = slice(k * CHUNK, (k + 1) * CHUNK)
                b_turned[:, here] = low(b_ref[here, :].T)
                c_turned[:, here] = low(c_ref[here, :].T)
                inner[k] = exact(b_ref[here, :], c_ref[here, :], NT)
                shown = (s <= t) & (meta_ref[0] + k * CHUNK + s >= row_ref[0:1, here])
                hide[k] = jnp.where(shown, 0.0, masked_score)

        before = (s < t).astype(jnp.float32)
        until = low((s >= t).astype(jnp.float32))
        low_lane = t < SSM_DIM
        pick_row = lax.broadcasted_iota(jnp.int32, (8, 2 * SSM_DIM), 0)
        pick_lane = lax.broadcasted_iota(jnp.int32, (8, 2 * SSM_DIM), 1) // SSM_DIM
        pick = low((pick_row == pick_lane).astype(jnp.float32))
        spreads = []
        states[0] = state_ref[...]
        for k in range(chunks):
            here = slice(k * CHUNK, (k + 1) * CHUNK)
            cums, entries, tails = chunk_rows(k, meta_ref, cum_ref, row_ref)
            entry, tail = spread(*entries), spread(*tails)
            steps = spread(step_ref[0, 0:1, here], step_ref[0, 1:2, here])
            spreads.append((cums, entry, tail, steps))
            if k < chunks - 1:
                fresh = dot(b_turned[:, here], low(x_ref[here, :] * steps * tail))
                states[k + 1] = entry[CHUNK - 1 :, :] * states[k] + fresh
        flow[...] = grad_ref[...]
        skip_sum = jnp.zeros((1, 2 * SSM_DIM), jnp.float32)
        for k in reversed(range(chunks)):
            here = slice(k * CHUNK, (k + 1) * CHUNK)
            cums, entry, tail, steps = spreads[k]
            x_now, dy_now = x_ref[here, :], dy_ref[here, :]
            b_low, c_low = low(b_ref[here, :]), low(c_ref[here, :])
            scaled = x_now * steps
            dy_low = low(dy_now)
            flow_low, state_low = low(flow[...]), low(states[k])
            both = low(
                jnp.concatenate([jnp.where(low_lane, scaled, 0.0), jnp.where(low_lane, 0.0, scaled)], axis=0)
            )
            reached = dot(both, dy_low, NT)
            mixes, weighed = [], []
            for e in range(2):
                across = jnp.broadcast_to(cums[e], (CHUNK, CHUNK))
                decays = jnp.exp(across - across.T + hide[k])
                reach = decays * reached[e * CHUNK : (e + 1) * CHUNK]
                inner_grad[k] += reach
                weighed.append(low(inner[k] * reach))
                mixes.append(low(inner[k] * decays))
            sums = dot(jnp.concatenate(weighed, axis=0), until)
            within = [
                jnp.sum(sums[e * CHUNK : (e + 1) * CHUNK] * before, axis=0, keepdims=True) for e in range(2)
            ]
            mixed = dot(jnp.concatenate(mixes, axis=0), dy_low)
            back = tail * dot(b_low, flow_low)
            dxs = jnp.where(low_lane, mixed[:CHUNK], mixed[CHUNK:]) + back
            db_ref[here, :] += dot(low(scaled * tail), flow_low, NT)
            entered = low(dy_now * entry)
            dc_ref[here, :] += dot(entered, state_low, NT)
            brought = dy_now * entry * dot(c_low, state_low)
            ends = dot(pick, low(brought), NT)
            begins = dot(pick, low(scaled * back), NT)
            direct = dot(pick, low(x_now * dxs), NT)
            through = jnp.sum(flow[...] * states[k], axis=0, keepdims=True) * entry[CHUNK - 1 :, :]
            log_grad = exact(ends, until.astype(jnp.float32)) + exact(begins, before)
            for e in range(2):
                lanes = slice(e * SSM_DIM, (e + 1) * SSM_DIM)
                kept = jnp.sum(through[:, lanes], axis=1, keepdims=True)
                small_ref[0, e : e + 1, here] = direct[e : e + 1, :]
                small_ref[0, 2 + e : 3 + e, here] = log_grad[e : e + 1, :] + within[e] + kept
            dx_ref[here, :] = dxs * steps + skip_ref[...] * dy_now
            skip_sum += jnp.sum(x_now * dy_now, axis=0, keepdims=True)
            flow[...] = entry[CHUNK - 1 :, :] * flow[...] + dot(c_turned[:, here], entered)
        small_ref[0, 4:8, :] = jnp.zeros((4, rows), jnp.float32)
        small_ref[0, 4:5, 0 : 2 * SSM_DIM] = skip_sum

        @pl.when(pl.program_id(0) == PAIRS - 1)
        def _():
            for k in range(chunks):
                here = slice(k * CHUNK, (k + 1) * CHUNK)
                grads = low(inner_grad[k])
                db_ref[here, :] += dot(grads, low(c_ref[here, :]))
                dc_ref[here, :] += dot(grads, low(b_ref[here, :]), TN)

    whole = lambda i, m: (0, 0)
    lanes = lambda i, m: (0, i)
    pair = lambda i, m: (i, 0, 0)
    return pl.pallas_call(
        pinned(kernel, 11, after),
        grid_spec=pltpu.PrefetchScalarGridSpec(
            num_scalar_prefetch=1,
            grid=(PAIRS,),
            in_specs=[
                pl.BlockSpec((rows, 2 * SSM_DIM), lanes),
                pl.BlockSpec((rows, 2 * SSM_DIM), lanes),
                pl.BlockSpec((rows, STATE), lambda i, m: (0, PAIRS)),
                pl.BlockSpec((rows, STATE), lambda i, m: (0, PAIRS + 1)),
                pl.BlockSpec((1, 2, rows), pair),
                pl.BlockSpec((1, 2, rows), pair),
                pl.BlockSpec((STATE, 2 * SSM_DIM), lanes),
                pl.BlockSpec((STATE, 2 * SSM_DIM), lanes),
                pl.BlockSpec((1, 2 * SSM_DIM), lanes),
                pl.BlockSpec((8, rows), whole),
            ] + pins(after),
            out_specs=[
                pl.BlockSpec((rows, 2 * SSM_DIM), lanes),
                pl.BlockSpec((rows, STATE), whole),
                pl.BlockSpec((rows, STATE), whole),
                pl.BlockSpec((1, 8, rows), pair),
            ],
            scratch_shapes=[
                pltpu.VMEM((chunks, CHUNK, CHUNK), jnp.float32),
                pltpu.VMEM((chunks, CHUNK, CHUNK), jnp.float32),
                pltpu.VMEM((chunks, CHUNK, CHUNK), jnp.float32),
                pltpu.VMEM((chunks, STATE, 2 * SSM_DIM), jnp.float32),
                pltpu.VMEM((STATE, 2 * SSM_DIM), jnp.float32),
                pltpu.VMEM((STATE, rows), jnp.bfloat16),
                pltpu.VMEM((STATE, rows), jnp.bfloat16),
            ],
        ),
        out_shape=[
            jax.ShapeDtypeStruct((rows, INNER), jnp.float32),
            jax.ShapeDtypeStruct((rows, STATE), jnp.float32),
            jax.ShapeDtypeStruct((rows, STATE), jnp.float32),
            jax.ShapeDtypeStruct((PAIRS, 8, rows), jnp.float32),
        ],
        compiler_params=pltpu.CompilerParams(vmem_limit_bytes=40 * 2**20),
        cost_estimate=pl.CostEstimate(flops=3 * 10**9, bytes_accessed=rows * INNER * 12, transcendentals=2**21),
        name="ssm_back",
    )(meta, conv, dy, conv, conv, cum.reshape(PAIRS, 2, rows), step.reshape(PAIRS, 2, rows), state_in, state_grad,
      skip, start_row, *after)


def chain_states(earlier, later):
    return (earlier[0] * later[0], earlier[1] * later[0] + later[1])


def scan_states(carry, state, span, fast, backward):
    wide = jnp.repeat(carry, SSM_DIM)[None, :]
    if not fast:
        ident = (jnp.ones_like(wide), jnp.zeros_like(state))
        return (carried_in if backward else prefix)((wide, state), span, chain_states, ident)[1]
    flow = Flow(scan_stages(carry, state, backward))
    while flow.sends:
        flow.go()
    return flow.result


def scan_stages(carry, state, backward, extra=None):
    total = (jnp.repeat(carry, SSM_DIM)[None, :], state)
    start = None
    for name in ("c", "x", "y"):
        place = lax.axis_index(name)
        at = lax.broadcasted_iota(jnp.int32, (16, INNER), 0)
        block = jnp.where(at == 0, total[0], 0.0)
        if extra is not None:
            rest = jnp.pad(extra, (0, INNER - extra.shape[0]))[None, :]
            for place_at in range(1, 4):
                term = lax.reduce_precision(rest, 8, 7)
                block = jnp.where(at == place_at, term, block)
                rest = rest - term
        packed = jnp.concatenate([total[1].astype(jnp.bfloat16), block.astype(jnp.bfloat16)], axis=0)
        (packed,) = yield [(packed, name, SWAP)]
        packed = packed.astype(jnp.float32)
        other = (packed[STATE : STATE + 1], packed[:STATE])
        if extra is not None:
            extra = extra + jnp.sum(packed[STATE + 1 : STATE + 4, : extra.shape[0]], axis=0)
        leads = place == (0 if backward else 1)
        seen = (jnp.where(leads, other[0], 1.0), jnp.where(leads, other[1], 0.0))
        start = seen if start is None else chain_states(seen, start)
        if name != "y":
            forward = chain_states(other, total)
            reverse = chain_states(total, other)
            total = jax.tree.map(lambda p, q: jnp.where(leads, p, q), forward, reverse)
    return start[1] if extra is None else [start[1], extra]


KEYS = 512
PAIR = 2 * HEAD_DIM


def attention_forward(q_wide, kv, meta, starts, after=()):
    rows = q_wide.shape[2]
    blocks = kv.shape[0]
    ratio = HEADS_Q // HEADS_KV
    wide = min(512, rows)

    def kernel(meta_ref, q_ref, kv_ref, start_ref, o_ref, log_ref, top, total):
        b = pl.program_id(1)

        @pl.when(b == 0)
        def _():
            top[...] = jnp.full(top.shape, masked_score, jnp.float32)
            total[...] = jnp.zeros(total.shape, jnp.float32)
            o_ref[...] = jnp.zeros(o_ref.shape, jnp.float32)

        def block(partial):
            pair = kv_ref[0, 0]
            turned = pair.T[HEAD_DIM:, :]
            for h in range(ratio):
                for r in range(0, rows, wide):
                    here = slice(r, r + wide)
                    scores = jnp.dot(pair, q_ref[h, :, here], preferred_element_type=jnp.float32)
                    if partial:
                        keys = b * KEYS + lax.broadcasted_iota(jnp.int32, scores.shape, 0)
                        mine = meta_ref[2] + r + lax.broadcasted_iota(jnp.int32, scores.shape, 1)
                        visible = (keys >= start_ref[0:1, here]) & (keys <= mine)
                        scores = jnp.where(visible, scores, masked_score)
                    before = top[h, 0:1, here]
                    peak = jnp.maximum(before, jnp.max(scores, axis=0, keepdims=True))
                    part = jnp.exp(scores - peak)
                    if partial:
                        part = jnp.where(visible, part, 0.0)
                    fade = jnp.exp(before - peak)
                    top[h, 0:1, here] = peak
                    total[h, 0:1, here] = total[h, 0:1, here] * fade + jnp.sum(part, axis=0, keepdims=True)
                    o_ref[h, :, here] = o_ref[h, :, here] * fade + jnp.dot(
                        turned, part.astype(jnp.bfloat16), preferred_element_type=jnp.float32
                    )

        needed = (b >= meta_ref[0]) & (b < meta_ref[1])
        partial = ((b + 1) * KEYS > meta_ref[2]) | (b * KEYS < meta_ref[3])

        @pl.when(needed & partial)
        def _():
            block(True)

        @pl.when(needed & jnp.logical_not(partial))
        def _():
            block(False)

        @pl.when(b == blocks - 1)
        def _():
            for h in range(ratio):
                sums = total[h, 0:1, :]
                o_ref[h] = o_ref[h] / sums
                log_ref[h] = jnp.broadcast_to(top[h, 0:1, :] + jnp.log(sums), (8, rows))

    heads = lambda g, b, m: (g, 0, 0)
    return pl.pallas_call(
        pinned(kernel, 4, after),
        grid_spec=pltpu.PrefetchScalarGridSpec(
            num_scalar_prefetch=1,
            grid=(HEADS_KV, blocks),
            in_specs=[
                pl.BlockSpec((ratio, PAIR, rows), heads),
                pl.BlockSpec((1, 1, KEYS, PAIR), lambda g, b, m: (b, g, 0, 0)),
                pl.BlockSpec((8, rows), lambda g, b, m: (0, 0)),
            ] + pins(after),
            out_specs=[
                pl.BlockSpec((ratio, HEAD_DIM, rows), heads),
                pl.BlockSpec((ratio, 8, rows), heads),
            ],
            scratch_shapes=[
                pltpu.VMEM((ratio, 8, rows), jnp.float32),
                pltpu.VMEM((ratio, 8, rows), jnp.float32),
            ],
        ),
        out_shape=[
            jax.ShapeDtypeStruct((HEADS_Q, HEAD_DIM, rows), jnp.float32),
            jax.ShapeDtypeStruct((HEADS_Q, 8, rows), jnp.float32),
        ],
        compiler_params=pltpu.CompilerParams(vmem_limit_bytes=48 * 2**20),
        cost_estimate=pl.CostEstimate(flops=2 * 10**10, bytes_accessed=2**23, transcendentals=2**23),
        name="attend",
    )(meta, q_wide, kv, starts, *after)


def attention_backward(q_wide, g_wide, kv, logs, mixed, meta, starts, group, after=()):
    rows = q_wide.shape[2]
    blocks = kv.shape[0]
    ratio = HEADS_Q // HEADS_KV
    wide = min(512, rows)

    def kernel(meta_ref, q_ref, g_ref, kv_ref, log_ref, o_ref, start_ref, dkv_ref, dq_ref, delta, sums):
        b = pl.program_id(0)

        @pl.when(b == 0)
        def _():
            dq_ref[...] = jnp.zeros(dq_ref.shape, jnp.float32)
            for h in range(ratio):
                both = g_ref[h, HEAD_DIM:, :].astype(jnp.float32) * o_ref[h]
                delta[h] = jnp.broadcast_to(jnp.sum(both, axis=0, keepdims=True), (8, rows))

        def block(partial):
            pair = kv_ref[0, 0]
            turned = pair.T[:HEAD_DIM, :]
            for h in range(ratio):
                for r in range(0, rows, wide):
                    here = slice(r, r + wide)
                    q_now = q_ref[h, :, here]
                    g_now = g_ref[h, :, here]
                    scores = jnp.dot(pair, q_now, preferred_element_type=jnp.float32)
                    probs = jnp.exp(scores - log_ref[h, 0:1, here])
                    if partial:
                        keys = b * KEYS + lax.broadcasted_iota(jnp.int32, scores.shape, 0)
                        mine = meta_ref[2] + r + lax.broadcasted_iota(jnp.int32, scores.shape, 1)
                        visible = (keys >= start_ref[0:1, here]) & (keys <= mine)
                        probs = jnp.where(visible, probs, 0.0)
                    grads = jnp.dot(pair, g_now, preferred_element_type=jnp.float32)
                    low_grads = (probs * (grads - delta[h, 0:1, here])).astype(jnp.bfloat16)
                    change = lax.dot_general(
                        probs.astype(jnp.bfloat16), g_now, NT, preferred_element_type=jnp.float32
                    ) + lax.dot_general(low_grads, q_now, NT, preferred_element_type=jnp.float32)
                    if h == 0 and r == 0:
                        sums[...] = change
                    else:
                        sums[...] += change
                    dq_ref[h, :, here] += jnp.dot(turned, low_grads, preferred_element_type=jnp.float32)
            dkv_ref[0, 0] = sums[...].astype(jnp.bfloat16)

        needed = (b >= meta_ref[0]) & (b < meta_ref[1])
        partial = ((b + 1) * KEYS > meta_ref[2]) | (b * KEYS < meta_ref[3])

        @pl.when(needed & partial)
        def _():
            block(True)

        @pl.when(needed & jnp.logical_not(partial))
        def _():
            block(False)

        @pl.when(jnp.logical_not(needed))
        def _():
            dkv_ref[0, 0] = jnp.zeros((KEYS, PAIR), jnp.bfloat16)

    heads = lambda b, m: (group, 0, 0)
    return pl.pallas_call(
        pinned(kernel, 7, after),
        grid_spec=pltpu.PrefetchScalarGridSpec(
            num_scalar_prefetch=1,
            grid=(blocks,),
            in_specs=[
                pl.BlockSpec((ratio, PAIR, rows), heads),
                pl.BlockSpec((ratio, PAIR, rows), heads),
                pl.BlockSpec((1, 1, KEYS, PAIR), lambda b, m: (b, group, 0, 0)),
                pl.BlockSpec((ratio, 8, rows), heads),
                pl.BlockSpec((ratio, HEAD_DIM, rows), heads),
                pl.BlockSpec((8, rows), lambda b, m: (0, 0)),
            ] + pins(after),
            out_specs=[
                pl.BlockSpec((1, 1, KEYS, PAIR), lambda b, m: (b, 0, 0, 0)),
                pl.BlockSpec((ratio, HEAD_DIM, rows), lambda b, m: (0, 0, 0)),
            ],
            scratch_shapes=[
                pltpu.VMEM((ratio, 8, rows), jnp.float32),
                pltpu.VMEM((KEYS, PAIR), jnp.float32),
            ],
        ),
        out_shape=[
            jax.ShapeDtypeStruct((blocks, 1, KEYS, PAIR), jnp.bfloat16),
            jax.ShapeDtypeStruct((ratio, HEAD_DIM, rows), jnp.float32),
        ],
        compiler_params=pltpu.CompilerParams(vmem_limit_bytes=48 * 2**20),
        cost_estimate=pl.CostEstimate(flops=2 * 10**10, bytes_accessed=2**23, transcendentals=2**23),
        name="attend_back",
    )(meta, q_wide, g_wide, kv, logs, mixed, starts, *after)


def scatter_span(value, span, fast):
    if not fast:
        return lax.psum_scatter(value, span, scatter_dimension=0).astype(jnp.float32)
    flow = Flow(scatter_stages(value))
    while flow.sends:
        flow.go()
    return flow.result


def scatter_stages(value):
    _, y, x, c = (lax.axis_index(name) for name in GRID)
    value = value.reshape((2, 2, 2) + value.shape[1:])
    for name, place, axis in (("c", c, 2), ("y", y, 0), ("x", x, 0)):
        send = lax.dynamic_index_in_dim(value, 1 - place, axis, keepdims=False)
        (arrived,) = yield [(send, name, SWAP)]
        keep = lax.dynamic_index_in_dim(value, place, axis, keepdims=False)
        value = keep.astype(jnp.float32) + arrived.astype(jnp.float32)
        if name != "x":
            value = value.astype(jnp.bfloat16)
    return value


def plane_stages(value):
    for pairs in ([(0, 1), (1, 0), (2, 3), (3, 2)], [(0, 2), (2, 0), (1, 3), (3, 1)]):
        (other,) = yield [(value, "z", pairs)]
        value = value + other
    return value


def offsets_of():
    places, at = {}, 0
    for name_key, extent in layout():
        places[name_key] = (at, extent)
        at += math.prod(extent)
    return places


def early_weights(params):
    places = offsets_of()
    buffers, spread_flow, (slots, all_slots), where = gather_lines(params)
    spread_flow.go()
    names = (W_QUERY, W_KEY, W_VALUE, W_ATTN_OUT, W_GATE_SSM, W_X_SSM, W_B_C)
    misc_at = places[W_STEP][0]
    first = unpack_lines(
        buffers[:16], slots, where, [flat_segment(name_key) for name_key in names] + [(0, 16, LINE), (misc_at, 288, LINE)]
    )
    weights = dict(zip(names, first))
    weights[NORM_ATTN] = first[-2].reshape(-1)[:D]
    misc = first[-1].reshape(-1)
    for name_key in (W_STEP,) + small_names[1:-1]:
        at, extent = places[name_key]
        weights[name_key] = misc[at - misc_at : at - misc_at + math.prod(extent)].reshape(extent)
    return weights, spread_flow, (buffers, all_slots, where)


def flat_segment(name_key):
    at, extent = offsets_of()[name_key]
    return (at, extent[0], extent[1])


def late_weights(held, after):
    buffers, slots, where = held
    names = (W_SSM_OUT, W_GATE, W_UP_PROJ, W_DOWN)
    norm_at = offsets_of()[NORM_FFN][0]
    second = unpack_lines(
        buffers, slots, where, [flat_segment(name_key) for name_key in names] + [(norm_at, 16, LINE)], after
    )
    weights = dict(zip(names, second))
    weights[NORM_FFN] = second[-1].reshape(-1)[norm_at % LINE : norm_at % LINE + D]
    return weights


def pack_late(gate, up, down, ssm_low, grad_branch, grad_norm_ffn, after):
    places = offsets_of()
    out_at = places[W_SSM_OUT][0]
    lane = places[W_GATE][0] % LINE
    boundary = 2 * PLANE * LINE
    tail_from = (boundary - out_at) // D
    tail = matmul_left_t(ssm_low[:, tail_from:], grad_branch).reshape(-1)
    tail = tail[boundary - out_at - tail_from * D :]
    head = jnp.concatenate([jnp.zeros((14 * LINE,), jnp.float32), tail, grad_norm_ffn])
    head_rows = head.shape[0] // LINE
    carry = jnp.zeros((8, LINE), jnp.float32).at[7, :lane].set(head[head_rows * LINE :])
    head = head[: head_rows * LINE].reshape(head_rows, LINE).astype(jnp.bfloat16)
    return pack_lines(
        None, 2 * PLANE + 32, head_rows, [gate, up, down], lane, 0, [(head, 0)], carry, 48, after
    )


def pack_out(ssm_low, grad_branch, after):
    out_at = offsets_of()[W_SSM_OUT][0]
    first_row = (8 + out_at // LINE) // 16 * 16
    rows = first_row + SSM_HEADS * SSM_DIM * D // LINE
    return pack_lines(
        None, rows, first_row, [(ssm_low, grad_branch)], out_at % LINE, (8 + out_at // LINE) % 8, [],
        jnp.zeros((8, LINE), jnp.float32), 0, after,
    )


def pack_ssm(target, segments, small, ssm_low, grad_branch, after):
    places = offsets_of()
    misc = [small[name_key].reshape(-1) for name_key in (W_STEP,) + small_names[1:-1]]
    count = sum(part.shape[0] for part in misc)
    misc_rows = (count // LINE + 16) // 16 * 16
    opening = matmul_left_t(ssm_low[:, :16], grad_branch).reshape(-1)
    misc = jnp.concatenate(misc + [opening[: misc_rows * LINE - count]])
    misc = misc.reshape(misc_rows, LINE).astype(jnp.bfloat16)
    first_row = 8 + places[W_ATTN_OUT][0] // LINE
    return pack_lines(
        target, target.shape[0], first_row, segments, 0, 0, [(misc, 8 + places[W_STEP][0] // LINE)], None, 0, after
    )


def pack_qkv(segments, attended, grad_branch, grad_norm_attn, after):
    places = offsets_of()
    out_row = 8 + places[W_ATTN_OUT][0] // LINE
    rows = (8 + SHARD) // 16 * 16 + 8 * PIECE
    closing = matmul_left_t(attended[:, :16], grad_branch).reshape(-1, LINE)
    closing = closing[: rows - out_row].astype(jnp.bfloat16)
    opening = jnp.concatenate([jnp.zeros((8, LINE), jnp.float32), grad_norm_attn.reshape(-1, LINE)]).astype(jnp.bfloat16)
    return pack_lines(
        None, rows, 16, segments, 0, 0, [(opening, 0), (closing, out_row)], None, 0, after
    )


def own_lines(early, late, corner):
    z, y, x, c = (lax.axis_index(name) for name in GRID)
    place = 4 * y + 2 * x + c
    shard = SHARD * place
    start = jnp.where(z < 2, (8 + shard) % 16, (14 + shard) % 16)
    lines = jnp.where(z < 2, early, late)
    lines = jnp.where((z == 0) & (place < 2), corner[:WIN], lines)
    lines = lax.dynamic_slice(lines, (start, 0), (SHARD, LINE)).astype(jnp.float32)
    return lines.reshape(-1)


def body(span, group, fast, tokens, params, cotangent, offsets):
    rows_dev = tokens.shape[0]
    group_rows = rows_dev * lax.axis_size(span)
    all_rows = group_rows * lax.axis_size(group)
    ssm_inner = SSM_HEADS * SSM_DIM
    score_scale = HEAD_DIM ** (-0.5)
    bounds = offsets[0]
    my_start = lax.axis_index(span) * rows_dev
    row_index = my_start + jnp.arange(rows_dev, dtype=jnp.int32)
    seq_id, positions = sequence_info(row_index, bounds)
    first_start = row_index[0] - positions[0]
    last_row = my_start + rows_dev - 1
    cosine, sine = rotary_tables(positions)
    if fast:
        weights, spread_flow, held = early_weights(params)
    else:
        weights = unpack(lax.all_gather(params, group + span, axis=0, tiled=True))
    small_f32 = {name_key: weights[name_key].astype(jnp.float32) for name_key in small_names[:-1]}
    x_rows = tokens.astype(jnp.float32)
    normed_one, norm_one_back = jax.vjp(rms_norm, x_rows, small_f32[NORM_ATTN])
    hidden = normed_one.astype(jnp.bfloat16)
    across = lambda weight: lax.dot_general(
        weight, hidden, (((0,), (1,)), ((), ())), preferred_element_type=jnp.float32
    )
    q_rot = rotate(across(weights[W_QUERY]), cosine, sine, HEADS_Q).astype(jnp.bfloat16)
    k_rot = rotate(across(weights[W_KEY]), cosine, sine, HEADS_KV).astype(jnp.bfloat16)
    value_low = across(weights[W_VALUE]).astype(jnp.bfloat16).reshape(HEADS_KV, HEAD_DIM, rows_dev)
    kv_mine = jnp.concatenate([k_rot, value_low], axis=1).transpose(0, 2, 1)
    row_starts = row_index - positions
    kv_local = kv_mine.reshape(HEADS_KV, rows_dev, PAIR)
    xbc = jnp.concatenate(
        [matmul(hidden, weights[W_X_SSM]), matmul(hidden, weights[W_B_C])], axis=1
    )
    step_raw = matmul(hidden, weights[W_STEP])
    q_wide = jnp.pad(q_rot * jnp.bfloat16(score_scale), ((0, 0), (0, HEAD_DIM), (0, 0)))
    rim_source = xbc[rows_dev - 8 :]
    if fast:
        (rim_source,) = fence([rim_source], [q_wide])
    rim_rows = passed_along(rim_source, span, 1)
    ssm_meta = jnp.concatenate([my_start[None], row_starts[CHUNK - 1 :: CHUNK]]).astype(jnp.int32)
    conv_bias = small_f32[CONV_BIAS][None, :]
    convolve = lambda after: conv_forward(
        xbc, rim_rows, small_f32[CONV_WEIGHT], conv_bias, ssm_meta, row_starts[:, None], after
    )
    if fast:
        key_blocks = lax.all_gather(kv_local, span)
        conv_values = convolve(())
    else:
        conv_values = convolve(())
    step_in = step_raw.T + small_f32[STEP_BIAS][:, None]
    step_rows = jax.nn.softplus(step_in)
    decay = -jnp.exp(small_f32[DECAY_LOG])
    logs_step = step_rows * decay[:, None]
    order = jnp.arange(rows_dev)
    upto = (order[:, None] <= order[None, :]).astype(jnp.float32)
    cumul = jnp.dot(logs_step, upto, precision=highest)
    chunk_cum = jnp.dot(
        logs_step.reshape(-1, CHUNK), upto[:CHUNK, :CHUNK], precision=highest
    ).reshape(SSM_HEADS, rows_dev)
    went_on = row_starts < my_start
    entry_rows = jnp.where(went_on[None, :], jnp.exp(cumul), 0.0)
    in_last = row_index >= row_starts[rows_dev - 1]
    tail_rows = jnp.exp(jnp.where(in_last[None, :], cumul[:, -1:] - cumul, masked_score))
    carry_all = entry_rows[:, -1]
    summarize = lambda after: weighted_state(conv_values, PAIRS, conv_values, tail_rows * step_rows, after)
    meta = jnp.stack(
        [first_start // KEYS, last_row // KEYS + 1, my_start, row_starts[rows_dev - 1]]
    ).astype(jnp.int32)
    start_row = jnp.broadcast_to(row_starts[None, :], (8, rows_dev))
    if fast:
        (local_state,) = bracket(summarize, [spread_flow])
        scan = Flow(scan_stages(carry_all, local_state, False))
        (gate_in,) = fence([hidden], scan.values())
        gate_ssm = matmul(gate_in, weights[W_GATE_SSM])
        scan.go()
        (gate_ssm,) = fence([gate_ssm], scan.values())
        scan.go()
        mixed, logs = bracket(
            lambda after: attention_forward(
                q_wide, key_blocks, meta, start_row, (*after, gate_ssm, *spread_flow.values())
            ),
            [scan],
        )
        spread_flow.go()
        state_in = scan.result
    else:
        gate_ssm = matmul(hidden, weights[W_GATE_SSM])
        key_blocks = lax.all_gather(kv_local, span)
        if rows_dev != KEYS:
            key_blocks = key_blocks.transpose(1, 0, 2, 3).reshape(HEADS_KV, -1, KEYS, PAIR).transpose(1, 0, 2, 3)
        state_in = scan_states(carry_all, summarize(()), span, fast, False)
        mixed, logs = attention_forward(q_wide, key_blocks, meta, start_row)
    attended = mixed.astype(jnp.bfloat16).reshape(HEADS_Q * HEAD_DIM, rows_dev).T
    attn_out = matmul(attended, weights[W_ATTN_OUT])
    skip_wide = jnp.repeat(small_f32[SKIP_GAIN], SSM_DIM)[None, :]
    ssm_y = ssm_forward(
        conv_values, chunk_cum, step_rows, state_in, skip_wide, ssm_meta, row_starts[:, None], start_row
    )
    normed_ssm, gnorm_back = jax.vjp(gated_norm, ssm_y, gate_ssm, small_f32[NORM_SSM])
    ssm_low = normed_ssm.astype(jnp.bfloat16)
    if fast:
        held = (held[0] + spread_flow.result,) + held[1:]
        weights.update(late_weights(held, [ssm_y]))
    small_f32[NORM_FFN] = weights[NORM_FFN].astype(jnp.float32)
    ssm_out = matmul(ssm_low, weights[W_SSM_OUT])
    middle = x_rows + attn_out + ssm_out
    normed_two, norm_two_back = jax.vjp(rms_norm, middle, small_f32[NORM_FFN])
    hidden_two = normed_two.astype(jnp.bfloat16)
    gate_ffn = matmul(hidden_two, weights[W_GATE])
    upper = matmul(hidden_two, weights[W_UP_PROJ])
    activation_f32, swiglu_back = jax.vjp(swiglu, gate_ffn, upper)
    activation = activation_f32.astype(jnp.bfloat16)
    ffn_out = matmul(activation, weights[W_DOWN])
    result = middle + ffn_out
    squares = jnp.stack(
        [
            jnp.sum(result * result),
            jnp.sum(attn_out * attn_out),
            jnp.sum(ssm_out * ssm_out),
            jnp.sum(ffn_out * ffn_out),
        ]
    )
    grad_out = cotangent.astype(jnp.float32)
    grad_activation = matmul_right_t(cotangent, weights[W_DOWN])
    grad_gate_f32, grad_upper_f32 = swiglu_back(grad_activation)
    grad_gate = grad_gate_f32.astype(jnp.bfloat16)
    grad_upper = grad_upper_f32.astype(jnp.bfloat16)
    grad_hidden_two = matmul_right_t(grad_gate, weights[W_GATE]) + matmul_right_t(
        grad_upper, weights[W_UP_PROJ]
    )
    grad_middle_norm, grad_norm_ffn = norm_two_back(grad_hidden_two)
    grad_middle = grad_out + grad_middle_norm
    grad_branch = grad_middle.astype(jnp.bfloat16)
    grad_attended = matmul_right_t(weights[W_ATTN_OUT], grad_branch).astype(jnp.bfloat16)
    grad_ssm_low = matmul_right_t(grad_branch, weights[W_SSM_OUT])
    grad_ssm_y, grad_gate_ssm_f32, grad_norm_ssm = gnorm_back(grad_ssm_low)
    grad_state_local = weighted_state(conv_values, PAIRS + 1, grad_ssm_y, entry_rows)
    if fast:
        scan = Flow(scan_stages(carry_all, grad_state_local, True, squares)).go()
        (late,) = bracket(
            lambda after: pack_late(
                (hidden_two, grad_gate), (hidden_two, grad_upper), (activation, cotangent),
                ssm_low, grad_branch, grad_norm_ffn, after,
            ),
            [scan],
        )
        late_flow = Flow(reduce_stages(late, 1, 14))
        (grad_branch_low,) = fence([grad_branch], scan.values() + late_flow.values())
        early = pack_out(ssm_low, grad_branch_low, ())
        scan.go()
        grad_state_out, squares = scan.result
        (early,) = fence([early], [grad_state_out])
        late_flow.go()
        (early,) = fence([early], late_flow.values())
        around = lambda call: bracket(call, [late_flow])
    else:
        grad_state_out = scan_states(carry_all, grad_state_local, span, fast, True)
        around = lambda call: call(())
    grad_x, grad_b, grad_c, grad_small = around(
        lambda after: ssm_backward(
            conv_values, grad_ssm_y, chunk_cum, step_rows, state_in, grad_state_out, skip_wide, ssm_meta, start_row,
            after,
        )
    )
    grad_direct = grad_small[:, 0:2].reshape(SSM_HEADS, rows_dev)
    grad_logs = grad_small[:, 2:4].reshape(SSM_HEADS, rows_dev)
    grad_decay_log = decay * jnp.sum(step_rows * grad_logs, axis=1)
    grad_step_rows = (grad_direct + decay[:, None] * grad_logs) * jax.nn.sigmoid(step_in)
    grad_step_bias = jnp.sum(grad_step_rows, axis=1)
    grad_step_raw_f32 = grad_step_rows.T
    grad_skip_gain = jnp.sum(grad_small[:, 4, : 2 * SSM_DIM].reshape(SSM_HEADS, SSM_DIM), axis=1)
    grad_main, grad_tail, grad_edge, grad_taps = around(
        lambda after: conv_backward(
            grad_x, grad_b, grad_c, xbc, rim_rows, small_f32[CONV_WEIGHT], conv_bias, ssm_meta,
            row_starts[:, None], after,
        )
    )
    grad_conv_weight = grad_taps[:CONV]
    grad_conv_bias = grad_taps[CONV]
    rim_back = passed_along(grad_edge, span, -1)
    grad_tail = grad_tail + jnp.pad(rim_back, ((8, 0), (0, 0)))
    grad_xbc = lax.dynamic_update_slice(grad_main, grad_tail.astype(jnp.bfloat16), (rows_dev - 16, 0))
    grad_gate_ssm = grad_gate_ssm_f32.astype(jnp.bfloat16)
    grad_step_raw = grad_step_raw_f32.astype(jnp.bfloat16)
    grad_w_step = matmul_left_t(hidden, grad_step_raw)
    grad_hidden_ssm = (
        matmul_right_t(grad_gate_ssm, weights[W_GATE_SSM])
        + matmul_right_t(grad_xbc[:, :ssm_inner], weights[W_X_SSM])
        + matmul_right_t(grad_xbc[:, ssm_inner:], weights[W_B_C])
        + matmul_right_t(grad_step_raw, weights[W_STEP])
    )
    small = {
        W_STEP: grad_w_step,
        CONV_WEIGHT: grad_conv_weight,
        CONV_BIAS: grad_conv_bias,
        STEP_BIAS: grad_step_bias,
        DECAY_LOG: grad_decay_log,
        SKIP_GAIN: grad_skip_gain,
        NORM_SSM: grad_norm_ssm,
        NORM_FFN: grad_norm_ffn,
    }
    parts = []
    if fast:
        early = pack_ssm(
            early,
            [
                (attended, grad_branch), (hidden, grad_gate_ssm),
                (hidden, grad_xbc[:, :ssm_inner]), (hidden, grad_xbc[:, ssm_inner:]),
            ],
            small, ssm_low, grad_branch, late_flow.values(),
        )
        early_flow = Flow(reduce_stages(early, 0, 8))
        (grad_attended,) = fence([grad_attended], early_flow.values() + late_flow.values())
        around = lambda call: bracket(call, [early_flow])
    g_wide = jnp.pad(grad_attended.reshape(HEADS_Q, HEAD_DIM, rows_dev), ((0, 0), (HEAD_DIM, 0), (0, 0)))
    if fast:
        early_flow.go()
        (g_wide,) = fence([g_wide], early_flow.values())
    for group_at in range(HEADS_KV):
        after_part = [part[1] for part in parts]
        if fast and group_at == 0:
            after_part = late_flow.values()
        parts.append(
            around(
                lambda after: attention_backward(
                    q_wide, g_wide, key_blocks, logs, mixed, meta, start_row, group_at, (*after, *after_part)
                )
            )
        )
    grad_kv = jnp.concatenate([part[0] for part in parts], axis=1)
    grad_q_turned = jnp.concatenate([part[1] for part in parts], axis=0)
    if rows_dev != KEYS:
        grad_kv = grad_kv.transpose(1, 0, 2, 3).reshape(HEADS_KV, -1, rows_dev, PAIR).transpose(1, 0, 2, 3)
    if fast:
        late_flow.go([parts[-1][1]])
        scatter = Flow(scatter_stages(grad_kv))
        (grad_q_turned,) = fence([grad_q_turned], scatter.values() + early_flow.values() + late_flow.values())
    turned_back = rotate(grad_q_turned * score_scale, cosine, -sine, HEADS_Q).astype(jnp.bfloat16)
    grad_query_low = turned_back.reshape(HEADS_Q * HEAD_DIM, rows_dev).T
    if fast:
        scatter.go()
        early_flow.go()
        (grad_query_low,) = fence([grad_query_low], scatter.values() + early_flow.values())
    grad_hidden = grad_hidden_ssm + matmul_right_t(grad_query_low, weights[W_QUERY])
    if fast:
        scatter.go()
        (grad_hidden,) = fence([grad_hidden], scatter.values())
        scatter.go()
        grad_kv_mine = scatter.result
    else:
        grad_kv_mine = scatter_span(grad_kv, span, fast)
    grad_kv_mine = grad_kv_mine.transpose(0, 2, 1)
    grad_key_low = rotate(grad_kv_mine[:, :HEAD_DIM], cosine, -sine, HEADS_KV).astype(jnp.bfloat16)
    grad_key_low = grad_key_low.reshape(HEADS_KV * HEAD_DIM, rows_dev).T
    grad_value_low = grad_kv_mine[:, HEAD_DIM:].astype(jnp.bfloat16).reshape(HEADS_KV * HEAD_DIM, rows_dev).T
    grad_hidden = (
        grad_hidden
        + matmul_right_t(grad_key_low, weights[W_KEY])
        + matmul_right_t(grad_value_low, weights[W_VALUE])
    )
    grad_x_norm, grad_norm_attn = norm_one_back(grad_hidden)
    grad_tokens = grad_middle + grad_x_norm
    if fast:
        corner = pack_qkv(
            [(hidden, grad_query_low), (hidden, grad_key_low), (hidden, grad_value_low)],
            attended, grad_branch, grad_norm_attn, early_flow.values(),
        )
        corner_flow = Flow(corner_stages(corner))
        for _ in range(3):
            corner_flow.go()
        early_flow.go()
        ((pieces, _, _), *_) = corner_flow.sends
        (pieces,) = fence([pieces], early_flow.values())
        corner_flow.sends = [(pieces, axis, pairs) for _, axis, pairs in corner_flow.sends]
        stats_flow = Flow(plane_stages(squares))
        stats_flow.hold([pieces])
        for flow in (early_flow, late_flow, corner_flow, stats_flow):
            while flow.sends:
                flow.go()
        stats = jnp.sqrt(stats_flow.result / (all_rows * D))
        grad_shard = own_lines(early_flow.result, late_flow.result, corner_flow.result)
        return (result.astype(jnp.bfloat16), grad_tokens, grad_shard, stats)
    small[NORM_ATTN] = grad_norm_attn
    stats = jnp.sqrt(lax.psum(squares, group + span) / (all_rows * D))
    pairs = {
        W_QUERY: (hidden, grad_query_low),
        W_KEY: (hidden, grad_key_low),
        W_VALUE: (hidden, grad_value_low),
        W_ATTN_OUT: (attended, grad_branch),
        W_GATE_SSM: (hidden, grad_gate_ssm),
        W_X_SSM: (hidden, grad_xbc[:, :ssm_inner]),
        W_B_C: (hidden, grad_xbc[:, ssm_inner:]),
        W_SSM_OUT: (ssm_low, grad_branch),
        W_GATE: (hidden_two, grad_gate),
        W_UP_PROJ: (hidden_two, grad_upper),
        W_DOWN: (activation, cotangent),
    }
    grad_dict = dict(small)
    for name_key, (left, right) in pairs.items():
        grad_dict[name_key] = matmul_left_t(left, right)
    flat_parts = [grad_dict[name_key].reshape(-1) for name_key, extent in layout()]
    used_entries = 0
    for part_array in flat_parts:
        used_entries += part_array.shape[0]
    flat_parts.append(jnp.zeros((params.shape[0] * lax.axis_size(group + span) - used_entries,), jnp.float32))
    grad_shard = lax.psum_scatter(
        jnp.concatenate(flat_parts), group + span, scatter_dimension=0, tiled=True
    )
    return (result.astype(jnp.bfloat16), grad_tokens, grad_shard, stats)


def solution(mesh):
    fast = (mesh.shape["group"], mesh.shape["span"]) == FAST
    if fast:
        mesh = Mesh(mesh.devices.reshape(4, 2, 2, 2), GRID)
        group, span = (GRID[:1], GRID[1:])
    else:
        group, span = (("group",), ("span",))

    def program(tokens, params, cotangent, offsets):
        return body(span, group, fast, tokens, params, cotangent, offsets)

    return jax.shard_map(
        program,
        mesh=mesh,
        in_specs=(P(group + span, None), P(group + span), P(group + span, None), P(group, None)),
        out_specs=(P(group + span, None), P(group + span, None), P(group + span), P()),
        check_vma=False,
    )
```

```python
import math

import jax
import jax.numpy as jnp
import numpy as np
from jax import lax
from jax.experimental import pallas as pl
from jax.experimental.pallas import tpu as pltpu
from jax.sharding import Mesh, PartitionSpec as P

D = 1024
HEADS_Q = 8
HEADS_KV = 2
HEAD_DIM = 64
SSM_HEADS = 24
SSM_DIM = 64
STATE = 128
CONV = 4
FF = 2048
(
    NORM_ATTN,
    W_QUERY,
    W_KEY,
    W_VALUE,
    W_ATTN_OUT,
    W_GATE_SSM,
    W_X_SSM,
    W_B_C,
    W_STEP,
    CONV_WEIGHT,
    CONV_BIAS,
    STEP_BIAS,
    DECAY_LOG,
    SKIP_GAIN,
    NORM_SSM,
    W_SSM_OUT,
    NORM_FFN,
    W_GATE,
    W_UP_PROJ,
    W_DOWN,
) = range(20)


epsilon = 1e-05
rope_base = 100000000000.0
masked_score = -1e30
highest = lax.Precision.HIGHEST
small_names = (
    NORM_ATTN,
    CONV_WEIGHT,
    CONV_BIAS,
    STEP_BIAS,
    DECAY_LOG,
    SKIP_GAIN,
    NORM_SSM,
    NORM_FFN,
)


def passed_along(value, axis, steps):
    count = lax.axis_size(axis)
    first, last = (max(0, -steps), min(count, count - steps))
    return lax.ppermute(value, axis, [(source, source + steps) for source in range(first, last)])


def prefix(value, axis, combine, identity):
    peers, place = (lax.axis_size(axis), lax.axis_index(axis))
    everything = jax.tree.map(
        lambda part, kind: lax.all_gather(part.astype(kind), axis),
        value,
        (jnp.bfloat16, jnp.bfloat16),
    )
    start = jax.tree.map(
        lambda part, zero: jnp.broadcast_to(jnp.asarray(zero, part.dtype), part.shape),
        value,
        identity,
    )

    def prefix_turn(k, before):
        reached = k < place
        new = combine(
            before, jax.tree.map(lambda part, own: part[k].astype(own.dtype), everything, value)
        )
        return jax.tree.map(lambda a, b: jnp.where(reached, a, b), new, before)

    return lax.fori_loop(0, peers, prefix_turn, start)


def carried_in(value, axis, combine, identity):
    peers, place = (lax.axis_size(axis), lax.axis_index(axis))
    everything = jax.tree.map(
        lambda part, kind: lax.all_gather(part.astype(kind), axis),
        value,
        jax.tree.map(lambda a: jnp.bfloat16 if a.dtype == jnp.float32 else a.dtype, value),
    )
    start = jax.tree.map(
        lambda part, zero: jnp.broadcast_to(jnp.asarray(zero, part.dtype), part.shape),
        value,
        identity,
    )

    def carried_turn(k, before):
        at = peers - 1 - k
        reached = at > place
        new = combine(
            before, jax.tree.map(lambda part, own: part[at].astype(own.dtype), everything, value)
        )
        return jax.tree.map(lambda a, b: jnp.where(reached, a, b), new, before)

    return lax.fori_loop(0, peers, carried_turn, start)


def layout():
    ssm_inner = SSM_HEADS * SSM_DIM
    channels = ssm_inner + 2 * STATE
    return [
        (NORM_ATTN, (D,)),
        (W_QUERY, (D, HEADS_Q * HEAD_DIM)),
        (W_KEY, (D, HEADS_KV * HEAD_DIM)),
        (W_VALUE, (D, HEADS_KV * HEAD_DIM)),
        (W_ATTN_OUT, (HEADS_Q * HEAD_DIM, D)),
        (W_GATE_SSM, (D, ssm_inner)),
        (W_X_SSM, (D, ssm_inner)),
        (W_B_C, (D, 2 * STATE)),
        (W_STEP, (D, SSM_HEADS)),
        (CONV_WEIGHT, (CONV, channels)),
        (CONV_BIAS, (channels,)),
        (STEP_BIAS, (SSM_HEADS,)),
        (DECAY_LOG, (SSM_HEADS,)),
        (SKIP_GAIN, (SSM_HEADS,)),
        (NORM_SSM, (ssm_inner,)),
        (W_SSM_OUT, (ssm_inner, D)),
        (NORM_FFN, (D,)),
        (W_GATE, (D, FF)),
        (W_UP_PROJ, (D, FF)),
        (W_DOWN, (FF, D)),
    ]


def unpack(flat_vector):
    unpacked = {}
    offset = 0
    for name_key, extent in layout():
        amount = math.prod(extent)
        unpacked[name_key] = flat_vector[offset : offset + amount].reshape(extent)
        offset += amount
    return unpacked


def matmul(left, right):
    return jnp.dot(left, right, preferred_element_type=jnp.float32)


def matmul_left_t(left, right):
    return lax.dot_general(
        left, right, (((0,), (0,)), ((), ())), preferred_element_type=jnp.float32
    )


def matmul_right_t(left, right):
    return lax.dot_general(
        left, right, (((1,), (1,)), ((), ())), preferred_element_type=jnp.float32
    )


def rms_norm(values, gain):
    return values * lax.rsqrt(jnp.mean(values * values, axis=-1, keepdims=True) + epsilon) * gain


def gated_norm(ssm_y, gate_ssm, gain):
    return rms_norm(ssm_y * jax.nn.silu(gate_ssm), gain)


def swiglu(gate_ffn, upper):
    return jax.nn.silu(gate_ffn) * upper


def sequence_info(row_index, bounds):
    starts = bounds[:-1]
    inside = row_index[:, None] >= starts[None, :]
    seq_id = jnp.sum(inside.astype(jnp.int32), axis=1) - 1
    seq_start = jnp.max(jnp.where(inside, starts[None, :], 0), axis=1)
    return (seq_id, row_index - seq_start)


def rotary_tables(positions):
    half_dim = HEAD_DIM // 2
    freqs = jnp.exp(
        -jnp.arange(half_dim, dtype=jnp.float32) * (2.0 * math.log(rope_base) / HEAD_DIM)
    )
    angles = freqs[:, None] * positions.astype(jnp.float32)[None, :]
    return (jnp.cos(angles), jnp.sin(angles))


def rotate(values, cosine, sine, heads):
    halves = values.reshape(heads, 2, HEAD_DIM // 2, -1)
    first_half, second_half = halves[:, 0], halves[:, 1]
    turned = jnp.stack(
        [first_half * cosine - second_half * sine, second_half * cosine + first_half * sine], axis=1
    )
    return turned.reshape(heads, HEAD_DIM, -1)


def add_rows(target, addend, first_row):
    current = lax.dynamic_slice_in_dim(target, first_row, addend.shape[0], 0)
    return lax.dynamic_update_slice_in_dim(target, current + addend, first_row, 0)


FAST = (4, 8)
LINE = 128
SHARD = 3082
SPAD = 3088
WIN = 3104
PLANE = 8 * SHARD
DEPTH = 4
TALL = {1: 1024, 2: 1024, 4: 512, 8: 256, 12: 128, 16: 128}
GRID = ("z", "y", "x", "c")
ZC = ("z", "c")
SWAP = [(0, 1), (1, 0)]


def zc_pairs(*pairs):
    return [(2 * a + c, 2 * b + c) for a, b, c in pairs]


def pinned(kernel, count, after):
    return lambda *refs: kernel(*refs[:count], *refs[count + len(after) :])


def pins(after):
    return [pl.BlockSpec(memory_space=pltpu.HBM)] * len(after)


class Flow:
    def __init__(self, stages):
        self.stages = stages
        self.sends = next(stages)
        self.result = None

    def values(self):
        return [value for value, _, _ in self.sends] or (list(self.result) if isinstance(self.result, list) else [self.result])

    def hold(self, after):
        held = fence(self.values(), after)
        self.sends = [(value, axis, pairs) for value, (_, axis, pairs) in zip(held, self.sends)]

    def go(self, after=()):
        arrived = [lax.ppermute(value, axis, pairs) for value, axis, pairs in self.sends]
        if after:
            arrived = fence(arrived, after)
        try:
            self.sends = self.stages.send(arrived)
        except StopIteration as stop:
            self.sends, self.result = [], stop.value
        return self


def fence(values, after):
    def kernel(*refs):
        del refs

    return pl.pallas_call(
        kernel,
        in_specs=pins(values) + pins(after),
        out_specs=pins(values),
        out_shape=[jax.ShapeDtypeStruct(value.shape, value.dtype) for value in values],
        input_output_aliases={k: k for k in range(len(values))},
        name="fence",
    )(*values, *after)


def bracket(call, flows):
    out = call([value for flow in flows for value in flow.values()])
    out = list(out) if isinstance(out, (list, tuple)) else [out]
    for flow in flows:
        flow.go()
    return fence(out, [v for flow in flows for v in flow.values()])


def gather_lines(params):
    z, y, x, c = (lax.axis_index(name) for name in GRID)
    lines = jnp.pad(params.reshape(SHARD, LINE), ((0, SPAD - SHARD), (0, 0)))
    sibling = lax.ppermute(lines, ZC, [(2 * k + 1 - k % 2, 2 * k + k % 2) for k in range(4)])
    buffers = []
    for part in range(2):
        here = jnp.where(c == part, lines, sibling)
        one = lax.ppermute(here, ZC, zc_pairs((0, 1, 0), (1, 2, 1)))
        side = lax.ppermute(here, ZC, zc_pairs((1, 0, 1)))
        two = lax.ppermute(one, ZC, zc_pairs((1, 2, 0), (2, 3, 1)))
        three = lax.ppermute(two, ZC, zc_pairs((2, 3, 0)))
        column = jnp.where(z == c, here, one + side + two + three)
        over_x = lax.ppermute(column, "x", SWAP)
        over_y = lax.ppermute(column, "y", SWAP)
        corner = lax.ppermute(over_y if part else over_x, "x" if part else "y", SWAP)
        local = [column, over_x, over_y, corner]
        buffers += [piece[None] for piece in local]
        buffers += [lax.ppermute(piece, "c", SWAP)[None] for piece in local]
    early = [(k, 0) for k in range(16)]
    here = jnp.where(c == 0, jnp.stack([lines, sibling]), jnp.stack([sibling, lines]))
    one = lax.ppermute(here, ZC, zc_pairs((2, 1, 0), (3, 2, 1)))
    side = lax.ppermute(here, ZC, zc_pairs((2, 3, 0)))
    two = lax.ppermute(one, ZC, zc_pairs((1, 0, 0), (2, 1, 1)))
    three = lax.ppermute(two, ZC, zc_pairs((1, 0, 1)))
    column = jnp.where(z == 2 + c, here, one + side + two + three)
    late = []
    for part in range(2):
        for first in (16, 21):
            late += [(first, part), (first + 1, part), (first + 2, part), (first + 3 + part, 0)]
    shard = np.arange(32)
    sz, sy, sx, sc = shard // 8, shard // 4 % 2, shard // 2 % 2, shard % 2
    away = jnp.where(sz % 2 == c, 0, 4)
    where = sc * 8 + away + 2 * (sy ^ y) + (sx ^ x) + 16 * (sz // 2)
    return buffers, Flow(spread_stages(column)), (early, early + late), where.astype(jnp.int32)


def spread_stages(column):
    over_x, over_y = yield [(column, "x", SWAP), (column, "y", SWAP)]
    corners = yield [(over_x[:1], "y", SWAP), (over_y[1:], "x", SWAP)]
    local = [column, over_x, over_y] + list(corners)
    return local + list((yield [(piece, "c", SWAP) for piece in local]))


def unpack_lines(buffers, slots, where, segments, after=()):
    jobs, starts = [], []
    reach = 0
    for offset, rows, columns in segments:
        per_row = columns // LINE
        lane, base = offset % LINE, offset // LINE
        if per_row == 1 and rows < 1024:
            lane, tall = 0, rows
        else:
            tall = TALL[per_row]
        starts.append(len(jobs))
        for k in range(rows // tall):
            jobs.append((base + k * tall * per_row, tall * per_row, 1 if lane else 0))
    window = max(job[1] for job in jobs) + 32
    table = np.zeros((len(jobs), 5), np.int32)
    for k, (line, count, extra) in enumerate(jobs):
        owner = line // SHARD
        inside = line - owner * SHARD
        begin = min(inside // 16 * 16, SPAD - window)
        crosses = int(line + count + extra > (owner + 1) * SHARD)
        table[k] = (owner, begin, begin - inside, crosses, (owner + 1) * SHARD - line)
    base_row = (int(-table[:, 2].min()) + 7) // 8 * 8
    table[:, 2] += base_row
    table[:, 4] += base_row
    room = int(max((table[:, 2] + window).max(), ((table[:, 4] + window) * table[:, 3]).max()))
    room = (room + 15) // 8 * 8
    total = len(jobs)
    count_buffers = len(buffers)
    shapes = []
    for offset, rows, columns in segments:
        per_row = columns // LINE
        tall = rows if per_row == 1 and rows < 1024 else TALL[per_row]
        shapes.append((rows, columns, tall, per_row, offset % LINE if tall != rows or per_row != 1 else 0))
    sizes = sorted({(tall, columns) for _, columns, tall, _, _ in shapes})

    def kernel(table_ref, where_ref, *refs):
        sources = refs[:count_buffers]
        outs = refs[count_buffers : count_buffers + len(segments)]
        rest = refs[count_buffers + len(segments) :]
        stages = dict(zip(sizes, rest))
        raw, flat, in_sem, out_sem = rest[len(sizes) :]
        step = pl.program_id(0)

        def fetch(job, slot):
            owner = table_ref[job, 0]
            begin = pl.multiple_of(table_ref[job, 1], 16)
            for b, (source, part) in enumerate(slots):

                @pl.when(where_ref[owner] == b)
                def _():
                    pltpu.make_async_copy(
                        sources[source].at[part, pl.ds(begin, window), :], raw.at[slot, 0], in_sem.at[slot, 0]
                    ).start()

            @pl.when(table_ref[job, 3] == 1)
            def _():
                for b, (source, part) in enumerate(slots):

                    @pl.when(where_ref[owner + 1] == b)
                    def _():
                        pltpu.make_async_copy(
                            sources[source].at[part, pl.ds(0, window), :], raw.at[slot, 1], in_sem.at[slot, 1]
                        ).start()

        def fetched(slot, half):
            return pltpu.make_async_copy(
                sources[0].at[0, pl.ds(0, window), :], raw.at[slot, half], in_sem.at[slot, half]
            )

        @pl.when(step == 0)
        def _():
            for k in range(min(DEPTH - 1, total)):
                fetch(k, k)

        @pl.when(step + DEPTH - 1 < total)
        def _():
            fetch(step + DEPTH - 1, lax.rem(step + DEPTH - 1, DEPTH))

        slot = lax.rem(step, DEPTH)
        fetched(slot, 0).wait()
        flat[pl.ds(table_ref[step, 2], window), :] = raw[slot, 0].astype(jnp.float32)

        @pl.when(table_ref[step, 3] == 1)
        def _():
            fetched(slot, 1).wait()
            flat[pl.ds(table_ref[step, 4], window), :] = raw[slot, 1].astype(jnp.float32)

        for index, (rows, columns, tall, per_row, lane) in enumerate(shapes):
            begin = starts[index]
            blocks = rows // tall
            stage = stages[(tall, columns)]

            @pl.when((step >= begin) & (step < begin + blocks))
            def _():
                block = step - begin
                side = lax.rem(block, DEPTH)

                def written(k, s):
                    return pltpu.make_async_copy(
                        stage.at[s],
                        outs[index].at[pl.ds(pl.multiple_of(k * tall, 16), tall), :],
                        out_sem.at[s],
                    )

                @pl.when(block >= DEPTH)
                def _():
                    written(block - DEPTH, side).wait()

                def tile(j):
                    picked = flat[pl.ds(base_row + j, tall, stride=per_row), :]
                    return pltpu.roll(picked, LINE - lane, 1) if lane else picked

                if lane:
                    lanes = lax.broadcasted_iota(jnp.int32, (tall, LINE), 1)
                    now = tile(0)
                    for j in range(per_row):
                        later = tile(j + 1)
                        stage[side, :, j * LINE : (j + 1) * LINE] = jnp.where(
                            lanes < LINE - lane, now, later
                        ).astype(jnp.bfloat16)
                        now = later
                else:
                    for j in range(per_row):
                        stage[side, :, j * LINE : (j + 1) * LINE] = tile(j).astype(jnp.bfloat16)
                written(block, side).start()

                @pl.when(block == blocks - 1)
                def _():
                    for back in reversed(range(min(DEPTH, blocks))):
                        written(block - back, lax.rem(block - back, DEPTH)).wait()

    return pl.pallas_call(
        pinned(kernel, 2 + count_buffers, after),
        grid_spec=pltpu.PrefetchScalarGridSpec(
            num_scalar_prefetch=2,
            grid=(total,),
            in_specs=[pl.BlockSpec(memory_space=pl.ANY)] * count_buffers + pins(after),
            out_specs=[pl.BlockSpec(memory_space=pl.ANY)] * len(segments),
            scratch_shapes=[pltpu.VMEM((DEPTH,) + size, jnp.bfloat16) for size in sizes]
            + [
                pltpu.VMEM((DEPTH, 2, window, LINE), jnp.bfloat16),
                pltpu.VMEM((room, LINE), jnp.float32),
                pltpu.SemaphoreType.DMA((DEPTH, 2)),
                pltpu.SemaphoreType.DMA((DEPTH,)),
            ],
        ),
        out_shape=[jax.ShapeDtypeStruct((rows, columns), jnp.bfloat16) for _, rows, columns in segments],
        compiler_params=pltpu.CompilerParams(vmem_limit_bytes=48 * 2**20),
        cost_estimate=pl.CostEstimate(flops=0, bytes_accessed=total * window * LINE * 4, transcendentals=0),
        name="unpack",
    )(jnp.asarray(table), where, *buffers, *after)


def pack_lines(target, target_rows, first_row, segments, lane, phase, extras, carry, tail_rows, after=()):
    tall = 256
    lefts, rights, plan = [], [], []
    left_of, right_of = {}, {}
    row = first_row
    begin = 0
    for left, right in segments:
        for value, seen, kept in ((left, left_of, lefts), (right, right_of, rights)):
            if id(value) not in seen:
                seen[id(value)] = len(kept)
                kept.append(value)
        blocks = left.shape[1] // tall
        plan.append((left_of[id(left)], right_of[id(right)], right.shape[1] // LINE, begin, blocks, row))
        begin += blocks
        row += left.shape[1] * right.shape[1] // LINE
    end_row = row
    total = begin
    biggest = max(entry[2] for entry in plan) * tall
    tokens = lefts[0].shape[0]
    count_left, count_right, count_extra = len(lefts), len(rights), len(extras)
    rolled = [jnp.roll(right, lane, axis=1) if lane else right for right in rights]
    carry_in = [carry] if lane else []
    targets = [] if target is None else [target]

    def left_spec(index):
        mine = [entry for entry in plan if entry[0] == index]

        def place(step):
            block = 0
            for _, _, _, start, blocks, _ in mine:
                block = jnp.where(step >= start, jnp.minimum(step - start, blocks - 1), block)
            return (0, block)

        return pl.BlockSpec((tokens, tall), place)

    def kernel(*refs):
        left_refs = refs[:count_left]
        right_refs = refs[count_left : count_left + count_right]
        at = count_left + count_right
        extra_refs = refs[at : at + count_extra]
        at += count_extra
        carry_refs = refs[at : at + len(carry_in)]
        at += len(carry_in) + len(targets)
        out = refs[at]
        flat, stage, shift, last, sems, extra_sems = refs[at + 1 :]
        step = pl.program_id(0)
        side = lax.rem(step, 2)

        def extra_copy(k):
            rows = extras[k][0].shape[0]
            return pltpu.make_async_copy(
                extra_refs[k], out.at[pl.ds(extras[k][1], rows), :], extra_sems.at[k]
            )

        @pl.when(step == 0)
        def _():
            for k in range(count_extra):
                extra_copy(k).start()
            if lane:
                shift[0:8, :] = carry_refs[0][...]
            if phase:
                flat[0:8, :] = jnp.zeros((8, LINE), jnp.float32)

        for left_at, right_at, per_row, start, blocks, row in plan:
            lines = per_row * tall

            def written(block, s, row=row, lines=lines):
                return pltpu.make_async_copy(
                    stage.at[s, pl.ds(0, lines), :],
                    out.at[pl.ds(pl.multiple_of(row + block * lines, 16), lines), :],
                    sems.at[s],
                )

            @pl.when((step >= start) & (step < start + blocks))
            def _():
                block = step - start
                if phase:

                    @pl.when(step > 0)
                    def _():
                        flat[0:8, :] = flat[lines : lines + 8, :]

                turned = left_refs[left_at][...].T
                lanes = lax.broadcasted_iota(jnp.int32, (tall, LINE), 1)
                for j0 in range(0, per_row, 2):
                    wide = min(2, per_row - j0)
                    tile = jnp.dot(
                        turned,
                        right_refs[right_at][:, j0 * LINE : (j0 + wide) * LINE],
                        preferred_element_type=jnp.float32,
                    )
                    for j in range(wide):
                        piece = tile[:, j * LINE : (j + 1) * LINE]
                        if lane and j0 + j == 0:
                            shift[8 : 8 + tall, :] = piece
                            piece = jnp.where(lanes < lane, shift[7 : 7 + tall, :], piece)
                            shift[0:8, :] = shift[tall : tall + 8, :]
                        if per_row == 1:
                            flat[phase : phase + tall, :] = piece
                        else:
                            flat[pl.ds(phase + j0 + j, tall, stride=per_row), :] = piece

                stage[side, 0:lines, :] = flat[0:lines, :].astype(jnp.bfloat16)
                written(block, side).start()

            @pl.when((step > start) & (step <= start + blocks))
            def _():
                written(step - start - 1, 1 - side).wait()

            if start + blocks == total:

                @pl.when(step == total - 1)
                def _():
                    written(blocks - 1, side).wait()

        @pl.when(step == total - 1)
        def _():
            if tail_rows:
                lanes = lax.broadcasted_iota(jnp.int32, (tail_rows, LINE), 1)
                rows_at = lax.broadcasted_iota(jnp.int32, (tail_rows, LINE), 0)
                final = jnp.broadcast_to(shift[7:8, :], (tail_rows, LINE))
                last[...] = jnp.where((rows_at == 0) & (lanes < lane), final, 0.0).astype(jnp.bfloat16)
                closing = pltpu.make_async_copy(
                    last, out.at[pl.ds(end_row, tail_rows), :], extra_sems.at[count_extra]
                )
                closing.start()
                closing.wait()
            for k in range(count_extra):
                extra_copy(k).wait()

    whole = [pl.BlockSpec(array.shape, lambda step: (0, 0)) for array in rolled]
    flops = sum(2 * tokens * entry[4] * tall * entry[2] * LINE for entry in plan)
    inputs = count_left + count_right + count_extra + len(carry_in) + len(targets)
    return pl.pallas_call(
        pinned(kernel, inputs, after),
        grid=(total,),
        in_specs=[left_spec(k) for k in range(count_left)]
        + whole
        + [pl.BlockSpec(array.shape, lambda step: (0, 0)) for array, _ in extras]
        + [pl.BlockSpec(array.shape, lambda step: (0, 0)) for array in carry_in]
        + [pl.BlockSpec(memory_space=pl.ANY)] * len(targets)
        + pins(after),
        out_specs=pl.BlockSpec(memory_space=pl.ANY),
        out_shape=jax.ShapeDtypeStruct((target_rows, LINE), jnp.bfloat16),
        scratch_shapes=[
            pltpu.VMEM((biggest + 16, LINE), jnp.float32),
            pltpu.VMEM((2, biggest, LINE), jnp.bfloat16),
            pltpu.VMEM((tall + 8, LINE), jnp.float32),
            pltpu.VMEM((max(tail_rows, 16), LINE), jnp.bfloat16),
            pltpu.SemaphoreType.DMA((2,)),
            pltpu.SemaphoreType.DMA((count_extra + 1,)),
        ],
        input_output_aliases={count_left + count_right + count_extra + len(carry_in): 0} if targets else {},
        compiler_params=pltpu.CompilerParams(vmem_limit_bytes=48 * 2**20),
        cost_estimate=pl.CostEstimate(flops=flops, bytes_accessed=total * biggest * LINE * 2, transcendentals=0),
        name="pack",
    )(*lefts, *rolled, *[array for array, _ in extras], *carry_in, *targets, *after)


def added(*parts):
    total = parts[0].astype(jnp.float32)
    for part in parts[1:]:
        total = total + part.astype(jnp.float32)
    return total.astype(jnp.bfloat16)


def reduce_stages(flat, batch, shift):
    z, y, x, c = (lax.axis_index(name) for name in GRID)
    length = PLANE + 32
    send = lax.dynamic_slice(flat, ((1 - c) * PLANE, 0), (length, LINE))
    (arrived,) = yield [(send, "c", SWAP)]
    chip = added(lax.dynamic_slice(flat, (c * PLANE, 0), (length, LINE)), arrived)

    def window(sy, sx, part):
        shard = sy * 4 + sx * 2 + part
        start = (shift + SHARD * shard) // 16 * 16
        return lax.dynamic_slice(chip, (start, 0), (WIN, LINE))

    away_0 = jnp.stack([window(1 - y, 0, 0), window(1 - y, 1, 0)])
    away_1 = jnp.stack([window(0, 1 - x, 1), window(1, 1 - x, 1)])
    home_0 = jnp.stack([window(y, 0, 0), window(y, 1, 0)])
    home_1 = jnp.stack([window(0, x, 1), window(1, x, 1)])
    got_0, got_1 = yield [(away_0, "y", SWAP), (away_1, "x", SWAP)]
    half_0, half_1 = added(home_0, got_0), added(home_1, got_1)
    pick = lambda value, at: lax.dynamic_index_in_dim(value, at, 0, keepdims=False)
    got_0, got_1 = yield [(pick(half_0, 1 - x), "x", SWAP), (pick(half_1, 1 - y), "y", SWAP)]
    columns = [added(pick(half_0, x), got_0), added(pick(half_1, y), got_1)]
    if batch == 0:
        hops = [((1, 0, 0), (2, 1, 1)), ((2, 0, 0), (3, 1, 1)), ((3, 0, 0), (0, 1, 1))]
    else:
        hops = [((1, 2, 0), (2, 3, 1)), ((0, 2, 0), (1, 3, 1)), ((3, 2, 0), (0, 3, 1))]
    if batch == 0:
        got = yield [(columns[0], ZC, zc_pairs(*hop)) for hop in hops]
        end = added(columns[0], *got)
        (column,) = fence(columns[1:], [end])
        got = yield [(column, ZC, zc_pairs(*hop)) for hop in hops]
        ends = [end, added(column, *got)]
    else:
        columns = jnp.stack(columns)
        got = yield [(columns, ZC, zc_pairs(*hop)) for hop in hops]
        ends = added(columns, *got)
    mine = jnp.where(c == 0, ends[0], ends[1])
    other = jnp.where(c == 0, ends[1], ends[0])
    (handed,) = yield [(other, ZC, [(2 * k + k % 2, 2 * k + 1 - k % 2) for k in range(4)])]
    return jnp.where(c == z % 2, mine, handed)


PIECE = 400


def corner_stages(flat):
    z, y, x, c = (lax.axis_index(name) for name in GRID)
    length = 8 * PIECE
    second = (8 + SHARD) // 16 * 16
    take = lambda at: lax.dynamic_slice(flat, (at * second, 0), (length, LINE))
    (arrived,) = yield [(take(1 - c), "c", SWAP)]
    chip = added(take(c), arrived).reshape(2, 2, 2, PIECE, LINE)
    pick = lambda value, at: lax.dynamic_index_in_dim(value, at, 0, keepdims=False)
    got = yield [(pick(chip[0], 1 - x), "x", SWAP), (pick(chip[1], 1 - y), "y", SWAP)]
    halves = [added(pick(chip[0], x), got[0]), added(pick(chip[1], y), got[1])]
    got = yield [(pick(halves[0], 1 - y), "y", SWAP), (pick(halves[1], 1 - x), "x", SWAP)]
    pieces = jnp.stack([added(pick(halves[0], y), got[0]), added(pick(halves[1], x), got[1])])
    got = yield [(pieces, "z", [(k, 0)]) for k in (1, 2, 3)]
    pieces = added(pieces, *got)
    got = yield [(pieces[0], "y", [(1, 0)]), (pieces[1], "x", [(1, 0)])]
    halves = [jnp.stack([pieces[0], got[0]]), jnp.stack([pieces[1], got[1]])]
    got = yield [(halves[0], "x", [(1, 0)]), (halves[1], "y", [(1, 0)])]
    return jnp.stack([halves[0], got[0], halves[1], got[1]]).reshape(length, LINE)


CHUNK = 128
NT = (((1,), (1,)), ((), ()))
TN = (((0,), (0,)), ((), ()))
INNER = SSM_HEADS * SSM_DIM
PAIRS = SSM_HEADS // 2


def spread(rows_a, rows_b):
    length = rows_a.shape[1]
    tall = jnp.concatenate(
        [jnp.broadcast_to(rows_a, (SSM_DIM, length)), jnp.broadcast_to(rows_b, (SSM_DIM, length))], axis=0
    )
    return tall.T


CHANNELS = INNER + 2 * STATE
LANES = 2 * SSM_DIM
COLUMNS = CHANNELS // LANES


def conv_masks(masks, start_ref, first, rows):
    place = first + lax.broadcasted_iota(jnp.int32, (rows, LANES), 0) - start_ref[...]
    for reach in range(1, CONV):
        masks[reach - 1] = jnp.where(place >= reach, 1.0, 0.0)


def conv_parts(ext, weight_ref, bias_ref, masks, rows):
    windows = []
    total = bias_ref[...]
    for tap in range(CONV):
        reach = CONV - 1 - tap
        window = ext[8 - reach : 8 - reach + rows, :]
        if reach:
            window = window * masks[reach - 1]
        windows.append(window)
        total = total + window * weight_ref[tap : tap + 1, :]
    return windows, total


def conv_forward(xbc, rim, weight, bias, meta, start_column, after=()):
    rows = xbc.shape[0]

    def kernel(meta_ref, x_ref, rim_ref, weight_ref, bias_ref, start_ref, out_ref, ext, masks):
        @pl.when(pl.program_id(0) == 0)
        def _():
            conv_masks(masks, start_ref, meta_ref[0], rows)

        ext[0:8, :] = rim_ref[...]
        ext[8:, :] = x_ref[...]
        _, total = conv_parts(ext, weight_ref, bias_ref, masks, rows)
        out_ref[...] = total * jax.nn.sigmoid(total)

    lanes = lambda i, m: (0, i)
    return pl.pallas_call(
        pinned(kernel, 6, after),
        grid_spec=pltpu.PrefetchScalarGridSpec(
            num_scalar_prefetch=1,
            grid=(COLUMNS,),
            in_specs=[
                pl.BlockSpec((rows, LANES), lanes),
                pl.BlockSpec((8, LANES), lanes),
                pl.BlockSpec((CONV, LANES), lanes),
                pl.BlockSpec((1, LANES), lanes),
                pl.BlockSpec((rows, 1), lambda i, m: (0, 0)),
            ] + pins(after),
            out_specs=pl.BlockSpec((rows, LANES), lanes),
            scratch_shapes=[
                pltpu.VMEM((rows + 8, LANES), jnp.float32),
                pltpu.VMEM((CONV - 1, rows, LANES), jnp.float32),
            ],
        ),
        out_shape=jax.ShapeDtypeStruct((rows, CHANNELS), jnp.float32),
        cost_estimate=pl.CostEstimate(flops=10**9, bytes_accessed=rows * CHANNELS * 8, transcendentals=0),
        name="conv",
    )(meta, xbc, rim, weight, bias, start_column, *after)


def conv_backward(dx, db, dc, xbc, rim, weight, bias, meta, start_column, after=()):
    rows = xbc.shape[0]

    def kernel(meta_ref, dx_ref, db_ref, dc_ref, x_ref, rim_ref, weight_ref, bias_ref, start_ref,
               low_ref, tail_ref, edge_ref, small_ref, ext, upper, masks):
        @pl.when(pl.program_id(0) == 0)
        def _():
            conv_masks(masks, start_ref, meta_ref[0], rows)
            upper[0:8, :] = jnp.zeros((8, LANES), jnp.float32)
            upper[8 + rows :, :] = jnp.zeros((8, LANES), jnp.float32)

        ext[0:8, :] = rim_ref[...]
        ext[8:, :] = x_ref[...]
        at = pl.program_id(0)
        arrived = jnp.where(at < PAIRS, dx_ref[...], jnp.where(at == PAIRS, db_ref[...], dc_ref[...]))
        windows, total = conv_parts(ext, weight_ref, bias_ref, masks, rows)
        gate = jax.nn.sigmoid(total)
        change = arrived * gate * (1.0 + total * (1.0 - gate))
        main = jnp.zeros((rows, LANES), jnp.float32)
        edge = jnp.zeros((8, LANES), jnp.float32)
        small_ref[...] = jnp.zeros((8, LANES), jnp.float32)
        small_ref[CONV : CONV + 1, :] = jnp.sum(change, axis=0, keepdims=True)
        for tap in range(CONV):
            reach = CONV - 1 - tap
            small_ref[tap : tap + 1, :] = jnp.sum(change * windows[tap], axis=0, keepdims=True)
            masked = change * masks[reach - 1] if reach else change
            upper[8 : 8 + rows, :] = masked * weight_ref[tap : tap + 1, :]
            main = main + upper[8 + reach : 8 + reach + rows, :]
            edge = edge + upper[reach : reach + 8, :]
        low_ref[...] = main.astype(jnp.bfloat16)
        tail_ref[...] = main[rows - 16 :, :]
        edge_ref[...] = edge

    lanes = lambda i, m: (0, i)
    whole = lambda i, m: (0, 0)
    return pl.pallas_call(
        pinned(kernel, 9, after),
        grid_spec=pltpu.PrefetchScalarGridSpec(
            num_scalar_prefetch=1,
            grid=(COLUMNS,),
            in_specs=[
                pl.BlockSpec((rows, LANES), lambda i, m: (0, jnp.minimum(i, PAIRS - 1))),
                pl.BlockSpec((rows, STATE), whole),
                pl.BlockSpec((rows, STATE), whole),
                pl.BlockSpec((rows, LANES), lanes),
                pl.BlockSpec((8, LANES), lanes),
                pl.BlockSpec((CONV, LANES), lanes),
                pl.BlockSpec((1, LANES), lanes),
                pl.BlockSpec((rows, 1), whole),
            ] + pins(after),
            out_specs=[
                pl.BlockSpec((rows, LANES), lanes),
                pl.BlockSpec((16, LANES), lanes),
                pl.BlockSpec((8, LANES), lanes),
                pl.BlockSpec((8, LANES), lanes),
            ],
            scratch_shapes=[
                pltpu.VMEM((rows + 8, LANES), jnp.float32),
                pltpu.VMEM((rows + 16, LANES), jnp.float32),
                pltpu.VMEM((CONV - 1, rows, LANES), jnp.float32),
            ],
        ),
        out_shape=[
            jax.ShapeDtypeStruct((rows, CHANNELS), jnp.bfloat16),
            jax.ShapeDtypeStruct((16, CHANNELS), jnp.float32),
            jax.ShapeDtypeStruct((8, CHANNELS), jnp.float32),
            jax.ShapeDtypeStruct((8, CHANNELS), jnp.float32),
        ],
        cost_estimate=pl.CostEstimate(flops=2 * 10**9, bytes_accessed=rows * CHANNELS * 10, transcendentals=0),
        name="conv_back",
    )(meta, dx, db, dc, xbc, rim, weight, bias, start_column, *after)


def weighted_state(left, left_block, values, weight_rows, after=()):
    rows = left.shape[0]

    def kernel(left_ref, value_ref, weight_ref, out_ref, turned):
        @pl.when(pl.program_id(0) == 0)
        def _():
            turned[...] = left_ref[...].T

        scaled = [(turned[...] * weight_ref[0, e : e + 1, :]).astype(jnp.bfloat16) for e in range(2)]
        both = jnp.dot(
            jnp.concatenate(scaled, axis=0), value_ref[...].astype(jnp.bfloat16), preferred_element_type=jnp.float32
        )
        low_lane = lax.broadcasted_iota(jnp.int32, (STATE, 2 * SSM_DIM), 1) < SSM_DIM
        out_ref[...] = jnp.where(low_lane, both[:STATE], both[STATE:])

    return pl.pallas_call(
        pinned(kernel, 3, after),
        grid=(PAIRS,),
        in_specs=[
            pl.BlockSpec((rows, STATE), lambda i: (0, left_block)),
            pl.BlockSpec((rows, 2 * SSM_DIM), lambda i: (0, i)),
            pl.BlockSpec((1, 2, rows), lambda i: (i, 0, 0)),
        ] + pins(after),
        out_specs=pl.BlockSpec((STATE, 2 * SSM_DIM), lambda i: (0, i)),
        out_shape=jax.ShapeDtypeStruct((STATE, INNER), jnp.float32),
        scratch_shapes=[pltpu.VMEM((STATE, rows), jnp.float32)],
        cost_estimate=pl.CostEstimate(flops=2 * rows * STATE * INNER, bytes_accessed=rows * INNER * 4, transcendentals=0),
        name="state",
    )(left, values, weight_rows.reshape(PAIRS, 2, rows), *after)


def chunk_rows(k, meta_ref, cum_ref, start_ref):
    here = slice(k * CHUNK, (k + 1) * CHUNK)
    first = meta_ref[0] + k * CHUNK
    index = first + lax.broadcasted_iota(jnp.int32, (1, CHUNK), 1)
    entering = start_ref[0:1, here] < first
    ending = index >= meta_ref[1 + k]
    cums, entries, tails = [], [], []
    for e in range(2):
        cum = cum_ref[0, e : e + 1, here]
        cums.append(cum)
        entries.append(jnp.where(entering, jnp.exp(cum), 0.0))
        gap = jnp.where(ending, cum[:, CHUNK - 1 :] - cum, masked_score)
        tails.append(jnp.exp(gap))
    return cums, entries, tails


def ssm_forward(conv, cum, step, state_in, skip, meta, start_column, start_row):
    rows = conv.shape[0]
    chunks = rows // CHUNK

    def kernel(meta_ref, x_ref, b_ref, c_ref, cum_ref, step_ref, state_ref, skip_ref, col_ref, row_ref,
               y_ref, inner, hide, state, b_turned):
        @pl.when(pl.program_id(0) == 0)
        def _():
            for k in range(chunks):
                here = slice(k * CHUNK, (k + 1) * CHUNK)
                b_turned[:, here] = b_ref[here, :].T.astype(jnp.bfloat16)
                inner[k] = lax.dot_general(
                    c_ref[here, :], b_ref[here, :], NT, precision=highest, preferred_element_type=jnp.float32
                )
                t = lax.broadcasted_iota(jnp.int32, (CHUNK, CHUNK), 0)
                s = lax.broadcasted_iota(jnp.int32, (CHUNK, CHUNK), 1)
                shown = (s <= t) & (meta_ref[0] + k * CHUNK + s >= col_ref[here, :])
                hide[k] = jnp.where(shown, 0.0, masked_score)

        low_lane = lax.broadcasted_iota(jnp.int32, (CHUNK, 2 * SSM_DIM), 1) < SSM_DIM
        state[...] = state_ref[...]
        for k in range(chunks):
            here = slice(k * CHUNK, (k + 1) * CHUNK)
            cums, entries, tails = chunk_rows(k, meta_ref, cum_ref, row_ref)
            x_now = x_ref[here, :]
            x_low = x_now.astype(jnp.bfloat16)
            entry = spread(*entries)
            weight = spread(*[tails[e] * step_ref[0, e : e + 1, here] for e in range(2)])
            parts = []
            for e in range(2):
                across = jnp.broadcast_to(cums[e], (CHUNK, CHUNK))
                decays = jnp.exp(across.T - across + hide[k])
                mix = (inner[k] * decays * step_ref[0, e : e + 1, here]).astype(jnp.bfloat16)
                parts.append(jnp.dot(mix, x_low, preferred_element_type=jnp.float32))
            carried = jnp.dot(
                c_ref[here, :].astype(jnp.bfloat16), state[...].astype(jnp.bfloat16),
                preferred_element_type=jnp.float32,
            )
            y_ref[here, :] = jnp.where(low_lane, parts[0], parts[1]) + entry * carried + skip_ref[...] * x_now
            fresh = jnp.dot(
                b_turned[:, here], (x_now * weight).astype(jnp.bfloat16), preferred_element_type=jnp.float32
            )
            state[...] = entry[CHUNK - 1 :, :] * state[...] + fresh

    whole = lambda i, m: (0, 0)
    lanes = lambda i, m: (0, i)
    return pl.pallas_call(
        kernel,
        grid_spec=pltpu.PrefetchScalarGridSpec(
            num_scalar_prefetch=1,
            grid=(PAIRS,),
            in_specs=[
                pl.BlockSpec((rows, 2 * SSM_DIM), lanes),
                pl.BlockSpec((rows, STATE), lambda i, m: (0, PAIRS)),
                pl.BlockSpec((rows, STATE), lambda i, m: (0, PAIRS + 1)),
                pl.BlockSpec((1, 2, rows), lambda i, m: (i, 0, 0)),
                pl.BlockSpec((1, 2, rows), lambda i, m: (i, 0, 0)),
                pl.BlockSpec((STATE, 2 * SSM_DIM), lanes),
                pl.BlockSpec((1, 2 * SSM_DIM), lanes),
                pl.BlockSpec((rows, 1), whole),
                pl.BlockSpec((8, rows), whole),
            ],
            out_specs=pl.BlockSpec((rows, 2 * SSM_DIM), lanes),
            scratch_shapes=[
                pltpu.VMEM((chunks, CHUNK, CHUNK), jnp.float32),
                pltpu.VMEM((chunks, CHUNK, CHUNK), jnp.float32),
                pltpu.VMEM((STATE, 2 * SSM_DIM), jnp.float32),
                pltpu.VMEM((STATE, rows), jnp.bfloat16),
            ],
        ),
        out_shape=jax.ShapeDtypeStruct((rows, INNER), jnp.float32),
        compiler_params=pltpu.CompilerParams(vmem_limit_bytes=40 * 2**20),
        cost_estimate=pl.CostEstimate(flops=10**9, bytes_accessed=rows * INNER * 8, transcendentals=2**21),
        name="ssm",
    )(meta, conv, conv, conv, cum.reshape(PAIRS, 2, rows), step.reshape(PAIRS, 2, rows), state_in, skip,
      start_column, start_row)


def ssm_backward(conv, dy, cum, step, state_in, state_grad, skip, meta, start_row, after=()):
    rows = conv.shape[0]
    chunks = rows // CHUNK

    def kernel(meta_ref, x_ref, dy_ref, b_ref, c_ref, cum_ref, step_ref, state_ref, grad_ref, skip_ref, row_ref,
               dx_ref, db_ref, dc_ref, small_ref, inner, hide, inner_grad, states, flow,
               b_turned, c_turned):
        low = lambda v: v.astype(jnp.bfloat16)
        dot = lambda p, q, dims=(((1,), (0,)), ((), ())): lax.dot_general(
            p, q, dims, preferred_element_type=jnp.float32
        )
        exact = lambda p, q, dims=(((1,), (0,)), ((), ())): lax.dot_general(
            p, q, dims, precision=highest, preferred_element_type=jnp.float32
        )
        s = lax.broadcasted_iota(jnp.int32, (CHUNK, CHUNK), 0)
        t = lax.broadcasted_iota(jnp.int32, (CHUNK, CHUNK), 1)

        @pl.when(pl.program_id(0) == 0)
        def _():
            db_ref[...] = jnp.zeros(db_ref.shape, jnp.float32)
            dc_ref[...] = jnp.zeros(dc_ref.shape, jnp.float32)
            inner_grad[...] = jnp.zeros(inner_grad.shape, jnp.float32)
            for k in range(chunks):
                here = slice(k * CHUNK, (k + 1) * CHUNK)
                b_turned[:, here] = low(b_ref[here, :].T)
                c_turned[:, here] = low(c_ref[here, :].T)
                inner[k] = exact(b_ref[here, :], c_ref[here, :], NT)
                shown = (s <= t) & (meta_ref[0] + k * CHUNK + s >= row_ref[0:1, here])
                hide[k] = jnp.where(shown, 0.0, masked_score)

        before = (s < t).astype(jnp.float32)
        until = low((s >= t).astype(jnp.float32))
        low_lane = t < SSM_DIM
        pick_row = lax.broadcasted_iota(jnp.int32, (8, 2 * SSM_DIM), 0)
        pick_lane = lax.broadcasted_iota(jnp.int32, (8, 2 * SSM_DIM), 1) // SSM_DIM
        pick = low((pick_row == pick_lane).astype(jnp.float32))
        spreads = []
        states[0] = state_ref[...]
        for k in range(chunks):
            here = slice(k * CHUNK, (k + 1) * CHUNK)
            cums, entries, tails = chunk_rows(k, meta_ref, cum_ref, row_ref)
            entry, tail = spread(*entries), spread(*tails)
            steps = spread(step_ref[0, 0:1, here], step_ref[0, 1:2, here])
            spreads.append((cums, entry, tail, steps))
            if k < chunks - 1:
                fresh = dot(b_turned[:, here], low(x_ref[here, :] * steps * tail))
                states[k + 1] = entry[CHUNK - 1 :, :] * states[k] + fresh
        flow[...] = grad_ref[...]
        skip_sum = jnp.zeros((1, 2 * SSM_DIM), jnp.float32)
        for k in reversed(range(chunks)):
            here = slice(k * CHUNK, (k + 1) * CHUNK)
            cums, entry, tail, steps = spreads[k]
            x_now, dy_now = x_ref[here, :], dy_ref[here, :]
            b_low, c_low = low(b_ref[here, :]), low(c_ref[here, :])
            scaled = x_now * steps
            dy_low = low(dy_now)
            flow_low, state_low = low(flow[...]), low(states[k])
            both = low(
                jnp.concatenate([jnp.where(low_lane, scaled, 0.0), jnp.where(low_lane, 0.0, scaled)], axis=0)
            )
            reached = dot(both, dy_low, NT)
            mixes, weighed = [], []
            for e in range(2):
                across = jnp.broadcast_to(cums[e], (CHUNK, CHUNK))
                decays = jnp.exp(across - across.T + hide[k])
                reach = decays * reached[e * CHUNK : (e + 1) * CHUNK]
                inner_grad[k] += reach
                weighed.append(low(inner[k] * reach))
                mixes.append(low(inner[k] * decays))
            sums = dot(jnp.concatenate(weighed, axis=0), until)
            within = [
                jnp.sum(sums[e * CHUNK : (e + 1) * CHUNK] * before, axis=0, keepdims=True) for e in range(2)
            ]
            mixed = dot(jnp.concatenate(mixes, axis=0), dy_low)
            back = tail * dot(b_low, flow_low)
            dxs = jnp.where(low_lane, mixed[:CHUNK], mixed[CHUNK:]) + back
            db_ref[here, :] += dot(low(scaled * tail), flow_low, NT)
            entered = low(dy_now * entry)
            dc_ref[here, :] += dot(entered, state_low, NT)
            brought = dy_now * entry * dot(c_low, state_low)
            ends = dot(pick, low(brought), NT)
            begins = dot(pick, low(scaled * back), NT)
            direct = dot(pick, low(x_now * dxs), NT)
            through = jnp.sum(flow[...] * states[k], axis=0, keepdims=True) * entry[CHUNK - 1 :, :]
            log_grad = exact(ends, until.astype(jnp.float32)) + exact(begins, before)
            for e in range(2):
                lanes = slice(e * SSM_DIM, (e + 1) * SSM_DIM)
                kept = jnp.sum(through[:, lanes], axis=1, keepdims=True)
                small_ref[0, e : e + 1, here] = direct[e : e + 1, :]
                small_ref[0, 2 + e : 3 + e, here] = log_grad[e : e + 1, :] + within[e] + kept
            dx_ref[here, :] = dxs * steps + skip_ref[...] * dy_now
            skip_sum += jnp.sum(x_now * dy_now, axis=0, keepdims=True)
            flow[...] = entry[CHUNK - 1 :, :] * flow[...] + dot(c_turned[:, here], entered)
        small_ref[0, 4:8, :] = jnp.zeros((4, rows), jnp.float32)
        small_ref[0, 4:5, 0 : 2 * SSM_DIM] = skip_sum

        @pl.when(pl.program_id(0) == PAIRS - 1)
        def _():
            for k in range(chunks):
                here = slice(k * CHUNK, (k + 1) * CHUNK)
                grads = low(inner_grad[k])
                db_ref[here, :] += dot(grads, low(c_ref[here, :]))
                dc_ref[here, :] += dot(grads, low(b_ref[here, :]), TN)

    whole = lambda i, m: (0, 0)
    lanes = lambda i, m: (0, i)
    pair = lambda i, m: (i, 0, 0)
    return pl.pallas_call(
        pinned(kernel, 11, after),
        grid_spec=pltpu.PrefetchScalarGridSpec(
            num_scalar_prefetch=1,
            grid=(PAIRS,),
            in_specs=[
                pl.BlockSpec((rows, 2 * SSM_DIM), lanes),
                pl.BlockSpec((rows, 2 * SSM_DIM), lanes),
                pl.BlockSpec((rows, STATE), lambda i, m: (0, PAIRS)),
                pl.BlockSpec((rows, STATE), lambda i, m: (0, PAIRS + 1)),
                pl.BlockSpec((1, 2, rows), pair),
                pl.BlockSpec((1, 2, rows), pair),
                pl.BlockSpec((STATE, 2 * SSM_DIM), lanes),
                pl.BlockSpec((STATE, 2 * SSM_DIM), lanes),
                pl.BlockSpec((1, 2 * SSM_DIM), lanes),
                pl.BlockSpec((8, rows), whole),
            ] + pins(after),
            out_specs=[
                pl.BlockSpec((rows, 2 * SSM_DIM), lanes),
                pl.BlockSpec((rows, STATE), whole),
                pl.BlockSpec((rows, STATE), whole),
                pl.BlockSpec((1, 8, rows), pair),
            ],
            scratch_shapes=[
                pltpu.VMEM((chunks, CHUNK, CHUNK), jnp.float32),
                pltpu.VMEM((chunks, CHUNK, CHUNK), jnp.float32),
                pltpu.VMEM((chunks, CHUNK, CHUNK), jnp.float32),
                pltpu.VMEM((chunks, STATE, 2 * SSM_DIM), jnp.float32),
                pltpu.VMEM((STATE, 2 * SSM_DIM), jnp.float32),
                pltpu.VMEM((STATE, rows), jnp.bfloat16),
                pltpu.VMEM((STATE, rows), jnp.bfloat16),
            ],
        ),
        out_shape=[
            jax.ShapeDtypeStruct((rows, INNER), jnp.float32),
            jax.ShapeDtypeStruct((rows, STATE), jnp.float32),
            jax.ShapeDtypeStruct((rows, STATE), jnp.float32),
            jax.ShapeDtypeStruct((PAIRS, 8, rows), jnp.float32),
        ],
        compiler_params=pltpu.CompilerParams(vmem_limit_bytes=40 * 2**20),
        cost_estimate=pl.CostEstimate(flops=3 * 10**9, bytes_accessed=rows * INNER * 12, transcendentals=2**21),
        name="ssm_back",
    )(meta, conv, dy, conv, conv, cum.reshape(PAIRS, 2, rows), step.reshape(PAIRS, 2, rows), state_in, state_grad,
      skip, start_row, *after)


def chain_states(earlier, later):
    return (earlier[0] * later[0], earlier[1] * later[0] + later[1])


def scan_states(carry, state, span, fast, backward):
    wide = jnp.repeat(carry, SSM_DIM)[None, :]
    if not fast:
        ident = (jnp.ones_like(wide), jnp.zeros_like(state))
        return (carried_in if backward else prefix)((wide, state), span, chain_states, ident)[1]
    flow = Flow(scan_stages(carry, state, backward))
    while flow.sends:
        flow.go()
    return flow.result


def scan_stages(carry, state, backward, extra=None):
    total = (jnp.repeat(carry, SSM_DIM)[None, :], state)
    start = None
    for name in ("c", "x", "y"):
        place = lax.axis_index(name)
        at = lax.broadcasted_iota(jnp.int32, (16, INNER), 0)
        block = jnp.where(at == 0, total[0], 0.0)
        if extra is not None:
            rest = jnp.pad(extra, (0, INNER - extra.shape[0]))[None, :]
            for place_at in range(1, 4):
                term = lax.reduce_precision(rest, 8, 7)
                block = jnp.where(at == place_at, term, block)
                rest = rest - term
        packed = jnp.concatenate([total[1].astype(jnp.bfloat16), block.astype(jnp.bfloat16)], axis=0)
        (packed,) = yield [(packed, name, SWAP)]
        packed = packed.astype(jnp.float32)
        other = (packed[STATE : STATE + 1], packed[:STATE])
        if extra is not None:
            extra = extra + jnp.sum(packed[STATE + 1 : STATE + 4, : extra.shape[0]], axis=0)
        leads = place == (0 if backward else 1)
        seen = (jnp.where(leads, other[0], 1.0), jnp.where(leads, other[1], 0.0))
        start = seen if start is None else chain_states(seen, start)
        if name != "y":
            forward = chain_states(other, total)
            reverse = chain_states(total, other)
            total = jax.tree.map(lambda p, q: jnp.where(leads, p, q), forward, reverse)
    return start[1] if extra is None else [start[1], extra]


KEYS = 512
PAIR = 2 * HEAD_DIM


def attention_forward(q_wide, kv, meta, starts, after=()):
    rows = q_wide.shape[2]
    blocks = kv.shape[0]
    ratio = HEADS_Q // HEADS_KV
    wide = min(512, rows)

    def kernel(meta_ref, q_ref, kv_ref, start_ref, o_ref, log_ref, top, total):
        b = pl.program_id(1)

        @pl.when(b == 0)
        def _():
            top[...] = jnp.full(top.shape, masked_score, jnp.float32)
            total[...] = jnp.zeros(total.shape, jnp.float32)
            o_ref[...] = jnp.zeros(o_ref.shape, jnp.float32)

        def block(partial):
            pair = kv_ref[0, 0]
            turned = pair.T[HEAD_DIM:, :]
            for h in range(ratio):
                for r in range(0, rows, wide):
                    here = slice(r, r + wide)
                    scores = jnp.dot(pair, q_ref[h, :, here], preferred_element_type=jnp.float32)
                    if partial:
                        keys = b * KEYS + lax.broadcasted_iota(jnp.int32, scores.shape, 0)
                        mine = meta_ref[2] + r + lax.broadcasted_iota(jnp.int32, scores.shape, 1)
                        visible = (keys >= start_ref[0:1, here]) & (keys <= mine)
                        scores = jnp.where(visible, scores, masked_score)
                    before = top[h, 0:1, here]
                    peak = jnp.maximum(before, jnp.max(scores, axis=0, keepdims=True))
                    part = jnp.exp(scores - peak)
                    if partial:
                        part = jnp.where(visible, part, 0.0)
                    fade = jnp.exp(before - peak)
                    top[h, 0:1, here] = peak
                    total[h, 0:1, here] = total[h, 0:1, here] * fade + jnp.sum(part, axis=0, keepdims=True)
                    o_ref[h, :, here] = o_ref[h, :, here] * fade + jnp.dot(
                        turned, part.astype(jnp.bfloat16), preferred_element_type=jnp.float32
                    )

        needed = (b >= meta_ref[0]) & (b < meta_ref[1])
        partial = ((b + 1) * KEYS > meta_ref[2]) | (b * KEYS < meta_ref[3])

        @pl.when(needed & partial)
        def _():
            block(True)

        @pl.when(needed & jnp.logical_not(partial))
        def _():
            block(False)

        @pl.when(b == blocks - 1)
        def _():
            for h in range(ratio):
                sums = total[h, 0:1, :]
                o_ref[h] = o_ref[h] / sums
                log_ref[h] = jnp.broadcast_to(top[h, 0:1, :] + jnp.log(sums), (8, rows))

    heads = lambda g, b, m: (g, 0, 0)
    return pl.pallas_call(
        pinned(kernel, 4, after),
        grid_spec=pltpu.PrefetchScalarGridSpec(
            num_scalar_prefetch=1,
            grid=(HEADS_KV, blocks),
            in_specs=[
                pl.BlockSpec((ratio, PAIR, rows), heads),
                pl.BlockSpec((1, 1, KEYS, PAIR), lambda g, b, m: (b, g, 0, 0)),
                pl.BlockSpec((8, rows), lambda g, b, m: (0, 0)),
            ] + pins(after),
            out_specs=[
                pl.BlockSpec((ratio, HEAD_DIM, rows), heads),
                pl.BlockSpec((ratio, 8, rows), heads),
            ],
            scratch_shapes=[
                pltpu.VMEM((ratio, 8, rows), jnp.float32),
                pltpu.VMEM((ratio, 8, rows), jnp.float32),
            ],
        ),
        out_shape=[
            jax.ShapeDtypeStruct((HEADS_Q, HEAD_DIM, rows), jnp.float32),
            jax.ShapeDtypeStruct((HEADS_Q, 8, rows), jnp.float32),
        ],
        compiler_params=pltpu.CompilerParams(vmem_limit_bytes=48 * 2**20),
        cost_estimate=pl.CostEstimate(flops=2 * 10**10, bytes_accessed=2**23, transcendentals=2**23),
        name="attend",
    )(meta, q_wide, kv, starts, *after)


def attention_backward(q_wide, g_wide, kv, logs, mixed, meta, starts, group, after=()):
    rows = q_wide.shape[2]
    blocks = kv.shape[0]
    ratio = HEADS_Q // HEADS_KV
    wide = min(512, rows)

    def kernel(meta_ref, q_ref, g_ref, kv_ref, log_ref, o_ref, start_ref, dkv_ref, dq_ref, delta, sums):
        b = pl.program_id(0)

        @pl.when(b == 0)
        def _():
            dq_ref[...] = jnp.zeros(dq_ref.shape, jnp.float32)
            for h in range(ratio):
                both = g_ref[h, HEAD_DIM:, :].astype(jnp.float32) * o_ref[h]
                delta[h] = jnp.broadcast_to(jnp.sum(both, axis=0, keepdims=True), (8, rows))

        def block(partial):
            pair = kv_ref[0, 0]
            turned = pair.T[:HEAD_DIM, :]
            for h in range(ratio):
                for r in range(0, rows, wide):
                    here = slice(r, r + wide)
                    q_now = q_ref[h, :, here]
                    g_now = g_ref[h, :, here]
                    scores = jnp.dot(pair, q_now, preferred_element_type=jnp.float32)
                    probs = jnp.exp(scores - log_ref[h, 0:1, here])
                    if partial:
                        keys = b * KEYS + lax.broadcasted_iota(jnp.int32, scores.shape, 0)
                        mine = meta_ref[2] + r + lax.broadcasted_iota(jnp.int32, scores.shape, 1)
                        visible = (keys >= start_ref[0:1, here]) & (keys <= mine)
                        probs = jnp.where(visible, probs, 0.0)
                    grads = jnp.dot(pair, g_now, preferred_element_type=jnp.float32)
                    low_grads = (probs * (grads - delta[h, 0:1, here])).astype(jnp.bfloat16)
                    change = lax.dot_general(
                        probs.astype(jnp.bfloat16), g_now, NT, preferred_element_type=jnp.float32
                    ) + lax.dot_general(low_grads, q_now, NT, preferred_element_type=jnp.float32)
                    if h == 0 and r == 0:
                        sums[...] = change
                    else:
                        sums[...] += change
                    dq_ref[h, :, here] += jnp.dot(turned, low_grads, preferred_element_type=jnp.float32)
            dkv_ref[0, 0] = sums[...].astype(jnp.bfloat16)

        needed = (b >= meta_ref[0]) & (b < meta_ref[1])
        partial = ((b + 1) * KEYS > meta_ref[2]) | (b * KEYS < meta_ref[3])

        @pl.when(needed & partial)
        def _():
            block(True)

        @pl.when(needed & jnp.logical_not(partial))
        def _():
            block(False)

        @pl.when(jnp.logical_not(needed))
        def _():
            dkv_ref[0, 0] = jnp.zeros((KEYS, PAIR), jnp.bfloat16)

    heads = lambda b, m: (group, 0, 0)
    return pl.pallas_call(
        pinned(kernel, 7, after),
        grid_spec=pltpu.PrefetchScalarGridSpec(
            num_scalar_prefetch=1,
            grid=(blocks,),
            in_specs=[
                pl.BlockSpec((ratio, PAIR, rows), heads),
                pl.BlockSpec((ratio, PAIR, rows), heads),
                pl.BlockSpec((1, 1, KEYS, PAIR), lambda b, m: (b, group, 0, 0)),
                pl.BlockSpec((ratio, 8, rows), heads),
                pl.BlockSpec((ratio, HEAD_DIM, rows), heads),
                pl.BlockSpec((8, rows), lambda b, m: (0, 0)),
            ] + pins(after),
            out_specs=[
                pl.BlockSpec((1, 1, KEYS, PAIR), lambda b, m: (b, 0, 0, 0)),
                pl.BlockSpec((ratio, HEAD_DIM, rows), lambda b, m: (0, 0, 0)),
            ],
            scratch_shapes=[
                pltpu.VMEM((ratio, 8, rows), jnp.float32),
                pltpu.VMEM((KEYS, PAIR), jnp.float32),
            ],
        ),
        out_shape=[
            jax.ShapeDtypeStruct((blocks, 1, KEYS, PAIR), jnp.bfloat16),
            jax.ShapeDtypeStruct((ratio, HEAD_DIM, rows), jnp.float32),
        ],
        compiler_params=pltpu.CompilerParams(vmem_limit_bytes=48 * 2**20),
        cost_estimate=pl.CostEstimate(flops=2 * 10**10, bytes_accessed=2**23, transcendentals=2**23),
        name="attend_back",
    )(meta, q_wide, g_wide, kv, logs, mixed, starts, *after)


def scatter_span(value, span, fast):
    if not fast:
        return lax.psum_scatter(value, span, scatter_dimension=0).astype(jnp.float32)
    flow = Flow(scatter_stages(value))
    while flow.sends:
        flow.go()
    return flow.result


def scatter_stages(value):
    _, y, x, c = (lax.axis_index(name) for name in GRID)
    value = value.reshape((2, 2, 2) + value.shape[1:])
    for name, place, axis in (("c", c, 2), ("y", y, 0), ("x", x, 0)):
        send = lax.dynamic_index_in_dim(value, 1 - place, axis, keepdims=False)
        (arrived,) = yield [(send, name, SWAP)]
        keep = lax.dynamic_index_in_dim(value, place, axis, keepdims=False)
        value = keep.astype(jnp.float32) + arrived.astype(jnp.float32)
        if name != "x":
            value = value.astype(jnp.bfloat16)
    return value


def plane_stages(value):
    for pairs in ([(0, 1), (1, 0), (2, 3), (3, 2)], [(0, 2), (2, 0), (1, 3), (3, 1)]):
        (other,) = yield [(value, "z", pairs)]
        value = value + other
    return value


def offsets_of():
    places, at = {}, 0
    for name_key, extent in layout():
        places[name_key] = (at, extent)
        at += math.prod(extent)
    return places


def early_weights(params):
    places = offsets_of()
    buffers, spread_flow, (slots, all_slots), where = gather_lines(params)
    spread_flow.go()
    names = (W_QUERY, W_KEY, W_VALUE, W_ATTN_OUT, W_GATE_SSM, W_X_SSM, W_B_C)
    misc_at = places[W_STEP][0]
    first = unpack_lines(
        buffers[:16], slots, where, [flat_segment(name_key) for name_key in names] + [(0, 16, LINE), (misc_at, 288, LINE)]
    )
    weights = dict(zip(names, first))
    weights[NORM_ATTN] = first[-2].reshape(-1)[:D]
    misc = first[-1].reshape(-1)
    for name_key in (W_STEP,) + small_names[1:-1]:
        at, extent = places[name_key]
        weights[name_key] = misc[at - misc_at : at - misc_at + math.prod(extent)].reshape(extent)
    return weights, spread_flow, (buffers, all_slots, where)


def flat_segment(name_key):
    at, extent = offsets_of()[name_key]
    return (at, extent[0], extent[1])


def late_weights(held, after):
    buffers, slots, where = held
    names = (W_SSM_OUT, W_GATE, W_UP_PROJ, W_DOWN)
    norm_at = offsets_of()[NORM_FFN][0]
    second = unpack_lines(
        buffers, slots, where, [flat_segment(name_key) for name_key in names] + [(norm_at, 16, LINE)], after
    )
    weights = dict(zip(names, second))
    weights[NORM_FFN] = second[-1].reshape(-1)[norm_at % LINE : norm_at % LINE + D]
    return weights


def pack_late(gate, up, down, ssm_low, grad_branch, grad_norm_ffn, after):
    places = offsets_of()
    out_at = places[W_SSM_OUT][0]
    lane = places[W_GATE][0] % LINE
    boundary = 2 * PLANE * LINE
    tail_from = (boundary - out_at) // D
    tail = matmul_left_t(ssm_low[:, tail_from:], grad_branch).reshape(-1)
    tail = tail[boundary - out_at - tail_from * D :]
    head = jnp.concatenate([jnp.zeros((14 * LINE,), jnp.float32), tail, grad_norm_ffn])
    head_rows = head.shape[0] // LINE
    carry = jnp.zeros((8, LINE), jnp.float32).at[7, :lane].set(head[head_rows * LINE :])
    head = head[: head_rows * LINE].reshape(head_rows, LINE).astype(jnp.bfloat16)
    return pack_lines(
        None, 2 * PLANE + 32, head_rows, [gate, up, down], lane, 0, [(head, 0)], carry, 48, after
    )


def pack_out(ssm_low, grad_branch, after):
    out_at = offsets_of()[W_SSM_OUT][0]
    first_row = (8 + out_at // LINE) // 16 * 16
    rows = first_row + SSM_HEADS * SSM_DIM * D // LINE
    return pack_lines(
        None, rows, first_row, [(ssm_low, grad_branch)], out_at % LINE, (8 + out_at // LINE) % 8, [],
        jnp.zeros((8, LINE), jnp.float32), 0, after,
    )


def pack_ssm(target, segments, small, ssm_low, grad_branch, after):
    places = offsets_of()
    misc = [small[name_key].reshape(-1) for name_key in (W_STEP,) + small_names[1:-1]]
    count = sum(part.shape[0] for part in misc)
    misc_rows = (count // LINE + 16) // 16 * 16
    opening = matmul_left_t(ssm_low[:, :16], grad_branch).reshape(-1)
    misc = jnp.concatenate(misc + [opening[: misc_rows * LINE - count]])
    misc = misc.reshape(misc_rows, LINE).astype(jnp.bfloat16)
    first_row = 8 + places[W_ATTN_OUT][0] // LINE
    return pack_lines(
        target, target.shape[0], first_row, segments, 0, 0, [(misc, 8 + places[W_STEP][0] // LINE)], None, 0, after
    )


def pack_qkv(segments, attended, grad_branch, grad_norm_attn, after):
    places = offsets_of()
    out_row = 8 + places[W_ATTN_OUT][0] // LINE
    rows = (8 + SHARD) // 16 * 16 + 8 * PIECE
    closing = matmul_left_t(attended[:, :16], grad_branch).reshape(-1, LINE)
    closing = closing[: rows - out_row].astype(jnp.bfloat16)
    opening = jnp.concatenate([jnp.zeros((8, LINE), jnp.float32), grad_norm_attn.reshape(-1, LINE)]).astype(jnp.bfloat16)
    return pack_lines(
        None, rows, 16, segments, 0, 0, [(opening, 0), (closing, out_row)], None, 0, after
    )


def own_lines(early, late, corner):
    z, y, x, c = (lax.axis_index(name) for name in GRID)
    place = 4 * y + 2 * x + c
    shard = SHARD * place
    start = jnp.where(z < 2, (8 + shard) % 16, (14 + shard) % 16)
    lines = jnp.where(z < 2, early, late)
    lines = jnp.where((z == 0) & (place < 2), corner[:WIN], lines)
    lines = lax.dynamic_slice(lines, (start, 0), (SHARD, LINE)).astype(jnp.float32)
    return lines.reshape(-1)


def body(span, group, fast, tokens, params, cotangent, offsets):
    rows_dev = tokens.shape[0]
    group_rows = rows_dev * lax.axis_size(span)
    all_rows = group_rows * lax.axis_size(group)
    ssm_inner = SSM_HEADS * SSM_DIM
    score_scale = HEAD_DIM ** (-0.5)
    bounds = offsets[0]
    my_start = lax.axis_index(span) * rows_dev
    row_index = my_start + jnp.arange(rows_dev, dtype=jnp.int32)
    seq_id, positions = sequence_info(row_index, bounds)
    first_start = row_index[0] - positions[0]
    last_row = my_start + rows_dev - 1
    cosine, sine = rotary_tables(positions)
    if fast:
        weights, spread_flow, held = early_weights(params)
    else:
        weights = unpack(lax.all_gather(params, group + span, axis=0, tiled=True))
    small_f32 = {name_key: weights[name_key].astype(jnp.float32) for name_key in small_names[:-1]}
    x_rows = tokens.astype(jnp.float32)
    normed_one, norm_one_back = jax.vjp(rms_norm, x_rows, small_f32[NORM_ATTN])
    hidden = normed_one.astype(jnp.bfloat16)
    across = lambda weight: lax.dot_general(
        weight, hidden, (((0,), (1,)), ((), ())), preferred_element_type=jnp.float32
    )
    q_rot = rotate(across(weights[W_QUERY]), cosine, sine, HEADS_Q).astype(jnp.bfloat16)
    k_rot = rotate(across(weights[W_KEY]), cosine, sine, HEADS_KV).astype(jnp.bfloat16)
    value_low = across(weights[W_VALUE]).astype(jnp.bfloat16).reshape(HEADS_KV, HEAD_DIM, rows_dev)
    kv_mine = jnp.concatenate([k_rot, value_low], axis=1).transpose(0, 2, 1)
    row_starts = row_index - positions
    kv_local = kv_mine.reshape(HEADS_KV, rows_dev, PAIR)
    xbc = jnp.concatenate(
        [matmul(hidden, weights[W_X_SSM]), matmul(hidden, weights[W_B_C])], axis=1
    )
    step_raw = matmul(hidden, weights[W_STEP])
    q_wide = jnp.pad(q_rot * jnp.bfloat16(score_scale), ((0, 0), (0, HEAD_DIM), (0, 0)))
    rim_source = xbc[rows_dev - 8 :]
    if fast:
        (rim_source,) = fence([rim_source], [q_wide])
    rim_rows = passed_along(rim_source, span, 1)
    ssm_meta = jnp.concatenate([my_start[None], row_starts[CHUNK - 1 :: CHUNK]]).astype(jnp.int32)
    conv_bias = small_f32[CONV_BIAS][None, :]
    convolve = lambda after: conv_forward(
        xbc, rim_rows, small_f32[CONV_WEIGHT], conv_bias, ssm_meta, row_starts[:, None], after
    )
    if fast:
        key_blocks = lax.all_gather(kv_local, span)
        conv_values = convolve(())
    else:
        conv_values = convolve(())
    step_in = step_raw.T + small_f32[STEP_BIAS][:, None]
    step_rows = jax.nn.softplus(step_in)
    decay = -jnp.exp(small_f32[DECAY_LOG])
    logs_step = step_rows * decay[:, None]
    order = jnp.arange(rows_dev)
    upto = (order[:, None] <= order[None, :]).astype(jnp.float32)
    cumul = jnp.dot(logs_step, upto, precision=highest)
    chunk_cum = jnp.dot(
        logs_step.reshape(-1, CHUNK), upto[:CHUNK, :CHUNK], precision=highest
    ).reshape(SSM_HEADS, rows_dev)
    went_on = row_starts < my_start
    entry_rows = jnp.where(went_on[None, :], jnp.exp(cumul), 0.0)
    in_last = row_index >= row_starts[rows_dev - 1]
    tail_rows = jnp.exp(jnp.where(in_last[None, :], cumul[:, -1:] - cumul, masked_score))
    carry_all = entry_rows[:, -1]
    summarize = lambda after: weighted_state(conv_values, PAIRS, conv_values, tail_rows * step_rows, after)
    meta = jnp.stack(
        [first_start // KEYS, last_row // KEYS + 1, my_start, row_starts[rows_dev - 1]]
    ).astype(jnp.int32)
    start_row = jnp.broadcast_to(row_starts[None, :], (8, rows_dev))
    if fast:
        (local_state,) = bracket(summarize, [spread_flow])
        scan = Flow(scan_stages(carry_all, local_state, False))
        (gate_in,) = fence([hidden], scan.values())
        gate_ssm = matmul(gate_in, weights[W_GATE_SSM])
        scan.go()
        (gate_ssm,) = fence([gate_ssm], scan.values())
        scan.go()
        mixed, logs = bracket(
            lambda after: attention_forward(
                q_wide, key_blocks, meta, start_row, (*after, gate_ssm, *spread_flow.values())
            ),
            [scan],
        )
        spread_flow.go()
        state_in = scan.result
    else:
        gate_ssm = matmul(hidden, weights[W_GATE_SSM])
        key_blocks = lax.all_gather(kv_local, span)
        if rows_dev != KEYS:
            key_blocks = key_blocks.transpose(1, 0, 2, 3).reshape(HEADS_KV, -1, KEYS, PAIR).transpose(1, 0, 2, 3)
        state_in = scan_states(carry_all, summarize(()), span, fast, False)
        mixed, logs = attention_forward(q_wide, key_blocks, meta, start_row)
    attended = mixed.astype(jnp.bfloat16).reshape(HEADS_Q * HEAD_DIM, rows_dev).T
    attn_out = matmul(attended, weights[W_ATTN_OUT])
    skip_wide = jnp.repeat(small_f32[SKIP_GAIN], SSM_DIM)[None, :]
    ssm_y = ssm_forward(
        conv_values, chunk_cum, step_rows, state_in, skip_wide, ssm_meta, row_starts[:, None], start_row
    )
    normed_ssm, gnorm_back = jax.vjp(gated_norm, ssm_y, gate_ssm, small_f32[NORM_SSM])
    ssm_low = normed_ssm.astype(jnp.bfloat16)
    if fast:
        held = (held[0] + spread_flow.result,) + held[1:]
        weights.update(late_weights(held, [ssm_y]))
    small_f32[NORM_FFN] = weights[NORM_FFN].astype(jnp.float32)
    ssm_out = matmul(ssm_low, weights[W_SSM_OUT])
    middle = x_rows + attn_out + ssm_out
    normed_two, norm_two_back = jax.vjp(rms_norm, middle, small_f32[NORM_FFN])
    hidden_two = normed_two.astype(jnp.bfloat16)
    gate_ffn = matmul(hidden_two, weights[W_GATE])
    upper = matmul(hidden_two, weights[W_UP_PROJ])
    activation_f32, swiglu_back = jax.vjp(swiglu, gate_ffn, upper)
    activation = activation_f32.astype(jnp.bfloat16)
    ffn_out = matmul(activation, weights[W_DOWN])
    result = middle + ffn_out
    squares = jnp.stack(
        [
            jnp.sum(result * result),
            jnp.sum(attn_out * attn_out),
            jnp.sum(ssm_out * ssm_out),
            jnp.sum(ffn_out * ffn_out),
        ]
    )
    grad_out = cotangent.astype(jnp.float32)
    grad_activation = matmul_right_t(cotangent, weights[W_DOWN])
    grad_gate_f32, grad_upper_f32 = swiglu_back(grad_activation)
    grad_gate = grad_gate_f32.astype(jnp.bfloat16)
    grad_upper = grad_upper_f32.astype(jnp.bfloat16)
    grad_hidden_two = matmul_right_t(grad_gate, weights[W_GATE]) + matmul_right_t(
        grad_upper, weights[W_UP_PROJ]
    )
    grad_middle_norm, grad_norm_ffn = norm_two_back(grad_hidden_two)
    grad_middle = grad_out + grad_middle_norm
    grad_branch = grad_middle.astype(jnp.bfloat16)
    grad_attended = matmul_right_t(weights[W_ATTN_OUT], grad_branch).astype(jnp.bfloat16)
    grad_ssm_low = matmul_right_t(grad_branch, weights[W_SSM_OUT])
    grad_ssm_y, grad_gate_ssm_f32, grad_norm_ssm = gnorm_back(grad_ssm_low)
    grad_state_local = weighted_state(conv_values, PAIRS + 1, grad_ssm_y, entry_rows)
    if fast:
        scan = Flow(scan_stages(carry_all, grad_state_local, True, squares)).go()
        (late,) = bracket(
            lambda after: pack_late(
                (hidden_two, grad_gate), (hidden_two, grad_upper), (activation, cotangent),
                ssm_low, grad_branch, grad_norm_ffn, after,
            ),
            [scan],
        )
        late_flow = Flow(reduce_stages(late, 1, 14))
        (grad_branch_low,) = fence([grad_branch], scan.values() + late_flow.values())
        early = pack_out(ssm_low, grad_branch_low, ())
        scan.go()
        grad_state_out, squares = scan.result
        (early,) = fence([early], [grad_state_out])
        late_flow.go()
        (early,) = fence([early], late_flow.values())
        stats_flow = Flow(plane_stages(squares))

        def around(call):
            out = bracket(lambda after: call((*after, *stats_flow.values())), [late_flow])
            stats_flow.go(out[:1])
            return out

    else:
        grad_state_out = scan_states(carry_all, grad_state_local, span, fast, True)
        around = lambda call: call(())
    grad_x, grad_b, grad_c, grad_small = around(
        lambda after: ssm_backward(
            conv_values, grad_ssm_y, chunk_cum, step_rows, state_in, grad_state_out, skip_wide, ssm_meta, start_row,
            after,
        )
    )
    grad_direct = grad_small[:, 0:2].reshape(SSM_HEADS, rows_dev)
    grad_logs = grad_small[:, 2:4].reshape(SSM_HEADS, rows_dev)
    grad_decay_log = decay * jnp.sum(step_rows * grad_logs, axis=1)
    grad_step_rows = (grad_direct + decay[:, None] * grad_logs) * jax.nn.sigmoid(step_in)
    grad_step_bias = jnp.sum(grad_step_rows, axis=1)
    grad_step_raw_f32 = grad_step_rows.T
    grad_skip_gain = jnp.sum(grad_small[:, 4, : 2 * SSM_DIM].reshape(SSM_HEADS, SSM_DIM), axis=1)
    grad_main, grad_tail, grad_edge, grad_taps = around(
        lambda after: conv_backward(
            grad_x, grad_b, grad_c, xbc, rim_rows, small_f32[CONV_WEIGHT], conv_bias, ssm_meta,
            row_starts[:, None], after,
        )
    )
    grad_conv_weight = grad_taps[:CONV]
    grad_conv_bias = grad_taps[CONV]
    rim_back = passed_along(grad_edge, span, -1)
    grad_tail = grad_tail + jnp.pad(rim_back, ((8, 0), (0, 0)))
    grad_xbc = lax.dynamic_update_slice(grad_main, grad_tail.astype(jnp.bfloat16), (rows_dev - 16, 0))
    grad_gate_ssm = grad_gate_ssm_f32.astype(jnp.bfloat16)
    grad_step_raw = grad_step_raw_f32.astype(jnp.bfloat16)
    grad_w_step = matmul_left_t(hidden, grad_step_raw)
    grad_hidden_ssm = (
        matmul_right_t(grad_gate_ssm, weights[W_GATE_SSM])
        + matmul_right_t(grad_xbc[:, :ssm_inner], weights[W_X_SSM])
        + matmul_right_t(grad_xbc[:, ssm_inner:], weights[W_B_C])
        + matmul_right_t(grad_step_raw, weights[W_STEP])
    )
    small = {
        W_STEP: grad_w_step,
        CONV_WEIGHT: grad_conv_weight,
        CONV_BIAS: grad_conv_bias,
        STEP_BIAS: grad_step_bias,
        DECAY_LOG: grad_decay_log,
        SKIP_GAIN: grad_skip_gain,
        NORM_SSM: grad_norm_ssm,
        NORM_FFN: grad_norm_ffn,
    }
    parts = []
    if fast:
        early = pack_ssm(
            early,
            [
                (attended, grad_branch), (hidden, grad_gate_ssm),
                (hidden, grad_xbc[:, :ssm_inner]), (hidden, grad_xbc[:, ssm_inner:]),
            ],
            small, ssm_low, grad_branch, late_flow.values(),
        )
        early_flow = Flow(reduce_stages(early, 0, 8))
        (grad_attended,) = fence([grad_attended], early_flow.values() + late_flow.values())
        around = lambda call: bracket(call, [early_flow])
    g_wide = jnp.pad(grad_attended.reshape(HEADS_Q, HEAD_DIM, rows_dev), ((0, 0), (HEAD_DIM, 0), (0, 0)))
    if fast:
        early_flow.go()
        (g_wide,) = fence([g_wide], early_flow.values())
    for group_at in range(HEADS_KV):
        after_part = [part[1] for part in parts]
        if fast and group_at == 0:
            after_part = late_flow.values()
        parts.append(
            around(
                lambda after: attention_backward(
                    q_wide, g_wide, key_blocks, logs, mixed, meta, start_row, group_at, (*after, *after_part)
                )
            )
        )
    grad_kv = jnp.concatenate([part[0] for part in parts], axis=1)
    grad_q_turned = jnp.concatenate([part[1] for part in parts], axis=0)
    if rows_dev != KEYS:
        grad_kv = grad_kv.transpose(1, 0, 2, 3).reshape(HEADS_KV, -1, rows_dev, PAIR).transpose(1, 0, 2, 3)
    if fast:
        late_flow.go([parts[-1][1]])
        scatter = Flow(scatter_stages(grad_kv))
        (grad_q_turned,) = fence([grad_q_turned], scatter.values() + early_flow.values() + late_flow.values())
    turned_back = rotate(grad_q_turned * score_scale, cosine, -sine, HEADS_Q).astype(jnp.bfloat16)
    grad_query_low = turned_back.reshape(HEADS_Q * HEAD_DIM, rows_dev).T
    if fast:
        scatter.go()
        early_flow.go()
        (grad_query_low,) = fence([grad_query_low], scatter.values() + early_flow.values())
    grad_hidden = grad_hidden_ssm + matmul_right_t(grad_query_low, weights[W_QUERY])
    if fast:
        scatter.go()
        (grad_hidden,) = fence([grad_hidden], scatter.values())
        scatter.go()
        grad_kv_mine = scatter.result
    else:
        grad_kv_mine = scatter_span(grad_kv, span, fast)
    grad_kv_mine = grad_kv_mine.transpose(0, 2, 1)
    grad_key_low = rotate(grad_kv_mine[:, :HEAD_DIM], cosine, -sine, HEADS_KV).astype(jnp.bfloat16)
    grad_key_low = grad_key_low.reshape(HEADS_KV * HEAD_DIM, rows_dev).T
    grad_value_low = grad_kv_mine[:, HEAD_DIM:].astype(jnp.bfloat16).reshape(HEADS_KV * HEAD_DIM, rows_dev).T
    grad_hidden = (
        grad_hidden
        + matmul_right_t(grad_key_low, weights[W_KEY])
        + matmul_right_t(grad_value_low, weights[W_VALUE])
    )
    grad_x_norm, grad_norm_attn = norm_one_back(grad_hidden)
    grad_tokens = grad_middle + grad_x_norm
    if fast:
        corner = pack_qkv(
            [(hidden, grad_query_low), (hidden, grad_key_low), (hidden, grad_value_low)],
            attended, grad_branch, grad_norm_attn, early_flow.values(),
        )
        corner_flow = Flow(corner_stages(corner))
        for _ in range(3):
            corner_flow.go()
        early_flow.go()
        ((pieces, _, _), *_) = corner_flow.sends
        (pieces,) = fence([pieces], early_flow.values())
        corner_flow.sends = [(pieces, axis, pairs) for _, axis, pairs in corner_flow.sends]
        for flow in (early_flow, late_flow, corner_flow):
            while flow.sends:
                flow.go()
        stats = jnp.sqrt(stats_flow.result / (all_rows * D))
        grad_shard = own_lines(early_flow.result, late_flow.result, corner_flow.result)
        return (result.astype(jnp.bfloat16), grad_tokens, grad_shard, stats)
    small[NORM_ATTN] = grad_norm_attn
    stats = jnp.sqrt(lax.psum(squares, group + span) / (all_rows * D))
    pairs = {
        W_QUERY: (hidden, grad_query_low),
        W_KEY: (hidden, grad_key_low),
        W_VALUE: (hidden, grad_value_low),
        W_ATTN_OUT: (attended, grad_branch),
        W_GATE_SSM: (hidden, grad_gate_ssm),
        W_X_SSM: (hidden, grad_xbc[:, :ssm_inner]),
        W_B_C: (hidden, grad_xbc[:, ssm_inner:]),
        W_SSM_OUT: (ssm_low, grad_branch),
        W_GATE: (hidden_two, grad_gate),
        W_UP_PROJ: (hidden_two, grad_upper),
        W_DOWN: (activation, cotangent),
    }
    grad_dict = dict(small)
    for name_key, (left, right) in pairs.items():
        grad_dict[name_key] = matmul_left_t(left, right)
    flat_parts = [grad_dict[name_key].reshape(-1) for name_key, extent in layout()]
    used_entries = 0
    for part_array in flat_parts:
        used_entries += part_array.shape[0]
    flat_parts.append(jnp.zeros((params.shape[0] * lax.axis_size(group + span) - used_entries,), jnp.float32))
    grad_shard = lax.psum_scatter(
        jnp.concatenate(flat_parts), group + span, scatter_dimension=0, tiled=True
    )
    return (result.astype(jnp.bfloat16), grad_tokens, grad_shard, stats)


def solution(mesh):
    fast = (mesh.shape["group"], mesh.shape["span"]) == FAST
    if fast:
        mesh = Mesh(mesh.devices.reshape(4, 2, 2, 2), GRID)
        group, span = (GRID[:1], GRID[1:])
    else:
        group, span = (("group",), ("span",))

    def program(tokens, params, cotangent, offsets):
        return body(span, group, fast, tokens, params, cotangent, offsets)

    return jax.shard_map(
        program,
        mesh=mesh,
        in_specs=(P(group + span, None), P(group + span), P(group + span, None), P(group, None)),
        out_specs=(P(group + span, None), P(group + span, None), P(group + span), P()),
        check_vma=False,
    )
```

```python
import math

import jax
import jax.numpy as jnp
import numpy as np
from jax import lax
from jax.experimental import pallas as pl
from jax.experimental.pallas import tpu as pltpu
from jax.sharding import Mesh, PartitionSpec as P

D = 1024
HEADS_Q = 8
HEADS_KV = 2
HEAD_DIM = 64
SSM_HEADS = 24
SSM_DIM = 64
STATE = 128
CONV = 4
FF = 2048
(
    NORM_ATTN,
    W_QUERY,
    W_KEY,
    W_VALUE,
    W_ATTN_OUT,
    W_GATE_SSM,
    W_X_SSM,
    W_B_C,
    W_STEP,
    CONV_WEIGHT,
    CONV_BIAS,
    STEP_BIAS,
    DECAY_LOG,
    SKIP_GAIN,
    NORM_SSM,
    W_SSM_OUT,
    NORM_FFN,
    W_GATE,
    W_UP_PROJ,
    W_DOWN,
) = range(20)


epsilon = 1e-05
rope_base = 100000000000.0
masked_score = -1e30
highest = lax.Precision.HIGHEST
small_names = (
    NORM_ATTN,
    CONV_WEIGHT,
    CONV_BIAS,
    STEP_BIAS,
    DECAY_LOG,
    SKIP_GAIN,
    NORM_SSM,
    NORM_FFN,
)


def passed_along(value, axis, steps):
    count = lax.axis_size(axis)
    first, last = (max(0, -steps), min(count, count - steps))
    return lax.ppermute(value, axis, [(source, source + steps) for source in range(first, last)])


def prefix(value, axis, combine, identity):
    peers, place = (lax.axis_size(axis), lax.axis_index(axis))
    everything = jax.tree.map(
        lambda part, kind: lax.all_gather(part.astype(kind), axis),
        value,
        (jnp.bfloat16, jnp.bfloat16),
    )
    start = jax.tree.map(
        lambda part, zero: jnp.broadcast_to(jnp.asarray(zero, part.dtype), part.shape),
        value,
        identity,
    )

    def prefix_turn(k, before):
        reached = k < place
        new = combine(
            before, jax.tree.map(lambda part, own: part[k].astype(own.dtype), everything, value)
        )
        return jax.tree.map(lambda a, b: jnp.where(reached, a, b), new, before)

    return lax.fori_loop(0, peers, prefix_turn, start)


def carried_in(value, axis, combine, identity):
    peers, place = (lax.axis_size(axis), lax.axis_index(axis))
    everything = jax.tree.map(
        lambda part, kind: lax.all_gather(part.astype(kind), axis),
        value,
        jax.tree.map(lambda a: jnp.bfloat16 if a.dtype == jnp.float32 else a.dtype, value),
    )
    start = jax.tree.map(
        lambda part, zero: jnp.broadcast_to(jnp.asarray(zero, part.dtype), part.shape),
        value,
        identity,
    )

    def carried_turn(k, before):
        at = peers - 1 - k
        reached = at > place
        new = combine(
            before, jax.tree.map(lambda part, own: part[at].astype(own.dtype), everything, value)
        )
        return jax.tree.map(lambda a, b: jnp.where(reached, a, b), new, before)

    return lax.fori_loop(0, peers, carried_turn, start)


def layout():
    ssm_inner = SSM_HEADS * SSM_DIM
    channels = ssm_inner + 2 * STATE
    return [
        (NORM_ATTN, (D,)),
        (W_QUERY, (D, HEADS_Q * HEAD_DIM)),
        (W_KEY, (D, HEADS_KV * HEAD_DIM)),
        (W_VALUE, (D, HEADS_KV * HEAD_DIM)),
        (W_ATTN_OUT, (HEADS_Q * HEAD_DIM, D)),
        (W_GATE_SSM, (D, ssm_inner)),
        (W_X_SSM, (D, ssm_inner)),
        (W_B_C, (D, 2 * STATE)),
        (W_STEP, (D, SSM_HEADS)),
        (CONV_WEIGHT, (CONV, channels)),
        (CONV_BIAS, (channels,)),
        (STEP_BIAS, (SSM_HEADS,)),
        (DECAY_LOG, (SSM_HEADS,)),
        (SKIP_GAIN, (SSM_HEADS,)),
        (NORM_SSM, (ssm_inner,)),
        (W_SSM_OUT, (ssm_inner, D)),
        (NORM_FFN, (D,)),
        (W_GATE, (D, FF)),
        (W_UP_PROJ, (D, FF)),
        (W_DOWN, (FF, D)),
    ]


def unpack(flat_vector):
    unpacked = {}
    offset = 0
    for name_key, extent in layout():
        amount = math.prod(extent)
        unpacked[name_key] = flat_vector[offset : offset + amount].reshape(extent)
        offset += amount
    return unpacked


def matmul(left, right):
    return jnp.dot(left, right, preferred_element_type=jnp.float32)


def matmul_left_t(left, right):
    return lax.dot_general(
        left, right, (((0,), (0,)), ((), ())), preferred_element_type=jnp.float32
    )


def matmul_right_t(left, right):
    return lax.dot_general(
        left, right, (((1,), (1,)), ((), ())), preferred_element_type=jnp.float32
    )


def rms_norm(values, gain):
    return values * lax.rsqrt(jnp.mean(values * values, axis=-1, keepdims=True) + epsilon) * gain


def gated_norm(ssm_y, gate_ssm, gain):
    return rms_norm(ssm_y * jax.nn.silu(gate_ssm), gain)


def swiglu(gate_ffn, upper):
    return jax.nn.silu(gate_ffn) * upper


def sequence_info(row_index, bounds):
    starts = bounds[:-1]
    inside = row_index[:, None] >= starts[None, :]
    seq_id = jnp.sum(inside.astype(jnp.int32), axis=1) - 1
    seq_start = jnp.max(jnp.where(inside, starts[None, :], 0), axis=1)
    return (seq_id, row_index - seq_start)


def rotary_tables(positions):
    half_dim = HEAD_DIM // 2
    freqs = jnp.exp(
        -jnp.arange(half_dim, dtype=jnp.float32) * (2.0 * math.log(rope_base) / HEAD_DIM)
    )
    angles = freqs[:, None] * positions.astype(jnp.float32)[None, :]
    return (jnp.cos(angles), jnp.sin(angles))


def rotate(values, cosine, sine, heads):
    halves = values.reshape(heads, 2, HEAD_DIM // 2, -1)
    first_half, second_half = halves[:, 0], halves[:, 1]
    turned = jnp.stack(
        [first_half * cosine - second_half * sine, second_half * cosine + first_half * sine], axis=1
    )
    return turned.reshape(heads, HEAD_DIM, -1)


def add_rows(target, addend, first_row):
    current = lax.dynamic_slice_in_dim(target, first_row, addend.shape[0], 0)
    return lax.dynamic_update_slice_in_dim(target, current + addend, first_row, 0)


FAST = (4, 8)
LINE = 128
SHARD = 3082
SPAD = 3088
WIN = 3104
PLANE = 8 * SHARD
DEPTH = 4
TALL = {1: 1024, 2: 1024, 4: 512, 8: 256, 12: 128, 16: 128}
GRID = ("z", "y", "x", "c")
ZC = ("z", "c")
SWAP = [(0, 1), (1, 0)]


def zc_pairs(*pairs):
    return [(2 * a + c, 2 * b + c) for a, b, c in pairs]


def pinned(kernel, count, after):
    return lambda *refs: kernel(*refs[:count], *refs[count + len(after) :])


def pins(after):
    return [pl.BlockSpec(memory_space=pltpu.HBM)] * len(after)


class Flow:
    def __init__(self, stages):
        self.stages = stages
        self.sends = next(stages)
        self.result = None

    def values(self):
        return [value for value, _, _ in self.sends] or (list(self.result) if isinstance(self.result, list) else [self.result])

    def hold(self, after):
        held = fence(self.values(), after)
        self.sends = [(value, axis, pairs) for value, (_, axis, pairs) in zip(held, self.sends)]

    def go(self, after=()):
        arrived = [lax.ppermute(value, axis, pairs) for value, axis, pairs in self.sends]
        if after:
            arrived = fence(arrived, after)
        try:
            self.sends = self.stages.send(arrived)
        except StopIteration as stop:
            self.sends, self.result = [], stop.value
        return self


def fence(values, after):
    def kernel(*refs):
        del refs

    return pl.pallas_call(
        kernel,
        in_specs=pins(values) + pins(after),
        out_specs=pins(values),
        out_shape=[jax.ShapeDtypeStruct(value.shape, value.dtype) for value in values],
        input_output_aliases={k: k for k in range(len(values))},
        name="fence",
    )(*values, *after)


def bracket(call, flows):
    out = call([value for flow in flows for value in flow.values()])
    out = list(out) if isinstance(out, (list, tuple)) else [out]
    for flow in flows:
        flow.go()
    return fence(out, [v for flow in flows for v in flow.values()])


def gather_lines(params):
    z, y, x, c = (lax.axis_index(name) for name in GRID)
    lines = jnp.pad(params.reshape(SHARD, LINE), ((0, SPAD - SHARD), (0, 0)))
    sibling = lax.ppermute(lines, ZC, [(2 * k + 1 - k % 2, 2 * k + k % 2) for k in range(4)])
    buffers = []
    for part in range(2):
        here = jnp.where(c == part, lines, sibling)
        one = lax.ppermute(here, ZC, zc_pairs((0, 1, 0), (1, 2, 1)))
        side = lax.ppermute(here, ZC, zc_pairs((1, 0, 1)))
        two = lax.ppermute(one, ZC, zc_pairs((1, 2, 0), (2, 3, 1)))
        three = lax.ppermute(two, ZC, zc_pairs((2, 3, 0)))
        column = jnp.where(z == c, here, one + side + two + three)
        over_x = lax.ppermute(column, "x", SWAP)
        over_y = lax.ppermute(column, "y", SWAP)
        corner = lax.ppermute(over_y if part else over_x, "x" if part else "y", SWAP)
        local = [column, over_x, over_y, corner]
        buffers += [piece[None] for piece in local]
        buffers += [lax.ppermute(piece, "c", SWAP)[None] for piece in local]
    early = [(k, 0) for k in range(16)]
    here = jnp.where(c == 0, jnp.stack([lines, sibling]), jnp.stack([sibling, lines]))
    one = lax.ppermute(here, ZC, zc_pairs((2, 1, 0), (3, 2, 1)))
    side = lax.ppermute(here, ZC, zc_pairs((2, 3, 0)))
    two = lax.ppermute(one, ZC, zc_pairs((1, 0, 0), (2, 1, 1)))
    three = lax.ppermute(two, ZC, zc_pairs((1, 0, 1)))
    column = jnp.where(z == 2 + c, here, one + side + two + three)
    late = []
    for part in range(2):
        for first in (16, 21):
            late += [(first, part), (first + 1, part), (first + 2, part), (first + 3 + part, 0)]
    shard = np.arange(32)
    sz, sy, sx, sc = shard // 8, shard // 4 % 2, shard // 2 % 2, shard % 2
    away = jnp.where(sz % 2 == c, 0, 4)
    where = sc * 8 + away + 2 * (sy ^ y) + (sx ^ x) + 16 * (sz // 2)
    return buffers, Flow(spread_stages(column)), (early, early + late), where.astype(jnp.int32)


def spread_stages(column):
    over_x, over_y = yield [(column, "x", SWAP), (column, "y", SWAP)]
    corners = yield [(over_x[:1], "y", SWAP), (over_y[1:], "x", SWAP)]
    local = [column, over_x, over_y] + list(corners)
    return local + list((yield [(piece, "c", SWAP) for piece in local]))


def unpack_lines(buffers, slots, where, segments, after=()):
    jobs, starts = [], []
    reach = 0
    for offset, rows, columns in segments:
        per_row = columns // LINE
        lane, base = offset % LINE, offset // LINE
        if per_row == 1 and rows < 1024:
            lane, tall = 0, rows
        else:
            tall = TALL[per_row]
        starts.append(len(jobs))
        for k in range(rows // tall):
            jobs.append((base + k * tall * per_row, tall * per_row, 1 if lane else 0))
    window = max(job[1] for job in jobs) + 32
    table = np.zeros((len(jobs), 5), np.int32)
    for k, (line, count, extra) in enumerate(jobs):
        owner = line // SHARD
        inside = line - owner * SHARD
        begin = min(inside // 16 * 16, SPAD - window)
        crosses = int(line + count + extra > (owner + 1) * SHARD)
        table[k] = (owner, begin, begin - inside, crosses, (owner + 1) * SHARD - line)
    base_row = (int(-table[:, 2].min()) + 7) // 8 * 8
    table[:, 2] += base_row
    table[:, 4] += base_row
    room = int(max((table[:, 2] + window).max(), ((table[:, 4] + window) * table[:, 3]).max()))
    room = (room + 15) // 8 * 8
    total = len(jobs)
    count_buffers = len(buffers)
    shapes = []
    for offset, rows, columns in segments:
        per_row = columns // LINE
        tall = rows if per_row == 1 and rows < 1024 else TALL[per_row]
        shapes.append((rows, columns, tall, per_row, offset % LINE if tall != rows or per_row != 1 else 0))
    sizes = sorted({(tall, columns) for _, columns, tall, _, _ in shapes})

    def kernel(table_ref, where_ref, *refs):
        sources = refs[:count_buffers]
        outs = refs[count_buffers : count_buffers + len(segments)]
        rest = refs[count_buffers + len(segments) :]
        stages = dict(zip(sizes, rest))
        raw, flat, in_sem, out_sem = rest[len(sizes) :]
        step = pl.program_id(0)

        def fetch(job, slot):
            owner = table_ref[job, 0]
            begin = pl.multiple_of(table_ref[job, 1], 16)
            for b, (source, part) in enumerate(slots):

                @pl.when(where_ref[owner] == b)
                def _():
                    pltpu.make_async_copy(
                        sources[source].at[part, pl.ds(begin, window), :], raw.at[slot, 0], in_sem.at[slot, 0]
                    ).start()

            @pl.when(table_ref[job, 3] == 1)
            def _():
                for b, (source, part) in enumerate(slots):

                    @pl.when(where_ref[owner + 1] == b)
                    def _():
                        pltpu.make_async_copy(
                            sources[source].at[part, pl.ds(0, window), :], raw.at[slot, 1], in_sem.at[slot, 1]
                        ).start()

        def fetched(slot, half):
            return pltpu.make_async_copy(
                sources[0].at[0, pl.ds(0, window), :], raw.at[slot, half], in_sem.at[slot, half]
            )

        @pl.when(step == 0)
        def _():
            for k in range(min(DEPTH - 1, total)):
                fetch(k, k)

        @pl.when(step + DEPTH - 1 < total)
        def _():
            fetch(step + DEPTH - 1, lax.rem(step + DEPTH - 1, DEPTH))

        slot = lax.rem(step, DEPTH)
        fetched(slot, 0).wait()
        flat[pl.ds(table_ref[step, 2], window), :] = raw[slot, 0].astype(jnp.float32)

        @pl.when(table_ref[step, 3] == 1)
        def _():
            fetched(slot, 1).wait()
            flat[pl.ds(table_ref[step, 4], window), :] = raw[slot, 1].astype(jnp.float32)

        for index, (rows, columns, tall, per_row, lane) in enumerate(shapes):
            begin = starts[index]
            blocks = rows // tall
            stage = stages[(tall, columns)]

            @pl.when((step >= begin) & (step < begin + blocks))
            def _():
                block = step - begin
                side = lax.rem(block, DEPTH)

                def written(k, s):
                    return pltpu.make_async_copy(
                        stage.at[s],
                        outs[index].at[pl.ds(pl.multiple_of(k * tall, 16), tall), :],
                        out_sem.at[s],
                    )

                @pl.when(block >= DEPTH)
                def _():
                    written(block - DEPTH, side).wait()

                def tile(j):
                    picked = flat[pl.ds(base_row + j, tall, stride=per_row), :]
                    return pltpu.roll(picked, LINE - lane, 1) if lane else picked

                if lane:
                    lanes = lax.broadcasted_iota(jnp.int32, (tall, LINE), 1)
                    now = tile(0)
                    for j in range(per_row):
                        later = tile(j + 1)
                        stage[side, :, j * LINE : (j + 1) * LINE] = jnp.where(
                            lanes < LINE - lane, now, later
                        ).astype(jnp.bfloat16)
                        now = later
                else:
                    for j in range(per_row):
                        stage[side, :, j * LINE : (j + 1) * LINE] = tile(j).astype(jnp.bfloat16)
                written(block, side).start()

                @pl.when(block == blocks - 1)
                def _():
                    for back in reversed(range(min(DEPTH, blocks))):
                        written(block - back, lax.rem(block - back, DEPTH)).wait()

    return pl.pallas_call(
        pinned(kernel, 2 + count_buffers, after),
        grid_spec=pltpu.PrefetchScalarGridSpec(
            num_scalar_prefetch=2,
            grid=(total,),
            in_specs=[pl.BlockSpec(memory_space=pl.ANY)] * count_buffers + pins(after),
            out_specs=[pl.BlockSpec(memory_space=pl.ANY)] * len(segments),
            scratch_shapes=[pltpu.VMEM((DEPTH,) + size, jnp.bfloat16) for size in sizes]
            + [
                pltpu.VMEM((DEPTH, 2, window, LINE), jnp.bfloat16),
                pltpu.VMEM((room, LINE), jnp.float32),
                pltpu.SemaphoreType.DMA((DEPTH, 2)),
                pltpu.SemaphoreType.DMA((DEPTH,)),
            ],
        ),
        out_shape=[jax.ShapeDtypeStruct((rows, columns), jnp.bfloat16) for _, rows, columns in segments],
        compiler_params=pltpu.CompilerParams(vmem_limit_bytes=48 * 2**20),
        cost_estimate=pl.CostEstimate(flops=0, bytes_accessed=total * window * LINE * 4, transcendentals=0),
        name="unpack",
    )(jnp.asarray(table), where, *buffers, *after)


def pack_lines(target, target_rows, first_row, segments, lane, phase, extras, carry, tail_rows, after=()):
    tall = 256
    lefts, rights, plan = [], [], []
    left_of, right_of = {}, {}
    row = first_row
    begin = 0
    for left, right in segments:
        for value, seen, kept in ((left, left_of, lefts), (right, right_of, rights)):
            if id(value) not in seen:
                seen[id(value)] = len(kept)
                kept.append(value)
        blocks = left.shape[1] // tall
        plan.append((left_of[id(left)], right_of[id(right)], right.shape[1] // LINE, begin, blocks, row))
        begin += blocks
        row += left.shape[1] * right.shape[1] // LINE
    end_row = row
    total = begin
    biggest = max(entry[2] for entry in plan) * tall
    tokens = lefts[0].shape[0]
    count_left, count_right, count_extra = len(lefts), len(rights), len(extras)
    rolled = [jnp.roll(right, lane, axis=1) if lane else right for right in rights]
    carry_in = [carry] if lane else []
    targets = [] if target is None else [target]

    def left_spec(index):
        mine = [entry for entry in plan if entry[0] == index]

        def place(step):
            block = 0
            for _, _, _, start, blocks, _ in mine:
                block = jnp.where(step >= start, jnp.minimum(step - start, blocks - 1), block)
            return (0, block)

        return pl.BlockSpec((tokens, tall), place)

    def kernel(*refs):
        left_refs = refs[:count_left]
        right_refs = refs[count_left : count_left + count_right]
        at = count_left + count_right
        extra_refs = refs[at : at + count_extra]
        at += count_extra
        carry_refs = refs[at : at + len(carry_in)]
        at += len(carry_in) + len(targets)
        out = refs[at]
        flat, stage, shift, last, sems, extra_sems = refs[at + 1 :]
        step = pl.program_id(0)
        side = lax.rem(step, 2)

        def extra_copy(k):
            rows = extras[k][0].shape[0]
            return pltpu.make_async_copy(
                extra_refs[k], out.at[pl.ds(extras[k][1], rows), :], extra_sems.at[k]
            )

        @pl.when(step == 0)
        def _():
            for k in range(count_extra):
                extra_copy(k).start()
            if lane:
                shift[0:8, :] = carry_refs[0][...]
            if phase:
                flat[0:8, :] = jnp.zeros((8, LINE), jnp.float32)

        for left_at, right_at, per_row, start, blocks, row in plan:
            lines = per_row * tall

            def written(block, s, row=row, lines=lines):
                return pltpu.make_async_copy(
                    stage.at[s, pl.ds(0, lines), :],
                    out.at[pl.ds(pl.multiple_of(row + block * lines, 16), lines), :],
                    sems.at[s],
                )

            @pl.when((step >= start) & (step < start + blocks))
            def _():
                block = step - start
                if phase:

                    @pl.when(step > 0)
                    def _():
                        flat[0:8, :] = flat[lines : lines + 8, :]

                turned = left_refs[left_at][...].T
                lanes = lax.broadcasted_iota(jnp.int32, (tall, LINE), 1)
                for j0 in range(0, per_row, 2):
                    wide = min(2, per_row - j0)
                    tile = jnp.dot(
                        turned,
                        right_refs[right_at][:, j0 * LINE : (j0 + wide) * LINE],
                        preferred_element_type=jnp.float32,
                    )
                    for j in range(wide):
                        piece = tile[:, j * LINE : (j + 1) * LINE]
                        if lane and j0 + j == 0:
                            shift[8 : 8 + tall, :] = piece
                            piece = jnp.where(lanes < lane, shift[7 : 7 + tall, :], piece)
                            shift[0:8, :] = shift[tall : tall + 8, :]
                        if per_row == 1:
                            flat[phase : phase + tall, :] = piece
                        else:
                            flat[pl.ds(phase + j0 + j, tall, stride=per_row), :] = piece

                stage[side, 0:lines, :] = flat[0:lines, :].astype(jnp.bfloat16)
                written(block, side).start()

            @pl.when((step > start) & (step <= start + blocks))
            def _():
                written(step - start - 1, 1 - side).wait()

            if start + blocks == total:

                @pl.when(step == total - 1)
                def _():
                    written(blocks - 1, side).wait()

        @pl.when(step == total - 1)
        def _():
            if tail_rows:
                lanes = lax.broadcasted_iota(jnp.int32, (tail_rows, LINE), 1)
                rows_at = lax.broadcasted_iota(jnp.int32, (tail_rows, LINE), 0)
                final = jnp.broadcast_to(shift[7:8, :], (tail_rows, LINE))
                last[...] = jnp.where((rows_at == 0) & (lanes < lane), final, 0.0).astype(jnp.bfloat16)
                closing = pltpu.make_async_copy(
                    last, out.at[pl.ds(end_row, tail_rows), :], extra_sems.at[count_extra]
                )
                closing.start()
                closing.wait()
            for k in range(count_extra):
                extra_copy(k).wait()

    whole = [pl.BlockSpec(array.shape, lambda step: (0, 0)) for array in rolled]
    flops = sum(2 * tokens * entry[4] * tall * entry[2] * LINE for entry in plan)
    inputs = count_left + count_right + count_extra + len(carry_in) + len(targets)
    return pl.pallas_call(
        pinned(kernel, inputs, after),
        grid=(total,),
        in_specs=[left_spec(k) for k in range(count_left)]
        + whole
        + [pl.BlockSpec(array.shape, lambda step: (0, 0)) for array, _ in extras]
        + [pl.BlockSpec(array.shape, lambda step: (0, 0)) for array in carry_in]
        + [pl.BlockSpec(memory_space=pl.ANY)] * len(targets)
        + pins(after),
        out_specs=pl.BlockSpec(memory_space=pl.ANY),
        out_shape=jax.ShapeDtypeStruct((target_rows, LINE), jnp.bfloat16),
        scratch_shapes=[
            pltpu.VMEM((biggest + 16, LINE), jnp.float32),
            pltpu.VMEM((2, biggest, LINE), jnp.bfloat16),
            pltpu.VMEM((tall + 8, LINE), jnp.float32),
            pltpu.VMEM((max(tail_rows, 16), LINE), jnp.bfloat16),
            pltpu.SemaphoreType.DMA((2,)),
            pltpu.SemaphoreType.DMA((count_extra + 1,)),
        ],
        input_output_aliases={count_left + count_right + count_extra + len(carry_in): 0} if targets else {},
        compiler_params=pltpu.CompilerParams(vmem_limit_bytes=48 * 2**20),
        cost_estimate=pl.CostEstimate(flops=flops, bytes_accessed=total * biggest * LINE * 2, transcendentals=0),
        name="pack",
    )(*lefts, *rolled, *[array for array, _ in extras], *carry_in, *targets, *after)


def added(*parts):
    total = parts[0].astype(jnp.float32)
    for part in parts[1:]:
        total = total + part.astype(jnp.float32)
    return total.astype(jnp.bfloat16)


def reduce_stages(flat, batch, shift):
    z, y, x, c = (lax.axis_index(name) for name in GRID)
    length = PLANE + 32
    send = lax.dynamic_slice(flat, ((1 - c) * PLANE, 0), (length, LINE))
    (arrived,) = yield [(send, "c", SWAP)]
    chip = added(lax.dynamic_slice(flat, (c * PLANE, 0), (length, LINE)), arrived)

    def window(sy, sx, part):
        shard = sy * 4 + sx * 2 + part
        start = (shift + SHARD * shard) // 16 * 16
        return lax.dynamic_slice(chip, (start, 0), (WIN, LINE))

    away_0 = jnp.stack([window(1 - y, 0, 0), window(1 - y, 1, 0)])
    away_1 = jnp.stack([window(0, 1 - x, 1), window(1, 1 - x, 1)])
    home_0 = jnp.stack([window(y, 0, 0), window(y, 1, 0)])
    home_1 = jnp.stack([window(0, x, 1), window(1, x, 1)])
    got_0, got_1 = yield [(away_0, "y", SWAP), (away_1, "x", SWAP)]
    half_0, half_1 = added(home_0, got_0), added(home_1, got_1)
    pick = lambda value, at: lax.dynamic_index_in_dim(value, at, 0, keepdims=False)
    got_0, got_1 = yield [(pick(half_0, 1 - x), "x", SWAP), (pick(half_1, 1 - y), "y", SWAP)]
    columns = [added(pick(half_0, x), got_0), added(pick(half_1, y), got_1)]
    if batch == 0:
        hops = [((1, 0, 0), (2, 1, 1)), ((2, 0, 0), (3, 1, 1)), ((3, 0, 0), (0, 1, 1))]
    else:
        hops = [((1, 2, 0), (2, 3, 1)), ((0, 2, 0), (1, 3, 1)), ((3, 2, 0), (0, 3, 1))]
    if batch == 0:
        got = yield [(columns[0], ZC, zc_pairs(*hop)) for hop in hops]
        end = added(columns[0], *got)
        (column,) = fence(columns[1:], [end])
        got = yield [(column, ZC, zc_pairs(*hop)) for hop in hops]
        ends = [end, added(column, *got)]
    else:
        columns = jnp.stack(columns)
        got = yield [(columns, ZC, zc_pairs(*hop)) for hop in hops]
        ends = added(columns, *got)
    mine = jnp.where(c == 0, ends[0], ends[1])
    other = jnp.where(c == 0, ends[1], ends[0])
    (handed,) = yield [(other, ZC, [(2 * k + k % 2, 2 * k + 1 - k % 2) for k in range(4)])]
    return jnp.where(c == z % 2, mine, handed)


PIECE = 400


def corner_stages(flat):
    z, y, x, c = (lax.axis_index(name) for name in GRID)
    length = 8 * PIECE
    second = (8 + SHARD) // 16 * 16
    take = lambda at: lax.dynamic_slice(flat, (at * second, 0), (length, LINE))
    (arrived,) = yield [(take(1 - c), "c", SWAP)]
    chip = added(take(c), arrived).reshape(2, 2, 2, PIECE, LINE)
    pick = lambda value, at: lax.dynamic_index_in_dim(value, at, 0, keepdims=False)
    got = yield [(pick(chip[0], 1 - x), "x", SWAP), (pick(chip[1], 1 - y), "y", SWAP)]
    halves = [added(pick(chip[0], x), got[0]), added(pick(chip[1], y), got[1])]
    got = yield [(pick(halves[0], 1 - y), "y", SWAP), (pick(halves[1], 1 - x), "x", SWAP)]
    pieces = jnp.stack([added(pick(halves[0], y), got[0]), added(pick(halves[1], x), got[1])])
    got = yield [(pieces, "z", [(k, 0)]) for k in (1, 2, 3)]
    pieces = added(pieces, *got)
    got = yield [(pieces[0], "y", [(1, 0)]), (pieces[1], "x", [(1, 0)])]
    halves = [jnp.stack([pieces[0], got[0]]), jnp.stack([pieces[1], got[1]])]
    got = yield [(halves[0], "x", [(1, 0)]), (halves[1], "y", [(1, 0)])]
    return jnp.stack([halves[0], got[0], halves[1], got[1]]).reshape(length, LINE)


CHUNK = 128
NT = (((1,), (1,)), ((), ()))
TN = (((0,), (0,)), ((), ()))
INNER = SSM_HEADS * SSM_DIM
PAIRS = SSM_HEADS // 2


def spread(rows_a, rows_b):
    length = rows_a.shape[1]
    tall = jnp.concatenate(
        [jnp.broadcast_to(rows_a, (SSM_DIM, length)), jnp.broadcast_to(rows_b, (SSM_DIM, length))], axis=0
    )
    return tall.T


CHANNELS = INNER + 2 * STATE
LANES = 2 * SSM_DIM
COLUMNS = CHANNELS // LANES


def conv_masks(masks, start_ref, first, rows):
    place = first + lax.broadcasted_iota(jnp.int32, (rows, LANES), 0) - start_ref[...]
    for reach in range(1, CONV):
        masks[reach - 1] = jnp.where(place >= reach, 1.0, 0.0)


def conv_parts(ext, weight_ref, bias_ref, masks, rows):
    windows = []
    total = bias_ref[...]
    for tap in range(CONV):
        reach = CONV - 1 - tap
        window = ext[8 - reach : 8 - reach + rows, :]
        if reach:
            window = window * masks[reach - 1]
        windows.append(window)
        total = total + window * weight_ref[tap : tap + 1, :]
    return windows, total


def conv_forward(xbc, rim, weight, bias, meta, start_column, after=()):
    rows = xbc.shape[0]

    def kernel(meta_ref, x_ref, rim_ref, weight_ref, bias_ref, start_ref, out_ref, ext, masks):
        @pl.when(pl.program_id(0) == 0)
        def _():
            conv_masks(masks, start_ref, meta_ref[0], rows)

        ext[0:8, :] = rim_ref[...]
        ext[8:, :] = x_ref[...]
        _, total = conv_parts(ext, weight_ref, bias_ref, masks, rows)
        out_ref[...] = total * jax.nn.sigmoid(total)

    lanes = lambda i, m: (0, i)
    return pl.pallas_call(
        pinned(kernel, 6, after),
        grid_spec=pltpu.PrefetchScalarGridSpec(
            num_scalar_prefetch=1,
            grid=(COLUMNS,),
            in_specs=[
                pl.BlockSpec((rows, LANES), lanes),
                pl.BlockSpec((8, LANES), lanes),
                pl.BlockSpec((CONV, LANES), lanes),
                pl.BlockSpec((1, LANES), lanes),
                pl.BlockSpec((rows, 1), lambda i, m: (0, 0)),
            ] + pins(after),
            out_specs=pl.BlockSpec((rows, LANES), lanes),
            scratch_shapes=[
                pltpu.VMEM((rows + 8, LANES), jnp.float32),
                pltpu.VMEM((CONV - 1, rows, LANES), jnp.float32),
            ],
        ),
        out_shape=jax.ShapeDtypeStruct((rows, CHANNELS), jnp.float32),
        cost_estimate=pl.CostEstimate(flops=10**9, bytes_accessed=rows * CHANNELS * 8, transcendentals=0),
        name="conv",
    )(meta, xbc, rim, weight, bias, start_column, *after)


def conv_backward(dx, db, dc, xbc, rim, weight, bias, meta, start_column, after=()):
    rows = xbc.shape[0]

    def kernel(meta_ref, dx_ref, db_ref, dc_ref, x_ref, rim_ref, weight_ref, bias_ref, start_ref,
               low_ref, tail_ref, edge_ref, small_ref, ext, upper, masks):
        @pl.when(pl.program_id(0) == 0)
        def _():
            conv_masks(masks, start_ref, meta_ref[0], rows)
            upper[0:8, :] = jnp.zeros((8, LANES), jnp.float32)
            upper[8 + rows :, :] = jnp.zeros((8, LANES), jnp.float32)

        ext[0:8, :] = rim_ref[...]
        ext[8:, :] = x_ref[...]
        at = pl.program_id(0)
        arrived = jnp.where(at < PAIRS, dx_ref[...], jnp.where(at == PAIRS, db_ref[...], dc_ref[...]))
        windows, total = conv_parts(ext, weight_ref, bias_ref, masks, rows)
        gate = jax.nn.sigmoid(total)
        change = arrived * gate * (1.0 + total * (1.0 - gate))
        main = jnp.zeros((rows, LANES), jnp.float32)
        edge = jnp.zeros((8, LANES), jnp.float32)
        small_ref[...] = jnp.zeros((8, LANES), jnp.float32)
        small_ref[CONV : CONV + 1, :] = jnp.sum(change, axis=0, keepdims=True)
        for tap in range(CONV):
            reach = CONV - 1 - tap
            small_ref[tap : tap + 1, :] = jnp.sum(change * windows[tap], axis=0, keepdims=True)
            masked = change * masks[reach - 1] if reach else change
            upper[8 : 8 + rows, :] = masked * weight_ref[tap : tap + 1, :]
            main = main + upper[8 + reach : 8 + reach + rows, :]
            edge = edge + upper[reach : reach + 8, :]
        low_ref[...] = main.astype(jnp.bfloat16)
        tail_ref[...] = main[rows - 16 :, :]
        edge_ref[...] = edge

    lanes = lambda i, m: (0, i)
    whole = lambda i, m: (0, 0)
    return pl.pallas_call(
        pinned(kernel, 9, after),
        grid_spec=pltpu.PrefetchScalarGridSpec(
            num_scalar_prefetch=1,
            grid=(COLUMNS,),
            in_specs=[
                pl.BlockSpec((rows, LANES), lambda i, m: (0, jnp.minimum(i, PAIRS - 1))),
                pl.BlockSpec((rows, STATE), whole),
                pl.BlockSpec((rows, STATE), whole),
                pl.BlockSpec((rows, LANES), lanes),
                pl.BlockSpec((8, LANES), lanes),
                pl.BlockSpec((CONV, LANES), lanes),
                pl.BlockSpec((1, LANES), lanes),
                pl.BlockSpec((rows, 1), whole),
            ] + pins(after),
            out_specs=[
                pl.BlockSpec((rows, LANES), lanes),
                pl.BlockSpec((16, LANES), lanes),
                pl.BlockSpec((8, LANES), lanes),
                pl.BlockSpec((8, LANES), lanes),
            ],
            scratch_shapes=[
                pltpu.VMEM((rows + 8, LANES), jnp.float32),
                pltpu.VMEM((rows + 16, LANES), jnp.float32),
                pltpu.VMEM((CONV - 1, rows, LANES), jnp.float32),
            ],
        ),
        out_shape=[
            jax.ShapeDtypeStruct((rows, CHANNELS), jnp.bfloat16),
            jax.ShapeDtypeStruct((16, CHANNELS), jnp.float32),
            jax.ShapeDtypeStruct((8, CHANNELS), jnp.float32),
            jax.ShapeDtypeStruct((8, CHANNELS), jnp.float32),
        ],
        cost_estimate=pl.CostEstimate(flops=2 * 10**9, bytes_accessed=rows * CHANNELS * 10, transcendentals=0),
        name="conv_back",
    )(meta, dx, db, dc, xbc, rim, weight, bias, start_column, *after)


def weighted_state(left, left_block, values, weight_rows, after=()):
    rows = left.shape[0]

    def kernel(left_ref, value_ref, weight_ref, out_ref, turned):
        @pl.when(pl.program_id(0) == 0)
        def _():
            turned[...] = left_ref[...].T

        scaled = [(turned[...] * weight_ref[0, e : e + 1, :]).astype(jnp.bfloat16) for e in range(2)]
        both = jnp.dot(
            jnp.concatenate(scaled, axis=0), value_ref[...].astype(jnp.bfloat16), preferred_element_type=jnp.float32
        )
        low_lane = lax.broadcasted_iota(jnp.int32, (STATE, 2 * SSM_DIM), 1) < SSM_DIM
        out_ref[...] = jnp.where(low_lane, both[:STATE], both[STATE:])

    return pl.pallas_call(
        pinned(kernel, 3, after),
        grid=(PAIRS,),
        in_specs=[
            pl.BlockSpec((rows, STATE), lambda i: (0, left_block)),
            pl.BlockSpec((rows, 2 * SSM_DIM), lambda i: (0, i)),
            pl.BlockSpec((1, 2, rows), lambda i: (i, 0, 0)),
        ] + pins(after),
        out_specs=pl.BlockSpec((STATE, 2 * SSM_DIM), lambda i: (0, i)),
        out_shape=jax.ShapeDtypeStruct((STATE, INNER), jnp.float32),
        scratch_shapes=[pltpu.VMEM((STATE, rows), jnp.float32)],
        cost_estimate=pl.CostEstimate(flops=2 * rows * STATE * INNER, bytes_accessed=rows * INNER * 4, transcendentals=0),
        name="state",
    )(left, values, weight_rows.reshape(PAIRS, 2, rows), *after)


def chunk_rows(k, meta_ref, cum_ref, start_ref):
    here = slice(k * CHUNK, (k + 1) * CHUNK)
    first = meta_ref[0] + k * CHUNK
    index = first + lax.broadcasted_iota(jnp.int32, (1, CHUNK), 1)
    entering = start_ref[0:1, here] < first
    ending = index >= meta_ref[1 + k]
    cums, entries, tails = [], [], []
    for e in range(2):
        cum = cum_ref[0, e : e + 1, here]
        cums.append(cum)
        entries.append(jnp.where(entering, jnp.exp(cum), 0.0))
        gap = jnp.where(ending, cum[:, CHUNK - 1 :] - cum, masked_score)
        tails.append(jnp.exp(gap))
    return cums, entries, tails


def ssm_forward(conv, cum, step, state_in, skip, meta, start_column, start_row):
    rows = conv.shape[0]
    chunks = rows // CHUNK

    def kernel(meta_ref, x_ref, b_ref, c_ref, cum_ref, step_ref, state_ref, skip_ref, col_ref, row_ref,
               y_ref, inner, hide, state, b_turned):
        @pl.when(pl.program_id(0) == 0)
        def _():
            for k in range(chunks):
                here = slice(k * CHUNK, (k + 1) * CHUNK)
                b_turned[:, here] = b_ref[here, :].T.astype(jnp.bfloat16)
                inner[k] = lax.dot_general(
                    c_ref[here, :], b_ref[here, :], NT, precision=highest, preferred_element_type=jnp.float32
                )
                t = lax.broadcasted_iota(jnp.int32, (CHUNK, CHUNK), 0)
                s = lax.broadcasted_iota(jnp.int32, (CHUNK, CHUNK), 1)
                shown = (s <= t) & (meta_ref[0] + k * CHUNK + s >= col_ref[here, :])
                hide[k] = jnp.where(shown, 0.0, masked_score)

        low_lane = lax.broadcasted_iota(jnp.int32, (CHUNK, 2 * SSM_DIM), 1) < SSM_DIM
        state[...] = state_ref[...]
        for k in range(chunks):
            here = slice(k * CHUNK, (k + 1) * CHUNK)
            cums, entries, tails = chunk_rows(k, meta_ref, cum_ref, row_ref)
            x_now = x_ref[here, :]
            x_low = x_now.astype(jnp.bfloat16)
            entry = spread(*entries)
            weight = spread(*[tails[e] * step_ref[0, e : e + 1, here] for e in range(2)])
            parts = []
            for e in range(2):
                across = jnp.broadcast_to(cums[e], (CHUNK, CHUNK))
                decays = jnp.exp(across.T - across + hide[k])
                mix = (inner[k] * decays * step_ref[0, e : e + 1, here]).astype(jnp.bfloat16)
                parts.append(jnp.dot(mix, x_low, preferred_element_type=jnp.float32))
            carried = jnp.dot(
                c_ref[here, :].astype(jnp.bfloat16), state[...].astype(jnp.bfloat16),
                preferred_element_type=jnp.float32,
            )
            y_ref[here, :] = jnp.where(low_lane, parts[0], parts[1]) + entry * carried + skip_ref[...] * x_now
            fresh = jnp.dot(
                b_turned[:, here], (x_now * weight).astype(jnp.bfloat16), preferred_element_type=jnp.float32
            )
            state[...] = entry[CHUNK - 1 :, :] * state[...] + fresh

    whole = lambda i, m: (0, 0)
    lanes = lambda i, m: (0, i)
    return pl.pallas_call(
        kernel,
        grid_spec=pltpu.PrefetchScalarGridSpec(
            num_scalar_prefetch=1,
            grid=(PAIRS,),
            in_specs=[
                pl.BlockSpec((rows, 2 * SSM_DIM), lanes),
                pl.BlockSpec((rows, STATE), lambda i, m: (0, PAIRS)),
                pl.BlockSpec((rows, STATE), lambda i, m: (0, PAIRS + 1)),
                pl.BlockSpec((1, 2, rows), lambda i, m: (i, 0, 0)),
                pl.BlockSpec((1, 2, rows), lambda i, m: (i, 0, 0)),
                pl.BlockSpec((STATE, 2 * SSM_DIM), lanes),
                pl.BlockSpec((1, 2 * SSM_DIM), lanes),
                pl.BlockSpec((rows, 1), whole),
                pl.BlockSpec((8, rows), whole),
            ],
            out_specs=pl.BlockSpec((rows, 2 * SSM_DIM), lanes),
            scratch_shapes=[
                pltpu.VMEM((chunks, CHUNK, CHUNK), jnp.float32),
                pltpu.VMEM((chunks, CHUNK, CHUNK), jnp.float32),
                pltpu.VMEM((STATE, 2 * SSM_DIM), jnp.float32),
                pltpu.VMEM((STATE, rows), jnp.bfloat16),
            ],
        ),
        out_shape=jax.ShapeDtypeStruct((rows, INNER), jnp.float32),
        compiler_params=pltpu.CompilerParams(vmem_limit_bytes=40 * 2**20),
        cost_estimate=pl.CostEstimate(flops=10**9, bytes_accessed=rows * INNER * 8, transcendentals=2**21),
        name="ssm",
    )(meta, conv, conv, conv, cum.reshape(PAIRS, 2, rows), step.reshape(PAIRS, 2, rows), state_in, skip,
      start_column, start_row)


def ssm_backward(conv, dy, cum, step, state_in, state_grad, skip, meta, start_row, after=()):
    rows = conv.shape[0]
    chunks = rows // CHUNK

    def kernel(meta_ref, x_ref, dy_ref, b_ref, c_ref, cum_ref, step_ref, state_ref, grad_ref, skip_ref, row_ref,
               dx_ref, db_ref, dc_ref, small_ref, inner, hide, inner_grad, states, flow,
               b_turned, c_turned):
        low = lambda v: v.astype(jnp.bfloat16)
        dot = lambda p, q, dims=(((1,), (0,)), ((), ())): lax.dot_general(
            p, q, dims, preferred_element_type=jnp.float32
        )
        exact = lambda p, q, dims=(((1,), (0,)), ((), ())): lax.dot_general(
            p, q, dims, precision=highest, preferred_element_type=jnp.float32
        )
        s = lax.broadcasted_iota(jnp.int32, (CHUNK, CHUNK), 0)
        t = lax.broadcasted_iota(jnp.int32, (CHUNK, CHUNK), 1)

        @pl.when(pl.program_id(0) == 0)
        def _():
            db_ref[...] = jnp.zeros(db_ref.shape, jnp.float32)
            dc_ref[...] = jnp.zeros(dc_ref.shape, jnp.float32)
            inner_grad[...] = jnp.zeros(inner_grad.shape, jnp.float32)
            for k in range(chunks):
                here = slice(k * CHUNK, (k + 1) * CHUNK)
                b_turned[:, here] = low(b_ref[here, :].T)
                c_turned[:, here] = low(c_ref[here, :].T)
                inner[k] = exact(b_ref[here, :], c_ref[here, :], NT)
                shown = (s <= t) & (meta_ref[0] + k * CHUNK + s >= row_ref[0:1, here])
                hide[k] = jnp.where(shown, 0.0, masked_score)

        before = (s < t).astype(jnp.float32)
        until = low((s >= t).astype(jnp.float32))
        low_lane = t < SSM_DIM
        pick_row = lax.broadcasted_iota(jnp.int32, (8, 2 * SSM_DIM), 0)
        pick_lane = lax.broadcasted_iota(jnp.int32, (8, 2 * SSM_DIM), 1) // SSM_DIM
        pick = low((pick_row == pick_lane).astype(jnp.float32))
        spreads = []
        states[0] = state_ref[...]
        for k in range(chunks):
            here = slice(k * CHUNK, (k + 1) * CHUNK)
            cums, entries, tails = chunk_rows(k, meta_ref, cum_ref, row_ref)
            entry, tail = spread(*entries), spread(*tails)
            steps = spread(step_ref[0, 0:1, here], step_ref[0, 1:2, here])
            spreads.append((cums, entry, tail, steps))
            if k < chunks - 1:
                fresh = dot(b_turned[:, here], low(x_ref[here, :] * steps * tail))
                states[k + 1] = entry[CHUNK - 1 :, :] * states[k] + fresh
        flow[...] = grad_ref[...]
        skip_sum = jnp.zeros((1, 2 * SSM_DIM), jnp.float32)
        for k in reversed(range(chunks)):
            here = slice(k * CHUNK, (k + 1) * CHUNK)
            cums, entry, tail, steps = spreads[k]
            x_now, dy_now = x_ref[here, :], dy_ref[here, :]
            b_low, c_low = low(b_ref[here, :]), low(c_ref[here, :])
            scaled = x_now * steps
            dy_low = low(dy_now)
            flow_low, state_low = low(flow[...]), low(states[k])
            both = low(
                jnp.concatenate([jnp.where(low_lane, scaled, 0.0), jnp.where(low_lane, 0.0, scaled)], axis=0)
            )
            reached = dot(both, dy_low, NT)
            mixes, weighed = [], []
            for e in range(2):
                across = jnp.broadcast_to(cums[e], (CHUNK, CHUNK))
                decays = jnp.exp(across - across.T + hide[k])
                reach = decays * reached[e * CHUNK : (e + 1) * CHUNK]
                inner_grad[k] += reach
                weighed.append(low(inner[k] * reach))
                mixes.append(low(inner[k] * decays))
            sums = dot(jnp.concatenate(weighed, axis=0), until)
            within = [
                jnp.sum(sums[e * CHUNK : (e + 1) * CHUNK] * before, axis=0, keepdims=True) for e in range(2)
            ]
            mixed = dot(jnp.concatenate(mixes, axis=0), dy_low)
            back = tail * dot(b_low, flow_low)
            dxs = jnp.where(low_lane, mixed[:CHUNK], mixed[CHUNK:]) + back
            db_ref[here, :] += dot(low(scaled * tail), flow_low, NT)
            entered = low(dy_now * entry)
            dc_ref[here, :] += dot(entered, state_low, NT)
            brought = dy_now * entry * dot(c_low, state_low)
            ends = dot(pick, low(brought), NT)
            begins = dot(pick, low(scaled * back), NT)
            direct = dot(pick, low(x_now * dxs), NT)
            through = jnp.sum(flow[...] * states[k], axis=0, keepdims=True) * entry[CHUNK - 1 :, :]
            log_grad = exact(ends, until.astype(jnp.float32)) + exact(begins, before)
            for e in range(2):
                lanes = slice(e * SSM_DIM, (e + 1) * SSM_DIM)
                kept = jnp.sum(through[:, lanes], axis=1, keepdims=True)
                small_ref[0, e : e + 1, here] = direct[e : e + 1, :]
                small_ref[0, 2 + e : 3 + e, here] = log_grad[e : e + 1, :] + within[e] + kept
            dx_ref[here, :] = dxs * steps + skip_ref[...] * dy_now
            skip_sum += jnp.sum(x_now * dy_now, axis=0, keepdims=True)
            flow[...] = entry[CHUNK - 1 :, :] * flow[...] + dot(c_turned[:, here], entered)
        small_ref[0, 4:8, :] = jnp.zeros((4, rows), jnp.float32)
        small_ref[0, 4:5, 0 : 2 * SSM_DIM] = skip_sum

        @pl.when(pl.program_id(0) == PAIRS - 1)
        def _():
            for k in range(chunks):
                here = slice(k * CHUNK, (k + 1) * CHUNK)
                grads = low(inner_grad[k])
                db_ref[here, :] += dot(grads, low(c_ref[here, :]))
                dc_ref[here, :] += dot(grads, low(b_ref[here, :]), TN)

    whole = lambda i, m: (0, 0)
    lanes = lambda i, m: (0, i)
    pair = lambda i, m: (i, 0, 0)
    return pl.pallas_call(
        pinned(kernel, 11, after),
        grid_spec=pltpu.PrefetchScalarGridSpec(
            num_scalar_prefetch=1,
            grid=(PAIRS,),
            in_specs=[
                pl.BlockSpec((rows, 2 * SSM_DIM), lanes),
                pl.BlockSpec((rows, 2 * SSM_DIM), lanes),
                pl.BlockSpec((rows, STATE), lambda i, m: (0, PAIRS)),
                pl.BlockSpec((rows, STATE), lambda i, m: (0, PAIRS + 1)),
                pl.BlockSpec((1, 2, rows), pair),
                pl.BlockSpec((1, 2, rows), pair),
                pl.BlockSpec((STATE, 2 * SSM_DIM), lanes),
                pl.BlockSpec((STATE, 2 * SSM_DIM), lanes),
                pl.BlockSpec((1, 2 * SSM_DIM), lanes),
                pl.BlockSpec((8, rows), whole),
            ] + pins(after),
            out_specs=[
                pl.BlockSpec((rows, 2 * SSM_DIM), lanes),
                pl.BlockSpec((rows, STATE), whole),
                pl.BlockSpec((rows, STATE), whole),
                pl.BlockSpec((1, 8, rows), pair),
            ],
            scratch_shapes=[
                pltpu.VMEM((chunks, CHUNK, CHUNK), jnp.float32),
                pltpu.VMEM((chunks, CHUNK, CHUNK), jnp.float32),
                pltpu.VMEM((chunks, CHUNK, CHUNK), jnp.float32),
                pltpu.VMEM((chunks, STATE, 2 * SSM_DIM), jnp.float32),
                pltpu.VMEM((STATE, 2 * SSM_DIM), jnp.float32),
                pltpu.VMEM((STATE, rows), jnp.bfloat16),
                pltpu.VMEM((STATE, rows), jnp.bfloat16),
            ],
        ),
        out_shape=[
            jax.ShapeDtypeStruct((rows, INNER), jnp.float32),
            jax.ShapeDtypeStruct((rows, STATE), jnp.float32),
            jax.ShapeDtypeStruct((rows, STATE), jnp.float32),
            jax.ShapeDtypeStruct((PAIRS, 8, rows), jnp.float32),
        ],
        compiler_params=pltpu.CompilerParams(vmem_limit_bytes=40 * 2**20),
        cost_estimate=pl.CostEstimate(flops=3 * 10**9, bytes_accessed=rows * INNER * 12, transcendentals=2**21),
        name="ssm_back",
    )(meta, conv, dy, conv, conv, cum.reshape(PAIRS, 2, rows), step.reshape(PAIRS, 2, rows), state_in, state_grad,
      skip, start_row, *after)


def chain_states(earlier, later):
    return (earlier[0] * later[0], earlier[1] * later[0] + later[1])


def scan_states(carry, state, span, fast, backward):
    wide = jnp.repeat(carry, SSM_DIM)[None, :]
    if not fast:
        ident = (jnp.ones_like(wide), jnp.zeros_like(state))
        return (carried_in if backward else prefix)((wide, state), span, chain_states, ident)[1]
    flow = Flow(scan_stages(carry, state, backward))
    while flow.sends:
        flow.go()
    return flow.result


def scan_stages(carry, state, backward, extra=None):
    total = (jnp.repeat(carry, SSM_DIM)[None, :], state)
    start = None
    for name in ("c", "x", "y"):
        place = lax.axis_index(name)
        at = lax.broadcasted_iota(jnp.int32, (16, INNER), 0)
        block = jnp.where(at == 0, total[0], 0.0)
        if extra is not None:
            rest = jnp.pad(extra, (0, INNER - extra.shape[0]))[None, :]
            for place_at in range(1, 4):
                term = lax.reduce_precision(rest, 8, 7)
                block = jnp.where(at == place_at, term, block)
                rest = rest - term
        packed = jnp.concatenate([total[1].astype(jnp.bfloat16), block.astype(jnp.bfloat16)], axis=0)
        (packed,) = yield [(packed, name, SWAP)]
        packed = packed.astype(jnp.float32)
        other = (packed[STATE : STATE + 1], packed[:STATE])
        if extra is not None:
            extra = extra + jnp.sum(packed[STATE + 1 : STATE + 4, : extra.shape[0]], axis=0)
        leads = place == (0 if backward else 1)
        seen = (jnp.where(leads, other[0], 1.0), jnp.where(leads, other[1], 0.0))
        start = seen if start is None else chain_states(seen, start)
        if name != "y":
            forward = chain_states(other, total)
            reverse = chain_states(total, other)
            total = jax.tree.map(lambda p, q: jnp.where(leads, p, q), forward, reverse)
    return start[1] if extra is None else [start[1], extra]


KEYS = 512
PAIR = 2 * HEAD_DIM


def attention_forward(q_wide, kv, meta, starts, after=()):
    rows = q_wide.shape[2]
    blocks = kv.shape[0]
    ratio = HEADS_Q // HEADS_KV
    wide = min(512, rows)

    def kernel(meta_ref, q_ref, kv_ref, start_ref, o_ref, log_ref, top, total):
        b = pl.program_id(1)

        @pl.when(b == 0)
        def _():
            top[...] = jnp.full(top.shape, masked_score, jnp.float32)
            total[...] = jnp.zeros(total.shape, jnp.float32)
            o_ref[...] = jnp.zeros(o_ref.shape, jnp.float32)

        def block(partial):
            pair = kv_ref[0, 0]
            turned = pair.T[HEAD_DIM:, :]
            for h in range(ratio):
                for r in range(0, rows, wide):
                    here = slice(r, r + wide)
                    scores = jnp.dot(pair, q_ref[h, :, here], preferred_element_type=jnp.float32)
                    if partial:
                        keys = b * KEYS + lax.broadcasted_iota(jnp.int32, scores.shape, 0)
                        mine = meta_ref[2] + r + lax.broadcasted_iota(jnp.int32, scores.shape, 1)
                        visible = (keys >= start_ref[0:1, here]) & (keys <= mine)
                        scores = jnp.where(visible, scores, masked_score)
                    before = top[h, 0:1, here]
                    peak = jnp.maximum(before, jnp.max(scores, axis=0, keepdims=True))
                    part = jnp.exp(scores - peak)
                    if partial:
                        part = jnp.where(visible, part, 0.0)
                    fade = jnp.exp(before - peak)
                    top[h, 0:1, here] = peak
                    total[h, 0:1, here] = total[h, 0:1, here] * fade + jnp.sum(part, axis=0, keepdims=True)
                    o_ref[h, :, here] = o_ref[h, :, here] * fade + jnp.dot(
                        turned, part.astype(jnp.bfloat16), preferred_element_type=jnp.float32
                    )

        needed = (b >= meta_ref[0]) & (b < meta_ref[1])
        partial = ((b + 1) * KEYS > meta_ref[2]) | (b * KEYS < meta_ref[3])

        @pl.when(needed & partial)
        def _():
            block(True)

        @pl.when(needed & jnp.logical_not(partial))
        def _():
            block(False)

        @pl.when(b == blocks - 1)
        def _():
            for h in range(ratio):
                sums = total[h, 0:1, :]
                o_ref[h] = o_ref[h] / sums
                log_ref[h] = jnp.broadcast_to(top[h, 0:1, :] + jnp.log(sums), (8, rows))

    heads = lambda g, b, m: (g, 0, 0)
    return pl.pallas_call(
        pinned(kernel, 4, after),
        grid_spec=pltpu.PrefetchScalarGridSpec(
            num_scalar_prefetch=1,
            grid=(HEADS_KV, blocks),
            in_specs=[
                pl.BlockSpec((ratio, PAIR, rows), heads),
                pl.BlockSpec((1, 1, KEYS, PAIR), lambda g, b, m: (b, g, 0, 0)),
                pl.BlockSpec((8, rows), lambda g, b, m: (0, 0)),
            ] + pins(after),
            out_specs=[
                pl.BlockSpec((ratio, HEAD_DIM, rows), heads),
                pl.BlockSpec((ratio, 8, rows), heads),
            ],
            scratch_shapes=[
                pltpu.VMEM((ratio, 8, rows), jnp.float32),
                pltpu.VMEM((ratio, 8, rows), jnp.float32),
            ],
        ),
        out_shape=[
            jax.ShapeDtypeStruct((HEADS_Q, HEAD_DIM, rows), jnp.float32),
            jax.ShapeDtypeStruct((HEADS_Q, 8, rows), jnp.float32),
        ],
        compiler_params=pltpu.CompilerParams(vmem_limit_bytes=48 * 2**20),
        cost_estimate=pl.CostEstimate(flops=2 * 10**10, bytes_accessed=2**23, transcendentals=2**23),
        name="attend",
    )(meta, q_wide, kv, starts, *after)


def attention_backward(q_wide, g_wide, kv, logs, mixed, meta, starts, group, after=()):
    rows = q_wide.shape[2]
    blocks = kv.shape[0]
    ratio = HEADS_Q // HEADS_KV
    wide = min(512, rows)

    def kernel(meta_ref, q_ref, g_ref, kv_ref, log_ref, o_ref, start_ref, dkv_ref, dq_ref, delta, sums):
        b = pl.program_id(0)

        @pl.when(b == 0)
        def _():
            dq_ref[...] = jnp.zeros(dq_ref.shape, jnp.float32)
            for h in range(ratio):
                both = g_ref[h, HEAD_DIM:, :].astype(jnp.float32) * o_ref[h]
                delta[h] = jnp.broadcast_to(jnp.sum(both, axis=0, keepdims=True), (8, rows))

        def block(partial):
            pair = kv_ref[0, 0]
            turned = pair.T[:HEAD_DIM, :]
            for h in range(ratio):
                for r in range(0, rows, wide):
                    here = slice(r, r + wide)
                    q_now = q_ref[h, :, here]
                    g_now = g_ref[h, :, here]
                    scores = jnp.dot(pair, q_now, preferred_element_type=jnp.float32)
                    probs = jnp.exp(scores - log_ref[h, 0:1, here])
                    if partial:
                        keys = b * KEYS + lax.broadcasted_iota(jnp.int32, scores.shape, 0)
                        mine = meta_ref[2] + r + lax.broadcasted_iota(jnp.int32, scores.shape, 1)
                        visible = (keys >= start_ref[0:1, here]) & (keys <= mine)
                        probs = jnp.where(visible, probs, 0.0)
                    grads = jnp.dot(pair, g_now, preferred_element_type=jnp.float32)
                    low_grads = (probs * (grads - delta[h, 0:1, here])).astype(jnp.bfloat16)
                    change = lax.dot_general(
                        probs.astype(jnp.bfloat16), g_now, NT, preferred_element_type=jnp.float32
                    ) + lax.dot_general(low_grads, q_now, NT, preferred_element_type=jnp.float32)
                    if h == 0 and r == 0:
                        sums[...] = change
                    else:
                        sums[...] += change
                    dq_ref[h, :, here] += jnp.dot(turned, low_grads, preferred_element_type=jnp.float32)
            dkv_ref[0, 0] = sums[...].astype(jnp.bfloat16)

        needed = (b >= meta_ref[0]) & (b < meta_ref[1])
        partial = ((b + 1) * KEYS > meta_ref[2]) | (b * KEYS < meta_ref[3])

        @pl.when(needed & partial)
        def _():
            block(True)

        @pl.when(needed & jnp.logical_not(partial))
        def _():
            block(False)

        @pl.when(jnp.logical_not(needed))
        def _():
            dkv_ref[0, 0] = jnp.zeros((KEYS, PAIR), jnp.bfloat16)

    heads = lambda b, m: (group, 0, 0)
    return pl.pallas_call(
        pinned(kernel, 7, after),
        grid_spec=pltpu.PrefetchScalarGridSpec(
            num_scalar_prefetch=1,
            grid=(blocks,),
            in_specs=[
                pl.BlockSpec((ratio, PAIR, rows), heads),
                pl.BlockSpec((ratio, PAIR, rows), heads),
                pl.BlockSpec((1, 1, KEYS, PAIR), lambda b, m: (b, group, 0, 0)),
                pl.BlockSpec((ratio, 8, rows), heads),
                pl.BlockSpec((ratio, HEAD_DIM, rows), heads),
                pl.BlockSpec((8, rows), lambda b, m: (0, 0)),
            ] + pins(after),
            out_specs=[
                pl.BlockSpec((1, 1, KEYS, PAIR), lambda b, m: (b, 0, 0, 0)),
                pl.BlockSpec((ratio, HEAD_DIM, rows), lambda b, m: (0, 0, 0)),
            ],
            scratch_shapes=[
                pltpu.VMEM((ratio, 8, rows), jnp.float32),
                pltpu.VMEM((KEYS, PAIR), jnp.float32),
            ],
        ),
        out_shape=[
            jax.ShapeDtypeStruct((blocks, 1, KEYS, PAIR), jnp.bfloat16),
            jax.ShapeDtypeStruct((ratio, HEAD_DIM, rows), jnp.float32),
        ],
        compiler_params=pltpu.CompilerParams(vmem_limit_bytes=48 * 2**20),
        cost_estimate=pl.CostEstimate(flops=2 * 10**10, bytes_accessed=2**23, transcendentals=2**23),
        name="attend_back",
    )(meta, q_wide, g_wide, kv, logs, mixed, starts, *after)


def scatter_span(value, span, fast):
    if not fast:
        return lax.psum_scatter(value, span, scatter_dimension=0).astype(jnp.float32)
    flow = Flow(scatter_stages(value))
    while flow.sends:
        flow.go()
    return flow.result


def scatter_stages(value):
    _, y, x, c = (lax.axis_index(name) for name in GRID)
    value = value.reshape((2, 2, 2) + value.shape[1:])
    for name, place, axis in (("c", c, 2), ("y", y, 0), ("x", x, 0)):
        send = lax.dynamic_index_in_dim(value, 1 - place, axis, keepdims=False)
        (arrived,) = yield [(send, name, SWAP)]
        keep = lax.dynamic_index_in_dim(value, place, axis, keepdims=False)
        value = keep.astype(jnp.float32) + arrived.astype(jnp.float32)
        if name != "x":
            value = value.astype(jnp.bfloat16)
    return value


def plane_stages(value):
    for pairs in ([(0, 1), (1, 0), (2, 3), (3, 2)], [(0, 2), (2, 0), (1, 3), (3, 1)]):
        (other,) = yield [(value, "z", pairs)]
        value = value + other
    return value


def offsets_of():
    places, at = {}, 0
    for name_key, extent in layout():
        places[name_key] = (at, extent)
        at += math.prod(extent)
    return places


def early_weights(params):
    places = offsets_of()
    buffers, spread_flow, (slots, all_slots), where = gather_lines(params)
    spread_flow.go()
    names = (W_QUERY, W_KEY, W_VALUE, W_ATTN_OUT, W_GATE_SSM, W_X_SSM, W_B_C)
    misc_at = places[W_STEP][0]
    first = unpack_lines(
        buffers[:16], slots, where, [flat_segment(name_key) for name_key in names] + [(0, 16, LINE), (misc_at, 288, LINE)]
    )
    weights = dict(zip(names, first))
    weights[NORM_ATTN] = first[-2].reshape(-1)[:D]
    misc = first[-1].reshape(-1)
    for name_key in (W_STEP,) + small_names[1:-1]:
        at, extent = places[name_key]
        weights[name_key] = misc[at - misc_at : at - misc_at + math.prod(extent)].reshape(extent)
    return weights, spread_flow, (buffers, all_slots, where)


def flat_segment(name_key):
    at, extent = offsets_of()[name_key]
    return (at, extent[0], extent[1])


def late_weights(held, after):
    buffers, slots, where = held
    names = (W_SSM_OUT, W_GATE, W_UP_PROJ, W_DOWN)
    norm_at = offsets_of()[NORM_FFN][0]
    second = unpack_lines(
        buffers, slots, where, [flat_segment(name_key) for name_key in names] + [(norm_at, 16, LINE)], after
    )
    weights = dict(zip(names, second))
    weights[NORM_FFN] = second[-1].reshape(-1)[norm_at % LINE : norm_at % LINE + D]
    return weights


def pack_late(gate, up, down, ssm_low, grad_branch, grad_norm_ffn, after):
    places = offsets_of()
    out_at = places[W_SSM_OUT][0]
    lane = places[W_GATE][0] % LINE
    boundary = 2 * PLANE * LINE
    tail_from = (boundary - out_at) // D
    tail = matmul_left_t(ssm_low[:, tail_from:], grad_branch).reshape(-1)
    tail = tail[boundary - out_at - tail_from * D :]
    head = jnp.concatenate([jnp.zeros((14 * LINE,), jnp.float32), tail, grad_norm_ffn])
    head_rows = head.shape[0] // LINE
    carry = jnp.zeros((8, LINE), jnp.float32).at[7, :lane].set(head[head_rows * LINE :])
    head = head[: head_rows * LINE].reshape(head_rows, LINE).astype(jnp.bfloat16)
    return pack_lines(
        None, 2 * PLANE + 32, head_rows, [gate, up, down], lane, 0, [(head, 0)], carry, 48, after
    )


def pack_out(ssm_low, grad_branch, after):
    out_at = offsets_of()[W_SSM_OUT][0]
    first_row = (8 + out_at // LINE) // 16 * 16
    rows = first_row + SSM_HEADS * SSM_DIM * D // LINE
    return pack_lines(
        None, rows, first_row, [(ssm_low, grad_branch)], out_at % LINE, (8 + out_at // LINE) % 8, [],
        jnp.zeros((8, LINE), jnp.float32), 0, after,
    )


def pack_ssm(target, segments, small, ssm_low, grad_branch, after):
    places = offsets_of()
    misc = [small[name_key].reshape(-1) for name_key in (W_STEP,) + small_names[1:-1]]
    count = sum(part.shape[0] for part in misc)
    misc_rows = (count // LINE + 16) // 16 * 16
    opening = matmul_left_t(ssm_low[:, :16], grad_branch).reshape(-1)
    misc = jnp.concatenate(misc + [opening[: misc_rows * LINE - count]])
    misc = misc.reshape(misc_rows, LINE).astype(jnp.bfloat16)
    first_row = 8 + places[W_ATTN_OUT][0] // LINE
    return pack_lines(
        target, target.shape[0], first_row, segments, 0, 0, [(misc, 8 + places[W_STEP][0] // LINE)], None, 0, after
    )


def pack_qkv(segments, attended, grad_branch, grad_norm_attn, after):
    places = offsets_of()
    out_row = 8 + places[W_ATTN_OUT][0] // LINE
    rows = (8 + SHARD) // 16 * 16 + 8 * PIECE
    closing = matmul_left_t(attended[:, :16], grad_branch).reshape(-1, LINE)
    closing = closing[: rows - out_row].astype(jnp.bfloat16)
    opening = jnp.concatenate([jnp.zeros((8, LINE), jnp.float32), grad_norm_attn.reshape(-1, LINE)]).astype(jnp.bfloat16)
    return pack_lines(
        None, rows, 16, segments, 0, 0, [(opening, 0), (closing, out_row)], None, 0, after
    )


def own_lines(early, late, corner):
    z, y, x, c = (lax.axis_index(name) for name in GRID)
    place = 4 * y + 2 * x + c
    shard = SHARD * place
    start = jnp.where(z < 2, (8 + shard) % 16, (14 + shard) % 16)
    lines = jnp.where(z < 2, early, late)
    lines = jnp.where((z == 0) & (place < 2), corner[:WIN], lines)
    lines = lax.dynamic_slice(lines, (start, 0), (SHARD, LINE)).astype(jnp.float32)
    return lines.reshape(-1)


def body(span, group, fast, tokens, params, cotangent, offsets):
    rows_dev = tokens.shape[0]
    group_rows = rows_dev * lax.axis_size(span)
    all_rows = group_rows * lax.axis_size(group)
    ssm_inner = SSM_HEADS * SSM_DIM
    score_scale = HEAD_DIM ** (-0.5)
    bounds = offsets[0]
    my_start = lax.axis_index(span) * rows_dev
    row_index = my_start + jnp.arange(rows_dev, dtype=jnp.int32)
    seq_id, positions = sequence_info(row_index, bounds)
    first_start = row_index[0] - positions[0]
    last_row = my_start + rows_dev - 1
    cosine, sine = rotary_tables(positions)
    if fast:
        weights, spread_flow, held = early_weights(params)
    else:
        weights = unpack(lax.all_gather(params, group + span, axis=0, tiled=True))
    small_f32 = {name_key: weights[name_key].astype(jnp.float32) for name_key in small_names[:-1]}
    x_rows = tokens.astype(jnp.float32)
    normed_one, norm_one_back = jax.vjp(rms_norm, x_rows, small_f32[NORM_ATTN])
    hidden = normed_one.astype(jnp.bfloat16)
    across = lambda weight: lax.dot_general(
        weight, hidden, (((0,), (1,)), ((), ())), preferred_element_type=jnp.float32
    )
    q_rot = rotate(across(weights[W_QUERY]), cosine, sine, HEADS_Q).astype(jnp.bfloat16)
    k_rot = rotate(across(weights[W_KEY]), cosine, sine, HEADS_KV).astype(jnp.bfloat16)
    value_low = across(weights[W_VALUE]).astype(jnp.bfloat16).reshape(HEADS_KV, HEAD_DIM, rows_dev)
    kv_mine = jnp.concatenate([k_rot, value_low], axis=1).transpose(0, 2, 1)
    row_starts = row_index - positions
    kv_local = kv_mine.reshape(HEADS_KV, rows_dev, PAIR)
    xbc = jnp.concatenate(
        [matmul(hidden, weights[W_X_SSM]), matmul(hidden, weights[W_B_C])], axis=1
    )
    step_raw = matmul(hidden, weights[W_STEP])
    q_wide = jnp.pad(q_rot * jnp.bfloat16(score_scale), ((0, 0), (0, HEAD_DIM), (0, 0)))
    rim_source = xbc[rows_dev - 8 :]
    if fast:
        (rim_source,) = fence([rim_source], [q_wide])
    rim_rows = passed_along(rim_source, span, 1)
    ssm_meta = jnp.concatenate([my_start[None], row_starts[CHUNK - 1 :: CHUNK]]).astype(jnp.int32)
    conv_bias = small_f32[CONV_BIAS][None, :]
    convolve = lambda after: conv_forward(
        xbc, rim_rows, small_f32[CONV_WEIGHT], conv_bias, ssm_meta, row_starts[:, None], after
    )
    if fast:
        key_blocks = lax.all_gather(kv_local, span)
        conv_values = convolve(())
    else:
        conv_values = convolve(())
    step_in = step_raw.T + small_f32[STEP_BIAS][:, None]
    step_rows = jax.nn.softplus(step_in)
    decay = -jnp.exp(small_f32[DECAY_LOG])
    logs_step = step_rows * decay[:, None]
    order = jnp.arange(rows_dev)
    upto = (order[:, None] <= order[None, :]).astype(jnp.float32)
    cumul = jnp.dot(logs_step, upto, precision=highest)
    chunk_cum = jnp.dot(
        logs_step.reshape(-1, CHUNK), upto[:CHUNK, :CHUNK], precision=highest
    ).reshape(SSM_HEADS, rows_dev)
    went_on = row_starts < my_start
    entry_rows = jnp.where(went_on[None, :], jnp.exp(cumul), 0.0)
    in_last = row_index >= row_starts[rows_dev - 1]
    tail_rows = jnp.exp(jnp.where(in_last[None, :], cumul[:, -1:] - cumul, masked_score))
    carry_all = entry_rows[:, -1]
    summarize = lambda after: weighted_state(conv_values, PAIRS, conv_values, tail_rows * step_rows, after)
    meta = jnp.stack(
        [first_start // KEYS, last_row // KEYS + 1, my_start, row_starts[rows_dev - 1]]
    ).astype(jnp.int32)
    start_row = jnp.broadcast_to(row_starts[None, :], (8, rows_dev))
    if fast:
        (local_state,) = bracket(summarize, [spread_flow])
        scan = Flow(scan_stages(carry_all, local_state, False))
        (gate_in,) = fence([hidden], scan.values())
        gate_ssm = matmul(gate_in, weights[W_GATE_SSM])
        scan.go()
        (gate_ssm,) = fence([gate_ssm], scan.values())
        scan.go()
        mixed, logs = bracket(
            lambda after: attention_forward(
                q_wide, key_blocks, meta, start_row, (*after, gate_ssm, *spread_flow.values())
            ),
            [scan],
        )
        spread_flow.go()
        state_in = scan.result
    else:
        gate_ssm = matmul(hidden, weights[W_GATE_SSM])
        key_blocks = lax.all_gather(kv_local, span)
        if rows_dev != KEYS:
            key_blocks = key_blocks.transpose(1, 0, 2, 3).reshape(HEADS_KV, -1, KEYS, PAIR).transpose(1, 0, 2, 3)
        state_in = scan_states(carry_all, summarize(()), span, fast, False)
        mixed, logs = attention_forward(q_wide, key_blocks, meta, start_row)
    attended = mixed.astype(jnp.bfloat16).reshape(HEADS_Q * HEAD_DIM, rows_dev).T
    attn_out = matmul(attended, weights[W_ATTN_OUT])
    skip_wide = jnp.repeat(small_f32[SKIP_GAIN], SSM_DIM)[None, :]
    ssm_y = ssm_forward(
        conv_values, chunk_cum, step_rows, state_in, skip_wide, ssm_meta, row_starts[:, None], start_row
    )
    normed_ssm, gnorm_back = jax.vjp(gated_norm, ssm_y, gate_ssm, small_f32[NORM_SSM])
    ssm_low = normed_ssm.astype(jnp.bfloat16)
    if fast:
        held = (held[0] + spread_flow.result,) + held[1:]
        weights.update(late_weights(held, [ssm_y]))
    small_f32[NORM_FFN] = weights[NORM_FFN].astype(jnp.float32)
    ssm_out = matmul(ssm_low, weights[W_SSM_OUT])
    middle = x_rows + attn_out + ssm_out
    normed_two, norm_two_back = jax.vjp(rms_norm, middle, small_f32[NORM_FFN])
    hidden_two = normed_two.astype(jnp.bfloat16)
    gate_ffn = matmul(hidden_two, weights[W_GATE])
    upper = matmul(hidden_two, weights[W_UP_PROJ])
    activation_f32, swiglu_back = jax.vjp(swiglu, gate_ffn, upper)
    activation = activation_f32.astype(jnp.bfloat16)
    ffn_out = matmul(activation, weights[W_DOWN])
    result = middle + ffn_out
    squares = jnp.stack(
        [
            jnp.sum(result * result),
            jnp.sum(attn_out * attn_out),
            jnp.sum(ssm_out * ssm_out),
            jnp.sum(ffn_out * ffn_out),
        ]
    )
    grad_out = cotangent.astype(jnp.float32)
    grad_activation = matmul_right_t(cotangent, weights[W_DOWN])
    grad_gate_f32, grad_upper_f32 = swiglu_back(grad_activation)
    grad_gate = grad_gate_f32.astype(jnp.bfloat16)
    grad_upper = grad_upper_f32.astype(jnp.bfloat16)
    grad_hidden_two = matmul_right_t(grad_gate, weights[W_GATE]) + matmul_right_t(
        grad_upper, weights[W_UP_PROJ]
    )
    grad_middle_norm, grad_norm_ffn = norm_two_back(grad_hidden_two)
    grad_middle = grad_out + grad_middle_norm
    grad_branch = grad_middle.astype(jnp.bfloat16)
    grad_attended = matmul_right_t(weights[W_ATTN_OUT], grad_branch).astype(jnp.bfloat16)
    grad_ssm_low = matmul_right_t(grad_branch, weights[W_SSM_OUT])
    grad_ssm_y, grad_gate_ssm_f32, grad_norm_ssm = gnorm_back(grad_ssm_low)
    grad_state_local = weighted_state(conv_values, PAIRS + 1, grad_ssm_y, entry_rows)
    if fast:
        scan = Flow(scan_stages(carry_all, grad_state_local, True, squares)).go()
        (late,) = bracket(
            lambda after: pack_late(
                (hidden_two, grad_gate), (hidden_two, grad_upper), (activation, cotangent),
                ssm_low, grad_branch, grad_norm_ffn, after,
            ),
            [scan],
        )
        late_flow = Flow(reduce_stages(late, 1, 14))
        (grad_branch_low,) = fence([grad_branch], scan.values() + late_flow.values())
        early = pack_out(ssm_low, grad_branch_low, ())
        scan.go()
        grad_state_out, squares = scan.result
        (early,) = fence([early], [grad_state_out])
        late_flow.go()
        (early,) = fence([early], late_flow.values())
        stats_flow = Flow(plane_stages(squares))

        def around(call):
            out = bracket(lambda after: call((*after, *stats_flow.values())), [late_flow])
            stats_flow.go(out[:1])
            return out

    else:
        grad_state_out = scan_states(carry_all, grad_state_local, span, fast, True)
        around = lambda call: call(())
    grad_x, grad_b, grad_c, grad_small = around(
        lambda after: ssm_backward(
            conv_values, grad_ssm_y, chunk_cum, step_rows, state_in, grad_state_out, skip_wide, ssm_meta, start_row,
            after,
        )
    )
    grad_direct = grad_small[:, 0:2].reshape(SSM_HEADS, rows_dev)
    grad_logs = grad_small[:, 2:4].reshape(SSM_HEADS, rows_dev)
    grad_decay_log = decay * jnp.sum(step_rows * grad_logs, axis=1)
    grad_step_rows = (grad_direct + decay[:, None] * grad_logs) * jax.nn.sigmoid(step_in)
    grad_step_bias = jnp.sum(grad_step_rows, axis=1)
    grad_step_raw_f32 = grad_step_rows.T
    grad_skip_gain = jnp.sum(grad_small[:, 4, : 2 * SSM_DIM].reshape(SSM_HEADS, SSM_DIM), axis=1)
    grad_main, grad_tail, grad_edge, grad_taps = around(
        lambda after: conv_backward(
            grad_x, grad_b, grad_c, xbc, rim_rows, small_f32[CONV_WEIGHT], conv_bias, ssm_meta,
            row_starts[:, None], after,
        )
    )
    grad_conv_weight = grad_taps[:CONV]
    grad_conv_bias = grad_taps[CONV]
    rim_back = passed_along(grad_edge, span, -1)
    grad_tail = grad_tail + jnp.pad(rim_back, ((8, 0), (0, 0)))
    grad_xbc = lax.dynamic_update_slice(grad_main, grad_tail.astype(jnp.bfloat16), (rows_dev - 16, 0))
    grad_gate_ssm = grad_gate_ssm_f32.astype(jnp.bfloat16)
    grad_step_raw = grad_step_raw_f32.astype(jnp.bfloat16)
    grad_w_step = matmul_left_t(hidden, grad_step_raw)
    grad_hidden_ssm = (
        matmul_right_t(grad_gate_ssm, weights[W_GATE_SSM])
        + matmul_right_t(grad_xbc[:, :ssm_inner], weights[W_X_SSM])
        + matmul_right_t(grad_xbc[:, ssm_inner:], weights[W_B_C])
        + matmul_right_t(grad_step_raw, weights[W_STEP])
    )
    small = {
        W_STEP: grad_w_step,
        CONV_WEIGHT: grad_conv_weight,
        CONV_BIAS: grad_conv_bias,
        STEP_BIAS: grad_step_bias,
        DECAY_LOG: grad_decay_log,
        SKIP_GAIN: grad_skip_gain,
        NORM_SSM: grad_norm_ssm,
        NORM_FFN: grad_norm_ffn,
    }
    parts = []
    if fast:
        early = pack_ssm(
            early,
            [
                (attended, grad_branch), (hidden, grad_gate_ssm),
                (hidden, grad_xbc[:, :ssm_inner]), (hidden, grad_xbc[:, ssm_inner:]),
            ],
            small, ssm_low, grad_branch, late_flow.values(),
        )
        early_flow = Flow(reduce_stages(early, 0, 8))
        (grad_attended,) = fence([grad_attended], early_flow.values() + late_flow.values())
        around = lambda call: bracket(call, [early_flow])
    g_wide = jnp.pad(grad_attended.reshape(HEADS_Q, HEAD_DIM, rows_dev), ((0, 0), (HEAD_DIM, 0), (0, 0)))
    if fast:
        early_flow.go()
        (g_wide,) = fence([g_wide], early_flow.values())
    for group_at in range(HEADS_KV):
        after_part = [part[1] for part in parts]
        if fast and group_at == 0:
            after_part = late_flow.values()
        parts.append(
            around(
                lambda after: attention_backward(
                    q_wide, g_wide, key_blocks, logs, mixed, meta, start_row, group_at, (*after, *after_part)
                )
            )
        )
    grad_kv = jnp.concatenate([part[0] for part in parts], axis=1)
    grad_q_turned = jnp.concatenate([part[1] for part in parts], axis=0)
    if rows_dev != KEYS:
        grad_kv = grad_kv.transpose(1, 0, 2, 3).reshape(HEADS_KV, -1, rows_dev, PAIR).transpose(1, 0, 2, 3)
    if fast:
        late_flow.go([parts[-1][1]])
        scatter = Flow(scatter_stages(grad_kv))
        (grad_q_turned,) = fence([grad_q_turned], scatter.values() + early_flow.values() + late_flow.values())
    turned_back = rotate(grad_q_turned * score_scale, cosine, -sine, HEADS_Q).astype(jnp.bfloat16)
    grad_query_low = turned_back.reshape(HEADS_Q * HEAD_DIM, rows_dev).T
    if fast:
        scatter.go()
        early_flow.go()
        (grad_query_low,) = fence([grad_query_low], scatter.values() + early_flow.values())
    grad_hidden = grad_hidden_ssm + matmul_right_t(grad_query_low, weights[W_QUERY])
    if fast:
        scatter.go()
        (grad_hidden,) = fence([grad_hidden], scatter.values())
        scatter.go()
        grad_kv_mine = scatter.result
    else:
        grad_kv_mine = scatter_span(grad_kv, span, fast)
    grad_kv_mine = grad_kv_mine.transpose(0, 2, 1)
    grad_key_low = rotate(grad_kv_mine[:, :HEAD_DIM], cosine, -sine, HEADS_KV).astype(jnp.bfloat16)
    grad_key_low = grad_key_low.reshape(HEADS_KV * HEAD_DIM, rows_dev).T
    grad_value_low = grad_kv_mine[:, HEAD_DIM:].astype(jnp.bfloat16).reshape(HEADS_KV * HEAD_DIM, rows_dev).T
    grad_hidden = (
        grad_hidden
        + matmul_right_t(grad_key_low, weights[W_KEY])
        + matmul_right_t(grad_value_low, weights[W_VALUE])
    )
    grad_x_norm, grad_norm_attn = norm_one_back(grad_hidden)
    grad_tokens = grad_middle + grad_x_norm
    if fast:
        corner = pack_qkv(
            [(hidden, grad_query_low), (hidden, grad_key_low), (hidden, grad_value_low)],
            attended, grad_branch, grad_norm_attn, early_flow.values(),
        )
        corner_flow = Flow(corner_stages(corner))
        for _ in range(3):
            corner_flow.go()
        early_flow.go(corner_flow.values()[:1])
        ((pieces, _, _), *_) = corner_flow.sends
        (pieces,) = fence([pieces], early_flow.values())
        corner_flow.sends = [(pieces, axis, pairs) for _, axis, pairs in corner_flow.sends]
        for flow in (early_flow, late_flow, corner_flow):
            while flow.sends:
                flow.go()
        stats = jnp.sqrt(stats_flow.result / (all_rows * D))
        grad_shard = own_lines(early_flow.result, late_flow.result, corner_flow.result)
        return (result.astype(jnp.bfloat16), grad_tokens, grad_shard, stats)
    small[NORM_ATTN] = grad_norm_attn
    stats = jnp.sqrt(lax.psum(squares, group + span) / (all_rows * D))
    pairs = {
        W_QUERY: (hidden, grad_query_low),
        W_KEY: (hidden, grad_key_low),
        W_VALUE: (hidden, grad_value_low),
        W_ATTN_OUT: (attended, grad_branch),
        W_GATE_SSM: (hidden, grad_gate_ssm),
        W_X_SSM: (hidden, grad_xbc[:, :ssm_inner]),
        W_B_C: (hidden, grad_xbc[:, ssm_inner:]),
        W_SSM_OUT: (ssm_low, grad_branch),
        W_GATE: (hidden_two, grad_gate),
        W_UP_PROJ: (hidden_two, grad_upper),
        W_DOWN: (activation, cotangent),
    }
    grad_dict = dict(small)
    for name_key, (left, right) in pairs.items():
        grad_dict[name_key] = matmul_left_t(left, right)
    flat_parts = [grad_dict[name_key].reshape(-1) for name_key, extent in layout()]
    used_entries = 0
    for part_array in flat_parts:
        used_entries += part_array.shape[0]
    flat_parts.append(jnp.zeros((params.shape[0] * lax.axis_size(group + span) - used_entries,), jnp.float32))
    grad_shard = lax.psum_scatter(
        jnp.concatenate(flat_parts), group + span, scatter_dimension=0, tiled=True
    )
    return (result.astype(jnp.bfloat16), grad_tokens, grad_shard, stats)


def solution(mesh):
    fast = (mesh.shape["group"], mesh.shape["span"]) == FAST
    if fast:
        mesh = Mesh(mesh.devices.reshape(4, 2, 2, 2), GRID)
        group, span = (GRID[:1], GRID[1:])
    else:
        group, span = (("group",), ("span",))

    def program(tokens, params, cotangent, offsets):
        return body(span, group, fast, tokens, params, cotangent, offsets)

    return jax.shard_map(
        program,
        mesh=mesh,
        in_specs=(P(group + span, None), P(group + span), P(group + span, None), P(group, None)),
        out_specs=(P(group + span, None), P(group + span, None), P(group + span), P()),
        check_vma=False,
    )
```

```python
import math

import jax
import jax.numpy as jnp
import numpy as np
from jax import lax
from jax.experimental import pallas as pl
from jax.experimental.pallas import tpu as pltpu
from jax.sharding import Mesh, PartitionSpec as P

D = 1024
HEADS_Q = 8
HEADS_KV = 2
HEAD_DIM = 64
SSM_HEADS = 24
SSM_DIM = 64
STATE = 128
CONV = 4
FF = 2048
(
    NORM_ATTN,
    W_QUERY,
    W_KEY,
    W_VALUE,
    W_ATTN_OUT,
    W_GATE_SSM,
    W_X_SSM,
    W_B_C,
    W_STEP,
    CONV_WEIGHT,
    CONV_BIAS,
    STEP_BIAS,
    DECAY_LOG,
    SKIP_GAIN,
    NORM_SSM,
    W_SSM_OUT,
    NORM_FFN,
    W_GATE,
    W_UP_PROJ,
    W_DOWN,
) = range(20)


epsilon = 1e-05
rope_base = 100000000000.0
masked_score = -1e30
highest = lax.Precision.HIGHEST
small_names = (
    NORM_ATTN,
    CONV_WEIGHT,
    CONV_BIAS,
    STEP_BIAS,
    DECAY_LOG,
    SKIP_GAIN,
    NORM_SSM,
    NORM_FFN,
)


def passed_along(value, axis, steps):
    count = lax.axis_size(axis)
    first, last = (max(0, -steps), min(count, count - steps))
    return lax.ppermute(value, axis, [(source, source + steps) for source in range(first, last)])


def prefix(value, axis, combine, identity):
    peers, place = (lax.axis_size(axis), lax.axis_index(axis))
    everything = jax.tree.map(
        lambda part, kind: lax.all_gather(part.astype(kind), axis),
        value,
        (jnp.bfloat16, jnp.bfloat16),
    )
    start = jax.tree.map(
        lambda part, zero: jnp.broadcast_to(jnp.asarray(zero, part.dtype), part.shape),
        value,
        identity,
    )

    def prefix_turn(k, before):
        reached = k < place
        new = combine(
            before, jax.tree.map(lambda part, own: part[k].astype(own.dtype), everything, value)
        )
        return jax.tree.map(lambda a, b: jnp.where(reached, a, b), new, before)

    return lax.fori_loop(0, peers, prefix_turn, start)


def carried_in(value, axis, combine, identity):
    peers, place = (lax.axis_size(axis), lax.axis_index(axis))
    everything = jax.tree.map(
        lambda part, kind: lax.all_gather(part.astype(kind), axis),
        value,
        jax.tree.map(lambda a: jnp.bfloat16 if a.dtype == jnp.float32 else a.dtype, value),
    )
    start = jax.tree.map(
        lambda part, zero: jnp.broadcast_to(jnp.asarray(zero, part.dtype), part.shape),
        value,
        identity,
    )

    def carried_turn(k, before):
        at = peers - 1 - k
        reached = at > place
        new = combine(
            before, jax.tree.map(lambda part, own: part[at].astype(own.dtype), everything, value)
        )
        return jax.tree.map(lambda a, b: jnp.where(reached, a, b), new, before)

    return lax.fori_loop(0, peers, carried_turn, start)


def layout():
    ssm_inner = SSM_HEADS * SSM_DIM
    channels = ssm_inner + 2 * STATE
    return [
        (NORM_ATTN, (D,)),
        (W_QUERY, (D, HEADS_Q * HEAD_DIM)),
        (W_KEY, (D, HEADS_KV * HEAD_DIM)),
        (W_VALUE, (D, HEADS_KV * HEAD_DIM)),
        (W_ATTN_OUT, (HEADS_Q * HEAD_DIM, D)),
        (W_GATE_SSM, (D, ssm_inner)),
        (W_X_SSM, (D, ssm_inner)),
        (W_B_C, (D, 2 * STATE)),
        (W_STEP, (D, SSM_HEADS)),
        (CONV_WEIGHT, (CONV, channels)),
        (CONV_BIAS, (channels,)),
        (STEP_BIAS, (SSM_HEADS,)),
        (DECAY_LOG, (SSM_HEADS,)),
        (SKIP_GAIN, (SSM_HEADS,)),
        (NORM_SSM, (ssm_inner,)),
        (W_SSM_OUT, (ssm_inner, D)),
        (NORM_FFN, (D,)),
        (W_GATE, (D, FF)),
        (W_UP_PROJ, (D, FF)),
        (W_DOWN, (FF, D)),
    ]


def unpack(flat_vector):
    unpacked = {}
    offset = 0
    for name_key, extent in layout():
        amount = math.prod(extent)
        unpacked[name_key] = flat_vector[offset : offset + amount].reshape(extent)
        offset += amount
    return unpacked


def matmul(left, right):
    return jnp.dot(left, right, preferred_element_type=jnp.float32)


def matmul_left_t(left, right):
    return lax.dot_general(
        left, right, (((0,), (0,)), ((), ())), preferred_element_type=jnp.float32
    )


def matmul_right_t(left, right):
    return lax.dot_general(
        left, right, (((1,), (1,)), ((), ())), preferred_element_type=jnp.float32
    )


def rms_norm(values, gain):
    return values * lax.rsqrt(jnp.mean(values * values, axis=-1, keepdims=True) + epsilon) * gain


def gated_norm(ssm_y, gate_ssm, gain):
    return rms_norm(ssm_y * jax.nn.silu(gate_ssm), gain)


def swiglu(gate_ffn, upper):
    return jax.nn.silu(gate_ffn) * upper


def sequence_info(row_index, bounds):
    starts = bounds[:-1]
    inside = row_index[:, None] >= starts[None, :]
    seq_id = jnp.sum(inside.astype(jnp.int32), axis=1) - 1
    seq_start = jnp.max(jnp.where(inside, starts[None, :], 0), axis=1)
    return (seq_id, row_index - seq_start)


def rotary_tables(positions):
    half_dim = HEAD_DIM // 2
    freqs = jnp.exp(
        -jnp.arange(half_dim, dtype=jnp.float32) * (2.0 * math.log(rope_base) / HEAD_DIM)
    )
    angles = freqs[:, None] * positions.astype(jnp.float32)[None, :]
    return (jnp.cos(angles), jnp.sin(angles))


def rotate(values, cosine, sine, heads):
    halves = values.reshape(heads, 2, HEAD_DIM // 2, -1)
    first_half, second_half = halves[:, 0], halves[:, 1]
    turned = jnp.stack(
        [first_half * cosine - second_half * sine, second_half * cosine + first_half * sine], axis=1
    )
    return turned.reshape(heads, HEAD_DIM, -1)


def add_rows(target, addend, first_row):
    current = lax.dynamic_slice_in_dim(target, first_row, addend.shape[0], 0)
    return lax.dynamic_update_slice_in_dim(target, current + addend, first_row, 0)


FAST = (4, 8)
LINE = 128
SHARD = 3082
SPAD = 3088
WIN = 3104
PLANE = 8 * SHARD
DEPTH = 4
TALL = {1: 1024, 2: 1024, 4: 512, 8: 256, 12: 128, 16: 128}
GRID = ("z", "y", "x", "c")
ZC = ("z", "c")
SWAP = [(0, 1), (1, 0)]


def zc_pairs(*pairs):
    return [(2 * a + c, 2 * b + c) for a, b, c in pairs]


def pinned(kernel, count, after):
    return lambda *refs: kernel(*refs[:count], *refs[count + len(after) :])


def pins(after):
    return [pl.BlockSpec(memory_space=pltpu.HBM)] * len(after)


class Flow:
    def __init__(self, stages):
        self.stages = stages
        self.sends = next(stages)
        self.result = None

    def values(self):
        return [value for value, _, _ in self.sends] or (list(self.result) if isinstance(self.result, list) else [self.result])

    def hold(self, after):
        held = fence(self.values(), after)
        self.sends = [(value, axis, pairs) for value, (_, axis, pairs) in zip(held, self.sends)]

    def go(self, after=()):
        arrived = [lax.ppermute(value, axis, pairs) for value, axis, pairs in self.sends]
        if after:
            arrived = fence(arrived, after)
        try:
            self.sends = self.stages.send(arrived)
        except StopIteration as stop:
            self.sends, self.result = [], stop.value
        return self


def fence(values, after):
    def kernel(*refs):
        del refs

    return pl.pallas_call(
        kernel,
        in_specs=pins(values) + pins(after),
        out_specs=pins(values),
        out_shape=[jax.ShapeDtypeStruct(value.shape, value.dtype) for value in values],
        input_output_aliases={k: k for k in range(len(values))},
        name="fence",
    )(*values, *after)


def bracket(call, flows):
    out = call([value for flow in flows for value in flow.values()])
    out = list(out) if isinstance(out, (list, tuple)) else [out]
    for flow in flows:
        flow.go()
    return fence(out, [v for flow in flows for v in flow.values()])


def gather_lines(params):
    z, y, x, c = (lax.axis_index(name) for name in GRID)
    lines = jnp.pad(params.reshape(SHARD, LINE), ((0, SPAD - SHARD), (0, 0)))
    sibling = lax.ppermute(lines, ZC, [(2 * k + 1 - k % 2, 2 * k + k % 2) for k in range(4)])
    buffers = []
    for part in range(2):
        here = jnp.where(c == part, lines, sibling)
        one = lax.ppermute(here, ZC, zc_pairs((0, 1, 0), (1, 2, 1)))
        side = lax.ppermute(here, ZC, zc_pairs((1, 0, 1)))
        two = lax.ppermute(one, ZC, zc_pairs((1, 2, 0), (2, 3, 1)))
        three = lax.ppermute(two, ZC, zc_pairs((2, 3, 0)))
        column = jnp.where(z == c, here, one + side + two + three)
        over_x = lax.ppermute(column, "x", SWAP)
        over_y = lax.ppermute(column, "y", SWAP)
        corner = lax.ppermute(over_y if part else over_x, "x" if part else "y", SWAP)
        local = [column, over_x, over_y, corner]
        buffers += [piece[None] for piece in local]
        buffers += [lax.ppermute(piece, "c", SWAP)[None] for piece in local]
    early = [(k, 0) for k in range(16)]
    here = jnp.where(c == 0, jnp.stack([lines, sibling]), jnp.stack([sibling, lines]))
    one = lax.ppermute(here, ZC, zc_pairs((2, 1, 0), (3, 2, 1)))
    side = lax.ppermute(here, ZC, zc_pairs((2, 3, 0)))
    two = lax.ppermute(one, ZC, zc_pairs((1, 0, 0), (2, 1, 1)))
    three = lax.ppermute(two, ZC, zc_pairs((1, 0, 1)))
    column = jnp.where(z == 2 + c, here, one + side + two + three)
    late = []
    for part in range(2):
        for first in (16, 21):
            late += [(first, part), (first + 1, part), (first + 2, part), (first + 3 + part, 0)]
    shard = np.arange(32)
    sz, sy, sx, sc = shard // 8, shard // 4 % 2, shard // 2 % 2, shard % 2
    away = jnp.where(sz % 2 == c, 0, 4)
    where = sc * 8 + away + 2 * (sy ^ y) + (sx ^ x) + 16 * (sz // 2)
    return buffers, Flow(spread_stages(column)), (early, early + late), where.astype(jnp.int32)


def spread_stages(column):
    over_x, over_y = yield [(column, "x", SWAP), (column, "y", SWAP)]
    corners = yield [(over_x[:1], "y", SWAP), (over_y[1:], "x", SWAP)]
    local = [column, over_x, over_y] + list(corners)
    return local + list((yield [(piece, "c", SWAP) for piece in local]))


def unpack_lines(buffers, slots, where, segments, after=()):
    jobs, starts = [], []
    reach = 0
    for offset, rows, columns in segments:
        per_row = columns // LINE
        lane, base = offset % LINE, offset // LINE
        if per_row == 1 and rows < 1024:
            lane, tall = 0, rows
        else:
            tall = TALL[per_row]
        starts.append(len(jobs))
        for k in range(rows // tall):
            jobs.append((base + k * tall * per_row, tall * per_row, 1 if lane else 0))
    window = max(job[1] for job in jobs) + 32
    table = np.zeros((len(jobs), 5), np.int32)
    for k, (line, count, extra) in enumerate(jobs):
        owner = line // SHARD
        inside = line - owner * SHARD
        begin = min(inside // 16 * 16, SPAD - window)
        crosses = int(line + count + extra > (owner + 1) * SHARD)
        table[k] = (owner, begin, begin - inside, crosses, (owner + 1) * SHARD - line)
    base_row = (int(-table[:, 2].min()) + 7) // 8 * 8
    table[:, 2] += base_row
    table[:, 4] += base_row
    room = int(max((table[:, 2] + window).max(), ((table[:, 4] + window) * table[:, 3]).max()))
    room = (room + 15) // 8 * 8
    total = len(jobs)
    count_buffers = len(buffers)
    shapes = []
    for offset, rows, columns in segments:
        per_row = columns // LINE
        tall = rows if per_row == 1 and rows < 1024 else TALL[per_row]
        shapes.append((rows, columns, tall, per_row, offset % LINE if tall != rows or per_row != 1 else 0))
    sizes = sorted({(tall, columns) for _, columns, tall, _, _ in shapes})

    def kernel(table_ref, where_ref, *refs):
        sources = refs[:count_buffers]
        outs = refs[count_buffers : count_buffers + len(segments)]
        rest = refs[count_buffers + len(segments) :]
        stages = dict(zip(sizes, rest))
        raw, flat, in_sem, out_sem = rest[len(sizes) :]
        step = pl.program_id(0)

        def fetch(job, slot):
            owner = table_ref[job, 0]
            begin = pl.multiple_of(table_ref[job, 1], 16)
            for b, (source, part) in enumerate(slots):

                @pl.when(where_ref[owner] == b)
                def _():
                    pltpu.make_async_copy(
                        sources[source].at[part, pl.ds(begin, window), :], raw.at[slot, 0], in_sem.at[slot, 0]
                    ).start()

            @pl.when(table_ref[job, 3] == 1)
            def _():
                for b, (source, part) in enumerate(slots):

                    @pl.when(where_ref[owner + 1] == b)
                    def _():
                        pltpu.make_async_copy(
                            sources[source].at[part, pl.ds(0, window), :], raw.at[slot, 1], in_sem.at[slot, 1]
                        ).start()

        def fetched(slot, half):
            return pltpu.make_async_copy(
                sources[0].at[0, pl.ds(0, window), :], raw.at[slot, half], in_sem.at[slot, half]
            )

        @pl.when(step == 0)
        def _():
            for k in range(min(DEPTH - 1, total)):
                fetch(k, k)

        @pl.when(step + DEPTH - 1 < total)
        def _():
            fetch(step + DEPTH - 1, lax.rem(step + DEPTH - 1, DEPTH))

        slot = lax.rem(step, DEPTH)
        fetched(slot, 0).wait()
        flat[pl.ds(table_ref[step, 2], window), :] = raw[slot, 0].astype(jnp.float32)

        @pl.when(table_ref[step, 3] == 1)
        def _():
            fetched(slot, 1).wait()
            flat[pl.ds(table_ref[step, 4], window), :] = raw[slot, 1].astype(jnp.float32)

        for index, (rows, columns, tall, per_row, lane) in enumerate(shapes):
            begin = starts[index]
            blocks = rows // tall
            stage = stages[(tall, columns)]

            @pl.when((step >= begin) & (step < begin + blocks))
            def _():
                block = step - begin
                side = lax.rem(block, DEPTH)

                def written(k, s):
                    return pltpu.make_async_copy(
                        stage.at[s],
                        outs[index].at[pl.ds(pl.multiple_of(k * tall, 16), tall), :],
                        out_sem.at[s],
                    )

                @pl.when(block >= DEPTH)
                def _():
                    written(block - DEPTH, side).wait()

                def tile(j):
                    picked = flat[pl.ds(base_row + j, tall, stride=per_row), :]
                    return pltpu.roll(picked, LINE - lane, 1) if lane else picked

                if lane:
                    lanes = lax.broadcasted_iota(jnp.int32, (tall, LINE), 1)
                    now = tile(0)
                    for j in range(per_row):
                        later = tile(j + 1)
                        stage[side, :, j * LINE : (j + 1) * LINE] = jnp.where(
                            lanes < LINE - lane, now, later
                        ).astype(jnp.bfloat16)
                        now = later
                else:
                    for j in range(per_row):
                        stage[side, :, j * LINE : (j + 1) * LINE] = tile(j).astype(jnp.bfloat16)
                written(block, side).start()

                @pl.when(block == blocks - 1)
                def _():
                    for back in reversed(range(min(DEPTH, blocks))):
                        written(block - back, lax.rem(block - back, DEPTH)).wait()

    return pl.pallas_call(
        pinned(kernel, 2 + count_buffers, after),
        grid_spec=pltpu.PrefetchScalarGridSpec(
            num_scalar_prefetch=2,
            grid=(total,),
            in_specs=[pl.BlockSpec(memory_space=pl.ANY)] * count_buffers + pins(after),
            out_specs=[pl.BlockSpec(memory_space=pl.ANY)] * len(segments),
            scratch_shapes=[pltpu.VMEM((DEPTH,) + size, jnp.bfloat16) for size in sizes]
            + [
                pltpu.VMEM((DEPTH, 2, window, LINE), jnp.bfloat16),
                pltpu.VMEM((room, LINE), jnp.float32),
                pltpu.SemaphoreType.DMA((DEPTH, 2)),
                pltpu.SemaphoreType.DMA((DEPTH,)),
            ],
        ),
        out_shape=[jax.ShapeDtypeStruct((rows, columns), jnp.bfloat16) for _, rows, columns in segments],
        compiler_params=pltpu.CompilerParams(vmem_limit_bytes=48 * 2**20),
        cost_estimate=pl.CostEstimate(flops=0, bytes_accessed=total * window * LINE * 4, transcendentals=0),
        name="unpack",
    )(jnp.asarray(table), where, *buffers, *after)


def pack_lines(target, target_rows, first_row, segments, lane, phase, extras, carry, tail_rows, after=()):
    tall = 512
    lefts, rights, plan = [], [], []
    left_of, right_of = {}, {}
    row = first_row
    begin = 0
    for left, right in segments:
        for value, seen, kept in ((left, left_of, lefts), (right, right_of, rights)):
            if id(value) not in seen:
                seen[id(value)] = len(kept)
                kept.append(value)
        blocks = left.shape[1] // tall
        plan.append((left_of[id(left)], right_of[id(right)], right.shape[1] // LINE, begin, blocks, row))
        begin += blocks
        row += left.shape[1] * right.shape[1] // LINE
    end_row = row
    total = begin
    biggest = max(entry[2] for entry in plan) * tall
    tokens = lefts[0].shape[0]
    count_left, count_right, count_extra = len(lefts), len(rights), len(extras)
    rolled = [jnp.roll(right, lane, axis=1) if lane else right for right in rights]
    carry_in = [carry] if lane else []
    targets = [] if target is None else [target]

    def left_spec(index):
        mine = [entry for entry in plan if entry[0] == index]

        def place(step):
            block = 0
            for _, _, _, start, blocks, _ in mine:
                block = jnp.where(step >= start, jnp.minimum(step - start, blocks - 1), block)
            return (0, block)

        return pl.BlockSpec((tokens, tall), place)

    def kernel(*refs):
        left_refs = refs[:count_left]
        right_refs = refs[count_left : count_left + count_right]
        at = count_left + count_right
        extra_refs = refs[at : at + count_extra]
        at += count_extra
        carry_refs = refs[at : at + len(carry_in)]
        at += len(carry_in) + len(targets)
        out = refs[at]
        flat, stage, shift, last, sems, extra_sems = refs[at + 1 :]
        step = pl.program_id(0)
        side = lax.rem(step, 2)

        def extra_copy(k):
            rows = extras[k][0].shape[0]
            return pltpu.make_async_copy(
                extra_refs[k], out.at[pl.ds(extras[k][1], rows), :], extra_sems.at[k]
            )

        @pl.when(step == 0)
        def _():
            for k in range(count_extra):
                extra_copy(k).start()
            if lane:
                shift[0:8, :] = carry_refs[0][...]
            if phase:
                flat[0:8, :] = jnp.zeros((8, LINE), jnp.float32)

        for left_at, right_at, per_row, start, blocks, row in plan:
            lines = per_row * tall

            def written(block, s, row=row, lines=lines):
                return pltpu.make_async_copy(
                    stage.at[s, pl.ds(0, lines), :],
                    out.at[pl.ds(pl.multiple_of(row + block * lines, 16), lines), :],
                    sems.at[s],
                )

            @pl.when((step >= start) & (step < start + blocks))
            def _():
                block = step - start
                if phase:

                    @pl.when(step > 0)
                    def _():
                        flat[0:8, :] = flat[lines : lines + 8, :]

                turned = left_refs[left_at][...].T
                lanes = lax.broadcasted_iota(jnp.int32, (tall, LINE), 1)
                for j0 in range(0, per_row, 2):
                    wide = min(2, per_row - j0)
                    tile = jnp.dot(
                        turned,
                        right_refs[right_at][:, j0 * LINE : (j0 + wide) * LINE],
                        preferred_element_type=jnp.float32,
                    )
                    for j in range(wide):
                        piece = tile[:, j * LINE : (j + 1) * LINE]
                        if lane and j0 + j == 0:
                            shift[8 : 8 + tall, :] = piece
                            piece = jnp.where(lanes < lane, shift[7 : 7 + tall, :], piece)
                            shift[0:8, :] = shift[tall : tall + 8, :]
                        if per_row == 1:
                            flat[phase : phase + tall, :] = piece
                        else:
                            flat[pl.ds(phase + j0 + j, tall, stride=per_row), :] = piece

                stage[side, 0:lines, :] = flat[0:lines, :].astype(jnp.bfloat16)
                written(block, side).start()

            @pl.when((step > start) & (step <= start + blocks))
            def _():
                written(step - start - 1, 1 - side).wait()

            if start + blocks == total:

                @pl.when(step == total - 1)
                def _():
                    written(blocks - 1, side).wait()

        @pl.when(step == total - 1)
        def _():
            if tail_rows:
                lanes = lax.broadcasted_iota(jnp.int32, (tail_rows, LINE), 1)
                rows_at = lax.broadcasted_iota(jnp.int32, (tail_rows, LINE), 0)
                final = jnp.broadcast_to(shift[7:8, :], (tail_rows, LINE))
                last[...] = jnp.where((rows_at == 0) & (lanes < lane), final, 0.0).astype(jnp.bfloat16)
                closing = pltpu.make_async_copy(
                    last, out.at[pl.ds(end_row, tail_rows), :], extra_sems.at[count_extra]
                )
                closing.start()
                closing.wait()
            for k in range(count_extra):
                extra_copy(k).wait()

    whole = [pl.BlockSpec(array.shape, lambda step: (0, 0)) for array in rolled]
    flops = sum(2 * tokens * entry[4] * tall * entry[2] * LINE for entry in plan)
    inputs = count_left + count_right + count_extra + len(carry_in) + len(targets)
    return pl.pallas_call(
        pinned(kernel, inputs, after),
        grid=(total,),
        in_specs=[left_spec(k) for k in range(count_left)]
        + whole
        + [pl.BlockSpec(array.shape, lambda step: (0, 0)) for array, _ in extras]
        + [pl.BlockSpec(array.shape, lambda step: (0, 0)) for array in carry_in]
        + [pl.BlockSpec(memory_space=pl.ANY)] * len(targets)
        + pins(after),
        out_specs=pl.BlockSpec(memory_space=pl.ANY),
        out_shape=jax.ShapeDtypeStruct((target_rows, LINE), jnp.bfloat16),
        scratch_shapes=[
            pltpu.VMEM((biggest + 16, LINE), jnp.float32),
            pltpu.VMEM((2, biggest, LINE), jnp.bfloat16),
            pltpu.VMEM((tall + 8, LINE), jnp.float32),
            pltpu.VMEM((max(tail_rows, 16), LINE), jnp.bfloat16),
            pltpu.SemaphoreType.DMA((2,)),
            pltpu.SemaphoreType.DMA((count_extra + 1,)),
        ],
        input_output_aliases={count_left + count_right + count_extra + len(carry_in): 0} if targets else {},
        compiler_params=pltpu.CompilerParams(vmem_limit_bytes=48 * 2**20),
        cost_estimate=pl.CostEstimate(flops=flops, bytes_accessed=total * biggest * LINE * 2, transcendentals=0),
        name="pack",
    )(*lefts, *rolled, *[array for array, _ in extras], *carry_in, *targets, *after)


def added(*parts):
    total = parts[0].astype(jnp.float32)
    for part in parts[1:]:
        total = total + part.astype(jnp.float32)
    return total.astype(jnp.bfloat16)


def reduce_stages(flat, batch, shift):
    z, y, x, c = (lax.axis_index(name) for name in GRID)
    length = PLANE + 32
    send = lax.dynamic_slice(flat, ((1 - c) * PLANE, 0), (length, LINE))
    (arrived,) = yield [(send, "c", SWAP)]
    chip = added(lax.dynamic_slice(flat, (c * PLANE, 0), (length, LINE)), arrived)

    def window(sy, sx, part):
        shard = sy * 4 + sx * 2 + part
        start = (shift + SHARD * shard) // 16 * 16
        return lax.dynamic_slice(chip, (start, 0), (WIN, LINE))

    away_0 = jnp.stack([window(1 - y, 0, 0), window(1 - y, 1, 0)])
    away_1 = jnp.stack([window(0, 1 - x, 1), window(1, 1 - x, 1)])
    home_0 = jnp.stack([window(y, 0, 0), window(y, 1, 0)])
    home_1 = jnp.stack([window(0, x, 1), window(1, x, 1)])
    got_0, got_1 = yield [(away_0, "y", SWAP), (away_1, "x", SWAP)]
    half_0, half_1 = added(home_0, got_0), added(home_1, got_1)
    pick = lambda value, at: lax.dynamic_index_in_dim(value, at, 0, keepdims=False)
    got_0, got_1 = yield [(pick(half_0, 1 - x), "x", SWAP), (pick(half_1, 1 - y), "y", SWAP)]
    columns = [added(pick(half_0, x), got_0), added(pick(half_1, y), got_1)]
    if batch == 0:
        hops = [((1, 0, 0), (2, 1, 1)), ((2, 0, 0), (3, 1, 1)), ((3, 0, 0), (0, 1, 1))]
    else:
        hops = [((1, 2, 0), (2, 3, 1)), ((0, 2, 0), (1, 3, 1)), ((3, 2, 0), (0, 3, 1))]
    if batch == 0:
        got = yield [(columns[0], ZC, zc_pairs(*hop)) for hop in hops]
        end = added(columns[0], *got)
        (column,) = fence(columns[1:], [end])
        got = yield [(column, ZC, zc_pairs(*hop)) for hop in hops]
        ends = [end, added(column, *got)]
    else:
        columns = jnp.stack(columns)
        got = yield [(columns, ZC, zc_pairs(*hop)) for hop in hops]
        ends = added(columns, *got)
    mine = jnp.where(c == 0, ends[0], ends[1])
    other = jnp.where(c == 0, ends[1], ends[0])
    (handed,) = yield [(other, ZC, [(2 * k + k % 2, 2 * k + 1 - k % 2) for k in range(4)])]
    return jnp.where(c == z % 2, mine, handed)


PIECE = 400


def corner_stages(flat):
    z, y, x, c = (lax.axis_index(name) for name in GRID)
    length = 8 * PIECE
    second = (8 + SHARD) // 16 * 16
    take = lambda at: lax.dynamic_slice(flat, (at * second, 0), (length, LINE))
    (arrived,) = yield [(take(1 - c), "c", SWAP)]
    chip = added(take(c), arrived).reshape(2, 2, 2, PIECE, LINE)
    pick = lambda value, at: lax.dynamic_index_in_dim(value, at, 0, keepdims=False)
    got = yield [(pick(chip[0], 1 - x), "x", SWAP), (pick(chip[1], 1 - y), "y", SWAP)]
    halves = [added(pick(chip[0], x), got[0]), added(pick(chip[1], y), got[1])]
    got = yield [(pick(halves[0], 1 - y), "y", SWAP), (pick(halves[1], 1 - x), "x", SWAP)]
    pieces = jnp.stack([added(pick(halves[0], y), got[0]), added(pick(halves[1], x), got[1])])
    got = yield [(pieces, "z", [(k, 0)]) for k in (1, 2, 3)]
    pieces = added(pieces, *got)
    got = yield [(pieces[0], "y", [(1, 0)]), (pieces[1], "x", [(1, 0)])]
    halves = [jnp.stack([pieces[0], got[0]]), jnp.stack([pieces[1], got[1]])]
    got = yield [(halves[0], "x", [(1, 0)]), (halves[1], "y", [(1, 0)])]
    return jnp.stack([halves[0], got[0], halves[1], got[1]]).reshape(length, LINE)


CHUNK = 128
NT = (((1,), (1,)), ((), ()))
TN = (((0,), (0,)), ((), ()))
INNER = SSM_HEADS * SSM_DIM
PAIRS = SSM_HEADS // 2


def spread(rows_a, rows_b):
    length = rows_a.shape[1]
    tall = jnp.concatenate(
        [jnp.broadcast_to(rows_a, (SSM_DIM, length)), jnp.broadcast_to(rows_b, (SSM_DIM, length))], axis=0
    )
    return tall.T


CHANNELS = INNER + 2 * STATE
LANES = 2 * SSM_DIM
COLUMNS = CHANNELS // LANES


def conv_masks(masks, start_ref, first, rows):
    place = first + lax.broadcasted_iota(jnp.int32, (rows, LANES), 0) - start_ref[...]
    for reach in range(1, CONV):
        masks[reach - 1] = jnp.where(place >= reach, 1.0, 0.0)


def conv_parts(ext, weight_ref, bias_ref, masks, rows):
    windows = []
    total = bias_ref[...]
    for tap in range(CONV):
        reach = CONV - 1 - tap
        window = ext[8 - reach : 8 - reach + rows, :]
        if reach:
            window = window * masks[reach - 1]
        windows.append(window)
        total = total + window * weight_ref[tap : tap + 1, :]
    return windows, total


def conv_forward(xbc, rim, weight, bias, meta, start_column, after=()):
    rows = xbc.shape[0]

    def kernel(meta_ref, x_ref, rim_ref, weight_ref, bias_ref, start_ref, out_ref, ext, masks):
        @pl.when(pl.program_id(0) == 0)
        def _():
            conv_masks(masks, start_ref, meta_ref[0], rows)

        ext[0:8, :] = rim_ref[...]
        ext[8:, :] = x_ref[...]
        _, total = conv_parts(ext, weight_ref, bias_ref, masks, rows)
        out_ref[...] = total * jax.nn.sigmoid(total)

    lanes = lambda i, m: (0, i)
    return pl.pallas_call(
        pinned(kernel, 6, after),
        grid_spec=pltpu.PrefetchScalarGridSpec(
            num_scalar_prefetch=1,
            grid=(COLUMNS,),
            in_specs=[
                pl.BlockSpec((rows, LANES), lanes),
                pl.BlockSpec((8, LANES), lanes),
                pl.BlockSpec((CONV, LANES), lanes),
                pl.BlockSpec((1, LANES), lanes),
                pl.BlockSpec((rows, 1), lambda i, m: (0, 0)),
            ] + pins(after),
            out_specs=pl.BlockSpec((rows, LANES), lanes),
            scratch_shapes=[
                pltpu.VMEM((rows + 8, LANES), jnp.float32),
                pltpu.VMEM((CONV - 1, rows, LANES), jnp.float32),
            ],
        ),
        out_shape=jax.ShapeDtypeStruct((rows, CHANNELS), jnp.float32),
        cost_estimate=pl.CostEstimate(flops=10**9, bytes_accessed=rows * CHANNELS * 8, transcendentals=0),
        name="conv",
    )(meta, xbc, rim, weight, bias, start_column, *after)


def conv_backward(dx, db, dc, xbc, rim, weight, bias, meta, start_column, after=()):
    rows = xbc.shape[0]

    def kernel(meta_ref, dx_ref, db_ref, dc_ref, x_ref, rim_ref, weight_ref, bias_ref, start_ref,
               low_ref, tail_ref, edge_ref, small_ref, ext, upper, masks):
        @pl.when(pl.program_id(0) == 0)
        def _():
            conv_masks(masks, start_ref, meta_ref[0], rows)
            upper[0:8, :] = jnp.zeros((8, LANES), jnp.float32)
            upper[8 + rows :, :] = jnp.zeros((8, LANES), jnp.float32)

        ext[0:8, :] = rim_ref[...]
        ext[8:, :] = x_ref[...]
        at = pl.program_id(0)
        arrived = jnp.where(at < PAIRS, dx_ref[...], jnp.where(at == PAIRS, db_ref[...], dc_ref[...]))
        windows, total = conv_parts(ext, weight_ref, bias_ref, masks, rows)
        gate = jax.nn.sigmoid(total)
        change = arrived * gate * (1.0 + total * (1.0 - gate))
        main = jnp.zeros((rows, LANES), jnp.float32)
        edge = jnp.zeros((8, LANES), jnp.float32)
        small_ref[...] = jnp.zeros((8, LANES), jnp.float32)
        small_ref[CONV : CONV + 1, :] = jnp.sum(change, axis=0, keepdims=True)
        for tap in range(CONV):
            reach = CONV - 1 - tap
            small_ref[tap : tap + 1, :] = jnp.sum(change * windows[tap], axis=0, keepdims=True)
            masked = change * masks[reach - 1] if reach else change
            upper[8 : 8 + rows, :] = masked * weight_ref[tap : tap + 1, :]
            main = main + upper[8 + reach : 8 + reach + rows, :]
            edge = edge + upper[reach : reach + 8, :]
        low_ref[...] = main.astype(jnp.bfloat16)
        tail_ref[...] = main[rows - 16 :, :]
        edge_ref[...] = edge

    lanes = lambda i, m: (0, i)
    whole = lambda i, m: (0, 0)
    return pl.pallas_call(
        pinned(kernel, 9, after),
        grid_spec=pltpu.PrefetchScalarGridSpec(
            num_scalar_prefetch=1,
            grid=(COLUMNS,),
            in_specs=[
                pl.BlockSpec((rows, LANES), lambda i, m: (0, jnp.minimum(i, PAIRS - 1))),
                pl.BlockSpec((rows, STATE), whole),
                pl.BlockSpec((rows, STATE), whole),
                pl.BlockSpec((rows, LANES), lanes),
                pl.BlockSpec((8, LANES), lanes),
                pl.BlockSpec((CONV, LANES), lanes),
                pl.BlockSpec((1, LANES), lanes),
                pl.BlockSpec((rows, 1), whole),
            ] + pins(after),
            out_specs=[
                pl.BlockSpec((rows, LANES), lanes),
                pl.BlockSpec((16, LANES), lanes),
                pl.BlockSpec((8, LANES), lanes),
                pl.BlockSpec((8, LANES), lanes),
            ],
            scratch_shapes=[
                pltpu.VMEM((rows + 8, LANES), jnp.float32),
                pltpu.VMEM((rows + 16, LANES), jnp.float32),
                pltpu.VMEM((CONV - 1, rows, LANES), jnp.float32),
            ],
        ),
        out_shape=[
            jax.ShapeDtypeStruct((rows, CHANNELS), jnp.bfloat16),
            jax.ShapeDtypeStruct((16, CHANNELS), jnp.float32),
            jax.ShapeDtypeStruct((8, CHANNELS), jnp.float32),
            jax.ShapeDtypeStruct((8, CHANNELS), jnp.float32),
        ],
        cost_estimate=pl.CostEstimate(flops=2 * 10**9, bytes_accessed=rows * CHANNELS * 10, transcendentals=0),
        name="conv_back",
    )(meta, dx, db, dc, xbc, rim, weight, bias, start_column, *after)


def weighted_state(left, left_block, values, weight_rows, after=()):
    rows = left.shape[0]

    def kernel(left_ref, value_ref, weight_ref, out_ref, turned):
        @pl.when(pl.program_id(0) == 0)
        def _():
            turned[...] = left_ref[...].T

        scaled = [(turned[...] * weight_ref[0, e : e + 1, :]).astype(jnp.bfloat16) for e in range(2)]
        both = jnp.dot(
            jnp.concatenate(scaled, axis=0), value_ref[...].astype(jnp.bfloat16), preferred_element_type=jnp.float32
        )
        low_lane = lax.broadcasted_iota(jnp.int32, (STATE, 2 * SSM_DIM), 1) < SSM_DIM
        out_ref[...] = jnp.where(low_lane, both[:STATE], both[STATE:])

    return pl.pallas_call(
        pinned(kernel, 3, after),
        grid=(PAIRS,),
        in_specs=[
            pl.BlockSpec((rows, STATE), lambda i: (0, left_block)),
            pl.BlockSpec((rows, 2 * SSM_DIM), lambda i: (0, i)),
            pl.BlockSpec((1, 2, rows), lambda i: (i, 0, 0)),
        ] + pins(after),
        out_specs=pl.BlockSpec((STATE, 2 * SSM_DIM), lambda i: (0, i)),
        out_shape=jax.ShapeDtypeStruct((STATE, INNER), jnp.float32),
        scratch_shapes=[pltpu.VMEM((STATE, rows), jnp.float32)],
        cost_estimate=pl.CostEstimate(flops=2 * rows * STATE * INNER, bytes_accessed=rows * INNER * 4, transcendentals=0),
        name="state",
    )(left, values, weight_rows.reshape(PAIRS, 2, rows), *after)


def chunk_rows(k, meta_ref, cum_ref, start_ref):
    here = slice(k * CHUNK, (k + 1) * CHUNK)
    first = meta_ref[0] + k * CHUNK
    index = first + lax.broadcasted_iota(jnp.int32, (1, CHUNK), 1)
    entering = start_ref[0:1, here] < first
    ending = index >= meta_ref[1 + k]
    cums, entries, tails = [], [], []
    for e in range(2):
        cum = cum_ref[0, e : e + 1, here]
        cums.append(cum)
        entries.append(jnp.where(entering, jnp.exp(cum), 0.0))
        gap = jnp.where(ending, cum[:, CHUNK - 1 :] - cum, masked_score)
        tails.append(jnp.exp(gap))
    return cums, entries, tails


def ssm_forward(conv, cum, step, state_in, skip, meta, start_column, start_row):
    rows = conv.shape[0]
    chunks = rows // CHUNK

    def kernel(meta_ref, x_ref, b_ref, c_ref, cum_ref, step_ref, state_ref, skip_ref, col_ref, row_ref,
               y_ref, inner, hide, state, b_turned):
        @pl.when(pl.program_id(0) == 0)
        def _():
            for k in range(chunks):
                here = slice(k * CHUNK, (k + 1) * CHUNK)
                b_turned[:, here] = b_ref[here, :].T.astype(jnp.bfloat16)
                inner[k] = lax.dot_general(
                    c_ref[here, :], b_ref[here, :], NT, precision=highest, preferred_element_type=jnp.float32
                )
                t = lax.broadcasted_iota(jnp.int32, (CHUNK, CHUNK), 0)
                s = lax.broadcasted_iota(jnp.int32, (CHUNK, CHUNK), 1)
                shown = (s <= t) & (meta_ref[0] + k * CHUNK + s >= col_ref[here, :])
                hide[k] = jnp.where(shown, 0.0, masked_score)

        low_lane = lax.broadcasted_iota(jnp.int32, (CHUNK, 2 * SSM_DIM), 1) < SSM_DIM
        state[...] = state_ref[...]
        for k in range(chunks):
            here = slice(k * CHUNK, (k + 1) * CHUNK)
            cums, entries, tails = chunk_rows(k, meta_ref, cum_ref, row_ref)
            x_now = x_ref[here, :]
            x_low = x_now.astype(jnp.bfloat16)
            entry = spread(*entries)
            weight = spread(*[tails[e] * step_ref[0, e : e + 1, here] for e in range(2)])
            parts = []
            for e in range(2):
                across = jnp.broadcast_to(cums[e], (CHUNK, CHUNK))
                decays = jnp.exp(across.T - across + hide[k])
                mix = (inner[k] * decays * step_ref[0, e : e + 1, here]).astype(jnp.bfloat16)
                parts.append(jnp.dot(mix, x_low, preferred_element_type=jnp.float32))
            carried = jnp.dot(
                c_ref[here, :].astype(jnp.bfloat16), state[...].astype(jnp.bfloat16),
                preferred_element_type=jnp.float32,
            )
            y_ref[here, :] = jnp.where(low_lane, parts[0], parts[1]) + entry * carried + skip_ref[...] * x_now
            fresh = jnp.dot(
                b_turned[:, here], (x_now * weight).astype(jnp.bfloat16), preferred_element_type=jnp.float32
            )
            state[...] = entry[CHUNK - 1 :, :] * state[...] + fresh

    whole = lambda i, m: (0, 0)
    lanes = lambda i, m: (0, i)
    return pl.pallas_call(
        kernel,
        grid_spec=pltpu.PrefetchScalarGridSpec(
            num_scalar_prefetch=1,
            grid=(PAIRS,),
            in_specs=[
                pl.BlockSpec((rows, 2 * SSM_DIM), lanes),
                pl.BlockSpec((rows, STATE), lambda i, m: (0, PAIRS)),
                pl.BlockSpec((rows, STATE), lambda i, m: (0, PAIRS + 1)),
                pl.BlockSpec((1, 2, rows), lambda i, m: (i, 0, 0)),
                pl.BlockSpec((1, 2, rows), lambda i, m: (i, 0, 0)),
                pl.BlockSpec((STATE, 2 * SSM_DIM), lanes),
                pl.BlockSpec((1, 2 * SSM_DIM), lanes),
                pl.BlockSpec((rows, 1), whole),
                pl.BlockSpec((8, rows), whole),
            ],
            out_specs=pl.BlockSpec((rows, 2 * SSM_DIM), lanes),
            scratch_shapes=[
                pltpu.VMEM((chunks, CHUNK, CHUNK), jnp.float32),
                pltpu.VMEM((chunks, CHUNK, CHUNK), jnp.float32),
                pltpu.VMEM((STATE, 2 * SSM_DIM), jnp.float32),
                pltpu.VMEM((STATE, rows), jnp.bfloat16),
            ],
        ),
        out_shape=jax.ShapeDtypeStruct((rows, INNER), jnp.float32),
        compiler_params=pltpu.CompilerParams(vmem_limit_bytes=40 * 2**20),
        cost_estimate=pl.CostEstimate(flops=10**9, bytes_accessed=rows * INNER * 8, transcendentals=2**21),
        name="ssm",
    )(meta, conv, conv, conv, cum.reshape(PAIRS, 2, rows), step.reshape(PAIRS, 2, rows), state_in, skip,
      start_column, start_row)


def ssm_backward(conv, dy, cum, step, state_in, state_grad, skip, meta, start_row, after=()):
    rows = conv.shape[0]
    chunks = rows // CHUNK

    def kernel(meta_ref, x_ref, dy_ref, b_ref, c_ref, cum_ref, step_ref, state_ref, grad_ref, skip_ref, row_ref,
               dx_ref, db_ref, dc_ref, small_ref, inner, hide, inner_grad, states, flow,
               b_turned, c_turned):
        low = lambda v: v.astype(jnp.bfloat16)
        dot = lambda p, q, dims=(((1,), (0,)), ((), ())): lax.dot_general(
            p, q, dims, preferred_element_type=jnp.float32
        )
        exact = lambda p, q, dims=(((1,), (0,)), ((), ())): lax.dot_general(
            p, q, dims, precision=highest, preferred_element_type=jnp.float32
        )
        s = lax.broadcasted_iota(jnp.int32, (CHUNK, CHUNK), 0)
        t = lax.broadcasted_iota(jnp.int32, (CHUNK, CHUNK), 1)

        @pl.when(pl.program_id(0) == 0)
        def _():
            db_ref[...] = jnp.zeros(db_ref.shape, jnp.float32)
            dc_ref[...] = jnp.zeros(dc_ref.shape, jnp.float32)
            inner_grad[...] = jnp.zeros(inner_grad.shape, jnp.float32)
            for k in range(chunks):
                here = slice(k * CHUNK, (k + 1) * CHUNK)
                b_turned[:, here] = low(b_ref[here, :].T)
                c_turned[:, here] = low(c_ref[here, :].T)
                inner[k] = exact(b_ref[here, :], c_ref[here, :], NT)
                shown = (s <= t) & (meta_ref[0] + k * CHUNK + s >= row_ref[0:1, here])
                hide[k] = jnp.where(shown, 0.0, masked_score)

        before = (s < t).astype(jnp.float32)
        until = low((s >= t).astype(jnp.float32))
        low_lane = t < SSM_DIM
        pick_row = lax.broadcasted_iota(jnp.int32, (8, 2 * SSM_DIM), 0)
        pick_lane = lax.broadcasted_iota(jnp.int32, (8, 2 * SSM_DIM), 1) // SSM_DIM
        pick = low((pick_row == pick_lane).astype(jnp.float32))
        spreads = []
        states[0] = state_ref[...]
        for k in range(chunks):
            here = slice(k * CHUNK, (k + 1) * CHUNK)
            cums, entries, tails = chunk_rows(k, meta_ref, cum_ref, row_ref)
            entry, tail = spread(*entries), spread(*tails)
            steps = spread(step_ref[0, 0:1, here], step_ref[0, 1:2, here])
            spreads.append((cums, entry, tail, steps))
            if k < chunks - 1:
                fresh = dot(b_turned[:, here], low(x_ref[here, :] * steps * tail))
                states[k + 1] = entry[CHUNK - 1 :, :] * states[k] + fresh
        flow[...] = grad_ref[...]
        skip_sum = jnp.zeros((1, 2 * SSM_DIM), jnp.float32)
        for k in reversed(range(chunks)):
            here = slice(k * CHUNK, (k + 1) * CHUNK)
            cums, entry, tail, steps = spreads[k]
            x_now, dy_now = x_ref[here, :], dy_ref[here, :]
            b_low, c_low = low(b_ref[here, :]), low(c_ref[here, :])
            scaled = x_now * steps
            dy_low = low(dy_now)
            flow_low, state_low = low(flow[...]), low(states[k])
            both = low(
                jnp.concatenate([jnp.where(low_lane, scaled, 0.0), jnp.where(low_lane, 0.0, scaled)], axis=0)
            )
            reached = dot(both, dy_low, NT)
            mixes, weighed = [], []
            for e in range(2):
                across = jnp.broadcast_to(cums[e], (CHUNK, CHUNK))
                decays = jnp.exp(across - across.T + hide[k])
                reach = decays * reached[e * CHUNK : (e + 1) * CHUNK]
                inner_grad[k] += reach
                weighed.append(low(inner[k] * reach))
                mixes.append(low(inner[k] * decays))
            sums = dot(jnp.concatenate(weighed, axis=0), until)
            within = [
                jnp.sum(sums[e * CHUNK : (e + 1) * CHUNK] * before, axis=0, keepdims=True) for e in range(2)
            ]
            mixed = dot(jnp.concatenate(mixes, axis=0), dy_low)
            back = tail * dot(b_low, flow_low)
            dxs = jnp.where(low_lane, mixed[:CHUNK], mixed[CHUNK:]) + back
            db_ref[here, :] += dot(low(scaled * tail), flow_low, NT)
            entered = low(dy_now * entry)
            dc_ref[here, :] += dot(entered, state_low, NT)
            brought = dy_now * entry * dot(c_low, state_low)
            ends = dot(pick, low(brought), NT)
            begins = dot(pick, low(scaled * back), NT)
            direct = dot(pick, low(x_now * dxs), NT)
            through = jnp.sum(flow[...] * states[k], axis=0, keepdims=True) * entry[CHUNK - 1 :, :]
            log_grad = exact(ends, until.astype(jnp.float32)) + exact(begins, before)
            for e in range(2):
                lanes = slice(e * SSM_DIM, (e + 1) * SSM_DIM)
                kept = jnp.sum(through[:, lanes], axis=1, keepdims=True)
                small_ref[0, e : e + 1, here] = direct[e : e + 1, :]
                small_ref[0, 2 + e : 3 + e, here] = log_grad[e : e + 1, :] + within[e] + kept
            dx_ref[here, :] = dxs * steps + skip_ref[...] * dy_now
            skip_sum += jnp.sum(x_now * dy_now, axis=0, keepdims=True)
            flow[...] = entry[CHUNK - 1 :, :] * flow[...] + dot(c_turned[:, here], entered)
        small_ref[0, 4:8, :] = jnp.zeros((4, rows), jnp.float32)
        small_ref[0, 4:5, 0 : 2 * SSM_DIM] = skip_sum

        @pl.when(pl.program_id(0) == PAIRS - 1)
        def _():
            for k in range(chunks):
                here = slice(k * CHUNK, (k + 1) * CHUNK)
                grads = low(inner_grad[k])
                db_ref[here, :] += dot(grads, low(c_ref[here, :]))
                dc_ref[here, :] += dot(grads, low(b_ref[here, :]), TN)

    whole = lambda i, m: (0, 0)
    lanes = lambda i, m: (0, i)
    pair = lambda i, m: (i, 0, 0)
    return pl.pallas_call(
        pinned(kernel, 11, after),
        grid_spec=pltpu.PrefetchScalarGridSpec(
            num_scalar_prefetch=1,
            grid=(PAIRS,),
            in_specs=[
                pl.BlockSpec((rows, 2 * SSM_DIM), lanes),
                pl.BlockSpec((rows, 2 * SSM_DIM), lanes),
                pl.BlockSpec((rows, STATE), lambda i, m: (0, PAIRS)),
                pl.BlockSpec((rows, STATE), lambda i, m: (0, PAIRS + 1)),
                pl.BlockSpec((1, 2, rows), pair),
                pl.BlockSpec((1, 2, rows), pair),
                pl.BlockSpec((STATE, 2 * SSM_DIM), lanes),
                pl.BlockSpec((STATE, 2 * SSM_DIM), lanes),
                pl.BlockSpec((1, 2 * SSM_DIM), lanes),
                pl.BlockSpec((8, rows), whole),
            ] + pins(after),
            out_specs=[
                pl.BlockSpec((rows, 2 * SSM_DIM), lanes),
                pl.BlockSpec((rows, STATE), whole),
                pl.BlockSpec((rows, STATE), whole),
                pl.BlockSpec((1, 8, rows), pair),
            ],
            scratch_shapes=[
                pltpu.VMEM((chunks, CHUNK, CHUNK), jnp.float32),
                pltpu.VMEM((chunks, CHUNK, CHUNK), jnp.float32),
                pltpu.VMEM((chunks, CHUNK, CHUNK), jnp.float32),
                pltpu.VMEM((chunks, STATE, 2 * SSM_DIM), jnp.float32),
                pltpu.VMEM((STATE, 2 * SSM_DIM), jnp.float32),
                pltpu.VMEM((STATE, rows), jnp.bfloat16),
                pltpu.VMEM((STATE, rows), jnp.bfloat16),
            ],
        ),
        out_shape=[
            jax.ShapeDtypeStruct((rows, INNER), jnp.float32),
            jax.ShapeDtypeStruct((rows, STATE), jnp.float32),
            jax.ShapeDtypeStruct((rows, STATE), jnp.float32),
            jax.ShapeDtypeStruct((PAIRS, 8, rows), jnp.float32),
        ],
        compiler_params=pltpu.CompilerParams(vmem_limit_bytes=40 * 2**20),
        cost_estimate=pl.CostEstimate(flops=3 * 10**9, bytes_accessed=rows * INNER * 12, transcendentals=2**21),
        name="ssm_back",
    )(meta, conv, dy, conv, conv, cum.reshape(PAIRS, 2, rows), step.reshape(PAIRS, 2, rows), state_in, state_grad,
      skip, start_row, *after)


def chain_states(earlier, later):
    return (earlier[0] * later[0], earlier[1] * later[0] + later[1])


def scan_states(carry, state, span, fast, backward):
    wide = jnp.repeat(carry, SSM_DIM)[None, :]
    if not fast:
        ident = (jnp.ones_like(wide), jnp.zeros_like(state))
        return (carried_in if backward else prefix)((wide, state), span, chain_states, ident)[1]
    flow = Flow(scan_stages(carry, state, backward))
    while flow.sends:
        flow.go()
    return flow.result


def scan_stages(carry, state, backward, extra=None):
    total = (jnp.repeat(carry, SSM_DIM)[None, :], state)
    start = None
    for name in ("c", "x", "y"):
        place = lax.axis_index(name)
        at = lax.broadcasted_iota(jnp.int32, (16, INNER), 0)
        block = jnp.where(at == 0, total[0], 0.0)
        if extra is not None:
            rest = jnp.pad(extra, (0, INNER - extra.shape[0]))[None, :]
            for place_at in range(1, 4):
                term = lax.reduce_precision(rest, 8, 7)
                block = jnp.where(at == place_at, term, block)
                rest = rest - term
        packed = jnp.concatenate([total[1].astype(jnp.bfloat16), block.astype(jnp.bfloat16)], axis=0)
        (packed,) = yield [(packed, name, SWAP)]
        packed = packed.astype(jnp.float32)
        other = (packed[STATE : STATE + 1], packed[:STATE])
        if extra is not None:
            extra = extra + jnp.sum(packed[STATE + 1 : STATE + 4, : extra.shape[0]], axis=0)
        leads = place == (0 if backward else 1)
        seen = (jnp.where(leads, other[0], 1.0), jnp.where(leads, other[1], 0.0))
        start = seen if start is None else chain_states(seen, start)
        if name != "y":
            forward = chain_states(other, total)
            reverse = chain_states(total, other)
            total = jax.tree.map(lambda p, q: jnp.where(leads, p, q), forward, reverse)
    return start[1] if extra is None else [start[1], extra]


KEYS = 512
PAIR = 2 * HEAD_DIM


def attention_forward(q_wide, kv, meta, starts, after=()):
    rows = q_wide.shape[2]
    blocks = kv.shape[0]
    ratio = HEADS_Q // HEADS_KV
    wide = min(512, rows)

    def kernel(meta_ref, q_ref, kv_ref, start_ref, o_ref, log_ref, top, total):
        b = pl.program_id(1)

        @pl.when(b == 0)
        def _():
            top[...] = jnp.full(top.shape, masked_score, jnp.float32)
            total[...] = jnp.zeros(total.shape, jnp.float32)
            o_ref[...] = jnp.zeros(o_ref.shape, jnp.float32)

        def block(partial):
            pair = kv_ref[0, 0]
            turned = pair.T[HEAD_DIM:, :]
            for h in range(ratio):
                for r in range(0, rows, wide):
                    here = slice(r, r + wide)
                    scores = jnp.dot(pair, q_ref[h, :, here], preferred_element_type=jnp.float32)
                    if partial:
                        keys = b * KEYS + lax.broadcasted_iota(jnp.int32, scores.shape, 0)
                        mine = meta_ref[2] + r + lax.broadcasted_iota(jnp.int32, scores.shape, 1)
                        visible = (keys >= start_ref[0:1, here]) & (keys <= mine)
                        scores = jnp.where(visible, scores, masked_score)
                    before = top[h, 0:1, here]
                    peak = jnp.maximum(before, jnp.max(scores, axis=0, keepdims=True))
                    part = jnp.exp(scores - peak)
                    if partial:
                        part = jnp.where(visible, part, 0.0)
                    fade = jnp.exp(before - peak)
                    top[h, 0:1, here] = peak
                    total[h, 0:1, here] = total[h, 0:1, here] * fade + jnp.sum(part, axis=0, keepdims=True)
                    o_ref[h, :, here] = o_ref[h, :, here] * fade + jnp.dot(
                        turned, part.astype(jnp.bfloat16), preferred_element_type=jnp.float32
                    )

        needed = (b >= meta_ref[0]) & (b < meta_ref[1])
        partial = ((b + 1) * KEYS > meta_ref[2]) | (b * KEYS < meta_ref[3])

        @pl.when(needed & partial)
        def _():
            block(True)

        @pl.when(needed & jnp.logical_not(partial))
        def _():
            block(False)

        @pl.when(b == blocks - 1)
        def _():
            for h in range(ratio):
                sums = total[h, 0:1, :]
                o_ref[h] = o_ref[h] / sums
                log_ref[h] = jnp.broadcast_to(top[h, 0:1, :] + jnp.log(sums), (8, rows))

    heads = lambda g, b, m: (g, 0, 0)
    return pl.pallas_call(
        pinned(kernel, 4, after),
        grid_spec=pltpu.PrefetchScalarGridSpec(
            num_scalar_prefetch=1,
            grid=(HEADS_KV, blocks),
            in_specs=[
                pl.BlockSpec((ratio, PAIR, rows), heads),
                pl.BlockSpec((1, 1, KEYS, PAIR), lambda g, b, m: (b, g, 0, 0)),
                pl.BlockSpec((8, rows), lambda g, b, m: (0, 0)),
            ] + pins(after),
            out_specs=[
                pl.BlockSpec((ratio, HEAD_DIM, rows), heads),
                pl.BlockSpec((ratio, 8, rows), heads),
            ],
            scratch_shapes=[
                pltpu.VMEM((ratio, 8, rows), jnp.float32),
                pltpu.VMEM((ratio, 8, rows), jnp.float32),
            ],
        ),
        out_shape=[
            jax.ShapeDtypeStruct((HEADS_Q, HEAD_DIM, rows), jnp.float32),
            jax.ShapeDtypeStruct((HEADS_Q, 8, rows), jnp.float32),
        ],
        compiler_params=pltpu.CompilerParams(vmem_limit_bytes=48 * 2**20),
        cost_estimate=pl.CostEstimate(flops=2 * 10**10, bytes_accessed=2**23, transcendentals=2**23),
        name="attend",
    )(meta, q_wide, kv, starts, *after)


def attention_backward(q_wide, g_wide, kv, logs, mixed, meta, starts, group, after=()):
    rows = q_wide.shape[2]
    blocks = kv.shape[0]
    ratio = HEADS_Q // HEADS_KV
    wide = min(512, rows)

    def kernel(meta_ref, q_ref, g_ref, kv_ref, log_ref, o_ref, start_ref, dkv_ref, dq_ref, delta, sums):
        b = pl.program_id(0)

        @pl.when(b == 0)
        def _():
            dq_ref[...] = jnp.zeros(dq_ref.shape, jnp.float32)
            for h in range(ratio):
                both = g_ref[h, HEAD_DIM:, :].astype(jnp.float32) * o_ref[h]
                delta[h] = jnp.broadcast_to(jnp.sum(both, axis=0, keepdims=True), (8, rows))

        def block(partial):
            pair = kv_ref[0, 0]
            turned = pair.T[:HEAD_DIM, :]
            for h in range(ratio):
                for r in range(0, rows, wide):
                    here = slice(r, r + wide)
                    q_now = q_ref[h, :, here]
                    g_now = g_ref[h, :, here]
                    scores = jnp.dot(pair, q_now, preferred_element_type=jnp.float32)
                    probs = jnp.exp(scores - log_ref[h, 0:1, here])
                    if partial:
                        keys = b * KEYS + lax.broadcasted_iota(jnp.int32, scores.shape, 0)
                        mine = meta_ref[2] + r + lax.broadcasted_iota(jnp.int32, scores.shape, 1)
                        visible = (keys >= start_ref[0:1, here]) & (keys <= mine)
                        probs = jnp.where(visible, probs, 0.0)
                    grads = jnp.dot(pair, g_now, preferred_element_type=jnp.float32)
                    low_grads = (probs * (grads - delta[h, 0:1, here])).astype(jnp.bfloat16)
                    change = lax.dot_general(
                        probs.astype(jnp.bfloat16), g_now, NT, preferred_element_type=jnp.float32
                    ) + lax.dot_general(low_grads, q_now, NT, preferred_element_type=jnp.float32)
                    if h == 0 and r == 0:
                        sums[...] = change
                    else:
                        sums[...] += change
                    dq_ref[h, :, here] += jnp.dot(turned, low_grads, preferred_element_type=jnp.float32)
            dkv_ref[0, 0] = sums[...].astype(jnp.bfloat16)

        needed = (b >= meta_ref[0]) & (b < meta_ref[1])
        partial = ((b + 1) * KEYS > meta_ref[2]) | (b * KEYS < meta_ref[3])

        @pl.when(needed & partial)
        def _():
            block(True)

        @pl.when(needed & jnp.logical_not(partial))
        def _():
            block(False)

        @pl.when(jnp.logical_not(needed))
        def _():
            dkv_ref[0, 0] = jnp.zeros((KEYS, PAIR), jnp.bfloat16)

    heads = lambda b, m: (group, 0, 0)
    return pl.pallas_call(
        pinned(kernel, 7, after),
        grid_spec=pltpu.PrefetchScalarGridSpec(
            num_scalar_prefetch=1,
            grid=(blocks,),
            in_specs=[
                pl.BlockSpec((ratio, PAIR, rows), heads),
                pl.BlockSpec((ratio, PAIR, rows), heads),
                pl.BlockSpec((1, 1, KEYS, PAIR), lambda b, m: (b, group, 0, 0)),
                pl.BlockSpec((ratio, 8, rows), heads),
                pl.BlockSpec((ratio, HEAD_DIM, rows), heads),
                pl.BlockSpec((8, rows), lambda b, m: (0, 0)),
            ] + pins(after),
            out_specs=[
                pl.BlockSpec((1, 1, KEYS, PAIR), lambda b, m: (b, 0, 0, 0)),
                pl.BlockSpec((ratio, HEAD_DIM, rows), lambda b, m: (0, 0, 0)),
            ],
            scratch_shapes=[
                pltpu.VMEM((ratio, 8, rows), jnp.float32),
                pltpu.VMEM((KEYS, PAIR), jnp.float32),
            ],
        ),
        out_shape=[
            jax.ShapeDtypeStruct((blocks, 1, KEYS, PAIR), jnp.bfloat16),
            jax.ShapeDtypeStruct((ratio, HEAD_DIM, rows), jnp.float32),
        ],
        compiler_params=pltpu.CompilerParams(vmem_limit_bytes=48 * 2**20),
        cost_estimate=pl.CostEstimate(flops=2 * 10**10, bytes_accessed=2**23, transcendentals=2**23),
        name="attend_back",
    )(meta, q_wide, g_wide, kv, logs, mixed, starts, *after)


def scatter_span(value, span, fast):
    if not fast:
        return lax.psum_scatter(value, span, scatter_dimension=0).astype(jnp.float32)
    flow = Flow(scatter_stages(value))
    while flow.sends:
        flow.go()
    return flow.result


def scatter_stages(value):
    _, y, x, c = (lax.axis_index(name) for name in GRID)
    value = value.reshape((2, 2, 2) + value.shape[1:])
    for name, place, axis in (("c", c, 2), ("y", y, 0), ("x", x, 0)):
        send = lax.dynamic_index_in_dim(value, 1 - place, axis, keepdims=False)
        (arrived,) = yield [(send, name, SWAP)]
        keep = lax.dynamic_index_in_dim(value, place, axis, keepdims=False)
        value = keep.astype(jnp.float32) + arrived.astype(jnp.float32)
        if name != "x":
            value = value.astype(jnp.bfloat16)
    return value


def plane_stages(value):
    for pairs in ([(0, 1), (1, 0), (2, 3), (3, 2)], [(0, 2), (2, 0), (1, 3), (3, 1)]):
        (other,) = yield [(value, "z", pairs)]
        value = value + other
    return value


def offsets_of():
    places, at = {}, 0
    for name_key, extent in layout():
        places[name_key] = (at, extent)
        at += math.prod(extent)
    return places


def early_weights(params):
    places = offsets_of()
    buffers, spread_flow, (slots, all_slots), where = gather_lines(params)
    spread_flow.go()
    names = (W_QUERY, W_KEY, W_VALUE, W_ATTN_OUT, W_GATE_SSM, W_X_SSM, W_B_C)
    misc_at = places[W_STEP][0]
    first = unpack_lines(
        buffers[:16], slots, where, [flat_segment(name_key) for name_key in names] + [(0, 16, LINE), (misc_at, 288, LINE)]
    )
    weights = dict(zip(names, first))
    weights[NORM_ATTN] = first[-2].reshape(-1)[:D]
    misc = first[-1].reshape(-1)
    for name_key in (W_STEP,) + small_names[1:-1]:
        at, extent = places[name_key]
        weights[name_key] = misc[at - misc_at : at - misc_at + math.prod(extent)].reshape(extent)
    return weights, spread_flow, (buffers, all_slots, where)


def flat_segment(name_key):
    at, extent = offsets_of()[name_key]
    return (at, extent[0], extent[1])


def late_weights(held, after):
    buffers, slots, where = held
    names = (W_SSM_OUT, W_GATE, W_UP_PROJ, W_DOWN)
    norm_at = offsets_of()[NORM_FFN][0]
    second = unpack_lines(
        buffers, slots, where, [flat_segment(name_key) for name_key in names] + [(norm_at, 16, LINE)], after
    )
    weights = dict(zip(names, second))
    weights[NORM_FFN] = second[-1].reshape(-1)[norm_at % LINE : norm_at % LINE + D]
    return weights


def pack_late(gate, up, down, ssm_low, grad_branch, grad_norm_ffn, after):
    places = offsets_of()
    out_at = places[W_SSM_OUT][0]
    lane = places[W_GATE][0] % LINE
    boundary = 2 * PLANE * LINE
    tail_from = (boundary - out_at) // D
    tail = matmul_left_t(ssm_low[:, tail_from:], grad_branch).reshape(-1)
    tail = tail[boundary - out_at - tail_from * D :]
    head = jnp.concatenate([jnp.zeros((14 * LINE,), jnp.float32), tail, grad_norm_ffn])
    head_rows = head.shape[0] // LINE
    carry = jnp.zeros((8, LINE), jnp.float32).at[7, :lane].set(head[head_rows * LINE :])
    head = head[: head_rows * LINE].reshape(head_rows, LINE).astype(jnp.bfloat16)
    return pack_lines(
        None, 2 * PLANE + 32, head_rows, [gate, up, down], lane, 0, [(head, 0)], carry, 48, after
    )


def pack_out(ssm_low, grad_branch, after):
    out_at = offsets_of()[W_SSM_OUT][0]
    first_row = (8 + out_at // LINE) // 16 * 16
    rows = first_row + SSM_HEADS * SSM_DIM * D // LINE
    return pack_lines(
        None, rows, first_row, [(ssm_low, grad_branch)], out_at % LINE, (8 + out_at // LINE) % 8, [],
        jnp.zeros((8, LINE), jnp.float32), 0, after,
    )


def pack_ssm(target, segments, small, ssm_low, grad_branch, after):
    places = offsets_of()
    misc = [small[name_key].reshape(-1) for name_key in (W_STEP,) + small_names[1:-1]]
    count = sum(part.shape[0] for part in misc)
    misc_rows = (count // LINE + 16) // 16 * 16
    opening = matmul_left_t(ssm_low[:, :16], grad_branch).reshape(-1)
    misc = jnp.concatenate(misc + [opening[: misc_rows * LINE - count]])
    misc = misc.reshape(misc_rows, LINE).astype(jnp.bfloat16)
    first_row = 8 + places[W_ATTN_OUT][0] // LINE
    return pack_lines(
        target, target.shape[0], first_row, segments, 0, 0, [(misc, 8 + places[W_STEP][0] // LINE)], None, 0, after
    )


def pack_qkv(segments, attended, grad_branch, grad_norm_attn, after):
    places = offsets_of()
    out_row = 8 + places[W_ATTN_OUT][0] // LINE
    rows = (8 + SHARD) // 16 * 16 + 8 * PIECE
    closing = matmul_left_t(attended[:, :16], grad_branch).reshape(-1, LINE)
    closing = closing[: rows - out_row].astype(jnp.bfloat16)
    opening = jnp.concatenate([jnp.zeros((8, LINE), jnp.float32), grad_norm_attn.reshape(-1, LINE)]).astype(jnp.bfloat16)
    return pack_lines(
        None, rows, 16, segments, 0, 0, [(opening, 0), (closing, out_row)], None, 0, after
    )


def own_lines(early, late, corner):
    z, y, x, c = (lax.axis_index(name) for name in GRID)
    place = 4 * y + 2 * x + c
    shard = SHARD * place
    start = jnp.where(z < 2, (8 + shard) % 16, (14 + shard) % 16)
    lines = jnp.where(z < 2, early, late)
    lines = jnp.where((z == 0) & (place < 2), corner[:WIN], lines)
    lines = lax.dynamic_slice(lines, (start, 0), (SHARD, LINE)).astype(jnp.float32)
    return lines.reshape(-1)


def body(span, group, fast, tokens, params, cotangent, offsets):
    rows_dev = tokens.shape[0]
    group_rows = rows_dev * lax.axis_size(span)
    all_rows = group_rows * lax.axis_size(group)
    ssm_inner = SSM_HEADS * SSM_DIM
    score_scale = HEAD_DIM ** (-0.5)
    bounds = offsets[0]
    my_start = lax.axis_index(span) * rows_dev
    row_index = my_start + jnp.arange(rows_dev, dtype=jnp.int32)
    seq_id, positions = sequence_info(row_index, bounds)
    first_start = row_index[0] - positions[0]
    last_row = my_start + rows_dev - 1
    cosine, sine = rotary_tables(positions)
    if fast:
        weights, spread_flow, held = early_weights(params)
    else:
        weights = unpack(lax.all_gather(params, group + span, axis=0, tiled=True))
    small_f32 = {name_key: weights[name_key].astype(jnp.float32) for name_key in small_names[:-1]}
    x_rows = tokens.astype(jnp.float32)
    normed_one, norm_one_back = jax.vjp(rms_norm, x_rows, small_f32[NORM_ATTN])
    hidden = normed_one.astype(jnp.bfloat16)
    across = lambda weight: lax.dot_general(
        weight, hidden, (((0,), (1,)), ((), ())), preferred_element_type=jnp.float32
    )
    q_rot = rotate(across(weights[W_QUERY]), cosine, sine, HEADS_Q).astype(jnp.bfloat16)
    k_rot = rotate(across(weights[W_KEY]), cosine, sine, HEADS_KV).astype(jnp.bfloat16)
    value_low = across(weights[W_VALUE]).astype(jnp.bfloat16).reshape(HEADS_KV, HEAD_DIM, rows_dev)
    kv_mine = jnp.concatenate([k_rot, value_low], axis=1).transpose(0, 2, 1)
    row_starts = row_index - positions
    kv_local = kv_mine.reshape(HEADS_KV, rows_dev, PAIR)
    xbc = jnp.concatenate(
        [matmul(hidden, weights[W_X_SSM]), matmul(hidden, weights[W_B_C])], axis=1
    )
    step_raw = matmul(hidden, weights[W_STEP])
    q_wide = jnp.pad(q_rot * jnp.bfloat16(score_scale), ((0, 0), (0, HEAD_DIM), (0, 0)))
    rim_source = xbc[rows_dev - 8 :]
    if fast:
        (rim_source,) = fence([rim_source], [q_wide])
    rim_rows = passed_along(rim_source, span, 1)
    ssm_meta = jnp.concatenate([my_start[None], row_starts[CHUNK - 1 :: CHUNK]]).astype(jnp.int32)
    conv_bias = small_f32[CONV_BIAS][None, :]
    convolve = lambda after: conv_forward(
        xbc, rim_rows, small_f32[CONV_WEIGHT], conv_bias, ssm_meta, row_starts[:, None], after
    )
    if fast:
        key_blocks = lax.all_gather(kv_local, span)
        conv_values = convolve(())
    else:
        conv_values = convolve(())
    step_in = step_raw.T + small_f32[STEP_BIAS][:, None]
    step_rows = jax.nn.softplus(step_in)
    decay = -jnp.exp(small_f32[DECAY_LOG])
    logs_step = step_rows * decay[:, None]
    order = jnp.arange(rows_dev)
    upto = (order[:, None] <= order[None, :]).astype(jnp.float32)
    cumul = jnp.dot(logs_step, upto, precision=highest)
    chunk_cum = jnp.dot(
        logs_step.reshape(-1, CHUNK), upto[:CHUNK, :CHUNK], precision=highest
    ).reshape(SSM_HEADS, rows_dev)
    went_on = row_starts < my_start
    entry_rows = jnp.where(went_on[None, :], jnp.exp(cumul), 0.0)
    in_last = row_index >= row_starts[rows_dev - 1]
    tail_rows = jnp.exp(jnp.where(in_last[None, :], cumul[:, -1:] - cumul, masked_score))
    carry_all = entry_rows[:, -1]
    summarize = lambda after: weighted_state(conv_values, PAIRS, conv_values, tail_rows * step_rows, after)
    meta = jnp.stack(
        [first_start // KEYS, last_row // KEYS + 1, my_start, row_starts[rows_dev - 1]]
    ).astype(jnp.int32)
    start_row = jnp.broadcast_to(row_starts[None, :], (8, rows_dev))
    if fast:
        (local_state,) = bracket(summarize, [spread_flow])
        scan = Flow(scan_stages(carry_all, local_state, False))
        (gate_in,) = fence([hidden], scan.values())
        gate_ssm = matmul(gate_in, weights[W_GATE_SSM])
        scan.go()
        (gate_ssm,) = fence([gate_ssm], scan.values())
        scan.go()
        mixed, logs = bracket(
            lambda after: attention_forward(
                q_wide, key_blocks, meta, start_row, (*after, gate_ssm, *spread_flow.values())
            ),
            [scan],
        )
        spread_flow.go()
        state_in = scan.result
    else:
        gate_ssm = matmul(hidden, weights[W_GATE_SSM])
        key_blocks = lax.all_gather(kv_local, span)
        if rows_dev != KEYS:
            key_blocks = key_blocks.transpose(1, 0, 2, 3).reshape(HEADS_KV, -1, KEYS, PAIR).transpose(1, 0, 2, 3)
        state_in = scan_states(carry_all, summarize(()), span, fast, False)
        mixed, logs = attention_forward(q_wide, key_blocks, meta, start_row)
    attended = mixed.astype(jnp.bfloat16).reshape(HEADS_Q * HEAD_DIM, rows_dev).T
    attn_out = matmul(attended, weights[W_ATTN_OUT])
    skip_wide = jnp.repeat(small_f32[SKIP_GAIN], SSM_DIM)[None, :]
    ssm_y = ssm_forward(
        conv_values, chunk_cum, step_rows, state_in, skip_wide, ssm_meta, row_starts[:, None], start_row
    )
    normed_ssm, gnorm_back = jax.vjp(gated_norm, ssm_y, gate_ssm, small_f32[NORM_SSM])
    ssm_low = normed_ssm.astype(jnp.bfloat16)
    if fast:
        held = (held[0] + spread_flow.result,) + held[1:]
        weights.update(late_weights(held, [ssm_y]))
    small_f32[NORM_FFN] = weights[NORM_FFN].astype(jnp.float32)
    ssm_out = matmul(ssm_low, weights[W_SSM_OUT])
    middle = x_rows + attn_out + ssm_out
    normed_two, norm_two_back = jax.vjp(rms_norm, middle, small_f32[NORM_FFN])
    hidden_two = normed_two.astype(jnp.bfloat16)
    gate_ffn = matmul(hidden_two, weights[W_GATE])
    upper = matmul(hidden_two, weights[W_UP_PROJ])
    activation_f32, swiglu_back = jax.vjp(swiglu, gate_ffn, upper)
    activation = activation_f32.astype(jnp.bfloat16)
    ffn_out = matmul(activation, weights[W_DOWN])
    result = middle + ffn_out
    squares = jnp.stack(
        [
            jnp.sum(result * result),
            jnp.sum(attn_out * attn_out),
            jnp.sum(ssm_out * ssm_out),
            jnp.sum(ffn_out * ffn_out),
        ]
    )
    grad_out = cotangent.astype(jnp.float32)
    grad_activation = matmul_right_t(cotangent, weights[W_DOWN])
    grad_gate_f32, grad_upper_f32 = swiglu_back(grad_activation)
    grad_gate = grad_gate_f32.astype(jnp.bfloat16)
    grad_upper = grad_upper_f32.astype(jnp.bfloat16)
    grad_hidden_two = matmul_right_t(grad_gate, weights[W_GATE]) + matmul_right_t(
        grad_upper, weights[W_UP_PROJ]
    )
    grad_middle_norm, grad_norm_ffn = norm_two_back(grad_hidden_two)
    grad_middle = grad_out + grad_middle_norm
    grad_branch = grad_middle.astype(jnp.bfloat16)
    grad_attended = matmul_right_t(weights[W_ATTN_OUT], grad_branch).astype(jnp.bfloat16)
    grad_ssm_low = matmul_right_t(grad_branch, weights[W_SSM_OUT])
    grad_ssm_y, grad_gate_ssm_f32, grad_norm_ssm = gnorm_back(grad_ssm_low)
    grad_state_local = weighted_state(conv_values, PAIRS + 1, grad_ssm_y, entry_rows)
    if fast:
        scan = Flow(scan_stages(carry_all, grad_state_local, True, squares)).go()
        (late,) = bracket(
            lambda after: pack_late(
                (hidden_two, grad_gate), (hidden_two, grad_upper), (activation, cotangent),
                ssm_low, grad_branch, grad_norm_ffn, after,
            ),
            [scan],
        )
        late_flow = Flow(reduce_stages(late, 1, 14))
        (grad_branch_low,) = fence([grad_branch], scan.values() + late_flow.values())
        early = pack_out(ssm_low, grad_branch_low, ())
        scan.go()
        grad_state_out, squares = scan.result
        (early,) = fence([early], [grad_state_out])
        late_flow.go()
        (early,) = fence([early], late_flow.values())
        stats_flow = Flow(plane_stages(squares))

        def around(call):
            out = bracket(lambda after: call((*after, *stats_flow.values())), [late_flow])
            stats_flow.go(out[:1])
            return out

    else:
        grad_state_out = scan_states(carry_all, grad_state_local, span, fast, True)
        around = lambda call: call(())
    grad_x, grad_b, grad_c, grad_small = around(
        lambda after: ssm_backward(
            conv_values, grad_ssm_y, chunk_cum, step_rows, state_in, grad_state_out, skip_wide, ssm_meta, start_row,
            after,
        )
    )
    grad_direct = grad_small[:, 0:2].reshape(SSM_HEADS, rows_dev)
    grad_logs = grad_small[:, 2:4].reshape(SSM_HEADS, rows_dev)
    grad_decay_log = decay * jnp.sum(step_rows * grad_logs, axis=1)
    grad_step_rows = (grad_direct + decay[:, None] * grad_logs) * jax.nn.sigmoid(step_in)
    grad_step_bias = jnp.sum(grad_step_rows, axis=1)
    grad_step_raw_f32 = grad_step_rows.T
    grad_skip_gain = jnp.sum(grad_small[:, 4, : 2 * SSM_DIM].reshape(SSM_HEADS, SSM_DIM), axis=1)
    grad_main, grad_tail, grad_edge, grad_taps = around(
        lambda after: conv_backward(
            grad_x, grad_b, grad_c, xbc, rim_rows, small_f32[CONV_WEIGHT], conv_bias, ssm_meta,
            row_starts[:, None], after,
        )
    )
    grad_conv_weight = grad_taps[:CONV]
    grad_conv_bias = grad_taps[CONV]
    rim_back = passed_along(grad_edge, span, -1)
    grad_tail = grad_tail + jnp.pad(rim_back, ((8, 0), (0, 0)))
    grad_xbc = lax.dynamic_update_slice(grad_main, grad_tail.astype(jnp.bfloat16), (rows_dev - 16, 0))
    grad_gate_ssm = grad_gate_ssm_f32.astype(jnp.bfloat16)
    grad_step_raw = grad_step_raw_f32.astype(jnp.bfloat16)
    grad_w_step = matmul_left_t(hidden, grad_step_raw)
    grad_hidden_ssm = (
        matmul_right_t(grad_gate_ssm, weights[W_GATE_SSM])
        + matmul_right_t(grad_xbc[:, :ssm_inner], weights[W_X_SSM])
        + matmul_right_t(grad_xbc[:, ssm_inner:], weights[W_B_C])
        + matmul_right_t(grad_step_raw, weights[W_STEP])
    )
    small = {
        W_STEP: grad_w_step,
        CONV_WEIGHT: grad_conv_weight,
        CONV_BIAS: grad_conv_bias,
        STEP_BIAS: grad_step_bias,
        DECAY_LOG: grad_decay_log,
        SKIP_GAIN: grad_skip_gain,
        NORM_SSM: grad_norm_ssm,
        NORM_FFN: grad_norm_ffn,
    }
    parts = []
    if fast:
        early = pack_ssm(
            early,
            [
                (attended, grad_branch), (hidden, grad_gate_ssm),
                (hidden, grad_xbc[:, :ssm_inner]), (hidden, grad_xbc[:, ssm_inner:]),
            ],
            small, ssm_low, grad_branch, late_flow.values(),
        )
        early_flow = Flow(reduce_stages(early, 0, 8))
        (grad_attended,) = fence([grad_attended], early_flow.values() + late_flow.values())
        around = lambda call: bracket(call, [early_flow])
    g_wide = jnp.pad(grad_attended.reshape(HEADS_Q, HEAD_DIM, rows_dev), ((0, 0), (HEAD_DIM, 0), (0, 0)))
    if fast:
        early_flow.go()
        (g_wide,) = fence([g_wide], early_flow.values())
    for group_at in range(HEADS_KV):
        after_part = [part[1] for part in parts]
        if fast and group_at == 0:
            after_part = late_flow.values()
        parts.append(
            around(
                lambda after: attention_backward(
                    q_wide, g_wide, key_blocks, logs, mixed, meta, start_row, group_at, (*after, *after_part)
                )
            )
        )
    grad_kv = jnp.concatenate([part[0] for part in parts], axis=1)
    grad_q_turned = jnp.concatenate([part[1] for part in parts], axis=0)
    if rows_dev != KEYS:
        grad_kv = grad_kv.transpose(1, 0, 2, 3).reshape(HEADS_KV, -1, rows_dev, PAIR).transpose(1, 0, 2, 3)
    if fast:
        late_flow.go([parts[-1][1]])
        scatter = Flow(scatter_stages(grad_kv))
        (grad_q_turned,) = fence([grad_q_turned], scatter.values() + early_flow.values() + late_flow.values())
    turned_back = rotate(grad_q_turned * score_scale, cosine, -sine, HEADS_Q).astype(jnp.bfloat16)
    grad_query_low = turned_back.reshape(HEADS_Q * HEAD_DIM, rows_dev).T
    if fast:
        scatter.go()
        early_flow.go()
        (grad_query_low,) = fence([grad_query_low], scatter.values() + early_flow.values())
    grad_hidden = grad_hidden_ssm + matmul_right_t(grad_query_low, weights[W_QUERY])
    if fast:
        scatter.go()
        (grad_hidden,) = fence([grad_hidden], scatter.values())
        scatter.go()
        grad_kv_mine = scatter.result
    else:
        grad_kv_mine = scatter_span(grad_kv, span, fast)
    grad_kv_mine = grad_kv_mine.transpose(0, 2, 1)
    grad_key_low = rotate(grad_kv_mine[:, :HEAD_DIM], cosine, -sine, HEADS_KV).astype(jnp.bfloat16)
    grad_key_low = grad_key_low.reshape(HEADS_KV * HEAD_DIM, rows_dev).T
    grad_value_low = grad_kv_mine[:, HEAD_DIM:].astype(jnp.bfloat16).reshape(HEADS_KV * HEAD_DIM, rows_dev).T
    grad_hidden = (
        grad_hidden
        + matmul_right_t(grad_key_low, weights[W_KEY])
        + matmul_right_t(grad_value_low, weights[W_VALUE])
    )
    grad_x_norm, grad_norm_attn = norm_one_back(grad_hidden)
    grad_tokens = grad_middle + grad_x_norm
    if fast:
        corner = pack_qkv(
            [(hidden, grad_query_low), (hidden, grad_key_low), (hidden, grad_value_low)],
            attended, grad_branch, grad_norm_attn, early_flow.values(),
        )
        corner_flow = Flow(corner_stages(corner))
        for _ in range(3):
            corner_flow.go()
        early_flow.go(corner_flow.values()[:1])
        ((pieces, _, _), *_) = corner_flow.sends
        (pieces,) = fence([pieces], early_flow.values())
        corner_flow.sends = [(pieces, axis, pairs) for _, axis, pairs in corner_flow.sends]
        for flow in (early_flow, late_flow, corner_flow):
            while flow.sends:
                flow.go()
        stats = jnp.sqrt(stats_flow.result / (all_rows * D))
        grad_shard = own_lines(early_flow.result, late_flow.result, corner_flow.result)
        return (result.astype(jnp.bfloat16), grad_tokens, grad_shard, stats)
    small[NORM_ATTN] = grad_norm_attn
    stats = jnp.sqrt(lax.psum(squares, group + span) / (all_rows * D))
    pairs = {
        W_QUERY: (hidden, grad_query_low),
        W_KEY: (hidden, grad_key_low),
        W_VALUE: (hidden, grad_value_low),
        W_ATTN_OUT: (attended, grad_branch),
        W_GATE_SSM: (hidden, grad_gate_ssm),
        W_X_SSM: (hidden, grad_xbc[:, :ssm_inner]),
        W_B_C: (hidden, grad_xbc[:, ssm_inner:]),
        W_SSM_OUT: (ssm_low, grad_branch),
        W_GATE: (hidden_two, grad_gate),
        W_UP_PROJ: (hidden_two, grad_upper),
        W_DOWN: (activation, cotangent),
    }
    grad_dict = dict(small)
    for name_key, (left, right) in pairs.items():
        grad_dict[name_key] = matmul_left_t(left, right)
    flat_parts = [grad_dict[name_key].reshape(-1) for name_key, extent in layout()]
    used_entries = 0
    for part_array in flat_parts:
        used_entries += part_array.shape[0]
    flat_parts.append(jnp.zeros((params.shape[0] * lax.axis_size(group + span) - used_entries,), jnp.float32))
    grad_shard = lax.psum_scatter(
        jnp.concatenate(flat_parts), group + span, scatter_dimension=0, tiled=True
    )
    return (result.astype(jnp.bfloat16), grad_tokens, grad_shard, stats)


def solution(mesh):
    fast = (mesh.shape["group"], mesh.shape["span"]) == FAST
    if fast:
        mesh = Mesh(mesh.devices.reshape(4, 2, 2, 2), GRID)
        group, span = (GRID[:1], GRID[1:])
    else:
        group, span = (("group",), ("span",))

    def program(tokens, params, cotangent, offsets):
        return body(span, group, fast, tokens, params, cotangent, offsets)

    return jax.shard_map(
        program,
        mesh=mesh,
        in_specs=(P(group + span, None), P(group + span), P(group + span, None), P(group, None)),
        out_specs=(P(group + span, None), P(group + span, None), P(group + span), P()),
        check_vma=False,
    )
```

```python
import math

import jax
import jax.numpy as jnp
import numpy as np
from jax import lax
from jax.experimental import pallas as pl
from jax.experimental.pallas import tpu as pltpu
from jax.sharding import Mesh, PartitionSpec as P

D = 1024
HEADS_Q = 8
HEADS_KV = 2
HEAD_DIM = 64
SSM_HEADS = 24
SSM_DIM = 64
STATE = 128
CONV = 4
FF = 2048
(
    NORM_ATTN,
    W_QUERY,
    W_KEY,
    W_VALUE,
    W_ATTN_OUT,
    W_GATE_SSM,
    W_X_SSM,
    W_B_C,
    W_STEP,
    CONV_WEIGHT,
    CONV_BIAS,
    STEP_BIAS,
    DECAY_LOG,
    SKIP_GAIN,
    NORM_SSM,
    W_SSM_OUT,
    NORM_FFN,
    W_GATE,
    W_UP_PROJ,
    W_DOWN,
) = range(20)


epsilon = 1e-05
rope_base = 100000000000.0
masked_score = -1e30
highest = lax.Precision.HIGHEST
small_names = (
    NORM_ATTN,
    CONV_WEIGHT,
    CONV_BIAS,
    STEP_BIAS,
    DECAY_LOG,
    SKIP_GAIN,
    NORM_SSM,
    NORM_FFN,
)


def passed_along(value, axis, steps):
    count = lax.axis_size(axis)
    first, last = (max(0, -steps), min(count, count - steps))
    return lax.ppermute(value, axis, [(source, source + steps) for source in range(first, last)])


def prefix(value, axis, combine, identity):
    peers, place = (lax.axis_size(axis), lax.axis_index(axis))
    everything = jax.tree.map(
        lambda part, kind: lax.all_gather(part.astype(kind), axis),
        value,
        (jnp.bfloat16, jnp.bfloat16),
    )
    start = jax.tree.map(
        lambda part, zero: jnp.broadcast_to(jnp.asarray(zero, part.dtype), part.shape),
        value,
        identity,
    )

    def prefix_turn(k, before):
        reached = k < place
        new = combine(
            before, jax.tree.map(lambda part, own: part[k].astype(own.dtype), everything, value)
        )
        return jax.tree.map(lambda a, b: jnp.where(reached, a, b), new, before)

    return lax.fori_loop(0, peers, prefix_turn, start)


def carried_in(value, axis, combine, identity):
    peers, place = (lax.axis_size(axis), lax.axis_index(axis))
    everything = jax.tree.map(
        lambda part, kind: lax.all_gather(part.astype(kind), axis),
        value,
        jax.tree.map(lambda a: jnp.bfloat16 if a.dtype == jnp.float32 else a.dtype, value),
    )
    start = jax.tree.map(
        lambda part, zero: jnp.broadcast_to(jnp.asarray(zero, part.dtype), part.shape),
        value,
        identity,
    )

    def carried_turn(k, before):
        at = peers - 1 - k
        reached = at > place
        new = combine(
            before, jax.tree.map(lambda part, own: part[at].astype(own.dtype), everything, value)
        )
        return jax.tree.map(lambda a, b: jnp.where(reached, a, b), new, before)

    return lax.fori_loop(0, peers, carried_turn, start)


def layout():
    ssm_inner = SSM_HEADS * SSM_DIM
    channels = ssm_inner + 2 * STATE
    return [
        (NORM_ATTN, (D,)),
        (W_QUERY, (D, HEADS_Q * HEAD_DIM)),
        (W_KEY, (D, HEADS_KV * HEAD_DIM)),
        (W_VALUE, (D, HEADS_KV * HEAD_DIM)),
        (W_ATTN_OUT, (HEADS_Q * HEAD_DIM, D)),
        (W_GATE_SSM, (D, ssm_inner)),
        (W_X_SSM, (D, ssm_inner)),
        (W_B_C, (D, 2 * STATE)),
        (W_STEP, (D, SSM_HEADS)),
        (CONV_WEIGHT, (CONV, channels)),
        (CONV_BIAS, (channels,)),
        (STEP_BIAS, (SSM_HEADS,)),
        (DECAY_LOG, (SSM_HEADS,)),
        (SKIP_GAIN, (SSM_HEADS,)),
        (NORM_SSM, (ssm_inner,)),
        (W_SSM_OUT, (ssm_inner, D)),
        (NORM_FFN, (D,)),
        (W_GATE, (D, FF)),
        (W_UP_PROJ, (D, FF)),
        (W_DOWN, (FF, D)),
    ]


def unpack(flat_vector):
    unpacked = {}
    offset = 0
    for name_key, extent in layout():
        amount = math.prod(extent)
        unpacked[name_key] = flat_vector[offset : offset + amount].reshape(extent)
        offset += amount
    return unpacked


def matmul(left, right):
    return jnp.dot(left, right, preferred_element_type=jnp.float32)


def matmul_left_t(left, right):
    return lax.dot_general(
        left, right, (((0,), (0,)), ((), ())), preferred_element_type=jnp.float32
    )


def matmul_right_t(left, right):
    return lax.dot_general(
        left, right, (((1,), (1,)), ((), ())), preferred_element_type=jnp.float32
    )


def rms_norm(values, gain):
    return values * lax.rsqrt(jnp.mean(values * values, axis=-1, keepdims=True) + epsilon) * gain


def gated_norm(ssm_y, gate_ssm, gain):
    return rms_norm(ssm_y * jax.nn.silu(gate_ssm), gain)


def swiglu(gate_ffn, upper):
    return jax.nn.silu(gate_ffn) * upper


def sequence_info(row_index, bounds):
    starts = bounds[:-1]
    inside = row_index[:, None] >= starts[None, :]
    seq_id = jnp.sum(inside.astype(jnp.int32), axis=1) - 1
    seq_start = jnp.max(jnp.where(inside, starts[None, :], 0), axis=1)
    return (seq_id, row_index - seq_start)


def rotary_tables(positions):
    half_dim = HEAD_DIM // 2
    freqs = jnp.exp(
        -jnp.arange(half_dim, dtype=jnp.float32) * (2.0 * math.log(rope_base) / HEAD_DIM)
    )
    angles = freqs[:, None] * positions.astype(jnp.float32)[None, :]
    return (jnp.cos(angles), jnp.sin(angles))


def rotate(values, cosine, sine, heads):
    halves = values.reshape(heads, 2, HEAD_DIM // 2, -1)
    first_half, second_half = halves[:, 0], halves[:, 1]
    turned = jnp.stack(
        [first_half * cosine - second_half * sine, second_half * cosine + first_half * sine], axis=1
    )
    return turned.reshape(heads, HEAD_DIM, -1)


def add_rows(target, addend, first_row):
    current = lax.dynamic_slice_in_dim(target, first_row, addend.shape[0], 0)
    return lax.dynamic_update_slice_in_dim(target, current + addend, first_row, 0)


FAST = (4, 8)
LINE = 128
SHARD = 3082
SPAD = 3088
WIN = 3104
PLANE = 8 * SHARD
DEPTH = 4
TALL = {1: 1024, 2: 1024, 4: 512, 8: 256, 12: 128, 16: 128}
GRID = ("z", "y", "x", "c")
ZC = ("z", "c")
SWAP = [(0, 1), (1, 0)]


def zc_pairs(*pairs):
    return [(2 * a + c, 2 * b + c) for a, b, c in pairs]


def pinned(kernel, count, after):
    return lambda *refs: kernel(*refs[:count], *refs[count + len(after) :])


def pins(after):
    return [pl.BlockSpec(memory_space=pltpu.HBM)] * len(after)


class Flow:
    def __init__(self, stages):
        self.stages = stages
        self.sends = next(stages)
        self.result = None

    def values(self):
        return [value for value, _, _ in self.sends] or (list(self.result) if isinstance(self.result, list) else [self.result])

    def hold(self, after):
        held = fence(self.values(), after)
        self.sends = [(value, axis, pairs) for value, (_, axis, pairs) in zip(held, self.sends)]

    def go(self, after=()):
        arrived = [lax.ppermute(value, axis, pairs) for value, axis, pairs in self.sends]
        if after:
            arrived = fence(arrived, after)
        try:
            self.sends = self.stages.send(arrived)
        except StopIteration as stop:
            self.sends, self.result = [], stop.value
        return self


def fence(values, after):
    def kernel(*refs):
        del refs

    return pl.pallas_call(
        kernel,
        in_specs=pins(values) + pins(after),
        out_specs=pins(values),
        out_shape=[jax.ShapeDtypeStruct(value.shape, value.dtype) for value in values],
        input_output_aliases={k: k for k in range(len(values))},
        name="fence",
    )(*values, *after)


def bracket(call, flows):
    out = call([value for flow in flows for value in flow.values()])
    out = list(out) if isinstance(out, (list, tuple)) else [out]
    for flow in flows:
        flow.go()
    return fence(out, [v for flow in flows for v in flow.values()])


def gather_lines(params):
    z, y, x, c = (lax.axis_index(name) for name in GRID)
    lines = jnp.pad(params.reshape(SHARD, LINE), ((0, SPAD - SHARD), (0, 0)))
    sibling = lax.ppermute(lines, ZC, [(2 * k + 1 - k % 2, 2 * k + k % 2) for k in range(4)])
    buffers = []
    for part in range(2):
        here = jnp.where(c == part, lines, sibling)
        one = lax.ppermute(here, ZC, zc_pairs((0, 1, 0), (1, 2, 1)))
        side = lax.ppermute(here, ZC, zc_pairs((1, 0, 1)))
        two = lax.ppermute(one, ZC, zc_pairs((1, 2, 0), (2, 3, 1)))
        three = lax.ppermute(two, ZC, zc_pairs((2, 3, 0)))
        column = jnp.where(z == c, here, one + side + two + three)
        over_x = lax.ppermute(column, "x", SWAP)
        over_y = lax.ppermute(column, "y", SWAP)
        corner = lax.ppermute(over_y if part else over_x, "x" if part else "y", SWAP)
        local = [column, over_x, over_y, corner]
        buffers += [piece[None] for piece in local]
        buffers += [lax.ppermute(piece, "c", SWAP)[None] for piece in local]
    early = [(k, 0) for k in range(16)]
    here = jnp.where(c == 0, jnp.stack([lines, sibling]), jnp.stack([sibling, lines]))
    one = lax.ppermute(here, ZC, zc_pairs((2, 1, 0), (3, 2, 1)))
    side = lax.ppermute(here, ZC, zc_pairs((2, 3, 0)))
    two = lax.ppermute(one, ZC, zc_pairs((1, 0, 0), (2, 1, 1)))
    three = lax.ppermute(two, ZC, zc_pairs((1, 0, 1)))
    column = jnp.where(z == 2 + c, here, one + side + two + three)
    late = []
    for part in range(2):
        for first in (16, 21):
            late += [(first, part), (first + 1, part), (first + 2, part), (first + 3 + part, 0)]
    shard = np.arange(32)
    sz, sy, sx, sc = shard // 8, shard // 4 % 2, shard // 2 % 2, shard % 2
    away = jnp.where(sz % 2 == c, 0, 4)
    where = sc * 8 + away + 2 * (sy ^ y) + (sx ^ x) + 16 * (sz // 2)
    return buffers, Flow(spread_stages(column)), (early, early + late), where.astype(jnp.int32)


def spread_stages(column):
    over_x, over_y = yield [(column, "x", SWAP), (column, "y", SWAP)]
    corners = yield [(over_x[:1], "y", SWAP), (over_y[1:], "x", SWAP)]
    local = [column, over_x, over_y] + list(corners)
    return local + list((yield [(piece, "c", SWAP) for piece in local]))


def unpack_lines(buffers, slots, where, segments, after=()):
    jobs, starts = [], []
    reach = 0
    for offset, rows, columns in segments:
        per_row = columns // LINE
        lane, base = offset % LINE, offset // LINE
        if per_row == 1 and rows < 1024:
            lane, tall = 0, rows
        else:
            tall = TALL[per_row]
        starts.append(len(jobs))
        for k in range(rows // tall):
            jobs.append((base + k * tall * per_row, tall * per_row, 1 if lane else 0))
    window = max(job[1] for job in jobs) + 32
    table = np.zeros((len(jobs), 5), np.int32)
    for k, (line, count, extra) in enumerate(jobs):
        owner = line // SHARD
        inside = line - owner * SHARD
        begin = min(inside // 16 * 16, SPAD - window)
        crosses = int(line + count + extra > (owner + 1) * SHARD)
        table[k] = (owner, begin, begin - inside, crosses, (owner + 1) * SHARD - line)
    base_row = (int(-table[:, 2].min()) + 7) // 8 * 8
    table[:, 2] += base_row
    table[:, 4] += base_row
    room = int(max((table[:, 2] + window).max(), ((table[:, 4] + window) * table[:, 3]).max()))
    room = (room + 15) // 8 * 8
    total = len(jobs)
    count_buffers = len(buffers)
    shapes = []
    for offset, rows, columns in segments:
        per_row = columns // LINE
        tall = rows if per_row == 1 and rows < 1024 else TALL[per_row]
        shapes.append((rows, columns, tall, per_row, offset % LINE if tall != rows or per_row != 1 else 0))
    sizes = sorted({(tall, columns) for _, columns, tall, _, _ in shapes})

    def kernel(table_ref, where_ref, *refs):
        sources = refs[:count_buffers]
        outs = refs[count_buffers : count_buffers + len(segments)]
        rest = refs[count_buffers + len(segments) :]
        stages = dict(zip(sizes, rest))
        raw, flat, in_sem, out_sem = rest[len(sizes) :]
        step = pl.program_id(0)

        def fetch(job, slot):
            owner = table_ref[job, 0]
            begin = pl.multiple_of(table_ref[job, 1], 16)
            for b, (source, part) in enumerate(slots):

                @pl.when(where_ref[owner] == b)
                def _():
                    pltpu.make_async_copy(
                        sources[source].at[part, pl.ds(begin, window), :], raw.at[slot, 0], in_sem.at[slot, 0]
                    ).start()

            @pl.when(table_ref[job, 3] == 1)
            def _():
                for b, (source, part) in enumerate(slots):

                    @pl.when(where_ref[owner + 1] == b)
                    def _():
                        pltpu.make_async_copy(
                            sources[source].at[part, pl.ds(0, window), :], raw.at[slot, 1], in_sem.at[slot, 1]
                        ).start()

        def fetched(slot, half):
            return pltpu.make_async_copy(
                sources[0].at[0, pl.ds(0, window), :], raw.at[slot, half], in_sem.at[slot, half]
            )

        @pl.when(step == 0)
        def _():
            for k in range(min(DEPTH - 1, total)):
                fetch(k, k)

        @pl.when(step + DEPTH - 1 < total)
        def _():
            fetch(step + DEPTH - 1, lax.rem(step + DEPTH - 1, DEPTH))

        slot = lax.rem(step, DEPTH)
        fetched(slot, 0).wait()
        flat[pl.ds(table_ref[step, 2], window), :] = raw[slot, 0].astype(jnp.float32)

        @pl.when(table_ref[step, 3] == 1)
        def _():
            fetched(slot, 1).wait()
            flat[pl.ds(table_ref[step, 4], window), :] = raw[slot, 1].astype(jnp.float32)

        for index, (rows, columns, tall, per_row, lane) in enumerate(shapes):
            begin = starts[index]
            blocks = rows // tall
            stage = stages[(tall, columns)]

            @pl.when((step >= begin) & (step < begin + blocks))
            def _():
                block = step - begin
                side = lax.rem(block, DEPTH)

                def written(k, s):
                    return pltpu.make_async_copy(
                        stage.at[s],
                        outs[index].at[pl.ds(pl.multiple_of(k * tall, 16), tall), :],
                        out_sem.at[s],
                    )

                @pl.when(block >= DEPTH)
                def _():
                    written(block - DEPTH, side).wait()

                def tile(j):
                    picked = flat[pl.ds(base_row + j, tall, stride=per_row), :]
                    return pltpu.roll(picked, LINE - lane, 1) if lane else picked

                if lane:
                    lanes = lax.broadcasted_iota(jnp.int32, (tall, LINE), 1)
                    now = tile(0)
                    for j in range(per_row):
                        later = tile(j + 1)
                        stage[side, :, j * LINE : (j + 1) * LINE] = jnp.where(
                            lanes < LINE - lane, now, later
                        ).astype(jnp.bfloat16)
                        now = later
                else:
                    for j in range(per_row):
                        stage[side, :, j * LINE : (j + 1) * LINE] = tile(j).astype(jnp.bfloat16)
                written(block, side).start()

                @pl.when(block == blocks - 1)
                def _():
                    for back in reversed(range(min(DEPTH, blocks))):
                        written(block - back, lax.rem(block - back, DEPTH)).wait()

    return pl.pallas_call(
        pinned(kernel, 2 + count_buffers, after),
        grid_spec=pltpu.PrefetchScalarGridSpec(
            num_scalar_prefetch=2,
            grid=(total,),
            in_specs=[pl.BlockSpec(memory_space=pl.ANY)] * count_buffers + pins(after),
            out_specs=[pl.BlockSpec(memory_space=pl.ANY)] * len(segments),
            scratch_shapes=[pltpu.VMEM((DEPTH,) + size, jnp.bfloat16) for size in sizes]
            + [
                pltpu.VMEM((DEPTH, 2, window, LINE), jnp.bfloat16),
                pltpu.VMEM((room, LINE), jnp.float32),
                pltpu.SemaphoreType.DMA((DEPTH, 2)),
                pltpu.SemaphoreType.DMA((DEPTH,)),
            ],
        ),
        out_shape=[jax.ShapeDtypeStruct((rows, columns), jnp.bfloat16) for _, rows, columns in segments],
        compiler_params=pltpu.CompilerParams(vmem_limit_bytes=48 * 2**20),
        cost_estimate=pl.CostEstimate(flops=0, bytes_accessed=total * window * LINE * 4, transcendentals=0),
        name="unpack",
    )(jnp.asarray(table), where, *buffers, *after)


def pack_lines(target, target_rows, first_row, segments, lane, phase, extras, carry, tail_rows, after=()):
    tall = 512
    lefts, rights, plan = [], [], []
    left_of, right_of = {}, {}
    row = first_row
    begin = 0
    for left, right in segments:
        for value, seen, kept in ((left, left_of, lefts), (right, right_of, rights)):
            if id(value) not in seen:
                seen[id(value)] = len(kept)
                kept.append(value)
        blocks = left.shape[1] // tall
        plan.append((left_of[id(left)], right_of[id(right)], right.shape[1] // LINE, begin, blocks, row))
        begin += blocks
        row += left.shape[1] * right.shape[1] // LINE
    end_row = row
    total = begin
    biggest = max(entry[2] for entry in plan) * tall
    tokens = lefts[0].shape[0]
    count_left, count_right, count_extra = len(lefts), len(rights), len(extras)
    rolled = [jnp.roll(right, lane, axis=1) if lane else right for right in rights]
    carry_in = [carry] if lane else []
    targets = [] if target is None else [target]

    def left_spec(index):
        mine = [entry for entry in plan if entry[0] == index]

        def place(step):
            block = 0
            for _, _, _, start, blocks, _ in mine:
                block = jnp.where(step >= start, jnp.minimum(step - start, blocks - 1), block)
            return (0, block)

        return pl.BlockSpec((tokens, tall), place)

    def kernel(*refs):
        left_refs = refs[:count_left]
        right_refs = refs[count_left : count_left + count_right]
        at = count_left + count_right
        extra_refs = refs[at : at + count_extra]
        at += count_extra
        carry_refs = refs[at : at + len(carry_in)]
        at += len(carry_in) + len(targets)
        out = refs[at]
        flat, stage, shift, last, sems, extra_sems = refs[at + 1 :]
        step = pl.program_id(0)
        side = lax.rem(step, 2)

        def extra_copy(k):
            rows = extras[k][0].shape[0]
            return pltpu.make_async_copy(
                extra_refs[k], out.at[pl.ds(extras[k][1], rows), :], extra_sems.at[k]
            )

        @pl.when(step == 0)
        def _():
            for k in range(count_extra):
                extra_copy(k).start()
            if lane:
                shift[0:8, :] = carry_refs[0][...]
            if phase:
                flat[0:8, :] = jnp.zeros((8, LINE), jnp.float32)

        for left_at, right_at, per_row, start, blocks, row in plan:
            lines = per_row * tall

            def written(block, s, row=row, lines=lines):
                return pltpu.make_async_copy(
                    stage.at[s, pl.ds(0, lines), :],
                    out.at[pl.ds(pl.multiple_of(row + block * lines, 16), lines), :],
                    sems.at[s],
                )

            @pl.when((step >= start) & (step < start + blocks))
            def _():
                block = step - start
                if phase:

                    @pl.when(step > 0)
                    def _():
                        flat[0:8, :] = flat[lines : lines + 8, :]

                turned = left_refs[left_at][...].T
                lanes = lax.broadcasted_iota(jnp.int32, (tall, LINE), 1)
                for j0 in range(0, per_row, 2):
                    wide = min(2, per_row - j0)
                    tile = jnp.dot(
                        turned,
                        right_refs[right_at][:, j0 * LINE : (j0 + wide) * LINE],
                        preferred_element_type=jnp.float32,
                    )
                    for j in range(wide):
                        piece = tile[:, j * LINE : (j + 1) * LINE]
                        if lane and j0 + j == 0:
                            shift[8 : 8 + tall, :] = piece
                            piece = jnp.where(lanes < lane, shift[7 : 7 + tall, :], piece)
                            shift[0:8, :] = shift[tall : tall + 8, :]
                        if per_row == 1:
                            flat[phase : phase + tall, :] = piece
                        else:
                            flat[pl.ds(phase + j0 + j, tall, stride=per_row), :] = piece

                stage[side, 0:lines, :] = flat[0:lines, :].astype(jnp.bfloat16)
                written(block, side).start()

            @pl.when((step > start) & (step <= start + blocks))
            def _():
                written(step - start - 1, 1 - side).wait()

            if start + blocks == total:

                @pl.when(step == total - 1)
                def _():
                    written(blocks - 1, side).wait()

        @pl.when(step == total - 1)
        def _():
            if tail_rows:
                lanes = lax.broadcasted_iota(jnp.int32, (tail_rows, LINE), 1)
                rows_at = lax.broadcasted_iota(jnp.int32, (tail_rows, LINE), 0)
                final = jnp.broadcast_to(shift[7:8, :], (tail_rows, LINE))
                last[...] = jnp.where((rows_at == 0) & (lanes < lane), final, 0.0).astype(jnp.bfloat16)
                closing = pltpu.make_async_copy(
                    last, out.at[pl.ds(end_row, tail_rows), :], extra_sems.at[count_extra]
                )
                closing.start()
                closing.wait()
            for k in range(count_extra):
                extra_copy(k).wait()

    whole = [pl.BlockSpec(array.shape, lambda step: (0, 0)) for array in rolled]
    flops = sum(2 * tokens * entry[4] * tall * entry[2] * LINE for entry in plan)
    inputs = count_left + count_right + count_extra + len(carry_in) + len(targets)
    return pl.pallas_call(
        pinned(kernel, inputs, after),
        grid=(total,),
        in_specs=[left_spec(k) for k in range(count_left)]
        + whole
        + [pl.BlockSpec(array.shape, lambda step: (0, 0)) for array, _ in extras]
        + [pl.BlockSpec(array.shape, lambda step: (0, 0)) for array in carry_in]
        + [pl.BlockSpec(memory_space=pl.ANY)] * len(targets)
        + pins(after),
        out_specs=pl.BlockSpec(memory_space=pl.ANY),
        out_shape=jax.ShapeDtypeStruct((target_rows, LINE), jnp.bfloat16),
        scratch_shapes=[
            pltpu.VMEM((biggest + 16, LINE), jnp.float32),
            pltpu.VMEM((2, biggest, LINE), jnp.bfloat16),
            pltpu.VMEM((tall + 8, LINE), jnp.float32),
            pltpu.VMEM((max(tail_rows, 16), LINE), jnp.bfloat16),
            pltpu.SemaphoreType.DMA((2,)),
            pltpu.SemaphoreType.DMA((count_extra + 1,)),
        ],
        input_output_aliases={count_left + count_right + count_extra + len(carry_in): 0} if targets else {},
        compiler_params=pltpu.CompilerParams(vmem_limit_bytes=48 * 2**20),
        cost_estimate=pl.CostEstimate(flops=flops, bytes_accessed=total * biggest * LINE * 2, transcendentals=0),
        name="pack",
    )(*lefts, *rolled, *[array for array, _ in extras], *carry_in, *targets, *after)


def added(*parts):
    total = parts[0].astype(jnp.float32)
    for part in parts[1:]:
        total = total + part.astype(jnp.float32)
    return total.astype(jnp.bfloat16)


def reduce_stages(flat, batch, shift):
    z, y, x, c = (lax.axis_index(name) for name in GRID)
    length = PLANE + 32
    send = lax.dynamic_slice(flat, ((1 - c) * PLANE, 0), (length, LINE))
    (arrived,) = yield [(send, "c", SWAP)]
    chip = added(lax.dynamic_slice(flat, (c * PLANE, 0), (length, LINE)), arrived)

    def window(sy, sx, part):
        shard = sy * 4 + sx * 2 + part
        start = (shift + SHARD * shard) // 16 * 16
        return lax.dynamic_slice(chip, (start, 0), (WIN, LINE))

    away_0 = jnp.stack([window(1 - y, 0, 0), window(1 - y, 1, 0)])
    away_1 = jnp.stack([window(0, 1 - x, 1), window(1, 1 - x, 1)])
    home_0 = jnp.stack([window(y, 0, 0), window(y, 1, 0)])
    home_1 = jnp.stack([window(0, x, 1), window(1, x, 1)])
    got_0, got_1 = yield [(away_0, "y", SWAP), (away_1, "x", SWAP)]
    half_0, half_1 = added(home_0, got_0), added(home_1, got_1)
    pick = lambda value, at: lax.dynamic_index_in_dim(value, at, 0, keepdims=False)
    got_0, got_1 = yield [(pick(half_0, 1 - x), "x", SWAP), (pick(half_1, 1 - y), "y", SWAP)]
    columns = [added(pick(half_0, x), got_0), added(pick(half_1, y), got_1)]
    if batch == 0:
        hops = [((1, 0, 0), (2, 1, 1)), ((2, 0, 0), (3, 1, 1)), ((3, 0, 0), (0, 1, 1))]
    else:
        hops = [((1, 2, 0), (2, 3, 1)), ((0, 2, 0), (1, 3, 1)), ((3, 2, 0), (0, 3, 1))]
    if batch == 0:
        got = yield [(columns[0], ZC, zc_pairs(*hop)) for hop in hops]
        end = added(columns[0], *got)
        (column,) = fence(columns[1:], [end])
        got = yield [(column, ZC, zc_pairs(*hop)) for hop in hops]
        ends = [end, added(column, *got)]
    else:
        columns = jnp.stack(columns)
        got = yield [(columns, ZC, zc_pairs(*hop)) for hop in hops]
        ends = added(columns, *got)
    mine = jnp.where(c == 0, ends[0], ends[1])
    other = jnp.where(c == 0, ends[1], ends[0])
    (handed,) = yield [(other, ZC, [(2 * k + k % 2, 2 * k + 1 - k % 2) for k in range(4)])]
    return jnp.where(c == z % 2, mine, handed)


PIECE = 400


def corner_stages(flat):
    z, y, x, c = (lax.axis_index(name) for name in GRID)
    length = 8 * PIECE
    second = (8 + SHARD) // 16 * 16
    take = lambda at: lax.dynamic_slice(flat, (at * second, 0), (length, LINE))
    (arrived,) = yield [(take(1 - c), "c", SWAP)]
    chip = added(take(c), arrived).reshape(2, 2, 2, PIECE, LINE)
    pick = lambda value, at: lax.dynamic_index_in_dim(value, at, 0, keepdims=False)
    got = yield [(pick(chip[0], 1 - x), "x", SWAP), (pick(chip[1], 1 - y), "y", SWAP)]
    halves = [added(pick(chip[0], x), got[0]), added(pick(chip[1], y), got[1])]
    got = yield [(pick(halves[0], 1 - y), "y", SWAP), (pick(halves[1], 1 - x), "x", SWAP)]
    pieces = jnp.stack([added(pick(halves[0], y), got[0]), added(pick(halves[1], x), got[1])])
    got = yield [(pieces, "z", [(k, 0)]) for k in (1, 2, 3)]
    pieces = added(pieces, *got)
    got = yield [(pieces[0], "y", [(1, 0)]), (pieces[1], "x", [(1, 0)])]
    halves = [jnp.stack([pieces[0], got[0]]), jnp.stack([pieces[1], got[1]])]
    got = yield [(halves[0], "x", [(1, 0)]), (halves[1], "y", [(1, 0)])]
    return jnp.stack([halves[0], got[0], halves[1], got[1]]).reshape(length, LINE)


CHUNK = 128
NT = (((1,), (1,)), ((), ()))
TN = (((0,), (0,)), ((), ()))
INNER = SSM_HEADS * SSM_DIM
PAIRS = SSM_HEADS // 2


def spread(rows_a, rows_b):
    length = rows_a.shape[1]
    tall = jnp.concatenate(
        [jnp.broadcast_to(rows_a, (SSM_DIM, length)), jnp.broadcast_to(rows_b, (SSM_DIM, length))], axis=0
    )
    return tall.T


CHANNELS = INNER + 2 * STATE
LANES = 2 * SSM_DIM
COLUMNS = CHANNELS // LANES


def conv_masks(masks, start_ref, first, rows):
    place = first + lax.broadcasted_iota(jnp.int32, (rows, LANES), 0) - start_ref[...]
    for reach in range(1, CONV):
        masks[reach - 1] = jnp.where(place >= reach, 1.0, 0.0)


def conv_parts(ext, weight_ref, bias_ref, masks, rows):
    windows = []
    total = bias_ref[...]
    for tap in range(CONV):
        reach = CONV - 1 - tap
        window = ext[8 - reach : 8 - reach + rows, :]
        if reach:
            window = window * masks[reach - 1]
        windows.append(window)
        total = total + window * weight_ref[tap : tap + 1, :]
    return windows, total


def conv_forward(xbc, rim, weight, bias, meta, start_column, after=()):
    rows = xbc.shape[0]

    def kernel(meta_ref, x_ref, rim_ref, weight_ref, bias_ref, start_ref, out_ref, ext, masks):
        @pl.when(pl.program_id(0) == 0)
        def _():
            conv_masks(masks, start_ref, meta_ref[0], rows)

        ext[0:8, :] = rim_ref[...]
        ext[8:, :] = x_ref[...]
        _, total = conv_parts(ext, weight_ref, bias_ref, masks, rows)
        out_ref[...] = total * jax.nn.sigmoid(total)

    lanes = lambda i, m: (0, i)
    return pl.pallas_call(
        pinned(kernel, 6, after),
        grid_spec=pltpu.PrefetchScalarGridSpec(
            num_scalar_prefetch=1,
            grid=(COLUMNS,),
            in_specs=[
                pl.BlockSpec((rows, LANES), lanes),
                pl.BlockSpec((8, LANES), lanes),
                pl.BlockSpec((CONV, LANES), lanes),
                pl.BlockSpec((1, LANES), lanes),
                pl.BlockSpec((rows, 1), lambda i, m: (0, 0)),
            ] + pins(after),
            out_specs=pl.BlockSpec((rows, LANES), lanes),
            scratch_shapes=[
                pltpu.VMEM((rows + 8, LANES), jnp.float32),
                pltpu.VMEM((CONV - 1, rows, LANES), jnp.float32),
            ],
        ),
        out_shape=jax.ShapeDtypeStruct((rows, CHANNELS), jnp.float32),
        cost_estimate=pl.CostEstimate(flops=10**9, bytes_accessed=rows * CHANNELS * 8, transcendentals=0),
        name="conv",
    )(meta, xbc, rim, weight, bias, start_column, *after)


def conv_backward(dx, db, dc, xbc, rim, weight, bias, meta, start_column, after=()):
    rows = xbc.shape[0]

    def kernel(meta_ref, dx_ref, db_ref, dc_ref, x_ref, rim_ref, weight_ref, bias_ref, start_ref,
               low_ref, tail_ref, edge_ref, small_ref, ext, upper, masks):
        @pl.when(pl.program_id(0) == 0)
        def _():
            conv_masks(masks, start_ref, meta_ref[0], rows)
            upper[0:8, :] = jnp.zeros((8, LANES), jnp.float32)
            upper[8 + rows :, :] = jnp.zeros((8, LANES), jnp.float32)

        ext[0:8, :] = rim_ref[...]
        ext[8:, :] = x_ref[...]
        at = pl.program_id(0)
        arrived = jnp.where(at < PAIRS, dx_ref[...], jnp.where(at == PAIRS, db_ref[...], dc_ref[...]))
        windows, total = conv_parts(ext, weight_ref, bias_ref, masks, rows)
        gate = jax.nn.sigmoid(total)
        change = arrived * gate * (1.0 + total * (1.0 - gate))
        main = jnp.zeros((rows, LANES), jnp.float32)
        edge = jnp.zeros((8, LANES), jnp.float32)
        small_ref[...] = jnp.zeros((8, LANES), jnp.float32)
        small_ref[CONV : CONV + 1, :] = jnp.sum(change, axis=0, keepdims=True)
        for tap in range(CONV):
            reach = CONV - 1 - tap
            small_ref[tap : tap + 1, :] = jnp.sum(change * windows[tap], axis=0, keepdims=True)
            masked = change * masks[reach - 1] if reach else change
            upper[8 : 8 + rows, :] = masked * weight_ref[tap : tap + 1, :]
            main = main + upper[8 + reach : 8 + reach + rows, :]
            edge = edge + upper[reach : reach + 8, :]
        low_ref[...] = main.astype(jnp.bfloat16)
        tail_ref[...] = main[rows - 16 :, :]
        edge_ref[...] = edge

    lanes = lambda i, m: (0, i)
    whole = lambda i, m: (0, 0)
    return pl.pallas_call(
        pinned(kernel, 9, after),
        grid_spec=pltpu.PrefetchScalarGridSpec(
            num_scalar_prefetch=1,
            grid=(COLUMNS,),
            in_specs=[
                pl.BlockSpec((rows, LANES), lambda i, m: (0, jnp.minimum(i, PAIRS - 1))),
                pl.BlockSpec((rows, STATE), whole),
                pl.BlockSpec((rows, STATE), whole),
                pl.BlockSpec((rows, LANES), lanes),
                pl.BlockSpec((8, LANES), lanes),
                pl.BlockSpec((CONV, LANES), lanes),
                pl.BlockSpec((1, LANES), lanes),
                pl.BlockSpec((rows, 1), whole),
            ] + pins(after),
            out_specs=[
                pl.BlockSpec((rows, LANES), lanes),
                pl.BlockSpec((16, LANES), lanes),
                pl.BlockSpec((8, LANES), lanes),
                pl.BlockSpec((8, LANES), lanes),
            ],
            scratch_shapes=[
                pltpu.VMEM((rows + 8, LANES), jnp.float32),
                pltpu.VMEM((rows + 16, LANES), jnp.float32),
                pltpu.VMEM((CONV - 1, rows, LANES), jnp.float32),
            ],
        ),
        out_shape=[
            jax.ShapeDtypeStruct((rows, CHANNELS), jnp.bfloat16),
            jax.ShapeDtypeStruct((16, CHANNELS), jnp.float32),
            jax.ShapeDtypeStruct((8, CHANNELS), jnp.float32),
            jax.ShapeDtypeStruct((8, CHANNELS), jnp.float32),
        ],
        cost_estimate=pl.CostEstimate(flops=2 * 10**9, bytes_accessed=rows * CHANNELS * 10, transcendentals=0),
        name="conv_back",
    )(meta, dx, db, dc, xbc, rim, weight, bias, start_column, *after)


def weighted_state(left, left_block, values, weight_rows, after=()):
    rows = left.shape[0]

    def kernel(left_ref, value_ref, weight_ref, out_ref, turned):
        @pl.when(pl.program_id(0) == 0)
        def _():
            turned[...] = left_ref[...].T

        scaled = [(turned[...] * weight_ref[0, e : e + 1, :]).astype(jnp.bfloat16) for e in range(2)]
        both = jnp.dot(
            jnp.concatenate(scaled, axis=0), value_ref[...].astype(jnp.bfloat16), preferred_element_type=jnp.float32
        )
        low_lane = lax.broadcasted_iota(jnp.int32, (STATE, 2 * SSM_DIM), 1) < SSM_DIM
        out_ref[...] = jnp.where(low_lane, both[:STATE], both[STATE:])

    return pl.pallas_call(
        pinned(kernel, 3, after),
        grid=(PAIRS,),
        in_specs=[
            pl.BlockSpec((rows, STATE), lambda i: (0, left_block)),
            pl.BlockSpec((rows, 2 * SSM_DIM), lambda i: (0, i)),
            pl.BlockSpec((1, 2, rows), lambda i: (i, 0, 0)),
        ] + pins(after),
        out_specs=pl.BlockSpec((STATE, 2 * SSM_DIM), lambda i: (0, i)),
        out_shape=jax.ShapeDtypeStruct((STATE, INNER), jnp.float32),
        scratch_shapes=[pltpu.VMEM((STATE, rows), jnp.float32)],
        cost_estimate=pl.CostEstimate(flops=2 * rows * STATE * INNER, bytes_accessed=rows * INNER * 4, transcendentals=0),
        name="state",
    )(left, values, weight_rows.reshape(PAIRS, 2, rows), *after)


def chunk_rows(k, meta_ref, cum_ref, start_ref):
    here = slice(k * CHUNK, (k + 1) * CHUNK)
    first = meta_ref[0] + k * CHUNK
    index = first + lax.broadcasted_iota(jnp.int32, (1, CHUNK), 1)
    entering = start_ref[0:1, here] < first
    ending = index >= meta_ref[1 + k]
    cums, entries, tails = [], [], []
    for e in range(2):
        cum = cum_ref[0, e : e + 1, here]
        cums.append(cum)
        entries.append(jnp.where(entering, jnp.exp(cum), 0.0))
        gap = jnp.where(ending, cum[:, CHUNK - 1 :] - cum, masked_score)
        tails.append(jnp.exp(gap))
    return cums, entries, tails


def ssm_forward(conv, cum, step, state_in, skip, meta, start_column, start_row):
    rows = conv.shape[0]
    chunks = rows // CHUNK

    def kernel(meta_ref, x_ref, b_ref, c_ref, cum_ref, step_ref, state_ref, skip_ref, col_ref, row_ref,
               y_ref, inner, hide, state, b_turned):
        @pl.when(pl.program_id(0) == 0)
        def _():
            for k in range(chunks):
                here = slice(k * CHUNK, (k + 1) * CHUNK)
                b_turned[:, here] = b_ref[here, :].T.astype(jnp.bfloat16)
                inner[k] = lax.dot_general(
                    c_ref[here, :], b_ref[here, :], NT, precision=highest, preferred_element_type=jnp.float32
                )
                t = lax.broadcasted_iota(jnp.int32, (CHUNK, CHUNK), 0)
                s = lax.broadcasted_iota(jnp.int32, (CHUNK, CHUNK), 1)
                shown = (s <= t) & (meta_ref[0] + k * CHUNK + s >= col_ref[here, :])
                hide[k] = jnp.where(shown, 0.0, masked_score)

        low_lane = lax.broadcasted_iota(jnp.int32, (CHUNK, 2 * SSM_DIM), 1) < SSM_DIM
        state[...] = state_ref[...]
        for k in range(chunks):
            here = slice(k * CHUNK, (k + 1) * CHUNK)
            cums, entries, tails = chunk_rows(k, meta_ref, cum_ref, row_ref)
            x_now = x_ref[here, :]
            x_low = x_now.astype(jnp.bfloat16)
            entry = spread(*entries)
            weight = spread(*[tails[e] * step_ref[0, e : e + 1, here] for e in range(2)])
            parts = []
            for e in range(2):
                across = jnp.broadcast_to(cums[e], (CHUNK, CHUNK))
                decays = jnp.exp(across.T - across + hide[k])
                mix = (inner[k] * decays * step_ref[0, e : e + 1, here]).astype(jnp.bfloat16)
                parts.append(jnp.dot(mix, x_low, preferred_element_type=jnp.float32))
            carried = jnp.dot(
                c_ref[here, :].astype(jnp.bfloat16), state[...].astype(jnp.bfloat16),
                preferred_element_type=jnp.float32,
            )
            y_ref[here, :] = jnp.where(low_lane, parts[0], parts[1]) + entry * carried + skip_ref[...] * x_now
            fresh = jnp.dot(
                b_turned[:, here], (x_now * weight).astype(jnp.bfloat16), preferred_element_type=jnp.float32
            )
            state[...] = entry[CHUNK - 1 :, :] * state[...] + fresh

    whole = lambda i, m: (0, 0)
    lanes = lambda i, m: (0, i)
    return pl.pallas_call(
        kernel,
        grid_spec=pltpu.PrefetchScalarGridSpec(
            num_scalar_prefetch=1,
            grid=(PAIRS,),
            in_specs=[
                pl.BlockSpec((rows, 2 * SSM_DIM), lanes),
                pl.BlockSpec((rows, STATE), lambda i, m: (0, PAIRS)),
                pl.BlockSpec((rows, STATE), lambda i, m: (0, PAIRS + 1)),
                pl.BlockSpec((1, 2, rows), lambda i, m: (i, 0, 0)),
                pl.BlockSpec((1, 2, rows), lambda i, m: (i, 0, 0)),
                pl.BlockSpec((STATE, 2 * SSM_DIM), lanes),
                pl.BlockSpec((1, 2 * SSM_DIM), lanes),
                pl.BlockSpec((rows, 1), whole),
                pl.BlockSpec((8, rows), whole),
            ],
            out_specs=pl.BlockSpec((rows, 2 * SSM_DIM), lanes),
            scratch_shapes=[
                pltpu.VMEM((chunks, CHUNK, CHUNK), jnp.float32),
                pltpu.VMEM((chunks, CHUNK, CHUNK), jnp.float32),
                pltpu.VMEM((STATE, 2 * SSM_DIM), jnp.float32),
                pltpu.VMEM((STATE, rows), jnp.bfloat16),
            ],
        ),
        out_shape=jax.ShapeDtypeStruct((rows, INNER), jnp.float32),
        compiler_params=pltpu.CompilerParams(vmem_limit_bytes=40 * 2**20),
        cost_estimate=pl.CostEstimate(flops=10**9, bytes_accessed=rows * INNER * 8, transcendentals=2**21),
        name="ssm",
    )(meta, conv, conv, conv, cum.reshape(PAIRS, 2, rows), step.reshape(PAIRS, 2, rows), state_in, skip,
      start_column, start_row)


def ssm_backward(conv, dy, cum, step, state_in, state_grad, skip, meta, start_row, after=()):
    rows = conv.shape[0]
    chunks = rows // CHUNK

    def kernel(meta_ref, x_ref, dy_ref, b_ref, c_ref, cum_ref, step_ref, state_ref, grad_ref, skip_ref, row_ref,
               dx_ref, db_ref, dc_ref, small_ref, inner, hide, inner_grad, states, flow,
               b_turned, c_turned):
        low = lambda v: v.astype(jnp.bfloat16)
        dot = lambda p, q, dims=(((1,), (0,)), ((), ())): lax.dot_general(
            p, q, dims, preferred_element_type=jnp.float32
        )
        exact = lambda p, q, dims=(((1,), (0,)), ((), ())): lax.dot_general(
            p, q, dims, precision=highest, preferred_element_type=jnp.float32
        )
        s = lax.broadcasted_iota(jnp.int32, (CHUNK, CHUNK), 0)
        t = lax.broadcasted_iota(jnp.int32, (CHUNK, CHUNK), 1)

        @pl.when(pl.program_id(0) == 0)
        def _():
            db_ref[...] = jnp.zeros(db_ref.shape, jnp.float32)
            dc_ref[...] = jnp.zeros(dc_ref.shape, jnp.float32)
            inner_grad[...] = jnp.zeros(inner_grad.shape, jnp.float32)
            for k in range(chunks):
                here = slice(k * CHUNK, (k + 1) * CHUNK)
                b_turned[:, here] = low(b_ref[here, :].T)
                c_turned[:, here] = low(c_ref[here, :].T)
                inner[k] = exact(b_ref[here, :], c_ref[here, :], NT)
                shown = (s <= t) & (meta_ref[0] + k * CHUNK + s >= row_ref[0:1, here])
                hide[k] = jnp.where(shown, 0.0, masked_score)

        before = (s < t).astype(jnp.float32)
        until = low((s >= t).astype(jnp.float32))
        low_lane = t < SSM_DIM
        pick_row = lax.broadcasted_iota(jnp.int32, (8, 2 * SSM_DIM), 0)
        pick_lane = lax.broadcasted_iota(jnp.int32, (8, 2 * SSM_DIM), 1) // SSM_DIM
        pick = low((pick_row == pick_lane).astype(jnp.float32))
        spreads = []
        states[0] = state_ref[...]
        for k in range(chunks):
            here = slice(k * CHUNK, (k + 1) * CHUNK)
            cums, entries, tails = chunk_rows(k, meta_ref, cum_ref, row_ref)
            entry, tail = spread(*entries), spread(*tails)
            steps = spread(step_ref[0, 0:1, here], step_ref[0, 1:2, here])
            spreads.append((cums, entry, tail, steps))
            if k < chunks - 1:
                fresh = dot(b_turned[:, here], low(x_ref[here, :] * steps * tail))
                states[k + 1] = entry[CHUNK - 1 :, :] * states[k] + fresh
        flow[...] = grad_ref[...]
        skip_sum = jnp.zeros((1, 2 * SSM_DIM), jnp.float32)
        for k in reversed(range(chunks)):
            here = slice(k * CHUNK, (k + 1) * CHUNK)
            cums, entry, tail, steps = spreads[k]
            x_now, dy_now = x_ref[here, :], dy_ref[here, :]
            b_low, c_low = low(b_ref[here, :]), low(c_ref[here, :])
            scaled = x_now * steps
            dy_low = low(dy_now)
            flow_low, state_low = low(flow[...]), low(states[k])
            both = low(
                jnp.concatenate([jnp.where(low_lane, scaled, 0.0), jnp.where(low_lane, 0.0, scaled)], axis=0)
            )
            reached = dot(both, dy_low, NT)
            mixes, weighed = [], []
            for e in range(2):
                across = jnp.broadcast_to(cums[e], (CHUNK, CHUNK))
                decays = jnp.exp(across - across.T + hide[k])
                reach = decays * reached[e * CHUNK : (e + 1) * CHUNK]
                inner_grad[k] += reach
                weighed.append(low(inner[k] * reach))
                mixes.append(low(inner[k] * decays))
            sums = dot(jnp.concatenate(weighed, axis=0), until)
            within = [
                jnp.sum(sums[e * CHUNK : (e + 1) * CHUNK] * before, axis=0, keepdims=True) for e in range(2)
            ]
            mixed = dot(jnp.concatenate(mixes, axis=0), dy_low)
            back = tail * dot(b_low, flow_low)
            dxs = jnp.where(low_lane, mixed[:CHUNK], mixed[CHUNK:]) + back
            db_ref[here, :] += dot(low(scaled * tail), flow_low, NT)
            entered = low(dy_now * entry)
            dc_ref[here, :] += dot(entered, state_low, NT)
            brought = dy_now * entry * dot(c_low, state_low)
            ends = dot(pick, low(brought), NT)
            begins = dot(pick, low(scaled * back), NT)
            direct = dot(pick, low(x_now * dxs), NT)
            through = jnp.sum(flow[...] * states[k], axis=0, keepdims=True) * entry[CHUNK - 1 :, :]
            log_grad = exact(ends, until.astype(jnp.float32)) + exact(begins, before)
            for e in range(2):
                lanes = slice(e * SSM_DIM, (e + 1) * SSM_DIM)
                kept = jnp.sum(through[:, lanes], axis=1, keepdims=True)
                small_ref[0, e : e + 1, here] = direct[e : e + 1, :]
                small_ref[0, 2 + e : 3 + e, here] = log_grad[e : e + 1, :] + within[e] + kept
            dx_ref[here, :] = dxs * steps + skip_ref[...] * dy_now
            skip_sum += jnp.sum(x_now * dy_now, axis=0, keepdims=True)
            flow[...] = entry[CHUNK - 1 :, :] * flow[...] + dot(c_turned[:, here], entered)
        small_ref[0, 4:8, :] = jnp.zeros((4, rows), jnp.float32)
        small_ref[0, 4:5, 0 : 2 * SSM_DIM] = skip_sum

        @pl.when(pl.program_id(0) == PAIRS - 1)
        def _():
            for k in range(chunks):
                here = slice(k * CHUNK, (k + 1) * CHUNK)
                grads = low(inner_grad[k])
                db_ref[here, :] += dot(grads, low(c_ref[here, :]))
                dc_ref[here, :] += dot(grads, low(b_ref[here, :]), TN)

    whole = lambda i, m: (0, 0)
    lanes = lambda i, m: (0, i)
    pair = lambda i, m: (i, 0, 0)
    return pl.pallas_call(
        pinned(kernel, 11, after),
        grid_spec=pltpu.PrefetchScalarGridSpec(
            num_scalar_prefetch=1,
            grid=(PAIRS,),
            in_specs=[
                pl.BlockSpec((rows, 2 * SSM_DIM), lanes),
                pl.BlockSpec((rows, 2 * SSM_DIM), lanes),
                pl.BlockSpec((rows, STATE), lambda i, m: (0, PAIRS)),
                pl.BlockSpec((rows, STATE), lambda i, m: (0, PAIRS + 1)),
                pl.BlockSpec((1, 2, rows), pair),
                pl.BlockSpec((1, 2, rows), pair),
                pl.BlockSpec((STATE, 2 * SSM_DIM), lanes),
                pl.BlockSpec((STATE, 2 * SSM_DIM), lanes),
                pl.BlockSpec((1, 2 * SSM_DIM), lanes),
                pl.BlockSpec((8, rows), whole),
            ] + pins(after),
            out_specs=[
                pl.BlockSpec((rows, 2 * SSM_DIM), lanes),
                pl.BlockSpec((rows, STATE), whole),
                pl.BlockSpec((rows, STATE), whole),
                pl.BlockSpec((1, 8, rows), pair),
            ],
            scratch_shapes=[
                pltpu.VMEM((chunks, CHUNK, CHUNK), jnp.float32),
                pltpu.VMEM((chunks, CHUNK, CHUNK), jnp.float32),
                pltpu.VMEM((chunks, CHUNK, CHUNK), jnp.float32),
                pltpu.VMEM((chunks, STATE, 2 * SSM_DIM), jnp.float32),
                pltpu.VMEM((STATE, 2 * SSM_DIM), jnp.float32),
                pltpu.VMEM((STATE, rows), jnp.bfloat16),
                pltpu.VMEM((STATE, rows), jnp.bfloat16),
            ],
        ),
        out_shape=[
            jax.ShapeDtypeStruct((rows, INNER), jnp.float32),
            jax.ShapeDtypeStruct((rows, STATE), jnp.float32),
            jax.ShapeDtypeStruct((rows, STATE), jnp.float32),
            jax.ShapeDtypeStruct((PAIRS, 8, rows), jnp.float32),
        ],
        compiler_params=pltpu.CompilerParams(vmem_limit_bytes=40 * 2**20),
        cost_estimate=pl.CostEstimate(flops=3 * 10**9, bytes_accessed=rows * INNER * 12, transcendentals=2**21),
        name="ssm_back",
    )(meta, conv, dy, conv, conv, cum.reshape(PAIRS, 2, rows), step.reshape(PAIRS, 2, rows), state_in, state_grad,
      skip, start_row, *after)


def chain_states(earlier, later):
    return (earlier[0] * later[0], earlier[1] * later[0] + later[1])


def scan_states(carry, state, span, fast, backward):
    wide = jnp.repeat(carry, SSM_DIM)[None, :]
    if not fast:
        ident = (jnp.ones_like(wide), jnp.zeros_like(state))
        return (carried_in if backward else prefix)((wide, state), span, chain_states, ident)[1]
    flow = Flow(scan_stages(carry, state, backward))
    while flow.sends:
        flow.go()
    return flow.result


def scan_stages(carry, state, backward, extra=None):
    total = (jnp.repeat(carry, SSM_DIM)[None, :], state)
    start = None
    for name in ("c", "x", "y"):
        place = lax.axis_index(name)
        at = lax.broadcasted_iota(jnp.int32, (16, INNER), 0)
        block = jnp.where(at == 0, total[0], 0.0)
        if extra is not None:
            rest = jnp.pad(extra, (0, INNER - extra.shape[0]))[None, :]
            for place_at in range(1, 4):
                term = lax.reduce_precision(rest, 8, 7)
                block = jnp.where(at == place_at, term, block)
                rest = rest - term
        packed = jnp.concatenate([total[1].astype(jnp.bfloat16), block.astype(jnp.bfloat16)], axis=0)
        (packed,) = yield [(packed, name, SWAP)]
        packed = packed.astype(jnp.float32)
        other = (packed[STATE : STATE + 1], packed[:STATE])
        if extra is not None:
            extra = extra + jnp.sum(packed[STATE + 1 : STATE + 4, : extra.shape[0]], axis=0)
        leads = place == (0 if backward else 1)
        seen = (jnp.where(leads, other[0], 1.0), jnp.where(leads, other[1], 0.0))
        start = seen if start is None else chain_states(seen, start)
        if name != "y":
            forward = chain_states(other, total)
            reverse = chain_states(total, other)
            total = jax.tree.map(lambda p, q: jnp.where(leads, p, q), forward, reverse)
    return start[1] if extra is None else [start[1], extra]


KEYS = 512
PAIR = 2 * HEAD_DIM


def attention_forward(q_wide, kv, meta, starts, after=()):
    rows = q_wide.shape[2]
    blocks = kv.shape[0]
    ratio = HEADS_Q // HEADS_KV
    wide = min(512, rows)

    def kernel(meta_ref, q_ref, kv_ref, start_ref, o_ref, log_ref, top, total):
        b = pl.program_id(1)

        @pl.when(b == 0)
        def _():
            top[...] = jnp.full(top.shape, masked_score, jnp.float32)
            total[...] = jnp.zeros(total.shape, jnp.float32)
            o_ref[...] = jnp.zeros(o_ref.shape, jnp.float32)

        def block(partial):
            pair = kv_ref[0, 0]
            turned = pair.T[HEAD_DIM:, :]
            for h in range(ratio):
                for r in range(0, rows, wide):
                    here = slice(r, r + wide)
                    scores = jnp.dot(pair, q_ref[h, :, here], preferred_element_type=jnp.float32)
                    if partial:
                        keys = b * KEYS + lax.broadcasted_iota(jnp.int32, scores.shape, 0)
                        mine = meta_ref[2] + r + lax.broadcasted_iota(jnp.int32, scores.shape, 1)
                        visible = (keys >= start_ref[0:1, here]) & (keys <= mine)
                        scores = jnp.where(visible, scores, masked_score)
                    before = top[h, 0:1, here]
                    peak = jnp.maximum(before, jnp.max(scores, axis=0, keepdims=True))
                    part = jnp.exp(scores - peak)
                    if partial:
                        part = jnp.where(visible, part, 0.0)
                    fade = jnp.exp(before - peak)
                    top[h, 0:1, here] = peak
                    total[h, 0:1, here] = total[h, 0:1, here] * fade + jnp.sum(part, axis=0, keepdims=True)
                    o_ref[h, :, here] = o_ref[h, :, here] * fade + jnp.dot(
                        turned, part.astype(jnp.bfloat16), preferred_element_type=jnp.float32
                    )

        needed = (b >= meta_ref[0]) & (b < meta_ref[1])
        partial = ((b + 1) * KEYS > meta_ref[2]) | (b * KEYS < meta_ref[3])

        @pl.when(needed & partial)
        def _():
            block(True)

        @pl.when(needed & jnp.logical_not(partial))
        def _():
            block(False)

        @pl.when(b == blocks - 1)
        def _():
            for h in range(ratio):
                sums = total[h, 0:1, :]
                o_ref[h] = o_ref[h] / sums
                log_ref[h] = jnp.broadcast_to(top[h, 0:1, :] + jnp.log(sums), (8, rows))

    heads = lambda g, b, m: (g, 0, 0)
    return pl.pallas_call(
        pinned(kernel, 4, after),
        grid_spec=pltpu.PrefetchScalarGridSpec(
            num_scalar_prefetch=1,
            grid=(HEADS_KV, blocks),
            in_specs=[
                pl.BlockSpec((ratio, PAIR, rows), heads),
                pl.BlockSpec((1, 1, KEYS, PAIR), lambda g, b, m: (b, g, 0, 0)),
                pl.BlockSpec((8, rows), lambda g, b, m: (0, 0)),
            ] + pins(after),
            out_specs=[
                pl.BlockSpec((ratio, HEAD_DIM, rows), heads),
                pl.BlockSpec((ratio, 8, rows), heads),
            ],
            scratch_shapes=[
                pltpu.VMEM((ratio, 8, rows), jnp.float32),
                pltpu.VMEM((ratio, 8, rows), jnp.float32),
            ],
        ),
        out_shape=[
            jax.ShapeDtypeStruct((HEADS_Q, HEAD_DIM, rows), jnp.float32),
            jax.ShapeDtypeStruct((HEADS_Q, 8, rows), jnp.float32),
        ],
        compiler_params=pltpu.CompilerParams(vmem_limit_bytes=48 * 2**20),
        cost_estimate=pl.CostEstimate(flops=2 * 10**10, bytes_accessed=2**23, transcendentals=2**23),
        name="attend",
    )(meta, q_wide, kv, starts, *after)


def attention_backward(q_wide, g_wide, kv, logs, mixed, meta, starts, group, after=()):
    rows = q_wide.shape[2]
    blocks = kv.shape[0]
    ratio = HEADS_Q // HEADS_KV
    wide = min(512, rows)

    def kernel(meta_ref, q_ref, g_ref, kv_ref, log_ref, o_ref, start_ref, dkv_ref, dq_ref, delta, sums):
        b = pl.program_id(0)

        @pl.when(b == 0)
        def _():
            dq_ref[...] = jnp.zeros(dq_ref.shape, jnp.float32)
            for h in range(ratio):
                both = g_ref[h, HEAD_DIM:, :].astype(jnp.float32) * o_ref[h]
                delta[h] = jnp.broadcast_to(jnp.sum(both, axis=0, keepdims=True), (8, rows))

        def block(partial):
            pair = kv_ref[0, 0]
            turned = pair.T[:HEAD_DIM, :]
            for h in range(ratio):
                for r in range(0, rows, wide):
                    here = slice(r, r + wide)
                    q_now = q_ref[h, :, here]
                    g_now = g_ref[h, :, here]
                    scores = jnp.dot(pair, q_now, preferred_element_type=jnp.float32)
                    probs = jnp.exp(scores - log_ref[h, 0:1, here])
                    if partial:
                        keys = b * KEYS + lax.broadcasted_iota(jnp.int32, scores.shape, 0)
                        mine = meta_ref[2] + r + lax.broadcasted_iota(jnp.int32, scores.shape, 1)
                        visible = (keys >= start_ref[0:1, here]) & (keys <= mine)
                        probs = jnp.where(visible, probs, 0.0)
                    grads = jnp.dot(pair, g_now, preferred_element_type=jnp.float32)
                    low_grads = (probs * (grads - delta[h, 0:1, here])).astype(jnp.bfloat16)
                    change = lax.dot_general(
                        probs.astype(jnp.bfloat16), g_now, NT, preferred_element_type=jnp.float32
                    ) + lax.dot_general(low_grads, q_now, NT, preferred_element_type=jnp.float32)
                    if h == 0 and r == 0:
                        sums[...] = change
                    else:
                        sums[...] += change
                    dq_ref[h, :, here] += jnp.dot(turned, low_grads, preferred_element_type=jnp.float32)
            dkv_ref[0, 0] = sums[...].astype(jnp.bfloat16)

        needed = (b >= meta_ref[0]) & (b < meta_ref[1])
        partial = ((b + 1) * KEYS > meta_ref[2]) | (b * KEYS < meta_ref[3])

        @pl.when(needed & partial)
        def _():
            block(True)

        @pl.when(needed & jnp.logical_not(partial))
        def _():
            block(False)

        @pl.when(jnp.logical_not(needed))
        def _():
            dkv_ref[0, 0] = jnp.zeros((KEYS, PAIR), jnp.bfloat16)

    heads = lambda b, m: (group, 0, 0)
    return pl.pallas_call(
        pinned(kernel, 7, after),
        grid_spec=pltpu.PrefetchScalarGridSpec(
            num_scalar_prefetch=1,
            grid=(blocks,),
            in_specs=[
                pl.BlockSpec((ratio, PAIR, rows), heads),
                pl.BlockSpec((ratio, PAIR, rows), heads),
                pl.BlockSpec((1, 1, KEYS, PAIR), lambda b, m: (b, group, 0, 0)),
                pl.BlockSpec((ratio, 8, rows), heads),
                pl.BlockSpec((ratio, HEAD_DIM, rows), heads),
                pl.BlockSpec((8, rows), lambda b, m: (0, 0)),
            ] + pins(after),
            out_specs=[
                pl.BlockSpec((1, 1, KEYS, PAIR), lambda b, m: (b, 0, 0, 0)),
                pl.BlockSpec((ratio, HEAD_DIM, rows), lambda b, m: (0, 0, 0)),
            ],
            scratch_shapes=[
                pltpu.VMEM((ratio, 8, rows), jnp.float32),
                pltpu.VMEM((KEYS, PAIR), jnp.float32),
            ],
        ),
        out_shape=[
            jax.ShapeDtypeStruct((blocks, 1, KEYS, PAIR), jnp.bfloat16),
            jax.ShapeDtypeStruct((ratio, HEAD_DIM, rows), jnp.float32),
        ],
        compiler_params=pltpu.CompilerParams(vmem_limit_bytes=48 * 2**20),
        cost_estimate=pl.CostEstimate(flops=2 * 10**10, bytes_accessed=2**23, transcendentals=2**23),
        name="attend_back",
    )(meta, q_wide, g_wide, kv, logs, mixed, starts, *after)


def scatter_span(value, span, fast):
    if not fast:
        return lax.psum_scatter(value, span, scatter_dimension=0).astype(jnp.float32)
    flow = Flow(scatter_stages(value))
    while flow.sends:
        flow.go()
    return flow.result


def scatter_stages(value):
    _, y, x, c = (lax.axis_index(name) for name in GRID)
    value = value.reshape((2, 2, 2) + value.shape[1:])
    for name, place, axis in (("c", c, 2), ("y", y, 0), ("x", x, 0)):
        send = lax.dynamic_index_in_dim(value, 1 - place, axis, keepdims=False)
        (arrived,) = yield [(send, name, SWAP)]
        keep = lax.dynamic_index_in_dim(value, place, axis, keepdims=False)
        value = keep.astype(jnp.float32) + arrived.astype(jnp.float32)
        if name != "x":
            value = value.astype(jnp.bfloat16)
    return value


def plane_stages(value):
    for pairs in ([(0, 1), (1, 0), (2, 3), (3, 2)], [(0, 2), (2, 0), (1, 3), (3, 1)]):
        (other,) = yield [(value, "z", pairs)]
        value = value + other
    return value


def offsets_of():
    places, at = {}, 0
    for name_key, extent in layout():
        places[name_key] = (at, extent)
        at += math.prod(extent)
    return places


def early_weights(params):
    places = offsets_of()
    buffers, spread_flow, (slots, all_slots), where = gather_lines(params)
    spread_flow.go()
    names = (W_QUERY, W_KEY, W_VALUE, W_ATTN_OUT, W_GATE_SSM, W_X_SSM, W_B_C)
    misc_at = places[W_STEP][0]
    first = unpack_lines(
        buffers[:16], slots, where, [flat_segment(name_key) for name_key in names] + [(0, 16, LINE), (misc_at, 288, LINE)]
    )
    weights = dict(zip(names, first))
    weights[NORM_ATTN] = first[-2].reshape(-1)[:D]
    misc = first[-1].reshape(-1)
    for name_key in (W_STEP,) + small_names[1:-1]:
        at, extent = places[name_key]
        weights[name_key] = misc[at - misc_at : at - misc_at + math.prod(extent)].reshape(extent)
    return weights, spread_flow, (buffers, all_slots, where)


def flat_segment(name_key):
    at, extent = offsets_of()[name_key]
    return (at, extent[0], extent[1])


def late_weights(held, after):
    buffers, slots, where = held
    names = (W_SSM_OUT, W_GATE, W_UP_PROJ, W_DOWN)
    norm_at = offsets_of()[NORM_FFN][0]
    second = unpack_lines(
        buffers, slots, where, [flat_segment(name_key) for name_key in names] + [(norm_at, 16, LINE)], after
    )
    weights = dict(zip(names, second))
    weights[NORM_FFN] = second[-1].reshape(-1)[norm_at % LINE : norm_at % LINE + D]
    return weights


def pack_late(gate, up, down, ssm_low, grad_branch, grad_norm_ffn, after):
    places = offsets_of()
    out_at = places[W_SSM_OUT][0]
    lane = places[W_GATE][0] % LINE
    boundary = 2 * PLANE * LINE
    tail_from = (boundary - out_at) // D
    tail = matmul_left_t(ssm_low[:, tail_from:], grad_branch).reshape(-1)
    tail = tail[boundary - out_at - tail_from * D :]
    head = jnp.concatenate([jnp.zeros((14 * LINE,), jnp.float32), tail, grad_norm_ffn])
    head_rows = head.shape[0] // LINE
    carry = jnp.zeros((8, LINE), jnp.float32).at[7, :lane].set(head[head_rows * LINE :])
    head = head[: head_rows * LINE].reshape(head_rows, LINE).astype(jnp.bfloat16)
    return pack_lines(
        None, 2 * PLANE + 32, head_rows, [gate, up, down], lane, 0, [(head, 0)], carry, 48, after
    )


def pack_out(ssm_low, grad_branch, after):
    out_at = offsets_of()[W_SSM_OUT][0]
    first_row = (8 + out_at // LINE) // 16 * 16
    rows = first_row + SSM_HEADS * SSM_DIM * D // LINE
    return pack_lines(
        None, rows, first_row, [(ssm_low, grad_branch)], out_at % LINE, (8 + out_at // LINE) % 8, [],
        jnp.zeros((8, LINE), jnp.float32), 0, after,
    )


def pack_ssm(target, segments, small, ssm_low, grad_branch, after):
    places = offsets_of()
    misc = [small[name_key].reshape(-1) for name_key in (W_STEP,) + small_names[1:-1]]
    count = sum(part.shape[0] for part in misc)
    misc_rows = (count // LINE + 16) // 16 * 16
    opening = matmul_left_t(ssm_low[:, :16], grad_branch).reshape(-1)
    misc = jnp.concatenate(misc + [opening[: misc_rows * LINE - count]])
    misc = misc.reshape(misc_rows, LINE).astype(jnp.bfloat16)
    first_row = 8 + places[W_ATTN_OUT][0] // LINE
    return pack_lines(
        target, target.shape[0], first_row, segments, 0, 0, [(misc, 8 + places[W_STEP][0] // LINE)], None, 0, after
    )


def pack_qkv(segments, attended, grad_branch, grad_norm_attn, after):
    places = offsets_of()
    out_row = 8 + places[W_ATTN_OUT][0] // LINE
    rows = (8 + SHARD) // 16 * 16 + 8 * PIECE
    closing = matmul_left_t(attended[:, :16], grad_branch).reshape(-1, LINE)
    closing = closing[: rows - out_row].astype(jnp.bfloat16)
    opening = jnp.concatenate([jnp.zeros((8, LINE), jnp.float32), grad_norm_attn.reshape(-1, LINE)]).astype(jnp.bfloat16)
    return pack_lines(
        None, rows, 16, segments, 0, 0, [(opening, 0), (closing, out_row)], None, 0, after
    )


def own_lines(early, late, corner):
    z, y, x, c = (lax.axis_index(name) for name in GRID)
    place = 4 * y + 2 * x + c
    shard = SHARD * place
    start = jnp.where(z < 2, (8 + shard) % 16, (14 + shard) % 16)
    lines = jnp.where(z < 2, early, late)
    lines = lax.dynamic_slice(lines, (start, 0), (SHARD, LINE))
    edge = lax.dynamic_slice(corner, (start, 0), (SHARD, LINE))
    lines = jnp.where((z == 0) & (place < 2), edge, lines).astype(jnp.float32)
    return lines.reshape(-1)


def body(span, group, fast, tokens, params, cotangent, offsets):
    rows_dev = tokens.shape[0]
    group_rows = rows_dev * lax.axis_size(span)
    all_rows = group_rows * lax.axis_size(group)
    ssm_inner = SSM_HEADS * SSM_DIM
    score_scale = HEAD_DIM ** (-0.5)
    bounds = offsets[0]
    my_start = lax.axis_index(span) * rows_dev
    row_index = my_start + jnp.arange(rows_dev, dtype=jnp.int32)
    seq_id, positions = sequence_info(row_index, bounds)
    first_start = row_index[0] - positions[0]
    last_row = my_start + rows_dev - 1
    cosine, sine = rotary_tables(positions)
    if fast:
        weights, spread_flow, held = early_weights(params)
    else:
        weights = unpack(lax.all_gather(params, group + span, axis=0, tiled=True))
    small_f32 = {name_key: weights[name_key].astype(jnp.float32) for name_key in small_names[:-1]}
    x_rows = tokens.astype(jnp.float32)
    normed_one, norm_one_back = jax.vjp(rms_norm, x_rows, small_f32[NORM_ATTN])
    hidden = normed_one.astype(jnp.bfloat16)
    across = lambda weight: lax.dot_general(
        weight, hidden, (((0,), (1,)), ((), ())), preferred_element_type=jnp.float32
    )
    q_rot = rotate(across(weights[W_QUERY]), cosine, sine, HEADS_Q).astype(jnp.bfloat16)
    k_rot = rotate(across(weights[W_KEY]), cosine, sine, HEADS_KV).astype(jnp.bfloat16)
    value_low = across(weights[W_VALUE]).astype(jnp.bfloat16).reshape(HEADS_KV, HEAD_DIM, rows_dev)
    kv_mine = jnp.concatenate([k_rot, value_low], axis=1).transpose(0, 2, 1)
    row_starts = row_index - positions
    kv_local = kv_mine.reshape(HEADS_KV, rows_dev, PAIR)
    xbc = jnp.concatenate(
        [matmul(hidden, weights[W_X_SSM]), matmul(hidden, weights[W_B_C])], axis=1
    )
    step_raw = matmul(hidden, weights[W_STEP])
    q_wide = jnp.pad(q_rot * jnp.bfloat16(score_scale), ((0, 0), (0, HEAD_DIM), (0, 0)))
    rim_source = xbc[rows_dev - 8 :]
    if fast:
        (rim_source,) = fence([rim_source], [q_wide])
    rim_rows = passed_along(rim_source, span, 1)
    ssm_meta = jnp.concatenate([my_start[None], row_starts[CHUNK - 1 :: CHUNK]]).astype(jnp.int32)
    conv_bias = small_f32[CONV_BIAS][None, :]
    convolve = lambda after: conv_forward(
        xbc, rim_rows, small_f32[CONV_WEIGHT], conv_bias, ssm_meta, row_starts[:, None], after
    )
    if fast:
        key_blocks = lax.all_gather(kv_local, span)
        conv_values = convolve(())
    else:
        conv_values = convolve(())
    step_in = step_raw.T + small_f32[STEP_BIAS][:, None]
    step_rows = jax.nn.softplus(step_in)
    decay = -jnp.exp(small_f32[DECAY_LOG])
    logs_step = step_rows * decay[:, None]
    order = jnp.arange(rows_dev)
    upto = (order[:, None] <= order[None, :]).astype(jnp.float32)
    cumul = jnp.dot(logs_step, upto, precision=highest)
    chunk_cum = jnp.dot(
        logs_step.reshape(-1, CHUNK), upto[:CHUNK, :CHUNK], precision=highest
    ).reshape(SSM_HEADS, rows_dev)
    went_on = row_starts < my_start
    entry_rows = jnp.where(went_on[None, :], jnp.exp(cumul), 0.0)
    in_last = row_index >= row_starts[rows_dev - 1]
    tail_rows = jnp.exp(jnp.where(in_last[None, :], cumul[:, -1:] - cumul, masked_score))
    carry_all = entry_rows[:, -1]
    summarize = lambda after: weighted_state(conv_values, PAIRS, conv_values, tail_rows * step_rows, after)
    meta = jnp.stack(
        [first_start // KEYS, last_row // KEYS + 1, my_start, row_starts[rows_dev - 1]]
    ).astype(jnp.int32)
    start_row = jnp.broadcast_to(row_starts[None, :], (8, rows_dev))
    if fast:
        (local_state,) = bracket(summarize, [spread_flow])
        scan = Flow(scan_stages(carry_all, local_state, False))
        (gate_in,) = fence([hidden], scan.values())
        gate_ssm = matmul(gate_in, weights[W_GATE_SSM])
        scan.go()
        (gate_ssm,) = fence([gate_ssm], scan.values())
        scan.go()
        mixed, logs = bracket(
            lambda after: attention_forward(
                q_wide, key_blocks, meta, start_row, (*after, gate_ssm, *spread_flow.values())
            ),
            [scan],
        )
        spread_flow.go()
        state_in = scan.result
    else:
        gate_ssm = matmul(hidden, weights[W_GATE_SSM])
        key_blocks = lax.all_gather(kv_local, span)
        if rows_dev != KEYS:
            key_blocks = key_blocks.transpose(1, 0, 2, 3).reshape(HEADS_KV, -1, KEYS, PAIR).transpose(1, 0, 2, 3)
        state_in = scan_states(carry_all, summarize(()), span, fast, False)
        mixed, logs = attention_forward(q_wide, key_blocks, meta, start_row)
    attended = mixed.astype(jnp.bfloat16).reshape(HEADS_Q * HEAD_DIM, rows_dev).T
    attn_out = matmul(attended, weights[W_ATTN_OUT])
    skip_wide = jnp.repeat(small_f32[SKIP_GAIN], SSM_DIM)[None, :]
    ssm_y = ssm_forward(
        conv_values, chunk_cum, step_rows, state_in, skip_wide, ssm_meta, row_starts[:, None], start_row
    )
    normed_ssm, gnorm_back = jax.vjp(gated_norm, ssm_y, gate_ssm, small_f32[NORM_SSM])
    ssm_low = normed_ssm.astype(jnp.bfloat16)
    if fast:
        held = (held[0] + spread_flow.result,) + held[1:]
        weights.update(late_weights(held, [ssm_y]))
    small_f32[NORM_FFN] = weights[NORM_FFN].astype(jnp.float32)
    ssm_out = matmul(ssm_low, weights[W_SSM_OUT])
    middle = x_rows + attn_out + ssm_out
    normed_two, norm_two_back = jax.vjp(rms_norm, middle, small_f32[NORM_FFN])
    hidden_two = normed_two.astype(jnp.bfloat16)
    gate_ffn = matmul(hidden_two, weights[W_GATE])
    upper = matmul(hidden_two, weights[W_UP_PROJ])
    activation_f32, swiglu_back = jax.vjp(swiglu, gate_ffn, upper)
    activation = activation_f32.astype(jnp.bfloat16)
    ffn_out = matmul(activation, weights[W_DOWN])
    result = middle + ffn_out
    squares = jnp.stack(
        [
            jnp.sum(result * result),
            jnp.sum(attn_out * attn_out),
            jnp.sum(ssm_out * ssm_out),
            jnp.sum(ffn_out * ffn_out),
        ]
    )
    grad_out = cotangent.astype(jnp.float32)
    grad_activation = matmul_right_t(cotangent, weights[W_DOWN])
    grad_gate_f32, grad_upper_f32 = swiglu_back(grad_activation)
    grad_gate = grad_gate_f32.astype(jnp.bfloat16)
    grad_upper = grad_upper_f32.astype(jnp.bfloat16)
    grad_hidden_two = matmul_right_t(grad_gate, weights[W_GATE]) + matmul_right_t(
        grad_upper, weights[W_UP_PROJ]
    )
    grad_middle_norm, grad_norm_ffn = norm_two_back(grad_hidden_two)
    grad_middle = grad_out + grad_middle_norm
    grad_branch = grad_middle.astype(jnp.bfloat16)
    grad_attended = matmul_right_t(weights[W_ATTN_OUT], grad_branch).astype(jnp.bfloat16)
    grad_ssm_low = matmul_right_t(grad_branch, weights[W_SSM_OUT])
    grad_ssm_y, grad_gate_ssm_f32, grad_norm_ssm = gnorm_back(grad_ssm_low)
    grad_state_local = weighted_state(conv_values, PAIRS + 1, grad_ssm_y, entry_rows)
    if fast:
        scan = Flow(scan_stages(carry_all, grad_state_local, True, squares)).go()
        (late,) = bracket(
            lambda after: pack_late(
                (hidden_two, grad_gate), (hidden_two, grad_upper), (activation, cotangent),
                ssm_low, grad_branch, grad_norm_ffn, after,
            ),
            [scan],
        )
        late_flow = Flow(reduce_stages(late, 1, 14))
        (grad_branch_low,) = fence([grad_branch], scan.values() + late_flow.values())
        early = pack_out(ssm_low, grad_branch_low, ())
        scan.go()
        grad_state_out, squares = scan.result
        (early,) = fence([early], [grad_state_out])
        late_flow.go()
        (early,) = fence([early], late_flow.values())
        stats_flow = Flow(plane_stages(squares))

        def around(call):
            out = bracket(lambda after: call((*after, *stats_flow.values())), [late_flow])
            stats_flow.go(out[:1])
            return out

    else:
        grad_state_out = scan_states(carry_all, grad_state_local, span, fast, True)
        around = lambda call: call(())
    grad_x, grad_b, grad_c, grad_small = around(
        lambda after: ssm_backward(
            conv_values, grad_ssm_y, chunk_cum, step_rows, state_in, grad_state_out, skip_wide, ssm_meta, start_row,
            after,
        )
    )
    grad_direct = grad_small[:, 0:2].reshape(SSM_HEADS, rows_dev)
    grad_logs = grad_small[:, 2:4].reshape(SSM_HEADS, rows_dev)
    grad_decay_log = decay * jnp.sum(step_rows * grad_logs, axis=1)
    grad_step_rows = (grad_direct + decay[:, None] * grad_logs) * jax.nn.sigmoid(step_in)
    grad_step_bias = jnp.sum(grad_step_rows, axis=1)
    grad_step_raw_f32 = grad_step_rows.T
    grad_skip_gain = jnp.sum(grad_small[:, 4, : 2 * SSM_DIM].reshape(SSM_HEADS, SSM_DIM), axis=1)
    grad_main, grad_tail, grad_edge, grad_taps = around(
        lambda after: conv_backward(
            grad_x, grad_b, grad_c, xbc, rim_rows, small_f32[CONV_WEIGHT], conv_bias, ssm_meta,
            row_starts[:, None], after,
        )
    )
    grad_conv_weight = grad_taps[:CONV]
    grad_conv_bias = grad_taps[CONV]
    rim_back = passed_along(grad_edge, span, -1)
    grad_tail = grad_tail + jnp.pad(rim_back, ((8, 0), (0, 0)))
    grad_xbc = lax.dynamic_update_slice(grad_main, grad_tail.astype(jnp.bfloat16), (rows_dev - 16, 0))
    grad_gate_ssm = grad_gate_ssm_f32.astype(jnp.bfloat16)
    grad_step_raw = grad_step_raw_f32.astype(jnp.bfloat16)
    grad_w_step = matmul_left_t(hidden, grad_step_raw)
    grad_hidden_ssm = (
        matmul_right_t(grad_gate_ssm, weights[W_GATE_SSM])
        + matmul_right_t(grad_xbc[:, :ssm_inner], weights[W_X_SSM])
        + matmul_right_t(grad_xbc[:, ssm_inner:], weights[W_B_C])
        + matmul_right_t(grad_step_raw, weights[W_STEP])
    )
    small = {
        W_STEP: grad_w_step,
        CONV_WEIGHT: grad_conv_weight,
        CONV_BIAS: grad_conv_bias,
        STEP_BIAS: grad_step_bias,
        DECAY_LOG: grad_decay_log,
        SKIP_GAIN: grad_skip_gain,
        NORM_SSM: grad_norm_ssm,
        NORM_FFN: grad_norm_ffn,
    }
    parts = []
    if fast:
        early = pack_ssm(
            early,
            [
                (attended, grad_branch), (hidden, grad_gate_ssm),
                (hidden, grad_xbc[:, :ssm_inner]), (hidden, grad_xbc[:, ssm_inner:]),
            ],
            small, ssm_low, grad_branch, late_flow.values(),
        )
        early_flow = Flow(reduce_stages(early, 0, 8))
        (grad_attended,) = fence([grad_attended], early_flow.values() + late_flow.values())
        around = lambda call: bracket(call, [early_flow])
    g_wide = jnp.pad(grad_attended.reshape(HEADS_Q, HEAD_DIM, rows_dev), ((0, 0), (HEAD_DIM, 0), (0, 0)))
    if fast:
        early_flow.go()
        (g_wide,) = fence([g_wide], early_flow.values())
    for group_at in range(HEADS_KV):
        after_part = [part[1] for part in parts]
        if fast and group_at == 0:
            after_part = late_flow.values()
        parts.append(
            around(
                lambda after: attention_backward(
                    q_wide, g_wide, key_blocks, logs, mixed, meta, start_row, group_at, (*after, *after_part)
                )
            )
        )
    grad_kv = jnp.concatenate([part[0] for part in parts], axis=1)
    grad_q_turned = jnp.concatenate([part[1] for part in parts], axis=0)
    if rows_dev != KEYS:
        grad_kv = grad_kv.transpose(1, 0, 2, 3).reshape(HEADS_KV, -1, rows_dev, PAIR).transpose(1, 0, 2, 3)
    if fast:
        late_flow.go([parts[-1][1]])
        scatter = Flow(scatter_stages(grad_kv))
        (grad_q_turned,) = fence([grad_q_turned], scatter.values() + early_flow.values() + late_flow.values())
    turned_back = rotate(grad_q_turned * score_scale, cosine, -sine, HEADS_Q).astype(jnp.bfloat16)
    grad_query_low = turned_back.reshape(HEADS_Q * HEAD_DIM, rows_dev).T
    if fast:
        scatter.go()
        early_flow.go()
        (grad_query_low,) = fence([grad_query_low], scatter.values() + early_flow.values())
    grad_hidden = grad_hidden_ssm + matmul_right_t(grad_query_low, weights[W_QUERY])
    if fast:
        scatter.go()
        (grad_hidden,) = fence([grad_hidden], scatter.values())
        scatter.go()
        grad_kv_mine = scatter.result
    else:
        grad_kv_mine = scatter_span(grad_kv, span, fast)
    grad_kv_mine = grad_kv_mine.transpose(0, 2, 1)
    grad_key_low = rotate(grad_kv_mine[:, :HEAD_DIM], cosine, -sine, HEADS_KV).astype(jnp.bfloat16)
    grad_key_low = grad_key_low.reshape(HEADS_KV * HEAD_DIM, rows_dev).T
    grad_value_low = grad_kv_mine[:, HEAD_DIM:].astype(jnp.bfloat16).reshape(HEADS_KV * HEAD_DIM, rows_dev).T
    grad_hidden = (
        grad_hidden
        + matmul_right_t(grad_key_low, weights[W_KEY])
        + matmul_right_t(grad_value_low, weights[W_VALUE])
    )
    grad_x_norm, grad_norm_attn = norm_one_back(grad_hidden)
    grad_tokens = grad_middle + grad_x_norm
    if fast:
        corner = pack_qkv(
            [(hidden, grad_query_low), (hidden, grad_key_low), (hidden, grad_value_low)],
            attended, grad_branch, grad_norm_attn, early_flow.values(),
        )
        corner_flow = Flow(corner_stages(corner))
        for _ in range(3):
            corner_flow.go()
        early_flow.go(corner_flow.values()[:1])
        ((pieces, _, _), *_) = corner_flow.sends
        (pieces,) = fence([pieces], early_flow.values())
        corner_flow.sends = [(pieces, axis, pairs) for _, axis, pairs in corner_flow.sends]
        for flow in (early_flow, late_flow, corner_flow):
            while flow.sends:
                flow.go()
        stats = jnp.sqrt(stats_flow.result / (all_rows * D))
        grad_shard = own_lines(early_flow.result, late_flow.result, corner_flow.result)
        return (result.astype(jnp.bfloat16), grad_tokens, grad_shard, stats)
    small[NORM_ATTN] = grad_norm_attn
    stats = jnp.sqrt(lax.psum(squares, group + span) / (all_rows * D))
    pairs = {
        W_QUERY: (hidden, grad_query_low),
        W_KEY: (hidden, grad_key_low),
        W_VALUE: (hidden, grad_value_low),
        W_ATTN_OUT: (attended, grad_branch),
        W_GATE_SSM: (hidden, grad_gate_ssm),
        W_X_SSM: (hidden, grad_xbc[:, :ssm_inner]),
        W_B_C: (hidden, grad_xbc[:, ssm_inner:]),
        W_SSM_OUT: (ssm_low, grad_branch),
        W_GATE: (hidden_two, grad_gate),
        W_UP_PROJ: (hidden_two, grad_upper),
        W_DOWN: (activation, cotangent),
    }
    grad_dict = dict(small)
    for name_key, (left, right) in pairs.items():
        grad_dict[name_key] = matmul_left_t(left, right)
    flat_parts = [grad_dict[name_key].reshape(-1) for name_key, extent in layout()]
    used_entries = 0
    for part_array in flat_parts:
        used_entries += part_array.shape[0]
    flat_parts.append(jnp.zeros((params.shape[0] * lax.axis_size(group + span) - used_entries,), jnp.float32))
    grad_shard = lax.psum_scatter(
        jnp.concatenate(flat_parts), group + span, scatter_dimension=0, tiled=True
    )
    return (result.astype(jnp.bfloat16), grad_tokens, grad_shard, stats)


def solution(mesh):
    fast = (mesh.shape["group"], mesh.shape["span"]) == FAST
    if fast:
        mesh = Mesh(mesh.devices.reshape(4, 2, 2, 2), GRID)
        group, span = (GRID[:1], GRID[1:])
    else:
        group, span = (("group",), ("span",))

    def program(tokens, params, cotangent, offsets):
        return body(span, group, fast, tokens, params, cotangent, offsets)

    return jax.shard_map(
        program,
        mesh=mesh,
        in_specs=(P(group + span, None), P(group + span), P(group + span, None), P(group, None)),
        out_specs=(P(group + span, None), P(group + span, None), P(group + span), P()),
        check_vma=False,
    )
```
